32 devices in a mesh: dp: 4 (over x, core), fsdp: 8 (over z, y).
Axes of the slice: x: 2, y: 2, z: 4, core: 2. Of those that a mesh axis runs over, the one named last changes fastest.
Arguments:
- content: bfloat16 [16384, 768], P(('dp', 'fsdp')), may hold values from -6 to 6
- query: bfloat16 [16384, 768], P(('dp', 'fsdp')), may hold values from -6 to 6
- lengths: int32 [32], P(('dp', 'fsdp')), may hold values from 32 to 512, as said below
- predicted: int32 [16384], P(('dp', 'fsdp')), may hold values 0 or 1
- content_cot: bfloat16 [16384, 768], P(('dp', 'fsdp')), may hold values from -6 to 6
- query_cot: bfloat16 [16384, 768], P(('dp', 'fsdp')), may hold values from -6 to 6
- attn_master: float32 [2, 4, 768, 768], P(None, None, 'fsdp')
- attn_first: float32 [2, 4, 768, 768], P(None, None, 'fsdp')
- attn_second: float32 [2, 4, 768, 768], P(None, None, 'fsdp')
- inner_master: float32 [2, 768, 3072], P(None, 'fsdp'), may hold values from -0.21875 to 0.21875
- inner_first: float32 [2, 768, 3072], P(None, 'fsdp')
- inner_second: float32 [2, 768, 3072], P(None, 'fsdp')
- outer_master: float32 [2, 3072, 768], P(None, 'fsdp'), may hold values from -0.109375 to 0.109375
- outer_first: float32 [2, 3072, 768], P(None, 'fsdp')
- outer_second: float32 [2, 3072, 768], P(None, 'fsdp')
- small_master: float32 [2, 9600], P(None, 'fsdp')
- small_first: float32 [2, 9600], P(None, 'fsdp')
- small_second: float32 [2, 9600], P(None, 'fsdp')
Outputs:
- content_out: bfloat16 [16384, 768], P(('dp', 'fsdp'))
- query_out: bfloat16 [16384, 768], P(('dp', 'fsdp'))
- content_grad: float32 [16384, 768], P(('dp', 'fsdp'))
- query_grad: float32 [16384, 768], P(('dp', 'fsdp'))
- attn_master_new: float32 [2, 4, 768, 768], P(None, None, 'fsdp')
- attn_first_new: float32 [2, 4, 768, 768], P(None, None, 'fsdp')
- attn_second_new: float32 [2, 4, 768, 768], P(None, None, 'fsdp')
- inner_master_new: float32 [2, 768, 3072], P(None, 'fsdp')
- inner_first_new: float32 [2, 768, 3072], P(None, 'fsdp')
- inner_second_new: float32 [2, 768, 3072], P(None, 'fsdp')
- outer_master_new: float32 [2, 3072, 768], P(None, 'fsdp')
- outer_first_new: float32 [2, 3072, 768], P(None, 'fsdp')
- outer_second_new: float32 [2, 3072, 768], P(None, 'fsdp')
- small_master_new: float32 [2, 9600], P(None, 'fsdp')
- small_first_new: float32 [2, 9600], P(None, 'fsdp')
- small_second_new: float32 [2, 9600], P(None, 'fsdp')
The draws below stay inside these ranges and needn't reach their ends.
Inputs may be any that keep to these rules, and one draw needn't show every extreme that they name: lengths: heavy-tailed; one sequence of the batch has exactly 512.
All inputs are finite; a program needn't handle non-finite values. No bound on the sum of `predicted` on one device may be relied on, other than what follows from the above.
Results may differ from the reference program's by a relative error of at most 0.02.
Values may be sent and summed in bfloat16 or wider, within the bound.
No kernel may reach another device: no remote copies, remote signals or barrier semaphores. Data moves between devices by JAX's collectives and lax.ppermute only.
A program may use at most 320 MiB of HBM per device.

```python
import math
from functools import partial
import jax
import jax.numpy as jnp
from jax import lax

D = 768
H = 12
DH = 64
FF = 3072
LEN = 512
NB = 32
MIN_LEN = 32
LAYERS = 2
STEP = 10
SEQS = 32
TOKENS = 16384
SMALL = 9600


def first_moment(key, shape, grad_size):
    return 0.1 / 0.9 * grad_size * jax.random.truncated_normal(key, -4.0, 4.0, shape, jnp.float32)


def second_moment(key, shape, grad_size):
    factor = jnp.exp(jax.random.uniform(key, shape, jnp.float32, 0.0, math.log(4.0)))
    return 0.001 / 0.999 * grad_size * grad_size * factor


def draw_lengths(key, part):
    key = jax.random.fold_in(key, 1)
    first_key, second_key = jax.random.split(key)
    raw_draw = jax.random.randint(first_key, (SEQS,), 0, 1024)
    cubed = raw_draw * raw_draw // 1024 * raw_draw // 1024
    length = MIN_LEN + (LEN - MIN_LEN) * cubed // 1024
    chosen = jax.random.randint(second_key, (), 0, SEQS)
    return jnp.where(jnp.arange(SEQS) == chosen, LEN, length).astype(jnp.int32)


def draw_attn_master(key, part):
    key = jax.random.fold_in(key, 2)
    noise = jax.random.truncated_normal(key, -4.0, 4.0, (LAYERS, 4, D, D), jnp.float32)
    which = jnp.arange(4)[None, :, None, None]
    return noise * jnp.where(which == 3, 6.0, 1.0) / math.sqrt(D)


def draw_small_master(key, part):
    key = jax.random.fold_in(key, 3)
    noise = jax.random.truncated_normal(key, -4.0, 4.0, (LAYERS, SMALL), jnp.float32)
    position = jnp.arange(SMALL)[None, :]
    gain_part = (position >= 3 * D) & (position < 4 * D) | (position >= 6 * D) & (position < 7 * D)
    table_part = position >= 8 * D + FF
    return jnp.where(gain_part, 1.0 + 0.1 * noise, jnp.where(table_part, 0.5 * noise, 0.2 * noise))


def draw_attn_first(key, part):
    key = jax.random.fold_in(key, 4)
    return first_moment(key, (LAYERS, 4, D, D), 0.3 * math.sqrt(TOKENS))


def draw_attn_second(key, part):
    key = jax.random.fold_in(key, 5)
    return second_moment(key, (LAYERS, 4, D, D), 0.3 * math.sqrt(TOKENS))


def draw_inner_first(key, part):
    key = jax.random.fold_in(key, 6)
    return first_moment(key, (LAYERS, D, FF), 0.4 * math.sqrt(TOKENS))


def draw_inner_second(key, part):
    key = jax.random.fold_in(key, 7)
    return second_moment(key, (LAYERS, D, FF), 0.4 * math.sqrt(TOKENS))


def draw_outer_first(key, part):
    key = jax.random.fold_in(key, 8)
    return first_moment(key, (LAYERS, FF, D), 0.4 * math.sqrt(TOKENS))


def draw_outer_second(key, part):
    key = jax.random.fold_in(key, 9)
    return second_moment(key, (LAYERS, FF, D), 0.4 * math.sqrt(TOKENS))


def draw_small_first(key, part):
    key = jax.random.fold_in(key, 10)
    return first_moment(key, (LAYERS, SMALL), math.sqrt(TOKENS))


def draw_small_second(key, part):
    key = jax.random.fold_in(key, 11)
    return second_moment(key, (LAYERS, SMALL), math.sqrt(TOKENS))


def place_ends(array, stream_key, low, top_value):
    dims = array.shape
    place = [jax.random.randint(jax.random.fold_in(stream_key, axis), (), 0, dims[axis]) for axis in range(len(dims))]
    array = array.at[tuple(place)].set(low)
    longest = dims.index(max(dims))
    place[longest] = (place[longest] + 1) % dims[longest]
    return array.at[tuple(place)].set(top_value)


def block_levels(own_key, shape, shards, least, top_value):
    def one(dim, shards_of):
        heights = jax.random.uniform(jax.random.fold_in(jax.random.fold_in(own_key, 6), dim), (shards_of,), jnp.float32, least / len(shards), top_value / len(shards))
        return jnp.repeat(jnp.exp(heights), shape[dim] // shards_of).reshape((-1,) + (1,) * (len(shape) - dim - 1))

    level = one(*shards[0])
    for cut in shards[1:]:
        level = level * one(*cut)
    return level


def bell_draw(rng, shape, width, reach, shards=(), kind=jnp.bfloat16):
    entries = width * jax.random.normal(rng, shape, jnp.float32)
    if shards:
        entries = entries * block_levels(rng, shape, shards, -0.22, 0.18)
    return jnp.clip(entries, -reach, reach).astype(kind)


def setup_inputs(seed: int = 0) -> dict:
    key_list = jax.random.split(jax.random.key(seed), 19)
    return {
        "content": bell_draw(key_list[0], (TOKENS, D), 1.0, 6.0, ((0, 32),)),
        "query": bell_draw(key_list[1], (TOKENS, D), 1.0, 6.0, ((0, 32),)),
        "lengths": draw_lengths(jax.random.fold_in(key_list[18], 71), 0),
        "predicted": place_ends((jax.random.randint(key_list[3], (TOKENS,), 0, 100) < 15).astype(jnp.int32), jax.random.fold_in(key_list[3], 1), 0, 1),
        "content_cot": bell_draw(key_list[4], (TOKENS, D), 1.0, 6.0, ((0, 32),)),
        "query_cot": bell_draw(key_list[5], (TOKENS, D), 1.0, 6.0, ((0, 32),)),
        "attn_master": draw_attn_master(jax.random.fold_in(key_list[18], 71), 0),
        "attn_first": draw_attn_first(jax.random.fold_in(key_list[18], 71), 0),
        "attn_second": draw_attn_second(jax.random.fold_in(key_list[18], 71), 0),
        "inner_master": bell_draw(key_list[9], (LAYERS, D, FF), D ** -0.5, 0.21875, ((1, 8),), jnp.float32),
        "inner_first": draw_inner_first(jax.random.fold_in(key_list[18], 71), 0),
        "inner_second": draw_inner_second(jax.random.fold_in(key_list[18], 71), 0),
        "outer_master": bell_draw(key_list[12], (LAYERS, FF, D), FF ** -0.5, 0.109375, ((1, 8),), jnp.float32),
        "outer_first": draw_outer_first(jax.random.fold_in(key_list[18], 71), 0),
        "outer_second": draw_outer_second(jax.random.fold_in(key_list[18], 71), 0),
        "small_master": draw_small_master(jax.random.fold_in(key_list[18], 71), 0),
        "small_first": draw_small_first(jax.random.fold_in(key_list[18], 71), 0),
        "small_second": draw_small_second(jax.random.fold_in(key_list[18], 71), 0),
    }


@jax.custom_vjp
def low(v):
    return lax.optimization_barrier(v.astype(jnp.bfloat16)).astype(jnp.float32)

@jax.custom_vjp
def low_back(v):
    return v

def low_keep(v):
    return (low(v), None)

def low_pass(kept, grad):
    return (grad,)

def back_keep(v):
    return (v, None)

def back_low(kept, grad):
    return (low(grad),)
low.defvjp(low_keep, low_pass)
low_back.defvjp(back_keep, back_low)
HIGHEST = lax.Precision.HIGHEST
NORM_EPS = 1e-05
MASKED = -1000000000.0
BETA_ONE = 0.9
BETA_TWO = 0.999
ATTENTION_RATE = 0.1
FEED_RATE = 0.02
SMALL_RATE = 0.4
WEIGHT_DECAY = 0.01
ADAM_EPS = 1e-08
SCORE_SCALE = 0.125

def lowboth(value):
    return low_back(low(value))

def matmul(left, right):
    return jnp.dot(left, right, precision=HIGHEST)

def layer_norm(values, gain, shift):
    centre = values - lax.optimization_barrier(jnp.mean(values, axis=-1, keepdims=True))
    spread = lax.optimization_barrier(jnp.mean(centre * centre, axis=-1, keepdims=True))
    return centre * lax.rsqrt(spread + NORM_EPS) * gain + shift

def unpack(vectors):
    pieces = [vectors[piece_index * D:(piece_index + 1) * D] for piece_index in range(8)]
    hidden_bias = vectors[8 * D:8 * D + FF]
    bias_table = vectors[8 * D + FF:].reshape(H, NB)
    return (pieces, hidden_bias, bias_table)

def bucket_ids():
    position = jnp.arange(LEN, dtype=jnp.int32)
    offset = position[None, :] - position[:, None]
    distance = jnp.abs(offset)
    far_bucket = jnp.full(distance.shape, 8, jnp.int32)
    for exponent in range(1, 8):
        far_bucket = far_bucket + (distance * distance >= 64 * 2 ** exponent).astype(jnp.int32)
    near_or_far = jnp.where(distance < 8, distance, far_bucket)
    return near_or_far + NB // 2 * (offset > 0).astype(jnp.int32)

def allowed_pairs(length, pred_flags):
    position = jnp.arange(LEN, dtype=jnp.int32)
    valid_key = (position < length)[None, :]
    row_pos = position[:, None]
    col_pos = position[None, :]
    free_key = (pred_flags == 0)[None, :]
    content_ok = valid_key & (free_key | (pred_flags[:, None] == 1) & (col_pos <= row_pos))
    query_ok = valid_key & (col_pos != row_pos) & (free_key | (col_pos < row_pos))
    return (content_ok, query_ok)

def one_sequence(bias_table, sequence_item):
    content_rows, query_rows, key_rows, value_rows, length, pred_flags = sequence_item
    position_bias = jnp.take(bias_table, bucket_ids(), axis=1)
    content_ok, query_ok = allowed_pairs(length, pred_flags)
    mixed_rows = []
    for row_block, allowed in ((content_rows, content_ok), (query_rows, query_ok)):
        scores = jnp.einsum('qhd,khd->hqk', row_block, key_rows, precision=HIGHEST) * SCORE_SCALE + position_bias
        scores = jnp.where(allowed[None], low_back(scores), MASKED)
        probs_low = low(jax.nn.softmax(scores, axis=-1))
        mixed_rows.append(lowboth(jnp.einsum('hqk,khd->qhd', probs_low, value_rows, precision=HIGHEST)))
    return (mixed_rows[0], mixed_rows[1])

def feed_forward(normed, inner_w, outer_w, hidden_bias, bias_two, gain_two, shift_two):
    pre_act = low_back(matmul(low(normed), inner_w) + hidden_bias)
    active = low(jax.nn.gelu(pre_act, approximate=True))
    branch = low_back(matmul(active, outer_w) + bias_two)
    return layer_norm(normed + branch, gain_two, shift_two)

def one_layer(content_in, query_in, weights, lengths, predicted):
    attn_w, inner_w, outer_w, small_w = weights
    pieces, hidden_bias, bias_table = unpack(small_w)
    bias_q, bias_v, bias_o, gain_one, shift_one, bias_two, gain_two, shift_two = pieces
    content_low = low(content_in)
    query_low = low(query_in)
    query_c = lowboth(matmul(content_low, attn_w[0]) + bias_q)
    key_rows = lowboth(matmul(content_low, attn_w[1]))
    value_rows = lowboth(matmul(content_low, attn_w[2]) + bias_v)
    query_q = lowboth(matmul(query_low, attn_w[0]) + bias_q)
    shape_four = (SEQS, LEN, H, DH)
    mixed_c, mixed_q = lax.map(jax.checkpoint(partial(one_sequence, bias_table)), (query_c.reshape(shape_four), query_q.reshape(shape_four), key_rows.reshape(shape_four), value_rows.reshape(shape_four), lengths, predicted.reshape(SEQS, LEN)))
    branch_c = low_back(matmul(mixed_c.reshape(TOKENS, D), attn_w[3]) + bias_o)
    branch_q = low_back(matmul(mixed_q.reshape(TOKENS, D), attn_w[3]) + bias_o)
    normed_c = layer_norm(content_in + branch_c, gain_one, shift_one)
    normed_q = layer_norm(query_in + branch_q, gain_one, shift_one)
    out_c = feed_forward(normed_c, inner_w, outer_w, hidden_bias, bias_two, gain_two, shift_two)
    out_q = feed_forward(normed_q, inner_w, outer_w, hidden_bias, bias_two, gain_two, shift_two)
    return (out_c, out_q)

def adam_update(master, first, second, grad, rate):
    first_new = BETA_ONE * first + (1.0 - BETA_ONE) * grad
    second_new = BETA_TWO * second + (1.0 - BETA_TWO) * grad * grad
    first_hat = first_new / (1.0 - BETA_ONE ** STEP)
    second_hat = second_new / (1.0 - BETA_TWO ** STEP)
    master_new = master - rate * (first_hat / (jnp.sqrt(second_hat) + ADAM_EPS) + WEIGHT_DECAY * master)
    return (master_new, first_new, second_new)

def reference(content, query, lengths, predicted, content_cot, query_cot, attn_master, attn_first, attn_second, inner_master, inner_first, inner_second, outer_master, outer_first, outer_second, small_master, small_first, small_second):
    working = (low(attn_master), low(inner_master), low(outer_master), low(small_master))

    def model(weights, content_in, query_in):
        for layer_index in range(LAYERS):
            content_in, query_in = one_layer(content_in, query_in, tuple((weight[layer_index] for weight in weights)), lengths, predicted)
        return (content_in, query_in)
    (out_c, out_q), pullback = jax.vjp(model, working, content.astype(jnp.float32), query.astype(jnp.float32))
    position = jnp.arange(LEN, dtype=jnp.int32)
    valid_rows = (position[None, :] < lengths[:, None]).reshape(TOKENS, 1).astype(jnp.float32)
    grads, grad_content, grad_query = pullback((content_cot.astype(jnp.float32) * valid_rows, query_cot.astype(jnp.float32) * valid_rows))
    attn_new = adam_update(attn_master, attn_first, attn_second, grads[0], ATTENTION_RATE)
    inner_new = adam_update(inner_master, inner_first, inner_second, grads[1], FEED_RATE)
    outer_new = adam_update(outer_master, outer_first, outer_second, grads[2], FEED_RATE)
    small_new = adam_update(small_master, small_first, small_second, grads[3], SMALL_RATE)
    return (out_c.astype(jnp.bfloat16), out_q.astype(jnp.bfloat16), grad_content, grad_query, attn_new[0], attn_new[1], attn_new[2], inner_new[0], inner_new[1], inner_new[2], outer_new[0], outer_new[1], outer_new[2], small_new[0], small_new[1], small_new[2])
```

```python
from functools import partial

import jax
import jax.numpy as jnp
from jax import lax
from jax.experimental import pallas as pl
from jax.experimental.pallas import tpu as pltpu
from jax.sharding import PartitionSpec as P

D = 768
H = 12
DH = 64
FF = 3072
LEN = 512
NB = 32
LAYERS = 2
STEP = 10


NORM_EPS = 1e-05
MASKED = -1000000000.0
BETA_ONE = 0.9
BETA_TWO = 0.999
ATTENTION_RATE = 0.1
FEED_RATE = 0.02
SMALL_RATE = 0.4
WEIGHT_DECAY = 0.01
ADAM_EPS = 1e-08
SCORE_SCALE = 0.125


def layer_norm(values, gain, shift):
    centre = values - jnp.mean(values, axis=-1, keepdims=True)
    spread = jnp.mean(centre * centre, axis=-1, keepdims=True)
    return centre * lax.rsqrt(spread + NORM_EPS) * gain + shift


def unpack(vectors):
    pieces = [vectors[piece_index * D : (piece_index + 1) * D] for piece_index in range(8)]
    hidden_bias = vectors[8 * D : 8 * D + FF]
    bias_table = vectors[8 * D + FF :].reshape(H, NB)
    return (pieces, hidden_bias, bias_table)


def bucket_ids():
    position = jnp.arange(LEN, dtype=jnp.int32)
    offset = position[None, :] - position[:, None]
    distance = jnp.abs(offset)
    far_bucket = jnp.full(distance.shape, 8, jnp.int32)
    for exponent in range(1, 8):
        far_bucket = far_bucket + (distance * distance >= 64 * 2**exponent).astype(jnp.int32)
    near_or_far = jnp.where(distance < 8, distance, far_bucket)
    return near_or_far + NB // 2 * (offset > 0).astype(jnp.int32)


def bucket_onehot():
    return (bucket_ids()[:, :, None] == jnp.arange(NB, dtype=jnp.int32)[None, None, :]).astype(
        jnp.bfloat16
    )


def allowed_pairs(length, pred_flags):
    position = jnp.arange(LEN, dtype=jnp.int32)
    valid_key = (position < length)[None, :]
    row_pos = position[:, None]
    col_pos = position[None, :]
    free_key = (pred_flags == 0)[None, :]
    content_ok = valid_key & (free_key | (pred_flags[:, None] == 1) & (col_pos <= row_pos))
    query_ok = valid_key & (col_pos != row_pos) & (free_key | (col_pos < row_pos))
    return (content_ok, query_ok)


def masked_scores(query_rows, key_rows, position_bias, allowed):
    scores = (
        jnp.einsum("qhd,khd->hqk", query_rows, key_rows, preferred_element_type=jnp.float32)
        * SCORE_SCALE
        + position_bias
    )
    return jnp.where(allowed[None], scores, MASKED)


def table_bias(onehot, table_low):
    return jnp.einsum("qkb,hb->hqk", onehot, table_low, preferred_element_type=jnp.float32)


def attend_slot(onehot, table_low, slot_item):
    query_c, query_q, key_rows, value_rows, length, pred_flags = slot_item
    position_bias = table_bias(onehot, table_low)
    content_ok, query_ok = allowed_pairs(length, pred_flags)
    results = []
    for query_rows, allowed in ((query_c, content_ok), (query_q, query_ok)):
        scores = masked_scores(query_rows, key_rows, position_bias, allowed)
        peak = jnp.max(scores, axis=-1, keepdims=True)
        expos = jnp.exp(scores - peak)
        totals = jnp.sum(expos, axis=-1, keepdims=True)
        probs = (expos / totals).astype(jnp.bfloat16)
        mixed = jnp.einsum(
            "hqk,khd->qhd", probs, value_rows, preferred_element_type=jnp.float32
        ).astype(jnp.bfloat16)
        results.append((mixed, peak[..., 0] + jnp.log(totals[..., 0])))
    return (results[0][0], results[1][0], results[0][1], results[1][1])


def attend_back(onehot, table_low, slot_item):
    (
        query_c,
        query_q,
        key_rows,
        value_rows,
        length,
        pred_flags,
        lse_c,
        lse_q,
        grad_mix_c,
        grad_mix_q,
    ) = slot_item
    position_bias = table_bias(onehot, table_low)
    content_ok, query_ok = allowed_pairs(length, pred_flags)
    grad_keys = jnp.zeros(key_rows.shape, jnp.float32)
    grad_values = jnp.zeros(value_rows.shape, jnp.float32)
    grad_table = jnp.zeros((H, NB), jnp.float32)
    grads_query = []
    for query_rows, allowed, log_total, grad_mix in (
        (query_c, content_ok, lse_c, grad_mix_c),
        (query_q, query_ok, lse_q, grad_mix_q),
    ):
        scores = masked_scores(query_rows, key_rows, position_bias, allowed)
        probs = jnp.exp(scores - log_total[..., None])
        grad_values = grad_values + jnp.einsum(
            "hqk,qhd->khd", probs.astype(jnp.bfloat16), grad_mix, preferred_element_type=jnp.float32
        )
        grad_probs = jnp.einsum(
            "qhd,khd->hqk", grad_mix, value_rows, preferred_element_type=jnp.float32
        )
        grad_scores = probs * (grad_probs - jnp.sum(probs * grad_probs, axis=-1, keepdims=True))
        grad_scores = jnp.where(allowed[None], grad_scores, 0.0).astype(jnp.bfloat16)
        grad_table = grad_table + jnp.einsum(
            "hqk,qkb->hb", grad_scores, onehot, preferred_element_type=jnp.float32
        )
        grads_query.append(
            jnp.einsum("hqk,khd->qhd", grad_scores, key_rows, preferred_element_type=jnp.float32)
            * SCORE_SCALE
        )
        grad_keys = (
            grad_keys
            + jnp.einsum(
                "hqk,qhd->khd", grad_scores, query_rows, preferred_element_type=jnp.float32
            )
            * SCORE_SCALE
        )
    return (grads_query[0], grads_query[1], grad_keys, grad_values, grad_table)


def to_heads(values):
    return values.reshape(-1, LEN, H, DH)


AXES = ("dp", "fsdp")
GRID = (2, 2, 4, 2)
ROWS = 96


def places():
    return [
        (x, c, z, y) for x in range(2) for c in range(2) for z in range(4) for y in range(2)
    ]


def flat(x, c, z, y):
    return ((x * 2 + c) * 4 + z) * 2 + y


def move(value, shift):
    pairs = [(flat(*place), flat(*shift(*place))) for place in places()]
    return lax.ppermute(value, AXES, pairs)


def swap_core(value):
    return move(value, lambda x, c, z, y: (x, 1 - c, z, y))


def swap_x(value):
    return move(value, lambda x, c, z, y: (1 - x, c, z, y))


def swap_y(value):
    return move(value, lambda x, c, z, y: (x, c, z, 1 - y))


def shift_z(value, step):
    return move(value, lambda x, c, z, y: (x, c, (z + step) % 4, y))


def my_place():
    dp = lax.axis_index("dp")
    fsdp = lax.axis_index("fsdp")
    return (dp // 2, dp % 2, fsdp // 2, fsdp % 2)


def spread_blocks(own):
    column = jnp.stack([own] + [shift_z(own, step) for step in (1, 2, 3)])
    from_x = swap_x(column)
    from_y = swap_y(column)
    corner_low = swap_x(from_y[:2])
    corner_high = swap_y(from_x[2:])
    mine = (column, from_x, from_y, corner_low, corner_high)
    return mine + tuple(swap_core(piece) for piece in mine)


PIECES = ((0, 0, 0, 4), (1, 0, 0, 4), (0, 1, 0, 4), (1, 1, 0, 2), (1, 1, 2, 4))


def assemble_kernel(kinds, place_ref, *refs):
    x, c, z, y = (place_ref[index] for index in range(4))
    pieces = refs[:10]
    outs = refs[10 : 10 + len(kinds)]
    sems = refs[10 + len(kinds)]
    copies = []
    for other in range(2):
        for piece, (dx, dy, first, last) in enumerate(PIECES):
            for k in range(first, last):
                quarter = (x ^ dx) * 2 + (c ^ other)
                owner = ((z - k) & 3) * 2 + (y ^ dy)
                for member, kind in enumerate(kinds):
                    if kind == "attn":
                        target = outs[member].at[quarter, pl.ds(owner * 96, 96), :]
                    elif kind == "inner":
                        target = outs[member].at[pl.ds(owner * 96, 96), pl.ds(quarter * 768, 768)]
                    else:
                        target = outs[member].at[pl.ds(owner * 384 + quarter * 96, 96), :]
                    copy = pltpu.make_async_copy(
                        pieces[other * 5 + piece].at[k - first, member],
                        target,
                        sems.at[len(copies)],
                    )
                    copy.start()
                    copies.append(copy)
    for copy in copies:
        copy.wait()


SHAPES = {"attn": (4, D, D), "inner": (D, FF), "outer": (FF, D)}


def assemble(kinds, place, pieces):
    any_spec = pl.BlockSpec(memory_space=pl.ANY)
    return pl.pallas_call(
        partial(assemble_kernel, kinds),
        out_shape=[jax.ShapeDtypeStruct(SHAPES[kind], jnp.bfloat16) for kind in kinds],
        in_specs=[pl.BlockSpec(memory_space=pltpu.SMEM)] + [any_spec] * 10,
        out_specs=[any_spec] * len(kinds),
        scratch_shapes=[pltpu.SemaphoreType.DMA((32 * len(kinds),))],
        name="assemble",
    )(place, *pieces)


def own_quarter(kind, shard, quarter):
    if kind == "attn":
        part = lax.dynamic_index_in_dim(shard, quarter, 0, keepdims=False)
    elif kind == "inner":
        part = lax.dynamic_slice_in_dim(shard, quarter * D, D, 1)
    else:
        part = lax.dynamic_slice_in_dim(shard, quarter * ROWS, ROWS, 0)
    return part.astype(jnp.bfloat16)


def gather_group(kinds, shards):
    x, c, z, y = my_place()
    own = jnp.stack([own_quarter(kind, shard, x * 2 + c) for kind, shard in zip(kinds, shards)])
    place = jnp.stack([x, c, z, y]).astype(jnp.int32)
    return assemble(kinds, place, spread_blocks(own))


def to_blocks(kind, grad):
    low = grad.astype(jnp.bfloat16)
    if kind == "attn":
        return low.reshape(2, 2, 4, 2, ROWS, D)
    if kind == "inner":
        return low.reshape(4, 2, ROWS, 2, 2, D).transpose(3, 4, 0, 1, 2, 5)
    return low.reshape(4, 2, 2, 2, ROWS, D).transpose(2, 3, 0, 1, 4, 5)


def add_low(*values):
    total = values[0].astype(jnp.float32)
    for value in values[1:]:
        total = total + value.astype(jnp.float32)
    return total.astype(jnp.bfloat16)


def pick(value, axis, index):
    return lax.dynamic_index_in_dim(value, index, axis, keepdims=False)


def reduce_group(kinds, grads):
    x, c, z, y = my_place()
    blocks = jnp.stack([to_blocks(kind, grad) for kind, grad in zip(kinds, grads)], axis=4)
    both = add_low(pick(blocks, 1, c), swap_core(pick(blocks, 1, 1 - c)))
    parts = {}
    for dx in range(2):
        for dy in range(2):
            parts[dx, dy] = pick(pick(both, 2, y ^ dy), 0, x ^ dx)
    corner = parts[1, 1]
    by_x = swap_x(corner[:2])
    by_y = swap_y(corner[2:])
    for_y = jnp.concatenate([add_low(parts[0, 1][:2], by_x), parts[0, 1][2:]])
    for_x = jnp.concatenate([parts[1, 0][:2], add_low(parts[1, 0][2:], by_y)])
    column = add_low(parts[0, 0], swap_x(for_x), swap_y(for_y))
    total = pick(column, 0, z).astype(jnp.float32)
    for step in (1, 2, 3):
        total = total + shift_z(pick(column, 0, (z + step) % 4), step).astype(jnp.float32)
    low = total.astype(jnp.bfloat16)
    pair = jnp.stack([low, swap_x(low)])
    both_pairs = jnp.stack([pair, swap_core(pair)], axis=1)
    quarters = jnp.stack(
        [
            jnp.stack([pick(pick(both_pairs, 1, c ^ core), 0, x ^ side) for core in range(2)])
            for side in range(2)
        ]
    )
    results = []
    for member, kind in enumerate(kinds):
        four = quarters[:, :, member].reshape(4, ROWS, D).astype(jnp.float32)
        if kind == "attn":
            results.append(four)
        elif kind == "inner":
            results.append(four.transpose(1, 0, 2).reshape(ROWS, FF))
        else:
            results.append(four.reshape(4 * ROWS, D))
    return results


def fetch_layer(fast, shards):
    if not fast:
        return fetch_forward(shards)
    (attn,) = gather_group(("attn",), shards[:1])
    inner, outer = gather_group(("inner", "outer"), shards[1:3])
    return (attn, inner, outer)


def reduce_fast(grads):
    inner, outer = reduce_group(("inner", "outer"), grads[1:3])
    (attn,) = reduce_group(("attn",), grads[:1])
    return (attn, inner, outer)


def fetch_forward(shards):
    low = tuple(shard.astype(jnp.bfloat16) for shard in shards)
    return (
        lax.all_gather(low[0], "fsdp", axis=1, tiled=True),
        lax.all_gather(low[1], "fsdp", axis=0, tiled=True),
        lax.all_gather(low[2], "fsdp", axis=0, tiled=True),
    )


def reduce_layer(grads):
    owned = tuple(
        lax.psum_scatter(
            grad.astype(jnp.bfloat16), "fsdp", scatter_dimension=axis, tiled=True
        ).astype(jnp.float32)
        for grad, axis in zip(grads, (1, 0, 0))
    )
    return lax.psum(owned, "dp")


def forward_layer(hidden_c, hidden_q, weights, lengths, flag_rows, onehot):
    attn_w, inner_w, outer_w, small_w = weights
    pieces, hidden_bias, bias_table = unpack(small_w.astype(jnp.float32))
    bias_q, bias_v, bias_o, gain_one, shift_one, bias_two, gain_two, shift_two = pieces
    table_low = bias_table.astype(jnp.bfloat16)
    low_c = hidden_c.astype(jnp.bfloat16)
    low_q = hidden_q.astype(jnp.bfloat16)
    projected = jnp.einsum("td,sde->ste", low_c, attn_w[:3], preferred_element_type=jnp.float32)
    query_c = (projected[0] + bias_q).astype(jnp.bfloat16)
    key_rows = projected[1].astype(jnp.bfloat16)
    value_rows = (projected[2] + bias_v).astype(jnp.bfloat16)
    query_q = (jnp.dot(low_q, attn_w[0], preferred_element_type=jnp.float32) + bias_q).astype(
        jnp.bfloat16
    )
    mixed_c, mixed_q, lse_c, lse_q = lax.map(
        partial(attend_slot, onehot, table_low),
        (
            to_heads(query_c),
            to_heads(query_q),
            to_heads(key_rows),
            to_heads(value_rows),
            lengths,
            flag_rows,
        ),
    )
    mixed_c = mixed_c.reshape(-1, D)
    mixed_q = mixed_q.reshape(-1, D)
    outputs = []
    kept = []
    for hidden_in, mixed in ((hidden_c, mixed_c), (hidden_q, mixed_q)):
        resid = hidden_in + jnp.dot(mixed, attn_w[3], preferred_element_type=jnp.float32) + bias_o
        normed = layer_norm(resid, gain_one, shift_one)
        pre_act = (
            jnp.dot(normed.astype(jnp.bfloat16), inner_w, preferred_element_type=jnp.float32)
            + hidden_bias
        )
        active = jax.nn.gelu(pre_act, approximate=True).astype(jnp.bfloat16)
        summed = normed + jnp.dot(active, outer_w, preferred_element_type=jnp.float32) + bias_two
        outputs.append(layer_norm(summed, gain_two, shift_two))
        kept.append((resid, summed, pre_act))
    saved = (
        hidden_c,
        hidden_q,
        query_c,
        query_q,
        key_rows,
        value_rows,
        lse_c,
        lse_q,
        mixed_c,
        mixed_q,
        kept[0],
        kept[1],
    )
    return (outputs[0], outputs[1], saved)


def backward_layer(saved, weights, grad_c, grad_q, lengths, flag_rows, onehot):
    attn_w, inner_w, outer_w, small_w = weights
    pieces, hidden_bias, bias_table = unpack(small_w.astype(jnp.float32))
    bias_q, bias_v, bias_o, gain_one, shift_one, bias_two, gain_two, shift_two = pieces
    table_low = bias_table.astype(jnp.bfloat16)
    (
        hidden_c,
        hidden_q,
        query_c,
        query_q,
        key_rows,
        value_rows,
        lse_c,
        lse_q,
        mixed_c,
        mixed_q,
        kept_c,
        kept_q,
    ) = saved
    gelu_tanh = partial(jax.nn.gelu, approximate=True)
    grad_outer = jnp.zeros(outer_w.shape, jnp.float32)
    grad_inner = jnp.zeros(inner_w.shape, jnp.float32)
    grad_attn_out = jnp.zeros((D, D), jnp.float32)
    grad_bias_two = jnp.zeros((D,), jnp.float32)
    grad_hidden_bias = jnp.zeros((FF,), jnp.float32)
    grad_bias_o = jnp.zeros((D,), jnp.float32)
    grad_gain_one = jnp.zeros((D,), jnp.float32)
    grad_shift_one = jnp.zeros((D,), jnp.float32)
    grad_gain_two = jnp.zeros((D,), jnp.float32)
    grad_shift_two = jnp.zeros((D,), jnp.float32)
    residual_grads = []
    mix_grads = []
    for kept_rows, grad_out, mixed in ((kept_c, grad_c, mixed_c), (kept_q, grad_q, mixed_q)):
        resid, summed, pre_act = kept_rows
        normed, norm_one_back = jax.vjp(layer_norm, resid, gain_one, shift_one)
        unused_out, norm_two_back = jax.vjp(layer_norm, summed, gain_two, shift_two)
        grad_summed, grad_g2, grad_s2 = norm_two_back(grad_out)
        grad_gain_two = grad_gain_two + grad_g2
        grad_shift_two = grad_shift_two + grad_s2
        grad_branch = grad_summed.astype(jnp.bfloat16)
        grad_bias_two = grad_bias_two + jnp.sum(grad_branch.astype(jnp.float32), axis=0)
        active, gelu_back = jax.vjp(gelu_tanh, pre_act)
        grad_outer = grad_outer + jnp.einsum(
            "tf,td->fd",
            active.astype(jnp.bfloat16),
            grad_branch,
            preferred_element_type=jnp.float32,
        )
        grad_active = jnp.einsum(
            "td,fd->tf", grad_branch, outer_w, preferred_element_type=jnp.float32
        )
        grad_pre = gelu_back(grad_active)[0].astype(jnp.bfloat16)
        grad_hidden_bias = grad_hidden_bias + jnp.sum(grad_pre.astype(jnp.float32), axis=0)
        grad_inner = grad_inner + jnp.einsum(
            "td,tf->df", normed.astype(jnp.bfloat16), grad_pre, preferred_element_type=jnp.float32
        )
        grad_normed = grad_summed + jnp.einsum(
            "tf,df->td", grad_pre, inner_w, preferred_element_type=jnp.float32
        )
        grad_resid, grad_g1, grad_s1 = norm_one_back(grad_normed)
        grad_gain_one = grad_gain_one + grad_g1
        grad_shift_one = grad_shift_one + grad_s1
        grad_proj = grad_resid.astype(jnp.bfloat16)
        grad_bias_o = grad_bias_o + jnp.sum(grad_proj.astype(jnp.float32), axis=0)
        grad_attn_out = grad_attn_out + jnp.einsum(
            "td,te->de", mixed, grad_proj, preferred_element_type=jnp.float32
        )
        mix_grads.append(
            jnp.einsum(
                "te,de->td", grad_proj, attn_w[3], preferred_element_type=jnp.float32
            ).astype(jnp.bfloat16)
        )
        residual_grads.append(grad_resid)
    grad_query_c, grad_query_q, grad_keys, grad_values, grad_table = lax.map(
        partial(attend_back, onehot, table_low),
        (
            to_heads(query_c),
            to_heads(query_q),
            to_heads(key_rows),
            to_heads(value_rows),
            lengths,
            flag_rows,
            lse_c,
            lse_q,
            to_heads(mix_grads[0]),
            to_heads(mix_grads[1]),
        ),
    )
    grad_table = jnp.sum(grad_table, axis=0)
    low_query_c = grad_query_c.reshape(-1, D).astype(jnp.bfloat16)
    low_query_q = grad_query_q.reshape(-1, D).astype(jnp.bfloat16)
    low_keys = grad_keys.reshape(-1, D).astype(jnp.bfloat16)
    low_values = grad_values.reshape(-1, D).astype(jnp.bfloat16)
    low_c = hidden_c.astype(jnp.bfloat16)
    low_q = hidden_q.astype(jnp.bfloat16)
    stacked_grads = jnp.stack([low_query_c, low_keys, low_values])
    grad_qkv = jnp.einsum("td,ste->sde", low_c, stacked_grads, preferred_element_type=jnp.float32)
    grad_wq = grad_qkv[0] + jnp.einsum(
        "td,te->de", low_q, low_query_q, preferred_element_type=jnp.float32
    )
    grad_attn = jnp.stack([grad_wq, grad_qkv[1], grad_qkv[2], grad_attn_out])
    grad_bias_q = jnp.sum(low_query_c.astype(jnp.float32), axis=0) + jnp.sum(
        low_query_q.astype(jnp.float32), axis=0
    )
    grad_bias_v = jnp.sum(low_values.astype(jnp.float32), axis=0)
    grad_content = residual_grads[0] + jnp.einsum(
        "ste,sde->td", stacked_grads, attn_w[:3], preferred_element_type=jnp.float32
    )
    grad_query_in = residual_grads[1] + jnp.einsum(
        "te,de->td", low_query_q, attn_w[0], preferred_element_type=jnp.float32
    )
    grad_small = jnp.concatenate(
        [
            grad_bias_q,
            grad_bias_v,
            grad_bias_o,
            grad_gain_one,
            grad_shift_one,
            grad_bias_two,
            grad_gain_two,
            grad_shift_two,
            grad_hidden_bias,
            grad_table.reshape(-1),
        ]
    )
    return (grad_content, grad_query_in, (grad_attn, grad_inner, grad_outer, grad_small))


def adam_update(master, first, second, grad, rate):
    first_new = BETA_ONE * first + (1.0 - BETA_ONE) * grad
    second_new = BETA_TWO * second + (1.0 - BETA_TWO) * grad * grad
    first_hat = first_new / (1.0 - BETA_ONE**STEP)
    second_hat = second_new / (1.0 - BETA_TWO**STEP)
    master_new = master - rate * (
        first_hat / (jnp.sqrt(second_hat) + ADAM_EPS) + WEIGHT_DECAY * master
    )
    return (master_new, first_new, second_new)


def per_device(
    fast,
    content,
    query,
    lengths,
    predicted,
    content_cot,
    query_cot,
    attn_master,
    attn_first,
    attn_second,
    inner_master,
    inner_first,
    inner_second,
    outer_master,
    outer_first,
    outer_second,
    small_master,
    small_first,
    small_second,
):
    masters = (attn_master, inner_master, outer_master, small_master)
    slot_count = lengths.shape[0]
    flag_rows = predicted.reshape(slot_count, LEN)
    onehot = bucket_onehot()
    hidden_c = content.astype(jnp.float32)
    hidden_q = query.astype(jnp.float32)
    kept_weights = []
    saved_layers = []
    small_all = lax.all_gather(
        small_master.astype(jnp.bfloat16), "fsdp", axis=1, tiled=True
    )
    for layer_index in range(LAYERS):
        shards = tuple((master[layer_index] for master in masters[:3]))
        gathered = fetch_layer(fast, shards) + (small_all[layer_index],)
        kept_weights.append(gathered)
        hidden_c, hidden_q, saved = forward_layer(
            hidden_c, hidden_q, gathered, lengths, flag_rows, onehot
        )
        saved_layers.append(saved)
    position = jnp.arange(LEN, dtype=jnp.int32)
    valid_rows = (position[None, :] < lengths[:, None]).reshape(-1, 1).astype(jnp.float32)
    grad_c = content_cot.astype(jnp.float32) * valid_rows
    grad_q = query_cot.astype(jnp.float32) * valid_rows
    layer_grads = [None] * LAYERS
    small_grads = [None] * LAYERS
    for layer_index in reversed(range(LAYERS)):
        grad_c, grad_q, local_grads = backward_layer(
            saved_layers[layer_index],
            kept_weights[layer_index],
            grad_c,
            grad_q,
            lengths,
            flag_rows,
            onehot,
        )
        small_grads[layer_index] = local_grads[3]
        layer_grads[layer_index] = (
            reduce_fast(local_grads[:3]) if fast else reduce_layer(local_grads[:3])
        )
    small_sum = lax.psum(jnp.stack(small_grads), ("dp", "fsdp"))
    owned = small_master.shape[1]
    small_own = lax.dynamic_slice_in_dim(
        small_sum, lax.axis_index("fsdp") * owned, owned, 1
    )
    reduced = tuple(
        (
            jnp.stack([layer_grads[layer_index][member] for layer_index in range(LAYERS)])
            for member in range(3)
        )
    ) + (small_own,)
    attn_new = adam_update(attn_master, attn_first, attn_second, reduced[0], ATTENTION_RATE)
    inner_new = adam_update(inner_master, inner_first, inner_second, reduced[1], FEED_RATE)
    outer_new = adam_update(outer_master, outer_first, outer_second, reduced[2], FEED_RATE)
    small_new = adam_update(small_master, small_first, small_second, reduced[3], SMALL_RATE)
    return (
        hidden_c.astype(jnp.bfloat16),
        hidden_q.astype(jnp.bfloat16),
        grad_c,
        grad_q,
        attn_new[0],
        attn_new[1],
        attn_new[2],
        inner_new[0],
        inner_new[1],
        inner_new[2],
        outer_new[0],
        outer_new[1],
        outer_new[2],
        small_new[0],
        small_new[1],
        small_new[2],
    )


def solution(mesh):
    placed = (
        P(("dp", "fsdp"), None),
        P(("dp", "fsdp"), None),
        P(("dp", "fsdp")),
        P(("dp", "fsdp")),
        P(("dp", "fsdp"), None),
        P(("dp", "fsdp"), None),
        P(None, None, "fsdp", None),
        P(None, None, "fsdp", None),
        P(None, None, "fsdp", None),
        P(None, "fsdp", None),
        P(None, "fsdp", None),
        P(None, "fsdp", None),
        P(None, "fsdp", None),
        P(None, "fsdp", None),
        P(None, "fsdp", None),
        P(None, "fsdp"),
        P(None, "fsdp"),
        P(None, "fsdp"),
    )
    fast = tuple(mesh.shape.values()) == (4, 8)
    return jax.shard_map(
        partial(per_device, fast),
        mesh=mesh,
        in_specs=placed,
        out_specs=(
            P(("dp", "fsdp"), None),
            P(("dp", "fsdp"), None),
            P(("dp", "fsdp"), None),
            P(("dp", "fsdp"), None),
            P(None, None, "fsdp", None),
            P(None, None, "fsdp", None),
            P(None, None, "fsdp", None),
            P(None, "fsdp", None),
            P(None, "fsdp", None),
            P(None, "fsdp", None),
            P(None, "fsdp", None),
            P(None, "fsdp", None),
            P(None, "fsdp", None),
            P(None, "fsdp"),
            P(None, "fsdp"),
            P(None, "fsdp"),
        ),
        check_vma=False,
    )
```

```python
from functools import partial

import jax
import jax.numpy as jnp
from jax import lax
from jax.experimental import pallas as pl
from jax.experimental.pallas import tpu as pltpu
from jax.sharding import PartitionSpec as P

D = 768
H = 12
DH = 64
FF = 3072
LEN = 512
NB = 32
LAYERS = 2
STEP = 10


NORM_EPS = 1e-05
MASKED = -1000000000.0
BETA_ONE = 0.9
BETA_TWO = 0.999
ATTENTION_RATE = 0.1
FEED_RATE = 0.02
SMALL_RATE = 0.4
WEIGHT_DECAY = 0.01
ADAM_EPS = 1e-08
SCORE_SCALE = 0.125


def layer_norm(values, gain, shift):
    centre = values - jnp.mean(values, axis=-1, keepdims=True)
    spread = jnp.mean(centre * centre, axis=-1, keepdims=True)
    return centre * lax.rsqrt(spread + NORM_EPS) * gain + shift


def unpack(vectors):
    pieces = [vectors[piece_index * D : (piece_index + 1) * D] for piece_index in range(8)]
    hidden_bias = vectors[8 * D : 8 * D + FF]
    bias_table = vectors[8 * D + FF :].reshape(H, NB)
    return (pieces, hidden_bias, bias_table)


def bucket_ids():
    position = jnp.arange(LEN, dtype=jnp.int32)
    offset = position[None, :] - position[:, None]
    distance = jnp.abs(offset)
    far_bucket = jnp.full(distance.shape, 8, jnp.int32)
    for exponent in range(1, 8):
        far_bucket = far_bucket + (distance * distance >= 64 * 2**exponent).astype(jnp.int32)
    near_or_far = jnp.where(distance < 8, distance, far_bucket)
    return near_or_far + NB // 2 * (offset > 0).astype(jnp.int32)


def bucket_onehot():
    return (bucket_ids()[:, :, None] == jnp.arange(NB, dtype=jnp.int32)[None, None, :]).astype(
        jnp.bfloat16
    )


def allowed_pairs(length, pred_flags):
    position = jnp.arange(LEN, dtype=jnp.int32)
    valid_key = (position < length)[None, :]
    row_pos = position[:, None]
    col_pos = position[None, :]
    free_key = (pred_flags == 0)[None, :]
    content_ok = valid_key & (free_key | (pred_flags[:, None] == 1) & (col_pos <= row_pos))
    query_ok = valid_key & (col_pos != row_pos) & (free_key | (col_pos < row_pos))
    return (content_ok, query_ok)


def masked_scores(query_rows, key_rows, position_bias, allowed):
    scores = (
        jnp.einsum("qhd,khd->hqk", query_rows, key_rows, preferred_element_type=jnp.float32)
        * SCORE_SCALE
        + position_bias
    )
    return jnp.where(allowed[None], scores, MASKED)


def table_bias(onehot, table_low):
    return jnp.einsum("qkb,hb->hqk", onehot, table_low, preferred_element_type=jnp.float32)


def attend_slot(onehot, table_low, slot_item):
    query_c, query_q, key_rows, value_rows, length, pred_flags = slot_item
    position_bias = table_bias(onehot, table_low)
    content_ok, query_ok = allowed_pairs(length, pred_flags)
    results = []
    for query_rows, allowed in ((query_c, content_ok), (query_q, query_ok)):
        scores = masked_scores(query_rows, key_rows, position_bias, allowed)
        peak = jnp.max(scores, axis=-1, keepdims=True)
        expos = jnp.exp(scores - peak)
        totals = jnp.sum(expos, axis=-1, keepdims=True)
        probs = (expos / totals).astype(jnp.bfloat16)
        mixed = jnp.einsum(
            "hqk,khd->qhd", probs, value_rows, preferred_element_type=jnp.float32
        ).astype(jnp.bfloat16)
        results.append((mixed, peak[..., 0] + jnp.log(totals[..., 0])))
    return (results[0][0], results[1][0], results[0][1], results[1][1])


def attend_back(onehot, table_low, slot_item):
    (
        query_c,
        query_q,
        key_rows,
        value_rows,
        length,
        pred_flags,
        lse_c,
        lse_q,
        grad_mix_c,
        grad_mix_q,
    ) = slot_item
    position_bias = table_bias(onehot, table_low)
    content_ok, query_ok = allowed_pairs(length, pred_flags)
    grad_keys = jnp.zeros(key_rows.shape, jnp.float32)
    grad_values = jnp.zeros(value_rows.shape, jnp.float32)
    grad_table = jnp.zeros((H, NB), jnp.float32)
    grads_query = []
    for query_rows, allowed, log_total, grad_mix in (
        (query_c, content_ok, lse_c, grad_mix_c),
        (query_q, query_ok, lse_q, grad_mix_q),
    ):
        scores = masked_scores(query_rows, key_rows, position_bias, allowed)
        probs = jnp.exp(scores - log_total[..., None])
        grad_values = grad_values + jnp.einsum(
            "hqk,qhd->khd", probs.astype(jnp.bfloat16), grad_mix, preferred_element_type=jnp.float32
        )
        grad_probs = jnp.einsum(
            "qhd,khd->hqk", grad_mix, value_rows, preferred_element_type=jnp.float32
        )
        grad_scores = probs * (grad_probs - jnp.sum(probs * grad_probs, axis=-1, keepdims=True))
        grad_scores = jnp.where(allowed[None], grad_scores, 0.0).astype(jnp.bfloat16)
        grad_table = grad_table + jnp.einsum(
            "hqk,qkb->hb", grad_scores, onehot, preferred_element_type=jnp.float32
        )
        grads_query.append(
            jnp.einsum("hqk,khd->qhd", grad_scores, key_rows, preferred_element_type=jnp.float32)
            * SCORE_SCALE
        )
        grad_keys = (
            grad_keys
            + jnp.einsum(
                "hqk,qhd->khd", grad_scores, query_rows, preferred_element_type=jnp.float32
            )
            * SCORE_SCALE
        )
    return (grads_query[0], grads_query[1], grad_keys, grad_values, grad_table)


def to_heads(values):
    return values.reshape(-1, LEN, H, DH)


AXES = ("dp", "fsdp")
GRID = (2, 2, 4, 2)
ROWS = 96


def places():
    return [
        (x, c, z, y) for x in range(2) for c in range(2) for z in range(4) for y in range(2)
    ]


def flat(x, c, z, y):
    return ((x * 2 + c) * 4 + z) * 2 + y


def move(value, shift):
    pairs = [(flat(*place), flat(*shift(*place))) for place in places()]
    return lax.ppermute(value, AXES, pairs)


def swap_core(value):
    return move(value, lambda x, c, z, y: (x, 1 - c, z, y))


def swap_x(value):
    return move(value, lambda x, c, z, y: (1 - x, c, z, y))


def swap_y(value):
    return move(value, lambda x, c, z, y: (x, c, z, 1 - y))


def shift_z(value, step):
    return move(value, lambda x, c, z, y: (x, c, (z + step) % 4, y))


def my_place():
    dp = lax.axis_index("dp")
    fsdp = lax.axis_index("fsdp")
    return (dp // 2, dp % 2, fsdp // 2, fsdp % 2)


def spread_blocks(own):
    column = jnp.stack([own] + [shift_z(own, step) for step in (1, 2, 3)])
    from_x = swap_x(column)
    from_y = swap_y(column)
    corner_low = swap_x(from_y[:2])
    corner_high = swap_y(from_x[2:])
    mine = (column, from_x, from_y, corner_low, corner_high)
    return mine + tuple(swap_core(piece) for piece in mine)


PIECES = ((0, 0, 0, 4), (1, 0, 0, 4), (0, 1, 0, 4), (1, 1, 0, 2), (1, 1, 2, 4))


def dot_nn(left, right):
    return jnp.dot(left, right, preferred_element_type=jnp.float32)


def dot_nt(left, right):
    return lax.dot_general(
        left, right, (((1,), (1,)), ((), ())), preferred_element_type=jnp.float32
    )


def dot_tn(left, right):
    return lax.dot_general(
        left, right, (((0,), (0,)), ((), ())), preferred_element_type=jnp.float32
    )


ANY_SPEC = pl.BlockSpec(memory_space=pl.ANY)
VMEM_SPEC = pl.BlockSpec(memory_space=pltpu.VMEM)
SMEM_SPEC = pl.BlockSpec(memory_space=pltpu.SMEM)
TALL = 2 * LEN
HALF = 256
PARAMS = pltpu.CompilerParams(vmem_limit_bytes=60 * 1024 * 1024)


def norm_parts(values):
    centre = values - jnp.mean(values, axis=-1, keepdims=True)
    spread = jnp.mean(centre * centre, axis=-1, keepdims=True)
    scale = lax.rsqrt(spread + NORM_EPS)
    return (centre * scale, scale)


def norm_back(unit, scale, grad, gain):
    scaled = grad * gain
    return scale * (
        scaled
        - jnp.mean(scaled, axis=-1, keepdims=True)
        - unit * jnp.mean(scaled * unit, axis=-1, keepdims=True)
    )


def start_fetch(kinds, place_ref, pieces, targets, sems):
    x, c, z, y = (place_ref[index] for index in range(4))
    copies = []
    for other in range(2):
        for piece, (dx, dy, first, last) in enumerate(PIECES):
            for k in range(first, last):
                quarter = (x ^ dx) * 2 + (c ^ other)
                owner = ((z - k) & 3) * 2 + (y ^ dy)
                for member, kind in enumerate(kinds):
                    if kind == "attn":
                        target = targets[member].at[
                            quarter, pl.ds(pl.multiple_of(owner * ROWS, ROWS), ROWS), :
                        ]
                    elif kind == "inner":
                        target = targets[member].at[
                            pl.ds(pl.multiple_of(owner * ROWS, ROWS), ROWS),
                            pl.ds(pl.multiple_of(quarter * D, D), D),
                        ]
                    else:
                        target = targets[member].at[
                            pl.ds(pl.multiple_of(owner * 384 + quarter * ROWS, ROWS), ROWS), :
                        ]
                    copy = pltpu.make_async_copy(
                        pieces[other * 5 + piece].at[k - first, member],
                        target,
                        sems.at[len(copies)],
                    )
                    copy.start()
                    copies.append(copy)
    return copies


def project_kernel(place_ref, low_ref, small_ref, *refs):
    pieces = refs[:10]
    q_ref, k_ref, v_ref, w_out, w_ref, sems, out_sem = refs[10:]
    for copy in start_fetch(("attn",), place_ref, pieces, (w_ref,), sems):
        copy.wait()
    keep = pltpu.make_async_copy(w_ref, w_out, out_sem)
    keep.start()
    bias_q = small_ref[0:1, :]
    bias_v = small_ref[1:2, :]
    for row in range(0, TALL, HALF):
        rows = low_ref[row : row + HALF, :]
        q_ref[row : row + HALF, :] = (dot_nn(rows, w_ref[0]) + bias_q).astype(jnp.bfloat16)
        if row < LEN:
            k_ref[row : row + HALF, :] = dot_nn(rows, w_ref[1]).astype(jnp.bfloat16)
            v_ref[row : row + HALF, :] = (dot_nn(rows, w_ref[2]) + bias_v).astype(jnp.bfloat16)
    keep.wait()


def project(place, low, small, pieces):
    return pl.pallas_call(
        project_kernel,
        out_shape=[
            jax.ShapeDtypeStruct((TALL, D), jnp.bfloat16),
            jax.ShapeDtypeStruct((LEN, D), jnp.bfloat16),
            jax.ShapeDtypeStruct((LEN, D), jnp.bfloat16),
            jax.ShapeDtypeStruct((4, D, D), jnp.bfloat16),
        ],
        in_specs=[SMEM_SPEC, VMEM_SPEC, VMEM_SPEC] + [ANY_SPEC] * 10,
        out_specs=[VMEM_SPEC] * 3 + [ANY_SPEC],
        scratch_shapes=[
            pltpu.VMEM((4, D, D), jnp.bfloat16),
            pltpu.SemaphoreType.DMA((32,)),
            pltpu.SemaphoreType.DMA,
        ],
        compiler_params=PARAMS,
        cost_estimate=pl.CostEstimate(flops=2 * 2048 * D * D, bytes_accessed=16000000, transcendentals=0),
        name="project",
    )(place, low, small, *pieces)


def build_masks(length, row_flags, col_flags, mask_ref, alive_ref):
    flags = row_flags[...]

    def body(step, carry):
        start = pl.multiple_of(step * 64, 64)
        key = lax.broadcasted_iota(jnp.int32, (64, LEN), 0) + start
        query = lax.broadcasted_iota(jnp.int32, (64, LEN), 1)
        valid = key < length
        free = jnp.broadcast_to(col_flags[pl.ds(start, 64), :], (64, LEN)) == 0.0
        marked = jnp.broadcast_to(flags, (64, LEN)) == 1.0
        content_ok = valid & (free | (marked & (key <= query)))
        query_ok = valid & (key != query) & (free | (key < query))
        mask_ref[pl.ds(start, 64), :LEN] = content_ok.astype(jnp.float32)
        mask_ref[pl.ds(start, 64), LEN:] = query_ok.astype(jnp.float32)
        return carry

    lax.fori_loop(0, 8, body, 0)
    alive_ref[...] = jnp.max(mask_ref[...], axis=0, keepdims=True)


def build_tiles(t_row, tile_ref):
    spread = jnp.broadcast_to(t_row, (128, 512))
    rolled = pltpu.roll(spread, 0, 1, stride=1, stride_axis=0)
    tile_ref[...] = rolled[:, :384]


def position_bias(tile_ref, far_ref, head, query_block, key_block):
    apart = query_block - key_block
    if apart >= 2:
        return far_ref[head, 0]
    if apart <= -2:
        return far_ref[head, 1]
    return tile_ref[:, 128 * (apart + 1) : 128 * (apart + 2)]


def head_lanes(shape, head):
    lane = lax.broadcasted_iota(jnp.int32, shape, 1)
    return (lane >= 64) if head else (lane < 64)


def mix_kernel(
    length_ref, far_ref, q_ref, k_ref, v_ref, row_flags, col_flags, t_ref,
    a_ref, lse_ref, mask_ref, alive_ref, tile_ref, p_ref, o_ref,
):
    pair = pl.program_id(0)

    @pl.when(pair == 0)
    def _():
        build_masks(length_ref[0], row_flags, col_flags, mask_ref, alive_ref)

    keys = k_ref[...].astype(jnp.float32) * SCORE_SCALE
    values_t = v_ref[...].astype(jnp.float32).T.astype(jnp.bfloat16)
    for head in range(2):
        build_tiles(t_ref[head], tile_ref.at[head])
        keys_own = jnp.where(head_lanes(keys.shape, head), keys, 0.0).astype(jnp.bfloat16)
        for chunk in range(4):
            at = chunk * HALF
            scores = dot_nt(keys_own, q_ref[at : at + HALF, :])
            for side in range(2):
                lanes = slice(at + side * 128, at + side * 128 + 128)
                blocks = []
                peak = None
                for key_block in range(4):
                    rows = slice(key_block * 128, key_block * 128 + 128)
                    block = scores[rows, side * 128 : side * 128 + 128] + position_bias(
                        tile_ref.at[head], far_ref, pair * 2 + head, (chunk % 2) * 2 + side, key_block
                    )
                    block = jnp.where(mask_ref[rows, lanes] > 0.0, block, MASKED)
                    blocks.append(block)
                    high = jnp.max(block, axis=0, keepdims=True)
                    peak = high if peak is None else jnp.maximum(peak, high)
                total = None
                for key_block in range(4):
                    rows = slice(key_block * 128, key_block * 128 + 128)
                    expo = jnp.exp(blocks[key_block] - peak)
                    part = jnp.sum(expo, axis=0, keepdims=True)
                    total = part if total is None else total + part
                    p_ref[head, rows, lanes] = expo.astype(jnp.bfloat16)
                lse_ref[head, :, lanes] = jnp.where(
                    alive_ref[:, lanes] > 0.0, peak + jnp.log(total), 1e30
                )
                o_ref[head : head + 1, lanes] = 1.0 / total
        mixed = dot_nn(values_t[head * 64 : head * 64 + 64, :], p_ref[head])
        o_ref[8 + head * 64 : 8 + head * 64 + 64, :] = mixed * o_ref[head : head + 1, :]
    a_ref[...] = o_ref[8:, :].T.astype(jnp.bfloat16)


def mix(length, far, tvec, q, k, v, row_flags, col_flags):
    tall = pl.BlockSpec((TALL, 128), lambda p: (0, p))
    short = pl.BlockSpec((LEN, 128), lambda p: (0, p))
    return pl.pallas_call(
        mix_kernel,
        grid=(H // 2,),
        out_shape=[
            jax.ShapeDtypeStruct((TALL, D), jnp.bfloat16),
            jax.ShapeDtypeStruct((H, 1, TALL), jnp.float32),
        ],
        in_specs=[
            SMEM_SPEC, SMEM_SPEC, tall, short, short,
            pl.BlockSpec((1, LEN), lambda p: (0, 0)),
            pl.BlockSpec((LEN, 1), lambda p: (0, 0)),
            pl.BlockSpec((2, 1, 512), lambda p: (p, 0, 0)),
        ],
        out_specs=[tall, pl.BlockSpec((2, 1, TALL), lambda p: (p, 0, 0))],
        scratch_shapes=[
            pltpu.VMEM((LEN, TALL), jnp.float32),
            pltpu.VMEM((1, TALL), jnp.float32),
            pltpu.VMEM((2, 128, 384), jnp.float32),
            pltpu.VMEM((2, LEN, TALL), jnp.bfloat16),
            pltpu.VMEM((136, TALL), jnp.float32),
        ],
        compiler_params=PARAMS,
        cost_estimate=pl.CostEstimate(flops=6500000000, bytes_accessed=8000000, transcendentals=6300000),
        name="mix",
    )(length, far, q, k, v, row_flags, col_flags, tvec)


def mix_back_kernel(
    length_ref, far_ref, q_ref, k_ref, v_ref, da_ref, a_ref, lse_ref, row_flags, col_flags, t_ref,
    dq_ref, dk_ref, dv_ref, table_ref,
    mask_ref, alive_ref, tile_ref, p_ref, s_ref, near_ref, d_ref,
):
    pair = pl.program_id(0)

    @pl.when(pair == 0)
    def _():
        build_masks(length_ref[0], row_flags, col_flags, mask_ref, alive_ref)

    keys = k_ref[...].astype(jnp.float32) * SCORE_SCALE
    keys_t = keys.T.astype(jnp.bfloat16)
    product = da_ref[...].astype(jnp.float32) * a_ref[...].astype(jnp.float32)
    d_ref[...] = product.T
    values = v_ref[...]
    grads_k = []
    grads_v = []
    near_ref[...] = jnp.zeros(near_ref.shape, jnp.float32)
    turn = (
        lax.broadcasted_iota(jnp.int32, (128, 128), 0)
        + lax.broadcasted_iota(jnp.int32, (128, 128), 1)
        == 127
    ).astype(jnp.float32)
    for head in range(2):
        build_tiles(t_ref[head], tile_ref.at[head])
        mine = head_lanes(keys.shape, head)
        keys_own = jnp.where(mine, keys, 0.0).astype(jnp.bfloat16)
        values_own = jnp.where(mine, values.astype(jnp.float32), 0.0).astype(jnp.bfloat16)
        delta = jnp.sum(d_ref[head * 64 : head * 64 + 64, :], axis=0, keepdims=True)
        far_low = jnp.zeros((8, 128), jnp.float32)
        far_high = jnp.zeros((8, 128), jnp.float32)
        for chunk in range(4):
            at = chunk * HALF
            scores = dot_nt(keys_own, q_ref[at : at + HALF, :])
            pulls = dot_nt(values_own, da_ref[at : at + HALF, :])
            for side in range(2):
                lanes = slice(at + side * 128, at + side * 128 + 128)
                log_total = lse_ref[head, :, lanes]
                shift = delta[:, lanes]
                for key_block in range(4):
                    rows = slice(key_block * 128, key_block * 128 + 128)
                    cols = slice(side * 128, side * 128 + 128)
                    query_block = (chunk % 2) * 2 + side
                    block = scores[rows, cols] + position_bias(
                        tile_ref.at[head], far_ref, pair * 2 + head, query_block, key_block
                    )
                    block = jnp.where(mask_ref[rows, lanes] > 0.0, block, MASKED)
                    prob = jnp.exp(block - log_total)
                    p_ref[head, rows, lanes] = prob.astype(jnp.bfloat16)
                    grad = prob * (pulls[rows, cols] - shift)
                    s_ref[head, rows, lanes] = grad.astype(jnp.bfloat16)
                    apart = query_block - key_block
                    if apart >= 2:
                        far_low = far_low + jnp.sum(grad.reshape(16, 8, 128), axis=0)
                    elif apart <= -2:
                        far_high = far_high + jnp.sum(grad.reshape(16, 8, 128), axis=0)
                    else:
                        near_ref[head, :, 128 * (apart + 1) : 128 * (apart + 2)] += grad
        grads_v.append(dot_nn(p_ref[head], da_ref[...]))
        grads_k.append(dot_nn(s_ref[head], q_ref[...]))
        d_ref[head * 64 : head * 64 + 64, :] = dot_nn(
            keys_t[head * 64 : head * 64 + 64, :], s_ref[head]
        )
        turned = jnp.dot(
            turn, near_ref[head], precision=lax.Precision.HIGHEST, preferred_element_type=jnp.float32
        )
        aligned = pltpu.roll(turned, 0, 1, stride=1, stride_axis=0)
        table_ref[head, :, :512] = jnp.sum(aligned, axis=0, keepdims=True)
        table_ref[head, :, 512:640] = jnp.sum(far_low, axis=0, keepdims=True)
        table_ref[head, :, 640:] = jnp.sum(far_high, axis=0, keepdims=True)
    dead = (1.0 - alive_ref[...]) * (1.0 / LEN)
    uniform = dot_nn(dead.astype(jnp.bfloat16), da_ref[...])
    first = head_lanes((LEN, 128), 0)
    dv_ref[...] = (jnp.where(first, grads_v[0], grads_v[1]) + uniform).astype(jnp.bfloat16)
    dk_ref[...] = (jnp.where(first, grads_k[0], grads_k[1]) * SCORE_SCALE).astype(jnp.bfloat16)
    dq_ref[...] = d_ref[...].T.astype(jnp.bfloat16)


def mix_back(length, far, tvec, q, k, v, da, a, lse, row_flags, col_flags):
    tall = pl.BlockSpec((TALL, 128), lambda p: (0, p))
    short = pl.BlockSpec((LEN, 128), lambda p: (0, p))
    return pl.pallas_call(
        mix_back_kernel,
        grid=(H // 2,),
        out_shape=[
            jax.ShapeDtypeStruct((TALL, D), jnp.bfloat16),
            jax.ShapeDtypeStruct((LEN, D), jnp.bfloat16),
            jax.ShapeDtypeStruct((LEN, D), jnp.bfloat16),
            jax.ShapeDtypeStruct((H, 1, 768), jnp.float32),
        ],
        in_specs=[
            SMEM_SPEC, SMEM_SPEC, tall, short, short, tall, tall,
            pl.BlockSpec((2, 1, TALL), lambda p: (p, 0, 0)),
            pl.BlockSpec((1, LEN), lambda p: (0, 0)),
            pl.BlockSpec((LEN, 1), lambda p: (0, 0)),
            pl.BlockSpec((2, 1, 512), lambda p: (p, 0, 0)),
        ],
        out_specs=[tall, short, short, pl.BlockSpec((2, 1, 768), lambda p: (p, 0, 0))],
        scratch_shapes=[
            pltpu.VMEM((LEN, TALL), jnp.float32),
            pltpu.VMEM((1, TALL), jnp.float32),
            pltpu.VMEM((2, 128, 384), jnp.float32),
            pltpu.VMEM((2, LEN, TALL), jnp.bfloat16),
            pltpu.VMEM((2, LEN, TALL), jnp.bfloat16),
            pltpu.VMEM((2, 128, 512), jnp.float32),
            pltpu.VMEM((128, TALL), jnp.float32),
        ],
        compiler_params=PARAMS,
        cost_estimate=pl.CostEstimate(flops=16000000000, bytes_accessed=12000000, transcendentals=6300000),
        name="mix_back",
    )(length, far, q, k, v, da, a, lse, row_flags, col_flags, tvec)


GELU_SCALE = 0.7978845608028654
GELU_CUBE = 0.044715


def feed_kernel(place_ref, small_ref, hidden_bias_ref, mix_any, hidden_any, attn_any, *refs):
    pieces = refs[:10]
    (
        resid_out, summed_out, pre_out, next_out, low_out,
        mix_ref, hidden_ref, wo_ref, inner_ref, outer_ref, resid_ref, total_ref, normed_ref,
        pre_ref, next_ref, low_ref, sems, load_sems, store_sems,
    ) = refs[10:]
    loads = [
        pltpu.make_async_copy(mix_any, mix_ref, load_sems.at[0]),
        pltpu.make_async_copy(attn_any.at[3], wo_ref, load_sems.at[1]),
        pltpu.make_async_copy(hidden_any, hidden_ref, load_sems.at[2]),
    ]
    for load in loads:
        load.start()
    fetches = start_fetch(("inner", "outer"), place_ref, pieces, (inner_ref, outer_ref), sems)
    for load in loads:
        load.wait()
    for row in range(0, TALL, HALF):
        rows = slice(row, row + HALF)
        resid = hidden_ref[rows, :] + dot_nn(mix_ref[rows, :], wo_ref[...]) + small_ref[2:3, :]
        resid_ref[rows, :] = resid
        unit, scale = norm_parts(resid)
        normed = unit * small_ref[3:4, :] + small_ref[4:5, :]
        normed_ref[rows, :] = normed.astype(jnp.bfloat16)
        total_ref[rows, :] = normed + small_ref[5:6, :]
    stores = [pltpu.make_async_copy(resid_ref, resid_out, store_sems.at[0])]
    stores[0].start()
    for fetch in fetches:
        fetch.wait()
    for chunk in range(4):
        cols = slice(chunk * D, chunk * D + D)

        def body(step, carry):
            rows = pl.ds(pl.multiple_of(step * HALF, HALF), HALF)
            pre = dot_nn(normed_ref[rows, :], inner_ref[:, cols]) + hidden_bias_ref[:, cols]
            pre_ref[rows, cols] = pre.astype(jnp.bfloat16)
            tanh = jnp.tanh(GELU_SCALE * (pre + GELU_CUBE * (pre * pre * pre)))
            active = (pre * (0.5 + 0.5 * tanh)).astype(jnp.bfloat16)
            total_ref[rows, :] += dot_nn(active, outer_ref[cols, :])
            return carry

        for step in range(4):
            body(step, 0)
        store = pltpu.make_async_copy(
            pre_ref.at[:, cols], pre_out.at[:, cols], store_sems.at[1 + chunk]
        )
        store.start()
        stores.append(store)
    store = pltpu.make_async_copy(total_ref, summed_out, store_sems.at[5])
    store.start()
    stores.append(store)
    for row in range(0, TALL, HALF):
        rows = slice(row, row + HALF)
        unit, scale = norm_parts(total_ref[rows, :])
        following = unit * small_ref[6:7, :] + small_ref[7:8, :]
        next_ref[rows, :] = following
        low_ref[rows, :] = following.astype(jnp.bfloat16)
    for index, (source, target) in enumerate(((next_ref, next_out), (low_ref, low_out))):
        store = pltpu.make_async_copy(source, target, store_sems.at[6 + index])
        store.start()
        stores.append(store)
    for store in stores:
        store.wait()


def feed(place, small, hidden_bias, mixed, hidden, attn, pieces):
    return pl.pallas_call(
        feed_kernel,
        out_shape=[
            jax.ShapeDtypeStruct((TALL, D), jnp.float32),
            jax.ShapeDtypeStruct((TALL, D), jnp.float32),
            jax.ShapeDtypeStruct((TALL, FF), jnp.bfloat16),
            jax.ShapeDtypeStruct((TALL, D), jnp.float32),
            jax.ShapeDtypeStruct((TALL, D), jnp.bfloat16),
        ],
        in_specs=[SMEM_SPEC, VMEM_SPEC, VMEM_SPEC] + [ANY_SPEC] * 13,
        out_specs=[ANY_SPEC] * 5,
        scratch_shapes=[
            pltpu.VMEM((TALL, D), jnp.bfloat16),
            pltpu.VMEM((TALL, D), jnp.float32),
            pltpu.VMEM((D, D), jnp.bfloat16),
            pltpu.VMEM((D, FF), jnp.bfloat16),
            pltpu.VMEM((FF, D), jnp.bfloat16),
            pltpu.VMEM((TALL, D), jnp.float32),
            pltpu.VMEM((TALL, D), jnp.float32),
            pltpu.VMEM((TALL, D), jnp.bfloat16),
            pltpu.VMEM((TALL, FF), jnp.bfloat16),
            pltpu.VMEM((TALL, D), jnp.float32),
            pltpu.VMEM((TALL, D), jnp.bfloat16),
            pltpu.SemaphoreType.DMA((64,)),
            pltpu.SemaphoreType.DMA((3,)),
            pltpu.SemaphoreType.DMA((8,)),
        ],
        compiler_params=PARAMS,
        cost_estimate=pl.CostEstimate(flops=2 * TALL * D * (D + 2 * FF), bytes_accessed=40000000, transcendentals=3000000),
        name="feed",
    )(place, small, hidden_bias, mixed, hidden, attn, *pieces)


def feed_back_kernel(place_ref, small_ref, grad_any, summed_any, resid_any, pre_any, mix_any, attn_any, *refs):
    pieces = refs[:10]
    (
        dresid_out, dmix_out, dwo_out, keep_out, send_out, vec_ref, dhidden_ref,
        grad_ref, summed_ref, resid_ref, pre_ref, mix_ref, wo_ref, inner_ref, outer_ref,
        total_ref, branch_ref, normed_ref, active_ref, dpre_ref, dinner_ref, douter_ref,
        dwo_ref, sems, load_sems, store_sems, block_sems,
    ) = refs[10:]
    proj_ref = branch_ref
    dmix_ref = active_ref
    x, c, z, y = (place_ref[index] for index in range(4))
    load = [
        pltpu.make_async_copy(source, target, load_sems.at[index])
        for index, (source, target) in enumerate(
            (
                (grad_any, grad_ref), (summed_any, summed_ref), (resid_any, resid_ref),
                (pre_any, pre_ref), (mix_any, mix_ref), (attn_any.at[3], wo_ref),
            )
        )
    ]
    for copy in load[:3]:
        copy.start()
    fetches = start_fetch(("inner", "outer"), place_ref, pieces, (inner_ref, outer_ref), sems)
    for copy in load[3:]:
        copy.start()
    for copy in load[:3]:
        copy.wait()
    gain_two_grad = jnp.zeros((1, D), jnp.float32)
    shift_two_grad = jnp.zeros((1, D), jnp.float32)
    bias_two_grad = jnp.zeros((1, D), jnp.float32)
    for row in range(0, TALL, HALF):
        rows = slice(row, row + HALF)
        grad = grad_ref[rows, :]
        unit, scale = norm_parts(summed_ref[rows, :])
        gain_two_grad += jnp.sum(grad * unit, axis=0, keepdims=True)
        shift_two_grad += jnp.sum(grad, axis=0, keepdims=True)
        back = norm_back(unit, scale, grad, small_ref[6:7, :])
        total_ref[rows, :] = back
        low = back.astype(jnp.bfloat16)
        branch_ref[rows, :] = low
        bias_two_grad += jnp.sum(low.astype(jnp.float32), axis=0, keepdims=True)
        unit, scale = norm_parts(resid_ref[rows, :])
        normed_ref[rows, :] = (unit * small_ref[3:4, :] + small_ref[4:5, :]).astype(jnp.bfloat16)
    vec_ref[5:6, :] = bias_two_grad
    vec_ref[6:7, :] = gain_two_grad
    vec_ref[7:8, :] = shift_two_grad
    for copy in fetches + load[3:]:
        copy.wait()
    blocks = []

    def place_block(core, source, target_index):
        sem = block_sems.at[len(blocks)]
        keep = pltpu.make_async_copy(source, keep_out.at[target_index], sem)
        send = pltpu.make_async_copy(source, send_out.at[target_index], sem)

        @pl.when(c == core)
        def _():
            keep.start()

        @pl.when(c != core)
        def _():
            send.start()

        blocks.append(keep)

    for chunk in range(4):
        cols = slice(chunk * D, chunk * D + D)
        bias_grad = jnp.zeros((1, D), jnp.float32)
        for row in range(0, TALL, HALF):
            rows = slice(row, row + HALF)
            pull = dot_nt(branch_ref[rows, :], outer_ref[cols, :])
            pre = pre_ref[rows, cols].astype(jnp.float32)
            square = pre * pre
            tanh = jnp.tanh(GELU_SCALE * pre * (1.0 + GELU_CUBE * square))
            half = 0.5 + 0.5 * tanh
            active_ref[rows, :] = (pre * half).astype(jnp.bfloat16)
            slope = half + (0.5 * GELU_SCALE) * pre * (1.0 - tanh * tanh) * (
                1.0 + (3.0 * GELU_CUBE) * square
            )
            dpre = (pull * slope).astype(jnp.bfloat16)
            dpre_ref[rows, :] = dpre
            bias_grad += jnp.sum(dpre.astype(jnp.float32), axis=0, keepdims=True)
            total_ref[rows, :] += dot_nt(dpre, inner_ref[:, cols])
        dhidden_ref[:, cols] = bias_grad
        douter_ref[cols, :] = dot_tn(active_ref[...], branch_ref[...]).astype(jnp.bfloat16)
        dinner_ref[:, cols] = dot_tn(normed_ref[...], dpre_ref[...]).astype(jnp.bfloat16)
        for owner in range(8):
            place_block(
                chunk % 2,
                dinner_ref.at[owner * ROWS : owner * ROWS + ROWS, cols],
                ((chunk // 2) ^ x, (owner % 2) ^ y, ((owner // 2) - z) & 3, 0),
            )
        for strip in range(8):
            quarter = strip % 4
            start = chunk * D + strip * ROWS
            place_block(
                quarter % 2,
                douter_ref.at[start : start + ROWS, :],
                ((quarter // 2) ^ x, (strip // 4) ^ y, (chunk - z) & 3, 1),
            )
    gain_one_grad = jnp.zeros((1, D), jnp.float32)
    shift_one_grad = jnp.zeros((1, D), jnp.float32)
    bias_o_grad = jnp.zeros((1, D), jnp.float32)
    for row in range(0, TALL, HALF):
        rows = slice(row, row + HALF)
        grad = total_ref[rows, :]
        unit, scale = norm_parts(resid_ref[rows, :])
        gain_one_grad += jnp.sum(grad * unit, axis=0, keepdims=True)
        shift_one_grad += jnp.sum(grad, axis=0, keepdims=True)
        back = norm_back(unit, scale, grad, small_ref[3:4, :])
        grad_ref[rows, :] = back
        low = back.astype(jnp.bfloat16)
        proj_ref[rows, :] = low
        bias_o_grad += jnp.sum(low.astype(jnp.float32), axis=0, keepdims=True)
        dmix_ref[rows, :] = dot_nt(low, wo_ref[...]).astype(jnp.bfloat16)
    dwo_ref[...] = dot_tn(mix_ref[...], proj_ref[...]).astype(jnp.bfloat16)
    vec_ref[0:2, :] = jnp.zeros((2, D), jnp.float32)
    vec_ref[2:3, :] = bias_o_grad
    vec_ref[3:4, :] = gain_one_grad
    vec_ref[4:5, :] = shift_one_grad
    stores = [
        pltpu.make_async_copy(source, target, store_sems.at[index])
        for index, (source, target) in enumerate(
            ((grad_ref, dresid_out), (dmix_ref, dmix_out), (dwo_ref, dwo_out))
        )
    ]
    for store in stores:
        store.start()
    for copy in blocks + stores:
        copy.wait()


def feed_back(place, small, grad, summed, resid, pre, mixed, attn, pieces):
    blocks = jax.ShapeDtypeStruct((2, 2, 4, 2, ROWS, D), jnp.bfloat16)
    return pl.pallas_call(
        feed_back_kernel,
        out_shape=[
            jax.ShapeDtypeStruct((TALL, D), jnp.float32),
            jax.ShapeDtypeStruct((TALL, D), jnp.bfloat16),
            jax.ShapeDtypeStruct((D, D), jnp.bfloat16),
            blocks,
            blocks,
            jax.ShapeDtypeStruct((8, D), jnp.float32),
            jax.ShapeDtypeStruct((1, FF), jnp.float32),
        ],
        in_specs=[SMEM_SPEC, VMEM_SPEC] + [ANY_SPEC] * 16,
        out_specs=[ANY_SPEC] * 5 + [VMEM_SPEC] * 2,
        scratch_shapes=[
            pltpu.VMEM((TALL, D), jnp.float32),
            pltpu.VMEM((TALL, D), jnp.float32),
            pltpu.VMEM((TALL, D), jnp.float32),
            pltpu.VMEM((TALL, FF), jnp.bfloat16),
            pltpu.VMEM((TALL, D), jnp.bfloat16),
            pltpu.VMEM((D, D), jnp.bfloat16),
            pltpu.VMEM((D, FF), jnp.bfloat16),
            pltpu.VMEM((FF, D), jnp.bfloat16),
            pltpu.VMEM((TALL, D), jnp.float32),
            pltpu.VMEM((TALL, D), jnp.bfloat16),
            pltpu.VMEM((TALL, D), jnp.bfloat16),
            pltpu.VMEM((TALL, D), jnp.bfloat16),
            pltpu.VMEM((TALL, D), jnp.bfloat16),
            pltpu.VMEM((D, FF), jnp.bfloat16),
            pltpu.VMEM((FF, D), jnp.bfloat16),
            pltpu.VMEM((D, D), jnp.bfloat16),
            pltpu.SemaphoreType.DMA((64,)),
            pltpu.SemaphoreType.DMA((6,)),
            pltpu.SemaphoreType.DMA((3,)),
            pltpu.SemaphoreType.DMA((64,)),
        ],
        compiler_params=PARAMS,
        cost_estimate=pl.CostEstimate(flops=4 * TALL * D * (D + 2 * FF), bytes_accessed=60000000, transcendentals=3000000),
        name="feed_back",
    )(place, small, grad, summed, resid, pre, mixed, attn, *pieces)


def weight_back_kernel(place_ref, low_ref, dq_ref, dk_ref, dv_ref, dwo_ref, keep_out, send_out, vec_ref, grads_ref, sems):
    x, c, z, y = (place_ref[index] for index in range(4))
    blocks = []

    def place_matrix(source, quarter):
        for owner in range(8):
            index = ((quarter // 2) ^ x, (owner % 2) ^ y, ((owner // 2) - z) & 3, 0)
            part = source.at[owner * ROWS : owner * ROWS + ROWS, :]
            sem = sems.at[len(blocks)]
            keep = pltpu.make_async_copy(part, keep_out.at[index], sem)
            send = pltpu.make_async_copy(part, send_out.at[index], sem)

            @pl.when(c == quarter % 2)
            def _():
                keep.start()

            @pl.when(c != quarter % 2)
            def _():
                send.start()

            blocks.append(keep)

    place_matrix(dwo_ref, 3)
    grads_ref[0] = dot_tn(low_ref[...], dq_ref[...]).astype(jnp.bfloat16)
    place_matrix(grads_ref.at[0], 0)
    grads_ref[1] = dot_tn(low_ref[:LEN, :], dk_ref[...]).astype(jnp.bfloat16)
    place_matrix(grads_ref.at[1], 1)
    grads_ref[2] = dot_tn(low_ref[:LEN, :], dv_ref[...]).astype(jnp.bfloat16)
    place_matrix(grads_ref.at[2], 2)
    vec_ref[0:1, :] = jnp.sum(dq_ref[...].astype(jnp.float32), axis=0, keepdims=True)
    vec_ref[1:2, :] = jnp.sum(dv_ref[...].astype(jnp.float32), axis=0, keepdims=True)
    for block in blocks:
        block.wait()


def weight_back(place, low, dq, dk, dv, dwo):
    blocks = jax.ShapeDtypeStruct((2, 2, 4, 1, ROWS, D), jnp.bfloat16)
    return pl.pallas_call(
        weight_back_kernel,
        out_shape=[blocks, blocks, jax.ShapeDtypeStruct((2, D), jnp.float32)],
        in_specs=[SMEM_SPEC] + [VMEM_SPEC] * 5,
        out_specs=[ANY_SPEC] * 2 + [VMEM_SPEC],
        scratch_shapes=[
            pltpu.VMEM((3, D, D), jnp.bfloat16),
            pltpu.SemaphoreType.DMA((32,)),
        ],
        compiler_params=PARAMS,
        cost_estimate=pl.CostEstimate(flops=2 * 2048 * D * D, bytes_accessed=12000000, transcendentals=0),
        name="weight_back",
    )(place, low, dq, dk, dv, dwo)


def input_back_kernel(dq_ref, dk_ref, dv_ref, w_ref, dresid_ref, first_ref, second_ref):
    for row in range(0, LEN, HALF):
        rows = slice(row, row + HALF)
        first_ref[rows, :] = (
            dresid_ref[rows, :]
            + dot_nt(dq_ref[rows, :], w_ref[0])
            + dot_nt(dk_ref[rows, :], w_ref[1])
            + dot_nt(dv_ref[rows, :], w_ref[2])
        )
        rest = slice(LEN + row, LEN + row + HALF)
        second_ref[rows, :] = dresid_ref[rest, :] + dot_nt(dq_ref[rest, :], w_ref[0])


def input_back(dq, dk, dv, attn, dresid):
    half = jax.ShapeDtypeStruct((LEN, D), jnp.float32)
    return pl.pallas_call(
        input_back_kernel,
        out_shape=[half, half],
        in_specs=[VMEM_SPEC] * 5,
        out_specs=[VMEM_SPEC] * 2,
        compiler_params=PARAMS,
        cost_estimate=pl.CostEstimate(flops=2 * 2048 * D * D, bytes_accessed=16000000, transcendentals=0),
        name="input_back",
    )(dq, dk, dv, attn, dresid)


def bias_vectors(table):
    lane = jnp.arange(512, dtype=jnp.int32)
    offset = jnp.where(lane < 384, 128 - lane, 640 - lane)
    onehot = bucket_of(offset)[:, None] == jnp.arange(NB, dtype=jnp.int32)[None, :]
    near = jnp.dot(table, onehot.astype(jnp.float32).T, precision=lax.Precision.HIGHEST)
    return (near[:, None, :], jnp.stack([table[:, 15], table[:, 31]], axis=1), onehot)


def bucket_of(offset):
    distance = jnp.abs(offset)
    far_bucket = jnp.full(distance.shape, 8, jnp.int32)
    for exponent in range(1, 8):
        far_bucket = far_bucket + (distance * distance >= 64 * 2**exponent).astype(jnp.int32)
    near_or_far = jnp.where(distance < 8, distance, far_bucket)
    return near_or_far + NB // 2 * (offset > 0).astype(jnp.int32)


def table_grad(sums, onehot):
    near = jnp.dot(
        sums[:, 0, :512],
        jnp.roll(onehot.astype(jnp.float32), 127, axis=0),
        precision=lax.Precision.HIGHEST,
    )
    low = jnp.sum(sums[:, 0, 512:640], axis=1)
    high = jnp.sum(sums[:, 0, 640:], axis=1)
    return near.at[:, 15].add(low).at[:, 31].add(high)

def fetch_forward(shards):
    low = tuple(shard.astype(jnp.bfloat16) for shard in shards)
    return (
        lax.all_gather(low[0], "fsdp", axis=1, tiled=True),
        lax.all_gather(low[1], "fsdp", axis=0, tiled=True),
        lax.all_gather(low[2], "fsdp", axis=0, tiled=True),
    )


def reduce_layer(grads):
    owned = tuple(
        lax.psum_scatter(
            grad.astype(jnp.bfloat16), "fsdp", scatter_dimension=axis, tiled=True
        ).astype(jnp.float32)
        for grad, axis in zip(grads, (1, 0, 0))
    )
    return lax.psum(owned, "dp")


def forward_layer(hidden_c, hidden_q, weights, lengths, flag_rows, onehot):
    attn_w, inner_w, outer_w, small_w = weights
    pieces, hidden_bias, bias_table = unpack(small_w.astype(jnp.float32))
    bias_q, bias_v, bias_o, gain_one, shift_one, bias_two, gain_two, shift_two = pieces
    table_low = bias_table.astype(jnp.bfloat16)
    low_c = hidden_c.astype(jnp.bfloat16)
    low_q = hidden_q.astype(jnp.bfloat16)
    projected = jnp.einsum("td,sde->ste", low_c, attn_w[:3], preferred_element_type=jnp.float32)
    query_c = (projected[0] + bias_q).astype(jnp.bfloat16)
    key_rows = projected[1].astype(jnp.bfloat16)
    value_rows = (projected[2] + bias_v).astype(jnp.bfloat16)
    query_q = (jnp.dot(low_q, attn_w[0], preferred_element_type=jnp.float32) + bias_q).astype(
        jnp.bfloat16
    )
    mixed_c, mixed_q, lse_c, lse_q = lax.map(
        partial(attend_slot, onehot, table_low),
        (
            to_heads(query_c),
            to_heads(query_q),
            to_heads(key_rows),
            to_heads(value_rows),
            lengths,
            flag_rows,
        ),
    )
    mixed_c = mixed_c.reshape(-1, D)
    mixed_q = mixed_q.reshape(-1, D)
    outputs = []
    kept = []
    for hidden_in, mixed in ((hidden_c, mixed_c), (hidden_q, mixed_q)):
        resid = hidden_in + jnp.dot(mixed, attn_w[3], preferred_element_type=jnp.float32) + bias_o
        normed = layer_norm(resid, gain_one, shift_one)
        pre_act = (
            jnp.dot(normed.astype(jnp.bfloat16), inner_w, preferred_element_type=jnp.float32)
            + hidden_bias
        )
        active = jax.nn.gelu(pre_act, approximate=True).astype(jnp.bfloat16)
        summed = normed + jnp.dot(active, outer_w, preferred_element_type=jnp.float32) + bias_two
        outputs.append(layer_norm(summed, gain_two, shift_two))
        kept.append((resid, summed, pre_act))
    saved = (
        hidden_c,
        hidden_q,
        query_c,
        query_q,
        key_rows,
        value_rows,
        lse_c,
        lse_q,
        mixed_c,
        mixed_q,
        kept[0],
        kept[1],
    )
    return (outputs[0], outputs[1], saved)


def backward_layer(saved, weights, grad_c, grad_q, lengths, flag_rows, onehot):
    attn_w, inner_w, outer_w, small_w = weights
    pieces, hidden_bias, bias_table = unpack(small_w.astype(jnp.float32))
    bias_q, bias_v, bias_o, gain_one, shift_one, bias_two, gain_two, shift_two = pieces
    table_low = bias_table.astype(jnp.bfloat16)
    (
        hidden_c,
        hidden_q,
        query_c,
        query_q,
        key_rows,
        value_rows,
        lse_c,
        lse_q,
        mixed_c,
        mixed_q,
        kept_c,
        kept_q,
    ) = saved
    gelu_tanh = partial(jax.nn.gelu, approximate=True)
    grad_outer = jnp.zeros(outer_w.shape, jnp.float32)
    grad_inner = jnp.zeros(inner_w.shape, jnp.float32)
    grad_attn_out = jnp.zeros((D, D), jnp.float32)
    grad_bias_two = jnp.zeros((D,), jnp.float32)
    grad_hidden_bias = jnp.zeros((FF,), jnp.float32)
    grad_bias_o = jnp.zeros((D,), jnp.float32)
    grad_gain_one = jnp.zeros((D,), jnp.float32)
    grad_shift_one = jnp.zeros((D,), jnp.float32)
    grad_gain_two = jnp.zeros((D,), jnp.float32)
    grad_shift_two = jnp.zeros((D,), jnp.float32)
    residual_grads = []
    mix_grads = []
    for kept_rows, grad_out, mixed in ((kept_c, grad_c, mixed_c), (kept_q, grad_q, mixed_q)):
        resid, summed, pre_act = kept_rows
        normed, norm_one_back = jax.vjp(layer_norm, resid, gain_one, shift_one)
        unused_out, norm_two_back = jax.vjp(layer_norm, summed, gain_two, shift_two)
        grad_summed, grad_g2, grad_s2 = norm_two_back(grad_out)
        grad_gain_two = grad_gain_two + grad_g2
        grad_shift_two = grad_shift_two + grad_s2
        grad_branch = grad_summed.astype(jnp.bfloat16)
        grad_bias_two = grad_bias_two + jnp.sum(grad_branch.astype(jnp.float32), axis=0)
        active, gelu_back = jax.vjp(gelu_tanh, pre_act)
        grad_outer = grad_outer + jnp.einsum(
            "tf,td->fd",
            active.astype(jnp.bfloat16),
            grad_branch,
            preferred_element_type=jnp.float32,
        )
        grad_active = jnp.einsum(
            "td,fd->tf", grad_branch, outer_w, preferred_element_type=jnp.float32
        )
        grad_pre = gelu_back(grad_active)[0].astype(jnp.bfloat16)
        grad_hidden_bias = grad_hidden_bias + jnp.sum(grad_pre.astype(jnp.float32), axis=0)
        grad_inner = grad_inner + jnp.einsum(
            "td,tf->df", normed.astype(jnp.bfloat16), grad_pre, preferred_element_type=jnp.float32
        )
        grad_normed = grad_summed + jnp.einsum(
            "tf,df->td", grad_pre, inner_w, preferred_element_type=jnp.float32
        )
        grad_resid, grad_g1, grad_s1 = norm_one_back(grad_normed)
        grad_gain_one = grad_gain_one + grad_g1
        grad_shift_one = grad_shift_one + grad_s1
        grad_proj = grad_resid.astype(jnp.bfloat16)
        grad_bias_o = grad_bias_o + jnp.sum(grad_proj.astype(jnp.float32), axis=0)
        grad_attn_out = grad_attn_out + jnp.einsum(
            "td,te->de", mixed, grad_proj, preferred_element_type=jnp.float32
        )
        mix_grads.append(
            jnp.einsum(
                "te,de->td", grad_proj, attn_w[3], preferred_element_type=jnp.float32
            ).astype(jnp.bfloat16)
        )
        residual_grads.append(grad_resid)
    grad_query_c, grad_query_q, grad_keys, grad_values, grad_table = lax.map(
        partial(attend_back, onehot, table_low),
        (
            to_heads(query_c),
            to_heads(query_q),
            to_heads(key_rows),
            to_heads(value_rows),
            lengths,
            flag_rows,
            lse_c,
            lse_q,
            to_heads(mix_grads[0]),
            to_heads(mix_grads[1]),
        ),
    )
    grad_table = jnp.sum(grad_table, axis=0)
    low_query_c = grad_query_c.reshape(-1, D).astype(jnp.bfloat16)
    low_query_q = grad_query_q.reshape(-1, D).astype(jnp.bfloat16)
    low_keys = grad_keys.reshape(-1, D).astype(jnp.bfloat16)
    low_values = grad_values.reshape(-1, D).astype(jnp.bfloat16)
    low_c = hidden_c.astype(jnp.bfloat16)
    low_q = hidden_q.astype(jnp.bfloat16)
    stacked_grads = jnp.stack([low_query_c, low_keys, low_values])
    grad_qkv = jnp.einsum("td,ste->sde", low_c, stacked_grads, preferred_element_type=jnp.float32)
    grad_wq = grad_qkv[0] + jnp.einsum(
        "td,te->de", low_q, low_query_q, preferred_element_type=jnp.float32
    )
    grad_attn = jnp.stack([grad_wq, grad_qkv[1], grad_qkv[2], grad_attn_out])
    grad_bias_q = jnp.sum(low_query_c.astype(jnp.float32), axis=0) + jnp.sum(
        low_query_q.astype(jnp.float32), axis=0
    )
    grad_bias_v = jnp.sum(low_values.astype(jnp.float32), axis=0)
    grad_content = residual_grads[0] + jnp.einsum(
        "ste,sde->td", stacked_grads, attn_w[:3], preferred_element_type=jnp.float32
    )
    grad_query_in = residual_grads[1] + jnp.einsum(
        "te,de->td", low_query_q, attn_w[0], preferred_element_type=jnp.float32
    )
    grad_small = jnp.concatenate(
        [
            grad_bias_q,
            grad_bias_v,
            grad_bias_o,
            grad_gain_one,
            grad_shift_one,
            grad_bias_two,
            grad_gain_two,
            grad_shift_two,
            grad_hidden_bias,
            grad_table.reshape(-1),
        ]
    )
    return (grad_content, grad_query_in, (grad_attn, grad_inner, grad_outer, grad_small))


def adam_update(master, first, second, grad, rate):
    first_new = BETA_ONE * first + (1.0 - BETA_ONE) * grad
    second_new = BETA_TWO * second + (1.0 - BETA_TWO) * grad * grad
    first_hat = first_new / (1.0 - BETA_ONE**STEP)
    second_hat = second_new / (1.0 - BETA_TWO**STEP)
    master_new = master - rate * (
        first_hat / (jnp.sqrt(second_hat) + ADAM_EPS) + WEIGHT_DECAY * master
    )
    return (master_new, first_new, second_new)


def per_device(
    content,
    query,
    lengths,
    predicted,
    content_cot,
    query_cot,
    attn_master,
    attn_first,
    attn_second,
    inner_master,
    inner_first,
    inner_second,
    outer_master,
    outer_first,
    outer_second,
    small_master,
    small_first,
    small_second,
):
    masters = (attn_master, inner_master, outer_master, small_master)
    slot_count = lengths.shape[0]
    flag_rows = predicted.reshape(slot_count, LEN)
    onehot = bucket_onehot()
    hidden_c = content.astype(jnp.float32)
    hidden_q = query.astype(jnp.float32)
    kept_weights = []
    saved_layers = []
    small_all = lax.all_gather(
        small_master.astype(jnp.bfloat16), "fsdp", axis=1, tiled=True
    )
    for layer_index in range(LAYERS):
        shards = tuple((master[layer_index] for master in masters[:3]))
        gathered = fetch_forward(shards) + (small_all[layer_index],)
        kept_weights.append(gathered)
        hidden_c, hidden_q, saved = forward_layer(
            hidden_c, hidden_q, gathered, lengths, flag_rows, onehot
        )
        saved_layers.append(saved)
    position = jnp.arange(LEN, dtype=jnp.int32)
    valid_rows = (position[None, :] < lengths[:, None]).reshape(-1, 1).astype(jnp.float32)
    grad_c = content_cot.astype(jnp.float32) * valid_rows
    grad_q = query_cot.astype(jnp.float32) * valid_rows
    layer_grads = [None] * LAYERS
    small_grads = [None] * LAYERS
    for layer_index in reversed(range(LAYERS)):
        grad_c, grad_q, local_grads = backward_layer(
            saved_layers[layer_index],
            kept_weights[layer_index],
            grad_c,
            grad_q,
            lengths,
            flag_rows,
            onehot,
        )
        small_grads[layer_index] = local_grads[3]
        layer_grads[layer_index] = reduce_layer(local_grads[:3])
    small_sum = lax.psum(jnp.stack(small_grads), ("dp", "fsdp"))
    owned = small_master.shape[1]
    small_own = lax.dynamic_slice_in_dim(
        small_sum, lax.axis_index("fsdp") * owned, owned, 1
    )
    reduced = tuple(
        (
            jnp.stack([layer_grads[layer_index][member] for layer_index in range(LAYERS)])
            for member in range(3)
        )
    ) + (small_own,)
    attn_new = adam_update(attn_master, attn_first, attn_second, reduced[0], ATTENTION_RATE)
    inner_new = adam_update(inner_master, inner_first, inner_second, reduced[1], FEED_RATE)
    outer_new = adam_update(outer_master, outer_first, outer_second, reduced[2], FEED_RATE)
    small_new = adam_update(small_master, small_first, small_second, reduced[3], SMALL_RATE)
    return (
        hidden_c.astype(jnp.bfloat16),
        hidden_q.astype(jnp.bfloat16),
        grad_c,
        grad_q,
        attn_new[0],
        attn_new[1],
        attn_new[2],
        inner_new[0],
        inner_new[1],
        inner_new[2],
        outer_new[0],
        outer_new[1],
        outer_new[2],
        small_new[0],
        small_new[1],
        small_new[2],
    )


def own_quarter(kind, shard, quarter):
    if kind == "attn":
        part = lax.dynamic_index_in_dim(shard, quarter, 0, keepdims=False)
    elif kind == "inner":
        part = lax.dynamic_slice_in_dim(shard, quarter * D, D, 1)
    else:
        part = lax.dynamic_slice_in_dim(shard, quarter * ROWS, ROWS, 0)
    return part.astype(jnp.bfloat16)


def gather_group(kinds, shards, place):
    quarter = place[0] * 2 + place[1]
    own = jnp.stack([own_quarter(kind, shard, quarter) for kind, shard in zip(kinds, shards)])
    return spread_blocks(own)


def gather_small(shard, place):
    z, y = place[2], place[3]
    column = jnp.stack([shift_z(shard, step) for step in (3, 2, 1)] + [shard])
    other = swap_y(column)
    pairs = jnp.where(y == 0, jnp.stack([column, other], 1), jnp.stack([other, column], 1))
    twice = jnp.concatenate([pairs, pairs])
    whole = lax.dynamic_slice_in_dim(twice, 3 - z, 4, 0)
    return whole.transpose(2, 0, 1, 3).reshape(shard.shape[0], -1)


def sum_small(value):
    value = value + swap_core(value)
    value = value + swap_x(value)
    value = value + swap_y(value)
    return value + shift_z(value, 1) + shift_z(value, 2) + shift_z(value, 3)


def add_low(*values):
    total = values[0].astype(jnp.float32)
    for value in values[1:]:
        total = total + value.astype(jnp.float32)
    return total.astype(jnp.bfloat16)


def reduce_blocks(keep, send):
    both = add_low(keep, swap_core(send))
    corner = both[1, 1]
    by_x = swap_x(corner[:2])
    by_y = swap_y(corner[2:])
    for_y = jnp.concatenate([add_low(both[0, 1, :2], by_x), both[0, 1, 2:]])
    for_x = jnp.concatenate([both[1, 0, :2], add_low(both[1, 0, 2:], by_y)])
    column = add_low(both[0, 0], swap_x(for_x), swap_y(for_y))
    total = column[0].astype(jnp.float32)
    for step in (1, 2, 3):
        total = total + shift_z(column[step], step).astype(jnp.float32)
    return total.astype(jnp.bfloat16)


def share_quarters(own, place):
    x, c = place[0], place[1]
    pair = jnp.stack([own, swap_x(own)])
    other = swap_core(pair)
    cores = jnp.where(c == 0, jnp.stack([pair, other], 1), jnp.stack([other, pair], 1))
    sides = jnp.where(x == 0, cores, cores[::-1])
    return sides.reshape((4,) + own.shape)


def shard_grad(kind, quarters):
    four = quarters.astype(jnp.float32)
    if kind == "attn":
        return four
    if kind == "inner":
        return four.transpose(1, 0, 2).reshape(ROWS, FF)
    return four.reshape(4 * ROWS, D)


def small_parts(vectors):
    values = vectors.astype(jnp.float32)
    return (
        values[: 8 * D].reshape(8, D),
        values[8 * D : 8 * D + FF].reshape(1, FF),
        bias_vectors(values[8 * D + FF :].reshape(H, NB)),
    )


def per_device_fast(
    content,
    query,
    lengths,
    predicted,
    content_cot,
    query_cot,
    attn_master,
    attn_first,
    attn_second,
    inner_master,
    inner_first,
    inner_second,
    outer_master,
    outer_first,
    outer_second,
    small_master,
    small_first,
    small_second,
):
    place_parts = my_place()
    place = jnp.stack(place_parts).astype(jnp.int32)
    small_all = gather_small(small_master.astype(jnp.bfloat16), place_parts)
    attn_pieces = []
    feed_pieces = []
    for layer in range(LAYERS):
        attn_pieces.append(gather_group(("attn",), (attn_master[layer],), place_parts))
        feed_pieces.append(
            gather_group(
                ("inner", "outer"), (inner_master[layer], outer_master[layer]), place_parts
            )
        )
    row_flags = predicted.reshape(1, LEN).astype(jnp.float32)
    col_flags = predicted.reshape(LEN, 1).astype(jnp.float32)
    low = jnp.concatenate([content, query])
    hidden = low.astype(jnp.float32)
    kept = []
    for layer in range(LAYERS):
        small, hidden_bias, (tvec, far, onehot) = small_parts(small_all[layer])
        q, k, v, attn = project(place, low, small, attn_pieces[layer])
        mixed, lse = mix(lengths, far, tvec, q, k, v, row_flags, col_flags)
        resid, summed, pre, hidden, next_low = feed(
            place, small, hidden_bias, mixed, hidden, attn, feed_pieces[layer]
        )
        kept.append((small, far, tvec, onehot, low, q, k, v, attn, mixed, lse, resid, summed, pre))
        low = next_low
    valid = (jnp.arange(LEN, dtype=jnp.int32) < lengths[0])[:, None].astype(jnp.float32)
    grad = jnp.concatenate(
        [content_cot.astype(jnp.float32) * valid, query_cot.astype(jnp.float32) * valid]
    )
    owned = [None] * LAYERS
    small_grads = [None] * LAYERS
    for layer in reversed(range(LAYERS)):
        small, far, tvec, onehot, low_in, q, k, v, attn, mixed, lse, resid, summed, pre = kept[layer]
        dresid, dmix, dwo, feed_keep, feed_send, feed_vec, dhidden = feed_back(
            place, small, grad, summed, resid, pre, mixed, attn, feed_pieces[layer]
        )
        feed_own = reduce_blocks(feed_keep, feed_send)
        dq, dk, dv, table_sums = mix_back(
            lengths, far, tvec, q, k, v, dmix, mixed, lse, row_flags, col_flags
        )
        attn_keep, attn_send, attn_vec = weight_back(place, low_in, dq, dk, dv, dwo)
        attn_own = reduce_blocks(attn_keep, attn_send)
        grad_c, grad_q = input_back(dq, dk, dv, attn, dresid)
        if layer:
            grad = jnp.concatenate([grad_c, grad_q])
        small_grads[layer] = jnp.concatenate(
            [
                attn_vec.reshape(-1),
                feed_vec[2:].reshape(-1),
                dhidden.reshape(-1),
                table_grad(table_sums, onehot).reshape(-1),
            ]
        )
        feed_four = share_quarters(feed_own, place_parts)
        attn_four = share_quarters(attn_own, place_parts)
        owned[layer] = (
            shard_grad("attn", attn_four[:, 0]),
            shard_grad("inner", feed_four[:, 0]),
            shard_grad("outer", feed_four[:, 1]),
        )
    small_sum = sum_small(jnp.stack(small_grads))
    size = small_master.shape[1]
    small_own = lax.dynamic_slice_in_dim(small_sum, lax.axis_index("fsdp") * size, size, 1)
    reduced = tuple(
        jnp.stack([owned[layer][member] for layer in range(LAYERS)]) for member in range(3)
    )
    attn_new = adam_update(attn_master, attn_first, attn_second, reduced[0], ATTENTION_RATE)
    inner_new = adam_update(inner_master, inner_first, inner_second, reduced[1], FEED_RATE)
    outer_new = adam_update(outer_master, outer_first, outer_second, reduced[2], FEED_RATE)
    small_new = adam_update(small_master, small_first, small_second, small_own, SMALL_RATE)
    return (
        (low[:LEN], low[LEN:], grad_c, grad_q) + attn_new + inner_new + outer_new + small_new
    )


def solution(mesh):
    placed = (
        P(("dp", "fsdp"), None),
        P(("dp", "fsdp"), None),
        P(("dp", "fsdp")),
        P(("dp", "fsdp")),
        P(("dp", "fsdp"), None),
        P(("dp", "fsdp"), None),
        P(None, None, "fsdp", None),
        P(None, None, "fsdp", None),
        P(None, None, "fsdp", None),
        P(None, "fsdp", None),
        P(None, "fsdp", None),
        P(None, "fsdp", None),
        P(None, "fsdp", None),
        P(None, "fsdp", None),
        P(None, "fsdp", None),
        P(None, "fsdp"),
        P(None, "fsdp"),
        P(None, "fsdp"),
    )
    fast = tuple(mesh.shape.values()) == (4, 8)
    return jax.shard_map(
        per_device_fast if fast else per_device,
        mesh=mesh,
        in_specs=placed,
        out_specs=(
            P(("dp", "fsdp"), None),
            P(("dp", "fsdp"), None),
            P(("dp", "fsdp"), None),
            P(("dp", "fsdp"), None),
            P(None, None, "fsdp", None),
            P(None, None, "fsdp", None),
            P(None, None, "fsdp", None),
            P(None, "fsdp", None),
            P(None, "fsdp", None),
            P(None, "fsdp", None),
            P(None, "fsdp", None),
            P(None, "fsdp", None),
            P(None, "fsdp", None),
            P(None, "fsdp"),
            P(None, "fsdp"),
            P(None, "fsdp"),
        ),
        check_vma=False,
    )
```

```python
from functools import partial

import jax
import jax.numpy as jnp
from jax import lax
from jax.experimental import pallas as pl
from jax.experimental.pallas import tpu as pltpu
from jax.sharding import PartitionSpec as P

D = 768
H = 12
DH = 64
FF = 3072
LEN = 512
NB = 32
LAYERS = 2
STEP = 10


NORM_EPS = 1e-05
MASKED = -1000000000.0
BETA_ONE = 0.9
BETA_TWO = 0.999
ATTENTION_RATE = 0.1
FEED_RATE = 0.02
SMALL_RATE = 0.4
WEIGHT_DECAY = 0.01
ADAM_EPS = 1e-08
SCORE_SCALE = 0.125


def layer_norm(values, gain, shift):
    centre = values - jnp.mean(values, axis=-1, keepdims=True)
    spread = jnp.mean(centre * centre, axis=-1, keepdims=True)
    return centre * lax.rsqrt(spread + NORM_EPS) * gain + shift


def unpack(vectors):
    pieces = [vectors[piece_index * D : (piece_index + 1) * D] for piece_index in range(8)]
    hidden_bias = vectors[8 * D : 8 * D + FF]
    bias_table = vectors[8 * D + FF :].reshape(H, NB)
    return (pieces, hidden_bias, bias_table)


def bucket_ids():
    position = jnp.arange(LEN, dtype=jnp.int32)
    offset = position[None, :] - position[:, None]
    distance = jnp.abs(offset)
    far_bucket = jnp.full(distance.shape, 8, jnp.int32)
    for exponent in range(1, 8):
        far_bucket = far_bucket + (distance * distance >= 64 * 2**exponent).astype(jnp.int32)
    near_or_far = jnp.where(distance < 8, distance, far_bucket)
    return near_or_far + NB // 2 * (offset > 0).astype(jnp.int32)


def bucket_onehot():
    return (bucket_ids()[:, :, None] == jnp.arange(NB, dtype=jnp.int32)[None, None, :]).astype(
        jnp.bfloat16
    )


def allowed_pairs(length, pred_flags):
    position = jnp.arange(LEN, dtype=jnp.int32)
    valid_key = (position < length)[None, :]
    row_pos = position[:, None]
    col_pos = position[None, :]
    free_key = (pred_flags == 0)[None, :]
    content_ok = valid_key & (free_key | (pred_flags[:, None] == 1) & (col_pos <= row_pos))
    query_ok = valid_key & (col_pos != row_pos) & (free_key | (col_pos < row_pos))
    return (content_ok, query_ok)


def masked_scores(query_rows, key_rows, position_bias, allowed):
    scores = (
        jnp.einsum("qhd,khd->hqk", query_rows, key_rows, preferred_element_type=jnp.float32)
        * SCORE_SCALE
        + position_bias
    )
    return jnp.where(allowed[None], scores, MASKED)


def table_bias(onehot, table_low):
    return jnp.einsum("qkb,hb->hqk", onehot, table_low, preferred_element_type=jnp.float32)


def attend_slot(onehot, table_low, slot_item):
    query_c, query_q, key_rows, value_rows, length, pred_flags = slot_item
    position_bias = table_bias(onehot, table_low)
    content_ok, query_ok = allowed_pairs(length, pred_flags)
    results = []
    for query_rows, allowed in ((query_c, content_ok), (query_q, query_ok)):
        scores = masked_scores(query_rows, key_rows, position_bias, allowed)
        peak = jnp.max(scores, axis=-1, keepdims=True)
        expos = jnp.exp(scores - peak)
        totals = jnp.sum(expos, axis=-1, keepdims=True)
        probs = (expos / totals).astype(jnp.bfloat16)
        mixed = jnp.einsum(
            "hqk,khd->qhd", probs, value_rows, preferred_element_type=jnp.float32
        ).astype(jnp.bfloat16)
        results.append((mixed, peak[..., 0] + jnp.log(totals[..., 0])))
    return (results[0][0], results[1][0], results[0][1], results[1][1])


def attend_back(onehot, table_low, slot_item):
    (
        query_c,
        query_q,
        key_rows,
        value_rows,
        length,
        pred_flags,
        lse_c,
        lse_q,
        grad_mix_c,
        grad_mix_q,
    ) = slot_item
    position_bias = table_bias(onehot, table_low)
    content_ok, query_ok = allowed_pairs(length, pred_flags)
    grad_keys = jnp.zeros(key_rows.shape, jnp.float32)
    grad_values = jnp.zeros(value_rows.shape, jnp.float32)
    grad_table = jnp.zeros((H, NB), jnp.float32)
    grads_query = []
    for query_rows, allowed, log_total, grad_mix in (
        (query_c, content_ok, lse_c, grad_mix_c),
        (query_q, query_ok, lse_q, grad_mix_q),
    ):
        scores = masked_scores(query_rows, key_rows, position_bias, allowed)
        probs = jnp.exp(scores - log_total[..., None])
        grad_values = grad_values + jnp.einsum(
            "hqk,qhd->khd", probs.astype(jnp.bfloat16), grad_mix, preferred_element_type=jnp.float32
        )
        grad_probs = jnp.einsum(
            "qhd,khd->hqk", grad_mix, value_rows, preferred_element_type=jnp.float32
        )
        grad_scores = probs * (grad_probs - jnp.sum(probs * grad_probs, axis=-1, keepdims=True))
        grad_scores = jnp.where(allowed[None], grad_scores, 0.0).astype(jnp.bfloat16)
        grad_table = grad_table + jnp.einsum(
            "hqk,qkb->hb", grad_scores, onehot, preferred_element_type=jnp.float32
        )
        grads_query.append(
            jnp.einsum("hqk,khd->qhd", grad_scores, key_rows, preferred_element_type=jnp.float32)
            * SCORE_SCALE
        )
        grad_keys = (
            grad_keys
            + jnp.einsum(
                "hqk,qhd->khd", grad_scores, query_rows, preferred_element_type=jnp.float32
            )
            * SCORE_SCALE
        )
    return (grads_query[0], grads_query[1], grad_keys, grad_values, grad_table)


def to_heads(values):
    return values.reshape(-1, LEN, H, DH)


AXES = ("dp", "fsdp")
GRID = (2, 2, 4, 2)
ROWS = 96


def places():
    return [
        (x, c, z, y) for x in range(2) for c in range(2) for z in range(4) for y in range(2)
    ]


def flat(x, c, z, y):
    return ((x * 2 + c) * 4 + z) * 2 + y


def move(value, shift):
    pairs = [(flat(*place), flat(*shift(*place))) for place in places()]
    return lax.ppermute(value, AXES, pairs)


def swap_core(value):
    return move(value, lambda x, c, z, y: (x, 1 - c, z, y))


def swap_x(value):
    return move(value, lambda x, c, z, y: (1 - x, c, z, y))


def swap_y(value):
    return move(value, lambda x, c, z, y: (x, c, z, 1 - y))


def shift_z(value, step):
    return move(value, lambda x, c, z, y: (x, c, (z + step) % 4, y))


def my_place():
    dp = lax.axis_index("dp")
    fsdp = lax.axis_index("fsdp")
    return (dp // 2, dp % 2, fsdp // 2, fsdp % 2)


PIECES = ((0, 0, 0, 4), (1, 0, 0, 4), (0, 1, 0, 4), (1, 1, 0, 2), (1, 1, 2, 4))


def dot_nn(left, right):
    return jnp.dot(left, right, preferred_element_type=jnp.float32)


def dot_nt(left, right):
    return lax.dot_general(
        left, right, (((1,), (1,)), ((), ())), preferred_element_type=jnp.float32
    )


def dot_tn(left, right):
    return lax.dot_general(
        left, right, (((0,), (0,)), ((), ())), preferred_element_type=jnp.float32
    )


ANY_SPEC = pl.BlockSpec(memory_space=pl.ANY)
VMEM_SPEC = pl.BlockSpec(memory_space=pltpu.VMEM)
SMEM_SPEC = pl.BlockSpec(memory_space=pltpu.SMEM)
TALL = 2 * LEN
HALF = 256
PARAMS = pltpu.CompilerParams(vmem_limit_bytes=60 * 1024 * 1024)


def norm_parts(values):
    centre = values - jnp.mean(values, axis=-1, keepdims=True)
    spread = jnp.mean(centre * centre, axis=-1, keepdims=True)
    scale = lax.rsqrt(spread + NORM_EPS)
    return (centre * scale, scale)


def norm_back(unit, scale, grad, gain):
    scaled = grad * gain
    return scale * (
        scaled
        - jnp.mean(scaled, axis=-1, keepdims=True)
        - unit * jnp.mean(scaled * unit, axis=-1, keepdims=True)
    )


def start_fetch(kinds, place_ref, pieces, targets, sems):
    x, c, z, y = (place_ref[index] for index in range(4))
    copies = []
    for other in range(2):
        for piece, (dx, dy, first, last) in enumerate(PIECES):
            for k in range(first, last):
                quarter = (x ^ dx) * 2 + (c ^ other)
                owner = ((z - k) & 3) * 2 + (y ^ dy)
                for member, kind in enumerate(kinds):
                    if kind == "attn":
                        target = targets[member].at[
                            quarter, pl.ds(pl.multiple_of(owner * ROWS, ROWS), ROWS), :
                        ]
                    elif kind == "inner":
                        target = targets[member].at[
                            pl.ds(pl.multiple_of(owner * ROWS, ROWS), ROWS),
                            pl.ds(pl.multiple_of(quarter * D, D), D),
                        ]
                    else:
                        target = targets[member].at[
                            pl.ds(pl.multiple_of(owner * 384 + quarter * ROWS, ROWS), ROWS), :
                        ]
                    copy = pltpu.make_async_copy(
                        pieces[other * 5 + piece].at[k - first, member],
                        target,
                        sems.at[len(copies)],
                    )
                    copy.start()
                    copies.append(copy)
    return copies


def project_kernel(place_ref, low_ref, small_ref, *refs):
    pieces = refs[:10]
    q_ref, k_ref, v_ref, w_out, w_ref, sems, out_sem = refs[10:]
    for copy in start_fetch(("attn",), place_ref, pieces, (w_ref,), sems):
        copy.wait()
    keep = pltpu.make_async_copy(w_ref, w_out, out_sem)
    keep.start()
    bias_q = small_ref[0:1, :]
    bias_v = small_ref[1:2, :]
    for row in range(0, TALL, HALF):
        rows = low_ref[row : row + HALF, :]
        q_ref[row : row + HALF, :] = (dot_nn(rows, w_ref[0]) + bias_q).astype(jnp.bfloat16)
        if row < LEN:
            k_ref[row : row + HALF, :] = dot_nn(rows, w_ref[1]).astype(jnp.bfloat16)
            v_ref[row : row + HALF, :] = (dot_nn(rows, w_ref[2]) + bias_v).astype(jnp.bfloat16)
    keep.wait()


def project(place, low, small, pieces):
    return pl.pallas_call(
        project_kernel,
        out_shape=[
            jax.ShapeDtypeStruct((TALL, D), jnp.bfloat16),
            jax.ShapeDtypeStruct((LEN, D), jnp.bfloat16),
            jax.ShapeDtypeStruct((LEN, D), jnp.bfloat16),
            jax.ShapeDtypeStruct((4, D, D), jnp.bfloat16),
        ],
        in_specs=[SMEM_SPEC, VMEM_SPEC, VMEM_SPEC] + [ANY_SPEC] * 10,
        out_specs=[VMEM_SPEC] * 3 + [ANY_SPEC],
        scratch_shapes=[
            pltpu.VMEM((4, D, D), jnp.bfloat16),
            pltpu.SemaphoreType.DMA((32,)),
            pltpu.SemaphoreType.DMA,
        ],
        compiler_params=PARAMS,
        cost_estimate=pl.CostEstimate(flops=2 * 2048 * D * D, bytes_accessed=16000000, transcendentals=0),
        name="project",
    )(place, low, small, *pieces)


def build_masks(length, row_flags, col_flags, mask_ref, alive_ref):
    flags = row_flags[...]

    def body(step, carry):
        start = pl.multiple_of(step * 64, 64)
        key = lax.broadcasted_iota(jnp.int32, (64, LEN), 0) + start
        query = lax.broadcasted_iota(jnp.int32, (64, LEN), 1)
        valid = key < length
        free = jnp.broadcast_to(col_flags[pl.ds(start, 64), :], (64, LEN)) == 0.0
        marked = jnp.broadcast_to(flags, (64, LEN)) == 1.0
        content_ok = valid & (free | (marked & (key <= query)))
        query_ok = valid & (key != query) & (free | (key < query))
        mask_ref[pl.ds(start, 64), :LEN] = content_ok.astype(jnp.float32)
        mask_ref[pl.ds(start, 64), LEN:] = query_ok.astype(jnp.float32)
        return carry

    lax.fori_loop(0, 8, body, 0)
    alive_ref[...] = jnp.max(mask_ref[...], axis=0, keepdims=True)


def build_tiles(t_row, tile_ref):
    spread = jnp.broadcast_to(t_row, (128, 512))
    rolled = pltpu.roll(spread, 0, 1, stride=1, stride_axis=0)
    tile_ref[...] = rolled[:, :384]


def position_bias(tile_ref, far_ref, head, query_block, key_block):
    apart = query_block - key_block
    if apart >= 2:
        return far_ref[head, 0]
    if apart <= -2:
        return far_ref[head, 1]
    return tile_ref[:, 128 * (apart + 1) : 128 * (apart + 2)]


def head_lanes(shape, head):
    lane = lax.broadcasted_iota(jnp.int32, shape, 1)
    return (lane >= 64) if head else (lane < 64)


def mix_kernel(
    length_ref, far_ref, q_ref, k_ref, v_ref, row_flags, col_flags, t_ref,
    a_ref, lse_ref, mask_ref, alive_ref, tile_ref, p_ref, o_ref,
):
    pair = pl.program_id(0)

    @pl.when(pair == 0)
    def _():
        build_masks(length_ref[0], row_flags, col_flags, mask_ref, alive_ref)

    keys = k_ref[...].astype(jnp.float32) * SCORE_SCALE
    values_t = v_ref[...].astype(jnp.float32).T.astype(jnp.bfloat16)
    for head in range(2):
        build_tiles(t_ref[head], tile_ref.at[head])
        keys_own = jnp.where(head_lanes(keys.shape, head), keys, 0.0).astype(jnp.bfloat16)
        for chunk in range(4):
            at = chunk * HALF
            scores = dot_nt(keys_own, q_ref[at : at + HALF, :])
            for side in range(2):
                lanes = slice(at + side * 128, at + side * 128 + 128)
                blocks = []
                peak = None
                for key_block in range(4):
                    rows = slice(key_block * 128, key_block * 128 + 128)
                    block = scores[rows, side * 128 : side * 128 + 128] + position_bias(
                        tile_ref.at[head], far_ref, pair * 2 + head, (chunk % 2) * 2 + side, key_block
                    )
                    block = jnp.where(mask_ref[rows, lanes] > 0.0, block, MASKED)
                    blocks.append(block)
                    high = jnp.max(block, axis=0, keepdims=True)
                    peak = high if peak is None else jnp.maximum(peak, high)
                total = None
                for key_block in range(4):
                    rows = slice(key_block * 128, key_block * 128 + 128)
                    expo = jnp.exp(blocks[key_block] - peak)
                    part = jnp.sum(expo, axis=0, keepdims=True)
                    total = part if total is None else total + part
                    p_ref[head, rows, lanes] = expo.astype(jnp.bfloat16)
                lse_ref[head, :, lanes] = jnp.where(
                    alive_ref[:, lanes] > 0.0, peak + jnp.log(total), 1e30
                )
                o_ref[head : head + 1, lanes] = 1.0 / total
        mixed = dot_nn(values_t[head * 64 : head * 64 + 64, :], p_ref[head])
        o_ref[8 + head * 64 : 8 + head * 64 + 64, :] = mixed * o_ref[head : head + 1, :]
    a_ref[...] = o_ref[8:, :].T.astype(jnp.bfloat16)


def mix(length, far, tvec, q, k, v, row_flags, col_flags):
    tall = pl.BlockSpec((TALL, 128), lambda p: (0, p))
    short = pl.BlockSpec((LEN, 128), lambda p: (0, p))
    return pl.pallas_call(
        mix_kernel,
        grid=(H // 2,),
        out_shape=[
            jax.ShapeDtypeStruct((TALL, D), jnp.bfloat16),
            jax.ShapeDtypeStruct((H, 1, TALL), jnp.float32),
        ],
        in_specs=[
            SMEM_SPEC, SMEM_SPEC, tall, short, short,
            pl.BlockSpec((1, LEN), lambda p: (0, 0)),
            pl.BlockSpec((LEN, 1), lambda p: (0, 0)),
            pl.BlockSpec((2, 1, 512), lambda p: (p, 0, 0)),
        ],
        out_specs=[tall, pl.BlockSpec((2, 1, TALL), lambda p: (p, 0, 0))],
        scratch_shapes=[
            pltpu.VMEM((LEN, TALL), jnp.float32),
            pltpu.VMEM((1, TALL), jnp.float32),
            pltpu.VMEM((2, 128, 384), jnp.float32),
            pltpu.VMEM((2, LEN, TALL), jnp.bfloat16),
            pltpu.VMEM((136, TALL), jnp.float32),
        ],
        compiler_params=PARAMS,
        cost_estimate=pl.CostEstimate(flops=6500000000, bytes_accessed=8000000, transcendentals=6300000),
        name="mix",
    )(length, far, q, k, v, row_flags, col_flags, tvec)


def mix_back_kernel(
    length_ref, far_ref, q_ref, k_ref, v_ref, da_ref, a_ref, lse_ref, row_flags, col_flags, t_ref,
    dq_ref, dk_ref, dv_ref, table_ref,
    mask_ref, alive_ref, tile_ref, p_ref, s_ref, near_ref, d_ref,
):
    pair = pl.program_id(0)

    @pl.when(pair == 0)
    def _():
        build_masks(length_ref[0], row_flags, col_flags, mask_ref, alive_ref)

    keys = k_ref[...].astype(jnp.float32) * SCORE_SCALE
    keys_t = keys.T.astype(jnp.bfloat16)
    product = da_ref[...].astype(jnp.float32) * a_ref[...].astype(jnp.float32)
    d_ref[...] = product.T
    values = v_ref[...]
    grads_k = []
    grads_v = []
    near_ref[...] = jnp.zeros(near_ref.shape, jnp.float32)
    turn = (
        lax.broadcasted_iota(jnp.int32, (128, 128), 0)
        + lax.broadcasted_iota(jnp.int32, (128, 128), 1)
        == 127
    ).astype(jnp.float32)
    for head in range(2):
        build_tiles(t_ref[head], tile_ref.at[head])
        mine = head_lanes(keys.shape, head)
        keys_own = jnp.where(mine, keys, 0.0).astype(jnp.bfloat16)
        values_own = jnp.where(mine, values.astype(jnp.float32), 0.0).astype(jnp.bfloat16)
        delta = jnp.sum(d_ref[head * 64 : head * 64 + 64, :], axis=0, keepdims=True)
        far_low = jnp.zeros((8, 128), jnp.float32)
        far_high = jnp.zeros((8, 128), jnp.float32)
        for chunk in range(4):
            at = chunk * HALF
            scores = dot_nt(keys_own, q_ref[at : at + HALF, :])
            pulls = dot_nt(values_own, da_ref[at : at + HALF, :])
            for side in range(2):
                lanes = slice(at + side * 128, at + side * 128 + 128)
                log_total = lse_ref[head, :, lanes]
                shift = delta[:, lanes]
                for key_block in range(4):
                    rows = slice(key_block * 128, key_block * 128 + 128)
                    cols = slice(side * 128, side * 128 + 128)
                    query_block = (chunk % 2) * 2 + side
                    block = scores[rows, cols] + position_bias(
                        tile_ref.at[head], far_ref, pair * 2 + head, query_block, key_block
                    )
                    block = jnp.where(mask_ref[rows, lanes] > 0.0, block, MASKED)
                    prob = jnp.exp(block - log_total)
                    p_ref[head, rows, lanes] = prob.astype(jnp.bfloat16)
                    grad = prob * (pulls[rows, cols] - shift)
                    s_ref[head, rows, lanes] = grad.astype(jnp.bfloat16)
                    apart = query_block - key_block
                    if apart >= 2:
                        far_low = far_low + jnp.sum(grad.reshape(16, 8, 128), axis=0)
                    elif apart <= -2:
                        far_high = far_high + jnp.sum(grad.reshape(16, 8, 128), axis=0)
                    else:
                        near_ref[head, :, 128 * (apart + 1) : 128 * (apart + 2)] += grad
        grads_v.append(dot_nn(p_ref[head], da_ref[...]))
        grads_k.append(dot_nn(s_ref[head], q_ref[...]))
        d_ref[head * 64 : head * 64 + 64, :] = dot_nn(
            keys_t[head * 64 : head * 64 + 64, :], s_ref[head]
        )
        turned = jnp.dot(
            turn, near_ref[head], precision=lax.Precision.HIGHEST, preferred_element_type=jnp.float32
        )
        aligned = pltpu.roll(turned, 0, 1, stride=1, stride_axis=0)
        table_ref[head, :, :512] = jnp.sum(aligned, axis=0, keepdims=True)
        table_ref[head, :, 512:640] = jnp.sum(far_low, axis=0, keepdims=True)
        table_ref[head, :, 640:] = jnp.sum(far_high, axis=0, keepdims=True)
    dead = (1.0 - alive_ref[...]) * (1.0 / LEN)
    uniform = dot_nn(dead.astype(jnp.bfloat16), da_ref[...])
    first = head_lanes((LEN, 128), 0)
    dv_ref[...] = (jnp.where(first, grads_v[0], grads_v[1]) + uniform).astype(jnp.bfloat16)
    dk_ref[...] = (jnp.where(first, grads_k[0], grads_k[1]) * SCORE_SCALE).astype(jnp.bfloat16)
    dq_ref[...] = d_ref[...].T.astype(jnp.bfloat16)


def mix_back(length, far, tvec, q, k, v, da, a, lse, row_flags, col_flags):
    tall = pl.BlockSpec((TALL, 128), lambda p: (0, p))
    short = pl.BlockSpec((LEN, 128), lambda p: (0, p))
    return pl.pallas_call(
        mix_back_kernel,
        grid=(H // 2,),
        out_shape=[
            jax.ShapeDtypeStruct((TALL, D), jnp.bfloat16),
            jax.ShapeDtypeStruct((LEN, D), jnp.bfloat16),
            jax.ShapeDtypeStruct((LEN, D), jnp.bfloat16),
            jax.ShapeDtypeStruct((H, 1, 768), jnp.float32),
        ],
        in_specs=[
            SMEM_SPEC, SMEM_SPEC, tall, short, short, tall, tall,
            pl.BlockSpec((2, 1, TALL), lambda p: (p, 0, 0)),
            pl.BlockSpec((1, LEN), lambda p: (0, 0)),
            pl.BlockSpec((LEN, 1), lambda p: (0, 0)),
            pl.BlockSpec((2, 1, 512), lambda p: (p, 0, 0)),
        ],
        out_specs=[tall, short, short, pl.BlockSpec((2, 1, 768), lambda p: (p, 0, 0))],
        scratch_shapes=[
            pltpu.VMEM((LEN, TALL), jnp.float32),
            pltpu.VMEM((1, TALL), jnp.float32),
            pltpu.VMEM((2, 128, 384), jnp.float32),
            pltpu.VMEM((2, LEN, TALL), jnp.bfloat16),
            pltpu.VMEM((2, LEN, TALL), jnp.bfloat16),
            pltpu.VMEM((2, 128, 512), jnp.float32),
            pltpu.VMEM((128, TALL), jnp.float32),
        ],
        compiler_params=PARAMS,
        cost_estimate=pl.CostEstimate(flops=16000000000, bytes_accessed=12000000, transcendentals=6300000),
        name="mix_back",
    )(length, far, q, k, v, da, a, lse, row_flags, col_flags, tvec)


GELU_SCALE = 0.7978845608028654
GELU_CUBE = 0.044715


def feed_kernel(place_ref, small_ref, hidden_bias_ref, mix_any, hidden_any, attn_any, *refs):
    pieces = refs[:10]
    (
        resid_out, summed_out, pre_out, next_out, low_out,
        mix_ref, hidden_ref, wo_ref, inner_ref, outer_ref, resid_ref, total_ref, normed_ref,
        pre_ref, next_ref, low_ref, sems, load_sems, store_sems,
    ) = refs[10:]
    loads = [
        pltpu.make_async_copy(mix_any, mix_ref, load_sems.at[0]),
        pltpu.make_async_copy(attn_any.at[3], wo_ref, load_sems.at[1]),
        pltpu.make_async_copy(hidden_any, hidden_ref, load_sems.at[2]),
    ]
    for load in loads:
        load.start()
    fetches = start_fetch(("inner", "outer"), place_ref, pieces, (inner_ref, outer_ref), sems)
    for load in loads:
        load.wait()
    for row in range(0, TALL, HALF):
        rows = slice(row, row + HALF)
        resid = hidden_ref[rows, :] + dot_nn(mix_ref[rows, :], wo_ref[...]) + small_ref[2:3, :]
        resid_ref[rows, :] = resid
        unit, scale = norm_parts(resid)
        normed = unit * small_ref[3:4, :] + small_ref[4:5, :]
        normed_ref[rows, :] = normed.astype(jnp.bfloat16)
        total_ref[rows, :] = normed + small_ref[5:6, :]
    stores = [pltpu.make_async_copy(resid_ref, resid_out, store_sems.at[0])]
    stores[0].start()
    for fetch in fetches:
        fetch.wait()
    for chunk in range(4):
        cols = slice(chunk * D, chunk * D + D)

        def body(step, carry):
            rows = pl.ds(pl.multiple_of(step * HALF, HALF), HALF)
            pre = dot_nn(normed_ref[rows, :], inner_ref[:, cols]) + hidden_bias_ref[:, cols]
            pre_ref[rows, cols] = pre.astype(jnp.bfloat16)
            tanh = jnp.tanh(GELU_SCALE * (pre + GELU_CUBE * (pre * pre * pre)))
            active = (pre * (0.5 + 0.5 * tanh)).astype(jnp.bfloat16)
            total_ref[rows, :] += dot_nn(active, outer_ref[cols, :])
            return carry

        for step in range(4):
            body(step, 0)
        store = pltpu.make_async_copy(
            pre_ref.at[:, cols], pre_out.at[:, cols], store_sems.at[1 + chunk]
        )
        store.start()
        stores.append(store)
    store = pltpu.make_async_copy(total_ref, summed_out, store_sems.at[5])
    store.start()
    stores.append(store)
    for row in range(0, TALL, HALF):
        rows = slice(row, row + HALF)
        unit, scale = norm_parts(total_ref[rows, :])
        following = unit * small_ref[6:7, :] + small_ref[7:8, :]
        next_ref[rows, :] = following
        low_ref[rows, :] = following.astype(jnp.bfloat16)
    for index, (source, target) in enumerate(((next_ref, next_out), (low_ref, low_out))):
        store = pltpu.make_async_copy(source, target, store_sems.at[6 + index])
        store.start()
        stores.append(store)
    for store in stores:
        store.wait()


def feed(place, small, hidden_bias, mixed, hidden, attn, pieces):
    return pl.pallas_call(
        feed_kernel,
        out_shape=[
            jax.ShapeDtypeStruct((TALL, D), jnp.float32),
            jax.ShapeDtypeStruct((TALL, D), jnp.float32),
            jax.ShapeDtypeStruct((TALL, FF), jnp.bfloat16),
            jax.ShapeDtypeStruct((TALL, D), jnp.float32),
            jax.ShapeDtypeStruct((TALL, D), jnp.bfloat16),
        ],
        in_specs=[SMEM_SPEC, VMEM_SPEC, VMEM_SPEC] + [ANY_SPEC] * 13,
        out_specs=[ANY_SPEC] * 5,
        scratch_shapes=[
            pltpu.VMEM((TALL, D), jnp.bfloat16),
            pltpu.VMEM((TALL, D), jnp.float32),
            pltpu.VMEM((D, D), jnp.bfloat16),
            pltpu.VMEM((D, FF), jnp.bfloat16),
            pltpu.VMEM((FF, D), jnp.bfloat16),
            pltpu.VMEM((TALL, D), jnp.float32),
            pltpu.VMEM((TALL, D), jnp.float32),
            pltpu.VMEM((TALL, D), jnp.bfloat16),
            pltpu.VMEM((TALL, FF), jnp.bfloat16),
            pltpu.VMEM((TALL, D), jnp.float32),
            pltpu.VMEM((TALL, D), jnp.bfloat16),
            pltpu.SemaphoreType.DMA((64,)),
            pltpu.SemaphoreType.DMA((3,)),
            pltpu.SemaphoreType.DMA((8,)),
        ],
        compiler_params=PARAMS,
        cost_estimate=pl.CostEstimate(flops=2 * TALL * D * (D + 2 * FF), bytes_accessed=40000000, transcendentals=3000000),
        name="feed",
    )(place, small, hidden_bias, mixed, hidden, attn, *pieces)


def feed_back_kernel(place_ref, small_ref, grad_any, summed_any, resid_any, pre_any, mix_any, attn_any, *refs):
    pieces = refs[:10]
    (
        dresid_out, dmix_out, dwo_out, keep_out, send_out, vec_ref, dhidden_ref,
        grad_ref, summed_ref, resid_ref, pre_ref, mix_ref, wo_ref, inner_ref, outer_ref,
        total_ref, branch_ref, normed_ref, active_ref, dpre_ref, dinner_ref, douter_ref,
        dwo_ref, sems, load_sems, store_sems, block_sems,
    ) = refs[10:]
    proj_ref = branch_ref
    dmix_ref = active_ref
    x, c, z, y = (place_ref[index] for index in range(4))
    load = [
        pltpu.make_async_copy(source, target, load_sems.at[index])
        for index, (source, target) in enumerate(
            (
                (grad_any, grad_ref), (summed_any, summed_ref), (resid_any, resid_ref),
                (pre_any, pre_ref), (mix_any, mix_ref), (attn_any.at[3], wo_ref),
            )
        )
    ]
    for copy in load[:3]:
        copy.start()
    fetches = start_fetch(("inner", "outer"), place_ref, pieces, (inner_ref, outer_ref), sems)
    for copy in load[3:]:
        copy.start()
    for copy in load[:3]:
        copy.wait()
    gain_two_grad = jnp.zeros((1, D), jnp.float32)
    shift_two_grad = jnp.zeros((1, D), jnp.float32)
    bias_two_grad = jnp.zeros((1, D), jnp.float32)
    for row in range(0, TALL, HALF):
        rows = slice(row, row + HALF)
        grad = grad_ref[rows, :]
        unit, scale = norm_parts(summed_ref[rows, :])
        gain_two_grad += jnp.sum(grad * unit, axis=0, keepdims=True)
        shift_two_grad += jnp.sum(grad, axis=0, keepdims=True)
        back = norm_back(unit, scale, grad, small_ref[6:7, :])
        total_ref[rows, :] = back
        low = back.astype(jnp.bfloat16)
        branch_ref[rows, :] = low
        bias_two_grad += jnp.sum(low.astype(jnp.float32), axis=0, keepdims=True)
        unit, scale = norm_parts(resid_ref[rows, :])
        normed_ref[rows, :] = (unit * small_ref[3:4, :] + small_ref[4:5, :]).astype(jnp.bfloat16)
    vec_ref[5:6, :] = bias_two_grad
    vec_ref[6:7, :] = gain_two_grad
    vec_ref[7:8, :] = shift_two_grad
    for copy in fetches + load[3:]:
        copy.wait()
    blocks = []

    def place_block(core, source, target_index):
        sem = block_sems.at[len(blocks)]
        keep = pltpu.make_async_copy(source, keep_out.at[target_index], sem)
        send = pltpu.make_async_copy(source, send_out.at[target_index], sem)

        @pl.when(c == core)
        def _():
            keep.start()

        @pl.when(c != core)
        def _():
            send.start()

        blocks.append(keep)

    for chunk in range(4):
        cols = slice(chunk * D, chunk * D + D)
        bias_grad = jnp.zeros((1, D), jnp.float32)
        for row in range(0, TALL, HALF):
            rows = slice(row, row + HALF)
            pull = dot_nt(branch_ref[rows, :], outer_ref[cols, :])
            pre = pre_ref[rows, cols].astype(jnp.float32)
            square = pre * pre
            tanh = jnp.tanh(GELU_SCALE * pre * (1.0 + GELU_CUBE * square))
            half = 0.5 + 0.5 * tanh
            active_ref[rows, :] = (pre * half).astype(jnp.bfloat16)
            slope = half + (0.5 * GELU_SCALE) * pre * (1.0 - tanh * tanh) * (
                1.0 + (3.0 * GELU_CUBE) * square
            )
            dpre = (pull * slope).astype(jnp.bfloat16)
            dpre_ref[rows, :] = dpre
            bias_grad += jnp.sum(dpre.astype(jnp.float32), axis=0, keepdims=True)
            total_ref[rows, :] += dot_nt(dpre, inner_ref[:, cols])
        dhidden_ref[:, cols] = bias_grad
        douter_ref[cols, :] = dot_tn(active_ref[...], branch_ref[...]).astype(jnp.bfloat16)
        dinner_ref[:, cols] = dot_tn(normed_ref[...], dpre_ref[...]).astype(jnp.bfloat16)
        for owner in range(8):
            place_block(
                chunk % 2,
                dinner_ref.at[owner * ROWS : owner * ROWS + ROWS, cols],
                ((chunk // 2) ^ x, (owner % 2) ^ y, ((owner // 2) - z) & 3, 0),
            )
        for strip in range(8):
            quarter = strip % 4
            start = chunk * D + strip * ROWS
            place_block(
                quarter % 2,
                douter_ref.at[start : start + ROWS, :],
                ((quarter // 2) ^ x, (strip // 4) ^ y, (chunk - z) & 3, 1),
            )
    gain_one_grad = jnp.zeros((1, D), jnp.float32)
    shift_one_grad = jnp.zeros((1, D), jnp.float32)
    bias_o_grad = jnp.zeros((1, D), jnp.float32)
    for row in range(0, TALL, HALF):
        rows = slice(row, row + HALF)
        grad = total_ref[rows, :]
        unit, scale = norm_parts(resid_ref[rows, :])
        gain_one_grad += jnp.sum(grad * unit, axis=0, keepdims=True)
        shift_one_grad += jnp.sum(grad, axis=0, keepdims=True)
        back = norm_back(unit, scale, grad, small_ref[3:4, :])
        grad_ref[rows, :] = back
        low = back.astype(jnp.bfloat16)
        proj_ref[rows, :] = low
        bias_o_grad += jnp.sum(low.astype(jnp.float32), axis=0, keepdims=True)
        dmix_ref[rows, :] = dot_nt(low, wo_ref[...]).astype(jnp.bfloat16)
    dwo_ref[...] = dot_tn(mix_ref[...], proj_ref[...]).astype(jnp.bfloat16)
    vec_ref[0:2, :] = jnp.zeros((2, D), jnp.float32)
    vec_ref[2:3, :] = bias_o_grad
    vec_ref[3:4, :] = gain_one_grad
    vec_ref[4:5, :] = shift_one_grad
    stores = [
        pltpu.make_async_copy(source, target, store_sems.at[index])
        for index, (source, target) in enumerate(
            ((grad_ref, dresid_out), (dmix_ref, dmix_out), (dwo_ref, dwo_out))
        )
    ]
    for store in stores:
        store.start()
    for copy in blocks + stores:
        copy.wait()


def feed_back(place, small, grad, summed, resid, pre, mixed, attn, pieces):
    blocks = jax.ShapeDtypeStruct((2, 2, 4, 2, ROWS, D), jnp.bfloat16)
    return pl.pallas_call(
        feed_back_kernel,
        out_shape=[
            jax.ShapeDtypeStruct((TALL, D), jnp.float32),
            jax.ShapeDtypeStruct((TALL, D), jnp.bfloat16),
            jax.ShapeDtypeStruct((D, D), jnp.bfloat16),
            blocks,
            blocks,
            jax.ShapeDtypeStruct((8, D), jnp.float32),
            jax.ShapeDtypeStruct((1, FF), jnp.float32),
        ],
        in_specs=[SMEM_SPEC, VMEM_SPEC] + [ANY_SPEC] * 16,
        out_specs=[ANY_SPEC] * 5 + [VMEM_SPEC] * 2,
        scratch_shapes=[
            pltpu.VMEM((TALL, D), jnp.float32),
            pltpu.VMEM((TALL, D), jnp.float32),
            pltpu.VMEM((TALL, D), jnp.float32),
            pltpu.VMEM((TALL, FF), jnp.bfloat16),
            pltpu.VMEM((TALL, D), jnp.bfloat16),
            pltpu.VMEM((D, D), jnp.bfloat16),
            pltpu.VMEM((D, FF), jnp.bfloat16),
            pltpu.VMEM((FF, D), jnp.bfloat16),
            pltpu.VMEM((TALL, D), jnp.float32),
            pltpu.VMEM((TALL, D), jnp.bfloat16),
            pltpu.VMEM((TALL, D), jnp.bfloat16),
            pltpu.VMEM((TALL, D), jnp.bfloat16),
            pltpu.VMEM((TALL, D), jnp.bfloat16),
            pltpu.VMEM((D, FF), jnp.bfloat16),
            pltpu.VMEM((FF, D), jnp.bfloat16),
            pltpu.VMEM((D, D), jnp.bfloat16),
            pltpu.SemaphoreType.DMA((64,)),
            pltpu.SemaphoreType.DMA((6,)),
            pltpu.SemaphoreType.DMA((3,)),
            pltpu.SemaphoreType.DMA((64,)),
        ],
        compiler_params=PARAMS,
        cost_estimate=pl.CostEstimate(flops=4 * TALL * D * (D + 2 * FF), bytes_accessed=60000000, transcendentals=3000000),
        name="feed_back",
    )(place, small, grad, summed, resid, pre, mixed, attn, *pieces)


def weight_back_kernel(place_ref, low_ref, dq_ref, dk_ref, dv_ref, dwo_ref, keep_out, send_out, vec_ref, grads_ref, sems):
    x, c, z, y = (place_ref[index] for index in range(4))
    blocks = []

    def place_matrix(source, quarter):
        for owner in range(8):
            index = ((quarter // 2) ^ x, (owner % 2) ^ y, ((owner // 2) - z) & 3, 0)
            part = source.at[owner * ROWS : owner * ROWS + ROWS, :]
            sem = sems.at[len(blocks)]
            keep = pltpu.make_async_copy(part, keep_out.at[index], sem)
            send = pltpu.make_async_copy(part, send_out.at[index], sem)

            @pl.when(c == quarter % 2)
            def _():
                keep.start()

            @pl.when(c != quarter % 2)
            def _():
                send.start()

            blocks.append(keep)

    place_matrix(dwo_ref, 3)
    grads_ref[0] = dot_tn(low_ref[...], dq_ref[...]).astype(jnp.bfloat16)
    place_matrix(grads_ref.at[0], 0)
    grads_ref[1] = dot_tn(low_ref[:LEN, :], dk_ref[...]).astype(jnp.bfloat16)
    place_matrix(grads_ref.at[1], 1)
    grads_ref[2] = dot_tn(low_ref[:LEN, :], dv_ref[...]).astype(jnp.bfloat16)
    place_matrix(grads_ref.at[2], 2)
    vec_ref[0:1, :] = jnp.sum(dq_ref[...].astype(jnp.float32), axis=0, keepdims=True)
    vec_ref[1:2, :] = jnp.sum(dv_ref[...].astype(jnp.float32), axis=0, keepdims=True)
    for block in blocks:
        block.wait()


def weight_back(place, low, dq, dk, dv, dwo):
    blocks = jax.ShapeDtypeStruct((2, 2, 4, 1, ROWS, D), jnp.bfloat16)
    return pl.pallas_call(
        weight_back_kernel,
        out_shape=[blocks, blocks, jax.ShapeDtypeStruct((2, D), jnp.float32)],
        in_specs=[SMEM_SPEC] + [VMEM_SPEC] * 5,
        out_specs=[ANY_SPEC] * 2 + [VMEM_SPEC],
        scratch_shapes=[
            pltpu.VMEM((3, D, D), jnp.bfloat16),
            pltpu.SemaphoreType.DMA((32,)),
        ],
        compiler_params=PARAMS,
        cost_estimate=pl.CostEstimate(flops=2 * 2048 * D * D, bytes_accessed=12000000, transcendentals=0),
        name="weight_back",
    )(place, low, dq, dk, dv, dwo)


def input_back_kernel(dq_ref, dk_ref, dv_ref, w_ref, dresid_ref, first_ref, second_ref):
    for row in range(0, LEN, HALF):
        rows = slice(row, row + HALF)
        first_ref[rows, :] = (
            dresid_ref[rows, :]
            + dot_nt(dq_ref[rows, :], w_ref[0])
            + dot_nt(dk_ref[rows, :], w_ref[1])
            + dot_nt(dv_ref[rows, :], w_ref[2])
        )
        rest = slice(LEN + row, LEN + row + HALF)
        second_ref[rows, :] = dresid_ref[rest, :] + dot_nt(dq_ref[rest, :], w_ref[0])


def input_back(dq, dk, dv, attn, dresid):
    half = jax.ShapeDtypeStruct((LEN, D), jnp.float32)
    return pl.pallas_call(
        input_back_kernel,
        out_shape=[half, half],
        in_specs=[VMEM_SPEC] * 5,
        out_specs=[VMEM_SPEC] * 2,
        compiler_params=PARAMS,
        cost_estimate=pl.CostEstimate(flops=2 * 2048 * D * D, bytes_accessed=16000000, transcendentals=0),
        name="input_back",
    )(dq, dk, dv, attn, dresid)


def bias_vectors(table):
    lane = jnp.arange(512, dtype=jnp.int32)
    offset = jnp.where(lane < 384, 128 - lane, 640 - lane)
    onehot = bucket_of(offset)[:, None] == jnp.arange(NB, dtype=jnp.int32)[None, :]
    near = jnp.dot(table, onehot.astype(jnp.float32).T, precision=lax.Precision.HIGHEST)
    return (near[:, None, :], jnp.stack([table[:, 15], table[:, 31]], axis=1), onehot)


def bucket_of(offset):
    distance = jnp.abs(offset)
    far_bucket = jnp.full(distance.shape, 8, jnp.int32)
    for exponent in range(1, 8):
        far_bucket = far_bucket + (distance * distance >= 64 * 2**exponent).astype(jnp.int32)
    near_or_far = jnp.where(distance < 8, distance, far_bucket)
    return near_or_far + NB // 2 * (offset > 0).astype(jnp.int32)


def table_grad(sums, onehot):
    near = jnp.dot(
        sums[:, 0, :512],
        jnp.roll(onehot.astype(jnp.float32), 127, axis=0),
        precision=lax.Precision.HIGHEST,
    )
    low = jnp.sum(sums[:, 0, 512:640], axis=1)
    high = jnp.sum(sums[:, 0, 640:], axis=1)
    return near.at[:, 15].add(low).at[:, 31].add(high)

def fetch_forward(shards):
    low = tuple(shard.astype(jnp.bfloat16) for shard in shards)
    return (
        lax.all_gather(low[0], "fsdp", axis=1, tiled=True),
        lax.all_gather(low[1], "fsdp", axis=0, tiled=True),
        lax.all_gather(low[2], "fsdp", axis=0, tiled=True),
    )


def reduce_layer(grads):
    owned = tuple(
        lax.psum_scatter(
            grad.astype(jnp.bfloat16), "fsdp", scatter_dimension=axis, tiled=True
        ).astype(jnp.float32)
        for grad, axis in zip(grads, (1, 0, 0))
    )
    return lax.psum(owned, "dp")


def forward_layer(hidden_c, hidden_q, weights, lengths, flag_rows, onehot):
    attn_w, inner_w, outer_w, small_w = weights
    pieces, hidden_bias, bias_table = unpack(small_w.astype(jnp.float32))
    bias_q, bias_v, bias_o, gain_one, shift_one, bias_two, gain_two, shift_two = pieces
    table_low = bias_table.astype(jnp.bfloat16)
    low_c = hidden_c.astype(jnp.bfloat16)
    low_q = hidden_q.astype(jnp.bfloat16)
    projected = jnp.einsum("td,sde->ste", low_c, attn_w[:3], preferred_element_type=jnp.float32)
    query_c = (projected[0] + bias_q).astype(jnp.bfloat16)
    key_rows = projected[1].astype(jnp.bfloat16)
    value_rows = (projected[2] + bias_v).astype(jnp.bfloat16)
    query_q = (jnp.dot(low_q, attn_w[0], preferred_element_type=jnp.float32) + bias_q).astype(
        jnp.bfloat16
    )
    mixed_c, mixed_q, lse_c, lse_q = lax.map(
        partial(attend_slot, onehot, table_low),
        (
            to_heads(query_c),
            to_heads(query_q),
            to_heads(key_rows),
            to_heads(value_rows),
            lengths,
            flag_rows,
        ),
    )
    mixed_c = mixed_c.reshape(-1, D)
    mixed_q = mixed_q.reshape(-1, D)
    outputs = []
    kept = []
    for hidden_in, mixed in ((hidden_c, mixed_c), (hidden_q, mixed_q)):
        resid = hidden_in + jnp.dot(mixed, attn_w[3], preferred_element_type=jnp.float32) + bias_o
        normed = layer_norm(resid, gain_one, shift_one)
        pre_act = (
            jnp.dot(normed.astype(jnp.bfloat16), inner_w, preferred_element_type=jnp.float32)
            + hidden_bias
        )
        active = jax.nn.gelu(pre_act, approximate=True).astype(jnp.bfloat16)
        summed = normed + jnp.dot(active, outer_w, preferred_element_type=jnp.float32) + bias_two
        outputs.append(layer_norm(summed, gain_two, shift_two))
        kept.append((resid, summed, pre_act))
    saved = (
        hidden_c,
        hidden_q,
        query_c,
        query_q,
        key_rows,
        value_rows,
        lse_c,
        lse_q,
        mixed_c,
        mixed_q,
        kept[0],
        kept[1],
    )
    return (outputs[0], outputs[1], saved)


def backward_layer(saved, weights, grad_c, grad_q, lengths, flag_rows, onehot):
    attn_w, inner_w, outer_w, small_w = weights
    pieces, hidden_bias, bias_table = unpack(small_w.astype(jnp.float32))
    bias_q, bias_v, bias_o, gain_one, shift_one, bias_two, gain_two, shift_two = pieces
    table_low = bias_table.astype(jnp.bfloat16)
    (
        hidden_c,
        hidden_q,
        query_c,
        query_q,
        key_rows,
        value_rows,
        lse_c,
        lse_q,
        mixed_c,
        mixed_q,
        kept_c,
        kept_q,
    ) = saved
    gelu_tanh = partial(jax.nn.gelu, approximate=True)
    grad_outer = jnp.zeros(outer_w.shape, jnp.float32)
    grad_inner = jnp.zeros(inner_w.shape, jnp.float32)
    grad_attn_out = jnp.zeros((D, D), jnp.float32)
    grad_bias_two = jnp.zeros((D,), jnp.float32)
    grad_hidden_bias = jnp.zeros((FF,), jnp.float32)
    grad_bias_o = jnp.zeros((D,), jnp.float32)
    grad_gain_one = jnp.zeros((D,), jnp.float32)
    grad_shift_one = jnp.zeros((D,), jnp.float32)
    grad_gain_two = jnp.zeros((D,), jnp.float32)
    grad_shift_two = jnp.zeros((D,), jnp.float32)
    residual_grads = []
    mix_grads = []
    for kept_rows, grad_out, mixed in ((kept_c, grad_c, mixed_c), (kept_q, grad_q, mixed_q)):
        resid, summed, pre_act = kept_rows
        normed, norm_one_back = jax.vjp(layer_norm, resid, gain_one, shift_one)
        unused_out, norm_two_back = jax.vjp(layer_norm, summed, gain_two, shift_two)
        grad_summed, grad_g2, grad_s2 = norm_two_back(grad_out)
        grad_gain_two = grad_gain_two + grad_g2
        grad_shift_two = grad_shift_two + grad_s2
        grad_branch = grad_summed.astype(jnp.bfloat16)
        grad_bias_two = grad_bias_two + jnp.sum(grad_branch.astype(jnp.float32), axis=0)
        active, gelu_back = jax.vjp(gelu_tanh, pre_act)
        grad_outer = grad_outer + jnp.einsum(
            "tf,td->fd",
            active.astype(jnp.bfloat16),
            grad_branch,
            preferred_element_type=jnp.float32,
        )
        grad_active = jnp.einsum(
            "td,fd->tf", grad_branch, outer_w, preferred_element_type=jnp.float32
        )
        grad_pre = gelu_back(grad_active)[0].astype(jnp.bfloat16)
        grad_hidden_bias = grad_hidden_bias + jnp.sum(grad_pre.astype(jnp.float32), axis=0)
        grad_inner = grad_inner + jnp.einsum(
            "td,tf->df", normed.astype(jnp.bfloat16), grad_pre, preferred_element_type=jnp.float32
        )
        grad_normed = grad_summed + jnp.einsum(
            "tf,df->td", grad_pre, inner_w, preferred_element_type=jnp.float32
        )
        grad_resid, grad_g1, grad_s1 = norm_one_back(grad_normed)
        grad_gain_one = grad_gain_one + grad_g1
        grad_shift_one = grad_shift_one + grad_s1
        grad_proj = grad_resid.astype(jnp.bfloat16)
        grad_bias_o = grad_bias_o + jnp.sum(grad_proj.astype(jnp.float32), axis=0)
        grad_attn_out = grad_attn_out + jnp.einsum(
            "td,te->de", mixed, grad_proj, preferred_element_type=jnp.float32
        )
        mix_grads.append(
            jnp.einsum(
                "te,de->td", grad_proj, attn_w[3], preferred_element_type=jnp.float32
            ).astype(jnp.bfloat16)
        )
        residual_grads.append(grad_resid)
    grad_query_c, grad_query_q, grad_keys, grad_values, grad_table = lax.map(
        partial(attend_back, onehot, table_low),
        (
            to_heads(query_c),
            to_heads(query_q),
            to_heads(key_rows),
            to_heads(value_rows),
            lengths,
            flag_rows,
            lse_c,
            lse_q,
            to_heads(mix_grads[0]),
            to_heads(mix_grads[1]),
        ),
    )
    grad_table = jnp.sum(grad_table, axis=0)
    low_query_c = grad_query_c.reshape(-1, D).astype(jnp.bfloat16)
    low_query_q = grad_query_q.reshape(-1, D).astype(jnp.bfloat16)
    low_keys = grad_keys.reshape(-1, D).astype(jnp.bfloat16)
    low_values = grad_values.reshape(-1, D).astype(jnp.bfloat16)
    low_c = hidden_c.astype(jnp.bfloat16)
    low_q = hidden_q.astype(jnp.bfloat16)
    stacked_grads = jnp.stack([low_query_c, low_keys, low_values])
    grad_qkv = jnp.einsum("td,ste->sde", low_c, stacked_grads, preferred_element_type=jnp.float32)
    grad_wq = grad_qkv[0] + jnp.einsum(
        "td,te->de", low_q, low_query_q, preferred_element_type=jnp.float32
    )
    grad_attn = jnp.stack([grad_wq, grad_qkv[1], grad_qkv[2], grad_attn_out])
    grad_bias_q = jnp.sum(low_query_c.astype(jnp.float32), axis=0) + jnp.sum(
        low_query_q.astype(jnp.float32), axis=0
    )
    grad_bias_v = jnp.sum(low_values.astype(jnp.float32), axis=0)
    grad_content = residual_grads[0] + jnp.einsum(
        "ste,sde->td", stacked_grads, attn_w[:3], preferred_element_type=jnp.float32
    )
    grad_query_in = residual_grads[1] + jnp.einsum(
        "te,de->td", low_query_q, attn_w[0], preferred_element_type=jnp.float32
    )
    grad_small = jnp.concatenate(
        [
            grad_bias_q,
            grad_bias_v,
            grad_bias_o,
            grad_gain_one,
            grad_shift_one,
            grad_bias_two,
            grad_gain_two,
            grad_shift_two,
            grad_hidden_bias,
            grad_table.reshape(-1),
        ]
    )
    return (grad_content, grad_query_in, (grad_attn, grad_inner, grad_outer, grad_small))


def adam_update(master, first, second, grad, rate):
    first_new = BETA_ONE * first + (1.0 - BETA_ONE) * grad
    second_new = BETA_TWO * second + (1.0 - BETA_TWO) * grad * grad
    first_hat = first_new / (1.0 - BETA_ONE**STEP)
    second_hat = second_new / (1.0 - BETA_TWO**STEP)
    master_new = master - rate * (
        first_hat / (jnp.sqrt(second_hat) + ADAM_EPS) + WEIGHT_DECAY * master
    )
    return (master_new, first_new, second_new)


def per_device(
    content,
    query,
    lengths,
    predicted,
    content_cot,
    query_cot,
    attn_master,
    attn_first,
    attn_second,
    inner_master,
    inner_first,
    inner_second,
    outer_master,
    outer_first,
    outer_second,
    small_master,
    small_first,
    small_second,
):
    masters = (attn_master, inner_master, outer_master, small_master)
    slot_count = lengths.shape[0]
    flag_rows = predicted.reshape(slot_count, LEN)
    onehot = bucket_onehot()
    hidden_c = content.astype(jnp.float32)
    hidden_q = query.astype(jnp.float32)
    kept_weights = []
    saved_layers = []
    small_all = lax.all_gather(
        small_master.astype(jnp.bfloat16), "fsdp", axis=1, tiled=True
    )
    for layer_index in range(LAYERS):
        shards = tuple((master[layer_index] for master in masters[:3]))
        gathered = fetch_forward(shards) + (small_all[layer_index],)
        kept_weights.append(gathered)
        hidden_c, hidden_q, saved = forward_layer(
            hidden_c, hidden_q, gathered, lengths, flag_rows, onehot
        )
        saved_layers.append(saved)
    position = jnp.arange(LEN, dtype=jnp.int32)
    valid_rows = (position[None, :] < lengths[:, None]).reshape(-1, 1).astype(jnp.float32)
    grad_c = content_cot.astype(jnp.float32) * valid_rows
    grad_q = query_cot.astype(jnp.float32) * valid_rows
    layer_grads = [None] * LAYERS
    small_grads = [None] * LAYERS
    for layer_index in reversed(range(LAYERS)):
        grad_c, grad_q, local_grads = backward_layer(
            saved_layers[layer_index],
            kept_weights[layer_index],
            grad_c,
            grad_q,
            lengths,
            flag_rows,
            onehot,
        )
        small_grads[layer_index] = local_grads[3]
        layer_grads[layer_index] = reduce_layer(local_grads[:3])
    small_sum = lax.psum(jnp.stack(small_grads), ("dp", "fsdp"))
    owned = small_master.shape[1]
    small_own = lax.dynamic_slice_in_dim(
        small_sum, lax.axis_index("fsdp") * owned, owned, 1
    )
    reduced = tuple(
        (
            jnp.stack([layer_grads[layer_index][member] for layer_index in range(LAYERS)])
            for member in range(3)
        )
    ) + (small_own,)
    attn_new = adam_update(attn_master, attn_first, attn_second, reduced[0], ATTENTION_RATE)
    inner_new = adam_update(inner_master, inner_first, inner_second, reduced[1], FEED_RATE)
    outer_new = adam_update(outer_master, outer_first, outer_second, reduced[2], FEED_RATE)
    small_new = adam_update(small_master, small_first, small_second, reduced[3], SMALL_RATE)
    return (
        hidden_c.astype(jnp.bfloat16),
        hidden_q.astype(jnp.bfloat16),
        grad_c,
        grad_q,
        attn_new[0],
        attn_new[1],
        attn_new[2],
        inner_new[0],
        inner_new[1],
        inner_new[2],
        outer_new[0],
        outer_new[1],
        outer_new[2],
        small_new[0],
        small_new[1],
        small_new[2],
    )


def own_quarter(kind, shard, quarter):
    if kind == "attn":
        part = lax.dynamic_index_in_dim(shard, quarter, 0, keepdims=False)
    elif kind == "inner":
        part = lax.dynamic_slice_in_dim(shard, quarter * D, D, 1)
    else:
        part = lax.dynamic_slice_in_dim(shard, quarter * ROWS, ROWS, 0)
    return part.astype(jnp.bfloat16)


def after(value, *others):
    return lax.optimization_barrier((value, others))[0]


def own_group(kinds, shards, place):
    quarter = place[0] * 2 + place[1]
    return jnp.stack([own_quarter(kind, shard, quarter) for kind, shard in zip(kinds, shards)])


def gather_column(own):
    return jnp.stack([own] + [shift_z(own, step) for step in (1, 2, 3)])


def gather_sides(column):
    return (swap_x(column), swap_y(column))


def gather_corners(from_x, from_y):
    return (swap_x(from_y[:2]), swap_y(from_x[2:]))


def gather_small(shard, place):
    z, y = place[2], place[3]
    column = jnp.stack([shift_z(shard, step) for step in (3, 2, 1)] + [shard])
    other = swap_y(column)
    pairs = jnp.where(y == 0, jnp.stack([column, other], 1), jnp.stack([other, column], 1))
    twice = jnp.concatenate([pairs, pairs])
    whole = lax.dynamic_slice_in_dim(twice, 3 - z, 4, 0)
    return whole.transpose(2, 0, 1, 3).reshape(shard.shape[0], -1)


def sum_small(value):
    value = value + swap_core(value)
    value = value + swap_x(value)
    value = value + swap_y(value)
    return value + shift_z(value, 1) + shift_z(value, 2) + shift_z(value, 3)


def add_low(*values):
    total = values[0].astype(jnp.float32)
    for value in values[1:]:
        total = total + value.astype(jnp.float32)
    return total.astype(jnp.bfloat16)


def reduce_core(keep, got):
    return add_low(keep, got)


def reduce_corners(both):
    corner = both[1, 1]
    return (swap_x(corner[:2]), swap_y(corner[2:]))


def reduce_sides(both, corners):
    by_x, by_y = corners
    for_y = jnp.concatenate([add_low(both[0, 1, :2], by_x), both[0, 1, 2:]])
    for_x = jnp.concatenate([both[1, 0, :2], add_low(both[1, 0, 2:], by_y)])
    return (swap_x(for_x), swap_y(for_y))


def reduce_column(both, sides):
    return add_low(both[0, 0], *sides)


def reduce_shifts(column):
    return tuple(shift_z(column[step], step) for step in (1, 2, 3))


def reduce_total(column, shifts):
    total = column[0].astype(jnp.float32)
    for value in shifts:
        total = total + value.astype(jnp.float32)
    return total.astype(jnp.bfloat16)


def share_quarters(own, place):
    x, c = place[0], place[1]
    pair = jnp.stack([own, swap_x(own)])
    other = swap_core(pair)
    cores = jnp.where(c == 0, jnp.stack([pair, other], 1), jnp.stack([other, pair], 1))
    sides = jnp.where(x == 0, cores, cores[::-1])
    return sides.reshape((4,) + own.shape)


def shard_grad(kind, quarters):
    four = quarters.astype(jnp.float32)
    if kind == "attn":
        return four
    if kind == "inner":
        return four.transpose(1, 0, 2).reshape(ROWS, FF)
    return four.reshape(4 * ROWS, D)


def small_parts(vectors):
    values = vectors.astype(jnp.float32)
    return (
        values[: 8 * D].reshape(8, D),
        values[8 * D : 8 * D + FF].reshape(1, FF),
        bias_vectors(values[8 * D + FF :].reshape(H, NB)),
    )


def per_device_fast(
    content,
    query,
    lengths,
    predicted,
    content_cot,
    query_cot,
    attn_master,
    attn_first,
    attn_second,
    inner_master,
    inner_first,
    inner_second,
    outer_master,
    outer_first,
    outer_second,
    small_master,
    small_first,
    small_second,
):
    place_parts = my_place()
    place = jnp.stack(place_parts).astype(jnp.int32)
    small_all = gather_small(small_master.astype(jnp.bfloat16), place_parts)
    own_a0, own_a1 = (own_group(("attn",), (attn_master[l],), place_parts) for l in range(2))
    own_f0, own_f1 = (
        own_group(("inner", "outer"), (inner_master[l], outer_master[l]), place_parts)
        for l in range(2)
    )
    col_a0 = gather_column(own_a0)
    sides_a0 = gather_sides(col_a0)
    col_f0 = gather_column(after(own_f0, col_a0))
    corners_a0 = gather_corners(*sides_a0)
    sides_f0 = gather_sides(after(col_f0, *sides_a0))
    mine_a0 = (col_a0,) + sides_a0 + corners_a0
    pieces_a0 = mine_a0 + tuple(swap_core(piece) for piece in mine_a0)
    col_a1 = gather_column(after(own_a1, col_f0))
    row_flags = predicted.reshape(1, LEN).astype(jnp.float32)
    col_flags = predicted.reshape(LEN, 1).astype(jnp.float32)
    low = jnp.concatenate([content, query])
    hidden = low.astype(jnp.float32)
    kept = []
    small0, hidden_bias0, (tvec0, far0, onehot) = small_parts(small_all[0])
    small1, hidden_bias1, (tvec1, far1, onehot) = small_parts(small_all[1])
    q0, k0, v0, attn0 = project(place, low, small0, pieces_a0)
    col_f1 = gather_column(after(own_f1, col_a1, q0))
    corners_f0 = gather_corners(*sides_f0)
    sides_a1 = gather_sides(after(col_a1, q0, *sides_f0))
    q0_late = after(q0, *sides_f0)
    mixed0, lse0 = mix(lengths, far0, tvec0, q0_late, k0, v0, row_flags, col_flags)
    mine_f0 = (col_f0,) + sides_f0 + corners_f0
    pieces_f0 = mine_f0 + tuple(swap_core(piece) for piece in mine_f0)
    corners_a1 = gather_corners(*sides_a1)
    sides_f1 = gather_sides(after(col_f1, mixed0, *sides_a1))
    mixed0_late = after(mixed0, *sides_a1)
    resid0, summed0, pre0, hidden1, low1 = feed(
        place, small0, hidden_bias0, mixed0_late, hidden, attn0, pieces_f0
    )
    mine_a1 = (col_a1,) + sides_a1 + corners_a1
    pieces_a1 = mine_a1 + tuple(swap_core(piece) for piece in mine_a1)
    q1, k1, v1, attn1 = project(place, low1, small1, pieces_a1)
    corners_f1 = gather_corners(*sides_f1)
    q1_late = after(q1, *sides_f1)
    mixed1, lse1 = mix(lengths, far1, tvec1, q1_late, k1, v1, row_flags, col_flags)
    mine_f1 = (col_f1,) + sides_f1 + corners_f1
    pieces_f1 = mine_f1 + tuple(swap_core(piece) for piece in mine_f1)
    resid1, summed1, pre1, unused, low_out = feed(
        place, small1, hidden_bias1, mixed1, hidden1, attn1, pieces_f1
    )
    valid = (jnp.arange(LEN, dtype=jnp.int32) < lengths[0])[:, None].astype(jnp.float32)
    grad = jnp.concatenate(
        [content_cot.astype(jnp.float32) * valid, query_cot.astype(jnp.float32) * valid]
    )
    dresid1, dmix1, dwo1, keep_f1, send_f1, vec_f1, dhidden1 = feed_back(
        place, small1, grad, summed1, resid1, pre1, mixed1, attn1, pieces_f1
    )
    get_f1 = swap_core(send_f1)
    dq1, dk1, dv1, table1 = mix_back(
        lengths, far1, tvec1, q1, k1, v1, dmix1, mixed1, lse1, row_flags, col_flags
    )
    both_f1 = reduce_core(keep_f1, after(get_f1, dq1))
    by_f1 = reduce_corners(both_f1)
    keep_a1, send_a1, vec_a1 = weight_back(place, low1, after(dq1, get_f1), dk1, dv1, dwo1)
    get_a1 = swap_core(send_a1)
    grad_c1, grad_q1 = input_back(after(dq1, keep_a1), dk1, dv1, attn1, dresid1)
    both_a1 = reduce_core(keep_a1, after(get_a1, grad_c1))
    by_a1 = reduce_corners(both_a1)
    sides_rf1 = reduce_sides(both_f1, after(by_f1, grad_c1))
    grad = after(jnp.concatenate([grad_c1, grad_q1]), by_f1, get_a1)
    dresid0, dmix0, dwo0, keep_f0, send_f0, vec_f0, dhidden0 = feed_back(
        place, small0, grad, summed0, resid0, pre0, mixed0, attn0, pieces_f0
    )
    get_f0 = swap_core(send_f0)
    column_f1 = reduce_column(both_f1, after(sides_rf1, dmix0))
    shifts_f1 = reduce_shifts(column_f1)
    sides_ra1 = reduce_sides(both_a1, after(by_a1, dmix0))
    dmix0_late = after(dmix0, by_a1, sides_rf1)
    dq0, dk0, dv0, table0 = mix_back(
        lengths, far0, tvec0, q0, k0, v0, dmix0_late, mixed0, lse0, row_flags, col_flags
    )
    both_f0 = reduce_core(keep_f0, after(get_f0, dq0))
    by_f0 = reduce_corners(both_f0)
    column_a1 = reduce_column(both_a1, after(sides_ra1, dq0))
    keep_a0, send_a0, vec_a0 = weight_back(
        place, low, after(dq0, shifts_f1, get_f0, sides_ra1), dk0, dv0, dwo0
    )
    get_a0 = swap_core(send_a0)
    shifts_a1 = reduce_shifts(after(column_a1, keep_a0))
    own_gf1 = reduce_total(column_f1, shifts_f1)
    four_f1 = share_quarters(after(own_gf1, keep_a0), place_parts)
    sides_rf0 = reduce_sides(both_f0, after(by_f0, keep_a0))
    grad_c, grad_q = input_back(after(dq0, keep_a0), dk0, dv0, attn0, dresid0)
    both_a0 = reduce_core(keep_a0, get_a0)
    by_a0 = reduce_corners(both_a0)
    own_ga1 = reduce_total(column_a1, shifts_a1)
    four_a1 = share_quarters(own_ga1, place_parts)
    sides_ra0 = reduce_sides(both_a0, by_a0)
    column_f0 = reduce_column(both_f0, sides_rf0)
    four_f0 = share_quarters(reduce_total(column_f0, reduce_shifts(column_f0)), place_parts)
    column_a0 = reduce_column(both_a0, sides_ra0)
    four_a0 = share_quarters(reduce_total(column_a0, reduce_shifts(column_a0)), place_parts)
    owned = [
        (
            shard_grad("attn", attn_four[:, 0]),
            shard_grad("inner", feed_four[:, 0]),
            shard_grad("outer", feed_four[:, 1]),
        )
        for attn_four, feed_four in ((four_a0, four_f0), (four_a1, four_f1))
    ]
    small_grads = [
        jnp.concatenate(
            [
                attn_vec.reshape(-1),
                feed_vec[2:].reshape(-1),
                dhidden.reshape(-1),
                table_grad(table_sums, onehot).reshape(-1),
            ]
        )
        for attn_vec, feed_vec, dhidden, table_sums in (
            (vec_a0, vec_f0, dhidden0, table0),
            (vec_a1, vec_f1, dhidden1, table1),
        )
    ]
    small_sum = sum_small(jnp.stack(small_grads))
    size = small_master.shape[1]
    small_own = lax.dynamic_slice_in_dim(small_sum, lax.axis_index("fsdp") * size, size, 1)
    reduced = tuple(
        jnp.stack([owned[layer][member] for layer in range(LAYERS)]) for member in range(3)
    )
    attn_new = adam_update(attn_master, attn_first, attn_second, reduced[0], ATTENTION_RATE)
    inner_new = adam_update(inner_master, inner_first, inner_second, reduced[1], FEED_RATE)
    outer_new = adam_update(outer_master, outer_first, outer_second, reduced[2], FEED_RATE)
    small_new = adam_update(small_master, small_first, small_second, small_own, SMALL_RATE)
    return (
        (low_out[:LEN], low_out[LEN:], grad_c, grad_q) + attn_new + inner_new + outer_new + small_new
    )


def solution(mesh):
    placed = (
        P(("dp", "fsdp"), None),
        P(("dp", "fsdp"), None),
        P(("dp", "fsdp")),
        P(("dp", "fsdp")),
        P(("dp", "fsdp"), None),
        P(("dp", "fsdp"), None),
        P(None, None, "fsdp", None),
        P(None, None, "fsdp", None),
        P(None, None, "fsdp", None),
        P(None, "fsdp", None),
        P(None, "fsdp", None),
        P(None, "fsdp", None),
        P(None, "fsdp", None),
        P(None, "fsdp", None),
        P(None, "fsdp", None),
        P(None, "fsdp"),
        P(None, "fsdp"),
        P(None, "fsdp"),
    )
    fast = tuple(mesh.shape.values()) == (4, 8)
    return jax.shard_map(
        per_device_fast if fast else per_device,
        mesh=mesh,
        in_specs=placed,
        out_specs=(
            P(("dp", "fsdp"), None),
            P(("dp", "fsdp"), None),
            P(("dp", "fsdp"), None),
            P(("dp", "fsdp"), None),
            P(None, None, "fsdp", None),
            P(None, None, "fsdp", None),
            P(None, None, "fsdp", None),
            P(None, "fsdp", None),
            P(None, "fsdp", None),
            P(None, "fsdp", None),
            P(None, "fsdp", None),
            P(None, "fsdp", None),
            P(None, "fsdp", None),
            P(None, "fsdp"),
            P(None, "fsdp"),
            P(None, "fsdp"),
        ),
        check_vma=False,
    )
```

```python
from functools import partial

import jax
import jax.numpy as jnp
from jax import lax
from jax.experimental import pallas as pl
from jax.experimental.pallas import tpu as pltpu
from jax.sharding import PartitionSpec as P

D = 768
H = 12
DH = 64
FF = 3072
LEN = 512
NB = 32
LAYERS = 2
STEP = 10


NORM_EPS = 1e-05
MASKED = -1000000000.0
BETA_ONE = 0.9
BETA_TWO = 0.999
ATTENTION_RATE = 0.1
FEED_RATE = 0.02
SMALL_RATE = 0.4
WEIGHT_DECAY = 0.01
ADAM_EPS = 1e-08
SCORE_SCALE = 0.125


def layer_norm(values, gain, shift):
    centre = values - jnp.mean(values, axis=-1, keepdims=True)
    spread = jnp.mean(centre * centre, axis=-1, keepdims=True)
    return centre * lax.rsqrt(spread + NORM_EPS) * gain + shift


def unpack(vectors):
    pieces = [vectors[piece_index * D : (piece_index + 1) * D] for piece_index in range(8)]
    hidden_bias = vectors[8 * D : 8 * D + FF]
    bias_table = vectors[8 * D + FF :].reshape(H, NB)
    return (pieces, hidden_bias, bias_table)


def bucket_ids():
    position = jnp.arange(LEN, dtype=jnp.int32)
    offset = position[None, :] - position[:, None]
    distance = jnp.abs(offset)
    far_bucket = jnp.full(distance.shape, 8, jnp.int32)
    for exponent in range(1, 8):
        far_bucket = far_bucket + (distance * distance >= 64 * 2**exponent).astype(jnp.int32)
    near_or_far = jnp.where(distance < 8, distance, far_bucket)
    return near_or_far + NB // 2 * (offset > 0).astype(jnp.int32)


def bucket_onehot():
    return (bucket_ids()[:, :, None] == jnp.arange(NB, dtype=jnp.int32)[None, None, :]).astype(
        jnp.bfloat16
    )


def allowed_pairs(length, pred_flags):
    position = jnp.arange(LEN, dtype=jnp.int32)
    valid_key = (position < length)[None, :]
    row_pos = position[:, None]
    col_pos = position[None, :]
    free_key = (pred_flags == 0)[None, :]
    content_ok = valid_key & (free_key | (pred_flags[:, None] == 1) & (col_pos <= row_pos))
    query_ok = valid_key & (col_pos != row_pos) & (free_key | (col_pos < row_pos))
    return (content_ok, query_ok)


def masked_scores(query_rows, key_rows, position_bias, allowed):
    scores = (
        jnp.einsum("qhd,khd->hqk", query_rows, key_rows, preferred_element_type=jnp.float32)
        * SCORE_SCALE
        + position_bias
    )
    return jnp.where(allowed[None], scores, MASKED)


def table_bias(onehot, table_low):
    return jnp.einsum("qkb,hb->hqk", onehot, table_low, preferred_element_type=jnp.float32)


def attend_slot(onehot, table_low, slot_item):
    query_c, query_q, key_rows, value_rows, length, pred_flags = slot_item
    position_bias = table_bias(onehot, table_low)
    content_ok, query_ok = allowed_pairs(length, pred_flags)
    results = []
    for query_rows, allowed in ((query_c, content_ok), (query_q, query_ok)):
        scores = masked_scores(query_rows, key_rows, position_bias, allowed)
        peak = jnp.max(scores, axis=-1, keepdims=True)
        expos = jnp.exp(scores - peak)
        totals = jnp.sum(expos, axis=-1, keepdims=True)
        probs = (expos / totals).astype(jnp.bfloat16)
        mixed = jnp.einsum(
            "hqk,khd->qhd", probs, value_rows, preferred_element_type=jnp.float32
        ).astype(jnp.bfloat16)
        results.append((mixed, peak[..., 0] + jnp.log(totals[..., 0])))
    return (results[0][0], results[1][0], results[0][1], results[1][1])


def attend_back(onehot, table_low, slot_item):
    (
        query_c,
        query_q,
        key_rows,
        value_rows,
        length,
        pred_flags,
        lse_c,
        lse_q,
        grad_mix_c,
        grad_mix_q,
    ) = slot_item
    position_bias = table_bias(onehot, table_low)
    content_ok, query_ok = allowed_pairs(length, pred_flags)
    grad_keys = jnp.zeros(key_rows.shape, jnp.float32)
    grad_values = jnp.zeros(value_rows.shape, jnp.float32)
    grad_table = jnp.zeros((H, NB), jnp.float32)
    grads_query = []
    for query_rows, allowed, log_total, grad_mix in (
        (query_c, content_ok, lse_c, grad_mix_c),
        (query_q, query_ok, lse_q, grad_mix_q),
    ):
        scores = masked_scores(query_rows, key_rows, position_bias, allowed)
        probs = jnp.exp(scores - log_total[..., None])
        grad_values = grad_values + jnp.einsum(
            "hqk,qhd->khd", probs.astype(jnp.bfloat16), grad_mix, preferred_element_type=jnp.float32
        )
        grad_probs = jnp.einsum(
            "qhd,khd->hqk", grad_mix, value_rows, preferred_element_type=jnp.float32
        )
        grad_scores = probs * (grad_probs - jnp.sum(probs * grad_probs, axis=-1, keepdims=True))
        grad_scores = jnp.where(allowed[None], grad_scores, 0.0).astype(jnp.bfloat16)
        grad_table = grad_table + jnp.einsum(
            "hqk,qkb->hb", grad_scores, onehot, preferred_element_type=jnp.float32
        )
        grads_query.append(
            jnp.einsum("hqk,khd->qhd", grad_scores, key_rows, preferred_element_type=jnp.float32)
            * SCORE_SCALE
        )
        grad_keys = (
            grad_keys
            + jnp.einsum(
                "hqk,qhd->khd", grad_scores, query_rows, preferred_element_type=jnp.float32
            )
            * SCORE_SCALE
        )
    return (grads_query[0], grads_query[1], grad_keys, grad_values, grad_table)


def to_heads(values):
    return values.reshape(-1, LEN, H, DH)


AXES = ("dp", "fsdp")
GRID = (2, 2, 4, 2)
ROWS = 96


def places():
    return [
        (x, c, z, y) for x in range(2) for c in range(2) for z in range(4) for y in range(2)
    ]


def flat(x, c, z, y):
    return ((x * 2 + c) * 4 + z) * 2 + y


def move(value, shift):
    pairs = [(flat(*place), flat(*shift(*place))) for place in places()]
    return lax.ppermute(value, AXES, pairs)


def swap_core(value):
    return move(value, lambda x, c, z, y: (x, 1 - c, z, y))


def swap_x(value):
    return move(value, lambda x, c, z, y: (1 - x, c, z, y))


def swap_y(value):
    return move(value, lambda x, c, z, y: (x, c, z, 1 - y))


def swap_z(value, apart):
    return move(value, lambda x, c, z, y: (x, c, z ^ apart, y))


def my_place():
    dp = lax.axis_index("dp")
    fsdp = lax.axis_index("fsdp")
    return (dp // 2, dp % 2, fsdp // 2, fsdp % 2)


def dot_nn(left, right):
    return jnp.dot(left, right, preferred_element_type=jnp.float32)


def dot_nt(left, right):
    return lax.dot_general(
        left, right, (((1,), (1,)), ((), ())), preferred_element_type=jnp.float32
    )


def dot_tn(left, right):
    return lax.dot_general(
        left, right, (((0,), (0,)), ((), ())), preferred_element_type=jnp.float32
    )


ANY_SPEC = pl.BlockSpec(memory_space=pl.ANY)
VMEM_SPEC = pl.BlockSpec(memory_space=pltpu.VMEM)
SMEM_SPEC = pl.BlockSpec(memory_space=pltpu.SMEM)
TALL = 2 * LEN
HALF = 256
PARAMS = pltpu.CompilerParams(vmem_limit_bytes=60 * 1024 * 1024)


def norm_parts(values):
    centre = values - jnp.mean(values, axis=-1, keepdims=True)
    spread = jnp.mean(centre * centre, axis=-1, keepdims=True)
    scale = lax.rsqrt(spread + NORM_EPS)
    return (centre * scale, scale)


def norm_back(unit, scale, grad, gain):
    scaled = grad * gain
    return scale * (
        scaled
        - jnp.mean(scaled, axis=-1, keepdims=True)
        - unit * jnp.mean(scaled * unit, axis=-1, keepdims=True)
    )


def start_fetch(kinds, plan, place_ref, refs, targets, sems):
    x, c, z, y = (place_ref[index] for index in range(4))
    mine = z * 2 + y
    copies = []

    def start(source, target):
        copy = pltpu.make_async_copy(source, target, sems.at[len(copies)])
        copy.start()
        copies.append(copy)

    for member, kind in enumerate(kinds):
        target = targets[member]
        if kind == "attn":
            start(refs[member], target.at[:, pl.ds(pl.multiple_of(mine * ROWS, ROWS), ROWS), :])
        elif kind == "inner":
            for quarter in range(4):
                start(
                    refs[member].at[:, quarter * D : quarter * D + D],
                    target.at[quarter, pl.ds(pl.multiple_of(mine * ROWS, ROWS), ROWS), :],
                )
        else:
            start(refs[member], target.at[z, pl.ds(pl.multiple_of(y * 384, ROWS), 384), :])
    for array, index, dx, dy, dc, dz, member in plan:
        quarter = (x ^ dx) * 2 + (c ^ dc)
        if kinds[member] == "outer":
            lead, row = z ^ dz, (y ^ dy) * 384 + quarter * ROWS
        else:
            lead, row = quarter, ((z ^ dz) * 2 + (y ^ dy)) * ROWS
        start(
            refs[len(kinds) + array].at[index],
            targets[member].at[lead, pl.ds(pl.multiple_of(row, ROWS), ROWS), :],
        )
    return copies


def project_kernel(plan, place_ref, low_ref, small_ref, *refs):
    pieces = refs[:-7]
    q_ref, k_ref, v_ref, w_out, w_ref, sems, out_sem = refs[-7:]
    for copy in start_fetch(("attn",), plan, place_ref, pieces, (w_ref,), sems):
        copy.wait()
    keep = pltpu.make_async_copy(w_ref, w_out, out_sem)
    keep.start()
    bias_q = small_ref[0:1, :]
    bias_v = small_ref[1:2, :]
    for row in range(0, TALL, HALF):
        rows = low_ref[row : row + HALF, :]
        q_ref[row : row + HALF, :] = (dot_nn(rows, w_ref[0]) + bias_q).astype(jnp.bfloat16)
        if row < LEN:
            k_ref[row : row + HALF, :] = dot_nn(rows, w_ref[1]).astype(jnp.bfloat16)
            v_ref[row : row + HALF, :] = (dot_nn(rows, w_ref[2]) + bias_v).astype(jnp.bfloat16)
    keep.wait()


def project(place, low, small, group):
    plan, pieces = group
    return pl.pallas_call(
        partial(project_kernel, plan),
        out_shape=[
            jax.ShapeDtypeStruct((TALL, D), jnp.bfloat16),
            jax.ShapeDtypeStruct((LEN, D), jnp.bfloat16),
            jax.ShapeDtypeStruct((LEN, D), jnp.bfloat16),
            jax.ShapeDtypeStruct((4, D, D), jnp.bfloat16),
        ],
        in_specs=[SMEM_SPEC, VMEM_SPEC, VMEM_SPEC] + [ANY_SPEC] * len(pieces),
        out_specs=[VMEM_SPEC] * 3 + [ANY_SPEC],
        scratch_shapes=[
            pltpu.VMEM((4, D, D), jnp.bfloat16),
            pltpu.SemaphoreType.DMA((32,)),
            pltpu.SemaphoreType.DMA,
        ],
        compiler_params=PARAMS,
        cost_estimate=pl.CostEstimate(flops=2 * 2048 * D * D, bytes_accessed=16000000, transcendentals=0),
        name="project",
    )(place, low, small, *pieces)


def build_masks(length, row_flags, col_flags, mask_ref, alive_ref):
    flags = row_flags[...]

    def body(step, carry):
        start = pl.multiple_of(step * 64, 64)
        key = lax.broadcasted_iota(jnp.int32, (64, LEN), 0) + start
        query = lax.broadcasted_iota(jnp.int32, (64, LEN), 1)
        valid = key < length
        free = jnp.broadcast_to(col_flags[pl.ds(start, 64), :], (64, LEN)) == 0.0
        marked = jnp.broadcast_to(flags, (64, LEN)) == 1.0
        content_ok = valid & (free | (marked & (key <= query)))
        query_ok = valid & (key != query) & (free | (key < query))
        mask_ref[pl.ds(start, 64), :LEN] = content_ok.astype(jnp.float32)
        mask_ref[pl.ds(start, 64), LEN:] = query_ok.astype(jnp.float32)
        return carry

    lax.fori_loop(0, 8, body, 0)
    alive_ref[...] = jnp.max(mask_ref[...], axis=0, keepdims=True)


def build_tiles(t_row, tile_ref):
    spread = jnp.broadcast_to(t_row, (128, 512))
    rolled = pltpu.roll(spread, 0, 1, stride=1, stride_axis=0)
    tile_ref[...] = rolled[:, :384]


def position_bias(tile_ref, far_ref, head, query_block, key_block):
    apart = query_block - key_block
    if apart >= 2:
        return far_ref[head, 0]
    if apart <= -2:
        return far_ref[head, 1]
    return tile_ref[:, 128 * (apart + 1) : 128 * (apart + 2)]


def head_lanes(shape, head):
    lane = lax.broadcasted_iota(jnp.int32, shape, 1)
    return (lane >= 64) if head else (lane < 64)


def mix_kernel(
    length_ref, far_ref, q_ref, k_ref, v_ref, row_flags, col_flags, t_ref,
    a_ref, p_ref, inverse_ref, dead_ref, mask_ref, alive_ref, tile_ref, o_ref,
):
    pair = pl.program_id(0)

    @pl.when(pair == 0)
    def _():
        build_masks(length_ref[0], row_flags, col_flags, mask_ref, alive_ref)
        dead_ref[...] = (1.0 - alive_ref[...]) * (1.0 / LEN)

    keys = k_ref[...].astype(jnp.float32) * SCORE_SCALE
    values_t = v_ref[...].astype(jnp.float32).T.astype(jnp.bfloat16)
    for head in range(2):
        build_tiles(t_ref[head], tile_ref.at[head])
        keys_own = jnp.where(head_lanes(keys.shape, head), keys, 0.0).astype(jnp.bfloat16)
        for chunk in range(4):
            at = chunk * HALF
            scores = dot_nt(keys_own, q_ref[at : at + HALF, :])
            for side in range(2):
                lanes = slice(at + side * 128, at + side * 128 + 128)
                blocks = []
                peak = None
                for key_block in range(4):
                    rows = slice(key_block * 128, key_block * 128 + 128)
                    block = scores[rows, side * 128 : side * 128 + 128] + position_bias(
                        tile_ref.at[head], far_ref, pair * 2 + head, (chunk % 2) * 2 + side, key_block
                    )
                    block = jnp.where(mask_ref[rows, lanes] > 0.0, block, MASKED)
                    blocks.append(block)
                    high = jnp.max(block, axis=0, keepdims=True)
                    peak = high if peak is None else jnp.maximum(peak, high)
                total = None
                for key_block in range(4):
                    rows = slice(key_block * 128, key_block * 128 + 128)
                    expo = jnp.exp(blocks[key_block] - peak)
                    part = jnp.sum(expo, axis=0, keepdims=True)
                    total = part if total is None else total + part
                    p_ref[head, rows, lanes] = expo.astype(jnp.bfloat16)
                inverse = 1.0 / total
                inverse_ref[head, :, lanes] = inverse * alive_ref[:, lanes]
                o_ref[head : head + 1, lanes] = inverse
        mixed = dot_nn(values_t[head * 64 : head * 64 + 64, :], p_ref[head])
        o_ref[8 + head * 64 : 8 + head * 64 + 64, :] = mixed * o_ref[head : head + 1, :]
    a_ref[...] = o_ref[8:, :].T.astype(jnp.bfloat16)


def mix(length, far, tvec, q, k, v, row_flags, col_flags):
    tall = pl.BlockSpec((TALL, 128), lambda p: (0, p))
    short = pl.BlockSpec((LEN, 128), lambda p: (0, p))
    return pl.pallas_call(
        mix_kernel,
        grid=(H // 2,),
        out_shape=[
            jax.ShapeDtypeStruct((TALL, D), jnp.bfloat16),
            jax.ShapeDtypeStruct((H, LEN, TALL), jnp.bfloat16),
            jax.ShapeDtypeStruct((H, 1, TALL), jnp.float32),
            jax.ShapeDtypeStruct((1, TALL), jnp.float32),
        ],
        in_specs=[
            SMEM_SPEC, SMEM_SPEC, tall, short, short,
            pl.BlockSpec((1, LEN), lambda p: (0, 0)),
            pl.BlockSpec((LEN, 1), lambda p: (0, 0)),
            pl.BlockSpec((2, 1, 512), lambda p: (p, 0, 0)),
        ],
        out_specs=[
            tall,
            pl.BlockSpec((2, LEN, TALL), lambda p: (p, 0, 0)),
            pl.BlockSpec((2, 1, TALL), lambda p: (p, 0, 0)),
            pl.BlockSpec((1, TALL), lambda p: (0, 0)),
        ],
        scratch_shapes=[
            pltpu.VMEM((LEN, TALL), jnp.float32),
            pltpu.VMEM((1, TALL), jnp.float32),
            pltpu.VMEM((2, 128, 384), jnp.float32),
            pltpu.VMEM((136, TALL), jnp.float32),
        ],
        compiler_params=PARAMS,
        cost_estimate=pl.CostEstimate(flops=6500000000, bytes_accessed=8000000, transcendentals=6300000),
        name="mix",
    )(length, far, q, k, v, row_flags, col_flags, tvec)


def mix_back_kernel(
    q_ref, k_ref, v_ref, da_ref, a_ref, p_ref, inverse_ref, dead_ref,
    dq_ref, dk_ref, dv_ref, table_ref,
    s_ref, near_ref, da_t, low_t, q_t, g_ref,
):
    keys = k_ref[...].astype(jnp.float32) * SCORE_SCALE
    keys_t = keys.T.astype(jnp.bfloat16)
    q_t[...] = q_ref[...].astype(jnp.float32).T.astype(jnp.bfloat16)
    da_t[...] = da_ref[...].astype(jnp.float32).T
    product = a_ref[...].astype(jnp.float32).T * da_t[...]
    values = v_ref[...].astype(jnp.float32)
    near_ref[...] = jnp.zeros(near_ref.shape, jnp.float32)
    turn = (
        lax.broadcasted_iota(jnp.int32, (128, 128), 0)
        + lax.broadcasted_iota(jnp.int32, (128, 128), 1)
        == 127
    ).astype(jnp.float32)
    deltas = []
    for head in range(2):
        rows = slice(head * 64, head * 64 + 64)
        inverse = inverse_ref[head]
        deltas.append(jnp.sum(product[rows, :], axis=0, keepdims=True) * inverse)
        low_t[rows, :] = (da_t[rows, :] * inverse).astype(jnp.bfloat16)
    for head in range(2):
        own = slice(head * 64, head * 64 + 64)
        values_own = jnp.where(head_lanes(values.shape, head), values, 0.0).astype(jnp.bfloat16)
        delta = deltas[head]
        far_low = jnp.zeros((8, 128), jnp.float32)
        far_high = jnp.zeros((8, 128), jnp.float32)
        for chunk in range(4):
            at = chunk * HALF
            pulls = dot_nn(values_own, low_t[:, at : at + HALF])
            for side in range(2):
                lanes = slice(at + side * 128, at + side * 128 + 128)
                shift = delta[:, lanes]
                query_block = (chunk % 2) * 2 + side
                for key_block in range(4):
                    rows = slice(key_block * 128, key_block * 128 + 128)
                    cols = slice(side * 128, side * 128 + 128)
                    grad = p_ref[head, rows, lanes].astype(jnp.float32) * (
                        pulls[rows, cols] - shift
                    )
                    s_ref[head, rows, lanes] = grad.astype(jnp.bfloat16)
                    apart = query_block - key_block
                    if apart >= 2:
                        far_low = far_low + jnp.sum(grad.reshape(16, 8, 128), axis=0)
                    elif apart <= -2:
                        far_high = far_high + jnp.sum(grad.reshape(16, 8, 128), axis=0)
                    else:
                        near_ref[head, :, 128 * (apart + 1) : 128 * (apart + 2)] += grad
        g_ref[own, :LEN] = dot_nt(low_t[own, :], p_ref[head])
        g_ref[own, LEN:] = dot_nt(q_t[own, :], s_ref[head]) * SCORE_SCALE
        da_t[own, :] = dot_nn(keys_t[own, :], s_ref[head])
        turned = jnp.dot(
            turn, near_ref[head], precision=lax.Precision.HIGHEST, preferred_element_type=jnp.float32
        )
        aligned = pltpu.roll(turned, 0, 1, stride=1, stride_axis=0)
        table_ref[head, :, :512] = jnp.sum(aligned, axis=0, keepdims=True)
        table_ref[head, :, 512:640] = jnp.sum(far_low, axis=0, keepdims=True)
        table_ref[head, :, 640:] = jnp.sum(far_high, axis=0, keepdims=True)
    uniform = dot_nn(dead_ref[...].astype(jnp.bfloat16), da_ref[...])
    dv_ref[...] = (g_ref[:, :LEN].T + uniform).astype(jnp.bfloat16)
    dk_ref[...] = g_ref[:, LEN:].T.astype(jnp.bfloat16)
    dq_ref[...] = da_t[...].T.astype(jnp.bfloat16)


def mix_back(first, q, k, v, da, a, p, inverse, dead):
    tall = pl.BlockSpec((TALL, 128), lambda i: (0, i + first))
    short = pl.BlockSpec((LEN, 128), lambda i: (0, i + first))
    return pl.pallas_call(
        mix_back_kernel,
        grid=(H // 4,),
        out_shape=[
            jax.ShapeDtypeStruct((TALL, D // 2), jnp.bfloat16),
            jax.ShapeDtypeStruct((LEN, D // 2), jnp.bfloat16),
            jax.ShapeDtypeStruct((LEN, D // 2), jnp.bfloat16),
            jax.ShapeDtypeStruct((H // 2, 1, 768), jnp.float32),
        ],
        in_specs=[
            tall, short, short, tall, tall,
            pl.BlockSpec((2, LEN, TALL), lambda i: (i + first, 0, 0)),
            pl.BlockSpec((2, 1, TALL), lambda i: (i + first, 0, 0)),
            pl.BlockSpec((1, TALL), lambda i: (0, 0)),
        ],
        out_specs=[
            pl.BlockSpec((TALL, 128), lambda i: (0, i)),
            pl.BlockSpec((LEN, 128), lambda i: (0, i)),
            pl.BlockSpec((LEN, 128), lambda i: (0, i)),
            pl.BlockSpec((2, 1, 768), lambda i: (i, 0, 0)),
        ],
        scratch_shapes=[
            pltpu.VMEM((2, LEN, TALL), jnp.bfloat16),
            pltpu.VMEM((2, 128, 512), jnp.float32),
            pltpu.VMEM((128, TALL), jnp.float32),
            pltpu.VMEM((128, TALL), jnp.bfloat16),
            pltpu.VMEM((128, TALL), jnp.bfloat16),
            pltpu.VMEM((128, TALL), jnp.float32),
        ],
        compiler_params=PARAMS,
        cost_estimate=pl.CostEstimate(flops=8000000000, bytes_accessed=16000000, transcendentals=0),
        name="mix_back",
    )(q, k, v, da, a, p, inverse, dead)


GELU_SCALE = 0.7978845608028654
GELU_CUBE = 0.044715


def feed_kernel(plan, place_ref, small_ref, hidden_bias_ref, mix_any, hidden_any, attn_any, *refs):
    pieces = refs[:-20]
    (
        resid_out, summed_out, pre_out, normed_out, next_out, low_out,
        mix_ref, hidden_ref, wo_ref, inner_ref, outer_ref, resid_ref, total_ref, normed_ref,
        pre_ref, next_ref, low_ref, sems, load_sems, store_sems,
    ) = refs[-20:]
    loads = [
        pltpu.make_async_copy(mix_any, mix_ref, load_sems.at[0]),
        pltpu.make_async_copy(attn_any.at[3], wo_ref, load_sems.at[1]),
        pltpu.make_async_copy(hidden_any, hidden_ref, load_sems.at[2]),
    ]
    for load in loads:
        load.start()
    fetches = start_fetch(("inner", "outer"), plan, place_ref, pieces, (inner_ref, outer_ref), sems)
    for load in loads:
        load.wait()
    for row in range(0, TALL, HALF):
        rows = slice(row, row + HALF)
        resid = hidden_ref[rows, :] + dot_nn(mix_ref[rows, :], wo_ref[...]) + small_ref[2:3, :]
        resid_ref[rows, :] = resid
        unit, scale = norm_parts(resid)
        normed = unit * small_ref[3:4, :] + small_ref[4:5, :]
        normed_ref[rows, :] = normed.astype(jnp.bfloat16)
        total_ref[rows, :] = normed + small_ref[5:6, :]
    stores = [
        pltpu.make_async_copy(resid_ref, resid_out, store_sems.at[0]),
        pltpu.make_async_copy(normed_ref, normed_out, store_sems.at[8]),
    ]
    for store in stores:
        store.start()
    for fetch in fetches:
        fetch.wait()
    for chunk in range(4):
        for row in range(0, TALL, HALF):
            rows = slice(row, row + HALF)
            pre = dot_nn(normed_ref[rows, :], inner_ref[chunk]) + hidden_bias_ref[
                :, chunk * D : chunk * D + D
            ]
            pre_ref[chunk, rows, :] = pre.astype(jnp.bfloat16)
            tanh = jnp.tanh(GELU_SCALE * (pre + GELU_CUBE * (pre * pre * pre)))
            active = (pre * (0.5 + 0.5 * tanh)).astype(jnp.bfloat16)
            total_ref[rows, :] += dot_nn(active, outer_ref[chunk])
        store = pltpu.make_async_copy(
            pre_ref.at[chunk], pre_out.at[chunk], store_sems.at[1 + chunk]
        )
        store.start()
        stores.append(store)
    store = pltpu.make_async_copy(total_ref, summed_out, store_sems.at[5])
    store.start()
    stores.append(store)
    for row in range(0, TALL, HALF):
        rows = slice(row, row + HALF)
        unit, scale = norm_parts(total_ref[rows, :])
        following = unit * small_ref[6:7, :] + small_ref[7:8, :]
        next_ref[rows, :] = following
        low_ref[rows, :] = following.astype(jnp.bfloat16)
    for index, (source, target) in enumerate(((next_ref, next_out), (low_ref, low_out))):
        store = pltpu.make_async_copy(source, target, store_sems.at[6 + index])
        store.start()
        stores.append(store)
    for store in stores:
        store.wait()


def feed(place, small, hidden_bias, mixed, hidden, attn, group):
    plan, pieces = group
    return pl.pallas_call(
        partial(feed_kernel, plan),
        out_shape=[
            jax.ShapeDtypeStruct((TALL, D), jnp.float32),
            jax.ShapeDtypeStruct((TALL, D), jnp.float32),
            jax.ShapeDtypeStruct((4, TALL, D), jnp.bfloat16),
            jax.ShapeDtypeStruct((TALL, D), jnp.bfloat16),
            jax.ShapeDtypeStruct((TALL, D), jnp.float32),
            jax.ShapeDtypeStruct((TALL, D), jnp.bfloat16),
        ],
        in_specs=[SMEM_SPEC, VMEM_SPEC, VMEM_SPEC] + [ANY_SPEC] * (3 + len(pieces)),
        out_specs=[ANY_SPEC] * 6,
        scratch_shapes=[
            pltpu.VMEM((TALL, D), jnp.bfloat16),
            pltpu.VMEM((TALL, D), jnp.float32),
            pltpu.VMEM((D, D), jnp.bfloat16),
            pltpu.VMEM((4, D, D), jnp.bfloat16),
            pltpu.VMEM((4, D, D), jnp.bfloat16),
            pltpu.VMEM((TALL, D), jnp.float32),
            pltpu.VMEM((TALL, D), jnp.float32),
            pltpu.VMEM((TALL, D), jnp.bfloat16),
            pltpu.VMEM((4, TALL, D), jnp.bfloat16),
            pltpu.VMEM((TALL, D), jnp.float32),
            pltpu.VMEM((TALL, D), jnp.bfloat16),
            pltpu.SemaphoreType.DMA((64,)),
            pltpu.SemaphoreType.DMA((3,)),
            pltpu.SemaphoreType.DMA((9,)),
        ],
        compiler_params=PARAMS,
        cost_estimate=pl.CostEstimate(flops=2 * TALL * D * (D + 2 * FF), bytes_accessed=40000000, transcendentals=3000000),
        name="feed",
    )(place, small, hidden_bias, mixed, hidden, attn, *pieces)


def feed_back_kernel(
    plan, place_ref, small_ref, grad_c_any, grad_q_any, summed_any, normed_any, resid_any, pre_any,
    mix_any, attn_any, *refs
):
    pieces = refs[:-26]
    (
        dresid_out, dmix_out, dwo_out, keep_out, send_out, vec_ref, dhidden_ref,
        grad_ref, summed_ref, resid_ref, pre_ref, mix_ref, wo_ref, inner_ref, outer_ref,
        branch_ref, normed_ref, active_ref, dpre_ref, dinner_ref, douter_ref,
        dwo_ref, sems, load_sems, store_sems, block_sems,
    ) = refs[-26:]
    x, c, z, y = (place_ref[index] for index in range(4))
    total_ref = summed_ref
    load = [
        pltpu.make_async_copy(source, target, load_sems.at[index])
        for index, (source, target) in enumerate(
            (
                (summed_any, summed_ref),
                (grad_c_any, grad_ref.at[:LEN, :]),
                (grad_q_any, grad_ref.at[LEN:, :]),
                (pre_any, pre_ref),
                (normed_any, normed_ref),
                (resid_any, resid_ref),
                (mix_any, mix_ref),
                (attn_any.at[3], wo_ref),
            )
        )
    ]
    for copy in load[:3]:
        copy.start()
    fetches = start_fetch(("inner", "outer"), plan, place_ref, pieces, (inner_ref, outer_ref), sems)
    for copy in load[3:]:
        copy.start()
    for copy in load[:3]:
        copy.wait()
    gain_two_grad = jnp.zeros((1, D), jnp.float32)
    shift_two_grad = jnp.zeros((1, D), jnp.float32)
    bias_two_grad = jnp.zeros((1, D), jnp.float32)
    for row in range(0, TALL, HALF):
        rows = slice(row, row + HALF)
        grad = grad_ref[rows, :]
        unit, scale = norm_parts(summed_ref[rows, :])
        gain_two_grad += jnp.sum(grad * unit, axis=0, keepdims=True)
        shift_two_grad += jnp.sum(grad, axis=0, keepdims=True)
        back = norm_back(unit, scale, grad, small_ref[6:7, :])
        total_ref[rows, :] = back
        low = back.astype(jnp.bfloat16)
        branch_ref[rows, :] = low
        bias_two_grad += jnp.sum(low.astype(jnp.float32), axis=0, keepdims=True)
    vec_ref[5:6, :] = bias_two_grad
    vec_ref[6:7, :] = gain_two_grad
    vec_ref[7:8, :] = shift_two_grad
    for copy in fetches + load[3:]:
        copy.wait()
    blocks = []

    def store(source, target):
        copy = pltpu.make_async_copy(source, target, block_sems.at[len(blocks)])
        copy.start()
        blocks.append(copy)

    for step in range(4):
        apart, side = 1 - step // 2, step % 2
        chunk = side * 2 + (c ^ apart)
        bias_grad = jnp.zeros((1, D), jnp.float32)
        for row in range(0, TALL, HALF):
            rows = slice(row, row + HALF)
            pull = dot_nt(branch_ref[rows, :], outer_ref[chunk])
            pre = pre_ref[chunk, rows, :].astype(jnp.float32)
            square = pre * pre
            tanh = jnp.tanh(GELU_SCALE * pre * (1.0 + GELU_CUBE * square))
            half = 0.5 + 0.5 * tanh
            active_ref[rows, :] = (pre * half).astype(jnp.bfloat16)
            slope = half + (0.5 * GELU_SCALE) * pre * (1.0 - tanh * tanh) * (
                1.0 + (3.0 * GELU_CUBE) * square
            )
            dpre = (pull * slope).astype(jnp.bfloat16)
            dpre_ref[rows, :] = dpre
            bias_grad += jnp.sum(dpre.astype(jnp.float32), axis=0, keepdims=True)
            total_ref[rows, :] += dot_nt(dpre, inner_ref[chunk])
        dhidden_ref[chunk] = bias_grad
        douter_ref[step] = (
            dot_tn(active_ref[...], branch_ref[...]).astype(jnp.bfloat16).reshape(2, 2, 2, ROWS, D)
        )
        for y_block in range(2):
            for x_block in range(2):
                spot = (y_block ^ y, x_block ^ x, chunk, 1)
                store(douter_ref.at[step, y_block, x_block, c], keep_out.at[spot])
                store(douter_ref.at[step, y_block, x_block, 1 - c], send_out.at[spot])
        dinner_ref[step] = (
            dot_tn(normed_ref[...], dpre_ref[...]).astype(jnp.bfloat16).reshape(4, 2, ROWS, D)
        )
        target = send_out if apart else keep_out
        for y_block in range(2):
            store(dinner_ref.at[step, :, y_block], target.at[y_block ^ y, side ^ x, :, 0])
    gain_one_grad = jnp.zeros((1, D), jnp.float32)
    shift_one_grad = jnp.zeros((1, D), jnp.float32)
    bias_o_grad = jnp.zeros((1, D), jnp.float32)
    for row in range(0, TALL, HALF):
        rows = slice(row, row + HALF)
        grad = total_ref[rows, :]
        unit, scale = norm_parts(resid_ref[rows, :])
        gain_one_grad += jnp.sum(grad * unit, axis=0, keepdims=True)
        shift_one_grad += jnp.sum(grad, axis=0, keepdims=True)
        back = norm_back(unit, scale, grad, small_ref[3:4, :])
        grad_ref[rows, :] = back
        low = back.astype(jnp.bfloat16)
        branch_ref[rows, :] = low
        bias_o_grad += jnp.sum(low.astype(jnp.float32), axis=0, keepdims=True)
        active_ref[rows, :] = dot_nt(low, wo_ref[...]).astype(jnp.bfloat16)
    stores = [
        pltpu.make_async_copy(source, target, store_sems.at[index])
        for index, (source, target) in enumerate(
            ((grad_ref, dresid_out), (active_ref, dmix_out), (dwo_ref, dwo_out))
        )
    ]
    stores[0].start()
    stores[1].start()
    dwo_ref[...] = dot_tn(mix_ref[...], branch_ref[...]).astype(jnp.bfloat16)
    stores[2].start()
    vec_ref[0:2, :] = jnp.zeros((2, D), jnp.float32)
    vec_ref[2:3, :] = bias_o_grad
    vec_ref[3:4, :] = gain_one_grad
    vec_ref[4:5, :] = shift_one_grad
    for copy in blocks + stores:
        copy.wait()


def feed_back(place, small, grads, summed, normed, resid, pre, mixed, attn, group):
    plan, pieces = group
    blocks = jax.ShapeDtypeStruct((2, 2, 4, 2, ROWS, D), jnp.bfloat16)
    return pl.pallas_call(
        partial(feed_back_kernel, plan),
        out_shape=[
            jax.ShapeDtypeStruct((TALL, D), jnp.float32),
            jax.ShapeDtypeStruct((TALL, D), jnp.bfloat16),
            jax.ShapeDtypeStruct((D, D), jnp.bfloat16),
            blocks,
            blocks,
            jax.ShapeDtypeStruct((8, D), jnp.float32),
            jax.ShapeDtypeStruct((4, 1, D), jnp.float32),
        ],
        in_specs=[SMEM_SPEC, VMEM_SPEC] + [ANY_SPEC] * (8 + len(pieces)),
        out_specs=[ANY_SPEC] * 5 + [VMEM_SPEC] * 2,
        scratch_shapes=[
            pltpu.VMEM((TALL, D), jnp.float32),
            pltpu.VMEM((TALL, D), jnp.float32),
            pltpu.VMEM((TALL, D), jnp.float32),
            pltpu.VMEM((4, TALL, D), jnp.bfloat16),
            pltpu.VMEM((TALL, D), jnp.bfloat16),
            pltpu.VMEM((D, D), jnp.bfloat16),
            pltpu.VMEM((4, D, D), jnp.bfloat16),
            pltpu.VMEM((4, D, D), jnp.bfloat16),
            pltpu.VMEM((TALL, D), jnp.bfloat16),
            pltpu.VMEM((TALL, D), jnp.bfloat16),
            pltpu.VMEM((TALL, D), jnp.bfloat16),
            pltpu.VMEM((TALL, D), jnp.bfloat16),
            pltpu.VMEM((4, 4, 2, ROWS, D), jnp.bfloat16),
            pltpu.VMEM((4, 2, 2, 2, ROWS, D), jnp.bfloat16),
            pltpu.VMEM((D, D), jnp.bfloat16),
            pltpu.SemaphoreType.DMA((64,)),
            pltpu.SemaphoreType.DMA((8,)),
            pltpu.SemaphoreType.DMA((3,)),
            pltpu.SemaphoreType.DMA((40,)),
        ],
        compiler_params=PARAMS,
        cost_estimate=pl.CostEstimate(flops=4 * TALL * D * (D + 2 * FF), bytes_accessed=60000000, transcendentals=3000000),
        name="feed_back",
    )(place, small, *grads, summed, normed, resid, pre, mixed, attn, *pieces)


def weight_back_kernel(
    place_ref, low_ref, dq_a, dk_a, dv_a, dq_b, dk_b, dv_b, dwo_ref, keep_out, send_out, vec_ref, grads_ref, sems
):
    x, c, z, y = (place_ref[index] for index in range(4))
    grads_ref[3] = dwo_ref[...].reshape(4, 2, ROWS, D)
    for matrix, halves in enumerate(((dq_a, dq_b), (dk_a, dk_b), (dv_a, dv_b))):
        for half, grad in enumerate(halves):
            cols = slice(half * 384, half * 384 + 384)
            grads_ref[matrix, :, :, :, cols] = (
                dot_tn(low_ref[: grad.shape[0], :], grad[...])
                .astype(jnp.bfloat16)
                .reshape(4, 2, ROWS, 384)
            )
            if matrix != 1:
                vec_ref[matrix // 2 : matrix // 2 + 1, cols] = jnp.sum(
                    grad[...].astype(jnp.float32), axis=0, keepdims=True
                )
    blocks = []
    for apart, target in ((1, send_out), (0, keep_out)):
        for side in range(2):
            for y_block in range(2):
                copy = pltpu.make_async_copy(
                    grads_ref.at[side * 2 + (c ^ apart), :, y_block],
                    target.at[y_block ^ y, side ^ x, :, 0],
                    sems.at[len(blocks)],
                )
                copy.start()
                blocks.append(copy)
    for block in blocks:
        block.wait()


def weight_back(place, low, first, second, dwo):
    blocks = jax.ShapeDtypeStruct((2, 2, 4, 1, ROWS, D), jnp.bfloat16)
    return pl.pallas_call(
        weight_back_kernel,
        out_shape=[blocks, blocks, jax.ShapeDtypeStruct((2, D), jnp.float32)],
        in_specs=[SMEM_SPEC] + [VMEM_SPEC] * 8,
        out_specs=[ANY_SPEC] * 2 + [VMEM_SPEC],
        scratch_shapes=[
            pltpu.VMEM((4, 4, 2, ROWS, D), jnp.bfloat16),
            pltpu.SemaphoreType.DMA((8,)),
        ],
        compiler_params=PARAMS,
        cost_estimate=pl.CostEstimate(flops=2 * 2048 * D * D, bytes_accessed=12000000, transcendentals=0),
        name="weight_back",
    )(place, low, *first, *second, dwo)


def input_back_kernel(
    dq_a, dk_a, dv_a, dq_b, dk_b, dv_b, w_ref, dresid_ref, first_ref, second_ref
):
    step = pl.program_id(0)
    total = (
        dresid_ref[...]
        + dot_nt(dq_a[...], w_ref[0, :, :384])
        + dot_nt(dq_b[...], w_ref[0, :, 384:])
    )

    @pl.when(step < 2)
    def _():
        content = total
        for matrix, halves in ((1, (dk_a, dk_b)), (2, (dv_a, dv_b))):
            for half, grad in enumerate(halves):
                content += dot_nt(grad[...], w_ref[matrix, :, half * 384 : half * 384 + 384])
        first_ref[...] = content

    @pl.when(step >= 2)
    def _():
        second_ref[...] = total


def input_back(first, second, attn, dresid):
    half = jax.ShapeDtypeStruct((LEN, D), jnp.float32)
    tall = pl.BlockSpec((HALF, D // 2), lambda i: (i, 0))
    short = pl.BlockSpec((HALF, D // 2), lambda i: (jnp.minimum(i, 1), 0))
    return pl.pallas_call(
        input_back_kernel,
        grid=(4,),
        out_shape=[half, half],
        in_specs=[
            tall, short, short, tall, short, short,
            pl.BlockSpec((3, D, D), lambda i: (0, 0, 0)),
            pl.BlockSpec((HALF, D), lambda i: (i, 0)),
        ],
        out_specs=[
            pl.BlockSpec((HALF, D), lambda i: (jnp.minimum(i, 1), 0)),
            pl.BlockSpec((HALF, D), lambda i: (jnp.maximum(i - 2, 0), 0)),
        ],
        compiler_params=PARAMS,
        cost_estimate=pl.CostEstimate(flops=2 * 2048 * D * D, bytes_accessed=16000000, transcendentals=0),
        name="input_back",
    )(*first, *second, attn, dresid)


def bias_vectors(table):
    lane = jnp.arange(512, dtype=jnp.int32)
    offset = jnp.where(lane < 384, 128 - lane, 640 - lane)
    onehot = bucket_of(offset)[:, None] == jnp.arange(NB, dtype=jnp.int32)[None, :]
    near = jnp.dot(table, onehot.astype(jnp.float32).T, precision=lax.Precision.HIGHEST)
    return (near[:, None, :], jnp.stack([table[:, 15], table[:, 31]], axis=1), onehot)


def bucket_of(offset):
    distance = jnp.abs(offset)
    far_bucket = jnp.full(distance.shape, 8, jnp.int32)
    for exponent in range(1, 8):
        far_bucket = far_bucket + (distance * distance >= 64 * 2**exponent).astype(jnp.int32)
    near_or_far = jnp.where(distance < 8, distance, far_bucket)
    return near_or_far + NB // 2 * (offset > 0).astype(jnp.int32)


def table_grad(sums, onehot):
    near = jnp.dot(
        sums[:, 0, :512],
        jnp.roll(onehot.astype(jnp.float32), 127, axis=0),
        precision=lax.Precision.HIGHEST,
    )
    low = jnp.sum(sums[:, 0, 512:640], axis=1)
    high = jnp.sum(sums[:, 0, 640:], axis=1)
    return near.at[:, 15].add(low).at[:, 31].add(high)


def adam_kernel(rate, master_ref, first_ref, second_ref, grad_ref, *refs):
    master_out, first_out, second_out = refs[-3:]
    grad = grad_ref[...].astype(jnp.float32).reshape(master_ref.shape)
    new = adam_update(master_ref[...], first_ref[...], second_ref[...], grad, rate)
    for target, value in zip((master_out, first_out, second_out), new):
        target[...] = value


def adam(kind, layer, rate, state, quarters, member, done):
    if kind == "attn":
        block = pl.BlockSpec((1, 1, ROWS, D), lambda i: (layer, i, 0, 0))
    elif kind == "inner":
        block = pl.BlockSpec((1, ROWS, D), lambda i: (layer, 0, i))
    else:
        block = pl.BlockSpec((1, ROWS, D), lambda i: (layer, i, 0))
    held = done or ()
    return pl.pallas_call(
        partial(adam_kernel, rate),
        grid=(4,),
        out_shape=[jax.ShapeDtypeStruct(array.shape, jnp.float32) for array in state],
        in_specs=[block] * 3
        + [pl.BlockSpec((1, 1, ROWS, D), lambda i: (i, member, 0, 0))]
        + [ANY_SPEC] * len(held),
        out_specs=[block] * 3,
        input_output_aliases={4 + index: index for index in range(len(held))},
        compiler_params=PARAMS,
        cost_estimate=pl.CostEstimate(flops=5000000, bytes_accessed=8000000, transcendentals=0),
        name="adam",
    )(*state, quarters, *held)


def fetch_forward(shards):
    low = tuple(shard.astype(jnp.bfloat16) for shard in shards)
    return (
        lax.all_gather(low[0], "fsdp", axis=1, tiled=True),
        lax.all_gather(low[1], "fsdp", axis=0, tiled=True),
        lax.all_gather(low[2], "fsdp", axis=0, tiled=True),
    )


def reduce_layer(grads):
    owned = tuple(
        lax.psum_scatter(
            grad.astype(jnp.bfloat16), "fsdp", scatter_dimension=axis, tiled=True
        ).astype(jnp.float32)
        for grad, axis in zip(grads, (1, 0, 0))
    )
    return lax.psum(owned, "dp")


def forward_layer(hidden_c, hidden_q, weights, lengths, flag_rows, onehot):
    attn_w, inner_w, outer_w, small_w = weights
    pieces, hidden_bias, bias_table = unpack(small_w.astype(jnp.float32))
    bias_q, bias_v, bias_o, gain_one, shift_one, bias_two, gain_two, shift_two = pieces
    table_low = bias_table.astype(jnp.bfloat16)
    low_c = hidden_c.astype(jnp.bfloat16)
    low_q = hidden_q.astype(jnp.bfloat16)
    projected = jnp.einsum("td,sde->ste", low_c, attn_w[:3], preferred_element_type=jnp.float32)
    query_c = (projected[0] + bias_q).astype(jnp.bfloat16)
    key_rows = projected[1].astype(jnp.bfloat16)
    value_rows = (projected[2] + bias_v).astype(jnp.bfloat16)
    query_q = (jnp.dot(low_q, attn_w[0], preferred_element_type=jnp.float32) + bias_q).astype(
        jnp.bfloat16
    )
    mixed_c, mixed_q, lse_c, lse_q = lax.map(
        partial(attend_slot, onehot, table_low),
        (
            to_heads(query_c),
            to_heads(query_q),
            to_heads(key_rows),
            to_heads(value_rows),
            lengths,
            flag_rows,
        ),
    )
    mixed_c = mixed_c.reshape(-1, D)
    mixed_q = mixed_q.reshape(-1, D)
    outputs = []
    kept = []
    for hidden_in, mixed in ((hidden_c, mixed_c), (hidden_q, mixed_q)):
        resid = hidden_in + jnp.dot(mixed, attn_w[3], preferred_element_type=jnp.float32) + bias_o
        normed = layer_norm(resid, gain_one, shift_one)
        pre_act = (
            jnp.dot(normed.astype(jnp.bfloat16), inner_w, preferred_element_type=jnp.float32)
            + hidden_bias
        )
        active = jax.nn.gelu(pre_act, approximate=True).astype(jnp.bfloat16)
        summed = normed + jnp.dot(active, outer_w, preferred_element_type=jnp.float32) + bias_two
        outputs.append(layer_norm(summed, gain_two, shift_two))
        kept.append((resid, summed, pre_act))
    saved = (
        hidden_c,
        hidden_q,
        query_c,
        query_q,
        key_rows,
        value_rows,
        lse_c,
        lse_q,
        mixed_c,
        mixed_q,
        kept[0],
        kept[1],
    )
    return (outputs[0], outputs[1], saved)


def backward_layer(saved, weights, grad_c, grad_q, lengths, flag_rows, onehot):
    attn_w, inner_w, outer_w, small_w = weights
    pieces, hidden_bias, bias_table = unpack(small_w.astype(jnp.float32))
    bias_q, bias_v, bias_o, gain_one, shift_one, bias_two, gain_two, shift_two = pieces
    table_low = bias_table.astype(jnp.bfloat16)
    (
        hidden_c,
        hidden_q,
        query_c,
        query_q,
        key_rows,
        value_rows,
        lse_c,
        lse_q,
        mixed_c,
        mixed_q,
        kept_c,
        kept_q,
    ) = saved
    gelu_tanh = partial(jax.nn.gelu, approximate=True)
    grad_outer = jnp.zeros(outer_w.shape, jnp.float32)
    grad_inner = jnp.zeros(inner_w.shape, jnp.float32)
    grad_attn_out = jnp.zeros((D, D), jnp.float32)
    grad_bias_two = jnp.zeros((D,), jnp.float32)
    grad_hidden_bias = jnp.zeros((FF,), jnp.float32)
    grad_bias_o = jnp.zeros((D,), jnp.float32)
    grad_gain_one = jnp.zeros((D,), jnp.float32)
    grad_shift_one = jnp.zeros((D,), jnp.float32)
    grad_gain_two = jnp.zeros((D,), jnp.float32)
    grad_shift_two = jnp.zeros((D,), jnp.float32)
    residual_grads = []
    mix_grads = []
    for kept_rows, grad_out, mixed in ((kept_c, grad_c, mixed_c), (kept_q, grad_q, mixed_q)):
        resid, summed, pre_act = kept_rows
        normed, norm_one_back = jax.vjp(layer_norm, resid, gain_one, shift_one)
        unused_out, norm_two_back = jax.vjp(layer_norm, summed, gain_two, shift_two)
        grad_summed, grad_g2, grad_s2 = norm_two_back(grad_out)
        grad_gain_two = grad_gain_two + grad_g2
        grad_shift_two = grad_shift_two + grad_s2
        grad_branch = grad_summed.astype(jnp.bfloat16)
        grad_bias_two = grad_bias_two + jnp.sum(grad_branch.astype(jnp.float32), axis=0)
        active, gelu_back = jax.vjp(gelu_tanh, pre_act)
        grad_outer = grad_outer + jnp.einsum(
            "tf,td->fd",
            active.astype(jnp.bfloat16),
            grad_branch,
            preferred_element_type=jnp.float32,
        )
        grad_active = jnp.einsum(
            "td,fd->tf", grad_branch, outer_w, preferred_element_type=jnp.float32
        )
        grad_pre = gelu_back(grad_active)[0].astype(jnp.bfloat16)
        grad_hidden_bias = grad_hidden_bias + jnp.sum(grad_pre.astype(jnp.float32), axis=0)
        grad_inner = grad_inner + jnp.einsum(
            "td,tf->df", normed.astype(jnp.bfloat16), grad_pre, preferred_element_type=jnp.float32
        )
        grad_normed = grad_summed + jnp.einsum(
            "tf,df->td", grad_pre, inner_w, preferred_element_type=jnp.float32
        )
        grad_resid, grad_g1, grad_s1 = norm_one_back(grad_normed)
        grad_gain_one = grad_gain_one + grad_g1
        grad_shift_one = grad_shift_one + grad_s1
        grad_proj = grad_resid.astype(jnp.bfloat16)
        grad_bias_o = grad_bias_o + jnp.sum(grad_proj.astype(jnp.float32), axis=0)
        grad_attn_out = grad_attn_out + jnp.einsum(
            "td,te->de", mixed, grad_proj, preferred_element_type=jnp.float32
        )
        mix_grads.append(
            jnp.einsum(
                "te,de->td", grad_proj, attn_w[3], preferred_element_type=jnp.float32
            ).astype(jnp.bfloat16)
        )
        residual_grads.append(grad_resid)
    grad_query_c, grad_query_q, grad_keys, grad_values, grad_table = lax.map(
        partial(attend_back, onehot, table_low),
        (
            to_heads(query_c),
            to_heads(query_q),
            to_heads(key_rows),
            to_heads(value_rows),
            lengths,
            flag_rows,
            lse_c,
            lse_q,
            to_heads(mix_grads[0]),
            to_heads(mix_grads[1]),
        ),
    )
    grad_table = jnp.sum(grad_table, axis=0)
    low_query_c = grad_query_c.reshape(-1, D).astype(jnp.bfloat16)
    low_query_q = grad_query_q.reshape(-1, D).astype(jnp.bfloat16)
    low_keys = grad_keys.reshape(-1, D).astype(jnp.bfloat16)
    low_values = grad_values.reshape(-1, D).astype(jnp.bfloat16)
    low_c = hidden_c.astype(jnp.bfloat16)
    low_q = hidden_q.astype(jnp.bfloat16)
    stacked_grads = jnp.stack([low_query_c, low_keys, low_values])
    grad_qkv = jnp.einsum("td,ste->sde", low_c, stacked_grads, preferred_element_type=jnp.float32)
    grad_wq = grad_qkv[0] + jnp.einsum(
        "td,te->de", low_q, low_query_q, preferred_element_type=jnp.float32
    )
    grad_attn = jnp.stack([grad_wq, grad_qkv[1], grad_qkv[2], grad_attn_out])
    grad_bias_q = jnp.sum(low_query_c.astype(jnp.float32), axis=0) + jnp.sum(
        low_query_q.astype(jnp.float32), axis=0
    )
    grad_bias_v = jnp.sum(low_values.astype(jnp.float32), axis=0)
    grad_content = residual_grads[0] + jnp.einsum(
        "ste,sde->td", stacked_grads, attn_w[:3], preferred_element_type=jnp.float32
    )
    grad_query_in = residual_grads[1] + jnp.einsum(
        "te,de->td", low_query_q, attn_w[0], preferred_element_type=jnp.float32
    )
    grad_small = jnp.concatenate(
        [
            grad_bias_q,
            grad_bias_v,
            grad_bias_o,
            grad_gain_one,
            grad_shift_one,
            grad_bias_two,
            grad_gain_two,
            grad_shift_two,
            grad_hidden_bias,
            grad_table.reshape(-1),
        ]
    )
    return (grad_content, grad_query_in, (grad_attn, grad_inner, grad_outer, grad_small))


def adam_update(master, first, second, grad, rate):
    first_new = BETA_ONE * first + (1.0 - BETA_ONE) * grad
    second_new = BETA_TWO * second + (1.0 - BETA_TWO) * grad * grad
    first_hat = first_new / (1.0 - BETA_ONE**STEP)
    second_hat = second_new / (1.0 - BETA_TWO**STEP)
    master_new = master - rate * (
        first_hat / (jnp.sqrt(second_hat) + ADAM_EPS) + WEIGHT_DECAY * master
    )
    return (master_new, first_new, second_new)


def per_device(
    content,
    query,
    lengths,
    predicted,
    content_cot,
    query_cot,
    attn_master,
    attn_first,
    attn_second,
    inner_master,
    inner_first,
    inner_second,
    outer_master,
    outer_first,
    outer_second,
    small_master,
    small_first,
    small_second,
):
    masters = (attn_master, inner_master, outer_master, small_master)
    slot_count = lengths.shape[0]
    flag_rows = predicted.reshape(slot_count, LEN)
    onehot = bucket_onehot()
    hidden_c = content.astype(jnp.float32)
    hidden_q = query.astype(jnp.float32)
    kept_weights = []
    saved_layers = []
    small_all = lax.all_gather(
        small_master.astype(jnp.bfloat16), "fsdp", axis=1, tiled=True
    )
    for layer_index in range(LAYERS):
        shards = tuple((master[layer_index] for master in masters[:3]))
        gathered = fetch_forward(shards) + (small_all[layer_index],)
        kept_weights.append(gathered)
        hidden_c, hidden_q, saved = forward_layer(
            hidden_c, hidden_q, gathered, lengths, flag_rows, onehot
        )
        saved_layers.append(saved)
    position = jnp.arange(LEN, dtype=jnp.int32)
    valid_rows = (position[None, :] < lengths[:, None]).reshape(-1, 1).astype(jnp.float32)
    grad_c = content_cot.astype(jnp.float32) * valid_rows
    grad_q = query_cot.astype(jnp.float32) * valid_rows
    layer_grads = [None] * LAYERS
    small_grads = [None] * LAYERS
    for layer_index in reversed(range(LAYERS)):
        grad_c, grad_q, local_grads = backward_layer(
            saved_layers[layer_index],
            kept_weights[layer_index],
            grad_c,
            grad_q,
            lengths,
            flag_rows,
            onehot,
        )
        small_grads[layer_index] = local_grads[3]
        layer_grads[layer_index] = reduce_layer(local_grads[:3])
    small_sum = lax.psum(jnp.stack(small_grads), ("dp", "fsdp"))
    owned = small_master.shape[1]
    small_own = lax.dynamic_slice_in_dim(
        small_sum, lax.axis_index("fsdp") * owned, owned, 1
    )
    reduced = tuple(
        (
            jnp.stack([layer_grads[layer_index][member] for layer_index in range(LAYERS)])
            for member in range(3)
        )
    ) + (small_own,)
    attn_new = adam_update(attn_master, attn_first, attn_second, reduced[0], ATTENTION_RATE)
    inner_new = adam_update(inner_master, inner_first, inner_second, reduced[1], FEED_RATE)
    outer_new = adam_update(outer_master, outer_first, outer_second, reduced[2], FEED_RATE)
    small_new = adam_update(small_master, small_first, small_second, reduced[3], SMALL_RATE)
    return (
        hidden_c.astype(jnp.bfloat16),
        hidden_q.astype(jnp.bfloat16),
        grad_c,
        grad_q,
        attn_new[0],
        attn_new[1],
        attn_new[2],
        inner_new[0],
        inner_new[1],
        inner_new[2],
        outer_new[0],
        outer_new[1],
        outer_new[2],
        small_new[0],
        small_new[1],
        small_new[2],
    )


def quarter_of(kind, shard, quarter):
    if kind == "attn":
        return lax.dynamic_index_in_dim(shard, quarter, 0, keepdims=False)
    if kind == "inner":
        return lax.dynamic_slice_in_dim(shard, quarter * D, D, 1)
    return lax.dynamic_slice_in_dim(shard, quarter * ROWS, ROWS, 0)


def after(value, *others):
    return lax.optimization_barrier((value, others))[0]


def own_blocks(kinds, shards, place, side):
    quarter = (place[0] ^ side) * 2 + place[1]
    return jnp.stack([quarter_of(kind, shard, quarter) for kind, shard in zip(kinds, shards)])


def gather_group(count, shards, plane, column, sides, corners, mine, theirs):
    plan = []
    for core, arrays in enumerate((mine, theirs)):
        base = core * len(mine)
        for member in range(count):
            array, first = plane
            plan += [
                (base + array, first + side * count + member, side, 1, core, 0, member)
                for side in range(2)
            ]
            for apart in (1, 2, 3):
                index = (apart - 1) * count + member
                array, first = column
                plan.append((base + array, first + index, 0, 0, core, apart, member))
                for dx, dy, (array, first) in ((1, 0, sides[0]), (0, 1, sides[1])):
                    plan.append((base + array, first + index, dx, dy, core, apart, member))
                skipped = 0
                for array, first, held in corners:
                    if skipped <= index < skipped + held:
                        plan.append(
                            (base + array, first + index - skipped, 1, 1, core, apart, member)
                        )
                    skipped += held
    return (tuple(plan), tuple(shards) + tuple(mine) + tuple(theirs))


def gather_small(shard, place):
    z, y = place[2], place[3]
    pair = jnp.stack([shard, swap_z(shard, 1)])
    blocks = jnp.concatenate([pair, swap_z(pair, 2)])
    low, high = z % 2, z // 2
    blocks = jnp.where(low == 0, blocks, blocks[jnp.array([1, 0, 3, 2])])
    blocks = jnp.where(high == 0, blocks, blocks[jnp.array([2, 3, 0, 1])])
    other = swap_y(blocks)
    pairs = jnp.where(y == 0, jnp.stack([blocks, other], 1), jnp.stack([other, blocks], 1))
    return pairs.transpose(2, 0, 1, 3).reshape(shard.shape[0], -1)


def sum_small(value):
    value = value + swap_core(value)
    value = value + swap_x(value)
    value = value + swap_y(value)
    value = value + swap_z(value, 1)
    return value + swap_z(value, 2)


def add_low(*values):
    total = values[0].astype(jnp.float32)
    for value in values[1:]:
        total = total + value.astype(jnp.float32)
    return total.astype(jnp.bfloat16)


def reduce_corners(keep, get):
    corner = add_low(keep[1, 1], get[1, 1])
    return (swap_x(corner[:2]), swap_y(corner[2:]))


def reduce_sides(keep, get, corners):
    by_x, by_y = corners
    for_y = jnp.concatenate([add_low(keep[1, 0, :2], get[1, 0, :2], by_x), add_low(keep[1, 0, 2:], get[1, 0, 2:])])
    for_x = jnp.concatenate([add_low(keep[0, 1, :2], get[0, 1, :2]), add_low(keep[0, 1, 2:], get[0, 1, 2:], by_y)])
    return (swap_x(for_x), swap_y(for_y))


def reduce_column(keep, get, sides):
    return add_low(keep[0, 0], get[0, 0], *sides)


def at_z(column, place, apart):
    return lax.dynamic_index_in_dim(column, place[2] ^ apart, 0, keepdims=False)


def reduce_far(column, place):
    return swap_z(jnp.stack([at_z(column, place, 2), at_z(column, place, 3)]), 2)


def reduce_near(column, far, place):
    return swap_z(add_low(at_z(column, place, 1), far[1]), 1)


def reduce_total(column, far, near, place):
    return add_low(at_z(column, place, 0), far[0], near)


def reduce_direct(column, place):
    return tuple(swap_z(at_z(column, place, apart), apart) for apart in (1, 2, 3))


def direct_total(column, shifts, place):
    return add_low(at_z(column, place, 0), *shifts)


def share_quarters(own, place):
    x, c = place[0], place[1]
    pair = jnp.stack([own, swap_x(own)])
    other = swap_core(pair)
    cores = jnp.where(c == 0, jnp.stack([pair, other], 1), jnp.stack([other, pair], 1))
    sides = jnp.where(x == 0, cores, cores[::-1])
    return sides.reshape((4,) + own.shape)


def small_parts(vectors):
    values = vectors.astype(jnp.float32)
    return (
        values[: 8 * D].reshape(8, D),
        values[8 * D : 8 * D + FF].reshape(1, FF),
        bias_vectors(values[8 * D + FF :].reshape(H, NB)),
    )


def per_device_fast(
    content,
    query,
    lengths,
    predicted,
    content_cot,
    query_cot,
    attn_master,
    attn_first,
    attn_second,
    inner_master,
    inner_first,
    inner_second,
    outer_master,
    outer_first,
    outer_second,
    small_master,
    small_first,
    small_second,
):
    place_parts = my_place()
    place = jnp.stack(place_parts).astype(jnp.int32)
    small_all = gather_small(small_master.astype(jnp.bfloat16), place_parts)
    attn_kinds, feed_kinds = ("attn",), ("inner", "outer")
    attn_low = [attn_master[layer].astype(jnp.bfloat16) for layer in range(LAYERS)]
    feed_low = [
        (inner_master[layer].astype(jnp.bfloat16), outer_master[layer].astype(jnp.bfloat16))
        for layer in range(LAYERS)
    ]
    own_a0, own_a1 = (own_blocks(attn_kinds, (w,), place_parts, 0) for w in attn_low)
    own_f0, own_f1 = (own_blocks(feed_kinds, w, place_parts, 0) for w in feed_low)
    oth_a0, oth_a1 = (own_blocks(attn_kinds, (w,), place_parts, 1) for w in attn_low)
    oth_f0, oth_f1 = (own_blocks(feed_kinds, w, place_parts, 1) for w in feed_low)
    near_a0 = swap_z(own_a0, 1)
    far_a0 = swap_z(jnp.concatenate([own_a0, near_a0]), 2)
    plane_a0 = swap_y(jnp.concatenate([own_a0, oth_a0]))
    near_f0 = swap_z(after(own_f0, near_a0), 1)
    plane_f0 = swap_y(after(jnp.concatenate([own_f0, oth_f0]), plane_a0))
    col_a0 = jnp.concatenate([near_a0, far_a0])
    x0 = swap_x(col_a0)
    y0 = swap_y(after(col_a0, plane_a0))
    far_f0 = swap_z(jnp.concatenate([own_f0, near_f0]), 2)
    far_f0_in = after(far_f0, x0, y0)
    near_a1 = swap_z(after(own_a1, near_f0), 1)
    near_f1 = swap_z(after(own_f1, near_a1), 1)
    mine_0 = jnp.concatenate([plane_a0, col_a0, x0, y0])
    theirs_0 = swap_core(after(mine_0, plane_f0))
    col_f0 = jnp.concatenate([near_f0, far_f0_in])
    x1 = swap_x(jnp.concatenate([col_f0, y0[:2]]))
    y1 = swap_y(jnp.concatenate([col_f0, x0[2:]]))
    far_a1 = swap_z(after(jnp.concatenate([own_a1, near_a1]), far_f0), 2)
    col_a1 = jnp.concatenate([near_a1, far_a1])
    mine_p0 = jnp.concatenate([plane_f0, col_f0])
    theirs_p0 = swap_core(mine_p0)
    mine_1 = jnp.concatenate([x1, y1])
    theirs_1 = swap_core(mine_1)
    group_a0 = gather_group(
        1, (attn_low[0],), (0, 0), (0, 2), ((0, 5), (0, 8)), ((1, 6, 2), (1, 14, 1)),
        (mine_0, mine_1), (theirs_0, theirs_1),
    )
    x2 = swap_x(jnp.concatenate([after(col_a1, x1, y1), y1[:4]]))
    y2 = swap_y(jnp.concatenate([after(col_a1, x1, y1), x1[4:6]]))
    plane_a1 = swap_y(after(jnp.concatenate([own_a1, oth_a1]), x1, y1))
    far_f1 = swap_z(after(jnp.concatenate([own_f1, near_f1]), far_a1, x1, y1), 2)
    row_flags = predicted.reshape(1, LEN).astype(jnp.float32)
    col_flags = predicted.reshape(LEN, 1).astype(jnp.float32)
    low0 = jnp.concatenate([content, query])
    hidden0 = low0.astype(jnp.float32)
    small0, hidden_bias0, (tvec0, far0, onehot) = small_parts(small_all[0])
    small1, hidden_bias1, (tvec1, far1, onehot) = small_parts(small_all[1])
    valid = (jnp.arange(LEN, dtype=jnp.int32) < lengths[0])[:, None].astype(jnp.float32)
    grads = (content_cot.astype(jnp.float32) * valid, query_cot.astype(jnp.float32) * valid)
    q0, k0, v0, attn0 = project(place, low0, small0, group_a0)
    q0_late = after(q0, far_f1)
    mixed0, p0, inverse0, dead = mix(
        lengths, far0, tvec0, q0_late, k0, v0, row_flags, col_flags
    )
    x2, y2, plane_a1 = after((x2, y2, plane_a1), mixed0)
    mine_2 = jnp.concatenate([plane_a1, col_a1, x2, y2])
    theirs_2 = swap_core(mine_2)
    group_f0 = gather_group(
        2, feed_low[0], (0, 0), (0, 4), ((1, 0), (1, 8)), ((2, 8, 4), (2, 15, 2)),
        (mine_p0, mine_1, mine_2), (theirs_p0, theirs_1, theirs_2),
    )
    far_f1 = after(far_f1, x2, y2)
    col_f1 = jnp.concatenate([near_f1, far_f1])
    x3 = swap_x(jnp.concatenate([col_f1, y2[:3]]))
    y3 = swap_y(col_f1)
    plane_f1 = swap_y(after(jnp.concatenate([own_f1, oth_f1]), x2, y2))
    resid0, summed0, pre0, normed0, hidden1, low1 = feed(
        place, small0, hidden_bias0, mixed0, hidden0, attn0, group_f0
    )
    x3, y3, plane_f1 = after((x3, y3, plane_f1), low1)
    x4 = swap_x(y3[:3])
    y4 = swap_y(x3[3:6])
    mine_3 = jnp.concatenate([x3[6:], x3[:6], y3])
    theirs_3 = swap_core(mine_3)
    group_a1 = gather_group(
        1, (attn_low[1],), (0, 0), (0, 2), ((0, 5), (0, 12)), ((1, 0, 3),),
        (mine_2, mine_3), (theirs_2, theirs_3),
    )
    q1, k1, v1, attn1 = project(place, low1, small1, group_a1)
    x4, y4 = after((x4, y4), q1)
    mine_4 = jnp.concatenate([plane_f1, col_f1, x4, y4])
    theirs_4 = swap_core(mine_4)
    group_f1 = gather_group(
        2, feed_low[1], (0, 0), (0, 4), ((1, 3), (1, 9)), ((0, 10, 3), (0, 13, 3)),
        (mine_4, mine_3), (theirs_4, theirs_3),
    )
    mixed1, p1, inverse1, dead = mix(
        lengths, far1, tvec1, q1, k1, v1, row_flags, col_flags
    )
    resid1, summed1, pre1, normed1, unused, low_out = feed(
        place, small1, hidden_bias1, mixed1, hidden1, attn1, group_f1
    )
    dresid1, dmix1, dwo1, keep_f1, send_f1, vec_f1, dhidden1 = feed_back(
        place, small1, grads, summed1, normed1, resid1, pre1, mixed1, attn1, group_f1
    )
    get_f1 = swap_core(send_f1)
    first1 = mix_back(0, q1, k1, v1, dmix1, mixed1, p1, inverse1, dead)
    by_f1 = reduce_corners(keep_f1, after(get_f1, first1[0]))
    second1 = mix_back(
        3, after(q1, get_f1, first1[0]), k1, v1, dmix1, mixed1, p1, inverse1, dead
    )
    sides_rf1 = reduce_sides(keep_f1, get_f1, after(by_f1, second1[0]))
    keep_a1, send_a1, vec_a1 = weight_back(
        place, low1, after(first1[:3], by_f1), second1[:3], dwo1
    )
    get_a1 = swap_core(send_a1)
    grads = input_back(after(first1[:3], keep_a1), second1[:3], attn1, dresid1)
    by_a1 = reduce_corners(keep_a1, after(get_a1, grads[0]))
    dresid0, dmix0, dwo0, keep_f0, send_f0, vec_f0, dhidden0 = feed_back(
        place, small0, after(grads, get_a1), summed0, normed0, resid0, pre0, mixed0, attn0, group_f0
    )
    get_f0 = swap_core(after(send_f0, sides_rf1))
    sides_ra1 = reduce_sides(keep_a1, get_a1, after(by_a1, dmix0))
    column_f1 = reduce_column(keep_f1, get_f1, after(sides_rf1, dmix0))
    zfar_f1 = reduce_far(column_f1, place_parts)
    first0 = mix_back(
        0, q0, k0, v0, after(dmix0, by_a1, sides_rf1), mixed0, p0, inverse0, dead
    )
    by_f0 = reduce_corners(keep_f0, after(get_f0, first0[0]))
    second0 = mix_back(
        3, after(q0, get_f0, first0[0]), k0, v0, dmix0, mixed0, p0, inverse0, dead
    )
    zfar_f1, sides_ra1 = after((zfar_f1, sides_ra1), second0[0])
    keep_a0, send_a0, vec_a0 = weight_back(
        place, low0, after(first0[:3], by_f0), second0[:3], dwo0
    )
    sides_rf0 = reduce_sides(keep_f0, get_f0, after(by_f0, second0[0]))
    get_a0 = swap_core(send_a0)
    by_a0 = reduce_corners(keep_a0, get_a0)
    znear_f1 = reduce_near(column_f1, after(zfar_f1, get_a0), place_parts)
    column_a1 = reduce_column(keep_a1, get_a1, after(sides_ra1, get_a0))
    zfar_a1 = reduce_far(column_a1, place_parts)
    content_grad, query_grad = input_back(after(first0[:3], get_a0), second0[:3], attn0, dresid0)
    column_f0 = reduce_column(keep_f0, get_f0, after(sides_rf0, content_grad))
    zfar_f0 = reduce_far(column_f0, place_parts)
    sides_ra0 = reduce_sides(keep_a0, get_a0, after(by_a0, column_f0))
    znear_a1 = reduce_near(column_a1, after(zfar_a1, column_f0), place_parts)
    four_f1 = share_quarters(
        reduce_total(column_f1, zfar_f1, after(znear_f1, column_f0), place_parts), place_parts
    )
    column_a0 = reduce_column(keep_a0, get_a0, sides_ra0)
    shifts_a0 = reduce_direct(after(column_a0, zfar_f0), place_parts)
    znear_f0 = reduce_near(column_f0, zfar_f0, place_parts)
    four_a1 = share_quarters(
        reduce_total(column_a1, zfar_a1, after(znear_a1, column_a0), place_parts), place_parts
    )
    four_f0 = share_quarters(
        reduce_total(column_f0, zfar_f0, znear_f0, place_parts), place_parts
    )
    attn_state = (attn_master, attn_first, attn_second)
    inner_state = (inner_master, inner_first, inner_second)
    outer_state = (outer_master, outer_first, outer_second)
    inner_new = adam("inner", 1, FEED_RATE, inner_state, four_f1, 0, None)
    outer_new = adam("outer", 1, FEED_RATE, outer_state, four_f1, 1, None)
    attn_new = adam("attn", 1, ATTENTION_RATE, attn_state, four_a1, 0, None)
    shifts_a0 = after(shifts_a0, inner_new, outer_new, attn_new)
    four_a0 = share_quarters(direct_total(column_a0, shifts_a0, place_parts), place_parts)
    small_grads = [
        jnp.concatenate(
            [
                attn_vec.reshape(-1),
                feed_vec[2:].reshape(-1),
                dhidden.reshape(-1),
                table_grad(jnp.concatenate([first[3], second[3]]), onehot).reshape(-1),
            ]
        )
        for attn_vec, feed_vec, dhidden, first, second in (
            (vec_a0, vec_f0, dhidden0, first0, second0),
            (vec_a1, vec_f1, dhidden1, first1, second1),
        )
    ]
    small_sum = sum_small(after(jnp.stack(small_grads), column_a0))
    size = small_master.shape[1]
    small_own = lax.dynamic_slice_in_dim(small_sum, lax.axis_index("fsdp") * size, size, 1)
    inner_new = adam("inner", 0, FEED_RATE, inner_state, four_f0, 0, tuple(inner_new))
    outer_new = adam("outer", 0, FEED_RATE, outer_state, four_f0, 1, tuple(outer_new))
    attn_new = adam("attn", 0, ATTENTION_RATE, attn_state, four_a0, 0, tuple(attn_new))
    small_new = adam_update(small_master, small_first, small_second, small_own, SMALL_RATE)
    return (
        (low_out[:LEN], low_out[LEN:], content_grad, query_grad)
        + tuple(attn_new)
        + tuple(inner_new)
        + tuple(outer_new)
        + small_new
    )


def solution(mesh):
    placed = (
        P(("dp", "fsdp"), None),
        P(("dp", "fsdp"), None),
        P(("dp", "fsdp")),
        P(("dp", "fsdp")),
        P(("dp", "fsdp"), None),
        P(("dp", "fsdp"), None),
        P(None, None, "fsdp", None),
        P(None, None, "fsdp", None),
        P(None, None, "fsdp", None),
        P(None, "fsdp", None),
        P(None, "fsdp", None),
        P(None, "fsdp", None),
        P(None, "fsdp", None),
        P(None, "fsdp", None),
        P(None, "fsdp", None),
        P(None, "fsdp"),
        P(None, "fsdp"),
        P(None, "fsdp"),
    )
    fast = tuple(mesh.shape.values()) == (4, 8)
    return jax.shard_map(
        per_device_fast if fast else per_device,
        mesh=mesh,
        in_specs=placed,
        out_specs=(
            P(("dp", "fsdp"), None),
            P(("dp", "fsdp"), None),
            P(("dp", "fsdp"), None),
            P(("dp", "fsdp"), None),
            P(None, None, "fsdp", None),
            P(None, None, "fsdp", None),
            P(None, None, "fsdp", None),
            P(None, "fsdp", None),
            P(None, "fsdp", None),
            P(None, "fsdp", None),
            P(None, "fsdp", None),
            P(None, "fsdp", None),
            P(None, "fsdp", None),
            P(None, "fsdp"),
            P(None, "fsdp"),
            P(None, "fsdp"),
        ),
        check_vma=False,
    )
```

```python
from functools import partial

import jax
import jax.numpy as jnp
from jax import lax
from jax.experimental import pallas as pl
from jax.experimental.pallas import tpu as pltpu
from jax.sharding import PartitionSpec as P

D = 768
H = 12
DH = 64
FF = 3072
LEN = 512
NB = 32
LAYERS = 2
STEP = 10


NORM_EPS = 1e-05
MASKED = -1000000000.0
BETA_ONE = 0.9
BETA_TWO = 0.999
ATTENTION_RATE = 0.1
FEED_RATE = 0.02
SMALL_RATE = 0.4
WEIGHT_DECAY = 0.01
ADAM_EPS = 1e-08
SCORE_SCALE = 0.125


def layer_norm(values, gain, shift):
    centre = values - jnp.mean(values, axis=-1, keepdims=True)
    spread = jnp.mean(centre * centre, axis=-1, keepdims=True)
    return centre * lax.rsqrt(spread + NORM_EPS) * gain + shift


def unpack(vectors):
    pieces = [vectors[piece_index * D : (piece_index + 1) * D] for piece_index in range(8)]
    hidden_bias = vectors[8 * D : 8 * D + FF]
    bias_table = vectors[8 * D + FF :].reshape(H, NB)
    return (pieces, hidden_bias, bias_table)


def bucket_ids():
    position = jnp.arange(LEN, dtype=jnp.int32)
    offset = position[None, :] - position[:, None]
    distance = jnp.abs(offset)
    far_bucket = jnp.full(distance.shape, 8, jnp.int32)
    for exponent in range(1, 8):
        far_bucket = far_bucket + (distance * distance >= 64 * 2**exponent).astype(jnp.int32)
    near_or_far = jnp.where(distance < 8, distance, far_bucket)
    return near_or_far + NB // 2 * (offset > 0).astype(jnp.int32)


def bucket_onehot():
    return (bucket_ids()[:, :, None] == jnp.arange(NB, dtype=jnp.int32)[None, None, :]).astype(
        jnp.bfloat16
    )


def allowed_pairs(length, pred_flags):
    position = jnp.arange(LEN, dtype=jnp.int32)
    valid_key = (position < length)[None, :]
    row_pos = position[:, None]
    col_pos = position[None, :]
    free_key = (pred_flags == 0)[None, :]
    content_ok = valid_key & (free_key | (pred_flags[:, None] == 1) & (col_pos <= row_pos))
    query_ok = valid_key & (col_pos != row_pos) & (free_key | (col_pos < row_pos))
    return (content_ok, query_ok)


def masked_scores(query_rows, key_rows, position_bias, allowed):
    scores = (
        jnp.einsum("qhd,khd->hqk", query_rows, key_rows, preferred_element_type=jnp.float32)
        * SCORE_SCALE
        + position_bias
    )
    return jnp.where(allowed[None], scores, MASKED)


def table_bias(onehot, table_low):
    return jnp.einsum("qkb,hb->hqk", onehot, table_low, preferred_element_type=jnp.float32)


def attend_slot(onehot, table_low, slot_item):
    query_c, query_q, key_rows, value_rows, length, pred_flags = slot_item
    position_bias = table_bias(onehot, table_low)
    content_ok, query_ok = allowed_pairs(length, pred_flags)
    results = []
    for query_rows, allowed in ((query_c, content_ok), (query_q, query_ok)):
        scores = masked_scores(query_rows, key_rows, position_bias, allowed)
        peak = jnp.max(scores, axis=-1, keepdims=True)
        expos = jnp.exp(scores - peak)
        totals = jnp.sum(expos, axis=-1, keepdims=True)
        probs = (expos / totals).astype(jnp.bfloat16)
        mixed = jnp.einsum(
            "hqk,khd->qhd", probs, value_rows, preferred_element_type=jnp.float32
        ).astype(jnp.bfloat16)
        results.append((mixed, peak[..., 0] + jnp.log(totals[..., 0])))
    return (results[0][0], results[1][0], results[0][1], results[1][1])


def attend_back(onehot, table_low, slot_item):
    (
        query_c,
        query_q,
        key_rows,
        value_rows,
        length,
        pred_flags,
        lse_c,
        lse_q,
        grad_mix_c,
        grad_mix_q,
    ) = slot_item
    position_bias = table_bias(onehot, table_low)
    content_ok, query_ok = allowed_pairs(length, pred_flags)
    grad_keys = jnp.zeros(key_rows.shape, jnp.float32)
    grad_values = jnp.zeros(value_rows.shape, jnp.float32)
    grad_table = jnp.zeros((H, NB), jnp.float32)
    grads_query = []
    for query_rows, allowed, log_total, grad_mix in (
        (query_c, content_ok, lse_c, grad_mix_c),
        (query_q, query_ok, lse_q, grad_mix_q),
    ):
        scores = masked_scores(query_rows, key_rows, position_bias, allowed)
        probs = jnp.exp(scores - log_total[..., None])
        grad_values = grad_values + jnp.einsum(
            "hqk,qhd->khd", probs.astype(jnp.bfloat16), grad_mix, preferred_element_type=jnp.float32
        )
        grad_probs = jnp.einsum(
            "qhd,khd->hqk", grad_mix, value_rows, preferred_element_type=jnp.float32
        )
        grad_scores = probs * (grad_probs - jnp.sum(probs * grad_probs, axis=-1, keepdims=True))
        grad_scores = jnp.where(allowed[None], grad_scores, 0.0).astype(jnp.bfloat16)
        grad_table = grad_table + jnp.einsum(
            "hqk,qkb->hb", grad_scores, onehot, preferred_element_type=jnp.float32
        )
        grads_query.append(
            jnp.einsum("hqk,khd->qhd", grad_scores, key_rows, preferred_element_type=jnp.float32)
            * SCORE_SCALE
        )
        grad_keys = (
            grad_keys
            + jnp.einsum(
                "hqk,qhd->khd", grad_scores, query_rows, preferred_element_type=jnp.float32
            )
            * SCORE_SCALE
        )
    return (grads_query[0], grads_query[1], grad_keys, grad_values, grad_table)


def to_heads(values):
    return values.reshape(-1, LEN, H, DH)


AXES = ("dp", "fsdp")
GRID = (2, 2, 4, 2)
ROWS = 96


def places():
    return [
        (x, c, z, y) for x in range(2) for c in range(2) for z in range(4) for y in range(2)
    ]


def flat(x, c, z, y):
    return ((x * 2 + c) * 4 + z) * 2 + y


def move(value, shift):
    pairs = [(flat(*place), flat(*shift(*place))) for place in places()]
    return lax.ppermute(value, AXES, pairs)


def swap_core(value):
    return move(value, lambda x, c, z, y: (x, 1 - c, z, y))


def swap_x(value):
    return move(value, lambda x, c, z, y: (1 - x, c, z, y))


def swap_y(value):
    return move(value, lambda x, c, z, y: (x, c, z, 1 - y))


def swap_z(value, apart):
    return move(value, lambda x, c, z, y: (x, c, z ^ apart, y))


def my_place():
    dp = lax.axis_index("dp")
    fsdp = lax.axis_index("fsdp")
    return (dp // 2, dp % 2, fsdp // 2, fsdp % 2)


def dot_nn(left, right):
    return jnp.dot(left, right, preferred_element_type=jnp.float32)


def dot_nt(left, right):
    return lax.dot_general(
        left, right, (((1,), (1,)), ((), ())), preferred_element_type=jnp.float32
    )


def dot_tn(left, right):
    return lax.dot_general(
        left, right, (((0,), (0,)), ((), ())), preferred_element_type=jnp.float32
    )


ANY_SPEC = pl.BlockSpec(memory_space=pl.ANY)
VMEM_SPEC = pl.BlockSpec(memory_space=pltpu.VMEM)
SMEM_SPEC = pl.BlockSpec(memory_space=pltpu.SMEM)
TALL = 2 * LEN
HALF = 256
PARAMS = pltpu.CompilerParams(vmem_limit_bytes=60 * 1024 * 1024)


def norm_parts(values):
    centre = values - jnp.mean(values, axis=-1, keepdims=True)
    spread = jnp.mean(centre * centre, axis=-1, keepdims=True)
    scale = lax.rsqrt(spread + NORM_EPS)
    return (centre * scale, scale)


def norm_back(unit, scale, grad, gain):
    scaled = grad * gain
    return scale * (
        scaled
        - jnp.mean(scaled, axis=-1, keepdims=True)
        - unit * jnp.mean(scaled * unit, axis=-1, keepdims=True)
    )


def start_fetch(kinds, plan, place_ref, refs, targets, sems):
    x, c, z, y = (place_ref[index] for index in range(4))
    mine = z * 2 + y
    copies = []

    def start(source, target):
        copy = pltpu.make_async_copy(source, target, sems.at[len(copies)])
        copy.start()
        copies.append(copy)

    for member, kind in enumerate(kinds):
        target = targets[member]
        if kind == "attn":
            start(refs[member], target.at[:, pl.ds(pl.multiple_of(mine * ROWS, ROWS), ROWS), :])
        elif kind == "inner":
            for quarter in range(4):
                start(
                    refs[member].at[:, quarter * D : quarter * D + D],
                    target.at[quarter, pl.ds(pl.multiple_of(mine * ROWS, ROWS), ROWS), :],
                )
        else:
            start(refs[member], target.at[z, pl.ds(pl.multiple_of(y * 384, ROWS), 384), :])
    for array, index, dx, dy, dc, dz, member in plan:
        quarter = (x ^ dx) * 2 + (c ^ dc)
        if kinds[member] == "outer":
            lead, row = z ^ dz, (y ^ dy) * 384 + quarter * ROWS
        else:
            lead, row = quarter, ((z ^ dz) * 2 + (y ^ dy)) * ROWS
        start(
            refs[len(kinds) + array].at[index],
            targets[member].at[lead, pl.ds(pl.multiple_of(row, ROWS), ROWS), :],
        )
    return copies


def project_kernel(plan, place_ref, low_ref, small_ref, *refs):
    pieces = refs[:-7]
    q_ref, k_ref, v_ref, w_out, w_ref, sems, out_sem = refs[-7:]
    for copy in start_fetch(("attn",), plan, place_ref, pieces, (w_ref,), sems):
        copy.wait()
    keep = pltpu.make_async_copy(w_ref, w_out, out_sem)
    keep.start()
    bias_q = small_ref[0:1, :]
    bias_v = small_ref[1:2, :]
    for row in range(0, TALL, HALF):
        rows = low_ref[row : row + HALF, :]
        q_ref[row : row + HALF, :] = (dot_nn(rows, w_ref[0]) + bias_q).astype(jnp.bfloat16)
        if row < LEN:
            k_ref[row : row + HALF, :] = dot_nn(rows, w_ref[1]).astype(jnp.bfloat16)
            v_ref[row : row + HALF, :] = (dot_nn(rows, w_ref[2]) + bias_v).astype(jnp.bfloat16)
    keep.wait()


def project(place, low, small, group):
    plan, pieces = group
    return pl.pallas_call(
        partial(project_kernel, plan),
        out_shape=[
            jax.ShapeDtypeStruct((TALL, D), jnp.bfloat16),
            jax.ShapeDtypeStruct((LEN, D), jnp.bfloat16),
            jax.ShapeDtypeStruct((LEN, D), jnp.bfloat16),
            jax.ShapeDtypeStruct((4, D, D), jnp.bfloat16),
        ],
        in_specs=[SMEM_SPEC, VMEM_SPEC, VMEM_SPEC] + [ANY_SPEC] * len(pieces),
        out_specs=[VMEM_SPEC] * 3 + [ANY_SPEC],
        scratch_shapes=[
            pltpu.VMEM((4, D, D), jnp.bfloat16),
            pltpu.SemaphoreType.DMA((32,)),
            pltpu.SemaphoreType.DMA,
        ],
        compiler_params=PARAMS,
        cost_estimate=pl.CostEstimate(flops=2 * 2048 * D * D, bytes_accessed=16000000, transcendentals=0),
        name="project",
    )(place, low, small, *pieces)


def build_masks(length, row_flags, col_flags, mask_ref, alive_ref):
    flags = row_flags[...]

    def body(step, carry):
        start = pl.multiple_of(step * 64, 64)
        key = lax.broadcasted_iota(jnp.int32, (64, LEN), 0) + start
        query = lax.broadcasted_iota(jnp.int32, (64, LEN), 1)
        valid = key < length
        free = jnp.broadcast_to(col_flags[pl.ds(start, 64), :], (64, LEN)) == 0.0
        marked = jnp.broadcast_to(flags, (64, LEN)) == 1.0
        content_ok = valid & (free | (marked & (key <= query)))
        query_ok = valid & (key != query) & (free | (key < query))
        mask_ref[pl.ds(start, 64), :LEN] = content_ok.astype(jnp.float32)
        mask_ref[pl.ds(start, 64), LEN:] = query_ok.astype(jnp.float32)
        return carry

    lax.fori_loop(0, 8, body, 0)
    alive_ref[...] = jnp.max(mask_ref[...], axis=0, keepdims=True)


def build_tiles(t_row, tile_ref):
    spread = jnp.broadcast_to(t_row, (128, 512))
    rolled = pltpu.roll(spread, 0, 1, stride=1, stride_axis=0)
    tile_ref[...] = rolled[:, :384]


def position_bias(tile_ref, far_ref, head, query_block, key_block):
    apart = query_block - key_block
    if apart >= 2:
        return far_ref[head, 0]
    if apart <= -2:
        return far_ref[head, 1]
    return tile_ref[:, 128 * (apart + 1) : 128 * (apart + 2)]


def head_lanes(shape, head):
    lane = lax.broadcasted_iota(jnp.int32, shape, 1)
    return (lane >= 64) if head else (lane < 64)


def mix_kernel(
    length_ref, far_ref, q_ref, k_ref, v_ref, row_flags, col_flags, t_ref,
    a_ref, p_ref, inverse_ref, dead_ref, mask_ref, alive_ref, tile_ref, o_ref,
):
    pair = pl.program_id(0)

    @pl.when(pair == 0)
    def _():
        build_masks(length_ref[0], row_flags, col_flags, mask_ref, alive_ref)
        dead_ref[...] = (1.0 - alive_ref[...]) * (1.0 / LEN)

    keys = k_ref[...].astype(jnp.float32) * SCORE_SCALE
    values_t = v_ref[...].astype(jnp.float32).T.astype(jnp.bfloat16)
    for head in range(2):
        build_tiles(t_ref[head], tile_ref.at[head])
        keys_own = jnp.where(head_lanes(keys.shape, head), keys, 0.0).astype(jnp.bfloat16)
        for chunk in range(4):
            at = chunk * HALF
            scores = dot_nt(keys_own, q_ref[at : at + HALF, :])
            for side in range(2):
                lanes = slice(at + side * 128, at + side * 128 + 128)
                blocks = []
                peak = None
                for key_block in range(4):
                    rows = slice(key_block * 128, key_block * 128 + 128)
                    block = scores[rows, side * 128 : side * 128 + 128] + position_bias(
                        tile_ref.at[head], far_ref, pair * 2 + head, (chunk % 2) * 2 + side, key_block
                    )
                    block = jnp.where(mask_ref[rows, lanes] > 0.0, block, MASKED)
                    blocks.append(block)
                    high = jnp.max(block, axis=0, keepdims=True)
                    peak = high if peak is None else jnp.maximum(peak, high)
                total = None
                for key_block in range(4):
                    rows = slice(key_block * 128, key_block * 128 + 128)
                    expo = jnp.exp(blocks[key_block] - peak)
                    part = jnp.sum(expo, axis=0, keepdims=True)
                    total = part if total is None else total + part
                    p_ref[head, rows, lanes] = expo.astype(jnp.bfloat16)
                inverse = 1.0 / total
                inverse_ref[head, :, lanes] = inverse * alive_ref[:, lanes]
                o_ref[head : head + 1, lanes] = inverse
        mixed = dot_nn(values_t[head * 64 : head * 64 + 64, :], p_ref[head])
        o_ref[8 + head * 64 : 8 + head * 64 + 64, :] = mixed * o_ref[head : head + 1, :]
    a_ref[...] = o_ref[8:, :].T.astype(jnp.bfloat16)


def mix(length, far, tvec, q, k, v, row_flags, col_flags):
    tall = pl.BlockSpec((TALL, 128), lambda p: (0, p))
    short = pl.BlockSpec((LEN, 128), lambda p: (0, p))
    return pl.pallas_call(
        mix_kernel,
        grid=(H // 2,),
        out_shape=[
            jax.ShapeDtypeStruct((TALL, D), jnp.bfloat16),
            jax.ShapeDtypeStruct((H, LEN, TALL), jnp.bfloat16),
            jax.ShapeDtypeStruct((H, 1, TALL), jnp.float32),
            jax.ShapeDtypeStruct((1, TALL), jnp.float32),
        ],
        in_specs=[
            SMEM_SPEC, SMEM_SPEC, tall, short, short,
            pl.BlockSpec((1, LEN), lambda p: (0, 0)),
            pl.BlockSpec((LEN, 1), lambda p: (0, 0)),
            pl.BlockSpec((2, 1, 512), lambda p: (p, 0, 0)),
        ],
        out_specs=[
            tall,
            pl.BlockSpec((2, LEN, TALL), lambda p: (p, 0, 0)),
            pl.BlockSpec((2, 1, TALL), lambda p: (p, 0, 0)),
            pl.BlockSpec((1, TALL), lambda p: (0, 0)),
        ],
        scratch_shapes=[
            pltpu.VMEM((LEN, TALL), jnp.float32),
            pltpu.VMEM((1, TALL), jnp.float32),
            pltpu.VMEM((2, 128, 384), jnp.float32),
            pltpu.VMEM((136, TALL), jnp.float32),
        ],
        compiler_params=PARAMS,
        cost_estimate=pl.CostEstimate(flops=6500000000, bytes_accessed=8000000, transcendentals=6300000),
        name="mix",
    )(length, far, q, k, v, row_flags, col_flags, tvec)


def mix_back_kernel(
    q_ref, k_ref, v_ref, da_ref, a_ref, p_ref, inverse_ref, dead_ref,
    dq_ref, dk_ref, dv_ref, table_ref,
    s_ref, near_ref, da_t, low_t, q_t, g_ref,
):
    keys = k_ref[...].astype(jnp.float32) * SCORE_SCALE
    keys_t = keys.T.astype(jnp.bfloat16)
    q_t[...] = q_ref[...].astype(jnp.float32).T.astype(jnp.bfloat16)
    da_t[...] = da_ref[...].astype(jnp.float32).T
    product = a_ref[...].astype(jnp.float32).T * da_t[...]
    values = v_ref[...].astype(jnp.float32)
    near_ref[...] = jnp.zeros(near_ref.shape, jnp.float32)
    turn = (
        lax.broadcasted_iota(jnp.int32, (128, 128), 0)
        + lax.broadcasted_iota(jnp.int32, (128, 128), 1)
        == 127
    ).astype(jnp.float32)
    deltas = []
    for head in range(2):
        rows = slice(head * 64, head * 64 + 64)
        inverse = inverse_ref[head]
        deltas.append(jnp.sum(product[rows, :], axis=0, keepdims=True) * inverse)
        low_t[rows, :] = (da_t[rows, :] * inverse).astype(jnp.bfloat16)
    for head in range(2):
        own = slice(head * 64, head * 64 + 64)
        values_own = jnp.where(head_lanes(values.shape, head), values, 0.0).astype(jnp.bfloat16)
        delta = deltas[head]
        far_low = jnp.zeros((8, 128), jnp.float32)
        far_high = jnp.zeros((8, 128), jnp.float32)
        for chunk in range(4):
            at = chunk * HALF
            pulls = dot_nn(values_own, low_t[:, at : at + HALF])
            for side in range(2):
                lanes = slice(at + side * 128, at + side * 128 + 128)
                shift = delta[:, lanes]
                query_block = (chunk % 2) * 2 + side
                for key_block in range(4):
                    rows = slice(key_block * 128, key_block * 128 + 128)
                    cols = slice(side * 128, side * 128 + 128)
                    grad = p_ref[head, rows, lanes].astype(jnp.float32) * (
                        pulls[rows, cols] - shift
                    )
                    s_ref[head, rows, lanes] = grad.astype(jnp.bfloat16)
                    apart = query_block - key_block
                    if apart >= 2:
                        far_low = far_low + jnp.sum(grad.reshape(16, 8, 128), axis=0)
                    elif apart <= -2:
                        far_high = far_high + jnp.sum(grad.reshape(16, 8, 128), axis=0)
                    else:
                        near_ref[head, :, 128 * (apart + 1) : 128 * (apart + 2)] += grad
        g_ref[own, :LEN] = dot_nt(low_t[own, :], p_ref[head])
        g_ref[own, LEN:] = dot_nt(q_t[own, :], s_ref[head]) * SCORE_SCALE
        da_t[own, :] = dot_nn(keys_t[own, :], s_ref[head])
        turned = jnp.dot(
            turn, near_ref[head], precision=lax.Precision.HIGHEST, preferred_element_type=jnp.float32
        )
        aligned = pltpu.roll(turned, 0, 1, stride=1, stride_axis=0)
        table_ref[head, :, :512] = jnp.sum(aligned, axis=0, keepdims=True)
        table_ref[head, :, 512:640] = jnp.sum(far_low, axis=0, keepdims=True)
        table_ref[head, :, 640:] = jnp.sum(far_high, axis=0, keepdims=True)
    uniform = dot_nn(dead_ref[...].astype(jnp.bfloat16), da_ref[...])
    dv_ref[...] = (g_ref[:, :LEN].T + uniform).astype(jnp.bfloat16)
    dk_ref[...] = g_ref[:, LEN:].T.astype(jnp.bfloat16)
    dq_ref[...] = da_t[...].T.astype(jnp.bfloat16)


def mix_back(first, q, k, v, da, a, p, inverse, dead):
    tall = pl.BlockSpec((TALL, 128), lambda i: (0, i + first))
    short = pl.BlockSpec((LEN, 128), lambda i: (0, i + first))
    return pl.pallas_call(
        mix_back_kernel,
        grid=(H // 4,),
        out_shape=[
            jax.ShapeDtypeStruct((TALL, D // 2), jnp.bfloat16),
            jax.ShapeDtypeStruct((LEN, D // 2), jnp.bfloat16),
            jax.ShapeDtypeStruct((LEN, D // 2), jnp.bfloat16),
            jax.ShapeDtypeStruct((H // 2, 1, 768), jnp.float32),
        ],
        in_specs=[
            tall, short, short, tall, tall,
            pl.BlockSpec((2, LEN, TALL), lambda i: (i + first, 0, 0)),
            pl.BlockSpec((2, 1, TALL), lambda i: (i + first, 0, 0)),
            pl.BlockSpec((1, TALL), lambda i: (0, 0)),
        ],
        out_specs=[
            pl.BlockSpec((TALL, 128), lambda i: (0, i)),
            pl.BlockSpec((LEN, 128), lambda i: (0, i)),
            pl.BlockSpec((LEN, 128), lambda i: (0, i)),
            pl.BlockSpec((2, 1, 768), lambda i: (i, 0, 0)),
        ],
        scratch_shapes=[
            pltpu.VMEM((2, LEN, TALL), jnp.bfloat16),
            pltpu.VMEM((2, 128, 512), jnp.float32),
            pltpu.VMEM((128, TALL), jnp.float32),
            pltpu.VMEM((128, TALL), jnp.bfloat16),
            pltpu.VMEM((128, TALL), jnp.bfloat16),
            pltpu.VMEM((128, TALL), jnp.float32),
        ],
        compiler_params=PARAMS,
        cost_estimate=pl.CostEstimate(flops=8000000000, bytes_accessed=16000000, transcendentals=0),
        name="mix_back",
    )(q, k, v, da, a, p, inverse, dead)


GELU_SCALE = 0.7978845608028654
GELU_CUBE = 0.044715


def feed_kernel(plan, place_ref, small_ref, hidden_bias_ref, mix_any, hidden_any, attn_any, *refs):
    pieces = refs[:-20]
    (
        resid_out, summed_out, pre_out, normed_out, next_out, low_out,
        mix_ref, hidden_ref, wo_ref, inner_ref, outer_ref, resid_ref, total_ref, normed_ref,
        pre_ref, next_ref, low_ref, sems, load_sems, store_sems,
    ) = refs[-20:]
    loads = [
        pltpu.make_async_copy(mix_any, mix_ref, load_sems.at[0]),
        pltpu.make_async_copy(attn_any.at[3], wo_ref, load_sems.at[1]),
        pltpu.make_async_copy(hidden_any, hidden_ref, load_sems.at[2]),
    ]
    for load in loads:
        load.start()
    fetches = start_fetch(("inner", "outer"), plan, place_ref, pieces, (inner_ref, outer_ref), sems)
    for load in loads:
        load.wait()
    for row in range(0, TALL, HALF):
        rows = slice(row, row + HALF)
        resid = hidden_ref[rows, :] + dot_nn(mix_ref[rows, :], wo_ref[...]) + small_ref[2:3, :]
        resid_ref[rows, :] = resid
        unit, scale = norm_parts(resid)
        normed = unit * small_ref[3:4, :] + small_ref[4:5, :]
        normed_ref[rows, :] = normed.astype(jnp.bfloat16)
        total_ref[rows, :] = normed + small_ref[5:6, :]
    stores = [
        pltpu.make_async_copy(resid_ref, resid_out, store_sems.at[0]),
        pltpu.make_async_copy(normed_ref, normed_out, store_sems.at[8]),
    ]
    for store in stores:
        store.start()
    for fetch in fetches:
        fetch.wait()
    for chunk in range(4):
        for row in range(0, TALL, HALF):
            rows = slice(row, row + HALF)
            pre = dot_nn(normed_ref[rows, :], inner_ref[chunk]) + hidden_bias_ref[
                :, chunk * D : chunk * D + D
            ]
            pre_ref[chunk, rows, :] = pre.astype(jnp.bfloat16)
            tanh = jnp.tanh(GELU_SCALE * (pre + GELU_CUBE * (pre * pre * pre)))
            active = (pre * (0.5 + 0.5 * tanh)).astype(jnp.bfloat16)
            total_ref[rows, :] += dot_nn(active, outer_ref[chunk])
        store = pltpu.make_async_copy(
            pre_ref.at[chunk], pre_out.at[chunk], store_sems.at[1 + chunk]
        )
        store.start()
        stores.append(store)
    store = pltpu.make_async_copy(total_ref, summed_out, store_sems.at[5])
    store.start()
    stores.append(store)
    for row in range(0, TALL, HALF):
        rows = slice(row, row + HALF)
        unit, scale = norm_parts(total_ref[rows, :])
        following = unit * small_ref[6:7, :] + small_ref[7:8, :]
        next_ref[rows, :] = following
        low_ref[rows, :] = following.astype(jnp.bfloat16)
    for index, (source, target) in enumerate(((next_ref, next_out), (low_ref, low_out))):
        store = pltpu.make_async_copy(source, target, store_sems.at[6 + index])
        store.start()
        stores.append(store)
    for store in stores:
        store.wait()


def feed(place, small, hidden_bias, mixed, hidden, attn, group):
    plan, pieces = group
    return pl.pallas_call(
        partial(feed_kernel, plan),
        out_shape=[
            jax.ShapeDtypeStruct((TALL, D), jnp.float32),
            jax.ShapeDtypeStruct((TALL, D), jnp.float32),
            jax.ShapeDtypeStruct((4, TALL, D), jnp.bfloat16),
            jax.ShapeDtypeStruct((TALL, D), jnp.bfloat16),
            jax.ShapeDtypeStruct((TALL, D), jnp.float32),
            jax.ShapeDtypeStruct((TALL, D), jnp.bfloat16),
        ],
        in_specs=[SMEM_SPEC, VMEM_SPEC, VMEM_SPEC] + [ANY_SPEC] * (3 + len(pieces)),
        out_specs=[ANY_SPEC] * 6,
        scratch_shapes=[
            pltpu.VMEM((TALL, D), jnp.bfloat16),
            pltpu.VMEM((TALL, D), jnp.float32),
            pltpu.VMEM((D, D), jnp.bfloat16),
            pltpu.VMEM((4, D, D), jnp.bfloat16),
            pltpu.VMEM((4, D, D), jnp.bfloat16),
            pltpu.VMEM((TALL, D), jnp.float32),
            pltpu.VMEM((TALL, D), jnp.float32),
            pltpu.VMEM((TALL, D), jnp.bfloat16),
            pltpu.VMEM((4, TALL, D), jnp.bfloat16),
            pltpu.VMEM((TALL, D), jnp.float32),
            pltpu.VMEM((TALL, D), jnp.bfloat16),
            pltpu.SemaphoreType.DMA((64,)),
            pltpu.SemaphoreType.DMA((3,)),
            pltpu.SemaphoreType.DMA((9,)),
        ],
        compiler_params=PARAMS,
        cost_estimate=pl.CostEstimate(flops=2 * TALL * D * (D + 2 * FF), bytes_accessed=40000000, transcendentals=3000000),
        name="feed",
    )(place, small, hidden_bias, mixed, hidden, attn, *pieces)


def feed_back_kernel(
    plan, place_ref, small_ref, grad_c_any, grad_q_any, summed_any, normed_any, resid_any, pre_any,
    mix_any, attn_any, *refs
):
    pieces = refs[:-26]
    (
        dresid_out, dmix_out, dwo_out, keep_out, send_out, vec_ref, dhidden_ref,
        grad_ref, summed_ref, resid_ref, pre_ref, mix_ref, wo_ref, inner_ref, outer_ref,
        branch_ref, normed_ref, active_ref, dpre_ref, dinner_ref, douter_ref,
        dwo_ref, sems, load_sems, store_sems, block_sems,
    ) = refs[-26:]
    x, c, z, y = (place_ref[index] for index in range(4))
    total_ref = summed_ref
    load = [
        pltpu.make_async_copy(source, target, load_sems.at[index])
        for index, (source, target) in enumerate(
            (
                (summed_any, summed_ref),
                (grad_c_any, grad_ref.at[:LEN, :]),
                (grad_q_any, grad_ref.at[LEN:, :]),
                (pre_any, pre_ref),
                (normed_any, normed_ref),
                (resid_any, resid_ref),
                (mix_any, mix_ref),
                (attn_any.at[3], wo_ref),
            )
        )
    ]
    for copy in load[:3]:
        copy.start()
    fetches = start_fetch(("inner", "outer"), plan, place_ref, pieces, (inner_ref, outer_ref), sems)
    for copy in load[3:]:
        copy.start()
    for copy in load[:3]:
        copy.wait()
    gain_two_grad = jnp.zeros((1, D), jnp.float32)
    shift_two_grad = jnp.zeros((1, D), jnp.float32)
    bias_two_grad = jnp.zeros((1, D), jnp.float32)
    for row in range(0, TALL, HALF):
        rows = slice(row, row + HALF)
        grad = grad_ref[rows, :]
        unit, scale = norm_parts(summed_ref[rows, :])
        gain_two_grad += jnp.sum(grad * unit, axis=0, keepdims=True)
        shift_two_grad += jnp.sum(grad, axis=0, keepdims=True)
        back = norm_back(unit, scale, grad, small_ref[6:7, :])
        total_ref[rows, :] = back
        low = back.astype(jnp.bfloat16)
        branch_ref[rows, :] = low
        bias_two_grad += jnp.sum(low.astype(jnp.float32), axis=0, keepdims=True)
    vec_ref[5:6, :] = bias_two_grad
    vec_ref[6:7, :] = gain_two_grad
    vec_ref[7:8, :] = shift_two_grad
    for copy in fetches + load[3:]:
        copy.wait()
    blocks = []

    def store(source, target):
        copy = pltpu.make_async_copy(source, target, block_sems.at[len(blocks)])
        copy.start()
        blocks.append(copy)

    for step in range(4):
        apart, side = 1 - step // 2, step % 2
        chunk = side * 2 + (c ^ apart)
        bias_grad = jnp.zeros((1, D), jnp.float32)
        for row in range(0, TALL, HALF):
            rows = slice(row, row + HALF)
            pull = dot_nt(branch_ref[rows, :], outer_ref[chunk])
            pre = pre_ref[chunk, rows, :].astype(jnp.float32)
            square = pre * pre
            tanh = jnp.tanh(GELU_SCALE * pre * (1.0 + GELU_CUBE * square))
            half = 0.5 + 0.5 * tanh
            active_ref[rows, :] = (pre * half).astype(jnp.bfloat16)
            slope = half + (0.5 * GELU_SCALE) * pre * (1.0 - tanh * tanh) * (
                1.0 + (3.0 * GELU_CUBE) * square
            )
            dpre = (pull * slope).astype(jnp.bfloat16)
            dpre_ref[rows, :] = dpre
            bias_grad += jnp.sum(dpre.astype(jnp.float32), axis=0, keepdims=True)
            total_ref[rows, :] += dot_nt(dpre, inner_ref[chunk])
        dhidden_ref[chunk] = bias_grad
        douter_ref[step] = (
            dot_tn(active_ref[...], branch_ref[...]).astype(jnp.bfloat16).reshape(2, 2, 2, ROWS, D)
        )
        for y_block in range(2):
            for x_block in range(2):
                spot = (y_block ^ y, x_block ^ x, chunk, 1)
                store(douter_ref.at[step, y_block, x_block, c], keep_out.at[spot])
                store(douter_ref.at[step, y_block, x_block, 1 - c], send_out.at[spot])
        dinner_ref[step] = (
            dot_tn(normed_ref[...], dpre_ref[...]).astype(jnp.bfloat16).reshape(4, 2, ROWS, D)
        )
        target = send_out if apart else keep_out
        for y_block in range(2):
            store(dinner_ref.at[step, :, y_block], target.at[y_block ^ y, side ^ x, :, 0])
    gain_one_grad = jnp.zeros((1, D), jnp.float32)
    shift_one_grad = jnp.zeros((1, D), jnp.float32)
    bias_o_grad = jnp.zeros((1, D), jnp.float32)
    for row in range(0, TALL, HALF):
        rows = slice(row, row + HALF)
        grad = total_ref[rows, :]
        unit, scale = norm_parts(resid_ref[rows, :])
        gain_one_grad += jnp.sum(grad * unit, axis=0, keepdims=True)
        shift_one_grad += jnp.sum(grad, axis=0, keepdims=True)
        back = norm_back(unit, scale, grad, small_ref[3:4, :])
        grad_ref[rows, :] = back
        low = back.astype(jnp.bfloat16)
        branch_ref[rows, :] = low
        bias_o_grad += jnp.sum(low.astype(jnp.float32), axis=0, keepdims=True)
        active_ref[rows, :] = dot_nt(low, wo_ref[...]).astype(jnp.bfloat16)
    stores = [
        pltpu.make_async_copy(source, target, store_sems.at[index])
        for index, (source, target) in enumerate(
            ((grad_ref, dresid_out), (active_ref, dmix_out), (dwo_ref, dwo_out))
        )
    ]
    stores[0].start()
    stores[1].start()
    dwo_ref[...] = dot_tn(mix_ref[...], branch_ref[...]).astype(jnp.bfloat16)
    stores[2].start()
    vec_ref[0:2, :] = jnp.zeros((2, D), jnp.float32)
    vec_ref[2:3, :] = bias_o_grad
    vec_ref[3:4, :] = gain_one_grad
    vec_ref[4:5, :] = shift_one_grad
    for copy in blocks + stores:
        copy.wait()


def feed_back(place, small, grads, summed, normed, resid, pre, mixed, attn, group):
    plan, pieces = group
    blocks = jax.ShapeDtypeStruct((2, 2, 4, 2, ROWS, D), jnp.bfloat16)
    return pl.pallas_call(
        partial(feed_back_kernel, plan),
        out_shape=[
            jax.ShapeDtypeStruct((TALL, D), jnp.float32),
            jax.ShapeDtypeStruct((TALL, D), jnp.bfloat16),
            jax.ShapeDtypeStruct((D, D), jnp.bfloat16),
            blocks,
            blocks,
            jax.ShapeDtypeStruct((8, D), jnp.float32),
            jax.ShapeDtypeStruct((4, 1, D), jnp.float32),
        ],
        in_specs=[SMEM_SPEC, VMEM_SPEC] + [ANY_SPEC] * (8 + len(pieces)),
        out_specs=[ANY_SPEC] * 5 + [VMEM_SPEC] * 2,
        scratch_shapes=[
            pltpu.VMEM((TALL, D), jnp.float32),
            pltpu.VMEM((TALL, D), jnp.float32),
            pltpu.VMEM((TALL, D), jnp.float32),
            pltpu.VMEM((4, TALL, D), jnp.bfloat16),
            pltpu.VMEM((TALL, D), jnp.bfloat16),
            pltpu.VMEM((D, D), jnp.bfloat16),
            pltpu.VMEM((4, D, D), jnp.bfloat16),
            pltpu.VMEM((4, D, D), jnp.bfloat16),
            pltpu.VMEM((TALL, D), jnp.bfloat16),
            pltpu.VMEM((TALL, D), jnp.bfloat16),
            pltpu.VMEM((TALL, D), jnp.bfloat16),
            pltpu.VMEM((TALL, D), jnp.bfloat16),
            pltpu.VMEM((4, 4, 2, ROWS, D), jnp.bfloat16),
            pltpu.VMEM((4, 2, 2, 2, ROWS, D), jnp.bfloat16),
            pltpu.VMEM((D, D), jnp.bfloat16),
            pltpu.SemaphoreType.DMA((64,)),
            pltpu.SemaphoreType.DMA((8,)),
            pltpu.SemaphoreType.DMA((3,)),
            pltpu.SemaphoreType.DMA((40,)),
        ],
        compiler_params=PARAMS,
        cost_estimate=pl.CostEstimate(flops=4 * TALL * D * (D + 2 * FF), bytes_accessed=60000000, transcendentals=3000000),
        name="feed_back",
    )(place, small, *grads, summed, normed, resid, pre, mixed, attn, *pieces)


def weight_back_kernel(
    place_ref, low_ref, dq_a, dk_a, dv_a, dq_b, dk_b, dv_b, dwo_ref, keep_out, send_out, vec_ref, grads_ref, sems
):
    x, c, z, y = (place_ref[index] for index in range(4))
    grads_ref[3] = dwo_ref[...].reshape(4, 2, ROWS, D)
    for matrix, halves in enumerate(((dq_a, dq_b), (dk_a, dk_b), (dv_a, dv_b))):
        for half, grad in enumerate(halves):
            cols = slice(half * 384, half * 384 + 384)
            grads_ref[matrix, :, :, :, cols] = (
                dot_tn(low_ref[: grad.shape[0], :], grad[...])
                .astype(jnp.bfloat16)
                .reshape(4, 2, ROWS, 384)
            )
            if matrix != 1:
                vec_ref[matrix // 2 : matrix // 2 + 1, cols] = jnp.sum(
                    grad[...].astype(jnp.float32), axis=0, keepdims=True
                )
    blocks = []
    for apart, target in ((1, send_out), (0, keep_out)):
        for side in range(2):
            for y_block in range(2):
                copy = pltpu.make_async_copy(
                    grads_ref.at[side * 2 + (c ^ apart), :, y_block],
                    target.at[y_block ^ y, side ^ x, :, 0],
                    sems.at[len(blocks)],
                )
                copy.start()
                blocks.append(copy)
    for block in blocks:
        block.wait()


def weight_back(place, low, first, second, dwo):
    blocks = jax.ShapeDtypeStruct((2, 2, 4, 1, ROWS, D), jnp.bfloat16)
    return pl.pallas_call(
        weight_back_kernel,
        out_shape=[blocks, blocks, jax.ShapeDtypeStruct((2, D), jnp.float32)],
        in_specs=[SMEM_SPEC] + [VMEM_SPEC] * 8,
        out_specs=[ANY_SPEC] * 2 + [VMEM_SPEC],
        scratch_shapes=[
            pltpu.VMEM((4, 4, 2, ROWS, D), jnp.bfloat16),
            pltpu.SemaphoreType.DMA((8,)),
        ],
        compiler_params=PARAMS,
        cost_estimate=pl.CostEstimate(flops=2 * 2048 * D * D, bytes_accessed=12000000, transcendentals=0),
        name="weight_back",
    )(place, low, *first, *second, dwo)


def input_back_kernel(
    dq_a, dk_a, dv_a, dq_b, dk_b, dv_b, w_ref, dresid_ref, first_ref, second_ref
):
    step = pl.program_id(0)
    total = (
        dresid_ref[...]
        + dot_nt(dq_a[...], w_ref[0, :, :384])
        + dot_nt(dq_b[...], w_ref[0, :, 384:])
    )

    @pl.when(step < 2)
    def _():
        content = total
        for matrix, halves in ((1, (dk_a, dk_b)), (2, (dv_a, dv_b))):
            for half, grad in enumerate(halves):
                content += dot_nt(grad[...], w_ref[matrix, :, half * 384 : half * 384 + 384])
        first_ref[...] = content

    @pl.when(step >= 2)
    def _():
        second_ref[...] = total


def input_back(first, second, attn, dresid):
    half = jax.ShapeDtypeStruct((LEN, D), jnp.float32)
    tall = pl.BlockSpec((HALF, D // 2), lambda i: (i, 0))
    short = pl.BlockSpec((HALF, D // 2), lambda i: (jnp.minimum(i, 1), 0))
    return pl.pallas_call(
        input_back_kernel,
        grid=(4,),
        out_shape=[half, half],
        in_specs=[
            tall, short, short, tall, short, short,
            pl.BlockSpec((3, D, D), lambda i: (0, 0, 0)),
            pl.BlockSpec((HALF, D), lambda i: (i, 0)),
        ],
        out_specs=[
            pl.BlockSpec((HALF, D), lambda i: (jnp.minimum(i, 1), 0)),
            pl.BlockSpec((HALF, D), lambda i: (jnp.maximum(i - 2, 0), 0)),
        ],
        compiler_params=PARAMS,
        cost_estimate=pl.CostEstimate(flops=2 * 2048 * D * D, bytes_accessed=16000000, transcendentals=0),
        name="input_back",
    )(*first, *second, attn, dresid)


def bias_vectors(table):
    lane = jnp.arange(512, dtype=jnp.int32)
    offset = jnp.where(lane < 384, 128 - lane, 640 - lane)
    onehot = bucket_of(offset)[:, None] == jnp.arange(NB, dtype=jnp.int32)[None, :]
    near = jnp.dot(table, onehot.astype(jnp.float32).T, precision=lax.Precision.HIGHEST)
    return (near[:, None, :], jnp.stack([table[:, 15], table[:, 31]], axis=1), onehot)


def bucket_of(offset):
    distance = jnp.abs(offset)
    far_bucket = jnp.full(distance.shape, 8, jnp.int32)
    for exponent in range(1, 8):
        far_bucket = far_bucket + (distance * distance >= 64 * 2**exponent).astype(jnp.int32)
    near_or_far = jnp.where(distance < 8, distance, far_bucket)
    return near_or_far + NB // 2 * (offset > 0).astype(jnp.int32)


def table_grad(sums, onehot):
    near = jnp.dot(
        sums[:, 0, :512],
        jnp.roll(onehot.astype(jnp.float32), 127, axis=0),
        precision=lax.Precision.HIGHEST,
    )
    low = jnp.sum(sums[:, 0, 512:640], axis=1)
    high = jnp.sum(sums[:, 0, 640:], axis=1)
    return near.at[:, 15].add(low).at[:, 31].add(high)


def adam_kernel(rate, master_ref, first_ref, second_ref, grad_ref, *refs):
    master_out, first_out, second_out = refs[-3:]
    grad = grad_ref[...].astype(jnp.float32).reshape(master_ref.shape)
    master = master_ref[...]
    first = BETA_ONE * first_ref[...] + (1.0 - BETA_ONE) * grad
    second = BETA_TWO * second_ref[...] + (1.0 - BETA_TWO) * grad * grad
    first_out[...] = first
    second_out[...] = second
    first_scale = rate / (1.0 - BETA_ONE**STEP)
    second_scale = 1.0 / (1.0 - BETA_TWO**STEP)
    step = (first_scale * first) / (jnp.sqrt(second_scale * second) + ADAM_EPS)
    master_out[...] = master - (step + (rate * WEIGHT_DECAY) * master)


def adam(kind, layer, rate, state, quarters, member, done):
    if kind == "attn":
        block = pl.BlockSpec((1, 1, ROWS, D), lambda i: (layer, i, 0, 0))
    elif kind == "inner":
        block = pl.BlockSpec((1, ROWS, D), lambda i: (layer, 0, i))
    else:
        block = pl.BlockSpec((1, ROWS, D), lambda i: (layer, i, 0))
    held = done or ()
    return pl.pallas_call(
        partial(adam_kernel, rate),
        grid=(4,),
        out_shape=[jax.ShapeDtypeStruct(array.shape, jnp.float32) for array in state],
        in_specs=[block] * 3
        + [pl.BlockSpec((1, 1, ROWS, D), lambda i: (i, member, 0, 0))]
        + [ANY_SPEC] * len(held),
        out_specs=[block] * 3,
        input_output_aliases={4 + index: index for index in range(len(held))},
        compiler_params=PARAMS,
        cost_estimate=pl.CostEstimate(flops=5000000, bytes_accessed=8000000, transcendentals=0),
        name="adam",
    )(*state, quarters, *held)


def fetch_forward(shards):
    low = tuple(shard.astype(jnp.bfloat16) for shard in shards)
    return (
        lax.all_gather(low[0], "fsdp", axis=1, tiled=True),
        lax.all_gather(low[1], "fsdp", axis=0, tiled=True),
        lax.all_gather(low[2], "fsdp", axis=0, tiled=True),
    )


def reduce_layer(grads):
    owned = tuple(
        lax.psum_scatter(
            grad.astype(jnp.bfloat16), "fsdp", scatter_dimension=axis, tiled=True
        ).astype(jnp.float32)
        for grad, axis in zip(grads, (1, 0, 0))
    )
    return lax.psum(owned, "dp")


def forward_layer(hidden_c, hidden_q, weights, lengths, flag_rows, onehot):
    attn_w, inner_w, outer_w, small_w = weights
    pieces, hidden_bias, bias_table = unpack(small_w.astype(jnp.float32))
    bias_q, bias_v, bias_o, gain_one, shift_one, bias_two, gain_two, shift_two = pieces
    table_low = bias_table.astype(jnp.bfloat16)
    low_c = hidden_c.astype(jnp.bfloat16)
    low_q = hidden_q.astype(jnp.bfloat16)
    projected = jnp.einsum("td,sde->ste", low_c, attn_w[:3], preferred_element_type=jnp.float32)
    query_c = (projected[0] + bias_q).astype(jnp.bfloat16)
    key_rows = projected[1].astype(jnp.bfloat16)
    value_rows = (projected[2] + bias_v).astype(jnp.bfloat16)
    query_q = (jnp.dot(low_q, attn_w[0], preferred_element_type=jnp.float32) + bias_q).astype(
        jnp.bfloat16
    )
    mixed_c, mixed_q, lse_c, lse_q = lax.map(
        partial(attend_slot, onehot, table_low),
        (
            to_heads(query_c),
            to_heads(query_q),
            to_heads(key_rows),
            to_heads(value_rows),
            lengths,
            flag_rows,
        ),
    )
    mixed_c = mixed_c.reshape(-1, D)
    mixed_q = mixed_q.reshape(-1, D)
    outputs = []
    kept = []
    for hidden_in, mixed in ((hidden_c, mixed_c), (hidden_q, mixed_q)):
        resid = hidden_in + jnp.dot(mixed, attn_w[3], preferred_element_type=jnp.float32) + bias_o
        normed = layer_norm(resid, gain_one, shift_one)
        pre_act = (
            jnp.dot(normed.astype(jnp.bfloat16), inner_w, preferred_element_type=jnp.float32)
            + hidden_bias
        )
        active = jax.nn.gelu(pre_act, approximate=True).astype(jnp.bfloat16)
        summed = normed + jnp.dot(active, outer_w, preferred_element_type=jnp.float32) + bias_two
        outputs.append(layer_norm(summed, gain_two, shift_two))
        kept.append((resid, summed, pre_act))
    saved = (
        hidden_c,
        hidden_q,
        query_c,
        query_q,
        key_rows,
        value_rows,
        lse_c,
        lse_q,
        mixed_c,
        mixed_q,
        kept[0],
        kept[1],
    )
    return (outputs[0], outputs[1], saved)


def backward_layer(saved, weights, grad_c, grad_q, lengths, flag_rows, onehot):
    attn_w, inner_w, outer_w, small_w = weights
    pieces, hidden_bias, bias_table = unpack(small_w.astype(jnp.float32))
    bias_q, bias_v, bias_o, gain_one, shift_one, bias_two, gain_two, shift_two = pieces
    table_low = bias_table.astype(jnp.bfloat16)
    (
        hidden_c,
        hidden_q,
        query_c,
        query_q,
        key_rows,
        value_rows,
        lse_c,
        lse_q,
        mixed_c,
        mixed_q,
        kept_c,
        kept_q,
    ) = saved
    gelu_tanh = partial(jax.nn.gelu, approximate=True)
    grad_outer = jnp.zeros(outer_w.shape, jnp.float32)
    grad_inner = jnp.zeros(inner_w.shape, jnp.float32)
    grad_attn_out = jnp.zeros((D, D), jnp.float32)
    grad_bias_two = jnp.zeros((D,), jnp.float32)
    grad_hidden_bias = jnp.zeros((FF,), jnp.float32)
    grad_bias_o = jnp.zeros((D,), jnp.float32)
    grad_gain_one = jnp.zeros((D,), jnp.float32)
    grad_shift_one = jnp.zeros((D,), jnp.float32)
    grad_gain_two = jnp.zeros((D,), jnp.float32)
    grad_shift_two = jnp.zeros((D,), jnp.float32)
    residual_grads = []
    mix_grads = []
    for kept_rows, grad_out, mixed in ((kept_c, grad_c, mixed_c), (kept_q, grad_q, mixed_q)):
        resid, summed, pre_act = kept_rows
        normed, norm_one_back = jax.vjp(layer_norm, resid, gain_one, shift_one)
        unused_out, norm_two_back = jax.vjp(layer_norm, summed, gain_two, shift_two)
        grad_summed, grad_g2, grad_s2 = norm_two_back(grad_out)
        grad_gain_two = grad_gain_two + grad_g2
        grad_shift_two = grad_shift_two + grad_s2
        grad_branch = grad_summed.astype(jnp.bfloat16)
        grad_bias_two = grad_bias_two + jnp.sum(grad_branch.astype(jnp.float32), axis=0)
        active, gelu_back = jax.vjp(gelu_tanh, pre_act)
        grad_outer = grad_outer + jnp.einsum(
            "tf,td->fd",
            active.astype(jnp.bfloat16),
            grad_branch,
            preferred_element_type=jnp.float32,
        )
        grad_active = jnp.einsum(
            "td,fd->tf", grad_branch, outer_w, preferred_element_type=jnp.float32
        )
        grad_pre = gelu_back(grad_active)[0].astype(jnp.bfloat16)
        grad_hidden_bias = grad_hidden_bias + jnp.sum(grad_pre.astype(jnp.float32), axis=0)
        grad_inner = grad_inner + jnp.einsum(
            "td,tf->df", normed.astype(jnp.bfloat16), grad_pre, preferred_element_type=jnp.float32
        )
        grad_normed = grad_summed + jnp.einsum(
            "tf,df->td", grad_pre, inner_w, preferred_element_type=jnp.float32
        )
        grad_resid, grad_g1, grad_s1 = norm_one_back(grad_normed)
        grad_gain_one = grad_gain_one + grad_g1
        grad_shift_one = grad_shift_one + grad_s1
        grad_proj = grad_resid.astype(jnp.bfloat16)
        grad_bias_o = grad_bias_o + jnp.sum(grad_proj.astype(jnp.float32), axis=0)
        grad_attn_out = grad_attn_out + jnp.einsum(
            "td,te->de", mixed, grad_proj, preferred_element_type=jnp.float32
        )
        mix_grads.append(
            jnp.einsum(
                "te,de->td", grad_proj, attn_w[3], preferred_element_type=jnp.float32
            ).astype(jnp.bfloat16)
        )
        residual_grads.append(grad_resid)
    grad_query_c, grad_query_q, grad_keys, grad_values, grad_table = lax.map(
        partial(attend_back, onehot, table_low),
        (
            to_heads(query_c),
            to_heads(query_q),
            to_heads(key_rows),
            to_heads(value_rows),
            lengths,
            flag_rows,
            lse_c,
            lse_q,
            to_heads(mix_grads[0]),
            to_heads(mix_grads[1]),
        ),
    )
    grad_table = jnp.sum(grad_table, axis=0)
    low_query_c = grad_query_c.reshape(-1, D).astype(jnp.bfloat16)
    low_query_q = grad_query_q.reshape(-1, D).astype(jnp.bfloat16)
    low_keys = grad_keys.reshape(-1, D).astype(jnp.bfloat16)
    low_values = grad_values.reshape(-1, D).astype(jnp.bfloat16)
    low_c = hidden_c.astype(jnp.bfloat16)
    low_q = hidden_q.astype(jnp.bfloat16)
    stacked_grads = jnp.stack([low_query_c, low_keys, low_values])
    grad_qkv = jnp.einsum("td,ste->sde", low_c, stacked_grads, preferred_element_type=jnp.float32)
    grad_wq = grad_qkv[0] + jnp.einsum(
        "td,te->de", low_q, low_query_q, preferred_element_type=jnp.float32
    )
    grad_attn = jnp.stack([grad_wq, grad_qkv[1], grad_qkv[2], grad_attn_out])
    grad_bias_q = jnp.sum(low_query_c.astype(jnp.float32), axis=0) + jnp.sum(
        low_query_q.astype(jnp.float32), axis=0
    )
    grad_bias_v = jnp.sum(low_values.astype(jnp.float32), axis=0)
    grad_content = residual_grads[0] + jnp.einsum(
        "ste,sde->td", stacked_grads, attn_w[:3], preferred_element_type=jnp.float32
    )
    grad_query_in = residual_grads[1] + jnp.einsum(
        "te,de->td", low_query_q, attn_w[0], preferred_element_type=jnp.float32
    )
    grad_small = jnp.concatenate(
        [
            grad_bias_q,
            grad_bias_v,
            grad_bias_o,
            grad_gain_one,
            grad_shift_one,
            grad_bias_two,
            grad_gain_two,
            grad_shift_two,
            grad_hidden_bias,
            grad_table.reshape(-1),
        ]
    )
    return (grad_content, grad_query_in, (grad_attn, grad_inner, grad_outer, grad_small))


def adam_update(master, first, second, grad, rate):
    first_new = BETA_ONE * first + (1.0 - BETA_ONE) * grad
    second_new = BETA_TWO * second + (1.0 - BETA_TWO) * grad * grad
    first_hat = first_new / (1.0 - BETA_ONE**STEP)
    second_hat = second_new / (1.0 - BETA_TWO**STEP)
    master_new = master - rate * (
        first_hat / (jnp.sqrt(second_hat) + ADAM_EPS) + WEIGHT_DECAY * master
    )
    return (master_new, first_new, second_new)


def per_device(
    content,
    query,
    lengths,
    predicted,
    content_cot,
    query_cot,
    attn_master,
    attn_first,
    attn_second,
    inner_master,
    inner_first,
    inner_second,
    outer_master,
    outer_first,
    outer_second,
    small_master,
    small_first,
    small_second,
):
    masters = (attn_master, inner_master, outer_master, small_master)
    slot_count = lengths.shape[0]
    flag_rows = predicted.reshape(slot_count, LEN)
    onehot = bucket_onehot()
    hidden_c = content.astype(jnp.float32)
    hidden_q = query.astype(jnp.float32)
    kept_weights = []
    saved_layers = []
    small_all = lax.all_gather(
        small_master.astype(jnp.bfloat16), "fsdp", axis=1, tiled=True
    )
    for layer_index in range(LAYERS):
        shards = tuple((master[layer_index] for master in masters[:3]))
        gathered = fetch_forward(shards) + (small_all[layer_index],)
        kept_weights.append(gathered)
        hidden_c, hidden_q, saved = forward_layer(
            hidden_c, hidden_q, gathered, lengths, flag_rows, onehot
        )
        saved_layers.append(saved)
    position = jnp.arange(LEN, dtype=jnp.int32)
    valid_rows = (position[None, :] < lengths[:, None]).reshape(-1, 1).astype(jnp.float32)
    grad_c = content_cot.astype(jnp.float32) * valid_rows
    grad_q = query_cot.astype(jnp.float32) * valid_rows
    layer_grads = [None] * LAYERS
    small_grads = [None] * LAYERS
    for layer_index in reversed(range(LAYERS)):
        grad_c, grad_q, local_grads = backward_layer(
            saved_layers[layer_index],
            kept_weights[layer_index],
            grad_c,
            grad_q,
            lengths,
            flag_rows,
            onehot,
        )
        small_grads[layer_index] = local_grads[3]
        layer_grads[layer_index] = reduce_layer(local_grads[:3])
    small_sum = lax.psum(jnp.stack(small_grads), ("dp", "fsdp"))
    owned = small_master.shape[1]
    small_own = lax.dynamic_slice_in_dim(
        small_sum, lax.axis_index("fsdp") * owned, owned, 1
    )
    reduced = tuple(
        (
            jnp.stack([layer_grads[layer_index][member] for layer_index in range(LAYERS)])
            for member in range(3)
        )
    ) + (small_own,)
    attn_new = adam_update(attn_master, attn_first, attn_second, reduced[0], ATTENTION_RATE)
    inner_new = adam_update(inner_master, inner_first, inner_second, reduced[1], FEED_RATE)
    outer_new = adam_update(outer_master, outer_first, outer_second, reduced[2], FEED_RATE)
    small_new = adam_update(small_master, small_first, small_second, reduced[3], SMALL_RATE)
    return (
        hidden_c.astype(jnp.bfloat16),
        hidden_q.astype(jnp.bfloat16),
        grad_c,
        grad_q,
        attn_new[0],
        attn_new[1],
        attn_new[2],
        inner_new[0],
        inner_new[1],
        inner_new[2],
        outer_new[0],
        outer_new[1],
        outer_new[2],
        small_new[0],
        small_new[1],
        small_new[2],
    )


def quarter_of(kind, shard, quarter):
    if kind == "attn":
        return lax.dynamic_index_in_dim(shard, quarter, 0, keepdims=False)
    if kind == "inner":
        return lax.dynamic_slice_in_dim(shard, quarter * D, D, 1)
    return lax.dynamic_slice_in_dim(shard, quarter * ROWS, ROWS, 0)


def after(value, *others):
    return lax.optimization_barrier((value, others))[0]


def join(*values):
    return lax.optimization_barrier(values)


def own_blocks(kinds, shards, place, side):
    quarter = (place[0] ^ side) * 2 + place[1]
    return jnp.stack(
        [
            quarter_of(kind, shard, quarter).astype(jnp.bfloat16)
            for kind, shard in zip(kinds, shards)
        ]
    )


def gather_group(count, shards, plane, column, sides, corners, mine, theirs):
    plan = []
    for core, arrays in enumerate((mine, theirs)):
        base = core * len(mine)
        for member in range(count):
            array, first = plane
            plan += [
                (base + array, first + side * count + member, side, 1, core, 0, member)
                for side in range(2)
            ]
            for apart in (1, 2, 3):
                index = (apart - 1) * count + member
                array, first = column
                plan.append((base + array, first + index, 0, 0, core, apart, member))
                for dx, dy, (array, first) in ((1, 0, sides[0]), (0, 1, sides[1])):
                    plan.append((base + array, first + index, dx, dy, core, apart, member))
                skipped = 0
                for array, first, held in corners:
                    if skipped <= index < skipped + held:
                        plan.append(
                            (base + array, first + index - skipped, 1, 1, core, apart, member)
                        )
                    skipped += held
    return (tuple(plan), tuple(shards) + tuple(mine) + tuple(theirs))


def gather_small(shard, place):
    z, y = place[2], place[3]
    pair = jnp.stack([shard, swap_z(shard, 1)])
    blocks = jnp.concatenate([pair, swap_z(pair, 2)])
    low, high = z % 2, z // 2
    blocks = jnp.where(low == 0, blocks, blocks[jnp.array([1, 0, 3, 2])])
    blocks = jnp.where(high == 0, blocks, blocks[jnp.array([2, 3, 0, 1])])
    other = swap_y(blocks)
    pairs = jnp.where(y == 0, jnp.stack([blocks, other], 1), jnp.stack([other, blocks], 1))
    return pairs.transpose(2, 0, 1, 3).reshape(shard.shape[0], -1)


def add_low(*values):
    total = values[0].astype(jnp.float32)
    for value in values[1:]:
        total = total + value.astype(jnp.float32)
    return total.astype(jnp.bfloat16)


def reduce_corners(keep, get):
    corner = add_low(keep[1, 1], get[1, 1])
    return (swap_x(corner[:2]), swap_y(corner[2:]))


def reduce_sides(keep, get, corners):
    by_x, by_y = corners
    for_y = jnp.concatenate([add_low(keep[1, 0, :2], get[1, 0, :2], by_x), add_low(keep[1, 0, 2:], get[1, 0, 2:])])
    for_x = jnp.concatenate([add_low(keep[0, 1, :2], get[0, 1, :2]), add_low(keep[0, 1, 2:], get[0, 1, 2:], by_y)])
    return (swap_x(for_x), swap_y(for_y))


def reduce_column(keep, get, sides):
    return add_low(keep[0, 0], get[0, 0], *sides)


def at_z(column, place, apart):
    return lax.dynamic_index_in_dim(column, place[2] ^ apart, 0, keepdims=False)


def reduce_far(column, place):
    return swap_z(jnp.stack([at_z(column, place, 2), at_z(column, place, 3)]), 2)


def reduce_near(column, far, place):
    return swap_z(add_low(at_z(column, place, 1), far[1]), 1)


def reduce_total(column, far, near, place):
    return add_low(at_z(column, place, 0), far[0], near)


def reduce_direct(column, place):
    return tuple(swap_z(at_z(column, place, apart), apart) for apart in (1, 2, 3))


def direct_total(column, shifts, place):
    return add_low(at_z(column, place, 0), *shifts)


def share_core(pair, place):
    x, c = place[0], place[1]
    other = swap_core(pair)
    cores = jnp.where(c == 0, jnp.stack([pair, other], 1), jnp.stack([other, pair], 1))
    sides = jnp.where(x == 0, cores, cores[::-1])
    return sides.reshape((4,) + pair.shape[1:])


def small_parts(vectors):
    values = vectors.astype(jnp.float32)
    return (
        values[: 8 * D].reshape(8, D),
        values[8 * D : 8 * D + FF].reshape(1, FF),
        bias_vectors(values[8 * D + FF :].reshape(H, NB)),
    )


def per_device_fast(
    content,
    query,
    lengths,
    predicted,
    content_cot,
    query_cot,
    attn_master,
    attn_first,
    attn_second,
    inner_master,
    inner_first,
    inner_second,
    outer_master,
    outer_first,
    outer_second,
    small_master,
    small_first,
    small_second,
):
    place_parts = my_place()
    place = jnp.stack(place_parts).astype(jnp.int32)
    attn_kinds, feed_kinds = ("attn",), ("inner", "outer")
    attn_shards = [(attn_master[layer],) for layer in range(LAYERS)]
    feed_shards = [(inner_master[layer], outer_master[layer]) for layer in range(LAYERS)]
    own_a0 = own_blocks(attn_kinds, attn_shards[0], place_parts, 0)
    oth_a0 = own_blocks(attn_kinds, attn_shards[0], place_parts, 1)
    own_f0 = own_blocks(feed_kinds, feed_shards[0], place_parts, 0)
    z_a0 = tuple(swap_z(own_a0, apart) for apart in (1, 2, 3))
    plane_a0 = swap_y(jnp.concatenate([own_a0, oth_a0]))
    near_f0 = swap_z(own_f0, 1)
    z_a0, plane_a0, near_f0 = join(z_a0, plane_a0, near_f0)
    oth_f0 = own_blocks(feed_kinds, feed_shards[0], place_parts, 1)
    own_a1 = own_blocks(attn_kinds, attn_shards[1], place_parts, 0)
    oth_a1 = own_blocks(attn_kinds, attn_shards[1], place_parts, 1)
    own_f1 = own_blocks(feed_kinds, feed_shards[1], place_parts, 0)
    oth_f1 = own_blocks(feed_kinds, feed_shards[1], place_parts, 1)
    attn_low = [tuple(w.astype(jnp.bfloat16) for w in shards) for shards in attn_shards]
    feed_low = [tuple(w.astype(jnp.bfloat16) for w in shards) for shards in feed_shards]
    col_a0 = jnp.concatenate(z_a0)
    x0 = swap_x(col_a0)
    y0 = swap_y(col_a0)
    far_f0 = swap_z(jnp.concatenate([own_f0, near_f0]), 2)
    plane_f0 = swap_y(after(jnp.concatenate([own_f0, oth_f0]), z_a0))
    near_1 = swap_z(after(jnp.concatenate([own_a1, own_f1]), z_a0), 1)
    x0, y0, far_f0, plane_f0, near_1 = join(x0, y0, far_f0, plane_f0, near_1)
    col_f0 = jnp.concatenate([near_f0, far_f0])
    x1 = swap_x(jnp.concatenate([col_f0, y0[:2]]))
    y1 = swap_y(jnp.concatenate([col_f0, x0[2:]]))
    far_a1 = swap_z(jnp.concatenate([own_a1, near_1[:1]]), 2)
    mine_0 = jnp.concatenate([plane_a0, col_a0, x0, y0])
    theirs_0 = swap_core(mine_0)
    small_all = gather_small(after(small_master.astype(jnp.bfloat16), far_f0), place_parts)
    x1, y1, far_a1, theirs_0, small_all = join(x1, y1, far_a1, theirs_0, small_all)
    col_a1 = jnp.concatenate([near_1[:1], far_a1])
    x2 = swap_x(jnp.concatenate([col_a1, y1[:4]]))
    y2 = swap_y(jnp.concatenate([col_a1, x1[4:6], own_a1, oth_a1]))
    far_f1 = swap_z(jnp.concatenate([own_f1, after(near_1[1:], far_a1)]), 2)
    mine_1 = jnp.concatenate([x1, y1])
    theirs_1 = swap_core(mine_1)
    mine_p0 = jnp.concatenate([plane_f0, col_f0])
    theirs_p0 = swap_core(after(mine_p0, theirs_1))
    group_a0 = gather_group(
        1, attn_low[0], (0, 0), (0, 2), ((0, 5), (0, 8)), ((1, 6, 2), (1, 14, 1)),
        (mine_0, mine_1), (theirs_0, theirs_1),
    )
    row_flags = predicted.reshape(1, LEN).astype(jnp.float32)
    col_flags = predicted.reshape(LEN, 1).astype(jnp.float32)
    low0 = jnp.concatenate([content, query])
    hidden0 = low0.astype(jnp.float32)
    small0, hidden_bias0, (tvec0, far0, onehot) = small_parts(small_all[0])
    small1, hidden_bias1, (tvec1, far1, onehot) = small_parts(small_all[1])
    valid = (jnp.arange(LEN, dtype=jnp.int32) < lengths[0])[:, None].astype(jnp.float32)
    grads = (content_cot.astype(jnp.float32) * valid, query_cot.astype(jnp.float32) * valid)
    q0, k0, v0, attn0 = project(place, low0, small0, group_a0)
    mixed0, p0, inverse0, dead = mix(lengths, far0, tvec0, q0, k0, v0, row_flags, col_flags)
    x2, y2, far_f1, mixed0, theirs_p0 = join(x2, y2, far_f1, mixed0, theirs_p0)
    col_f1 = jnp.concatenate([near_1[1:], far_f1])
    x3 = swap_x(jnp.concatenate([col_f1, y2[:3]]))
    y3 = swap_y(jnp.concatenate([col_f1, own_f1, oth_f1]))
    mine_2 = jnp.concatenate([x2, y2, col_a1])
    theirs_2 = swap_core(mine_2)
    group_f0 = gather_group(
        2, feed_low[0], (0, 0), (0, 4), ((1, 0), (1, 8)), ((2, 3, 4), (2, 10, 2)),
        (mine_p0, mine_1, mine_2), (theirs_p0, theirs_1, theirs_2),
    )
    resid0, summed0, pre0, normed0, hidden1, low1 = feed(
        place, small0, hidden_bias0, mixed0, hidden0, attn0, group_f0
    )
    x3, y3, low1, hidden1 = join(x3, y3, low1, hidden1)
    x4 = swap_x(y3[:3])
    y4 = swap_y(x3[3:6])
    mine_3 = jnp.concatenate([x3, y3])
    theirs_3 = swap_core(mine_3)
    group_a1 = gather_group(
        1, attn_low[1], (0, 12), (0, 14), ((0, 0), (0, 7)), ((1, 6, 3),),
        (mine_2, mine_3), (theirs_2, theirs_3),
    )
    q1, k1, v1, attn1 = project(place, low1, small1, group_a1)
    x4, y4, q1 = join(x4, y4, q1)
    mine_4 = jnp.concatenate([col_f1, x4, y4])
    theirs_4 = swap_core(mine_4)
    group_f1 = gather_group(
        2, feed_low[1], (0, 15), (1, 0), ((0, 0), (0, 9)), ((1, 6, 3), (1, 9, 3)),
        (mine_3, mine_4), (theirs_3, theirs_4),
    )
    mixed1, p1, inverse1, dead = mix(
        lengths, far1, tvec1, q1, k1, v1, row_flags, col_flags
    )
    resid1, summed1, pre1, normed1, unused, low_out = feed(
        place, small1, hidden_bias1, mixed1, hidden1, attn1, group_f1
    )
    dresid1, dmix1, dwo1, keep_f1, send_f1, vec_f1, dhidden1 = feed_back(
        place, small1, grads, summed1, normed1, resid1, pre1, mixed1, attn1, group_f1
    )
    get_f1 = swap_core(send_f1)
    first1 = mix_back(0, q1, k1, v1, dmix1, mixed1, p1, inverse1, dead)
    by_f1 = reduce_corners(keep_f1, after(get_f1, first1[0]))
    second1 = mix_back(
        3, after(q1, get_f1, first1[0]), k1, v1, dmix1, mixed1, p1, inverse1, dead
    )
    sides_rf1 = reduce_sides(keep_f1, get_f1, after(by_f1, second1[0]))
    keep_a1, send_a1, vec_a1 = weight_back(
        place, low1, after(first1[:3], by_f1), second1[:3], dwo1
    )
    get_a1 = swap_core(send_a1)
    grads = input_back(after(first1[:3], keep_a1), second1[:3], attn1, dresid1)
    by_a1 = reduce_corners(keep_a1, after(get_a1, grads[0]))
    dresid0, dmix0, dwo0, keep_f0, send_f0, vec_f0, dhidden0 = feed_back(
        place, small0, after(grads, get_a1), summed0, normed0, resid0, pre0, mixed0, attn0, group_f0
    )
    get_f0 = swap_core(after(send_f0, sides_rf1, by_a1))
    sides_ra1 = reduce_sides(keep_a1, get_a1, after(by_a1, dmix0))
    first0 = mix_back(
        0, q0, k0, v0, after(dmix0, by_a1, sides_rf1), mixed0, p0, inverse0, dead
    )
    by_f0 = reduce_corners(keep_f0, after(get_f0, first0[0]))
    column_f1 = reduce_column(keep_f1, get_f1, after(sides_rf1, first0[0]))
    zfar_f1 = reduce_far(column_f1, place_parts)
    second0 = mix_back(
        3, after(q0, get_f0, first0[0]), k0, v0, dmix0, mixed0, p0, inverse0, dead
    )
    by_f0, sides_ra1, zfar_f1, second0_q = join(by_f0, sides_ra1, zfar_f1, second0[0])
    sides_rf0 = reduce_sides(keep_f0, get_f0, by_f0)
    keep_a0, send_a0, vec_a0 = weight_back(
        place, low0, first0[:3], [second0_q, second0[1], second0[2]], dwo0
    )
    get_a0 = swap_core(send_a0)
    znear_f1 = reduce_near(column_f1, zfar_f1, place_parts)
    column_a1 = reduce_column(keep_a1, get_a1, sides_ra1)
    zfar_a1 = reduce_far(column_a1, place_parts)
    small_sum = jnp.stack(
        [
            jnp.concatenate(
                [
                    attn_vec.reshape(-1),
                    feed_vec[2:].reshape(-1),
                    dhidden.reshape(-1),
                    table_grad(jnp.concatenate([first[3], second[3]]), onehot).reshape(-1),
                ]
            )
            for attn_vec, feed_vec, dhidden, first, second in (
                (vec_a0, vec_f0, dhidden0, first0, second0),
                (vec_a1, vec_f1, dhidden1, first1, second1),
            )
        ]
    )
    small_sum = small_sum + swap_core(small_sum)
    sides_rf0, get_a0, znear_f1, zfar_a1, small_sum = join(
        sides_rf0, get_a0, znear_f1, zfar_a1, small_sum
    )
    column_f0 = reduce_column(keep_f0, get_f0, sides_rf0)
    zfar_f0 = reduce_far(column_f0, place_parts)
    by_a0 = reduce_corners(keep_a0, get_a0)
    own_f1 = reduce_total(column_f1, zfar_f1, znear_f1, place_parts)
    pair_f1 = jnp.stack([own_f1, swap_x(own_f1)])
    content_grad, query_grad = input_back(
        after(first0[:3], sides_rf0), [second0_q, second0[1], second0[2]], attn0, dresid0
    )
    by_a0, pair_f1, content_grad = join(by_a0, pair_f1, content_grad)
    sides_ra0 = reduce_sides(keep_a0, get_a0, by_a0)
    znear_a1 = reduce_near(column_a1, zfar_a1, place_parts)
    four_f1 = share_core(pair_f1, place_parts)
    attn_state = (attn_master, attn_first, attn_second)
    inner_state = (inner_master, inner_first, inner_second)
    outer_state = (outer_master, outer_first, outer_second)
    inner_new = adam("inner", 1, FEED_RATE, inner_state, four_f1, 0, None)
    outer_new = adam("outer", 1, FEED_RATE, outer_state, four_f1, 1, None)
    sides_ra0, zfar_f0, znear_a1, inner_new, outer_new = join(
        sides_ra0, zfar_f0, znear_a1, inner_new, outer_new
    )
    column_a0 = reduce_column(keep_a0, get_a0, sides_ra0)
    shifts_a0 = reduce_direct(column_a0, place_parts)
    znear_f0 = reduce_near(column_f0, zfar_f0, place_parts)
    own_a1 = reduce_total(column_a1, zfar_a1, znear_a1, place_parts)
    pair_a1 = jnp.stack([own_a1, swap_x(after(own_a1, column_a0))])
    shifts_a0, znear_f0, pair_a1 = join(shifts_a0, znear_f0, pair_a1)
    own_0 = jnp.concatenate(
        [
            reduce_total(column_f0, zfar_f0, znear_f0, place_parts),
            direct_total(column_a0, shifts_a0, place_parts),
        ]
    )
    pair_0 = jnp.stack([own_0, swap_x(own_0)])
    four_a1 = share_core(pair_a1, place_parts)
    small_sum = small_sum + swap_y(small_sum)
    attn_new = adam("attn", 1, ATTENTION_RATE, attn_state, four_a1, 0, None)
    pair_0, attn_new, small_sum = join(pair_0, attn_new, small_sum)
    four_0 = share_core(pair_0, place_parts)
    small_sum = small_sum + swap_x(small_sum)
    four_0, small_sum = join(four_0, small_sum)
    small_far = swap_z(small_sum, 1)
    inner_new = adam("inner", 0, FEED_RATE, inner_state, four_0, 0, tuple(inner_new))
    small_sum = small_sum + small_far
    outer_new = adam("outer", 0, FEED_RATE, outer_state, four_0, 1, tuple(outer_new))
    small_sum = small_sum + swap_z(small_sum, 2)
    attn_new = adam("attn", 0, ATTENTION_RATE, attn_state, four_0, 2, tuple(attn_new))
    size = small_master.shape[1]
    small_own = lax.dynamic_slice_in_dim(small_sum, lax.axis_index("fsdp") * size, size, 1)
    small_new = adam_update(small_master, small_first, small_second, small_own, SMALL_RATE)
    return (
        (low_out[:LEN], low_out[LEN:], content_grad, query_grad)
        + tuple(attn_new)
        + tuple(inner_new)
        + tuple(outer_new)
        + small_new
    )


def solution(mesh):
    placed = (
        P(("dp", "fsdp"), None),
        P(("dp", "fsdp"), None),
        P(("dp", "fsdp")),
        P(("dp", "fsdp")),
        P(("dp", "fsdp"), None),
        P(("dp", "fsdp"), None),
        P(None, None, "fsdp", None),
        P(None, None, "fsdp", None),
        P(None, None, "fsdp", None),
        P(None, "fsdp", None),
        P(None, "fsdp", None),
        P(None, "fsdp", None),
        P(None, "fsdp", None),
        P(None, "fsdp", None),
        P(None, "fsdp", None),
        P(None, "fsdp"),
        P(None, "fsdp"),
        P(None, "fsdp"),
    )
    fast = tuple(mesh.shape.values()) == (4, 8)
    return jax.shard_map(
        per_device_fast if fast else per_device,
        mesh=mesh,
        in_specs=placed,
        out_specs=(
            P(("dp", "fsdp"), None),
            P(("dp", "fsdp"), None),
            P(("dp", "fsdp"), None),
            P(("dp", "fsdp"), None),
            P(None, None, "fsdp", None),
            P(None, None, "fsdp", None),
            P(None, None, "fsdp", None),
            P(None, "fsdp", None),
            P(None, "fsdp", None),
            P(None, "fsdp", None),
            P(None, "fsdp", None),
            P(None, "fsdp", None),
            P(None, "fsdp", None),
            P(None, "fsdp"),
            P(None, "fsdp"),
            P(None, "fsdp"),
        ),
        check_vma=False,
    )
```

```python
from functools import partial

import jax
import jax.numpy as jnp
from jax import lax
from jax.experimental import pallas as pl
from jax.experimental.pallas import tpu as pltpu
from jax.sharding import PartitionSpec as P

D = 768
H = 12
DH = 64
FF = 3072
LEN = 512
NB = 32
LAYERS = 2
STEP = 10


NORM_EPS = 1e-05
MASKED = -1000000000.0
BETA_ONE = 0.9
BETA_TWO = 0.999
ATTENTION_RATE = 0.1
FEED_RATE = 0.02
SMALL_RATE = 0.4
WEIGHT_DECAY = 0.01
ADAM_EPS = 1e-08
SCORE_SCALE = 0.125


def layer_norm(values, gain, shift):
    centre = values - jnp.mean(values, axis=-1, keepdims=True)
    spread = jnp.mean(centre * centre, axis=-1, keepdims=True)
    return centre * lax.rsqrt(spread + NORM_EPS) * gain + shift


def unpack(vectors):
    pieces = [vectors[piece_index * D : (piece_index + 1) * D] for piece_index in range(8)]
    hidden_bias = vectors[8 * D : 8 * D + FF]
    bias_table = vectors[8 * D + FF :].reshape(H, NB)
    return (pieces, hidden_bias, bias_table)


def bucket_ids():
    position = jnp.arange(LEN, dtype=jnp.int32)
    offset = position[None, :] - position[:, None]
    distance = jnp.abs(offset)
    far_bucket = jnp.full(distance.shape, 8, jnp.int32)
    for exponent in range(1, 8):
        far_bucket = far_bucket + (distance * distance >= 64 * 2**exponent).astype(jnp.int32)
    near_or_far = jnp.where(distance < 8, distance, far_bucket)
    return near_or_far + NB // 2 * (offset > 0).astype(jnp.int32)


def bucket_onehot():
    return (bucket_ids()[:, :, None] == jnp.arange(NB, dtype=jnp.int32)[None, None, :]).astype(
        jnp.bfloat16
    )


def allowed_pairs(length, pred_flags):
    position = jnp.arange(LEN, dtype=jnp.int32)
    valid_key = (position < length)[None, :]
    row_pos = position[:, None]
    col_pos = position[None, :]
    free_key = (pred_flags == 0)[None, :]
    content_ok = valid_key & (free_key | (pred_flags[:, None] == 1) & (col_pos <= row_pos))
    query_ok = valid_key & (col_pos != row_pos) & (free_key | (col_pos < row_pos))
    return (content_ok, query_ok)


def masked_scores(query_rows, key_rows, position_bias, allowed):
    scores = (
        jnp.einsum("qhd,khd->hqk", query_rows, key_rows, preferred_element_type=jnp.float32)
        * SCORE_SCALE
        + position_bias
    )
    return jnp.where(allowed[None], scores, MASKED)


def table_bias(onehot, table_low):
    return jnp.einsum("qkb,hb->hqk", onehot, table_low, preferred_element_type=jnp.float32)


def attend_slot(onehot, table_low, slot_item):
    query_c, query_q, key_rows, value_rows, length, pred_flags = slot_item
    position_bias = table_bias(onehot, table_low)
    content_ok, query_ok = allowed_pairs(length, pred_flags)
    results = []
    for query_rows, allowed in ((query_c, content_ok), (query_q, query_ok)):
        scores = masked_scores(query_rows, key_rows, position_bias, allowed)
        peak = jnp.max(scores, axis=-1, keepdims=True)
        expos = jnp.exp(scores - peak)
        totals = jnp.sum(expos, axis=-1, keepdims=True)
        probs = (expos / totals).astype(jnp.bfloat16)
        mixed = jnp.einsum(
            "hqk,khd->qhd", probs, value_rows, preferred_element_type=jnp.float32
        ).astype(jnp.bfloat16)
        results.append((mixed, peak[..., 0] + jnp.log(totals[..., 0])))
    return (results[0][0], results[1][0], results[0][1], results[1][1])


def attend_back(onehot, table_low, slot_item):
    (
        query_c,
        query_q,
        key_rows,
        value_rows,
        length,
        pred_flags,
        lse_c,
        lse_q,
        grad_mix_c,
        grad_mix_q,
    ) = slot_item
    position_bias = table_bias(onehot, table_low)
    content_ok, query_ok = allowed_pairs(length, pred_flags)
    grad_keys = jnp.zeros(key_rows.shape, jnp.float32)
    grad_values = jnp.zeros(value_rows.shape, jnp.float32)
    grad_table = jnp.zeros((H, NB), jnp.float32)
    grads_query = []
    for query_rows, allowed, log_total, grad_mix in (
        (query_c, content_ok, lse_c, grad_mix_c),
        (query_q, query_ok, lse_q, grad_mix_q),
    ):
        scores = masked_scores(query_rows, key_rows, position_bias, allowed)
        probs = jnp.exp(scores - log_total[..., None])
        grad_values = grad_values + jnp.einsum(
            "hqk,qhd->khd", probs.astype(jnp.bfloat16), grad_mix, preferred_element_type=jnp.float32
        )
        grad_probs = jnp.einsum(
            "qhd,khd->hqk", grad_mix, value_rows, preferred_element_type=jnp.float32
        )
        grad_scores = probs * (grad_probs - jnp.sum(probs * grad_probs, axis=-1, keepdims=True))
        grad_scores = jnp.where(allowed[None], grad_scores, 0.0).astype(jnp.bfloat16)
        grad_table = grad_table + jnp.einsum(
            "hqk,qkb->hb", grad_scores, onehot, preferred_element_type=jnp.float32
        )
        grads_query.append(
            jnp.einsum("hqk,khd->qhd", grad_scores, key_rows, preferred_element_type=jnp.float32)
            * SCORE_SCALE
        )
        grad_keys = (
            grad_keys
            + jnp.einsum(
                "hqk,qhd->khd", grad_scores, query_rows, preferred_element_type=jnp.float32
            )
            * SCORE_SCALE
        )
    return (grads_query[0], grads_query[1], grad_keys, grad_values, grad_table)


def to_heads(values):
    return values.reshape(-1, LEN, H, DH)


AXES = ("dp", "fsdp")
GRID = (2, 2, 4, 2)
ROWS = 96


def places():
    return [
        (x, c, z, y) for x in range(2) for c in range(2) for z in range(4) for y in range(2)
    ]


def flat(x, c, z, y):
    return ((x * 2 + c) * 4 + z) * 2 + y


def move(value, shift):
    pairs = [(flat(*place), flat(*shift(*place))) for place in places()]
    return lax.ppermute(value, AXES, pairs)


def swap_core(value):
    return move(value, lambda x, c, z, y: (x, 1 - c, z, y))


def swap_x(value):
    return move(value, lambda x, c, z, y: (1 - x, c, z, y))


def swap_y(value):
    return move(value, lambda x, c, z, y: (x, c, z, 1 - y))


def swap_z(value, apart):
    return move(value, lambda x, c, z, y: (x, c, z ^ apart, y))


def my_place():
    dp = lax.axis_index("dp")
    fsdp = lax.axis_index("fsdp")
    return (dp // 2, dp % 2, fsdp // 2, fsdp % 2)


def dot_nn(left, right):
    return jnp.dot(left, right, preferred_element_type=jnp.float32)


def dot_nt(left, right):
    return lax.dot_general(
        left, right, (((1,), (1,)), ((), ())), preferred_element_type=jnp.float32
    )


def dot_tn(left, right):
    return lax.dot_general(
        left, right, (((0,), (0,)), ((), ())), preferred_element_type=jnp.float32
    )


ANY_SPEC = pl.BlockSpec(memory_space=pl.ANY)
VMEM_SPEC = pl.BlockSpec(memory_space=pltpu.VMEM)
SMEM_SPEC = pl.BlockSpec(memory_space=pltpu.SMEM)
TALL = 2 * LEN
HALF = 256
PARAMS = pltpu.CompilerParams(vmem_limit_bytes=60 * 1024 * 1024)


def norm_parts(values):
    centre = values - jnp.mean(values, axis=-1, keepdims=True)
    spread = jnp.mean(centre * centre, axis=-1, keepdims=True)
    scale = lax.rsqrt(spread + NORM_EPS)
    return (centre * scale, scale)


def norm_back(unit, scale, grad, gain):
    scaled = grad * gain
    return scale * (
        scaled
        - jnp.mean(scaled, axis=-1, keepdims=True)
        - unit * jnp.mean(scaled * unit, axis=-1, keepdims=True)
    )


def start_fetch(kinds, plan, place_ref, refs, targets, sems):
    x, c, z, y = (place_ref[index] for index in range(4))
    mine = z * 2 + y
    copies = []

    def start(source, target):
        copy = pltpu.make_async_copy(source, target, sems.at[len(copies)])
        copy.start()
        copies.append(copy)

    for member, kind in enumerate(kinds):
        target = targets[member]
        if kind == "attn":
            start(refs[member], target.at[:, pl.ds(pl.multiple_of(mine * ROWS, ROWS), ROWS), :])
        elif kind == "inner":
            for quarter in range(4):
                start(
                    refs[member].at[:, quarter * D : quarter * D + D],
                    target.at[quarter, pl.ds(pl.multiple_of(mine * ROWS, ROWS), ROWS), :],
                )
        else:
            start(refs[member], target.at[z, pl.ds(pl.multiple_of(y * 384, ROWS), 384), :])
    for array, index, dx, dy, dc, dz, member in plan:
        quarter = (x ^ dx) * 2 + (c ^ dc)
        if kinds[member] == "outer":
            lead, row = z ^ dz, (y ^ dy) * 384 + quarter * ROWS
        else:
            lead, row = quarter, ((z ^ dz) * 2 + (y ^ dy)) * ROWS
        start(
            refs[len(kinds) + array].at[index],
            targets[member].at[lead, pl.ds(pl.multiple_of(row, ROWS), ROWS), :],
        )
    return copies


def project_kernel(plan, place_ref, small_ref, low_any, *refs):
    pieces = refs[:-14]
    (
        q_out, k_out, v_out, w_out, low_ref, q_ref, k_ref, v_ref, w_ref,
        sems, load_sem, keep_sem, store_sems, unused,
    ) = refs[-14:]
    load = pltpu.make_async_copy(low_any, low_ref, load_sem)
    load.start()
    fetches = start_fetch(("attn",), plan, place_ref, pieces, (w_ref,), sems)
    load.wait()
    for copy in fetches:
        copy.wait()
    keep = pltpu.make_async_copy(w_ref, w_out, keep_sem)
    keep.start()
    bias_q = small_ref[0:1, :]
    bias_v = small_ref[1:2, :]
    stores = []

    def store(source, target):
        copy = pltpu.make_async_copy(source, target, store_sems.at[len(stores)])
        copy.start()
        stores.append(copy)

    for row in range(0, TALL, HALF):
        span = slice(row, row + HALF)
        rows = low_ref[span, :]
        q_ref[span, :] = (dot_nn(rows, w_ref[0]) + bias_q).astype(jnp.bfloat16)
        if row < LEN:
            k_ref[span, :] = dot_nn(rows, w_ref[1]).astype(jnp.bfloat16)
            v_ref[span, :] = (dot_nn(rows, w_ref[2]) + bias_v).astype(jnp.bfloat16)
        if row == LEN - HALF:
            store(k_ref, k_out)
            store(v_ref, v_out)
            store(q_ref.at[:LEN, :], q_out.at[:LEN, :])
    store(q_ref.at[LEN:, :], q_out.at[LEN:, :])
    for copy in stores:
        copy.wait()
    keep.wait()


def project(place, low, small, group):
    plan, pieces = group
    return pl.pallas_call(
        partial(project_kernel, plan),
        out_shape=[
            jax.ShapeDtypeStruct((TALL, D), jnp.bfloat16),
            jax.ShapeDtypeStruct((LEN, D), jnp.bfloat16),
            jax.ShapeDtypeStruct((LEN, D), jnp.bfloat16),
            jax.ShapeDtypeStruct((4, D, D), jnp.bfloat16),
        ],
        in_specs=[SMEM_SPEC, VMEM_SPEC, ANY_SPEC] + [ANY_SPEC] * len(pieces),
        out_specs=[ANY_SPEC] * 4,
        scratch_shapes=[
            pltpu.VMEM((TALL, D), jnp.bfloat16),
            pltpu.VMEM((TALL, D), jnp.bfloat16),
            pltpu.VMEM((LEN, D), jnp.bfloat16),
            pltpu.VMEM((LEN, D), jnp.bfloat16),
            pltpu.VMEM((4, D, D), jnp.bfloat16),
            pltpu.SemaphoreType.DMA((32,)),
            pltpu.SemaphoreType.DMA,
            pltpu.SemaphoreType.DMA,
            pltpu.SemaphoreType.DMA((4,)),
            pltpu.SemaphoreType.DMA,
        ],
        compiler_params=PARAMS,
        cost_estimate=pl.CostEstimate(flops=2 * 2048 * D * D, bytes_accessed=16000000, transcendentals=0),
        name="project",
    )(place, small, low, *pieces)


def build_masks(length, row_flags, col_flags, mask_ref, alive_ref):
    flags = row_flags[...]

    def body(step, carry):
        start = pl.multiple_of(step * 64, 64)
        key = lax.broadcasted_iota(jnp.int32, (64, LEN), 0) + start
        query = lax.broadcasted_iota(jnp.int32, (64, LEN), 1)
        valid = key < length
        free = jnp.broadcast_to(col_flags[pl.ds(start, 64), :], (64, LEN)) == 0.0
        marked = jnp.broadcast_to(flags, (64, LEN)) == 1.0
        content_ok = valid & (free | (marked & (key <= query)))
        query_ok = valid & (key != query) & (free | (key < query))
        mask_ref[pl.ds(start, 64), :LEN] = content_ok.astype(jnp.float32)
        mask_ref[pl.ds(start, 64), LEN:] = query_ok.astype(jnp.float32)
        return carry

    lax.fori_loop(0, 8, body, 0)
    alive_ref[...] = jnp.max(mask_ref[...], axis=0, keepdims=True)


def build_tiles(t_row, tile_ref):
    spread = jnp.broadcast_to(t_row, (128, 512))
    rolled = pltpu.roll(spread, 0, 1, stride=1, stride_axis=0)
    tile_ref[...] = rolled[:, :384]


def position_bias(tile_ref, far_ref, head, query_block, key_block):
    apart = query_block - key_block
    if apart >= 2:
        return far_ref[head, 0]
    if apart <= -2:
        return far_ref[head, 1]
    return tile_ref[:, 128 * (apart + 1) : 128 * (apart + 2)]


def head_lanes(shape, head):
    lane = lax.broadcasted_iota(jnp.int32, shape, 1)
    return (lane >= 64) if head else (lane < 64)


def mix_kernel(
    length_ref, far_ref, q_ref, k_ref, v_ref, row_flags, col_flags, t_ref,
    a_ref, p_ref, inverse_ref, dead_ref, mask_ref, alive_ref, tile_ref, o_ref,
):
    pair = pl.program_id(0)

    @pl.when(pair == 0)
    def _():
        build_masks(length_ref[0], row_flags, col_flags, mask_ref, alive_ref)
        dead_ref[...] = (1.0 - alive_ref[...]) * (1.0 / LEN)

    keys = k_ref[...].astype(jnp.float32) * SCORE_SCALE
    values_t = v_ref[...].astype(jnp.float32).T.astype(jnp.bfloat16)
    for head in range(2):
        build_tiles(t_ref[head], tile_ref.at[head])
        keys_own = jnp.where(head_lanes(keys.shape, head), keys, 0.0).astype(jnp.bfloat16)
        for chunk in range(4):
            at = chunk * HALF
            scores = dot_nt(keys_own, q_ref[at : at + HALF, :])
            for side in range(2):
                lanes = slice(at + side * 128, at + side * 128 + 128)
                blocks = []
                peak = None
                for key_block in range(4):
                    rows = slice(key_block * 128, key_block * 128 + 128)
                    block = scores[rows, side * 128 : side * 128 + 128] + position_bias(
                        tile_ref.at[head], far_ref, pair * 2 + head, (chunk % 2) * 2 + side, key_block
                    )
                    block = jnp.where(mask_ref[rows, lanes] > 0.0, block, MASKED)
                    blocks.append(block)
                    high = jnp.max(block, axis=0, keepdims=True)
                    peak = high if peak is None else jnp.maximum(peak, high)
                total = None
                for key_block in range(4):
                    rows = slice(key_block * 128, key_block * 128 + 128)
                    expo = jnp.exp(blocks[key_block] - peak)
                    part = jnp.sum(expo, axis=0, keepdims=True)
                    total = part if total is None else total + part
                    p_ref[head, rows, lanes] = expo.astype(jnp.bfloat16)
                inverse = 1.0 / total
                inverse_ref[head, :, lanes] = inverse * alive_ref[:, lanes]
                o_ref[head : head + 1, lanes] = inverse
        mixed = dot_nn(values_t[head * 64 : head * 64 + 64, :], p_ref[head])
        o_ref[8 + head * 64 : 8 + head * 64 + 64, :] = mixed * o_ref[head : head + 1, :]
    a_ref[...] = o_ref[8:, :].T.astype(jnp.bfloat16)


def mix(length, far, tvec, q, k, v, row_flags, col_flags):
    tall = pl.BlockSpec((TALL, 128), lambda p: (0, p))
    short = pl.BlockSpec((LEN, 128), lambda p: (0, p))
    return pl.pallas_call(
        mix_kernel,
        grid=(H // 2,),
        out_shape=[
            jax.ShapeDtypeStruct((TALL, D), jnp.bfloat16),
            jax.ShapeDtypeStruct((H, LEN, TALL), jnp.bfloat16),
            jax.ShapeDtypeStruct((H, 1, TALL), jnp.float32),
            jax.ShapeDtypeStruct((1, TALL), jnp.float32),
        ],
        in_specs=[
            SMEM_SPEC, SMEM_SPEC, tall, short, short,
            pl.BlockSpec((1, LEN), lambda p: (0, 0)),
            pl.BlockSpec((LEN, 1), lambda p: (0, 0)),
            pl.BlockSpec((2, 1, 512), lambda p: (p, 0, 0)),
        ],
        out_specs=[
            tall,
            pl.BlockSpec((2, LEN, TALL), lambda p: (p, 0, 0)),
            pl.BlockSpec((2, 1, TALL), lambda p: (p, 0, 0)),
            pl.BlockSpec((1, TALL), lambda p: (0, 0)),
        ],
        scratch_shapes=[
            pltpu.VMEM((LEN, TALL), jnp.float32),
            pltpu.VMEM((1, TALL), jnp.float32),
            pltpu.VMEM((2, 128, 384), jnp.float32),
            pltpu.VMEM((136, TALL), jnp.float32),
        ],
        compiler_params=PARAMS,
        cost_estimate=pl.CostEstimate(flops=6500000000, bytes_accessed=8000000, transcendentals=6300000),
        name="mix",
    )(length, far, q, k, v, row_flags, col_flags, tvec)


def mix_back_kernel(q_ref, k_ref, v_ref, da_ref, a_ref, p_ref, inverse_ref, dead_ref, *refs):
    (
        dq_ref, dk_ref, dv_ref, table_ref, s_ref, near_ref, da_t, low_t, q_t, g_ref,
    ) = refs[-10:]
    keys = k_ref[...].astype(jnp.float32) * SCORE_SCALE
    keys_t = keys.T.astype(jnp.bfloat16)
    q_t[...] = q_ref[...].astype(jnp.float32).T.astype(jnp.bfloat16)
    da_t[...] = da_ref[...].astype(jnp.float32).T
    product = a_ref[...].astype(jnp.float32).T * da_t[...]
    values = v_ref[...].astype(jnp.float32)
    near_ref[...] = jnp.zeros(near_ref.shape, jnp.float32)
    turn = (
        lax.broadcasted_iota(jnp.int32, (128, 128), 0)
        + lax.broadcasted_iota(jnp.int32, (128, 128), 1)
        == 127
    ).astype(jnp.float32)
    deltas = []
    for head in range(2):
        rows = slice(head * 64, head * 64 + 64)
        inverse = inverse_ref[head]
        deltas.append(jnp.sum(product[rows, :], axis=0, keepdims=True) * inverse)
        low_t[rows, :] = (da_t[rows, :] * inverse).astype(jnp.bfloat16)
    for head in range(2):
        own = slice(head * 64, head * 64 + 64)
        values_own = jnp.where(head_lanes(values.shape, head), values, 0.0).astype(jnp.bfloat16)
        delta = deltas[head]
        far_low = jnp.zeros((8, 128), jnp.float32)
        far_high = jnp.zeros((8, 128), jnp.float32)
        for chunk in range(4):
            at = chunk * HALF
            pulls = dot_nn(values_own, low_t[:, at : at + HALF])
            for side in range(2):
                lanes = slice(at + side * 128, at + side * 128 + 128)
                shift = delta[:, lanes]
                query_block = (chunk % 2) * 2 + side
                for key_block in range(4):
                    rows = slice(key_block * 128, key_block * 128 + 128)
                    cols = slice(side * 128, side * 128 + 128)
                    grad = p_ref[head, rows, lanes].astype(jnp.float32) * (
                        pulls[rows, cols] - shift
                    )
                    s_ref[head, rows, lanes] = grad.astype(jnp.bfloat16)
                    apart = query_block - key_block
                    if apart >= 2:
                        far_low = far_low + jnp.sum(grad.reshape(16, 8, 128), axis=0)
                    elif apart <= -2:
                        far_high = far_high + jnp.sum(grad.reshape(16, 8, 128), axis=0)
                    else:
                        near_ref[head, :, 128 * (apart + 1) : 128 * (apart + 2)] += grad
        g_ref[own, :LEN] = dot_nt(low_t[own, :], p_ref[head])
        g_ref[own, LEN:] = dot_nt(q_t[own, :], s_ref[head]) * SCORE_SCALE
        da_t[own, :] = dot_nn(keys_t[own, :], s_ref[head])
        turned = jnp.dot(
            turn, near_ref[head], precision=lax.Precision.HIGHEST, preferred_element_type=jnp.float32
        )
        aligned = pltpu.roll(turned, 0, 1, stride=1, stride_axis=0)
        table_ref[head, :, :512] = jnp.sum(aligned, axis=0, keepdims=True)
        table_ref[head, :, 512:640] = jnp.sum(far_low, axis=0, keepdims=True)
        table_ref[head, :, 640:] = jnp.sum(far_high, axis=0, keepdims=True)
    uniform = dot_nn(dead_ref[...].astype(jnp.bfloat16), da_ref[...])
    dv_ref[...] = (g_ref[:, :LEN].T + uniform).astype(jnp.bfloat16)
    dk_ref[...] = g_ref[:, LEN:].T.astype(jnp.bfloat16)
    dq_ref[...] = da_t[...].T.astype(jnp.bfloat16)


def mix_back(first, q, k, v, da, a, p, inverse, dead, held=()):
    tall = pl.BlockSpec((TALL, 128), lambda i: (0, i + first))
    short = pl.BlockSpec((LEN, 128), lambda i: (0, i + first))
    return pl.pallas_call(
        mix_back_kernel,
        grid=(H // 4,),
        out_shape=[
            jax.ShapeDtypeStruct((TALL, D), jnp.bfloat16),
            jax.ShapeDtypeStruct((LEN, D), jnp.bfloat16),
            jax.ShapeDtypeStruct((LEN, D), jnp.bfloat16),
            jax.ShapeDtypeStruct((H // 2, 1, 768), jnp.float32),
        ],
        in_specs=[
            tall, short, short, tall, tall,
            pl.BlockSpec((2, LEN, TALL), lambda i: (i + first, 0, 0)),
            pl.BlockSpec((2, 1, TALL), lambda i: (i + first, 0, 0)),
            pl.BlockSpec((1, TALL), lambda i: (0, 0)),
        ]
        + [ANY_SPEC] * len(held),
        out_specs=[tall, short, short, pl.BlockSpec((2, 1, 768), lambda i: (i, 0, 0))],
        input_output_aliases={8 + index: index for index in range(len(held))},
        scratch_shapes=[
            pltpu.VMEM((2, LEN, TALL), jnp.bfloat16),
            pltpu.VMEM((2, 128, 512), jnp.float32),
            pltpu.VMEM((128, TALL), jnp.float32),
            pltpu.VMEM((128, TALL), jnp.bfloat16),
            pltpu.VMEM((128, TALL), jnp.bfloat16),
            pltpu.VMEM((128, TALL), jnp.float32),
        ],
        compiler_params=PARAMS,
        cost_estimate=pl.CostEstimate(flops=8000000000, bytes_accessed=16000000, transcendentals=0),
        name="mix_back",
    )(q, k, v, da, a, p, inverse, dead, *held)


GELU_SCALE = 0.7978845608028654
GELU_CUBE = 0.044715


def feed_rows(rows, small_ref, hidden_bias_ref, resid, normed_ref, pre_ref, inner_ref, outer_ref):
    unit, scale = norm_parts(resid)
    normed = unit * small_ref[3:4, :] + small_ref[4:5, :]
    low = normed.astype(jnp.bfloat16)
    normed_ref[rows, :] = low
    total = normed + small_ref[5:6, :]
    for chunk in range(4):
        pre = dot_nn(low, inner_ref[chunk]) + hidden_bias_ref[:, chunk * D : chunk * D + D]
        pre_ref[chunk, rows, :] = pre.astype(jnp.bfloat16)
        tanh = jnp.tanh(GELU_SCALE * (pre + GELU_CUBE * (pre * pre * pre)))
        active = (pre * (0.5 + 0.5 * tanh)).astype(jnp.bfloat16)
        total = total + dot_nn(active, outer_ref[chunk])
    return total


def norm_two_back(unit, scale, grad, small_ref, sums):
    back = norm_back(unit, scale, grad, small_ref[6:7, :])
    low = back.astype(jnp.bfloat16)
    parts = (low.astype(jnp.float32), grad * unit, grad)
    return back, low, [
        total + jnp.sum(part, axis=0, keepdims=True) for total, part in zip(sums, parts)
    ]


def issue(pairs, sems, first=0):
    copies = [
        pltpu.make_async_copy(source, target, sems.at[first + index])
        for index, (source, target) in enumerate(pairs)
    ]
    for copy in copies:
        copy.start()
    return copies


def finish(copies):
    for copy in copies:
        copy.wait()


def storer(sems):
    copies = []

    def store(source, target):
        copy = pltpu.make_async_copy(source, target, sems.at[len(copies)])
        copy.start()
        copies.append(copy)

    return store, copies


def feed_kernel(
    plan, place_ref, small_ref, hidden_bias_ref, mix_any, hidden_any, attn_any, *refs
):
    (
        resid_out, pre_out, normed_out, low_out, summed_out,
        mix_ref, hidden_ref, wo_ref, inner_ref, outer_ref, resid_ref, total_ref, normed_ref,
        pre_ref, low_ref, sems, load_sems, store_sems,
    ) = refs[-18:]
    finish(
        issue(
            ((mix_any, mix_ref), (attn_any.at[3], wo_ref), (hidden_any, hidden_ref)), load_sems
        )
    )
    fetches = start_fetch(
        ("inner", "outer"), plan, place_ref, refs[:-18], (inner_ref, outer_ref), sems
    )
    for row in range(0, TALL, HALF):
        rows = slice(row, row + HALF)
        resid_ref[rows, :] = (
            hidden_ref[rows, :].astype(jnp.float32)
            + dot_nn(mix_ref[rows, :], wo_ref[...])
            + small_ref[2:3, :]
        )
    finish(fetches)
    store, stores = storer(store_sems)
    store(resid_ref, resid_out)
    for row in range(0, TALL, HALF):
        rows = slice(row, row + HALF)
        total = feed_rows(
            rows, small_ref, hidden_bias_ref, resid_ref[rows, :], normed_ref, pre_ref, inner_ref,
            outer_ref,
        )
        total_ref[rows, :] = total
        store(pre_ref.at[:, rows, :], pre_out.at[:, rows, :])
        store(total_ref.at[rows, :], summed_out.at[rows, :])
        store(normed_ref.at[rows, :], normed_out.at[rows, :])
        unit, scale = norm_parts(total)
        following = unit * small_ref[6:7, :] + small_ref[7:8, :]
        low_ref[rows, :] = following.astype(jnp.bfloat16)
        store(low_ref.at[rows, :], low_out.at[rows, :])
    finish(stores)


def feed(place, small, hidden_bias, mixed, hidden, attn, group):
    plan, pieces = group
    tall = jax.ShapeDtypeStruct((TALL, D), jnp.float32)
    tall_low = jax.ShapeDtypeStruct((TALL, D), jnp.bfloat16)
    return pl.pallas_call(
        partial(feed_kernel, plan),
        out_shape=[
            tall, jax.ShapeDtypeStruct((4, TALL, D), jnp.bfloat16), tall_low, tall_low, tall
        ],
        in_specs=[SMEM_SPEC, VMEM_SPEC, VMEM_SPEC] + [ANY_SPEC] * (3 + len(pieces)),
        out_specs=[ANY_SPEC] * 5,
        scratch_shapes=[
            pltpu.VMEM((TALL, D), jnp.bfloat16),
            pltpu.VMEM((TALL, D), jnp.bfloat16),
            pltpu.VMEM((D, D), jnp.bfloat16),
            pltpu.VMEM((4, D, D), jnp.bfloat16),
            pltpu.VMEM((4, D, D), jnp.bfloat16),
            pltpu.VMEM((TALL, D), jnp.float32),
            pltpu.VMEM((TALL, D), jnp.float32),
            pltpu.VMEM((TALL, D), jnp.bfloat16),
            pltpu.VMEM((4, TALL, D), jnp.bfloat16),
            pltpu.VMEM((TALL, D), jnp.bfloat16),
            pltpu.SemaphoreType.DMA((64,)),
            pltpu.SemaphoreType.DMA((3,)),
            pltpu.SemaphoreType.DMA((17,)),
        ],
        compiler_params=PARAMS,
        cost_estimate=pl.CostEstimate(flops=2 * TALL * D * (D + 2 * FF), bytes_accessed=30000000, transcendentals=3000000),
        name="feed",
    )(place, small, hidden_bias, mixed, hidden, attn, *pieces)


def back_steps(
    place_ref, small_ref, before, store, outs, vec_ref, dhidden_ref, branch_ref, total_ref,
    normed_ref, resid_ref, pre_ref, mix_ref, wo_ref, inner_ref, outer_ref, active_ref, dpre_ref,
    dinner_ref, douter_ref, dwo_ref,
):
    dresid_out, dmix_out, dwo_out, keep_out, send_out = outs
    x, c, z, y = (place_ref[index] for index in range(4))
    order = [(1 - step // 2, step % 2) for step in range(4)]
    chunks = [side * 2 + (c ^ apart) for apart, side in order]
    sums = [jnp.zeros((1, D), jnp.float32)] * 3
    for step in range(4):
        apart, side = order[step]
        chunk = chunks[step]
        before(step)
        bias_grad = jnp.zeros((1, D), jnp.float32)
        for row in range(0, TALL, HALF):
            rows = slice(row, row + HALF)
            pull = dot_nt(branch_ref[rows, :], outer_ref[chunk])
            pre = pre_ref[chunk, rows, :].astype(jnp.float32)
            square = pre * pre
            tanh = jnp.tanh(GELU_SCALE * pre * (1.0 + GELU_CUBE * square))
            half = 0.5 + 0.5 * tanh
            active_ref[rows, :] = (pre * half).astype(jnp.bfloat16)
            slope = half + (0.5 * GELU_SCALE) * pre * (1.0 - tanh * tanh) * (
                1.0 + (3.0 * GELU_CUBE) * square
            )
            dpre = (pull * slope).astype(jnp.bfloat16)
            dpre_ref[rows, :] = dpre
            bias_grad += jnp.sum(dpre.astype(jnp.float32), axis=0, keepdims=True)
            grad = total_ref[rows, :] + dot_nt(dpre, inner_ref[chunk])
            if step < 3:
                total_ref[rows, :] = grad
            else:
                unit, scale = norm_parts(resid_ref[rows, :])
                back = norm_back(unit, scale, grad, small_ref[3:4, :])
                resid_ref[rows, :] = back
                low = back.astype(jnp.bfloat16)
                pre_ref[chunks[0], rows, :] = low
                pre_ref[chunks[1], rows, :] = dot_nt(low, wo_ref[...]).astype(jnp.bfloat16)
                parts = (low.astype(jnp.float32), grad * unit, grad)
                sums = [
                    value + jnp.sum(part, axis=0, keepdims=True)
                    for value, part in zip(sums, parts)
                ]
        dhidden_ref[chunk] = bias_grad
        if step == 3:
            store(resid_ref, dresid_out)
            store(pre_ref.at[chunks[1]], dmix_out)
        douter_ref[step] = (
            dot_tn(active_ref[...], branch_ref[...]).astype(jnp.bfloat16).reshape(2, 2, 2, ROWS, D)
        )
        for y_block in range(2):
            for x_block in range(2):
                spot = (y_block ^ y, x_block ^ x, chunk, 1)
                store(douter_ref.at[step, y_block, x_block, c], keep_out.at[spot])
                store(douter_ref.at[step, y_block, x_block, 1 - c], send_out.at[spot])
        dinner_ref[step] = (
            dot_tn(normed_ref[...], dpre_ref[...]).astype(jnp.bfloat16).reshape(4, 2, ROWS, D)
        )
        target = send_out if apart else keep_out
        for y_block in range(2):
            store(dinner_ref.at[step, :, y_block], target.at[y_block ^ y, side ^ x, :, 0])
    dwo_ref[...] = dot_tn(mix_ref[...], pre_ref[chunks[0]]).astype(jnp.bfloat16)
    store(dwo_ref, dwo_out)
    for index, value in enumerate(sums):
        vec_ref[index : index + 1, :] = value


BACK_SHAPES = [
    jax.ShapeDtypeStruct((TALL, D), jnp.float32),
    jax.ShapeDtypeStruct((TALL, D), jnp.bfloat16),
    jax.ShapeDtypeStruct((D, D), jnp.bfloat16),
    jax.ShapeDtypeStruct((2, 2, 4, 2, ROWS, D), jnp.bfloat16),
    jax.ShapeDtypeStruct((2, 2, 4, 2, ROWS, D), jnp.bfloat16),
    jax.ShapeDtypeStruct((6, D), jnp.float32),
    jax.ShapeDtypeStruct((4, 1, D), jnp.float32),
]
BACK_SCRATCH = [
    pltpu.VMEM((TALL, D), jnp.bfloat16),
    pltpu.VMEM((TALL, D), jnp.float32),
    pltpu.VMEM((TALL, D), jnp.bfloat16),
    pltpu.VMEM((TALL, D), jnp.float32),
    pltpu.VMEM((4, TALL, D), jnp.bfloat16),
    pltpu.VMEM((TALL, D), jnp.bfloat16),
    pltpu.VMEM((D, D), jnp.bfloat16),
    pltpu.VMEM((4, D, D), jnp.bfloat16),
    pltpu.VMEM((4, D, D), jnp.bfloat16),
    pltpu.VMEM((TALL, D), jnp.bfloat16),
    pltpu.VMEM((TALL, D), jnp.bfloat16),
    pltpu.VMEM((4, 4, 2, ROWS, D), jnp.bfloat16),
    pltpu.VMEM((4, 2, 2, 2, ROWS, D), jnp.bfloat16),
    pltpu.VMEM((D, D), jnp.bfloat16),
    pltpu.SemaphoreType.DMA((64,)),
    pltpu.SemaphoreType.DMA((16,)),
    pltpu.SemaphoreType.DMA((48,)),
]


def turn_kernel(
    plan, place_ref, length_ref, small_ref, below_ref, hidden_bias_ref, mix_any, summed_any,
    attn_any, cot_c_any, cot_q_any, *refs
):
    content_out, query_out = refs[-27:-25]
    outs = refs[-25:-20]
    vec_ref, dhidden_ref = refs[-20:-18]
    low_ref = refs[-18]
    (
        branch_ref, total_ref, normed_ref, resid_ref, pre_ref, mix_ref, wo_ref, inner_ref,
        outer_ref, active_ref, dpre_ref, dinner_ref, douter_ref, dwo_ref,
        sems, load_sems, store_sems,
    ) = refs[-17:]
    store, stores = storer(store_sems)
    finish(
        issue(
            ((mix_any, mix_ref), (attn_any.at[3], wo_ref), (summed_any, resid_ref)), load_sems
        )
    )
    fetches = start_fetch(
        ("inner", "outer"), plan, place_ref, refs[:-27], (inner_ref, outer_ref), sems
    )
    fetches += issue(
        ((cot_c_any, low_ref.at[:LEN, :]), (cot_q_any, low_ref.at[LEN:, :])), load_sems, 3
    )
    for row in range(0, TALL, HALF):
        rows = slice(row, row + HALF)
        unit, scale = norm_parts(resid_ref[rows, :])
        resid_ref[rows, :] = (
            unit * below_ref[6:7, :]
            + below_ref[7:8, :]
            + dot_nn(mix_ref[rows, :], wo_ref[...])
            + small_ref[2:3, :]
        )
    finish(fetches)
    sums = [jnp.zeros((1, D), jnp.float32)] * 3
    for row in range(0, TALL, HALF):
        rows = slice(row, row + HALF)
        total = feed_rows(
            rows, small_ref, hidden_bias_ref, resid_ref[rows, :], normed_ref, pre_ref, inner_ref,
            outer_ref,
        )
        unit, scale = norm_parts(total)
        position = lax.broadcasted_iota(jnp.int32, (HALF, 1), 0) + row % LEN
        valid = (position < length_ref[0]).astype(jnp.float32)
        grad = low_ref[rows, :].astype(jnp.float32) * valid
        low_ref[rows, :] = (unit * small_ref[6:7, :] + small_ref[7:8, :]).astype(jnp.bfloat16)
        total_ref[rows, :], branch_ref[rows, :], sums = norm_two_back(
            unit, scale, grad, small_ref, sums
        )
    store(low_ref.at[:LEN, :], content_out)
    store(low_ref.at[LEN:, :], query_out)
    for index, value in enumerate(sums):
        vec_ref[3 + index : 4 + index, :] = value
    back_steps(
        place_ref, small_ref, lambda step: None, store, outs, vec_ref, dhidden_ref, branch_ref,
        total_ref, normed_ref, resid_ref, pre_ref, mix_ref, wo_ref, inner_ref, outer_ref,
        active_ref, dpre_ref, dinner_ref, douter_ref, dwo_ref,
    )
    finish(stores)


def turn(place, length, small, below, hidden_bias, mixed, summed, attn, cots, group):
    plan, pieces = group
    half_low = jax.ShapeDtypeStruct((LEN, D), jnp.bfloat16)
    return pl.pallas_call(
        partial(turn_kernel, plan),
        out_shape=[half_low, half_low] + BACK_SHAPES,
        in_specs=[SMEM_SPEC] * 2 + [VMEM_SPEC] * 3 + [ANY_SPEC] * (5 + len(pieces)),
        out_specs=[ANY_SPEC] * 7 + [VMEM_SPEC] * 2,
        scratch_shapes=[pltpu.VMEM((TALL, D), jnp.bfloat16)] + BACK_SCRATCH,
        compiler_params=PARAMS,
        cost_estimate=pl.CostEstimate(flops=6 * TALL * D * (D + 2 * FF), bytes_accessed=60000000, transcendentals=6000000),
        name="turn",
    )(place, length, small, below, hidden_bias, mixed, summed, attn, *cots, *pieces)


def down_kernel(
    plan, place_ref, small_ref, dq_any, dk_any, dv_any, w_any, dresid_any, summed_any,
    normed_any, resid_any, pre_any, mix_any, attn_any, *refs
):
    outs = refs[-29:-24]
    vec_ref, dhidden_ref = refs[-24:-22]
    dq_ref, dk_ref, dv_ref, w_ref, summed_ref = refs[-22:-17]
    (
        branch_ref, total_ref, normed_ref, resid_ref, pre_ref, mix_ref, wo_ref, inner_ref,
        outer_ref, active_ref, dpre_ref, dinner_ref, douter_ref, dwo_ref,
        sems, load_sems, store_sems,
    ) = refs[-17:]
    x, c, z, y = (place_ref[index] for index in range(4))
    chunks = [side * 2 + (c ^ apart) for apart in (1, 0) for side in range(2)]
    store, stores = storer(store_sems)
    loads = issue(
        (
            (w_any.at[0], w_ref.at[0]), (dq_any, dq_ref), (dresid_any, total_ref),
            (summed_any, summed_ref), (w_any.at[1:3], w_ref.at[1:3]), (dk_any, dk_ref),
            (dv_any, dv_ref),
        ),
        load_sems,
    )
    finish(loads[:4])
    fetches = start_fetch(
        ("inner", "outer"), plan, place_ref, refs[:-29], (inner_ref, outer_ref), sems
    )
    fetches += issue(((pre_any.at[chunks[0]], pre_ref.at[chunks[0]]),), load_sems, 7)
    sums = [jnp.zeros((1, D), jnp.float32)] * 3
    for index, row in enumerate((LEN, LEN + HALF, 0, HALF)):
        rows = slice(row, row + HALF)
        if index == 2:
            finish(loads[4:])
        total = total_ref[rows, :] + dot_nt(dq_ref[rows, :], w_ref[0])
        if index >= 2:
            total = total + dot_nt(dk_ref[rows, :], w_ref[1]) + dot_nt(dv_ref[rows, :], w_ref[2])
        unit, scale = norm_parts(summed_ref[rows, :])
        total_ref[rows, :], branch_ref[rows, :], sums = norm_two_back(
            unit, scale, total, small_ref, sums
        )
    for index, value in enumerate(sums):
        vec_ref[3 + index : 4 + index, :] = value
    finish(fetches)
    late = []

    def before(step):
        if step == 0:
            late.append(issue(((normed_any, normed_ref),), load_sems, 8))
        else:
            finish(late.pop())
        if step < 3:
            chunk = chunks[step + 1]
            late.insert(0, issue(((pre_any.at[chunk], pre_ref.at[chunk]),), load_sems, 9 + step))
        if step == 0:
            finish(late.pop())
        if step == 2:
            late[0].extend(
                issue(
                    ((resid_any, resid_ref), (mix_any, mix_ref), (attn_any.at[3], wo_ref)),
                    load_sems,
                    12,
                )
            )

    back_steps(
        place_ref, small_ref, before, store, outs, vec_ref, dhidden_ref, branch_ref, total_ref,
        normed_ref, resid_ref, pre_ref, mix_ref, wo_ref, inner_ref, outer_ref, active_ref,
        dpre_ref, dinner_ref, douter_ref, dwo_ref,
    )
    finish(stores)


def down(place, small, dq, dk, dv, w_above, dresid, summed, normed, resid, pre, mixed, attn, group):
    plan, pieces = group
    return pl.pallas_call(
        partial(down_kernel, plan),
        out_shape=BACK_SHAPES,
        in_specs=[SMEM_SPEC, VMEM_SPEC] + [ANY_SPEC] * (11 + len(pieces)),
        out_specs=[ANY_SPEC] * 5 + [VMEM_SPEC] * 2,
        scratch_shapes=[
            pltpu.VMEM((TALL, D), jnp.bfloat16),
            pltpu.VMEM((LEN, D), jnp.bfloat16),
            pltpu.VMEM((LEN, D), jnp.bfloat16),
            pltpu.VMEM((3, D, D), jnp.bfloat16),
            pltpu.VMEM((TALL, D), jnp.float32),
        ]
        + BACK_SCRATCH,
        compiler_params=PARAMS,
        cost_estimate=pl.CostEstimate(flops=5 * TALL * D * (D + 2 * FF), bytes_accessed=60000000, transcendentals=3000000),
        name="down",
    )(place, small, dq, dk, dv, w_above, dresid, summed, normed, resid, pre, mixed, attn, *pieces)


def weight_back_kernel(
    place_ref, low_any, dq_any, dk_any, dv_any, dwo_any, keep_out, send_out, vec_ref,
    low_ref, dq_ref, dk_ref, dv_ref, dwo_ref, grads_ref, load_sems, sems,
):
    x, c, z, y = (place_ref[index] for index in range(4))
    load = [
        pltpu.make_async_copy(source, target, load_sems.at[index])
        for index, (source, target) in enumerate(
            (
                (low_any.at[:LEN, :], low_ref.at[:LEN, :]), (dk_any, dk_ref), (dv_any, dv_ref),
                (low_any.at[LEN:, :], low_ref.at[LEN:, :]), (dq_any, dq_ref), (dwo_any, dwo_ref),
            )
        )
    ]
    for copy in load:
        copy.start()
    load[0].wait()
    load[1].wait()
    grads_ref[1] = (
        dot_tn(low_ref[:LEN, :], dk_ref[...]).astype(jnp.bfloat16).reshape(4, 2, ROWS, D)
    )
    load[2].wait()
    grads_ref[2] = (
        dot_tn(low_ref[:LEN, :], dv_ref[...]).astype(jnp.bfloat16).reshape(4, 2, ROWS, D)
    )
    vec_ref[1:2, :] = jnp.sum(dv_ref[...].astype(jnp.float32), axis=0, keepdims=True)
    for copy in load[3:]:
        copy.wait()
    grads_ref[3] = dwo_ref[...].reshape(4, 2, ROWS, D)
    grads_ref[0] = dot_tn(low_ref[...], dq_ref[...]).astype(jnp.bfloat16).reshape(4, 2, ROWS, D)
    vec_ref[0:1, :] = jnp.sum(dq_ref[...].astype(jnp.float32), axis=0, keepdims=True)
    blocks = []
    for apart, target in ((1, send_out), (0, keep_out)):
        for side in range(2):
            for y_block in range(2):
                copy = pltpu.make_async_copy(
                    grads_ref.at[side * 2 + (c ^ apart), :, y_block],
                    target.at[y_block ^ y, side ^ x, :, 0],
                    sems.at[len(blocks)],
                )
                copy.start()
                blocks.append(copy)
    for block in blocks:
        block.wait()


def weight_back(place, low, dq, dk, dv, dwo):
    blocks = jax.ShapeDtypeStruct((2, 2, 4, 1, ROWS, D), jnp.bfloat16)
    return pl.pallas_call(
        weight_back_kernel,
        out_shape=[blocks, blocks, jax.ShapeDtypeStruct((2, D), jnp.float32)],
        in_specs=[SMEM_SPEC] + [ANY_SPEC] * 5,
        out_specs=[ANY_SPEC] * 2 + [VMEM_SPEC],
        scratch_shapes=[
            pltpu.VMEM((TALL, D), jnp.bfloat16),
            pltpu.VMEM((TALL, D), jnp.bfloat16),
            pltpu.VMEM((LEN, D), jnp.bfloat16),
            pltpu.VMEM((LEN, D), jnp.bfloat16),
            pltpu.VMEM((D, D), jnp.bfloat16),
            pltpu.VMEM((4, 4, 2, ROWS, D), jnp.bfloat16),
            pltpu.SemaphoreType.DMA((6,)),
            pltpu.SemaphoreType.DMA((8,)),
        ],
        compiler_params=PARAMS,
        cost_estimate=pl.CostEstimate(flops=2 * 2048 * D * D, bytes_accessed=12000000, transcendentals=0),
        name="weight_back",
    )(place, low, dq, dk, dv, dwo)


def input_back_kernel(
    dq_any, dk_any, dv_any, w_any, dresid_any, first_out, second_out,
    dq_ref, dk_ref, dv_ref, w_ref, dresid_ref, load_sems, store_sems,
):
    loads = issue(
        (
            (w_any.at[0], w_ref.at[0]), (dq_any, dq_ref), (dresid_any, dresid_ref),
            (w_any.at[1:3], w_ref.at[1:3]), (dk_any, dk_ref), (dv_any, dv_ref),
        ),
        load_sems,
    )
    finish(loads[:3])
    store, stores = storer(store_sems)
    for index, row in enumerate((LEN, LEN + HALF, 0, HALF)):
        rows = slice(row, row + HALF)
        if index == 2:
            finish(loads[3:])
        total = dresid_ref[rows, :] + dot_nt(dq_ref[rows, :], w_ref[0])
        if index >= 2:
            total = total + dot_nt(dk_ref[rows, :], w_ref[1]) + dot_nt(dv_ref[rows, :], w_ref[2])
        dresid_ref[rows, :] = total
        target = first_out if index >= 2 else second_out
        store(dresid_ref.at[rows, :], target.at[row % LEN : row % LEN + HALF, :])
    finish(stores)


def input_back(dq, dk, dv, attn, dresid):
    half = jax.ShapeDtypeStruct((LEN, D), jnp.float32)
    return pl.pallas_call(
        input_back_kernel,
        out_shape=[half, half],
        in_specs=[ANY_SPEC] * 5,
        out_specs=[ANY_SPEC] * 2,
        scratch_shapes=[
            pltpu.VMEM((TALL, D), jnp.bfloat16),
            pltpu.VMEM((LEN, D), jnp.bfloat16),
            pltpu.VMEM((LEN, D), jnp.bfloat16),
            pltpu.VMEM((3, D, D), jnp.bfloat16),
            pltpu.VMEM((TALL, D), jnp.float32),
            pltpu.SemaphoreType.DMA((6,)),
            pltpu.SemaphoreType.DMA((4,)),
        ],
        compiler_params=PARAMS,
        cost_estimate=pl.CostEstimate(flops=2 * 2048 * D * D, bytes_accessed=16000000, transcendentals=0),
        name="input_back",
    )(dq, dk, dv, attn, dresid)


def bias_vectors(table):
    lane = jnp.arange(512, dtype=jnp.int32)
    offset = jnp.where(lane < 384, 128 - lane, 640 - lane)
    onehot = bucket_of(offset)[:, None] == jnp.arange(NB, dtype=jnp.int32)[None, :]
    near = jnp.dot(table, onehot.astype(jnp.float32).T, precision=lax.Precision.HIGHEST)
    return (near[:, None, :], jnp.stack([table[:, 15], table[:, 31]], axis=1), onehot)


def bucket_of(offset):
    distance = jnp.abs(offset)
    far_bucket = jnp.full(distance.shape, 8, jnp.int32)
    for exponent in range(1, 8):
        far_bucket = far_bucket + (distance * distance >= 64 * 2**exponent).astype(jnp.int32)
    near_or_far = jnp.where(distance < 8, distance, far_bucket)
    return near_or_far + NB // 2 * (offset > 0).astype(jnp.int32)


def table_grad(sums, onehot):
    near = jnp.roll(onehot.astype(jnp.float32), 127, axis=0)
    far = jnp.arange(NB, dtype=jnp.int32)[None, :] == jnp.repeat(jnp.array([15, 31]), 128)[:, None]
    return jnp.dot(
        sums[:, 0, :],
        jnp.concatenate([near, far.astype(jnp.float32)]),
        precision=lax.Precision.HIGHEST,
    )


def adam_kernel(rate, master_ref, first_ref, second_ref, grad_ref, *refs):
    master_out, first_out, second_out = refs[-3:]
    grad = grad_ref[...].astype(jnp.float32).reshape(master_ref.shape)
    master = master_ref[...]
    first = BETA_ONE * first_ref[...] + (1.0 - BETA_ONE) * grad
    second = BETA_TWO * second_ref[...] + (1.0 - BETA_TWO) * grad * grad
    first_out[...] = first
    second_out[...] = second
    first_scale = rate / (1.0 - BETA_ONE**STEP)
    second_scale = 1.0 / (1.0 - BETA_TWO**STEP)
    step = (first_scale * first) / (jnp.sqrt(second_scale * second) + ADAM_EPS)
    master_out[...] = master - (step + (rate * WEIGHT_DECAY) * master)


def adam(kind, layer, rate, state, quarters, member, done):
    if kind == "attn":
        block = pl.BlockSpec((1, 1, ROWS, D), lambda i: (layer, i, 0, 0))
    elif kind == "inner":
        block = pl.BlockSpec((1, ROWS, D), lambda i: (layer, 0, i))
    else:
        block = pl.BlockSpec((1, ROWS, D), lambda i: (layer, i, 0))
    held = done or ()
    return pl.pallas_call(
        partial(adam_kernel, rate),
        grid=(4,),
        out_shape=[jax.ShapeDtypeStruct(array.shape, jnp.float32) for array in state],
        in_specs=[block] * 3
        + [pl.BlockSpec((1, 1, ROWS, D), lambda i: (i, member, 0, 0))]
        + [ANY_SPEC] * len(held),
        out_specs=[block] * 3,
        input_output_aliases={4 + index: index for index in range(len(held))},
        compiler_params=PARAMS,
        cost_estimate=pl.CostEstimate(flops=5000000, bytes_accessed=8000000, transcendentals=0),
        name="adam",
    )(*state, quarters, *held)


def fetch_forward(shards):
    low = tuple(shard.astype(jnp.bfloat16) for shard in shards)
    return (
        lax.all_gather(low[0], "fsdp", axis=1, tiled=True),
        lax.all_gather(low[1], "fsdp", axis=0, tiled=True),
        lax.all_gather(low[2], "fsdp", axis=0, tiled=True),
    )


def reduce_layer(grads):
    owned = tuple(
        lax.psum_scatter(
            grad.astype(jnp.bfloat16), "fsdp", scatter_dimension=axis, tiled=True
        ).astype(jnp.float32)
        for grad, axis in zip(grads, (1, 0, 0))
    )
    return lax.psum(owned, "dp")


def forward_layer(hidden_c, hidden_q, weights, lengths, flag_rows, onehot):
    attn_w, inner_w, outer_w, small_w = weights
    pieces, hidden_bias, bias_table = unpack(small_w.astype(jnp.float32))
    bias_q, bias_v, bias_o, gain_one, shift_one, bias_two, gain_two, shift_two = pieces
    table_low = bias_table.astype(jnp.bfloat16)
    low_c = hidden_c.astype(jnp.bfloat16)
    low_q = hidden_q.astype(jnp.bfloat16)
    projected = jnp.einsum("td,sde->ste", low_c, attn_w[:3], preferred_element_type=jnp.float32)
    query_c = (projected[0] + bias_q).astype(jnp.bfloat16)
    key_rows = projected[1].astype(jnp.bfloat16)
    value_rows = (projected[2] + bias_v).astype(jnp.bfloat16)
    query_q = (jnp.dot(low_q, attn_w[0], preferred_element_type=jnp.float32) + bias_q).astype(
        jnp.bfloat16
    )
    mixed_c, mixed_q, lse_c, lse_q = lax.map(
        partial(attend_slot, onehot, table_low),
        (
            to_heads(query_c),
            to_heads(query_q),
            to_heads(key_rows),
            to_heads(value_rows),
            lengths,
            flag_rows,
        ),
    )
    mixed_c = mixed_c.reshape(-1, D)
    mixed_q = mixed_q.reshape(-1, D)
    outputs = []
    kept = []
    for hidden_in, mixed in ((hidden_c, mixed_c), (hidden_q, mixed_q)):
        resid = hidden_in + jnp.dot(mixed, attn_w[3], preferred_element_type=jnp.float32) + bias_o
        normed = layer_norm(resid, gain_one, shift_one)
        pre_act = (
            jnp.dot(normed.astype(jnp.bfloat16), inner_w, preferred_element_type=jnp.float32)
            + hidden_bias
        )
        active = jax.nn.gelu(pre_act, approximate=True).astype(jnp.bfloat16)
        summed = normed + jnp.dot(active, outer_w, preferred_element_type=jnp.float32) + bias_two
        outputs.append(layer_norm(summed, gain_two, shift_two))
        kept.append((resid, summed, pre_act))
    saved = (
        hidden_c,
        hidden_q,
        query_c,
        query_q,
        key_rows,
        value_rows,
        lse_c,
        lse_q,
        mixed_c,
        mixed_q,
        kept[0],
        kept[1],
    )
    return (outputs[0], outputs[1], saved)


def backward_layer(saved, weights, grad_c, grad_q, lengths, flag_rows, onehot):
    attn_w, inner_w, outer_w, small_w = weights
    pieces, hidden_bias, bias_table = unpack(small_w.astype(jnp.float32))
    bias_q, bias_v, bias_o, gain_one, shift_one, bias_two, gain_two, shift_two = pieces
    table_low = bias_table.astype(jnp.bfloat16)
    (
        hidden_c,
        hidden_q,
        query_c,
        query_q,
        key_rows,
        value_rows,
        lse_c,
        lse_q,
        mixed_c,
        mixed_q,
        kept_c,
        kept_q,
    ) = saved
    gelu_tanh = partial(jax.nn.gelu, approximate=True)
    grad_outer = jnp.zeros(outer_w.shape, jnp.float32)
    grad_inner = jnp.zeros(inner_w.shape, jnp.float32)
    grad_attn_out = jnp.zeros((D, D), jnp.float32)
    grad_bias_two = jnp.zeros((D,), jnp.float32)
    grad_hidden_bias = jnp.zeros((FF,), jnp.float32)
    grad_bias_o = jnp.zeros((D,), jnp.float32)
    grad_gain_one = jnp.zeros((D,), jnp.float32)
    grad_shift_one = jnp.zeros((D,), jnp.float32)
    grad_gain_two = jnp.zeros((D,), jnp.float32)
    grad_shift_two = jnp.zeros((D,), jnp.float32)
    residual_grads = []
    mix_grads = []
    for kept_rows, grad_out, mixed in ((kept_c, grad_c, mixed_c), (kept_q, grad_q, mixed_q)):
        resid, summed, pre_act = kept_rows
        normed, norm_one_back = jax.vjp(layer_norm, resid, gain_one, shift_one)
        unused_out, norm_two_back = jax.vjp(layer_norm, summed, gain_two, shift_two)
        grad_summed, grad_g2, grad_s2 = norm_two_back(grad_out)
        grad_gain_two = grad_gain_two + grad_g2
        grad_shift_two = grad_shift_two + grad_s2
        grad_branch = grad_summed.astype(jnp.bfloat16)
        grad_bias_two = grad_bias_two + jnp.sum(grad_branch.astype(jnp.float32), axis=0)
        active, gelu_back = jax.vjp(gelu_tanh, pre_act)
        grad_outer = grad_outer + jnp.einsum(
            "tf,td->fd",
            active.astype(jnp.bfloat16),
            grad_branch,
            preferred_element_type=jnp.float32,
        )
        grad_active = jnp.einsum(
            "td,fd->tf", grad_branch, outer_w, preferred_element_type=jnp.float32
        )
        grad_pre = gelu_back(grad_active)[0].astype(jnp.bfloat16)
        grad_hidden_bias = grad_hidden_bias + jnp.sum(grad_pre.astype(jnp.float32), axis=0)
        grad_inner = grad_inner + jnp.einsum(
            "td,tf->df", normed.astype(jnp.bfloat16), grad_pre, preferred_element_type=jnp.float32
        )
        grad_normed = grad_summed + jnp.einsum(
            "tf,df->td", grad_pre, inner_w, preferred_element_type=jnp.float32
        )
        grad_resid, grad_g1, grad_s1 = norm_one_back(grad_normed)
        grad_gain_one = grad_gain_one + grad_g1
        grad_shift_one = grad_shift_one + grad_s1
        grad_proj = grad_resid.astype(jnp.bfloat16)
        grad_bias_o = grad_bias_o + jnp.sum(grad_proj.astype(jnp.float32), axis=0)
        grad_attn_out = grad_attn_out + jnp.einsum(
            "td,te->de", mixed, grad_proj, preferred_element_type=jnp.float32
        )
        mix_grads.append(
            jnp.einsum(
                "te,de->td", grad_proj, attn_w[3], preferred_element_type=jnp.float32
            ).astype(jnp.bfloat16)
        )
        residual_grads.append(grad_resid)
    grad_query_c, grad_query_q, grad_keys, grad_values, grad_table = lax.map(
        partial(attend_back, onehot, table_low),
        (
            to_heads(query_c),
            to_heads(query_q),
            to_heads(key_rows),
            to_heads(value_rows),
            lengths,
            flag_rows,
            lse_c,
            lse_q,
            to_heads(mix_grads[0]),
            to_heads(mix_grads[1]),
        ),
    )
    grad_table = jnp.sum(grad_table, axis=0)
    low_query_c = grad_query_c.reshape(-1, D).astype(jnp.bfloat16)
    low_query_q = grad_query_q.reshape(-1, D).astype(jnp.bfloat16)
    low_keys = grad_keys.reshape(-1, D).astype(jnp.bfloat16)
    low_values = grad_values.reshape(-1, D).astype(jnp.bfloat16)
    low_c = hidden_c.astype(jnp.bfloat16)
    low_q = hidden_q.astype(jnp.bfloat16)
    stacked_grads = jnp.stack([low_query_c, low_keys, low_values])
    grad_qkv = jnp.einsum("td,ste->sde", low_c, stacked_grads, preferred_element_type=jnp.float32)
    grad_wq = grad_qkv[0] + jnp.einsum(
        "td,te->de", low_q, low_query_q, preferred_element_type=jnp.float32
    )
    grad_attn = jnp.stack([grad_wq, grad_qkv[1], grad_qkv[2], grad_attn_out])
    grad_bias_q = jnp.sum(low_query_c.astype(jnp.float32), axis=0) + jnp.sum(
        low_query_q.astype(jnp.float32), axis=0
    )
    grad_bias_v = jnp.sum(low_values.astype(jnp.float32), axis=0)
    grad_content = residual_grads[0] + jnp.einsum(
        "ste,sde->td", stacked_grads, attn_w[:3], preferred_element_type=jnp.float32
    )
    grad_query_in = residual_grads[1] + jnp.einsum(
        "te,de->td", low_query_q, attn_w[0], preferred_element_type=jnp.float32
    )
    grad_small = jnp.concatenate(
        [
            grad_bias_q,
            grad_bias_v,
            grad_bias_o,
            grad_gain_one,
            grad_shift_one,
            grad_bias_two,
            grad_gain_two,
            grad_shift_two,
            grad_hidden_bias,
            grad_table.reshape(-1),
        ]
    )
    return (grad_content, grad_query_in, (grad_attn, grad_inner, grad_outer, grad_small))


def adam_update(master, first, second, grad, rate):
    first_new = BETA_ONE * first + (1.0 - BETA_ONE) * grad
    second_new = BETA_TWO * second + (1.0 - BETA_TWO) * grad * grad
    first_hat = first_new / (1.0 - BETA_ONE**STEP)
    second_hat = second_new / (1.0 - BETA_TWO**STEP)
    master_new = master - rate * (
        first_hat / (jnp.sqrt(second_hat) + ADAM_EPS) + WEIGHT_DECAY * master
    )
    return (master_new, first_new, second_new)


def per_device(
    content,
    query,
    lengths,
    predicted,
    content_cot,
    query_cot,
    attn_master,
    attn_first,
    attn_second,
    inner_master,
    inner_first,
    inner_second,
    outer_master,
    outer_first,
    outer_second,
    small_master,
    small_first,
    small_second,
):
    masters = (attn_master, inner_master, outer_master, small_master)
    slot_count = lengths.shape[0]
    flag_rows = predicted.reshape(slot_count, LEN)
    onehot = bucket_onehot()
    hidden_c = content.astype(jnp.float32)
    hidden_q = query.astype(jnp.float32)
    kept_weights = []
    saved_layers = []
    small_all = lax.all_gather(
        small_master.astype(jnp.bfloat16), "fsdp", axis=1, tiled=True
    )
    for layer_index in range(LAYERS):
        shards = tuple((master[layer_index] for master in masters[:3]))
        gathered = fetch_forward(shards) + (small_all[layer_index],)
        kept_weights.append(gathered)
        hidden_c, hidden_q, saved = forward_layer(
            hidden_c, hidden_q, gathered, lengths, flag_rows, onehot
        )
        saved_layers.append(saved)
    position = jnp.arange(LEN, dtype=jnp.int32)
    valid_rows = (position[None, :] < lengths[:, None]).reshape(-1, 1).astype(jnp.float32)
    grad_c = content_cot.astype(jnp.float32) * valid_rows
    grad_q = query_cot.astype(jnp.float32) * valid_rows
    layer_grads = [None] * LAYERS
    small_grads = [None] * LAYERS
    for layer_index in reversed(range(LAYERS)):
        grad_c, grad_q, local_grads = backward_layer(
            saved_layers[layer_index],
            kept_weights[layer_index],
            grad_c,
            grad_q,
            lengths,
            flag_rows,
            onehot,
        )
        small_grads[layer_index] = local_grads[3]
        layer_grads[layer_index] = reduce_layer(local_grads[:3])
    small_sum = lax.psum(jnp.stack(small_grads), ("dp", "fsdp"))
    owned = small_master.shape[1]
    small_own = lax.dynamic_slice_in_dim(
        small_sum, lax.axis_index("fsdp") * owned, owned, 1
    )
    reduced = tuple(
        (
            jnp.stack([layer_grads[layer_index][member] for layer_index in range(LAYERS)])
            for member in range(3)
        )
    ) + (small_own,)
    attn_new = adam_update(attn_master, attn_first, attn_second, reduced[0], ATTENTION_RATE)
    inner_new = adam_update(inner_master, inner_first, inner_second, reduced[1], FEED_RATE)
    outer_new = adam_update(outer_master, outer_first, outer_second, reduced[2], FEED_RATE)
    small_new = adam_update(small_master, small_first, small_second, reduced[3], SMALL_RATE)
    return (
        hidden_c.astype(jnp.bfloat16),
        hidden_q.astype(jnp.bfloat16),
        grad_c,
        grad_q,
        attn_new[0],
        attn_new[1],
        attn_new[2],
        inner_new[0],
        inner_new[1],
        inner_new[2],
        outer_new[0],
        outer_new[1],
        outer_new[2],
        small_new[0],
        small_new[1],
        small_new[2],
    )


def quarter_of(kind, shard, quarter):
    if kind == "attn":
        return lax.dynamic_index_in_dim(shard, quarter, 0, keepdims=False)
    if kind == "inner":
        return lax.dynamic_slice_in_dim(shard, quarter * D, D, 1)
    return lax.dynamic_slice_in_dim(shard, quarter * ROWS, ROWS, 0)


def after(value, *others):
    return lax.optimization_barrier((value, others))[0]


def join(*values):
    return lax.optimization_barrier(values)


def own_blocks(kinds, shards, place, side):
    quarter = (place[0] ^ side) * 2 + place[1]
    return jnp.stack(
        [
            quarter_of(kind, shard, quarter).astype(jnp.bfloat16)
            for kind, shard in zip(kinds, shards)
        ]
    )


def gather_group(count, shards, plane, column, sides, corners, mine, theirs):
    plan = []
    for core, arrays in enumerate((mine, theirs)):
        base = core * len(mine)
        for member in range(count):
            array, first = plane
            plan += [
                (base + array, first + side * count + member, side, 1, core, 0, member)
                for side in range(2)
            ]
            for apart in (1, 2, 3):
                index = (apart - 1) * count + member
                array, first = column
                plan.append((base + array, first + index, 0, 0, core, apart, member))
                for dx, dy, (array, first) in ((1, 0, sides[0]), (0, 1, sides[1])):
                    plan.append((base + array, first + index, dx, dy, core, apart, member))
                skipped = 0
                for array, first, held in corners:
                    if skipped <= index < skipped + held:
                        plan.append(
                            (base + array, first + index - skipped, 1, 1, core, apart, member)
                        )
                    skipped += held
    return (tuple(plan), tuple(shards) + tuple(mine) + tuple(theirs))


def gather_small(shard, place):
    z, y = place[2], place[3]
    pair = jnp.stack([shard, swap_z(shard, 1)])
    blocks = jnp.concatenate([pair, swap_z(pair, 2)])
    low, high = z % 2, z // 2
    blocks = jnp.where(low == 0, blocks, blocks[jnp.array([1, 0, 3, 2])])
    blocks = jnp.where(high == 0, blocks, blocks[jnp.array([2, 3, 0, 1])])
    other = swap_y(blocks)
    pairs = jnp.where(y == 0, jnp.stack([blocks, other], 1), jnp.stack([other, blocks], 1))
    return pairs.transpose(2, 0, 1, 3).reshape(shard.shape[0], -1)


def add_low(*values):
    total = values[0].astype(jnp.float32)
    for value in values[1:]:
        total = total + value.astype(jnp.float32)
    return total.astype(jnp.bfloat16)


def reduce_corners(keep, get):
    corner = add_low(keep[1, 1], get[1, 1])
    return (swap_x(corner[:2]), swap_y(corner[2:]))


def reduce_sides(keep, get, corners):
    by_x, by_y = corners
    for_y = jnp.concatenate([add_low(keep[1, 0, :2], get[1, 0, :2], by_x), add_low(keep[1, 0, 2:], get[1, 0, 2:])])
    for_x = jnp.concatenate([add_low(keep[0, 1, :2], get[0, 1, :2]), add_low(keep[0, 1, 2:], get[0, 1, 2:], by_y)])
    return (swap_x(for_x), swap_y(for_y))


def reduce_column(keep, get, sides):
    return add_low(keep[0, 0], get[0, 0], *sides)


def at_z(column, place, apart):
    return lax.dynamic_index_in_dim(column, place[2] ^ apart, 0, keepdims=False)


def reduce_far(column, place):
    return swap_z(jnp.stack([at_z(column, place, 2), at_z(column, place, 3)]), 2)


def reduce_near(column, far, place):
    return swap_z(add_low(at_z(column, place, 1), far[1]), 1)


def reduce_total(column, far, near, place):
    return add_low(at_z(column, place, 0), far[0], near)


def reduce_direct(column, place):
    return tuple(swap_z(at_z(column, place, apart), apart) for apart in (1, 2, 3))


def direct_total(column, shifts, place):
    return add_low(at_z(column, place, 0), *shifts)


def share_core(pair, place):
    x, c = place[0], place[1]
    other = swap_core(pair)
    cores = jnp.where(c == 0, jnp.stack([pair, other], 1), jnp.stack([other, pair], 1))
    sides = jnp.where(x == 0, cores, cores[::-1])
    return sides.reshape((4,) + pair.shape[1:])


def small_parts(vectors):
    values = vectors.astype(jnp.float32)
    return (
        values[: 8 * D].reshape(8, D),
        values[8 * D : 8 * D + FF].reshape(1, FF),
        bias_vectors(values[8 * D + FF :].reshape(H, NB)),
    )


def per_device_fast(
    content,
    query,
    lengths,
    predicted,
    content_cot,
    query_cot,
    attn_master,
    attn_first,
    attn_second,
    inner_master,
    inner_first,
    inner_second,
    outer_master,
    outer_first,
    outer_second,
    small_master,
    small_first,
    small_second,
):
    place_parts = my_place()
    place = jnp.stack(place_parts).astype(jnp.int32)
    attn_kinds, feed_kinds = ("attn",), ("inner", "outer")
    attn_shards = [(attn_master[layer],) for layer in range(LAYERS)]
    feed_shards = [(inner_master[layer], outer_master[layer]) for layer in range(LAYERS)]
    own_a0 = own_blocks(attn_kinds, attn_shards[0], place_parts, 0)
    oth_a0 = own_blocks(attn_kinds, attn_shards[0], place_parts, 1)
    own_f0 = own_blocks(feed_kinds, feed_shards[0], place_parts, 0)
    z_a0 = tuple(swap_z(own_a0, apart) for apart in (1, 2, 3))
    plane_a0 = swap_y(jnp.concatenate([own_a0, oth_a0]))
    near_f0 = swap_z(own_f0, 1)
    z_a0, plane_a0, near_f0 = join(z_a0, plane_a0, near_f0)
    oth_f0 = own_blocks(feed_kinds, feed_shards[0], place_parts, 1)
    own_a1 = own_blocks(attn_kinds, attn_shards[1], place_parts, 0)
    oth_a1 = own_blocks(attn_kinds, attn_shards[1], place_parts, 1)
    own_f1 = own_blocks(feed_kinds, feed_shards[1], place_parts, 0)
    oth_f1 = own_blocks(feed_kinds, feed_shards[1], place_parts, 1)
    attn_low = [tuple(w.astype(jnp.bfloat16) for w in shards) for shards in attn_shards]
    feed_low = [tuple(w.astype(jnp.bfloat16) for w in shards) for shards in feed_shards]
    col_a0 = jnp.concatenate(z_a0)
    x0 = swap_x(col_a0)
    y0 = swap_y(col_a0)
    far_f0 = swap_z(jnp.concatenate([own_f0, near_f0]), 2)
    plane_f0 = swap_y(after(jnp.concatenate([own_f0, oth_f0]), z_a0))
    near_1 = swap_z(after(jnp.concatenate([own_a1, own_f1]), z_a0), 1)
    x0, y0, far_f0, plane_f0, near_1 = join(x0, y0, far_f0, plane_f0, near_1)
    col_f0 = jnp.concatenate([near_f0, far_f0])
    x1 = swap_x(jnp.concatenate([col_f0, y0[:2]]))
    y1 = swap_y(jnp.concatenate([col_f0, x0[2:]]))
    far_a1 = swap_z(jnp.concatenate([own_a1, near_1[:1]]), 2)
    mine_0 = jnp.concatenate([plane_a0, col_a0, x0, y0])
    theirs_0 = swap_core(mine_0)
    small_all = gather_small(after(small_master.astype(jnp.bfloat16), far_f0), place_parts)
    x1, y1, far_a1, theirs_0, small_all = join(x1, y1, far_a1, theirs_0, small_all)
    col_a1 = jnp.concatenate([near_1[:1], far_a1])
    x2 = swap_x(jnp.concatenate([col_a1, y1[:4]]))
    y2 = swap_y(jnp.concatenate([col_a1, x1[4:6], own_a1, oth_a1]))
    far_f1 = swap_z(jnp.concatenate([own_f1, after(near_1[1:], far_a1)]), 2)
    mine_1 = jnp.concatenate([x1, y1])
    theirs_1 = swap_core(mine_1)
    mine_p0 = jnp.concatenate([plane_f0, col_f0])
    theirs_p0 = swap_core(after(mine_p0, theirs_1))
    group_a0 = gather_group(
        1, attn_low[0], (0, 0), (0, 2), ((0, 5), (0, 8)), ((1, 6, 2), (1, 14, 1)),
        (mine_0, mine_1), (theirs_0, theirs_1),
    )
    row_flags = predicted.reshape(1, LEN).astype(jnp.float32)
    col_flags = predicted.reshape(LEN, 1).astype(jnp.float32)
    low0 = jnp.concatenate([content, query])
    small0, hidden_bias0, (tvec0, far0, onehot) = small_parts(small_all[0])
    small1, hidden_bias1, (tvec1, far1, onehot) = small_parts(small_all[1])
    q0, k0, v0, attn0 = project(place, low0, small0, group_a0)
    mixed0, p0, inverse0, dead = mix(lengths, far0, tvec0, q0, k0, v0, row_flags, col_flags)
    x2, y2, far_f1, mixed0, theirs_p0 = join(x2, y2, far_f1, mixed0, theirs_p0)
    col_f1 = jnp.concatenate([near_1[1:], far_f1])
    x3 = swap_x(jnp.concatenate([col_f1, y2[:3]]))
    y3 = swap_y(jnp.concatenate([col_f1, own_f1, oth_f1]))
    mine_2 = jnp.concatenate([x2, y2, col_a1])
    theirs_2 = swap_core(mine_2)
    group_f0 = gather_group(
        2, feed_low[0], (0, 0), (0, 4), ((1, 0), (1, 8)), ((2, 3, 4), (2, 10, 2)),
        (mine_p0, mine_1, mine_2), (theirs_p0, theirs_1, theirs_2),
    )
    resid0, pre0, normed0, low1, summed0 = feed(
        place, small0, hidden_bias0, mixed0, low0, attn0, group_f0
    )
    x3, y3, low1 = join(x3, y3, low1)
    x4 = swap_x(y3[:3])
    y4 = swap_y(x3[3:6])
    mine_3 = jnp.concatenate([x3, y3])
    theirs_3 = swap_core(mine_3)
    group_a1 = gather_group(
        1, attn_low[1], (0, 12), (0, 14), ((0, 0), (0, 7)), ((1, 6, 3),),
        (mine_2, mine_3), (theirs_2, theirs_3),
    )
    q1, k1, v1, attn1 = project(place, low1, small1, group_a1)
    x4, y4, q1 = join(x4, y4, q1)
    mine_4 = jnp.concatenate([col_f1, x4, y4])
    theirs_4 = swap_core(mine_4)
    group_f1 = gather_group(
        2, feed_low[1], (0, 15), (1, 0), ((0, 0), (0, 9)), ((1, 6, 3), (1, 9, 3)),
        (mine_3, mine_4), (theirs_3, theirs_4),
    )
    mixed1, p1, inverse1, dead = mix(
        lengths, far1, tvec1, q1, k1, v1, row_flags, col_flags
    )
    content_out, query_out, dresid1, dmix1, dwo1, keep_f1, send_f1, vec_f1, dhidden1 = turn(
        place, lengths, small1, small0, hidden_bias1, mixed1, summed0, attn1,
        (content_cot, query_cot), group_f1
    )
    get_f1 = swap_core(send_f1)
    *first1, table1_a = mix_back(0, q1, k1, v1, dmix1, mixed1, p1, inverse1, dead)
    by_f1 = reduce_corners(keep_f1, after(get_f1, table1_a))
    dq1, dk1, dv1, table1_b = mix_back(
        3, after(q1, get_f1, table1_a), k1, v1, dmix1, mixed1, p1, inverse1, dead, tuple(first1)
    )
    sides_rf1 = reduce_sides(keep_f1, get_f1, after(by_f1, table1_b))
    keep_a1, send_a1, vec_a1 = weight_back(place, after(low1, by_f1), dq1, dk1, dv1, dwo1)
    get_a1 = swap_core(send_a1)
    by_a1 = reduce_corners(keep_a1, get_a1)
    dresid0, dmix0, dwo0, keep_f0, send_f0, vec_f0, dhidden0 = down(
        place, small0, dq1, dk1, dv1, after(attn1, get_a1), dresid1, summed0, normed0, resid0,
        pre0, mixed0, attn0, group_f0
    )
    get_f0 = swap_core(after(send_f0, sides_rf1, by_a1))
    sides_ra1 = reduce_sides(keep_a1, get_a1, after(by_a1, dmix0))
    column_f1 = reduce_column(keep_f1, get_f1, after(sides_rf1, dmix0))
    zfar_f1 = reduce_far(column_f1, place_parts)
    *first0, table0_a = mix_back(
        0, after(q0, by_a1, sides_rf1), k0, v0, dmix0, mixed0, p0, inverse0, dead
    )
    by_f0 = reduce_corners(keep_f0, after(get_f0, table0_a))
    zfar_f1 = after(zfar_f1, table0_a)
    znear_f1 = reduce_near(column_f1, zfar_f1, place_parts)
    dq0, dk0, dv0, table0_b = mix_back(
        3, after(q0, get_f0, zfar_f1), k0, v0, dmix0, mixed0, p0, inverse0, dead, tuple(first0)
    )
    by_f0, sides_ra1, znear_f1, table0_b = join(by_f0, sides_ra1, znear_f1, table0_b)
    sides_rf0 = reduce_sides(keep_f0, get_f0, by_f0)
    keep_a0, send_a0, vec_a0 = weight_back(place, after(low0, table0_b), dq0, dk0, dv0, dwo0)
    get_a0 = swap_core(send_a0)
    column_a1 = reduce_column(keep_a1, get_a1, sides_ra1)
    zfar_a1 = reduce_far(column_a1, place_parts)
    sides_rf0, get_a0, zfar_a1, vec_a0 = join(sides_rf0, get_a0, zfar_a1, vec_a0)
    column_f0 = reduce_column(keep_f0, get_f0, sides_rf0)
    zfar_f0 = reduce_far(column_f0, place_parts)
    by_a0 = reduce_corners(keep_a0, get_a0)
    own_f1 = reduce_total(column_f1, zfar_f1, znear_f1, place_parts)
    pair_f1 = jnp.stack([own_f1, swap_x(own_f1)])
    content_grad, query_grad = input_back(after(dq0, sides_rf0), dk0, dv0, attn0, dresid0)
    small_sum = jnp.concatenate(
        [
            jnp.stack([vec_a0, vec_a1]).reshape(LAYERS, -1),
            jnp.stack([vec_f0, vec_f1]).reshape(LAYERS, -1),
            jnp.stack([dhidden0, dhidden1]).reshape(LAYERS, -1),
            table_grad(
                jnp.concatenate([table0_a, table0_b, table1_a, table1_b]), onehot
            ).reshape(LAYERS, -1),
        ],
        axis=1,
    )
    small_sum = small_sum + swap_core(small_sum)
    by_a0, pair_f1, content_grad, small_sum = join(by_a0, pair_f1, content_grad, small_sum)
    sides_ra0 = reduce_sides(keep_a0, get_a0, by_a0)
    znear_a1 = reduce_near(column_a1, zfar_a1, place_parts)
    four_f1 = share_core(pair_f1, place_parts)
    attn_state = (attn_master, attn_first, attn_second)
    inner_state = (inner_master, inner_first, inner_second)
    outer_state = (outer_master, outer_first, outer_second)
    inner_new = adam("inner", 1, FEED_RATE, inner_state, four_f1, 0, None)
    outer_new = adam("outer", 1, FEED_RATE, outer_state, four_f1, 1, None)
    sides_ra0, zfar_f0, znear_a1, inner_new, outer_new = join(
        sides_ra0, zfar_f0, znear_a1, inner_new, outer_new
    )
    column_a0 = reduce_column(keep_a0, get_a0, sides_ra0)
    shifts_a0 = reduce_direct(column_a0, place_parts)
    znear_f0 = reduce_near(column_f0, zfar_f0, place_parts)
    own_a1 = reduce_total(column_a1, zfar_a1, znear_a1, place_parts)
    pair_a1 = jnp.stack([own_a1, swap_x(after(own_a1, column_a0))])
    shifts_a0, znear_f0, pair_a1 = join(shifts_a0, znear_f0, pair_a1)
    own_0 = jnp.concatenate(
        [
            reduce_total(column_f0, zfar_f0, znear_f0, place_parts),
            direct_total(column_a0, shifts_a0, place_parts),
        ]
    )
    pair_0 = jnp.stack([own_0, swap_x(own_0)])
    four_a1 = share_core(pair_a1, place_parts)
    small_sum = small_sum + swap_y(small_sum)
    attn_new = adam("attn", 1, ATTENTION_RATE, attn_state, four_a1, 0, None)
    pair_0, attn_new, small_sum = join(pair_0, attn_new, small_sum)
    four_0 = share_core(pair_0, place_parts)
    small_sum = small_sum + swap_x(small_sum)
    four_0, small_sum = join(four_0, small_sum)
    small_far = swap_z(small_sum, 1)
    inner_new = adam("inner", 0, FEED_RATE, inner_state, four_0, 0, tuple(inner_new))
    small_sum = small_sum + small_far
    outer_new = adam("outer", 0, FEED_RATE, outer_state, four_0, 1, tuple(outer_new))
    small_sum = small_sum + swap_z(small_sum, 2)
    attn_new = adam("attn", 0, ATTENTION_RATE, attn_state, four_0, 2, tuple(attn_new))
    size = small_master.shape[1]
    small_own = lax.dynamic_slice_in_dim(small_sum, lax.axis_index("fsdp") * size, size, 1)
    small_new = adam_update(small_master, small_first, small_second, small_own, SMALL_RATE)
    return (
        (content_out, query_out, content_grad, query_grad)
        + tuple(attn_new)
        + tuple(inner_new)
        + tuple(outer_new)
        + small_new
    )


def solution(mesh):
    placed = (
        P(("dp", "fsdp"), None),
        P(("dp", "fsdp"), None),
        P(("dp", "fsdp")),
        P(("dp", "fsdp")),
        P(("dp", "fsdp"), None),
        P(("dp", "fsdp"), None),
        P(None, None, "fsdp", None),
        P(None, None, "fsdp", None),
        P(None, None, "fsdp", None),
        P(None, "fsdp", None),
        P(None, "fsdp", None),
        P(None, "fsdp", None),
        P(None, "fsdp", None),
        P(None, "fsdp", None),
        P(None, "fsdp", None),
        P(None, "fsdp"),
        P(None, "fsdp"),
        P(None, "fsdp"),
    )
    fast = tuple(mesh.shape.values()) == (4, 8)
    return jax.shard_map(
        per_device_fast if fast else per_device,
        mesh=mesh,
        in_specs=placed,
        out_specs=(
            P(("dp", "fsdp"), None),
            P(("dp", "fsdp"), None),
            P(("dp", "fsdp"), None),
            P(("dp", "fsdp"), None),
            P(None, None, "fsdp", None),
            P(None, None, "fsdp", None),
            P(None, None, "fsdp", None),
            P(None, "fsdp", None),
            P(None, "fsdp", None),
            P(None, "fsdp", None),
            P(None, "fsdp", None),
            P(None, "fsdp", None),
            P(None, "fsdp", None),
            P(None, "fsdp"),
            P(None, "fsdp"),
            P(None, "fsdp"),
        ),
        check_vma=False,
    )
```

```python
from functools import partial

import jax
import jax.numpy as jnp
from jax import lax
from jax.experimental import pallas as pl
from jax.experimental.pallas import tpu as pltpu
from jax.sharding import PartitionSpec as P

D = 768
H = 12
DH = 64
FF = 3072
LEN = 512
NB = 32
LAYERS = 2
STEP = 10


NORM_EPS = 1e-05
MASKED = -1000000000.0
BETA_ONE = 0.9
BETA_TWO = 0.999
ATTENTION_RATE = 0.1
FEED_RATE = 0.02
SMALL_RATE = 0.4
WEIGHT_DECAY = 0.01
ADAM_EPS = 1e-08
SCORE_SCALE = 0.125


def layer_norm(values, gain, shift):
    centre = values - jnp.mean(values, axis=-1, keepdims=True)
    spread = jnp.mean(centre * centre, axis=-1, keepdims=True)
    return centre * lax.rsqrt(spread + NORM_EPS) * gain + shift


def unpack(vectors):
    pieces = [vectors[piece_index * D : (piece_index + 1) * D] for piece_index in range(8)]
    hidden_bias = vectors[8 * D : 8 * D + FF]
    bias_table = vectors[8 * D + FF :].reshape(H, NB)
    return (pieces, hidden_bias, bias_table)


def bucket_ids():
    position = jnp.arange(LEN, dtype=jnp.int32)
    offset = position[None, :] - position[:, None]
    distance = jnp.abs(offset)
    far_bucket = jnp.full(distance.shape, 8, jnp.int32)
    for exponent in range(1, 8):
        far_bucket = far_bucket + (distance * distance >= 64 * 2**exponent).astype(jnp.int32)
    near_or_far = jnp.where(distance < 8, distance, far_bucket)
    return near_or_far + NB // 2 * (offset > 0).astype(jnp.int32)


def bucket_onehot():
    return (bucket_ids()[:, :, None] == jnp.arange(NB, dtype=jnp.int32)[None, None, :]).astype(
        jnp.bfloat16
    )


def allowed_pairs(length, pred_flags):
    position = jnp.arange(LEN, dtype=jnp.int32)
    valid_key = (position < length)[None, :]
    row_pos = position[:, None]
    col_pos = position[None, :]
    free_key = (pred_flags == 0)[None, :]
    content_ok = valid_key & (free_key | (pred_flags[:, None] == 1) & (col_pos <= row_pos))
    query_ok = valid_key & (col_pos != row_pos) & (free_key | (col_pos < row_pos))
    return (content_ok, query_ok)


def masked_scores(query_rows, key_rows, position_bias, allowed):
    scores = (
        jnp.einsum("qhd,khd->hqk", query_rows, key_rows, preferred_element_type=jnp.float32)
        * SCORE_SCALE
        + position_bias
    )
    return jnp.where(allowed[None], scores, MASKED)


def table_bias(onehot, table_low):
    return jnp.einsum("qkb,hb->hqk", onehot, table_low, preferred_element_type=jnp.float32)


def attend_slot(onehot, table_low, slot_item):
    query_c, query_q, key_rows, value_rows, length, pred_flags = slot_item
    position_bias = table_bias(onehot, table_low)
    content_ok, query_ok = allowed_pairs(length, pred_flags)
    results = []
    for query_rows, allowed in ((query_c, content_ok), (query_q, query_ok)):
        scores = masked_scores(query_rows, key_rows, position_bias, allowed)
        peak = jnp.max(scores, axis=-1, keepdims=True)
        expos = jnp.exp(scores - peak)
        totals = jnp.sum(expos, axis=-1, keepdims=True)
        probs = (expos / totals).astype(jnp.bfloat16)
        mixed = jnp.einsum(
            "hqk,khd->qhd", probs, value_rows, preferred_element_type=jnp.float32
        ).astype(jnp.bfloat16)
        results.append((mixed, peak[..., 0] + jnp.log(totals[..., 0])))
    return (results[0][0], results[1][0], results[0][1], results[1][1])


def attend_back(onehot, table_low, slot_item):
    (
        query_c,
        query_q,
        key_rows,
        value_rows,
        length,
        pred_flags,
        lse_c,
        lse_q,
        grad_mix_c,
        grad_mix_q,
    ) = slot_item
    position_bias = table_bias(onehot, table_low)
    content_ok, query_ok = allowed_pairs(length, pred_flags)
    grad_keys = jnp.zeros(key_rows.shape, jnp.float32)
    grad_values = jnp.zeros(value_rows.shape, jnp.float32)
    grad_table = jnp.zeros((H, NB), jnp.float32)
    grads_query = []
    for query_rows, allowed, log_total, grad_mix in (
        (query_c, content_ok, lse_c, grad_mix_c),
        (query_q, query_ok, lse_q, grad_mix_q),
    ):
        scores = masked_scores(query_rows, key_rows, position_bias, allowed)
        probs = jnp.exp(scores - log_total[..., None])
        grad_values = grad_values + jnp.einsum(
            "hqk,qhd->khd", probs.astype(jnp.bfloat16), grad_mix, preferred_element_type=jnp.float32
        )
        grad_probs = jnp.einsum(
            "qhd,khd->hqk", grad_mix, value_rows, preferred_element_type=jnp.float32
        )
        grad_scores = probs * (grad_probs - jnp.sum(probs * grad_probs, axis=-1, keepdims=True))
        grad_scores = jnp.where(allowed[None], grad_scores, 0.0).astype(jnp.bfloat16)
        grad_table = grad_table + jnp.einsum(
            "hqk,qkb->hb", grad_scores, onehot, preferred_element_type=jnp.float32
        )
        grads_query.append(
            jnp.einsum("hqk,khd->qhd", grad_scores, key_rows, preferred_element_type=jnp.float32)
            * SCORE_SCALE
        )
        grad_keys = (
            grad_keys
            + jnp.einsum(
                "hqk,qhd->khd", grad_scores, query_rows, preferred_element_type=jnp.float32
            )
            * SCORE_SCALE
        )
    return (grads_query[0], grads_query[1], grad_keys, grad_values, grad_table)


def to_heads(values):
    return values.reshape(-1, LEN, H, DH)


AXES = ("dp", "fsdp")
GRID = (2, 2, 4, 2)
ROWS = 96


def places():
    return [
        (x, c, z, y) for x in range(2) for c in range(2) for z in range(4) for y in range(2)
    ]


def flat(x, c, z, y):
    return ((x * 2 + c) * 4 + z) * 2 + y


def move(value, shift):
    pairs = [(flat(*place), flat(*shift(*place))) for place in places()]
    return lax.ppermute(value, AXES, pairs)


def swap_core(value):
    return move(value, lambda x, c, z, y: (x, 1 - c, z, y))


def swap_x(value):
    return move(value, lambda x, c, z, y: (1 - x, c, z, y))


def swap_y(value):
    return move(value, lambda x, c, z, y: (x, c, z, 1 - y))


def swap_z(value, apart):
    return move(value, lambda x, c, z, y: (x, c, z ^ apart, y))


def my_place():
    dp = lax.axis_index("dp")
    fsdp = lax.axis_index("fsdp")
    return (dp // 2, dp % 2, fsdp // 2, fsdp % 2)


def dot_nn(left, right):
    return jnp.dot(left, right, preferred_element_type=jnp.float32)


def dot_nt(left, right):
    return lax.dot_general(
        left, right, (((1,), (1,)), ((), ())), preferred_element_type=jnp.float32
    )


def dot_tn(left, right):
    return lax.dot_general(
        left, right, (((0,), (0,)), ((), ())), preferred_element_type=jnp.float32
    )


ANY_SPEC = pl.BlockSpec(memory_space=pl.ANY)
VMEM_SPEC = pl.BlockSpec(memory_space=pltpu.VMEM)
SMEM_SPEC = pl.BlockSpec(memory_space=pltpu.SMEM)
TALL = 2 * LEN
HALF = 256
PARAMS = pltpu.CompilerParams(vmem_limit_bytes=60 * 1024 * 1024)


def norm_parts(values):
    centre = values - jnp.mean(values, axis=-1, keepdims=True)
    spread = jnp.mean(centre * centre, axis=-1, keepdims=True)
    scale = lax.rsqrt(spread + NORM_EPS)
    return (centre * scale, scale)


def norm_back(unit, scale, grad, gain):
    scaled = grad * gain
    return scale * (
        scaled
        - jnp.mean(scaled, axis=-1, keepdims=True)
        - unit * jnp.mean(scaled * unit, axis=-1, keepdims=True)
    )


def start_fetch(kinds, plan, place_ref, refs, targets, sems):
    x, c, z, y = (place_ref[index] for index in range(4))
    mine = z * 2 + y
    copies = []

    def start(source, target):
        copy = pltpu.make_async_copy(source, target, sems.at[len(copies)])
        copy.start()
        copies.append(copy)

    for member, kind in enumerate(kinds):
        target = targets[member]
        if kind == "attn":
            start(refs[member], target.at[:, pl.ds(pl.multiple_of(mine * ROWS, ROWS), ROWS), :])
        elif kind == "inner":
            for quarter in range(4):
                start(
                    refs[member].at[:, quarter * D : quarter * D + D],
                    target.at[quarter, pl.ds(pl.multiple_of(mine * ROWS, ROWS), ROWS), :],
                )
        else:
            start(refs[member], target.at[z, pl.ds(pl.multiple_of(y * 384, ROWS), 384), :])
    for array, index, dx, dy, dc, dz, member in plan:
        quarter = (x ^ dx) * 2 + (c ^ dc)
        if kinds[member] == "outer":
            lead, row = z ^ dz, (y ^ dy) * 384 + quarter * ROWS
        else:
            lead, row = quarter, ((z ^ dz) * 2 + (y ^ dy)) * ROWS
        start(
            refs[len(kinds) + array].at[index],
            targets[member].at[lead, pl.ds(pl.multiple_of(row, ROWS), ROWS), :],
        )
    return copies


def project_kernel(plan, place_ref, small_ref, low_any, *refs):
    pieces = refs[:-14]
    (
        q_out, k_out, v_out, w_out, low_ref, q_ref, k_ref, v_ref, w_ref,
        sems, load_sem, keep_sem, store_sems, unused,
    ) = refs[-14:]
    load = pltpu.make_async_copy(low_any, low_ref, load_sem)
    load.start()
    fetches = start_fetch(("attn",), plan, place_ref, pieces, (w_ref,), sems)
    load.wait()
    for copy in fetches:
        copy.wait()
    keep = pltpu.make_async_copy(w_ref, w_out, keep_sem)
    keep.start()
    bias_q = small_ref[0:1, :]
    bias_v = small_ref[1:2, :]
    stores = []

    def store(source, target):
        copy = pltpu.make_async_copy(source, target, store_sems.at[len(stores)])
        copy.start()
        stores.append(copy)

    for row in range(0, TALL, HALF):
        span = slice(row, row + HALF)
        rows = low_ref[span, :]
        q_ref[span, :] = (dot_nn(rows, w_ref[0]) + bias_q).astype(jnp.bfloat16)
        if row < LEN:
            k_ref[span, :] = dot_nn(rows, w_ref[1]).astype(jnp.bfloat16)
            v_ref[span, :] = (dot_nn(rows, w_ref[2]) + bias_v).astype(jnp.bfloat16)
        if row == LEN - HALF:
            store(k_ref, k_out)
            store(v_ref, v_out)
            store(q_ref.at[:LEN, :], q_out.at[:LEN, :])
    store(q_ref.at[LEN:, :], q_out.at[LEN:, :])
    for copy in stores:
        copy.wait()
    keep.wait()


def project(place, low, small, group):
    plan, pieces = group
    return pl.pallas_call(
        partial(project_kernel, plan),
        out_shape=[
            jax.ShapeDtypeStruct((TALL, D), jnp.bfloat16),
            jax.ShapeDtypeStruct((LEN, D), jnp.bfloat16),
            jax.ShapeDtypeStruct((LEN, D), jnp.bfloat16),
            jax.ShapeDtypeStruct((4, D, D), jnp.bfloat16),
        ],
        in_specs=[SMEM_SPEC, VMEM_SPEC, ANY_SPEC] + [ANY_SPEC] * len(pieces),
        out_specs=[ANY_SPEC] * 4,
        scratch_shapes=[
            pltpu.VMEM((TALL, D), jnp.bfloat16),
            pltpu.VMEM((TALL, D), jnp.bfloat16),
            pltpu.VMEM((LEN, D), jnp.bfloat16),
            pltpu.VMEM((LEN, D), jnp.bfloat16),
            pltpu.VMEM((4, D, D), jnp.bfloat16),
            pltpu.SemaphoreType.DMA((32,)),
            pltpu.SemaphoreType.DMA,
            pltpu.SemaphoreType.DMA,
            pltpu.SemaphoreType.DMA((4,)),
            pltpu.SemaphoreType.DMA,
        ],
        compiler_params=PARAMS,
        cost_estimate=pl.CostEstimate(flops=2 * 2048 * D * D, bytes_accessed=16000000, transcendentals=0),
        name="project",
    )(place, small, low, *pieces)


def build_masks(length, row_flags, col_flags, mask_ref, alive_ref):
    flags = row_flags[...]

    def body(step, carry):
        start = pl.multiple_of(step * 64, 64)
        key = lax.broadcasted_iota(jnp.int32, (64, LEN), 0) + start
        query = lax.broadcasted_iota(jnp.int32, (64, LEN), 1)
        valid = key < length
        free = jnp.broadcast_to(col_flags[pl.ds(start, 64), :], (64, LEN)) == 0.0
        marked = jnp.broadcast_to(flags, (64, LEN)) == 1.0
        content_ok = valid & (free | (marked & (key <= query)))
        query_ok = valid & (key != query) & (free | (key < query))
        mask_ref[pl.ds(start, 64), :LEN] = content_ok.astype(jnp.float32)
        mask_ref[pl.ds(start, 64), LEN:] = query_ok.astype(jnp.float32)
        return carry

    lax.fori_loop(0, 8, body, 0)
    alive_ref[...] = jnp.max(mask_ref[...], axis=0, keepdims=True)


def build_tiles(t_row, tile_ref):
    spread = jnp.broadcast_to(t_row, (128, 512))
    rolled = pltpu.roll(spread, 0, 1, stride=1, stride_axis=0)
    tile_ref[...] = rolled[:, :384]


def position_bias(tile_ref, far_ref, head, query_block, key_block):
    apart = query_block - key_block
    if apart >= 2:
        return far_ref[head, 0]
    if apart <= -2:
        return far_ref[head, 1]
    return tile_ref[:, 128 * (apart + 1) : 128 * (apart + 2)]


def head_lanes(shape, head):
    lane = lax.broadcasted_iota(jnp.int32, shape, 1)
    return (lane >= 64) if head else (lane < 64)


def mix_kernel(
    length_ref, far_ref, q_ref, k_ref, v_ref, row_flags, col_flags, t_ref,
    a_ref, p_ref, inverse_ref, dead_ref, mask_ref, alive_ref, tile_ref, o_ref,
):
    pair = pl.program_id(0)

    @pl.when(pair == 0)
    def _():
        build_masks(length_ref[0], row_flags, col_flags, mask_ref, alive_ref)
        dead_ref[...] = (1.0 - alive_ref[...]) * (1.0 / LEN)

    keys = k_ref[...].astype(jnp.float32) * SCORE_SCALE
    values_t = v_ref[...].astype(jnp.float32).T.astype(jnp.bfloat16)
    keys_own = [
        jnp.where(head_lanes(keys.shape, head), keys, 0.0).astype(jnp.bfloat16) for head in range(2)
    ]
    for head in range(2):
        build_tiles(t_ref[head], tile_ref.at[head])
    work = [(head, chunk) for head in range(2) for chunk in range(4)]

    def score(head, chunk):
        return dot_nt(keys_own[head], q_ref[chunk * HALF : chunk * HALF + HALF, :])

    def mixture(head, chunk):
        span = slice(chunk * HALF, chunk * HALF + HALF)
        own = slice(8 + head * 64, 8 + head * 64 + 64)
        mixed = dot_nn(values_t[head * 64 : head * 64 + 64, :], p_ref[head, :, span])
        o_ref[own, span] = mixed * o_ref[head : head + 1, span]

    following = score(*work[0])
    for index, (head, chunk) in enumerate(work):
        scores = following
        if index + 1 < len(work):
            following = score(*work[index + 1])
        at = chunk * HALF
        for side in range(2):
            lanes = slice(at + side * 128, at + side * 128 + 128)
            blocks = []
            peak = None
            for key_block in range(4):
                rows = slice(key_block * 128, key_block * 128 + 128)
                block = scores[rows, side * 128 : side * 128 + 128] + position_bias(
                    tile_ref.at[head], far_ref, pair * 2 + head, (chunk % 2) * 2 + side, key_block
                )
                block = jnp.where(mask_ref[rows, lanes] > 0.0, block, MASKED)
                blocks.append(block)
                high = jnp.max(block, axis=0, keepdims=True)
                peak = high if peak is None else jnp.maximum(peak, high)
            total = None
            for key_block in range(4):
                rows = slice(key_block * 128, key_block * 128 + 128)
                expo = jnp.exp(blocks[key_block] - peak)
                part = jnp.sum(expo, axis=0, keepdims=True)
                total = part if total is None else total + part
                p_ref[head, rows, lanes] = expo.astype(jnp.bfloat16)
            inverse = 1.0 / total
            inverse_ref[head, :, lanes] = inverse * alive_ref[:, lanes]
            o_ref[head : head + 1, lanes] = inverse
        if index:
            mixture(*work[index - 1])
    mixture(*work[-1])
    a_ref[...] = o_ref[8:, :].T.astype(jnp.bfloat16)


def mix(length, far, tvec, q, k, v, row_flags, col_flags):
    tall = pl.BlockSpec((TALL, 128), lambda p: (0, p))
    short = pl.BlockSpec((LEN, 128), lambda p: (0, p))
    return pl.pallas_call(
        mix_kernel,
        grid=(H // 2,),
        out_shape=[
            jax.ShapeDtypeStruct((TALL, D), jnp.bfloat16),
            jax.ShapeDtypeStruct((H, LEN, TALL), jnp.bfloat16),
            jax.ShapeDtypeStruct((H, 1, TALL), jnp.float32),
            jax.ShapeDtypeStruct((1, TALL), jnp.float32),
        ],
        in_specs=[
            SMEM_SPEC, SMEM_SPEC, tall, short, short,
            pl.BlockSpec((1, LEN), lambda p: (0, 0)),
            pl.BlockSpec((LEN, 1), lambda p: (0, 0)),
            pl.BlockSpec((2, 1, 512), lambda p: (p, 0, 0)),
        ],
        out_specs=[
            tall,
            pl.BlockSpec((2, LEN, TALL), lambda p: (p, 0, 0)),
            pl.BlockSpec((2, 1, TALL), lambda p: (p, 0, 0)),
            pl.BlockSpec((1, TALL), lambda p: (0, 0)),
        ],
        scratch_shapes=[
            pltpu.VMEM((LEN, TALL), jnp.float32),
            pltpu.VMEM((1, TALL), jnp.float32),
            pltpu.VMEM((2, 128, 384), jnp.float32),
            pltpu.VMEM((136, TALL), jnp.float32),
        ],
        compiler_params=PARAMS,
        cost_estimate=pl.CostEstimate(flops=6500000000, bytes_accessed=8000000, transcendentals=6300000),
        name="mix",
    )(length, far, q, k, v, row_flags, col_flags, tvec)


def mix_back_kernel(q_ref, k_ref, v_ref, da_ref, a_ref, p_ref, inverse_ref, dead_ref, *refs):
    (
        dq_ref, dk_ref, dv_ref, table_ref, s_ref, near_ref, da_t, low_t, q_t, g_ref,
    ) = refs[-10:]
    keys = k_ref[...].astype(jnp.float32) * SCORE_SCALE
    keys_t = keys.T.astype(jnp.bfloat16)
    q_t[...] = q_ref[...].astype(jnp.float32).T.astype(jnp.bfloat16)
    da_t[...] = da_ref[...].astype(jnp.float32).T
    product = a_ref[...].astype(jnp.float32).T * da_t[...]
    values = v_ref[...].astype(jnp.float32)
    near_ref[...] = jnp.zeros(near_ref.shape, jnp.float32)
    turn = (
        lax.broadcasted_iota(jnp.int32, (128, 128), 0)
        + lax.broadcasted_iota(jnp.int32, (128, 128), 1)
        == 127
    ).astype(jnp.float32)
    deltas = []
    for head in range(2):
        rows = slice(head * 64, head * 64 + 64)
        inverse = inverse_ref[head]
        deltas.append(jnp.sum(product[rows, :], axis=0, keepdims=True) * inverse)
        low_t[rows, :] = (da_t[rows, :] * inverse).astype(jnp.bfloat16)
    for head in range(2):
        own = slice(head * 64, head * 64 + 64)
        values_own = jnp.where(head_lanes(values.shape, head), values, 0.0).astype(jnp.bfloat16)
        delta = deltas[head]
        far_low = jnp.zeros((8, 128), jnp.float32)
        far_high = jnp.zeros((8, 128), jnp.float32)
        for chunk in range(4):
            at = chunk * HALF
            pulls = dot_nn(values_own, low_t[:, at : at + HALF])
            for side in range(2):
                lanes = slice(at + side * 128, at + side * 128 + 128)
                shift = delta[:, lanes]
                query_block = (chunk % 2) * 2 + side
                for key_block in range(4):
                    rows = slice(key_block * 128, key_block * 128 + 128)
                    cols = slice(side * 128, side * 128 + 128)
                    grad = p_ref[head, rows, lanes].astype(jnp.float32) * (
                        pulls[rows, cols] - shift
                    )
                    s_ref[head, rows, lanes] = grad.astype(jnp.bfloat16)
                    apart = query_block - key_block
                    if apart >= 2:
                        far_low = far_low + jnp.sum(grad.reshape(16, 8, 128), axis=0)
                    elif apart <= -2:
                        far_high = far_high + jnp.sum(grad.reshape(16, 8, 128), axis=0)
                    else:
                        near_ref[head, :, 128 * (apart + 1) : 128 * (apart + 2)] += grad
        g_ref[own, :LEN] = dot_nt(low_t[own, :], p_ref[head])
        g_ref[own, LEN:] = dot_nt(q_t[own, :], s_ref[head]) * SCORE_SCALE
        da_t[own, :] = dot_nn(keys_t[own, :], s_ref[head])
        turned = jnp.dot(
            turn, near_ref[head], precision=lax.Precision.HIGHEST, preferred_element_type=jnp.float32
        )
        aligned = pltpu.roll(turned, 0, 1, stride=1, stride_axis=0)
        table_ref[head, :, :512] = jnp.sum(aligned, axis=0, keepdims=True)
        table_ref[head, :, 512:640] = jnp.sum(far_low, axis=0, keepdims=True)
        table_ref[head, :, 640:] = jnp.sum(far_high, axis=0, keepdims=True)
    uniform = dot_nn(dead_ref[...].astype(jnp.bfloat16), da_ref[...])
    dv_ref[...] = (g_ref[:, :LEN].T + uniform).astype(jnp.bfloat16)
    dk_ref[...] = g_ref[:, LEN:].T.astype(jnp.bfloat16)
    dq_ref[...] = da_t[...].T.astype(jnp.bfloat16)


def mix_back(first, q, k, v, da, a, p, inverse, dead, held=()):
    tall = pl.BlockSpec((TALL, 128), lambda i: (0, i + first))
    short = pl.BlockSpec((LEN, 128), lambda i: (0, i + first))
    return pl.pallas_call(
        mix_back_kernel,
        grid=(H // 4,),
        out_shape=[
            jax.ShapeDtypeStruct((TALL, D), jnp.bfloat16),
            jax.ShapeDtypeStruct((LEN, D), jnp.bfloat16),
            jax.ShapeDtypeStruct((LEN, D), jnp.bfloat16),
            jax.ShapeDtypeStruct((H // 2, 1, 768), jnp.float32),
        ],
        in_specs=[
            tall, short, short, tall, tall,
            pl.BlockSpec((2, LEN, TALL), lambda i: (i + first, 0, 0)),
            pl.BlockSpec((2, 1, TALL), lambda i: (i + first, 0, 0)),
            pl.BlockSpec((1, TALL), lambda i: (0, 0)),
        ]
        + [ANY_SPEC] * len(held),
        out_specs=[tall, short, short, pl.BlockSpec((2, 1, 768), lambda i: (i, 0, 0))],
        input_output_aliases={8 + index: index for index in range(len(held))},
        scratch_shapes=[
            pltpu.VMEM((2, LEN, TALL), jnp.bfloat16),
            pltpu.VMEM((2, 128, 512), jnp.float32),
            pltpu.VMEM((128, TALL), jnp.float32),
            pltpu.VMEM((128, TALL), jnp.bfloat16),
            pltpu.VMEM((128, TALL), jnp.bfloat16),
            pltpu.VMEM((128, TALL), jnp.float32),
        ],
        compiler_params=PARAMS,
        cost_estimate=pl.CostEstimate(flops=8000000000, bytes_accessed=16000000, transcendentals=0),
        name="mix_back",
    )(q, k, v, da, a, p, inverse, dead, *held)


GELU_SCALE = 0.7978845608028654
GELU_CUBE = 0.044715


def feed_rows(rows, small_ref, hidden_bias_ref, resid, normed_ref, pre_ref, inner_ref, outer_ref):
    unit, scale = norm_parts(resid)
    normed = unit * small_ref[3:4, :] + small_ref[4:5, :]
    low = normed.astype(jnp.bfloat16)
    normed_ref[rows, :] = low
    total = normed + small_ref[5:6, :]
    for chunk in range(4):
        pre = dot_nn(low, inner_ref[chunk]) + hidden_bias_ref[:, chunk * D : chunk * D + D]
        pre_ref[chunk, rows, :] = pre.astype(jnp.bfloat16)
        tanh = jnp.tanh(GELU_SCALE * (pre + GELU_CUBE * (pre * pre * pre)))
        active = (pre * (0.5 + 0.5 * tanh)).astype(jnp.bfloat16)
        total = total + dot_nn(active, outer_ref[chunk])
    return total


def norm_two_back(unit, scale, grad, small_ref, sums):
    back = norm_back(unit, scale, grad, small_ref[6:7, :])
    low = back.astype(jnp.bfloat16)
    parts = (low.astype(jnp.float32), grad * unit, grad)
    return back, low, [
        total + jnp.sum(part, axis=0, keepdims=True) for total, part in zip(sums, parts)
    ]


def issue(pairs, sems, first=0):
    copies = [
        pltpu.make_async_copy(source, target, sems.at[first + index])
        for index, (source, target) in enumerate(pairs)
    ]
    for copy in copies:
        copy.start()
    return copies


def finish(copies):
    for copy in copies:
        copy.wait()


def storer(sems):
    copies = []

    def store(source, target):
        copy = pltpu.make_async_copy(source, target, sems.at[len(copies)])
        copy.start()
        copies.append(copy)

    return store, copies


def feed_kernel(
    plan, place_ref, small_ref, hidden_bias_ref, mix_any, hidden_any, attn_any, *refs
):
    (
        resid_out, pre_out, normed_out, low_out, summed_out,
        mix_ref, hidden_ref, wo_ref, inner_ref, outer_ref, resid_ref, total_ref, normed_ref,
        pre_ref, low_ref, sems, load_sems, store_sems,
    ) = refs[-18:]
    finish(
        issue(
            ((mix_any, mix_ref), (attn_any.at[3], wo_ref), (hidden_any, hidden_ref)), load_sems
        )
    )
    fetches = start_fetch(
        ("inner", "outer"), plan, place_ref, refs[:-18], (inner_ref, outer_ref), sems
    )
    for row in range(0, TALL, HALF):
        rows = slice(row, row + HALF)
        resid_ref[rows, :] = (
            hidden_ref[rows, :].astype(jnp.float32)
            + dot_nn(mix_ref[rows, :], wo_ref[...])
            + small_ref[2:3, :]
        )
    finish(fetches)
    store, stores = storer(store_sems)
    store(resid_ref, resid_out)
    for row in range(0, TALL, HALF):
        rows = slice(row, row + HALF)
        total = feed_rows(
            rows, small_ref, hidden_bias_ref, resid_ref[rows, :], normed_ref, pre_ref, inner_ref,
            outer_ref,
        )
        total_ref[rows, :] = total
        store(pre_ref.at[:, rows, :], pre_out.at[:, rows, :])
        store(total_ref.at[rows, :], summed_out.at[rows, :])
        store(normed_ref.at[rows, :], normed_out.at[rows, :])
        unit, scale = norm_parts(total)
        following = unit * small_ref[6:7, :] + small_ref[7:8, :]
        low_ref[rows, :] = following.astype(jnp.bfloat16)
        store(low_ref.at[rows, :], low_out.at[rows, :])
    finish(stores)


def feed(place, small, hidden_bias, mixed, hidden, attn, group):
    plan, pieces = group
    tall = jax.ShapeDtypeStruct((TALL, D), jnp.float32)
    tall_low = jax.ShapeDtypeStruct((TALL, D), jnp.bfloat16)
    return pl.pallas_call(
        partial(feed_kernel, plan),
        out_shape=[
            tall, jax.ShapeDtypeStruct((4, TALL, D), jnp.bfloat16), tall_low, tall_low, tall
        ],
        in_specs=[SMEM_SPEC, VMEM_SPEC, VMEM_SPEC] + [ANY_SPEC] * (3 + len(pieces)),
        out_specs=[ANY_SPEC] * 5,
        scratch_shapes=[
            pltpu.VMEM((TALL, D), jnp.bfloat16),
            pltpu.VMEM((TALL, D), jnp.bfloat16),
            pltpu.VMEM((D, D), jnp.bfloat16),
            pltpu.VMEM((4, D, D), jnp.bfloat16),
            pltpu.VMEM((4, D, D), jnp.bfloat16),
            pltpu.VMEM((TALL, D), jnp.float32),
            pltpu.VMEM((TALL, D), jnp.float32),
            pltpu.VMEM((TALL, D), jnp.bfloat16),
            pltpu.VMEM((4, TALL, D), jnp.bfloat16),
            pltpu.VMEM((TALL, D), jnp.bfloat16),
            pltpu.SemaphoreType.DMA((64,)),
            pltpu.SemaphoreType.DMA((3,)),
            pltpu.SemaphoreType.DMA((17,)),
        ],
        compiler_params=PARAMS,
        cost_estimate=pl.CostEstimate(flops=2 * TALL * D * (D + 2 * FF), bytes_accessed=30000000, transcendentals=3000000),
        name="feed",
    )(place, small, hidden_bias, mixed, hidden, attn, *pieces)


def back_steps(
    place_ref, small_ref, before, store, outs, vec_ref, dhidden_ref, branch_ref, total_ref,
    normed_ref, resid_ref, pre_ref, mix_ref, wo_ref, inner_ref, outer_ref, active_ref, dpre_ref,
    dinner_ref, douter_ref, dwo_ref,
):
    dresid_out, dmix_out, dwo_out, keep_out, send_out = outs
    x, c, z, y = (place_ref[index] for index in range(4))
    order = [(1 - step // 2, step % 2) for step in range(4)]
    chunks = [side * 2 + (c ^ apart) for apart, side in order]
    sums = [jnp.zeros((1, D), jnp.float32)] * 3
    for step in range(4):
        apart, side = order[step]
        chunk = chunks[step]
        before(step)
        bias_grad = jnp.zeros((1, D), jnp.float32)
        for row in range(0, TALL, HALF):
            rows = slice(row, row + HALF)
            pull = dot_nt(branch_ref[rows, :], outer_ref[chunk])
            pre = pre_ref[chunk, rows, :].astype(jnp.float32)
            square = pre * pre
            tanh = jnp.tanh(GELU_SCALE * pre * (1.0 + GELU_CUBE * square))
            half = 0.5 + 0.5 * tanh
            active_ref[rows, :] = (pre * half).astype(jnp.bfloat16)
            slope = half + (0.5 * GELU_SCALE) * pre * (1.0 - tanh * tanh) * (
                1.0 + (3.0 * GELU_CUBE) * square
            )
            dpre = (pull * slope).astype(jnp.bfloat16)
            dpre_ref[rows, :] = dpre
            bias_grad += jnp.sum(dpre.astype(jnp.float32), axis=0, keepdims=True)
            grad = total_ref[rows, :] + dot_nt(dpre, inner_ref[chunk])
            if step < 3:
                total_ref[rows, :] = grad
            else:
                unit, scale = norm_parts(resid_ref[rows, :])
                back = norm_back(unit, scale, grad, small_ref[3:4, :])
                resid_ref[rows, :] = back
                low = back.astype(jnp.bfloat16)
                pre_ref[chunks[0], rows, :] = low
                pre_ref[chunks[1], rows, :] = dot_nt(low, wo_ref[...]).astype(jnp.bfloat16)
                parts = (low.astype(jnp.float32), grad * unit, grad)
                sums = [
                    value + jnp.sum(part, axis=0, keepdims=True)
                    for value, part in zip(sums, parts)
                ]
        dhidden_ref[chunk] = bias_grad
        if step == 3:
            store(resid_ref, dresid_out)
            store(pre_ref.at[chunks[1]], dmix_out)
        douter_ref[step] = (
            dot_tn(active_ref[...], branch_ref[...]).astype(jnp.bfloat16).reshape(2, 2, 2, ROWS, D)
        )
        for y_block in range(2):
            for x_block in range(2):
                spot = (y_block ^ y, x_block ^ x, chunk, 1)
                store(douter_ref.at[step, y_block, x_block, c], keep_out.at[spot])
                store(douter_ref.at[step, y_block, x_block, 1 - c], send_out.at[spot])
        dinner_ref[step] = (
            dot_tn(normed_ref[...], dpre_ref[...]).astype(jnp.bfloat16).reshape(4, 2, ROWS, D)
        )
        target = send_out if apart else keep_out
        for y_block in range(2):
            store(dinner_ref.at[step, :, y_block], target.at[y_block ^ y, side ^ x, :, 0])
    dwo_ref[...] = dot_tn(mix_ref[...], pre_ref[chunks[0]]).astype(jnp.bfloat16)
    store(dwo_ref, dwo_out)
    for index, value in enumerate(sums):
        vec_ref[index : index + 1, :] = value


BACK_SHAPES = [
    jax.ShapeDtypeStruct((TALL, D), jnp.float32),
    jax.ShapeDtypeStruct((TALL, D), jnp.bfloat16),
    jax.ShapeDtypeStruct((D, D), jnp.bfloat16),
    jax.ShapeDtypeStruct((2, 2, 4, 2, ROWS, D), jnp.bfloat16),
    jax.ShapeDtypeStruct((2, 2, 4, 2, ROWS, D), jnp.bfloat16),
    jax.ShapeDtypeStruct((6, D), jnp.float32),
    jax.ShapeDtypeStruct((4, 1, D), jnp.float32),
]
BACK_SCRATCH = [
    pltpu.VMEM((TALL, D), jnp.bfloat16),
    pltpu.VMEM((TALL, D), jnp.float32),
    pltpu.VMEM((TALL, D), jnp.bfloat16),
    pltpu.VMEM((TALL, D), jnp.float32),
    pltpu.VMEM((4, TALL, D), jnp.bfloat16),
    pltpu.VMEM((TALL, D), jnp.bfloat16),
    pltpu.VMEM((D, D), jnp.bfloat16),
    pltpu.VMEM((4, D, D), jnp.bfloat16),
    pltpu.VMEM((4, D, D), jnp.bfloat16),
    pltpu.VMEM((TALL, D), jnp.bfloat16),
    pltpu.VMEM((TALL, D), jnp.bfloat16),
    pltpu.VMEM((4, 4, 2, ROWS, D), jnp.bfloat16),
    pltpu.VMEM((4, 2, 2, 2, ROWS, D), jnp.bfloat16),
    pltpu.VMEM((D, D), jnp.bfloat16),
    pltpu.SemaphoreType.DMA((64,)),
    pltpu.SemaphoreType.DMA((16,)),
    pltpu.SemaphoreType.DMA((48,)),
]


def turn_kernel(
    plan, place_ref, length_ref, small_ref, below_ref, hidden_bias_ref, mix_any, summed_any,
    attn_any, cot_c_any, cot_q_any, *refs
):
    content_out, query_out = refs[-27:-25]
    outs = refs[-25:-20]
    vec_ref, dhidden_ref = refs[-20:-18]
    low_ref = refs[-18]
    (
        branch_ref, total_ref, normed_ref, resid_ref, pre_ref, mix_ref, wo_ref, inner_ref,
        outer_ref, active_ref, dpre_ref, dinner_ref, douter_ref, dwo_ref,
        sems, load_sems, store_sems,
    ) = refs[-17:]
    store, stores = storer(store_sems)
    finish(
        issue(
            ((mix_any, mix_ref), (attn_any.at[3], wo_ref), (summed_any, resid_ref)), load_sems
        )
    )
    fetches = start_fetch(
        ("inner", "outer"), plan, place_ref, refs[:-27], (inner_ref, outer_ref), sems
    )
    fetches += issue(
        ((cot_c_any, low_ref.at[:LEN, :]), (cot_q_any, low_ref.at[LEN:, :])), load_sems, 3
    )
    for row in range(0, TALL, HALF):
        rows = slice(row, row + HALF)
        unit, scale = norm_parts(resid_ref[rows, :])
        resid_ref[rows, :] = (
            unit * below_ref[6:7, :]
            + below_ref[7:8, :]
            + dot_nn(mix_ref[rows, :], wo_ref[...])
            + small_ref[2:3, :]
        )
    finish(fetches)
    sums = [jnp.zeros((1, D), jnp.float32)] * 3
    for row in range(0, TALL, HALF):
        rows = slice(row, row + HALF)
        total = feed_rows(
            rows, small_ref, hidden_bias_ref, resid_ref[rows, :], normed_ref, pre_ref, inner_ref,
            outer_ref,
        )
        unit, scale = norm_parts(total)
        position = lax.broadcasted_iota(jnp.int32, (HALF, 1), 0) + row % LEN
        valid = (position < length_ref[0]).astype(jnp.float32)
        grad = low_ref[rows, :].astype(jnp.float32) * valid
        low_ref[rows, :] = (unit * small_ref[6:7, :] + small_ref[7:8, :]).astype(jnp.bfloat16)
        total_ref[rows, :], branch_ref[rows, :], sums = norm_two_back(
            unit, scale, grad, small_ref, sums
        )
    store(low_ref.at[:LEN, :], content_out)
    store(low_ref.at[LEN:, :], query_out)
    for index, value in enumerate(sums):
        vec_ref[3 + index : 4 + index, :] = value
    back_steps(
        place_ref, small_ref, lambda step: None, store, outs, vec_ref, dhidden_ref, branch_ref,
        total_ref, normed_ref, resid_ref, pre_ref, mix_ref, wo_ref, inner_ref, outer_ref,
        active_ref, dpre_ref, dinner_ref, douter_ref, dwo_ref,
    )
    finish(stores)


def turn(place, length, small, below, hidden_bias, mixed, summed, attn, cots, group):
    plan, pieces = group
    half_low = jax.ShapeDtypeStruct((LEN, D), jnp.bfloat16)
    return pl.pallas_call(
        partial(turn_kernel, plan),
        out_shape=[half_low, half_low] + BACK_SHAPES,
        in_specs=[SMEM_SPEC] * 2 + [VMEM_SPEC] * 3 + [ANY_SPEC] * (5 + len(pieces)),
        out_specs=[ANY_SPEC] * 7 + [VMEM_SPEC] * 2,
        scratch_shapes=[pltpu.VMEM((TALL, D), jnp.bfloat16)] + BACK_SCRATCH,
        compiler_params=PARAMS,
        cost_estimate=pl.CostEstimate(flops=6 * TALL * D * (D + 2 * FF), bytes_accessed=60000000, transcendentals=6000000),
        name="turn",
    )(place, length, small, below, hidden_bias, mixed, summed, attn, *cots, *pieces)


def down_kernel(
    plan, place_ref, small_ref, dq_any, dk_any, dv_any, w_any, dresid_any, summed_any,
    normed_any, resid_any, pre_any, mix_any, attn_any, *refs
):
    outs = refs[-29:-24]
    vec_ref, dhidden_ref = refs[-24:-22]
    dq_ref, dk_ref, dv_ref, w_ref, summed_ref = refs[-22:-17]
    (
        branch_ref, total_ref, normed_ref, resid_ref, pre_ref, mix_ref, wo_ref, inner_ref,
        outer_ref, active_ref, dpre_ref, dinner_ref, douter_ref, dwo_ref,
        sems, load_sems, store_sems,
    ) = refs[-17:]
    x, c, z, y = (place_ref[index] for index in range(4))
    chunks = [side * 2 + (c ^ apart) for apart in (1, 0) for side in range(2)]
    store, stores = storer(store_sems)
    loads = issue(
        (
            (w_any.at[0], w_ref.at[0]), (dq_any, dq_ref), (dresid_any, total_ref),
            (summed_any, summed_ref), (w_any.at[1:3], w_ref.at[1:3]), (dk_any, dk_ref),
            (dv_any, dv_ref),
        ),
        load_sems,
    )
    finish(loads[:4])
    fetches = start_fetch(
        ("inner", "outer"), plan, place_ref, refs[:-29], (inner_ref, outer_ref), sems
    )
    fetches += issue(((pre_any.at[chunks[0]], pre_ref.at[chunks[0]]),), load_sems, 7)
    sums = [jnp.zeros((1, D), jnp.float32)] * 3
    for index, row in enumerate((LEN, LEN + HALF, 0, HALF)):
        rows = slice(row, row + HALF)
        if index == 2:
            finish(loads[4:])
        total = total_ref[rows, :] + dot_nt(dq_ref[rows, :], w_ref[0])
        if index >= 2:
            total = total + dot_nt(dk_ref[rows, :], w_ref[1]) + dot_nt(dv_ref[rows, :], w_ref[2])
        unit, scale = norm_parts(summed_ref[rows, :])
        total_ref[rows, :], branch_ref[rows, :], sums = norm_two_back(
            unit, scale, total, small_ref, sums
        )
    for index, value in enumerate(sums):
        vec_ref[3 + index : 4 + index, :] = value
    finish(fetches)
    late = []

    def before(step):
        if step == 0:
            late.append(issue(((normed_any, normed_ref),), load_sems, 8))
        else:
            finish(late.pop())
        if step < 3:
            chunk = chunks[step + 1]
            late.insert(0, issue(((pre_any.at[chunk], pre_ref.at[chunk]),), load_sems, 9 + step))
        if step == 0:
            finish(late.pop())
        if step == 2:
            late[0].extend(
                issue(
                    ((resid_any, resid_ref), (mix_any, mix_ref), (attn_any.at[3], wo_ref)),
                    load_sems,
                    12,
                )
            )

    back_steps(
        place_ref, small_ref, before, store, outs, vec_ref, dhidden_ref, branch_ref, total_ref,
        normed_ref, resid_ref, pre_ref, mix_ref, wo_ref, inner_ref, outer_ref, active_ref,
        dpre_ref, dinner_ref, douter_ref, dwo_ref,
    )
    finish(stores)


def down(place, small, dq, dk, dv, w_above, dresid, summed, normed, resid, pre, mixed, attn, group):
    plan, pieces = group
    return pl.pallas_call(
        partial(down_kernel, plan),
        out_shape=BACK_SHAPES,
        in_specs=[SMEM_SPEC, VMEM_SPEC] + [ANY_SPEC] * (11 + len(pieces)),
        out_specs=[ANY_SPEC] * 5 + [VMEM_SPEC] * 2,
        scratch_shapes=[
            pltpu.VMEM((TALL, D), jnp.bfloat16),
            pltpu.VMEM((LEN, D), jnp.bfloat16),
            pltpu.VMEM((LEN, D), jnp.bfloat16),
            pltpu.VMEM((3, D, D), jnp.bfloat16),
            pltpu.VMEM((TALL, D), jnp.float32),
        ]
        + BACK_SCRATCH,
        compiler_params=PARAMS,
        cost_estimate=pl.CostEstimate(flops=5 * TALL * D * (D + 2 * FF), bytes_accessed=60000000, transcendentals=3000000),
        name="down",
    )(place, small, dq, dk, dv, w_above, dresid, summed, normed, resid, pre, mixed, attn, *pieces)


def weight_back_kernel(
    place_ref, low_any, dq_any, dk_any, dv_any, dwo_any, keep_out, send_out, vec_ref,
    low_ref, dq_ref, dk_ref, dv_ref, dwo_ref, grads_ref, load_sems, sems,
):
    x, c, z, y = (place_ref[index] for index in range(4))
    load = [
        pltpu.make_async_copy(source, target, load_sems.at[index])
        for index, (source, target) in enumerate(
            (
                (low_any.at[:LEN, :], low_ref.at[:LEN, :]), (dk_any, dk_ref), (dv_any, dv_ref),
                (low_any.at[LEN:, :], low_ref.at[LEN:, :]), (dq_any, dq_ref), (dwo_any, dwo_ref),
            )
        )
    ]
    for copy in load:
        copy.start()
    load[0].wait()
    load[1].wait()
    grads_ref[1] = (
        dot_tn(low_ref[:LEN, :], dk_ref[...]).astype(jnp.bfloat16).reshape(4, 2, ROWS, D)
    )
    load[2].wait()
    grads_ref[2] = (
        dot_tn(low_ref[:LEN, :], dv_ref[...]).astype(jnp.bfloat16).reshape(4, 2, ROWS, D)
    )
    vec_ref[1:2, :] = jnp.sum(dv_ref[...].astype(jnp.float32), axis=0, keepdims=True)
    for copy in load[3:]:
        copy.wait()
    grads_ref[3] = dwo_ref[...].reshape(4, 2, ROWS, D)
    grads_ref[0] = dot_tn(low_ref[...], dq_ref[...]).astype(jnp.bfloat16).reshape(4, 2, ROWS, D)
    vec_ref[0:1, :] = jnp.sum(dq_ref[...].astype(jnp.float32), axis=0, keepdims=True)
    blocks = []
    for apart, target in ((1, send_out), (0, keep_out)):
        for side in range(2):
            for y_block in range(2):
                copy = pltpu.make_async_copy(
                    grads_ref.at[side * 2 + (c ^ apart), :, y_block],
                    target.at[y_block ^ y, side ^ x, :, 0],
                    sems.at[len(blocks)],
                )
                copy.start()
                blocks.append(copy)
    for block in blocks:
        block.wait()


def weight_back(place, low, dq, dk, dv, dwo):
    blocks = jax.ShapeDtypeStruct((2, 2, 4, 1, ROWS, D), jnp.bfloat16)
    return pl.pallas_call(
        weight_back_kernel,
        out_shape=[blocks, blocks, jax.ShapeDtypeStruct((2, D), jnp.float32)],
        in_specs=[SMEM_SPEC] + [ANY_SPEC] * 5,
        out_specs=[ANY_SPEC] * 2 + [VMEM_SPEC],
        scratch_shapes=[
            pltpu.VMEM((TALL, D), jnp.bfloat16),
            pltpu.VMEM((TALL, D), jnp.bfloat16),
            pltpu.VMEM((LEN, D), jnp.bfloat16),
            pltpu.VMEM((LEN, D), jnp.bfloat16),
            pltpu.VMEM((D, D), jnp.bfloat16),
            pltpu.VMEM((4, 4, 2, ROWS, D), jnp.bfloat16),
            pltpu.SemaphoreType.DMA((6,)),
            pltpu.SemaphoreType.DMA((8,)),
        ],
        compiler_params=PARAMS,
        cost_estimate=pl.CostEstimate(flops=2 * 2048 * D * D, bytes_accessed=12000000, transcendentals=0),
        name="weight_back",
    )(place, low, dq, dk, dv, dwo)


def input_back_kernel(
    dq_any, dk_any, dv_any, w_any, dresid_any, first_out, second_out,
    dq_ref, dk_ref, dv_ref, w_ref, dresid_ref, load_sems, store_sems,
):
    loads = issue(
        (
            (w_any.at[0], w_ref.at[0]), (dq_any, dq_ref), (dresid_any, dresid_ref),
            (w_any.at[1:3], w_ref.at[1:3]), (dk_any, dk_ref), (dv_any, dv_ref),
        ),
        load_sems,
    )
    finish(loads[:3])
    store, stores = storer(store_sems)
    for index, row in enumerate((LEN, LEN + HALF, 0, HALF)):
        rows = slice(row, row + HALF)
        if index == 2:
            finish(loads[3:])
        total = dresid_ref[rows, :] + dot_nt(dq_ref[rows, :], w_ref[0])
        if index >= 2:
            total = total + dot_nt(dk_ref[rows, :], w_ref[1]) + dot_nt(dv_ref[rows, :], w_ref[2])
        dresid_ref[rows, :] = total
        target = first_out if index >= 2 else second_out
        store(dresid_ref.at[rows, :], target.at[row % LEN : row % LEN + HALF, :])
    finish(stores)


def input_back(dq, dk, dv, attn, dresid):
    half = jax.ShapeDtypeStruct((LEN, D), jnp.float32)
    return pl.pallas_call(
        input_back_kernel,
        out_shape=[half, half],
        in_specs=[ANY_SPEC] * 5,
        out_specs=[ANY_SPEC] * 2,
        scratch_shapes=[
            pltpu.VMEM((TALL, D), jnp.bfloat16),
            pltpu.VMEM((LEN, D), jnp.bfloat16),
            pltpu.VMEM((LEN, D), jnp.bfloat16),
            pltpu.VMEM((3, D, D), jnp.bfloat16),
            pltpu.VMEM((TALL, D), jnp.float32),
            pltpu.SemaphoreType.DMA((6,)),
            pltpu.SemaphoreType.DMA((4,)),
        ],
        compiler_params=PARAMS,
        cost_estimate=pl.CostEstimate(flops=2 * 2048 * D * D, bytes_accessed=16000000, transcendentals=0),
        name="input_back",
    )(dq, dk, dv, attn, dresid)


def bias_vectors(table):
    lane = jnp.arange(512, dtype=jnp.int32)
    offset = jnp.where(lane < 384, 128 - lane, 640 - lane)
    onehot = bucket_of(offset)[:, None] == jnp.arange(NB, dtype=jnp.int32)[None, :]
    near = jnp.dot(table, onehot.astype(jnp.float32).T, precision=lax.Precision.HIGHEST)
    return (near[:, None, :], jnp.stack([table[:, 15], table[:, 31]], axis=1), onehot)


def bucket_of(offset):
    distance = jnp.abs(offset)
    far_bucket = jnp.full(distance.shape, 8, jnp.int32)
    for exponent in range(1, 8):
        far_bucket = far_bucket + (distance * distance >= 64 * 2**exponent).astype(jnp.int32)
    near_or_far = jnp.where(distance < 8, distance, far_bucket)
    return near_or_far + NB // 2 * (offset > 0).astype(jnp.int32)


def table_grad(sums, onehot):
    near = jnp.roll(onehot.astype(jnp.float32), 127, axis=0)
    far = jnp.arange(NB, dtype=jnp.int32)[None, :] == jnp.repeat(jnp.array([15, 31]), 128)[:, None]
    return jnp.dot(
        sums[:, 0, :],
        jnp.concatenate([near, far.astype(jnp.float32)]),
        precision=lax.Precision.HIGHEST,
    )


RATES = (ATTENTION_RATE, FEED_RATE, FEED_RATE)


def adam_kernel(*refs):
    states, grads, outs = refs[:9], refs[9:12], refs[-9:]
    for kind, rate in enumerate(RATES):
        master_ref, first_ref, second_ref = states[3 * kind : 3 * kind + 3]
        master_out, first_out, second_out = outs[3 * kind : 3 * kind + 3]
        grad = grads[kind][...].astype(jnp.float32).reshape(master_ref.shape)
        master = master_ref[...]
        first = BETA_ONE * first_ref[...] + (1.0 - BETA_ONE) * grad
        second = BETA_TWO * second_ref[...] + (1.0 - BETA_TWO) * grad * grad
        first_out[...] = first
        second_out[...] = second
        first_scale = rate / (1.0 - BETA_ONE**STEP)
        second_scale = 1.0 / (1.0 - BETA_TWO**STEP)
        step = (first_scale * first) / (jnp.sqrt(second_scale * second) + ADAM_EPS)
        master_out[...] = master - (step + (rate * WEIGHT_DECAY) * master)


def adam(layer, state, quarters, held):
    half = ROWS // 2
    blocks = (
        [pl.BlockSpec((1, 1, half, D), lambda i: (layer, i // 2, i % 2, 0))] * 3
        + [pl.BlockSpec((1, half, D), lambda i: (layer, i % 2, i // 2))] * 3
        + [pl.BlockSpec((1, half, D), lambda i: (layer, i, 0))] * 3
    )
    grads = [
        pl.BlockSpec((1, 1, half, D), partial(lambda member, i: (i // 2, member, i % 2, 0), member))
        for member in (2, 0, 1)
    ]
    return pl.pallas_call(
        adam_kernel,
        grid=(8,),
        out_shape=[jax.ShapeDtypeStruct(array.shape, jnp.float32) for array in state],
        in_specs=blocks + grads + [ANY_SPEC] * len(held),
        out_specs=blocks,
        input_output_aliases={12 + index: index for index in range(len(held))},
        compiler_params=pltpu.CompilerParams(vmem_limit_bytes=16 * 1024 * 1024),
        cost_estimate=pl.CostEstimate(flops=20000000, bytes_accessed=22000000, transcendentals=0),
        name="adam",
    )(*state, quarters, quarters, quarters, *held)


def fetch_forward(shards):
    low = tuple(shard.astype(jnp.bfloat16) for shard in shards)
    return (
        lax.all_gather(low[0], "fsdp", axis=1, tiled=True),
        lax.all_gather(low[1], "fsdp", axis=0, tiled=True),
        lax.all_gather(low[2], "fsdp", axis=0, tiled=True),
    )


def reduce_layer(grads):
    owned = tuple(
        lax.psum_scatter(
            grad.astype(jnp.bfloat16), "fsdp", scatter_dimension=axis, tiled=True
        ).astype(jnp.float32)
        for grad, axis in zip(grads, (1, 0, 0))
    )
    return lax.psum(owned, "dp")


def forward_layer(hidden_c, hidden_q, weights, lengths, flag_rows, onehot):
    attn_w, inner_w, outer_w, small_w = weights
    pieces, hidden_bias, bias_table = unpack(small_w.astype(jnp.float32))
    bias_q, bias_v, bias_o, gain_one, shift_one, bias_two, gain_two, shift_two = pieces
    table_low = bias_table.astype(jnp.bfloat16)
    low_c = hidden_c.astype(jnp.bfloat16)
    low_q = hidden_q.astype(jnp.bfloat16)
    projected = jnp.einsum("td,sde->ste", low_c, attn_w[:3], preferred_element_type=jnp.float32)
    query_c = (projected[0] + bias_q).astype(jnp.bfloat16)
    key_rows = projected[1].astype(jnp.bfloat16)
    value_rows = (projected[2] + bias_v).astype(jnp.bfloat16)
    query_q = (jnp.dot(low_q, attn_w[0], preferred_element_type=jnp.float32) + bias_q).astype(
        jnp.bfloat16
    )
    mixed_c, mixed_q, lse_c, lse_q = lax.map(
        partial(attend_slot, onehot, table_low),
        (
            to_heads(query_c),
            to_heads(query_q),
            to_heads(key_rows),
            to_heads(value_rows),
            lengths,
            flag_rows,
        ),
    )
    mixed_c = mixed_c.reshape(-1, D)
    mixed_q = mixed_q.reshape(-1, D)
    outputs = []
    kept = []
    for hidden_in, mixed in ((hidden_c, mixed_c), (hidden_q, mixed_q)):
        resid = hidden_in + jnp.dot(mixed, attn_w[3], preferred_element_type=jnp.float32) + bias_o
        normed = layer_norm(resid, gain_one, shift_one)
        pre_act = (
            jnp.dot(normed.astype(jnp.bfloat16), inner_w, preferred_element_type=jnp.float32)
            + hidden_bias
        )
        active = jax.nn.gelu(pre_act, approximate=True).astype(jnp.bfloat16)
        summed = normed + jnp.dot(active, outer_w, preferred_element_type=jnp.float32) + bias_two
        outputs.append(layer_norm(summed, gain_two, shift_two))
        kept.append((resid, summed, pre_act))
    saved = (
        hidden_c,
        hidden_q,
        query_c,
        query_q,
        key_rows,
        value_rows,
        lse_c,
        lse_q,
        mixed_c,
        mixed_q,
        kept[0],
        kept[1],
    )
    return (outputs[0], outputs[1], saved)


def backward_layer(saved, weights, grad_c, grad_q, lengths, flag_rows, onehot):
    attn_w, inner_w, outer_w, small_w = weights
    pieces, hidden_bias, bias_table = unpack(small_w.astype(jnp.float32))
    bias_q, bias_v, bias_o, gain_one, shift_one, bias_two, gain_two, shift_two = pieces
    table_low = bias_table.astype(jnp.bfloat16)
    (
        hidden_c,
        hidden_q,
        query_c,
        query_q,
        key_rows,
        value_rows,
        lse_c,
        lse_q,
        mixed_c,
        mixed_q,
        kept_c,
        kept_q,
    ) = saved
    gelu_tanh = partial(jax.nn.gelu, approximate=True)
    grad_outer = jnp.zeros(outer_w.shape, jnp.float32)
    grad_inner = jnp.zeros(inner_w.shape, jnp.float32)
    grad_attn_out = jnp.zeros((D, D), jnp.float32)
    grad_bias_two = jnp.zeros((D,), jnp.float32)
    grad_hidden_bias = jnp.zeros((FF,), jnp.float32)
    grad_bias_o = jnp.zeros((D,), jnp.float32)
    grad_gain_one = jnp.zeros((D,), jnp.float32)
    grad_shift_one = jnp.zeros((D,), jnp.float32)
    grad_gain_two = jnp.zeros((D,), jnp.float32)
    grad_shift_two = jnp.zeros((D,), jnp.float32)
    residual_grads = []
    mix_grads = []
    for kept_rows, grad_out, mixed in ((kept_c, grad_c, mixed_c), (kept_q, grad_q, mixed_q)):
        resid, summed, pre_act = kept_rows
        normed, norm_one_back = jax.vjp(layer_norm, resid, gain_one, shift_one)
        unused_out, norm_two_back = jax.vjp(layer_norm, summed, gain_two, shift_two)
        grad_summed, grad_g2, grad_s2 = norm_two_back(grad_out)
        grad_gain_two = grad_gain_two + grad_g2
        grad_shift_two = grad_shift_two + grad_s2
        grad_branch = grad_summed.astype(jnp.bfloat16)
        grad_bias_two = grad_bias_two + jnp.sum(grad_branch.astype(jnp.float32), axis=0)
        active, gelu_back = jax.vjp(gelu_tanh, pre_act)
        grad_outer = grad_outer + jnp.einsum(
            "tf,td->fd",
            active.astype(jnp.bfloat16),
            grad_branch,
            preferred_element_type=jnp.float32,
        )
        grad_active = jnp.einsum(
            "td,fd->tf", grad_branch, outer_w, preferred_element_type=jnp.float32
        )
        grad_pre = gelu_back(grad_active)[0].astype(jnp.bfloat16)
        grad_hidden_bias = grad_hidden_bias + jnp.sum(grad_pre.astype(jnp.float32), axis=0)
        grad_inner = grad_inner + jnp.einsum(
            "td,tf->df", normed.astype(jnp.bfloat16), grad_pre, preferred_element_type=jnp.float32
        )
        grad_normed = grad_summed + jnp.einsum(
            "tf,df->td", grad_pre, inner_w, preferred_element_type=jnp.float32
        )
        grad_resid, grad_g1, grad_s1 = norm_one_back(grad_normed)
        grad_gain_one = grad_gain_one + grad_g1
        grad_shift_one = grad_shift_one + grad_s1
        grad_proj = grad_resid.astype(jnp.bfloat16)
        grad_bias_o = grad_bias_o + jnp.sum(grad_proj.astype(jnp.float32), axis=0)
        grad_attn_out = grad_attn_out + jnp.einsum(
            "td,te->de", mixed, grad_proj, preferred_element_type=jnp.float32
        )
        mix_grads.append(
            jnp.einsum(
                "te,de->td", grad_proj, attn_w[3], preferred_element_type=jnp.float32
            ).astype(jnp.bfloat16)
        )
        residual_grads.append(grad_resid)
    grad_query_c, grad_query_q, grad_keys, grad_values, grad_table = lax.map(
        partial(attend_back, onehot, table_low),
        (
            to_heads(query_c),
            to_heads(query_q),
            to_heads(key_rows),
            to_heads(value_rows),
            lengths,
            flag_rows,
            lse_c,
            lse_q,
            to_heads(mix_grads[0]),
            to_heads(mix_grads[1]),
        ),
    )
    grad_table = jnp.sum(grad_table, axis=0)
    low_query_c = grad_query_c.reshape(-1, D).astype(jnp.bfloat16)
    low_query_q = grad_query_q.reshape(-1, D).astype(jnp.bfloat16)
    low_keys = grad_keys.reshape(-1, D).astype(jnp.bfloat16)
    low_values = grad_values.reshape(-1, D).astype(jnp.bfloat16)
    low_c = hidden_c.astype(jnp.bfloat16)
    low_q = hidden_q.astype(jnp.bfloat16)
    stacked_grads = jnp.stack([low_query_c, low_keys, low_values])
    grad_qkv = jnp.einsum("td,ste->sde", low_c, stacked_grads, preferred_element_type=jnp.float32)
    grad_wq = grad_qkv[0] + jnp.einsum(
        "td,te->de", low_q, low_query_q, preferred_element_type=jnp.float32
    )
    grad_attn = jnp.stack([grad_wq, grad_qkv[1], grad_qkv[2], grad_attn_out])
    grad_bias_q = jnp.sum(low_query_c.astype(jnp.float32), axis=0) + jnp.sum(
        low_query_q.astype(jnp.float32), axis=0
    )
    grad_bias_v = jnp.sum(low_values.astype(jnp.float32), axis=0)
    grad_content = residual_grads[0] + jnp.einsum(
        "ste,sde->td", stacked_grads, attn_w[:3], preferred_element_type=jnp.float32
    )
    grad_query_in = residual_grads[1] + jnp.einsum(
        "te,de->td", low_query_q, attn_w[0], preferred_element_type=jnp.float32
    )
    grad_small = jnp.concatenate(
        [
            grad_bias_q,
            grad_bias_v,
            grad_bias_o,
            grad_gain_one,
            grad_shift_one,
            grad_bias_two,
            grad_gain_two,
            grad_shift_two,
            grad_hidden_bias,
            grad_table.reshape(-1),
        ]
    )
    return (grad_content, grad_query_in, (grad_attn, grad_inner, grad_outer, grad_small))


def adam_update(master, first, second, grad, rate):
    first_new = BETA_ONE * first + (1.0 - BETA_ONE) * grad
    second_new = BETA_TWO * second + (1.0 - BETA_TWO) * grad * grad
    first_hat = first_new / (1.0 - BETA_ONE**STEP)
    second_hat = second_new / (1.0 - BETA_TWO**STEP)
    master_new = master - rate * (
        first_hat / (jnp.sqrt(second_hat) + ADAM_EPS) + WEIGHT_DECAY * master
    )
    return (master_new, first_new, second_new)


def per_device(
    content,
    query,
    lengths,
    predicted,
    content_cot,
    query_cot,
    attn_master,
    attn_first,
    attn_second,
    inner_master,
    inner_first,
    inner_second,
    outer_master,
    outer_first,
    outer_second,
    small_master,
    small_first,
    small_second,
):
    masters = (attn_master, inner_master, outer_master, small_master)
    slot_count = lengths.shape[0]
    flag_rows = predicted.reshape(slot_count, LEN)
    onehot = bucket_onehot()
    hidden_c = content.astype(jnp.float32)
    hidden_q = query.astype(jnp.float32)
    kept_weights = []
    saved_layers = []
    small_all = lax.all_gather(
        small_master.astype(jnp.bfloat16), "fsdp", axis=1, tiled=True
    )
    for layer_index in range(LAYERS):
        shards = tuple((master[layer_index] for master in masters[:3]))
        gathered = fetch_forward(shards) + (small_all[layer_index],)
        kept_weights.append(gathered)
        hidden_c, hidden_q, saved = forward_layer(
            hidden_c, hidden_q, gathered, lengths, flag_rows, onehot
        )
        saved_layers.append(saved)
    position = jnp.arange(LEN, dtype=jnp.int32)
    valid_rows = (position[None, :] < lengths[:, None]).reshape(-1, 1).astype(jnp.float32)
    grad_c = content_cot.astype(jnp.float32) * valid_rows
    grad_q = query_cot.astype(jnp.float32) * valid_rows
    layer_grads = [None] * LAYERS
    small_grads = [None] * LAYERS
    for layer_index in reversed(range(LAYERS)):
        grad_c, grad_q, local_grads = backward_layer(
            saved_layers[layer_index],
            kept_weights[layer_index],
            grad_c,
            grad_q,
            lengths,
            flag_rows,
            onehot,
        )
        small_grads[layer_index] = local_grads[3]
        layer_grads[layer_index] = reduce_layer(local_grads[:3])
    small_sum = lax.psum(jnp.stack(small_grads), ("dp", "fsdp"))
    owned = small_master.shape[1]
    small_own = lax.dynamic_slice_in_dim(
        small_sum, lax.axis_index("fsdp") * owned, owned, 1
    )
    reduced = tuple(
        (
            jnp.stack([layer_grads[layer_index][member] for layer_index in range(LAYERS)])
            for member in range(3)
        )
    ) + (small_own,)
    attn_new = adam_update(attn_master, attn_first, attn_second, reduced[0], ATTENTION_RATE)
    inner_new = adam_update(inner_master, inner_first, inner_second, reduced[1], FEED_RATE)
    outer_new = adam_update(outer_master, outer_first, outer_second, reduced[2], FEED_RATE)
    small_new = adam_update(small_master, small_first, small_second, reduced[3], SMALL_RATE)
    return (
        hidden_c.astype(jnp.bfloat16),
        hidden_q.astype(jnp.bfloat16),
        grad_c,
        grad_q,
        attn_new[0],
        attn_new[1],
        attn_new[2],
        inner_new[0],
        inner_new[1],
        inner_new[2],
        outer_new[0],
        outer_new[1],
        outer_new[2],
        small_new[0],
        small_new[1],
        small_new[2],
    )


def quarter_of(kind, shard, quarter):
    if kind == "attn":
        return lax.dynamic_index_in_dim(shard, quarter, 0, keepdims=False)
    if kind == "inner":
        return lax.dynamic_slice_in_dim(shard, quarter * D, D, 1)
    return lax.dynamic_slice_in_dim(shard, quarter * ROWS, ROWS, 0)


def after(value, *others):
    return lax.optimization_barrier((value, others))[0]


def join(*values):
    return lax.optimization_barrier(values)


def own_blocks(kinds, shards, place, side):
    quarter = (place[0] ^ side) * 2 + place[1]
    return jnp.stack(
        [
            quarter_of(kind, shard, quarter).astype(jnp.bfloat16)
            for kind, shard in zip(kinds, shards)
        ]
    )


def gather_group(count, shards, plane, column, sides, corners, mine, theirs):
    plan = []
    for core, arrays in enumerate((mine, theirs)):
        base = core * len(mine)
        for member in range(count):
            array, first = plane
            plan += [
                (base + array, first + side * count + member, side, 1, core, 0, member)
                for side in range(2)
            ]
            for apart in (1, 2, 3):
                index = (apart - 1) * count + member
                array, first = column
                plan.append((base + array, first + index, 0, 0, core, apart, member))
                for dx, dy, (array, first) in ((1, 0, sides[0]), (0, 1, sides[1])):
                    plan.append((base + array, first + index, dx, dy, core, apart, member))
                skipped = 0
                for array, first, held in corners:
                    if skipped <= index < skipped + held:
                        plan.append(
                            (base + array, first + index - skipped, 1, 1, core, apart, member)
                        )
                    skipped += held
    return (tuple(plan), tuple(shards) + tuple(mine) + tuple(theirs))


def gather_small(blocks, place):
    z, y = place[2], place[3]
    low, high = z % 2, z // 2
    blocks = jnp.where(low == 0, blocks, blocks[jnp.array([1, 0, 3, 2])])
    blocks = jnp.where(high == 0, blocks, blocks[jnp.array([2, 3, 0, 1])])
    other = swap_y(blocks)
    pairs = jnp.where(y == 0, jnp.stack([blocks, other], 1), jnp.stack([other, blocks], 1))
    return pairs.transpose(2, 0, 1, 3).reshape(blocks.shape[1], -1)


def add_low(*values):
    total = values[0].astype(jnp.float32)
    for value in values[1:]:
        total = total + value.astype(jnp.float32)
    return total.astype(jnp.bfloat16)


def reduce_corners(keep, get):
    corner = add_low(keep[1, 1], get[1, 1])
    return (swap_x(corner[:2]), swap_y(corner[2:]))


def side_payloads(keep, get, corners):
    by_x, by_y = corners
    pad = ((0, 0),) * 3
    for_x = add_low(keep[0, 1], get[0, 1], jnp.pad(by_y, ((2, 0),) + pad))
    for_y = add_low(keep[1, 0], get[1, 0], jnp.pad(by_x, ((0, 2),) + pad))
    return (for_x, for_y)


def reduce_sides(payloads):
    return (swap_x(payloads[0]), swap_y(payloads[1]))


def z_pair(values, half):
    return add_low(*(lax.dynamic_slice_in_dim(value, 2 * half, 2, 0) for value in values))


def far_payload(keep, get, sides, place):
    return z_pair((keep[0, 0], get[0, 0]) + tuple(sides), 1 - place[2] // 2)


def own_pair(keep, get, sides, far, place):
    half = place[2] // 2
    pair = (
        lax.dynamic_slice_in_dim(value, 2 * half, 2, 0)
        for value in (keep[0, 0], get[0, 0]) + tuple(sides)
    )
    return add_low(*pair, far)


def pick(pair, index):
    return lax.dynamic_index_in_dim(pair, index, 0, keepdims=False)


def reduce_near(pair, place):
    return swap_z(pick(pair, 1 - place[2] % 2), 1)


def reduce_total(pair, near, place):
    return add_low(pick(pair, place[2] % 2), near)


def reduce_direct(column, place):
    return tuple(swap_z(pick(column, place[2] ^ apart), apart) for apart in (1, 2, 3))


def share_core(pair, place):
    x, c = place[0], place[1]
    other = swap_core(pair)
    cores = jnp.where(c == 0, jnp.stack([pair, other], 1), jnp.stack([other, pair], 1))
    sides = jnp.where(x == 0, cores, cores[::-1])
    return sides.reshape((4,) + pair.shape[1:])


def small_parts(vectors):
    values = vectors.astype(jnp.float32)
    return (
        values[: 8 * D].reshape(8, D),
        values[8 * D : 8 * D + FF].reshape(1, FF),
        bias_vectors(values[8 * D + FF :].reshape(H, NB)),
    )


def per_device_fast(
    content,
    query,
    lengths,
    predicted,
    content_cot,
    query_cot,
    attn_master,
    attn_first,
    attn_second,
    inner_master,
    inner_first,
    inner_second,
    outer_master,
    outer_first,
    outer_second,
    small_master,
    small_first,
    small_second,
):
    place_parts = my_place()
    place = jnp.stack(place_parts).astype(jnp.int32)
    attn_kinds, feed_kinds = ("attn",), ("inner", "outer")
    attn_shards = [(attn_master[layer],) for layer in range(LAYERS)]
    feed_shards = [(inner_master[layer], outer_master[layer]) for layer in range(LAYERS)]
    own_a0 = own_blocks(attn_kinds, attn_shards[0], place_parts, 0)
    oth_a0 = own_blocks(attn_kinds, attn_shards[0], place_parts, 1)
    own_f0 = own_blocks(feed_kinds, feed_shards[0], place_parts, 0)
    z_a0 = tuple(swap_z(own_a0, apart) for apart in (1, 2, 3))
    plane_a0 = swap_y(jnp.concatenate([own_a0, oth_a0]))
    near_f0 = swap_z(own_f0, 1)
    z_a0, plane_a0, near_f0 = join(z_a0, plane_a0, near_f0)
    oth_f0 = own_blocks(feed_kinds, feed_shards[0], place_parts, 1)
    own_a1 = own_blocks(attn_kinds, attn_shards[1], place_parts, 0)
    oth_a1 = own_blocks(attn_kinds, attn_shards[1], place_parts, 1)
    own_f1 = own_blocks(feed_kinds, feed_shards[1], place_parts, 0)
    oth_f1 = own_blocks(feed_kinds, feed_shards[1], place_parts, 1)
    attn_low = [tuple(w.astype(jnp.bfloat16) for w in shards) for shards in attn_shards]
    feed_low = [tuple(w.astype(jnp.bfloat16) for w in shards) for shards in feed_shards]
    col_a0 = jnp.concatenate(z_a0)
    x0 = swap_x(col_a0)
    y0 = swap_y(jnp.concatenate([col_a0, own_f0, oth_f0]))
    far_f0 = swap_z(jnp.concatenate([own_f0, near_f0]), 2)
    near_1 = swap_z(after(jnp.concatenate([own_a1, own_f1]), z_a0), 1)
    small_low = small_master.astype(jnp.bfloat16)
    small_near = swap_z(after(small_low, z_a0), 1)
    x0, y0, far_f0, near_1, small_near = join(x0, y0, far_f0, near_1, small_near)
    col_f0 = jnp.concatenate([near_f0, far_f0])
    x1 = swap_x(jnp.concatenate([col_f0, y0[:2]]))
    y1 = swap_y(jnp.concatenate([col_f0, x0[2:]]))
    far_a1 = swap_z(jnp.concatenate([own_a1, near_1[:1]]), 2)
    mine_0 = jnp.concatenate([plane_a0, col_a0, x0, y0, col_f0])
    theirs_0 = swap_core(mine_0)
    small_pair = jnp.stack([small_low, small_near])
    small_far = swap_z(small_pair, 2)
    small_all = gather_small(jnp.concatenate([small_pair, small_far]), place_parts)
    x1, y1, far_a1, theirs_0, small_all = join(x1, y1, far_a1, theirs_0, small_all)
    col_a1 = jnp.concatenate([near_1[:1], far_a1])
    x2 = swap_x(jnp.concatenate([col_a1, y1[:4]]))
    y2 = swap_y(jnp.concatenate([col_a1, x1[4:6], own_a1, oth_a1]))
    far_f1 = swap_z(jnp.concatenate([own_f1, after(near_1[1:], far_a1)]), 2)
    their_x1, their_y1 = swap_core(x1), swap_core(y1)
    group_a0 = gather_group(
        1, attn_low[0], (0, 0), (0, 2), ((0, 5), (0, 8)), ((1, 6, 2), (2, 6, 1)),
        (mine_0, x1, y1), (theirs_0, their_x1, their_y1),
    )
    row_flags = predicted.reshape(1, LEN).astype(jnp.float32)
    col_flags = predicted.reshape(LEN, 1).astype(jnp.float32)
    low0 = jnp.concatenate([content, query])
    small0, hidden_bias0, (tvec0, far0, onehot) = small_parts(small_all[0])
    small1, hidden_bias1, (tvec1, far1, onehot) = small_parts(small_all[1])
    q0, k0, v0, attn0 = project(place, low0, small0, group_a0)
    mixed0, p0, inverse0, dead = mix(lengths, far0, tvec0, q0, k0, v0, row_flags, col_flags)
    x2, y2, far_f1, mixed0 = join(x2, y2, far_f1, mixed0)
    col_f1 = jnp.concatenate([near_1[1:], far_f1])
    x3 = swap_x(jnp.concatenate([col_f1, y2[:3]]))
    y3 = swap_y(jnp.concatenate([col_f1, own_f1, oth_f1]))
    their_x2, their_y2, their_a1 = swap_core(x2), swap_core(y2), swap_core(after(col_a1, x2))
    group_f0 = gather_group(
        2, feed_low[0], (0, 11), (0, 15), ((1, 0), (2, 0)), ((3, 3, 4), (4, 3, 2)),
        (mine_0, x1, y1, x2, y2), (theirs_0, their_x1, their_y1, their_x2, their_y2),
    )
    resid0, pre0, normed0, low1, summed0 = feed(
        place, small0, hidden_bias0, mixed0, low0, attn0, group_f0
    )
    x3, y3, low1 = join(x3, y3, low1)
    x4 = swap_x(y3[:3])
    y4 = swap_y(x3[3:6])
    their_x3, their_y3 = swap_core(x3), swap_core(y3)
    group_a1 = gather_group(
        1, attn_low[1], (1, 5), (2, 0), ((0, 0), (1, 0)), ((3, 6, 3),),
        (x2, y2, col_a1, x3), (their_x2, their_y2, their_a1, their_x3),
    )
    q1, k1, v1, attn1 = project(place, low1, small1, group_a1)
    x4, y4, q1 = join(x4, y4, q1)
    their_x4, their_y4, their_f1 = swap_core(x4), swap_core(y4), swap_core(after(col_f1, q1))
    group_f1 = gather_group(
        2, feed_low[1], (1, 6), (4, 0), ((0, 0), (1, 0)), ((2, 0, 3), (3, 0, 3)),
        (x3, y3, x4, y4, col_f1), (their_x3, their_y3, their_x4, their_y4, their_f1),
    )
    mixed1, p1, inverse1, dead = mix(
        lengths, far1, tvec1, q1, k1, v1, row_flags, col_flags
    )
    content_out, query_out, dresid1, dmix1, dwo1, keep_f1, send_f1, vec_f1, dhidden1 = turn(
        place, lengths, small1, small0, hidden_bias1, mixed1, summed0, attn1,
        (content_cot, query_cot), group_f1
    )
    get_f1 = swap_core(send_f1)
    *first1, table1_a = mix_back(0, q1, k1, v1, dmix1, mixed1, p1, inverse1, dead)
    by_f1 = reduce_corners(keep_f1, after(get_f1, table1_a))
    dq1, dk1, dv1, table1_b = mix_back(
        3, after(q1, get_f1, table1_a), k1, v1, dmix1, mixed1, p1, inverse1, dead, tuple(first1)
    )
    sides_rf1 = reduce_sides(side_payloads(keep_f1, get_f1, after(by_f1, table1_b)))
    keep_a1, send_a1, vec_a1 = weight_back(place, after(low1, by_f1), dq1, dk1, dv1, dwo1)
    get_a1 = swap_core(send_a1)
    by_a1 = reduce_corners(keep_a1, get_a1)
    dresid0, dmix0, dwo0, keep_f0, send_f0, vec_f0, dhidden0 = down(
        place, small0, dq1, dk1, dv1, after(attn1, get_a1), dresid1, summed0, normed0, resid0,
        pre0, mixed0, attn0, group_f0
    )
    get_f0 = swap_core(after(send_f0, sides_rf1, by_a1))
    sides_ra1 = reduce_sides(side_payloads(keep_a1, get_a1, after(by_a1, dmix0)))
    sides_rf1 = after(sides_rf1, dmix0)
    zfar_f1 = swap_z(far_payload(keep_f1, get_f1, sides_rf1, place_parts), 2)
    *first0, table0_a = mix_back(
        0, after(q0, by_a1, sides_rf1), k0, v0, dmix0, mixed0, p0, inverse0, dead
    )
    by_f0 = reduce_corners(keep_f0, after(get_f0, table0_a))
    pair_f1 = own_pair(keep_f1, get_f1, sides_rf1, after(zfar_f1, table0_a), place_parts)
    znear_f1 = reduce_near(pair_f1, place_parts)
    dq0, dk0, dv0, table0_b = mix_back(
        3, after(q0, get_f0, zfar_f1), k0, v0, dmix0, mixed0, p0, inverse0, dead, tuple(first0)
    )
    by_f0, sides_ra1, znear_f1, table0_b = join(by_f0, sides_ra1, znear_f1, table0_b)
    payloads_f0 = side_payloads(keep_f0, get_f0, by_f0)
    sides_rf0 = reduce_sides(payloads_f0)
    keep_a0, send_a0, vec_a0 = weight_back(
        place, after(low0, payloads_f0, table0_b), dq0, dk0, dv0, dwo0
    )
    get_a0 = swap_core(send_a0)
    zfar_a1 = swap_z(far_payload(keep_a1, get_a1, sides_ra1, place_parts), 2)
    sides_rf0, get_a0, zfar_a1, vec_a0 = join(sides_rf0, get_a0, zfar_a1, vec_a0)
    payload_f0 = far_payload(keep_f0, get_f0, sides_rf0, place_parts)
    zfar_f0 = swap_z(payload_f0, 2)
    by_a0 = reduce_corners(keep_a0, after(get_a0, payload_f0))
    pair_a1 = own_pair(keep_a1, get_a1, sides_ra1, zfar_a1, place_parts)
    znear_a1 = reduce_near(after(pair_a1, payload_f0), place_parts)
    content_grad, query_grad = input_back(after(dq0, sides_rf0), dk0, dv0, attn0, dresid0)
    small_sum = jnp.concatenate(
        [
            jnp.stack([vec_a0, vec_a1]).reshape(LAYERS, -1),
            jnp.stack([vec_f0, vec_f1]).reshape(LAYERS, -1),
            jnp.stack([dhidden0, dhidden1]).reshape(LAYERS, -1),
            table_grad(
                jnp.concatenate([table0_a, table0_b, table1_a, table1_b]), onehot
            ).reshape(LAYERS, -1),
        ],
        axis=1,
    )
    by_a0, content_grad, znear_a1 = join(by_a0, content_grad, znear_a1)
    payloads_a0 = side_payloads(keep_a0, get_a0, by_a0)
    sides_ra0 = reduce_sides(payloads_a0)
    own_1 = jnp.concatenate(
        [
            reduce_total(pair_f1, znear_f1, place_parts),
            reduce_total(pair_a1, znear_a1, place_parts),
        ]
    )
    across_1 = swap_x(after(own_1, payloads_a0))
    small_sum = small_sum + swap_core(after(small_sum, payloads_a0))
    sides_ra0, zfar_f0, small_sum = join(sides_ra0, zfar_f0, small_sum)
    column_a0 = add_low(keep_a0[0, 0], get_a0[0, 0], *sides_ra0)
    shifts_a0 = reduce_direct(column_a0, place_parts)
    pair_f0 = own_pair(keep_f0, get_f0, sides_rf0, zfar_f0, place_parts)
    znear_f0 = reduce_near(after(pair_f0, column_a0), place_parts)
    small_sum = small_sum + swap_y(after(small_sum, column_a0))
    shifts_a0, znear_f0, across_1, small_sum = join(shifts_a0, znear_f0, across_1, small_sum)
    own_0 = jnp.concatenate(
        [
            reduce_total(pair_f0, znear_f0, place_parts),
            add_low(pick(column_a0, place_parts[2]), *shifts_a0),
        ]
    )
    across_0 = swap_x(own_0)
    four_1 = share_core(jnp.stack([own_1, after(across_1, own_0)]), place_parts)
    state = (
        attn_master, attn_first, attn_second, inner_master, inner_first, inner_second,
        outer_master, outer_first, outer_second,
    )
    new_1 = adam(1, state, four_1, ())
    small_sum = small_sum + swap_z(after(small_sum, own_0), 1)
    small_sum = small_sum + swap_z(small_sum, 2)
    across_0, new_1, small_sum = join(across_0, new_1, small_sum)
    four_0 = share_core(jnp.stack([own_0, across_0]), place_parts)
    small_x = swap_x(small_sum)
    new_0 = adam(0, state, four_0, tuple(new_1))
    small_sum = small_sum + small_x
    size = small_master.shape[1]
    small_own = lax.dynamic_slice_in_dim(small_sum, lax.axis_index("fsdp") * size, size, 1)
    small_new = adam_update(small_master, small_first, small_second, small_own, SMALL_RATE)
    return (
        (content_out, query_out, content_grad, query_grad)
        + tuple(new_0)
        + small_new
    )


def solution(mesh):
    placed = (
        P(("dp", "fsdp"), None),
        P(("dp", "fsdp"), None),
        P(("dp", "fsdp")),
        P(("dp", "fsdp")),
        P(("dp", "fsdp"), None),
        P(("dp", "fsdp"), None),
        P(None, None, "fsdp", None),
        P(None, None, "fsdp", None),
        P(None, None, "fsdp", None),
        P(None, "fsdp", None),
        P(None, "fsdp", None),
        P(None, "fsdp", None),
        P(None, "fsdp", None),
        P(None, "fsdp", None),
        P(None, "fsdp", None),
        P(None, "fsdp"),
        P(None, "fsdp"),
        P(None, "fsdp"),
    )
    fast = tuple(mesh.shape.values()) == (4, 8)
    return jax.shard_map(
        per_device_fast if fast else per_device,
        mesh=mesh,
        in_specs=placed,
        out_specs=(
            P(("dp", "fsdp"), None),
            P(("dp", "fsdp"), None),
            P(("dp", "fsdp"), None),
            P(("dp", "fsdp"), None),
            P(None, None, "fsdp", None),
            P(None, None, "fsdp", None),
            P(None, None, "fsdp", None),
            P(None, "fsdp", None),
            P(None, "fsdp", None),
            P(None, "fsdp", None),
            P(None, "fsdp", None),
            P(None, "fsdp", None),
            P(None, "fsdp", None),
            P(None, "fsdp"),
            P(None, "fsdp"),
            P(None, "fsdp"),
        ),
        check_vma=False,
    )
```

```python
from functools import partial

import jax
import jax.numpy as jnp
from jax import lax
from jax.experimental import pallas as pl
from jax.experimental.pallas import tpu as pltpu
from jax.sharding import PartitionSpec as P

D = 768
H = 12
DH = 64
FF = 3072
LEN = 512
NB = 32
LAYERS = 2
STEP = 10


NORM_EPS = 1e-05
MASKED = -1000000000.0
BETA_ONE = 0.9
BETA_TWO = 0.999
ATTENTION_RATE = 0.1
FEED_RATE = 0.02
SMALL_RATE = 0.4
WEIGHT_DECAY = 0.01
ADAM_EPS = 1e-08
SCORE_SCALE = 0.125


def layer_norm(values, gain, shift):
    centre = values - jnp.mean(values, axis=-1, keepdims=True)
    spread = jnp.mean(centre * centre, axis=-1, keepdims=True)
    return centre * lax.rsqrt(spread + NORM_EPS) * gain + shift


def unpack(vectors):
    pieces = [vectors[piece_index * D : (piece_index + 1) * D] for piece_index in range(8)]
    hidden_bias = vectors[8 * D : 8 * D + FF]
    bias_table = vectors[8 * D + FF :].reshape(H, NB)
    return (pieces, hidden_bias, bias_table)


def bucket_ids():
    position = jnp.arange(LEN, dtype=jnp.int32)
    offset = position[None, :] - position[:, None]
    distance = jnp.abs(offset)
    far_bucket = jnp.full(distance.shape, 8, jnp.int32)
    for exponent in range(1, 8):
        far_bucket = far_bucket + (distance * distance >= 64 * 2**exponent).astype(jnp.int32)
    near_or_far = jnp.where(distance < 8, distance, far_bucket)
    return near_or_far + NB // 2 * (offset > 0).astype(jnp.int32)


def bucket_onehot():
    return (bucket_ids()[:, :, None] == jnp.arange(NB, dtype=jnp.int32)[None, None, :]).astype(
        jnp.bfloat16
    )


def allowed_pairs(length, pred_flags):
    position = jnp.arange(LEN, dtype=jnp.int32)
    valid_key = (position < length)[None, :]
    row_pos = position[:, None]
    col_pos = position[None, :]
    free_key = (pred_flags == 0)[None, :]
    content_ok = valid_key & (free_key | (pred_flags[:, None] == 1) & (col_pos <= row_pos))
    query_ok = valid_key & (col_pos != row_pos) & (free_key | (col_pos < row_pos))
    return (content_ok, query_ok)


def masked_scores(query_rows, key_rows, position_bias, allowed):
    scores = (
        jnp.einsum("qhd,khd->hqk", query_rows, key_rows, preferred_element_type=jnp.float32)
        * SCORE_SCALE
        + position_bias
    )
    return jnp.where(allowed[None], scores, MASKED)


def table_bias(onehot, table_low):
    return jnp.einsum("qkb,hb->hqk", onehot, table_low, preferred_element_type=jnp.float32)


def attend_slot(onehot, table_low, slot_item):
    query_c, query_q, key_rows, value_rows, length, pred_flags = slot_item
    position_bias = table_bias(onehot, table_low)
    content_ok, query_ok = allowed_pairs(length, pred_flags)
    results = []
    for query_rows, allowed in ((query_c, content_ok), (query_q, query_ok)):
        scores = masked_scores(query_rows, key_rows, position_bias, allowed)
        peak = jnp.max(scores, axis=-1, keepdims=True)
        expos = jnp.exp(scores - peak)
        totals = jnp.sum(expos, axis=-1, keepdims=True)
        probs = (expos / totals).astype(jnp.bfloat16)
        mixed = jnp.einsum(
            "hqk,khd->qhd", probs, value_rows, preferred_element_type=jnp.float32
        ).astype(jnp.bfloat16)
        results.append((mixed, peak[..., 0] + jnp.log(totals[..., 0])))
    return (results[0][0], results[1][0], results[0][1], results[1][1])


def attend_back(onehot, table_low, slot_item):
    (
        query_c,
        query_q,
        key_rows,
        value_rows,
        length,
        pred_flags,
        lse_c,
        lse_q,
        grad_mix_c,
        grad_mix_q,
    ) = slot_item
    position_bias = table_bias(onehot, table_low)
    content_ok, query_ok = allowed_pairs(length, pred_flags)
    grad_keys = jnp.zeros(key_rows.shape, jnp.float32)
    grad_values = jnp.zeros(value_rows.shape, jnp.float32)
    grad_table = jnp.zeros((H, NB), jnp.float32)
    grads_query = []
    for query_rows, allowed, log_total, grad_mix in (
        (query_c, content_ok, lse_c, grad_mix_c),
        (query_q, query_ok, lse_q, grad_mix_q),
    ):
        scores = masked_scores(query_rows, key_rows, position_bias, allowed)
        probs = jnp.exp(scores - log_total[..., None])
        grad_values = grad_values + jnp.einsum(
            "hqk,qhd->khd", probs.astype(jnp.bfloat16), grad_mix, preferred_element_type=jnp.float32
        )
        grad_probs = jnp.einsum(
            "qhd,khd->hqk", grad_mix, value_rows, preferred_element_type=jnp.float32
        )
        grad_scores = probs * (grad_probs - jnp.sum(probs * grad_probs, axis=-1, keepdims=True))
        grad_scores = jnp.where(allowed[None], grad_scores, 0.0).astype(jnp.bfloat16)
        grad_table = grad_table + jnp.einsum(
            "hqk,qkb->hb", grad_scores, onehot, preferred_element_type=jnp.float32
        )
        grads_query.append(
            jnp.einsum("hqk,khd->qhd", grad_scores, key_rows, preferred_element_type=jnp.float32)
            * SCORE_SCALE
        )
        grad_keys = (
            grad_keys
            + jnp.einsum(
                "hqk,qhd->khd", grad_scores, query_rows, preferred_element_type=jnp.float32
            )
            * SCORE_SCALE
        )
    return (grads_query[0], grads_query[1], grad_keys, grad_values, grad_table)


def to_heads(values):
    return values.reshape(-1, LEN, H, DH)


AXES = ("dp", "fsdp")
GRID = (2, 2, 4, 2)
ROWS = 96


def places():
    return [
        (x, c, z, y) for x in range(2) for c in range(2) for z in range(4) for y in range(2)
    ]


def flat(x, c, z, y):
    return ((x * 2 + c) * 4 + z) * 2 + y


def move(value, shift):
    pairs = [(flat(*place), flat(*shift(*place))) for place in places()]
    return lax.ppermute(value, AXES, pairs)


def swap_core(value):
    return move(value, lambda x, c, z, y: (x, 1 - c, z, y))


def swap_x(value):
    return move(value, lambda x, c, z, y: (1 - x, c, z, y))


def swap_y(value):
    return move(value, lambda x, c, z, y: (x, c, z, 1 - y))


def swap_z(value, apart):
    return move(value, lambda x, c, z, y: (x, c, z ^ apart, y))


def my_place():
    dp = lax.axis_index("dp")
    fsdp = lax.axis_index("fsdp")
    return (dp // 2, dp % 2, fsdp // 2, fsdp % 2)


def dot_nn(left, right):
    return jnp.dot(left, right, preferred_element_type=jnp.float32)


def dot_nt(left, right):
    return lax.dot_general(
        left, right, (((1,), (1,)), ((), ())), preferred_element_type=jnp.float32
    )


def dot_tn(left, right):
    return lax.dot_general(
        left, right, (((0,), (0,)), ((), ())), preferred_element_type=jnp.float32
    )


ANY_SPEC = pl.BlockSpec(memory_space=pl.ANY)
VMEM_SPEC = pl.BlockSpec(memory_space=pltpu.VMEM)
SMEM_SPEC = pl.BlockSpec(memory_space=pltpu.SMEM)
TALL = 2 * LEN
HALF = 256
PARAMS = pltpu.CompilerParams(vmem_limit_bytes=60 * 1024 * 1024)


def norm_parts(values):
    centre = values - jnp.mean(values, axis=-1, keepdims=True)
    spread = jnp.mean(centre * centre, axis=-1, keepdims=True)
    scale = lax.rsqrt(spread + NORM_EPS)
    return (centre * scale, scale)


def norm_back(unit, scale, grad, gain):
    scaled = grad * gain
    return scale * (
        scaled
        - jnp.mean(scaled, axis=-1, keepdims=True)
        - unit * jnp.mean(scaled * unit, axis=-1, keepdims=True)
    )


def start_fetch(kinds, plan, place_ref, refs, targets, sems):
    x, c, z, y = (place_ref[index] for index in range(4))
    mine = z * 2 + y
    copies = []

    def start(source, target):
        copy = pltpu.make_async_copy(source, target, sems.at[len(copies)])
        copy.start()
        copies.append(copy)

    for member, kind in enumerate(kinds):
        target = targets[member]
        if kind == "attn":
            start(refs[member], target.at[:, pl.ds(pl.multiple_of(mine * ROWS, ROWS), ROWS), :])
        elif kind == "inner":
            for quarter in range(4):
                start(
                    refs[member].at[:, quarter * D : quarter * D + D],
                    target.at[quarter, pl.ds(pl.multiple_of(mine * ROWS, ROWS), ROWS), :],
                )
        else:
            start(refs[member], target.at[z, pl.ds(pl.multiple_of(y * 384, ROWS), 384), :])
    for array, index, dx, dy, dc, dz, member in plan:
        quarter = (x ^ dx) * 2 + (c ^ dc)
        if kinds[member] == "outer":
            lead, row = z ^ dz, (y ^ dy) * 384 + quarter * ROWS
        else:
            lead, row = quarter, ((z ^ dz) * 2 + (y ^ dy)) * ROWS
        start(
            refs[len(kinds) + array].at[index],
            targets[member].at[lead, pl.ds(pl.multiple_of(row, ROWS), ROWS), :],
        )
    return copies


def quarter_spans(place_ref, side):
    quarter = (place_ref[0] ^ side) * 2 + place_ref[1]
    return (
        quarter,
        pl.ds(pl.multiple_of(quarter * D, D), D),
        pl.ds(pl.multiple_of(quarter * ROWS, ROWS), ROWS),
    )


def cast_first_kernel(
    place_ref, attn_any, inner_any, outer_any, own_a0, plane_a0, own_f0, hold_ref, sems
):
    index, cols, rows = quarter_spans(place_ref, 0)
    other = quarter_spans(place_ref, 1)[0]
    finish(
        issue(
            (
                (attn_any.at[0, index], hold_ref.at[0]),
                (attn_any.at[0, other], hold_ref.at[1]),
                (inner_any.at[0, :, cols], hold_ref.at[2]),
                (outer_any.at[0, rows, :], hold_ref.at[3]),
            ),
            sems,
        )
    )
    own_a0[...] = hold_ref[0:1].astype(jnp.bfloat16)
    plane_a0[...] = hold_ref[0:2].astype(jnp.bfloat16)
    own_f0[...] = hold_ref[2:4].astype(jnp.bfloat16)


def cast_first(place, attn, inner, outer):
    return pl.pallas_call(
        cast_first_kernel,
        out_shape=[jax.ShapeDtypeStruct((count, ROWS, D), jnp.bfloat16) for count in (1, 2, 2)],
        in_specs=[SMEM_SPEC] + [ANY_SPEC] * 3,
        out_specs=[VMEM_SPEC] * 3,
        scratch_shapes=[pltpu.VMEM((4, ROWS, D), jnp.float32), pltpu.SemaphoreType.DMA((4,))],
        compiler_params=PARAMS,
        cost_estimate=pl.CostEstimate(flops=1000000, bytes_accessed=2000000, transcendentals=0),
        name="cast_first",
    )(place, attn, inner, outer)


def cast_rest_kernel(
    place_ref, attn_ref, inner_ref, outer_ref, attn_0, attn_1, inner_0, inner_1, outer_0, outer_1,
    plane_f0, own_1, oth_1,
):
    for layer, (attn_low, inner_low, outer_low) in enumerate(
        ((attn_0, inner_0, outer_0), (attn_1, inner_1, outer_1))
    ):
        attn_low[...] = attn_ref[layer].astype(jnp.bfloat16)
        inner_low[...] = inner_ref[layer].astype(jnp.bfloat16)
        outer_low[...] = outer_ref[layer].astype(jnp.bfloat16)
    for side, (target, first) in enumerate(((own_1, 0), (oth_1, 0))):
        index, cols, rows = quarter_spans(place_ref, side)
        plane_f0[2 * side] = inner_ref[0, :, cols].astype(jnp.bfloat16)
        plane_f0[2 * side + 1] = outer_ref[0, rows, :].astype(jnp.bfloat16)
        target[0] = attn_ref[1, index].astype(jnp.bfloat16)
        target[1] = inner_ref[1, :, cols].astype(jnp.bfloat16)
        target[2] = outer_ref[1, rows, :].astype(jnp.bfloat16)


def cast_rest(place, attn, inner, outer):
    low = [
        jax.ShapeDtypeStruct(array.shape[1:], jnp.bfloat16)
        for array in (attn, attn, inner, inner, outer, outer)
    ]
    return pl.pallas_call(
        cast_rest_kernel,
        out_shape=low
        + [jax.ShapeDtypeStruct((count, ROWS, D), jnp.bfloat16) for count in (4, 3, 3)],
        in_specs=[SMEM_SPEC] + [VMEM_SPEC] * 3,
        out_specs=[VMEM_SPEC] * 9,
        compiler_params=PARAMS,
        cost_estimate=pl.CostEstimate(flops=10000000, bytes_accessed=12000000, transcendentals=0),
        name="cast_rest",
    )(place, attn, inner, outer)


def project_kernel(plan, place_ref, small_ref, low_any, *refs):
    pieces = refs[:-14]
    (
        q_out, k_out, v_out, w_out, low_ref, q_ref, k_ref, v_ref, w_ref,
        sems, load_sem, keep_sem, store_sems, unused,
    ) = refs[-14:]
    load = pltpu.make_async_copy(low_any, low_ref, load_sem)
    load.start()
    fetches = start_fetch(("attn",), plan, place_ref, pieces, (w_ref,), sems)
    load.wait()
    for copy in fetches:
        copy.wait()
    keep = pltpu.make_async_copy(w_ref, w_out, keep_sem)
    keep.start()
    bias_q = small_ref[0:1, :]
    bias_v = small_ref[1:2, :]
    stores = []

    def store(source, target):
        copy = pltpu.make_async_copy(source, target, store_sems.at[len(stores)])
        copy.start()
        stores.append(copy)

    for row in range(0, TALL, HALF):
        span = slice(row, row + HALF)
        rows = low_ref[span, :]
        q_ref[span, :] = (dot_nn(rows, w_ref[0]) + bias_q).astype(jnp.bfloat16)
        if row < LEN:
            k_ref[span, :] = dot_nn(rows, w_ref[1]).astype(jnp.bfloat16)
            v_ref[span, :] = (dot_nn(rows, w_ref[2]) + bias_v).astype(jnp.bfloat16)
        if row == LEN - HALF:
            store(k_ref, k_out)
            store(v_ref, v_out)
            store(q_ref.at[:LEN, :], q_out.at[:LEN, :])
    store(q_ref.at[LEN:, :], q_out.at[LEN:, :])
    for copy in stores:
        copy.wait()
    keep.wait()


def project(place, low, small, group):
    plan, pieces = group
    return pl.pallas_call(
        partial(project_kernel, plan),
        out_shape=[
            jax.ShapeDtypeStruct((TALL, D), jnp.bfloat16),
            jax.ShapeDtypeStruct((LEN, D), jnp.bfloat16),
            jax.ShapeDtypeStruct((LEN, D), jnp.bfloat16),
            jax.ShapeDtypeStruct((4, D, D), jnp.bfloat16),
        ],
        in_specs=[SMEM_SPEC, VMEM_SPEC, ANY_SPEC] + [ANY_SPEC] * len(pieces),
        out_specs=[ANY_SPEC] * 4,
        scratch_shapes=[
            pltpu.VMEM((TALL, D), jnp.bfloat16),
            pltpu.VMEM((TALL, D), jnp.bfloat16),
            pltpu.VMEM((LEN, D), jnp.bfloat16),
            pltpu.VMEM((LEN, D), jnp.bfloat16),
            pltpu.VMEM((4, D, D), jnp.bfloat16),
            pltpu.SemaphoreType.DMA((32,)),
            pltpu.SemaphoreType.DMA,
            pltpu.SemaphoreType.DMA,
            pltpu.SemaphoreType.DMA((4,)),
            pltpu.SemaphoreType.DMA,
        ],
        compiler_params=PARAMS,
        cost_estimate=pl.CostEstimate(flops=2 * 2048 * D * D, bytes_accessed=16000000, transcendentals=0),
        name="project",
    )(place, small, low, *pieces)


def build_masks(length, row_flags, col_flags, mask_ref, alive_ref):
    flags = row_flags[...]

    def body(step, carry):
        start = pl.multiple_of(step * 64, 64)
        key = lax.broadcasted_iota(jnp.int32, (64, LEN), 0) + start
        query = lax.broadcasted_iota(jnp.int32, (64, LEN), 1)
        valid = key < length
        free = jnp.broadcast_to(col_flags[pl.ds(start, 64), :], (64, LEN)) == 0.0
        marked = jnp.broadcast_to(flags, (64, LEN)) == 1.0
        content_ok = valid & (free | (marked & (key <= query)))
        query_ok = valid & (key != query) & (free | (key < query))
        mask_ref[pl.ds(start, 64), :LEN] = content_ok.astype(jnp.float32)
        mask_ref[pl.ds(start, 64), LEN:] = query_ok.astype(jnp.float32)
        return carry

    lax.fori_loop(0, 8, body, 0)
    alive_ref[...] = jnp.max(mask_ref[...], axis=0, keepdims=True)


def build_tiles(t_row, tile_ref):
    spread = jnp.broadcast_to(t_row, (128, 512))
    rolled = pltpu.roll(spread, 0, 1, stride=1, stride_axis=0)
    tile_ref[...] = rolled[:, :384]


def position_bias(tile_ref, far_ref, head, query_block, key_block):
    apart = query_block - key_block
    if apart >= 2:
        return far_ref[head, 0]
    if apart <= -2:
        return far_ref[head, 1]
    return tile_ref[:, 128 * (apart + 1) : 128 * (apart + 2)]


def head_lanes(shape, head):
    lane = lax.broadcasted_iota(jnp.int32, shape, 1)
    return (lane >= 64) if head else (lane < 64)


def mix_kernel(
    length_ref, far_ref, q_ref, k_ref, v_ref, row_flags, col_flags, t_ref,
    a_ref, p_ref, inverse_ref, dead_ref, mask_ref, alive_ref, tile_ref, o_ref,
):
    pair = pl.program_id(0)

    @pl.when(pair == 0)
    def _():
        build_masks(length_ref[0], row_flags, col_flags, mask_ref, alive_ref)
        dead_ref[...] = (1.0 - alive_ref[...]) * (1.0 / LEN)

    keys = k_ref[...].astype(jnp.float32) * SCORE_SCALE
    values_t = v_ref[...].astype(jnp.float32).T.astype(jnp.bfloat16)
    keys_own = [
        jnp.where(head_lanes(keys.shape, head), keys, 0.0).astype(jnp.bfloat16) for head in range(2)
    ]
    for head in range(2):
        build_tiles(t_ref[head], tile_ref.at[head])
    work = [(head, chunk) for head in range(2) for chunk in range(4)]

    def score(head, chunk):
        return dot_nt(keys_own[head], q_ref[chunk * HALF : chunk * HALF + HALF, :])

    def mixture(head, chunk):
        span = slice(chunk * HALF, chunk * HALF + HALF)
        own = slice(8 + head * 64, 8 + head * 64 + 64)
        mixed = dot_nn(values_t[head * 64 : head * 64 + 64, :], p_ref[head, :, span])
        o_ref[own, span] = mixed * o_ref[head : head + 1, span]

    following = score(*work[0])
    for index, (head, chunk) in enumerate(work):
        scores = following
        if index + 1 < len(work):
            following = score(*work[index + 1])
        at = chunk * HALF
        for side in range(2):
            lanes = slice(at + side * 128, at + side * 128 + 128)
            blocks = []
            peak = None
            for key_block in range(4):
                rows = slice(key_block * 128, key_block * 128 + 128)
                block = scores[rows, side * 128 : side * 128 + 128] + position_bias(
                    tile_ref.at[head], far_ref, pair * 2 + head, (chunk % 2) * 2 + side, key_block
                )
                block = jnp.where(mask_ref[rows, lanes] > 0.0, block, MASKED)
                blocks.append(block)
                high = jnp.max(block, axis=0, keepdims=True)
                peak = high if peak is None else jnp.maximum(peak, high)
            total = None
            for key_block in range(4):
                rows = slice(key_block * 128, key_block * 128 + 128)
                expo = jnp.exp(blocks[key_block] - peak)
                part = jnp.sum(expo, axis=0, keepdims=True)
                total = part if total is None else total + part
                p_ref[head, rows, lanes] = expo.astype(jnp.bfloat16)
            inverse = 1.0 / total
            inverse_ref[head, :, lanes] = inverse * alive_ref[:, lanes]
            o_ref[head : head + 1, lanes] = inverse
        if index:
            mixture(*work[index - 1])
    mixture(*work[-1])
    a_ref[...] = o_ref[8:, :].T.astype(jnp.bfloat16)


def mix(length, far, tvec, q, k, v, row_flags, col_flags):
    tall = pl.BlockSpec((TALL, 128), lambda p: (0, p))
    short = pl.BlockSpec((LEN, 128), lambda p: (0, p))
    return pl.pallas_call(
        mix_kernel,
        grid=(H // 2,),
        out_shape=[
            jax.ShapeDtypeStruct((TALL, D), jnp.bfloat16),
            jax.ShapeDtypeStruct((H, LEN, TALL), jnp.bfloat16),
            jax.ShapeDtypeStruct((H, 1, TALL), jnp.float32),
            jax.ShapeDtypeStruct((1, TALL), jnp.float32),
        ],
        in_specs=[
            SMEM_SPEC, SMEM_SPEC, tall, short, short,
            pl.BlockSpec((1, LEN), lambda p: (0, 0)),
            pl.BlockSpec((LEN, 1), lambda p: (0, 0)),
            pl.BlockSpec((2, 1, 512), lambda p: (p, 0, 0)),
        ],
        out_specs=[
            tall,
            pl.BlockSpec((2, LEN, TALL), lambda p: (p, 0, 0)),
            pl.BlockSpec((2, 1, TALL), lambda p: (p, 0, 0)),
            pl.BlockSpec((1, TALL), lambda p: (0, 0)),
        ],
        scratch_shapes=[
            pltpu.VMEM((LEN, TALL), jnp.float32),
            pltpu.VMEM((1, TALL), jnp.float32),
            pltpu.VMEM((2, 128, 384), jnp.float32),
            pltpu.VMEM((136, TALL), jnp.float32),
        ],
        compiler_params=PARAMS,
        cost_estimate=pl.CostEstimate(flops=6500000000, bytes_accessed=8000000, transcendentals=6300000),
        name="mix",
    )(length, far, q, k, v, row_flags, col_flags, tvec)


def mix_back_kernel(q_ref, k_ref, v_ref, da_ref, a_ref, p_ref, inverse_ref, dead_ref, *refs):
    (
        dq_ref, dk_ref, dv_ref, table_ref, s_ref, near_ref, da_t, low_t, q_t, g_ref,
    ) = refs[-10:]
    keys = k_ref[...].astype(jnp.float32) * SCORE_SCALE
    keys_t = keys.T.astype(jnp.bfloat16)
    q_t[...] = q_ref[...].astype(jnp.float32).T.astype(jnp.bfloat16)
    da_t[...] = da_ref[...].astype(jnp.float32).T
    product = a_ref[...].astype(jnp.float32).T * da_t[...]
    values = v_ref[...].astype(jnp.float32)
    near_ref[...] = jnp.zeros(near_ref.shape, jnp.float32)
    turn = (
        lax.broadcasted_iota(jnp.int32, (128, 128), 0)
        + lax.broadcasted_iota(jnp.int32, (128, 128), 1)
        == 127
    ).astype(jnp.float32)
    deltas = []
    for head in range(2):
        rows = slice(head * 64, head * 64 + 64)
        inverse = inverse_ref[head]
        deltas.append(jnp.sum(product[rows, :], axis=0, keepdims=True) * inverse)
        low_t[rows, :] = (da_t[rows, :] * inverse).astype(jnp.bfloat16)
    for head in range(2):
        own = slice(head * 64, head * 64 + 64)
        values_own = jnp.where(head_lanes(values.shape, head), values, 0.0).astype(jnp.bfloat16)
        delta = deltas[head]
        far_low = jnp.zeros((8, 128), jnp.float32)
        far_high = jnp.zeros((8, 128), jnp.float32)
        for chunk in range(4):
            at = chunk * HALF
            pulls = dot_nn(values_own, low_t[:, at : at + HALF])
            for side in range(2):
                lanes = slice(at + side * 128, at + side * 128 + 128)
                shift = delta[:, lanes]
                query_block = (chunk % 2) * 2 + side
                for key_block in range(4):
                    rows = slice(key_block * 128, key_block * 128 + 128)
                    cols = slice(side * 128, side * 128 + 128)
                    grad = p_ref[head, rows, lanes].astype(jnp.float32) * (
                        pulls[rows, cols] - shift
                    )
                    s_ref[head, rows, lanes] = grad.astype(jnp.bfloat16)
                    apart = query_block - key_block
                    if apart >= 2:
                        far_low = far_low + jnp.sum(grad.reshape(16, 8, 128), axis=0)
                    elif apart <= -2:
                        far_high = far_high + jnp.sum(grad.reshape(16, 8, 128), axis=0)
                    else:
                        near_ref[head, :, 128 * (apart + 1) : 128 * (apart + 2)] += grad
        g_ref[own, :LEN] = dot_nt(low_t[own, :], p_ref[head])
        g_ref[own, LEN:] = dot_nt(q_t[own, :], s_ref[head]) * SCORE_SCALE
        da_t[own, :] = dot_nn(keys_t[own, :], s_ref[head])
        turned = jnp.dot(
            turn, near_ref[head], precision=lax.Precision.HIGHEST, preferred_element_type=jnp.float32
        )
        aligned = pltpu.roll(turned, 0, 1, stride=1, stride_axis=0)
        table_ref[head, :, :512] = jnp.sum(aligned, axis=0, keepdims=True)
        table_ref[head, :, 512:640] = jnp.sum(far_low, axis=0, keepdims=True)
        table_ref[head, :, 640:] = jnp.sum(far_high, axis=0, keepdims=True)
    uniform = dot_nn(dead_ref[...].astype(jnp.bfloat16), da_ref[...])
    dv_ref[...] = (g_ref[:, :LEN].T + uniform).astype(jnp.bfloat16)
    dk_ref[...] = g_ref[:, LEN:].T.astype(jnp.bfloat16)
    dq_ref[...] = da_t[...].T.astype(jnp.bfloat16)


def mix_back(first, q, k, v, da, a, p, inverse, dead, held=()):
    tall = pl.BlockSpec((TALL, 128), lambda i: (0, i + first))
    short = pl.BlockSpec((LEN, 128), lambda i: (0, i + first))
    return pl.pallas_call(
        mix_back_kernel,
        grid=(H // 4,),
        out_shape=[
            jax.ShapeDtypeStruct((TALL, D), jnp.bfloat16),
            jax.ShapeDtypeStruct((LEN, D), jnp.bfloat16),
            jax.ShapeDtypeStruct((LEN, D), jnp.bfloat16),
            jax.ShapeDtypeStruct((H // 2, 1, 768), jnp.float32),
        ],
        in_specs=[
            tall, short, short, tall, tall,
            pl.BlockSpec((2, LEN, TALL), lambda i: (i + first, 0, 0)),
            pl.BlockSpec((2, 1, TALL), lambda i: (i + first, 0, 0)),
            pl.BlockSpec((1, TALL), lambda i: (0, 0)),
        ]
        + [ANY_SPEC] * len(held),
        out_specs=[tall, short, short, pl.BlockSpec((2, 1, 768), lambda i: (i, 0, 0))],
        input_output_aliases={8 + index: index for index in range(len(held))},
        scratch_shapes=[
            pltpu.VMEM((2, LEN, TALL), jnp.bfloat16),
            pltpu.VMEM((2, 128, 512), jnp.float32),
            pltpu.VMEM((128, TALL), jnp.float32),
            pltpu.VMEM((128, TALL), jnp.bfloat16),
            pltpu.VMEM((128, TALL), jnp.bfloat16),
            pltpu.VMEM((128, TALL), jnp.float32),
        ],
        compiler_params=PARAMS,
        cost_estimate=pl.CostEstimate(flops=8000000000, bytes_accessed=16000000, transcendentals=0),
        name="mix_back",
    )(q, k, v, da, a, p, inverse, dead, *held)


GELU_SCALE = 0.7978845608028654
GELU_CUBE = 0.044715


def feed_rows(rows, small_ref, hidden_bias_ref, resid, normed_ref, pre_ref, inner_ref, outer_ref):
    unit, scale = norm_parts(resid)
    normed = unit * small_ref[3:4, :] + small_ref[4:5, :]
    low = normed.astype(jnp.bfloat16)
    normed_ref[rows, :] = low
    total = normed + small_ref[5:6, :]
    for chunk in range(4):
        pre = dot_nn(low, inner_ref[chunk]) + hidden_bias_ref[:, chunk * D : chunk * D + D]
        pre_ref[chunk, rows, :] = pre.astype(jnp.bfloat16)
        tanh = jnp.tanh(GELU_SCALE * (pre + GELU_CUBE * (pre * pre * pre)))
        active = (pre * (0.5 + 0.5 * tanh)).astype(jnp.bfloat16)
        total = total + dot_nn(active, outer_ref[chunk])
    return total


def norm_two_back(unit, scale, grad, small_ref, sums):
    back = norm_back(unit, scale, grad, small_ref[6:7, :])
    low = back.astype(jnp.bfloat16)
    parts = (low.astype(jnp.float32), grad * unit, grad)
    return back, low, [
        total + jnp.sum(part, axis=0, keepdims=True) for total, part in zip(sums, parts)
    ]


def issue(pairs, sems, first=0):
    copies = [
        pltpu.make_async_copy(source, target, sems.at[first + index])
        for index, (source, target) in enumerate(pairs)
    ]
    for copy in copies:
        copy.start()
    return copies


def finish(copies):
    for copy in copies:
        copy.wait()


def storer(sems):
    copies = []

    def store(source, target):
        copy = pltpu.make_async_copy(source, target, sems.at[len(copies)])
        copy.start()
        copies.append(copy)

    return store, copies


def feed_kernel(
    plan, place_ref, small_ref, hidden_bias_ref, mix_any, hidden_any, attn_any, *refs
):
    (
        resid_out, pre_out, normed_out, low_out, summed_out,
        mix_ref, hidden_ref, wo_ref, inner_ref, outer_ref, resid_ref, total_ref, normed_ref,
        pre_ref, low_ref, sems, load_sems, store_sems,
    ) = refs[-18:]
    finish(
        issue(
            ((mix_any, mix_ref), (attn_any.at[3], wo_ref), (hidden_any, hidden_ref)), load_sems
        )
    )
    fetches = start_fetch(
        ("inner", "outer"), plan, place_ref, refs[:-18], (inner_ref, outer_ref), sems
    )
    for row in range(0, TALL, HALF):
        rows = slice(row, row + HALF)
        resid_ref[rows, :] = (
            hidden_ref[rows, :].astype(jnp.float32)
            + dot_nn(mix_ref[rows, :], wo_ref[...])
            + small_ref[2:3, :]
        )
    finish(fetches)
    store, stores = storer(store_sems)
    store(resid_ref, resid_out)
    for row in range(0, TALL, HALF):
        rows = slice(row, row + HALF)
        total = feed_rows(
            rows, small_ref, hidden_bias_ref, resid_ref[rows, :], normed_ref, pre_ref, inner_ref,
            outer_ref,
        )
        total_ref[rows, :] = total
        store(pre_ref.at[:, rows, :], pre_out.at[:, rows, :])
        store(total_ref.at[rows, :], summed_out.at[rows, :])
        store(normed_ref.at[rows, :], normed_out.at[rows, :])
        unit, scale = norm_parts(total)
        following = unit * small_ref[6:7, :] + small_ref[7:8, :]
        low_ref[rows, :] = following.astype(jnp.bfloat16)
        store(low_ref.at[rows, :], low_out.at[rows, :])
    finish(stores)


def feed(place, small, hidden_bias, mixed, hidden, attn, group):
    plan, pieces = group
    tall = jax.ShapeDtypeStruct((TALL, D), jnp.float32)
    tall_low = jax.ShapeDtypeStruct((TALL, D), jnp.bfloat16)
    return pl.pallas_call(
        partial(feed_kernel, plan),
        out_shape=[
            tall, jax.ShapeDtypeStruct((4, TALL, D), jnp.bfloat16), tall_low, tall_low, tall
        ],
        in_specs=[SMEM_SPEC, VMEM_SPEC, VMEM_SPEC] + [ANY_SPEC] * (3 + len(pieces)),
        out_specs=[ANY_SPEC] * 5,
        scratch_shapes=[
            pltpu.VMEM((TALL, D), jnp.bfloat16),
            pltpu.VMEM((TALL, D), jnp.bfloat16),
            pltpu.VMEM((D, D), jnp.bfloat16),
            pltpu.VMEM((4, D, D), jnp.bfloat16),
            pltpu.VMEM((4, D, D), jnp.bfloat16),
            pltpu.VMEM((TALL, D), jnp.float32),
            pltpu.VMEM((TALL, D), jnp.float32),
            pltpu.VMEM((TALL, D), jnp.bfloat16),
            pltpu.VMEM((4, TALL, D), jnp.bfloat16),
            pltpu.VMEM((TALL, D), jnp.bfloat16),
            pltpu.SemaphoreType.DMA((64,)),
            pltpu.SemaphoreType.DMA((3,)),
            pltpu.SemaphoreType.DMA((17,)),
        ],
        compiler_params=PARAMS,
        cost_estimate=pl.CostEstimate(flops=2 * TALL * D * (D + 2 * FF), bytes_accessed=30000000, transcendentals=3000000),
        name="feed",
    )(place, small, hidden_bias, mixed, hidden, attn, *pieces)


def back_steps(
    place_ref, small_ref, before, store, outs, vec_ref, dhidden_ref, branch_ref, total_ref,
    normed_ref, resid_ref, pre_ref, mix_ref, wo_ref, inner_ref, outer_ref, active_ref, dpre_ref,
    dinner_ref, douter_ref, dwo_ref,
):
    dresid_out, dmix_out, dwo_out, keep_out, send_out = outs
    x, c, z, y = (place_ref[index] for index in range(4))
    order = [(1 - step // 2, step % 2) for step in range(4)]
    chunks = [side * 2 + (c ^ apart) for apart, side in order]
    sums = [jnp.zeros((1, D), jnp.float32)] * 3
    for step in range(4):
        apart, side = order[step]
        chunk = chunks[step]
        before(step)
        bias_grad = jnp.zeros((1, D), jnp.float32)
        for row in range(0, TALL, HALF):
            rows = slice(row, row + HALF)
            pull = dot_nt(branch_ref[rows, :], outer_ref[chunk])
            pre = pre_ref[chunk, rows, :].astype(jnp.float32)
            square = pre * pre
            tanh = jnp.tanh(GELU_SCALE * pre * (1.0 + GELU_CUBE * square))
            half = 0.5 + 0.5 * tanh
            active_ref[rows, :] = (pre * half).astype(jnp.bfloat16)
            slope = half + (0.5 * GELU_SCALE) * pre * (1.0 - tanh * tanh) * (
                1.0 + (3.0 * GELU_CUBE) * square
            )
            dpre = (pull * slope).astype(jnp.bfloat16)
            dpre_ref[rows, :] = dpre
            bias_grad += jnp.sum(dpre.astype(jnp.float32), axis=0, keepdims=True)
            grad = total_ref[rows, :] + dot_nt(dpre, inner_ref[chunk])
            if step < 3:
                total_ref[rows, :] = grad
            else:
                unit, scale = norm_parts(resid_ref[rows, :])
                back = norm_back(unit, scale, grad, small_ref[3:4, :])
                resid_ref[rows, :] = back
                low = back.astype(jnp.bfloat16)
                pre_ref[chunks[0], rows, :] = low
                pre_ref[chunks[1], rows, :] = dot_nt(low, wo_ref[...]).astype(jnp.bfloat16)
                parts = (low.astype(jnp.float32), grad * unit, grad)
                sums = [
                    value + jnp.sum(part, axis=0, keepdims=True)
                    for value, part in zip(sums, parts)
                ]
        dhidden_ref[chunk] = bias_grad
        if step == 3:
            store(resid_ref, dresid_out)
            store(pre_ref.at[chunks[1]], dmix_out)
        douter_ref[step] = (
            dot_tn(active_ref[...], branch_ref[...]).astype(jnp.bfloat16).reshape(2, 2, 2, ROWS, D)
        )
        for y_block in range(2):
            for x_block in range(2):
                spot = (y_block ^ y, x_block ^ x, chunk, 1)
                store(douter_ref.at[step, y_block, x_block, c], keep_out.at[spot])
                store(douter_ref.at[step, y_block, x_block, 1 - c], send_out.at[spot])
        dinner_ref[step] = (
            dot_tn(normed_ref[...], dpre_ref[...]).astype(jnp.bfloat16).reshape(4, 2, ROWS, D)
        )
        target = send_out if apart else keep_out
        for y_block in range(2):
            store(dinner_ref.at[step, :, y_block], target.at[y_block ^ y, side ^ x, :, 0])
    dwo_ref[...] = dot_tn(mix_ref[...], pre_ref[chunks[0]]).astype(jnp.bfloat16)
    store(dwo_ref, dwo_out)
    for index, value in enumerate(sums):
        vec_ref[index : index + 1, :] = value


BACK_SHAPES = [
    jax.ShapeDtypeStruct((TALL, D), jnp.float32),
    jax.ShapeDtypeStruct((TALL, D), jnp.bfloat16),
    jax.ShapeDtypeStruct((D, D), jnp.bfloat16),
    jax.ShapeDtypeStruct((2, 2, 4, 2, ROWS, D), jnp.bfloat16),
    jax.ShapeDtypeStruct((2, 2, 4, 2, ROWS, D), jnp.bfloat16),
    jax.ShapeDtypeStruct((6, D), jnp.float32),
    jax.ShapeDtypeStruct((4, 1, D), jnp.float32),
]
BACK_SCRATCH = [
    pltpu.VMEM((TALL, D), jnp.bfloat16),
    pltpu.VMEM((TALL, D), jnp.float32),
    pltpu.VMEM((TALL, D), jnp.bfloat16),
    pltpu.VMEM((TALL, D), jnp.float32),
    pltpu.VMEM((4, TALL, D), jnp.bfloat16),
    pltpu.VMEM((TALL, D), jnp.bfloat16),
    pltpu.VMEM((D, D), jnp.bfloat16),
    pltpu.VMEM((4, D, D), jnp.bfloat16),
    pltpu.VMEM((4, D, D), jnp.bfloat16),
    pltpu.VMEM((TALL, D), jnp.bfloat16),
    pltpu.VMEM((TALL, D), jnp.bfloat16),
    pltpu.VMEM((4, 4, 2, ROWS, D), jnp.bfloat16),
    pltpu.VMEM((4, 2, 2, 2, ROWS, D), jnp.bfloat16),
    pltpu.VMEM((D, D), jnp.bfloat16),
    pltpu.SemaphoreType.DMA((64,)),
    pltpu.SemaphoreType.DMA((16,)),
    pltpu.SemaphoreType.DMA((48,)),
]


def turn_kernel(
    plan, place_ref, length_ref, small_ref, below_ref, hidden_bias_ref, mix_any, summed_any,
    attn_any, cot_c_any, cot_q_any, *refs
):
    content_out, query_out = refs[-27:-25]
    outs = refs[-25:-20]
    vec_ref, dhidden_ref = refs[-20:-18]
    low_ref = refs[-18]
    (
        branch_ref, total_ref, normed_ref, resid_ref, pre_ref, mix_ref, wo_ref, inner_ref,
        outer_ref, active_ref, dpre_ref, dinner_ref, douter_ref, dwo_ref,
        sems, load_sems, store_sems,
    ) = refs[-17:]
    store, stores = storer(store_sems)
    finish(
        issue(
            ((mix_any, mix_ref), (attn_any.at[3], wo_ref), (summed_any, resid_ref)), load_sems
        )
    )
    fetches = start_fetch(
        ("inner", "outer"), plan, place_ref, refs[:-27], (inner_ref, outer_ref), sems
    )
    fetches += issue(
        ((cot_c_any, low_ref.at[:LEN, :]), (cot_q_any, low_ref.at[LEN:, :])), load_sems, 3
    )
    for row in range(0, TALL, HALF):
        rows = slice(row, row + HALF)
        unit, scale = norm_parts(resid_ref[rows, :])
        resid_ref[rows, :] = (
            unit * below_ref[6:7, :]
            + below_ref[7:8, :]
            + dot_nn(mix_ref[rows, :], wo_ref[...])
            + small_ref[2:3, :]
        )
    finish(fetches)
    sums = [jnp.zeros((1, D), jnp.float32)] * 3
    for row in range(0, TALL, HALF):
        rows = slice(row, row + HALF)
        total = feed_rows(
            rows, small_ref, hidden_bias_ref, resid_ref[rows, :], normed_ref, pre_ref, inner_ref,
            outer_ref,
        )
        unit, scale = norm_parts(total)
        position = lax.broadcasted_iota(jnp.int32, (HALF, 1), 0) + row % LEN
        valid = (position < length_ref[0]).astype(jnp.float32)
        grad = low_ref[rows, :].astype(jnp.float32) * valid
        low_ref[rows, :] = (unit * small_ref[6:7, :] + small_ref[7:8, :]).astype(jnp.bfloat16)
        total_ref[rows, :], branch_ref[rows, :], sums = norm_two_back(
            unit, scale, grad, small_ref, sums
        )
    store(low_ref.at[:LEN, :], content_out)
    store(low_ref.at[LEN:, :], query_out)
    for index, value in enumerate(sums):
        vec_ref[3 + index : 4 + index, :] = value
    back_steps(
        place_ref, small_ref, lambda step: None, store, outs, vec_ref, dhidden_ref, branch_ref,
        total_ref, normed_ref, resid_ref, pre_ref, mix_ref, wo_ref, inner_ref, outer_ref,
        active_ref, dpre_ref, dinner_ref, douter_ref, dwo_ref,
    )
    finish(stores)


def turn(place, length, small, below, hidden_bias, mixed, summed, attn, cots, group):
    plan, pieces = group
    half_low = jax.ShapeDtypeStruct((LEN, D), jnp.bfloat16)
    return pl.pallas_call(
        partial(turn_kernel, plan),
        out_shape=[half_low, half_low] + BACK_SHAPES,
        in_specs=[SMEM_SPEC] * 2 + [VMEM_SPEC] * 3 + [ANY_SPEC] * (5 + len(pieces)),
        out_specs=[ANY_SPEC] * 7 + [VMEM_SPEC] * 2,
        scratch_shapes=[pltpu.VMEM((TALL, D), jnp.bfloat16)] + BACK_SCRATCH,
        compiler_params=PARAMS,
        cost_estimate=pl.CostEstimate(flops=6 * TALL * D * (D + 2 * FF), bytes_accessed=60000000, transcendentals=6000000),
        name="turn",
    )(place, length, small, below, hidden_bias, mixed, summed, attn, *cots, *pieces)


def down_kernel(
    plan, place_ref, small_ref, dq_any, dk_any, dv_any, w_any, dresid_any, summed_any,
    normed_any, resid_any, pre_any, mix_any, attn_any, *refs
):
    outs = refs[-29:-24]
    vec_ref, dhidden_ref = refs[-24:-22]
    dq_ref, dk_ref, dv_ref, w_ref, summed_ref = refs[-22:-17]
    (
        branch_ref, total_ref, normed_ref, resid_ref, pre_ref, mix_ref, wo_ref, inner_ref,
        outer_ref, active_ref, dpre_ref, dinner_ref, douter_ref, dwo_ref,
        sems, load_sems, store_sems,
    ) = refs[-17:]
    x, c, z, y = (place_ref[index] for index in range(4))
    chunks = [side * 2 + (c ^ apart) for apart in (1, 0) for side in range(2)]
    store, stores = storer(store_sems)
    loads = issue(
        (
            (w_any.at[0], w_ref.at[0]), (dq_any, dq_ref), (dresid_any, total_ref),
            (summed_any, summed_ref), (w_any.at[1:3], w_ref.at[1:3]), (dk_any, dk_ref),
            (dv_any, dv_ref),
        ),
        load_sems,
    )
    finish(loads[:4])
    fetches = start_fetch(
        ("inner", "outer"), plan, place_ref, refs[:-29], (inner_ref, outer_ref), sems
    )
    fetches += issue(((pre_any.at[chunks[0]], pre_ref.at[chunks[0]]),), load_sems, 7)
    sums = [jnp.zeros((1, D), jnp.float32)] * 3
    for index, row in enumerate((LEN, LEN + HALF, 0, HALF)):
        rows = slice(row, row + HALF)
        if index == 2:
            finish(loads[4:])
        total = total_ref[rows, :] + dot_nt(dq_ref[rows, :], w_ref[0])
        if index >= 2:
            total = total + dot_nt(dk_ref[rows, :], w_ref[1]) + dot_nt(dv_ref[rows, :], w_ref[2])
        unit, scale = norm_parts(summed_ref[rows, :])
        total_ref[rows, :], branch_ref[rows, :], sums = norm_two_back(
            unit, scale, total, small_ref, sums
        )
    for index, value in enumerate(sums):
        vec_ref[3 + index : 4 + index, :] = value
    finish(fetches)
    late = []

    def before(step):
        if step == 0:
            late.append(issue(((normed_any, normed_ref),), load_sems, 8))
        else:
            finish(late.pop())
        if step < 3:
            chunk = chunks[step + 1]
            late.insert(0, issue(((pre_any.at[chunk], pre_ref.at[chunk]),), load_sems, 9 + step))
        if step == 0:
            finish(late.pop())
        if step == 2:
            late[0].extend(
                issue(
                    ((resid_any, resid_ref), (mix_any, mix_ref), (attn_any.at[3], wo_ref)),
                    load_sems,
                    12,
                )
            )

    back_steps(
        place_ref, small_ref, before, store, outs, vec_ref, dhidden_ref, branch_ref, total_ref,
        normed_ref, resid_ref, pre_ref, mix_ref, wo_ref, inner_ref, outer_ref, active_ref,
        dpre_ref, dinner_ref, douter_ref, dwo_ref,
    )
    finish(stores)


def down(place, small, dq, dk, dv, w_above, dresid, summed, normed, resid, pre, mixed, attn, group):
    plan, pieces = group
    return pl.pallas_call(
        partial(down_kernel, plan),
        out_shape=BACK_SHAPES,
        in_specs=[SMEM_SPEC, VMEM_SPEC] + [ANY_SPEC] * (11 + len(pieces)),
        out_specs=[ANY_SPEC] * 5 + [VMEM_SPEC] * 2,
        scratch_shapes=[
            pltpu.VMEM((TALL, D), jnp.bfloat16),
            pltpu.VMEM((LEN, D), jnp.bfloat16),
            pltpu.VMEM((LEN, D), jnp.bfloat16),
            pltpu.VMEM((3, D, D), jnp.bfloat16),
            pltpu.VMEM((TALL, D), jnp.float32),
        ]
        + BACK_SCRATCH,
        compiler_params=PARAMS,
        cost_estimate=pl.CostEstimate(flops=5 * TALL * D * (D + 2 * FF), bytes_accessed=60000000, transcendentals=3000000),
        name="down",
    )(place, small, dq, dk, dv, w_above, dresid, summed, normed, resid, pre, mixed, attn, *pieces)


def weight_back_kernel(
    place_ref, low_any, dq_any, dk_any, dv_any, dwo_any, keep_out, send_out, vec_ref,
    low_ref, dq_ref, dk_ref, dv_ref, dwo_ref, grads_ref, load_sems, sems,
):
    x, c, z, y = (place_ref[index] for index in range(4))
    load = [
        pltpu.make_async_copy(source, target, load_sems.at[index])
        for index, (source, target) in enumerate(
            (
                (low_any.at[:LEN, :], low_ref.at[:LEN, :]), (dk_any, dk_ref), (dv_any, dv_ref),
                (low_any.at[LEN:, :], low_ref.at[LEN:, :]), (dq_any, dq_ref), (dwo_any, dwo_ref),
            )
        )
    ]
    for copy in load:
        copy.start()
    load[0].wait()
    load[1].wait()
    grads_ref[1] = (
        dot_tn(low_ref[:LEN, :], dk_ref[...]).astype(jnp.bfloat16).reshape(4, 2, ROWS, D)
    )
    load[2].wait()
    grads_ref[2] = (
        dot_tn(low_ref[:LEN, :], dv_ref[...]).astype(jnp.bfloat16).reshape(4, 2, ROWS, D)
    )
    vec_ref[1:2, :] = jnp.sum(dv_ref[...].astype(jnp.float32), axis=0, keepdims=True)
    for copy in load[3:]:
        copy.wait()
    grads_ref[3] = dwo_ref[...].reshape(4, 2, ROWS, D)
    grads_ref[0] = dot_tn(low_ref[...], dq_ref[...]).astype(jnp.bfloat16).reshape(4, 2, ROWS, D)
    vec_ref[0:1, :] = jnp.sum(dq_ref[...].astype(jnp.float32), axis=0, keepdims=True)
    blocks = []
    for apart, target in ((1, send_out), (0, keep_out)):
        for side in range(2):
            for y_block in range(2):
                copy = pltpu.make_async_copy(
                    grads_ref.at[side * 2 + (c ^ apart), :, y_block],
                    target.at[y_block ^ y, side ^ x, :, 0],
                    sems.at[len(blocks)],
                )
                copy.start()
                blocks.append(copy)
    for block in blocks:
        block.wait()


def weight_back(place, low, dq, dk, dv, dwo):
    blocks = jax.ShapeDtypeStruct((2, 2, 4, 1, ROWS, D), jnp.bfloat16)
    return pl.pallas_call(
        weight_back_kernel,
        out_shape=[blocks, blocks, jax.ShapeDtypeStruct((2, D), jnp.float32)],
        in_specs=[SMEM_SPEC] + [ANY_SPEC] * 5,
        out_specs=[ANY_SPEC] * 2 + [VMEM_SPEC],
        scratch_shapes=[
            pltpu.VMEM((TALL, D), jnp.bfloat16),
            pltpu.VMEM((TALL, D), jnp.bfloat16),
            pltpu.VMEM((LEN, D), jnp.bfloat16),
            pltpu.VMEM((LEN, D), jnp.bfloat16),
            pltpu.VMEM((D, D), jnp.bfloat16),
            pltpu.VMEM((4, 4, 2, ROWS, D), jnp.bfloat16),
            pltpu.SemaphoreType.DMA((6,)),
            pltpu.SemaphoreType.DMA((8,)),
        ],
        compiler_params=PARAMS,
        cost_estimate=pl.CostEstimate(flops=2 * 2048 * D * D, bytes_accessed=12000000, transcendentals=0),
        name="weight_back",
    )(place, low, dq, dk, dv, dwo)


def input_back_kernel(
    dq_any, dk_any, dv_any, w_any, dresid_any, first_out, second_out,
    dq_ref, dk_ref, dv_ref, w_ref, dresid_ref, load_sems, store_sems,
):
    loads = issue(
        (
            (w_any.at[0], w_ref.at[0]), (dq_any, dq_ref), (dresid_any, dresid_ref),
            (w_any.at[1:3], w_ref.at[1:3]), (dk_any, dk_ref), (dv_any, dv_ref),
        ),
        load_sems,
    )
    finish(loads[:3])
    store, stores = storer(store_sems)
    for index, row in enumerate((LEN, LEN + HALF, 0, HALF)):
        rows = slice(row, row + HALF)
        if index == 2:
            finish(loads[3:])
        total = dresid_ref[rows, :] + dot_nt(dq_ref[rows, :], w_ref[0])
        if index >= 2:
            total = total + dot_nt(dk_ref[rows, :], w_ref[1]) + dot_nt(dv_ref[rows, :], w_ref[2])
        dresid_ref[rows, :] = total
        target = first_out if index >= 2 else second_out
        store(dresid_ref.at[rows, :], target.at[row % LEN : row % LEN + HALF, :])
    finish(stores)


def input_back(dq, dk, dv, attn, dresid):
    half = jax.ShapeDtypeStruct((LEN, D), jnp.float32)
    return pl.pallas_call(
        input_back_kernel,
        out_shape=[half, half],
        in_specs=[ANY_SPEC] * 5,
        out_specs=[ANY_SPEC] * 2,
        scratch_shapes=[
            pltpu.VMEM((TALL, D), jnp.bfloat16),
            pltpu.VMEM((LEN, D), jnp.bfloat16),
            pltpu.VMEM((LEN, D), jnp.bfloat16),
            pltpu.VMEM((3, D, D), jnp.bfloat16),
            pltpu.VMEM((TALL, D), jnp.float32),
            pltpu.SemaphoreType.DMA((6,)),
            pltpu.SemaphoreType.DMA((4,)),
        ],
        compiler_params=PARAMS,
        cost_estimate=pl.CostEstimate(flops=2 * 2048 * D * D, bytes_accessed=16000000, transcendentals=0),
        name="input_back",
    )(dq, dk, dv, attn, dresid)


def bias_vectors(table):
    lane = jnp.arange(512, dtype=jnp.int32)
    offset = jnp.where(lane < 384, 128 - lane, 640 - lane)
    onehot = bucket_of(offset)[:, None] == jnp.arange(NB, dtype=jnp.int32)[None, :]
    near = jnp.dot(table, onehot.astype(jnp.float32).T, precision=lax.Precision.HIGHEST)
    return (near[:, None, :], jnp.stack([table[:, 15], table[:, 31]], axis=1), onehot)


def bucket_of(offset):
    distance = jnp.abs(offset)
    far_bucket = jnp.full(distance.shape, 8, jnp.int32)
    for exponent in range(1, 8):
        far_bucket = far_bucket + (distance * distance >= 64 * 2**exponent).astype(jnp.int32)
    near_or_far = jnp.where(distance < 8, distance, far_bucket)
    return near_or_far + NB // 2 * (offset > 0).astype(jnp.int32)


def table_grad(sums, onehot):
    near = jnp.roll(onehot.astype(jnp.float32), 127, axis=0)
    far = jnp.arange(NB, dtype=jnp.int32)[None, :] == jnp.repeat(jnp.array([15, 31]), 128)[:, None]
    return jnp.dot(
        sums[:, 0, :],
        jnp.concatenate([near, far.astype(jnp.float32)]),
        precision=lax.Precision.HIGHEST,
    )


RATES = (ATTENTION_RATE, FEED_RATE, FEED_RATE)


def adam_kernel(*refs):
    states, grads, outs = refs[:9], refs[9:12], refs[-9:]
    for kind, rate in enumerate(RATES):
        master_ref, first_ref, second_ref = states[3 * kind : 3 * kind + 3]
        master_out, first_out, second_out = outs[3 * kind : 3 * kind + 3]
        grad = grads[kind][...].astype(jnp.float32).reshape(master_ref.shape)
        master = master_ref[...]
        first = BETA_ONE * first_ref[...] + (1.0 - BETA_ONE) * grad
        second = BETA_TWO * second_ref[...] + (1.0 - BETA_TWO) * grad * grad
        first_out[...] = first
        second_out[...] = second
        first_scale = rate / (1.0 - BETA_ONE**STEP)
        second_scale = 1.0 / (1.0 - BETA_TWO**STEP)
        step = (first_scale * first) / (jnp.sqrt(second_scale * second) + ADAM_EPS)
        master_out[...] = master - (step + (rate * WEIGHT_DECAY) * master)


def adam(layer, state, quarters, held):
    half = ROWS // 2
    blocks = (
        [pl.BlockSpec((1, 1, half, D), lambda i: (layer, i // 2, i % 2, 0))] * 3
        + [pl.BlockSpec((1, half, D), lambda i: (layer, i % 2, i // 2))] * 3
        + [pl.BlockSpec((1, half, D), lambda i: (layer, i, 0))] * 3
    )
    grads = [
        pl.BlockSpec((1, 1, half, D), partial(lambda member, i: (i // 2, member, i % 2, 0), member))
        for member in (2, 0, 1)
    ]
    return pl.pallas_call(
        adam_kernel,
        grid=(8,),
        out_shape=[jax.ShapeDtypeStruct(array.shape, jnp.float32) for array in state],
        in_specs=blocks + grads + [ANY_SPEC] * len(held),
        out_specs=blocks,
        input_output_aliases={12 + index: index for index in range(len(held))},
        compiler_params=PARAMS,
        cost_estimate=pl.CostEstimate(flops=20000000, bytes_accessed=22000000, transcendentals=0),
        name="adam",
    )(*state, quarters, quarters, quarters, *held)


def fetch_forward(shards):
    low = tuple(shard.astype(jnp.bfloat16) for shard in shards)
    return (
        lax.all_gather(low[0], "fsdp", axis=1, tiled=True),
        lax.all_gather(low[1], "fsdp", axis=0, tiled=True),
        lax.all_gather(low[2], "fsdp", axis=0, tiled=True),
    )


def reduce_layer(grads):
    owned = tuple(
        lax.psum_scatter(
            grad.astype(jnp.bfloat16), "fsdp", scatter_dimension=axis, tiled=True
        ).astype(jnp.float32)
        for grad, axis in zip(grads, (1, 0, 0))
    )
    return lax.psum(owned, "dp")


def forward_layer(hidden_c, hidden_q, weights, lengths, flag_rows, onehot):
    attn_w, inner_w, outer_w, small_w = weights
    pieces, hidden_bias, bias_table = unpack(small_w.astype(jnp.float32))
    bias_q, bias_v, bias_o, gain_one, shift_one, bias_two, gain_two, shift_two = pieces
    table_low = bias_table.astype(jnp.bfloat16)
    low_c = hidden_c.astype(jnp.bfloat16)
    low_q = hidden_q.astype(jnp.bfloat16)
    projected = jnp.einsum("td,sde->ste", low_c, attn_w[:3], preferred_element_type=jnp.float32)
    query_c = (projected[0] + bias_q).astype(jnp.bfloat16)
    key_rows = projected[1].astype(jnp.bfloat16)
    value_rows = (projected[2] + bias_v).astype(jnp.bfloat16)
    query_q = (jnp.dot(low_q, attn_w[0], preferred_element_type=jnp.float32) + bias_q).astype(
        jnp.bfloat16
    )
    mixed_c, mixed_q, lse_c, lse_q = lax.map(
        partial(attend_slot, onehot, table_low),
        (
            to_heads(query_c),
            to_heads(query_q),
            to_heads(key_rows),
            to_heads(value_rows),
            lengths,
            flag_rows,
        ),
    )
    mixed_c = mixed_c.reshape(-1, D)
    mixed_q = mixed_q.reshape(-1, D)
    outputs = []
    kept = []
    for hidden_in, mixed in ((hidden_c, mixed_c), (hidden_q, mixed_q)):
        resid = hidden_in + jnp.dot(mixed, attn_w[3], preferred_element_type=jnp.float32) + bias_o
        normed = layer_norm(resid, gain_one, shift_one)
        pre_act = (
            jnp.dot(normed.astype(jnp.bfloat16), inner_w, preferred_element_type=jnp.float32)
            + hidden_bias
        )
        active = jax.nn.gelu(pre_act, approximate=True).astype(jnp.bfloat16)
        summed = normed + jnp.dot(active, outer_w, preferred_element_type=jnp.float32) + bias_two
        outputs.append(layer_norm(summed, gain_two, shift_two))
        kept.append((resid, summed, pre_act))
    saved = (
        hidden_c,
        hidden_q,
        query_c,
        query_q,
        key_rows,
        value_rows,
        lse_c,
        lse_q,
        mixed_c,
        mixed_q,
        kept[0],
        kept[1],
    )
    return (outputs[0], outputs[1], saved)


def backward_layer(saved, weights, grad_c, grad_q, lengths, flag_rows, onehot):
    attn_w, inner_w, outer_w, small_w = weights
    pieces, hidden_bias, bias_table = unpack(small_w.astype(jnp.float32))
    bias_q, bias_v, bias_o, gain_one, shift_one, bias_two, gain_two, shift_two = pieces
    table_low = bias_table.astype(jnp.bfloat16)
    (
        hidden_c,
        hidden_q,
        query_c,
        query_q,
        key_rows,
        value_rows,
        lse_c,
        lse_q,
        mixed_c,
        mixed_q,
        kept_c,
        kept_q,
    ) = saved
    gelu_tanh = partial(jax.nn.gelu, approximate=True)
    grad_outer = jnp.zeros(outer_w.shape, jnp.float32)
    grad_inner = jnp.zeros(inner_w.shape, jnp.float32)
    grad_attn_out = jnp.zeros((D, D), jnp.float32)
    grad_bias_two = jnp.zeros((D,), jnp.float32)
    grad_hidden_bias = jnp.zeros((FF,), jnp.float32)
    grad_bias_o = jnp.zeros((D,), jnp.float32)
    grad_gain_one = jnp.zeros((D,), jnp.float32)
    grad_shift_one = jnp.zeros((D,), jnp.float32)
    grad_gain_two = jnp.zeros((D,), jnp.float32)
    grad_shift_two = jnp.zeros((D,), jnp.float32)
    residual_grads = []
    mix_grads = []
    for kept_rows, grad_out, mixed in ((kept_c, grad_c, mixed_c), (kept_q, grad_q, mixed_q)):
        resid, summed, pre_act = kept_rows
        normed, norm_one_back = jax.vjp(layer_norm, resid, gain_one, shift_one)
        unused_out, norm_two_back = jax.vjp(layer_norm, summed, gain_two, shift_two)
        grad_summed, grad_g2, grad_s2 = norm_two_back(grad_out)
        grad_gain_two = grad_gain_two + grad_g2
        grad_shift_two = grad_shift_two + grad_s2
        grad_branch = grad_summed.astype(jnp.bfloat16)
        grad_bias_two = grad_bias_two + jnp.sum(grad_branch.astype(jnp.float32), axis=0)
        active, gelu_back = jax.vjp(gelu_tanh, pre_act)
        grad_outer = grad_outer + jnp.einsum(
            "tf,td->fd",
            active.astype(jnp.bfloat16),
            grad_branch,
            preferred_element_type=jnp.float32,
        )
        grad_active = jnp.einsum(
            "td,fd->tf", grad_branch, outer_w, preferred_element_type=jnp.float32
        )
        grad_pre = gelu_back(grad_active)[0].astype(jnp.bfloat16)
        grad_hidden_bias = grad_hidden_bias + jnp.sum(grad_pre.astype(jnp.float32), axis=0)
        grad_inner = grad_inner + jnp.einsum(
            "td,tf->df", normed.astype(jnp.bfloat16), grad_pre, preferred_element_type=jnp.float32
        )
        grad_normed = grad_summed + jnp.einsum(
            "tf,df->td", grad_pre, inner_w, preferred_element_type=jnp.float32
        )
        grad_resid, grad_g1, grad_s1 = norm_one_back(grad_normed)
        grad_gain_one = grad_gain_one + grad_g1
        grad_shift_one = grad_shift_one + grad_s1
        grad_proj = grad_resid.astype(jnp.bfloat16)
        grad_bias_o = grad_bias_o + jnp.sum(grad_proj.astype(jnp.float32), axis=0)
        grad_attn_out = grad_attn_out + jnp.einsum(
            "td,te->de", mixed, grad_proj, preferred_element_type=jnp.float32
        )
        mix_grads.append(
            jnp.einsum(
                "te,de->td", grad_proj, attn_w[3], preferred_element_type=jnp.float32
            ).astype(jnp.bfloat16)
        )
        residual_grads.append(grad_resid)
    grad_query_c, grad_query_q, grad_keys, grad_values, grad_table = lax.map(
        partial(attend_back, onehot, table_low),
        (
            to_heads(query_c),
            to_heads(query_q),
            to_heads(key_rows),
            to_heads(value_rows),
            lengths,
            flag_rows,
            lse_c,
            lse_q,
            to_heads(mix_grads[0]),
            to_heads(mix_grads[1]),
        ),
    )
    grad_table = jnp.sum(grad_table, axis=0)
    low_query_c = grad_query_c.reshape(-1, D).astype(jnp.bfloat16)
    low_query_q = grad_query_q.reshape(-1, D).astype(jnp.bfloat16)
    low_keys = grad_keys.reshape(-1, D).astype(jnp.bfloat16)
    low_values = grad_values.reshape(-1, D).astype(jnp.bfloat16)
    low_c = hidden_c.astype(jnp.bfloat16)
    low_q = hidden_q.astype(jnp.bfloat16)
    stacked_grads = jnp.stack([low_query_c, low_keys, low_values])
    grad_qkv = jnp.einsum("td,ste->sde", low_c, stacked_grads, preferred_element_type=jnp.float32)
    grad_wq = grad_qkv[0] + jnp.einsum(
        "td,te->de", low_q, low_query_q, preferred_element_type=jnp.float32
    )
    grad_attn = jnp.stack([grad_wq, grad_qkv[1], grad_qkv[2], grad_attn_out])
    grad_bias_q = jnp.sum(low_query_c.astype(jnp.float32), axis=0) + jnp.sum(
        low_query_q.astype(jnp.float32), axis=0
    )
    grad_bias_v = jnp.sum(low_values.astype(jnp.float32), axis=0)
    grad_content = residual_grads[0] + jnp.einsum(
        "ste,sde->td", stacked_grads, attn_w[:3], preferred_element_type=jnp.float32
    )
    grad_query_in = residual_grads[1] + jnp.einsum(
        "te,de->td", low_query_q, attn_w[0], preferred_element_type=jnp.float32
    )
    grad_small = jnp.concatenate(
        [
            grad_bias_q,
            grad_bias_v,
            grad_bias_o,
            grad_gain_one,
            grad_shift_one,
            grad_bias_two,
            grad_gain_two,
            grad_shift_two,
            grad_hidden_bias,
            grad_table.reshape(-1),
        ]
    )
    return (grad_content, grad_query_in, (grad_attn, grad_inner, grad_outer, grad_small))


def adam_update(master, first, second, grad, rate):
    first_new = BETA_ONE * first + (1.0 - BETA_ONE) * grad
    second_new = BETA_TWO * second + (1.0 - BETA_TWO) * grad * grad
    first_hat = first_new / (1.0 - BETA_ONE**STEP)
    second_hat = second_new / (1.0 - BETA_TWO**STEP)
    master_new = master - rate * (
        first_hat / (jnp.sqrt(second_hat) + ADAM_EPS) + WEIGHT_DECAY * master
    )
    return (master_new, first_new, second_new)


def per_device(
    content,
    query,
    lengths,
    predicted,
    content_cot,
    query_cot,
    attn_master,
    attn_first,
    attn_second,
    inner_master,
    inner_first,
    inner_second,
    outer_master,
    outer_first,
    outer_second,
    small_master,
    small_first,
    small_second,
):
    masters = (attn_master, inner_master, outer_master, small_master)
    slot_count = lengths.shape[0]
    flag_rows = predicted.reshape(slot_count, LEN)
    onehot = bucket_onehot()
    hidden_c = content.astype(jnp.float32)
    hidden_q = query.astype(jnp.float32)
    kept_weights = []
    saved_layers = []
    small_all = lax.all_gather(
        small_master.astype(jnp.bfloat16), "fsdp", axis=1, tiled=True
    )
    for layer_index in range(LAYERS):
        shards = tuple((master[layer_index] for master in masters[:3]))
        gathered = fetch_forward(shards) + (small_all[layer_index],)
        kept_weights.append(gathered)
        hidden_c, hidden_q, saved = forward_layer(
            hidden_c, hidden_q, gathered, lengths, flag_rows, onehot
        )
        saved_layers.append(saved)
    position = jnp.arange(LEN, dtype=jnp.int32)
    valid_rows = (position[None, :] < lengths[:, None]).reshape(-1, 1).astype(jnp.float32)
    grad_c = content_cot.astype(jnp.float32) * valid_rows
    grad_q = query_cot.astype(jnp.float32) * valid_rows
    layer_grads = [None] * LAYERS
    small_grads = [None] * LAYERS
    for layer_index in reversed(range(LAYERS)):
        grad_c, grad_q, local_grads = backward_layer(
            saved_layers[layer_index],
            kept_weights[layer_index],
            grad_c,
            grad_q,
            lengths,
            flag_rows,
            onehot,
        )
        small_grads[layer_index] = local_grads[3]
        layer_grads[layer_index] = reduce_layer(local_grads[:3])
    small_sum = lax.psum(jnp.stack(small_grads), ("dp", "fsdp"))
    owned = small_master.shape[1]
    small_own = lax.dynamic_slice_in_dim(
        small_sum, lax.axis_index("fsdp") * owned, owned, 1
    )
    reduced = tuple(
        (
            jnp.stack([layer_grads[layer_index][member] for layer_index in range(LAYERS)])
            for member in range(3)
        )
    ) + (small_own,)
    attn_new = adam_update(attn_master, attn_first, attn_second, reduced[0], ATTENTION_RATE)
    inner_new = adam_update(inner_master, inner_first, inner_second, reduced[1], FEED_RATE)
    outer_new = adam_update(outer_master, outer_first, outer_second, reduced[2], FEED_RATE)
    small_new = adam_update(small_master, small_first, small_second, reduced[3], SMALL_RATE)
    return (
        hidden_c.astype(jnp.bfloat16),
        hidden_q.astype(jnp.bfloat16),
        grad_c,
        grad_q,
        attn_new[0],
        attn_new[1],
        attn_new[2],
        inner_new[0],
        inner_new[1],
        inner_new[2],
        outer_new[0],
        outer_new[1],
        outer_new[2],
        small_new[0],
        small_new[1],
        small_new[2],
    )


def after(value, *others):
    return lax.optimization_barrier((value, others))[0]


def join(*values):
    return lax.optimization_barrier(values)


def gather_group(count, shards, plane, column, sides, corners, mine, theirs):
    plan = []
    for core, arrays in enumerate((mine, theirs)):
        base = core * len(mine)
        for member in range(count):
            array, first = plane
            plan += [
                (base + array, first + side * count + member, side, 1, core, 0, member)
                for side in range(2)
            ]
            for apart in (1, 2, 3):
                index = (apart - 1) * count + member
                array, first = column
                plan.append((base + array, first + index, 0, 0, core, apart, member))
                for dx, dy, (array, first) in ((1, 0, sides[0]), (0, 1, sides[1])):
                    plan.append((base + array, first + index, dx, dy, core, apart, member))
                skipped = 0
                for array, first, held in corners:
                    if skipped <= index < skipped + held:
                        plan.append(
                            (base + array, first + index - skipped, 1, 1, core, apart, member)
                        )
                    skipped += held
    return (tuple(plan), tuple(shards) + tuple(mine) + tuple(theirs))


def gather_small(blocks, place):
    z, y = place[2], place[3]
    low, high = z % 2, z // 2
    blocks = jnp.where(low == 0, blocks, blocks[jnp.array([1, 0, 3, 2])])
    blocks = jnp.where(high == 0, blocks, blocks[jnp.array([2, 3, 0, 1])])
    other = swap_y(blocks)
    pairs = jnp.where(y == 0, jnp.stack([blocks, other], 1), jnp.stack([other, blocks], 1))
    return pairs.transpose(2, 0, 1, 3).reshape(blocks.shape[1], -1)


def add_low(*values):
    total = values[0].astype(jnp.float32)
    for value in values[1:]:
        total = total + value.astype(jnp.float32)
    return total.astype(jnp.bfloat16)


def reduce_corners(keep, get):
    corner = add_low(keep[1, 1], get[1, 1])
    return (swap_x(corner[:2]), swap_y(corner[2:]))


def side_payloads(keep, get, corners):
    by_x, by_y = corners
    pad = ((0, 0),) * 3
    for_x = add_low(keep[0, 1], get[0, 1], jnp.pad(by_y, ((2, 0),) + pad))
    for_y = add_low(keep[1, 0], get[1, 0], jnp.pad(by_x, ((0, 2),) + pad))
    return (for_x, for_y)


def reduce_sides(payloads):
    return (swap_x(payloads[0]), swap_y(payloads[1]))


def z_pair(values, half):
    return add_low(*(lax.dynamic_slice_in_dim(value, 2 * half, 2, 0) for value in values))


def far_payload(keep, get, sides, place):
    return z_pair((keep[0, 0], get[0, 0]) + tuple(sides), 1 - place[2] // 2)


def own_pair(keep, get, sides, far, place):
    half = place[2] // 2
    pair = (
        lax.dynamic_slice_in_dim(value, 2 * half, 2, 0)
        for value in (keep[0, 0], get[0, 0]) + tuple(sides)
    )
    return add_low(*pair, far)


def pick(pair, index):
    return lax.dynamic_index_in_dim(pair, index, 0, keepdims=False)


def reduce_near(pair, place):
    return swap_z(pick(pair, 1 - place[2] % 2), 1)


def reduce_total(pair, near, place):
    return add_low(pick(pair, place[2] % 2), near)


def reduce_direct(column, place):
    return tuple(swap_z(pick(column, place[2] ^ apart), apart) for apart in (1, 2, 3))


def share_core(pair, place):
    x, c = place[0], place[1]
    other = swap_core(pair)
    cores = jnp.where(c == 0, jnp.stack([pair, other], 1), jnp.stack([other, pair], 1))
    sides = jnp.where(x == 0, cores, cores[::-1])
    return sides.reshape((4,) + pair.shape[1:])


def small_parts(vectors):
    values = vectors.astype(jnp.float32)
    return (
        values[: 8 * D].reshape(8, D),
        values[8 * D : 8 * D + FF].reshape(1, FF),
        bias_vectors(values[8 * D + FF :].reshape(H, NB)),
    )


def per_device_fast(
    content,
    query,
    lengths,
    predicted,
    content_cot,
    query_cot,
    attn_master,
    attn_first,
    attn_second,
    inner_master,
    inner_first,
    inner_second,
    outer_master,
    outer_first,
    outer_second,
    small_master,
    small_first,
    small_second,
):
    place_parts = my_place()
    place = jnp.stack(place_parts).astype(jnp.int32)
    own_a0, plane_a0, own_f0 = cast_first(place, attn_master, inner_master, outer_master)
    z_a0 = tuple(swap_z(own_a0, apart) for apart in (1, 2, 3))
    plane_a0 = swap_y(plane_a0)
    near_f0 = swap_z(own_f0, 1)
    attn_low0, attn_low1, inner_low0, inner_low1, outer_low0, outer_low1, plane_f0, own_1, oth_1 = (
        cast_rest(place, attn_master, inner_master, outer_master)
    )
    low0 = jnp.concatenate([content, query])
    row_flags = predicted.reshape(1, LEN).astype(jnp.float32)
    col_flags = predicted.reshape(LEN, 1).astype(jnp.float32)
    small_low = small_master.astype(jnp.bfloat16)
    z_a0, plane_a0, near_f0, plane_f0, own_1, oth_1, low0, row_flags, col_flags, small_low = join(
        z_a0, plane_a0, near_f0, plane_f0, own_1, oth_1, low0, row_flags, col_flags, small_low
    )
    col_a0 = jnp.concatenate(z_a0)
    x0 = swap_x(col_a0)
    y0 = swap_y(col_a0)
    far_f0 = swap_z(jnp.concatenate([own_f0, near_f0]), 2)
    plane_f0 = swap_y(after(plane_f0, col_a0))
    near_1 = swap_z(after(own_1, col_a0), 1)
    small_near = swap_z(small_low, 1)
    x0, y0, far_f0, plane_f0, near_1, small_near = join(
        x0, y0, far_f0, plane_f0, near_1, small_near
    )
    col_f0 = jnp.concatenate([near_f0, far_f0])
    to_x1 = jnp.concatenate([col_f0, y0[:2]])
    to_y1 = jnp.concatenate([col_f0, x0[2:]])
    x1 = swap_x(to_x1)
    y1 = swap_y(to_y1)
    far_a1 = swap_z(jnp.concatenate([own_1[:1], near_1[:1]]), 2)
    held = after((plane_a0, col_a0, x0, y0, plane_f0, col_f0), to_x1, to_y1)
    mine_0 = jnp.concatenate(held)
    theirs_0 = swap_core(mine_0)
    small_pair = jnp.stack([small_low, small_near])
    small_far = swap_z(small_pair, 2)
    small_all = gather_small(jnp.concatenate([small_pair, small_far]), place_parts)
    x1, y1, far_a1, theirs_0, small_all = join(x1, y1, far_a1, theirs_0, small_all)
    col_a1 = jnp.concatenate([near_1[:1], far_a1])
    x2 = swap_x(jnp.concatenate([col_a1, y1[:4]]))
    y2 = swap_y(jnp.concatenate([col_a1, x1[4:6], own_1[:1], oth_1[:1]]))
    far_f1 = swap_z(jnp.concatenate([own_1[1:], after(near_1[1:], far_a1)]), 2)
    their_x1, their_y1 = swap_core(x1), swap_core(y1)
    group_a0 = gather_group(
        1, (attn_low0,), (0, 0), (0, 2), ((0, 5), (0, 8)), ((1, 6, 2), (2, 6, 1)),
        (mine_0, x1, y1), (theirs_0, their_x1, their_y1),
    )
    small0, hidden_bias0, (tvec0, far0, onehot) = small_parts(small_all[0])
    small1, hidden_bias1, (tvec1, far1, onehot) = small_parts(small_all[1])
    q0, k0, v0, attn0 = project(place, low0, small0, group_a0)
    mixed0, p0, inverse0, dead = mix(lengths, far0, tvec0, q0, k0, v0, row_flags, col_flags)
    x2, y2, far_f1, mixed0 = join(x2, y2, far_f1, mixed0)
    col_f1 = jnp.concatenate([near_1[1:], far_f1])
    x3 = swap_x(jnp.concatenate([col_f1, y2[:3]]))
    y3 = swap_y(jnp.concatenate([col_f1, own_1[1:], oth_1[1:]]))
    their_x2, their_y2, their_a1 = swap_core(x2), swap_core(y2), swap_core(after(col_a1, x2))
    group_f0 = gather_group(
        2, (inner_low0, outer_low0), (0, 11), (0, 15), ((1, 0), (2, 0)), ((3, 3, 4), (4, 3, 2)),
        (mine_0, x1, y1, x2, y2), (theirs_0, their_x1, their_y1, their_x2, their_y2),
    )
    resid0, pre0, normed0, low1, summed0 = feed(
        place, small0, hidden_bias0, mixed0, low0, attn0, group_f0
    )
    x3, y3, low1 = join(x3, y3, low1)
    x4 = swap_x(y3[:3])
    y4 = swap_y(x3[3:6])
    their_x3, their_y3 = swap_core(x3), swap_core(y3)
    group_a1 = gather_group(
        1, (attn_low1,), (1, 5), (2, 0), ((0, 0), (1, 0)), ((3, 6, 3),),
        (x2, y2, col_a1, x3), (their_x2, their_y2, their_a1, their_x3),
    )
    q1, k1, v1, attn1 = project(place, low1, small1, group_a1)
    x4, y4, q1 = join(x4, y4, q1)
    their_x4, their_y4, their_f1 = swap_core(x4), swap_core(y4), swap_core(after(col_f1, q1))
    group_f1 = gather_group(
        2, (inner_low1, outer_low1), (1, 6), (4, 0), ((0, 0), (1, 0)), ((2, 0, 3), (3, 0, 3)),
        (x3, y3, x4, y4, col_f1), (their_x3, their_y3, their_x4, their_y4, their_f1),
    )
    mixed1, p1, inverse1, dead = mix(
        lengths, far1, tvec1, q1, k1, v1, row_flags, col_flags
    )
    content_out, query_out, dresid1, dmix1, dwo1, keep_f1, send_f1, vec_f1, dhidden1 = turn(
        place, lengths, small1, small0, hidden_bias1, mixed1, summed0, attn1,
        (content_cot, query_cot), group_f1
    )
    get_f1 = swap_core(send_f1)
    *first1, table1_a = mix_back(0, q1, k1, v1, dmix1, mixed1, p1, inverse1, dead)
    by_f1 = reduce_corners(keep_f1, after(get_f1, table1_a))
    dq1, dk1, dv1, table1_b = mix_back(
        3, after(q1, get_f1, table1_a), k1, v1, dmix1, mixed1, p1, inverse1, dead, tuple(first1)
    )
    sides_rf1 = reduce_sides(side_payloads(keep_f1, get_f1, after(by_f1, table1_b)))
    keep_a1, send_a1, vec_a1 = weight_back(place, after(low1, by_f1), dq1, dk1, dv1, dwo1)
    get_a1 = swap_core(send_a1)
    by_a1 = reduce_corners(keep_a1, get_a1)
    dresid0, dmix0, dwo0, keep_f0, send_f0, vec_f0, dhidden0 = down(
        place, small0, dq1, dk1, dv1, after(attn1, get_a1), dresid1, summed0, normed0, resid0,
        pre0, mixed0, attn0, group_f0
    )
    get_f0 = swap_core(after(send_f0, sides_rf1, by_a1))
    sides_ra1 = reduce_sides(side_payloads(keep_a1, get_a1, after(by_a1, dmix0)))
    sides_rf1 = after(sides_rf1, dmix0)
    zfar_f1 = swap_z(far_payload(keep_f1, get_f1, sides_rf1, place_parts), 2)
    *first0, table0_a = mix_back(
        0, after(q0, by_a1, sides_rf1), k0, v0, dmix0, mixed0, p0, inverse0, dead
    )
    by_f0 = reduce_corners(keep_f0, after(get_f0, table0_a))
    dq0, dk0, dv0, table0_b = mix_back(
        3, after(q0, get_f0, table0_a), k0, v0, dmix0, mixed0, p0, inverse0, dead, tuple(first0)
    )
    by_f0, sides_ra1, zfar_f1, table0_b = join(by_f0, sides_ra1, zfar_f1, table0_b)
    payloads_f0 = side_payloads(keep_f0, get_f0, by_f0)
    sides_rf0 = reduce_sides(payloads_f0)
    keep_a0, send_a0, vec_a0 = weight_back(
        place, after(low0, payloads_f0, table0_b), dq0, dk0, dv0, dwo0
    )
    get_a0 = swap_core(send_a0)
    zfar_a1 = swap_z(far_payload(keep_a1, get_a1, sides_ra1, place_parts), 2)
    pair_f1 = own_pair(keep_f1, get_f1, sides_rf1, after(zfar_f1, get_a0), place_parts)
    znear_f1 = reduce_near(pair_f1, place_parts)
    sides_rf0, get_a0, zfar_a1, znear_f1, vec_a0 = join(
        sides_rf0, get_a0, zfar_a1, znear_f1, vec_a0
    )
    payload_f0 = far_payload(keep_f0, get_f0, sides_rf0, place_parts)
    zfar_f0 = swap_z(payload_f0, 2)
    by_a0 = reduce_corners(keep_a0, after(get_a0, payload_f0))
    pair_a1 = own_pair(keep_a1, get_a1, sides_ra1, zfar_a1, place_parts)
    znear_a1 = reduce_near(after(pair_a1, payload_f0), place_parts)
    content_grad, query_grad = input_back(after(dq0, sides_rf0), dk0, dv0, attn0, dresid0)
    small_sum = jnp.concatenate(
        [
            jnp.stack([vec_a0, vec_a1]).reshape(LAYERS, -1),
            jnp.stack([vec_f0, vec_f1]).reshape(LAYERS, -1),
            jnp.stack([dhidden0, dhidden1]).reshape(LAYERS, -1),
            table_grad(
                jnp.concatenate([table0_a, table0_b, table1_a, table1_b]), onehot
            ).reshape(LAYERS, -1),
        ],
        axis=1,
    )
    by_a0, content_grad, znear_a1 = join(by_a0, content_grad, znear_a1)
    payloads_a0 = side_payloads(keep_a0, get_a0, by_a0)
    sides_ra0 = reduce_sides(payloads_a0)
    own_1 = jnp.concatenate(
        [
            reduce_total(pair_f1, znear_f1, place_parts),
            reduce_total(pair_a1, znear_a1, place_parts),
        ]
    )
    across_1 = swap_x(after(own_1, payloads_a0))
    small_sum = small_sum + swap_core(after(small_sum, payloads_a0))
    sides_ra0, zfar_f0, small_sum = join(sides_ra0, zfar_f0, small_sum)
    column_a0 = add_low(keep_a0[0, 0], get_a0[0, 0], *sides_ra0)
    shifts_a0 = reduce_direct(column_a0, place_parts)
    pair_f0 = own_pair(keep_f0, get_f0, sides_rf0, zfar_f0, place_parts)
    znear_f0 = reduce_near(after(pair_f0, column_a0), place_parts)
    small_sum = small_sum + swap_y(after(small_sum, column_a0))
    shifts_a0, znear_f0, across_1, small_sum = join(shifts_a0, znear_f0, across_1, small_sum)
    own_0 = jnp.concatenate(
        [
            reduce_total(pair_f0, znear_f0, place_parts),
            add_low(pick(column_a0, place_parts[2]), *shifts_a0),
        ]
    )
    across_0 = swap_x(own_0)
    four_1 = share_core(jnp.stack([own_1, after(across_1, own_0)]), place_parts)
    state = (
        attn_master, attn_first, attn_second, inner_master, inner_first, inner_second,
        outer_master, outer_first, outer_second,
    )
    new_1 = adam(1, state, four_1, ())
    small_z = swap_z(after(small_sum, own_0), 1)
    across_0, new_1, small_z = join(across_0, new_1, small_z)
    small_sum = small_sum + small_z
    four_0 = share_core(jnp.stack([own_0, across_0]), place_parts)
    small_sum = small_sum + swap_z(small_sum, 2)
    small_x = swap_x(small_sum)
    new_0 = adam(0, state, four_0, tuple(new_1))
    small_sum = small_sum + small_x
    size = small_master.shape[1]
    small_own = lax.dynamic_slice_in_dim(small_sum, lax.axis_index("fsdp") * size, size, 1)
    small_new = adam_update(small_master, small_first, small_second, small_own, SMALL_RATE)
    return (
        (content_out, query_out, content_grad, query_grad)
        + tuple(new_0)
        + small_new
    )


def solution(mesh):
    placed = (
        P(("dp", "fsdp"), None),
        P(("dp", "fsdp"), None),
        P(("dp", "fsdp")),
        P(("dp", "fsdp")),
        P(("dp", "fsdp"), None),
        P(("dp", "fsdp"), None),
        P(None, None, "fsdp", None),
        P(None, None, "fsdp", None),
        P(None, None, "fsdp", None),
        P(None, "fsdp", None),
        P(None, "fsdp", None),
        P(None, "fsdp", None),
        P(None, "fsdp", None),
        P(None, "fsdp", None),
        P(None, "fsdp", None),
        P(None, "fsdp"),
        P(None, "fsdp"),
        P(None, "fsdp"),
    )
    fast = tuple(mesh.shape.values()) == (4, 8)
    return jax.shard_map(
        per_device_fast if fast else per_device,
        mesh=mesh,
        in_specs=placed,
        out_specs=(
            P(("dp", "fsdp"), None),
            P(("dp", "fsdp"), None),
            P(("dp", "fsdp"), None),
            P(("dp", "fsdp"), None),
            P(None, None, "fsdp", None),
            P(None, None, "fsdp", None),
            P(None, None, "fsdp", None),
            P(None, "fsdp", None),
            P(None, "fsdp", None),
            P(None, "fsdp", None),
            P(None, "fsdp", None),
            P(None, "fsdp", None),
            P(None, "fsdp", None),
            P(None, "fsdp"),
            P(None, "fsdp"),
            P(None, "fsdp"),
        ),
        check_vma=False,
    )
```

```python
from functools import partial

import jax
import jax.numpy as jnp
from jax import lax
from jax.experimental import pallas as pl
from jax.experimental.pallas import tpu as pltpu
from jax.sharding import PartitionSpec as P

D = 768
H = 12
DH = 64
FF = 3072
LEN = 512
NB = 32
LAYERS = 2
STEP = 10


NORM_EPS = 1e-05
MASKED = -1000000000.0
BETA_ONE = 0.9
BETA_TWO = 0.999
ATTENTION_RATE = 0.1
FEED_RATE = 0.02
SMALL_RATE = 0.4
WEIGHT_DECAY = 0.01
ADAM_EPS = 1e-08
SCORE_SCALE = 0.125


def layer_norm(values, gain, shift):
    centre = values - jnp.mean(values, axis=-1, keepdims=True)
    spread = jnp.mean(centre * centre, axis=-1, keepdims=True)
    return centre * lax.rsqrt(spread + NORM_EPS) * gain + shift


def unpack(vectors):
    pieces = [vectors[piece_index * D : (piece_index + 1) * D] for piece_index in range(8)]
    hidden_bias = vectors[8 * D : 8 * D + FF]
    bias_table = vectors[8 * D + FF :].reshape(H, NB)
    return (pieces, hidden_bias, bias_table)


def bucket_ids():
    position = jnp.arange(LEN, dtype=jnp.int32)
    offset = position[None, :] - position[:, None]
    distance = jnp.abs(offset)
    far_bucket = jnp.full(distance.shape, 8, jnp.int32)
    for exponent in range(1, 8):
        far_bucket = far_bucket + (distance * distance >= 64 * 2**exponent).astype(jnp.int32)
    near_or_far = jnp.where(distance < 8, distance, far_bucket)
    return near_or_far + NB // 2 * (offset > 0).astype(jnp.int32)


def bucket_onehot():
    return (bucket_ids()[:, :, None] == jnp.arange(NB, dtype=jnp.int32)[None, None, :]).astype(
        jnp.bfloat16
    )


def allowed_pairs(length, pred_flags):
    position = jnp.arange(LEN, dtype=jnp.int32)
    valid_key = (position < length)[None, :]
    row_pos = position[:, None]
    col_pos = position[None, :]
    free_key = (pred_flags == 0)[None, :]
    content_ok = valid_key & (free_key | (pred_flags[:, None] == 1) & (col_pos <= row_pos))
    query_ok = valid_key & (col_pos != row_pos) & (free_key | (col_pos < row_pos))
    return (content_ok, query_ok)


def masked_scores(query_rows, key_rows, position_bias, allowed):
    scores = (
        jnp.einsum("qhd,khd->hqk", query_rows, key_rows, preferred_element_type=jnp.float32)
        * SCORE_SCALE
        + position_bias
    )
    return jnp.where(allowed[None], scores, MASKED)


def table_bias(onehot, table_low):
    return jnp.einsum("qkb,hb->hqk", onehot, table_low, preferred_element_type=jnp.float32)


def attend_slot(onehot, table_low, slot_item):
    query_c, query_q, key_rows, value_rows, length, pred_flags = slot_item
    position_bias = table_bias(onehot, table_low)
    content_ok, query_ok = allowed_pairs(length, pred_flags)
    results = []
    for query_rows, allowed in ((query_c, content_ok), (query_q, query_ok)):
        scores = masked_scores(query_rows, key_rows, position_bias, allowed)
        peak = jnp.max(scores, axis=-1, keepdims=True)
        expos = jnp.exp(scores - peak)
        totals = jnp.sum(expos, axis=-1, keepdims=True)
        probs = (expos / totals).astype(jnp.bfloat16)
        mixed = jnp.einsum(
            "hqk,khd->qhd", probs, value_rows, preferred_element_type=jnp.float32
        ).astype(jnp.bfloat16)
        results.append((mixed, peak[..., 0] + jnp.log(totals[..., 0])))
    return (results[0][0], results[1][0], results[0][1], results[1][1])


def attend_back(onehot, table_low, slot_item):
    (
        query_c,
        query_q,
        key_rows,
        value_rows,
        length,
        pred_flags,
        lse_c,
        lse_q,
        grad_mix_c,
        grad_mix_q,
    ) = slot_item
    position_bias = table_bias(onehot, table_low)
    content_ok, query_ok = allowed_pairs(length, pred_flags)
    grad_keys = jnp.zeros(key_rows.shape, jnp.float32)
    grad_values = jnp.zeros(value_rows.shape, jnp.float32)
    grad_table = jnp.zeros((H, NB), jnp.float32)
    grads_query = []
    for query_rows, allowed, log_total, grad_mix in (
        (query_c, content_ok, lse_c, grad_mix_c),
        (query_q, query_ok, lse_q, grad_mix_q),
    ):
        scores = masked_scores(query_rows, key_rows, position_bias, allowed)
        probs = jnp.exp(scores - log_total[..., None])
        grad_values = grad_values + jnp.einsum(
            "hqk,qhd->khd", probs.astype(jnp.bfloat16), grad_mix, preferred_element_type=jnp.float32
        )
        grad_probs = jnp.einsum(
            "qhd,khd->hqk", grad_mix, value_rows, preferred_element_type=jnp.float32
        )
        grad_scores = probs * (grad_probs - jnp.sum(probs * grad_probs, axis=-1, keepdims=True))
        grad_scores = jnp.where(allowed[None], grad_scores, 0.0).astype(jnp.bfloat16)
        grad_table = grad_table + jnp.einsum(
            "hqk,qkb->hb", grad_scores, onehot, preferred_element_type=jnp.float32
        )
        grads_query.append(
            jnp.einsum("hqk,khd->qhd", grad_scores, key_rows, preferred_element_type=jnp.float32)
            * SCORE_SCALE
        )
        grad_keys = (
            grad_keys
            + jnp.einsum(
                "hqk,qhd->khd", grad_scores, query_rows, preferred_element_type=jnp.float32
            )
            * SCORE_SCALE
        )
    return (grads_query[0], grads_query[1], grad_keys, grad_values, grad_table)


def to_heads(values):
    return values.reshape(-1, LEN, H, DH)


AXES = ("dp", "fsdp")
GRID = (2, 2, 4, 2)
ROWS = 96


def places():
    return [
        (x, c, z, y) for x in range(2) for c in range(2) for z in range(4) for y in range(2)
    ]


def flat(x, c, z, y):
    return ((x * 2 + c) * 4 + z) * 2 + y


def move(value, shift):
    pairs = [(flat(*place), flat(*shift(*place))) for place in places()]
    return lax.ppermute(value, AXES, pairs)


def swap_core(value):
    return move(value, lambda x, c, z, y: (x, 1 - c, z, y))


def swap_x(value):
    return move(value, lambda x, c, z, y: (1 - x, c, z, y))


def swap_y(value):
    return move(value, lambda x, c, z, y: (x, c, z, 1 - y))


def swap_z(value, apart):
    return move(value, lambda x, c, z, y: (x, c, z ^ apart, y))


def my_place():
    dp = lax.axis_index("dp")
    fsdp = lax.axis_index("fsdp")
    return (dp // 2, dp % 2, fsdp // 2, fsdp % 2)


def dot_nn(left, right):
    return jnp.dot(left, right, preferred_element_type=jnp.float32)


def dot_nt(left, right):
    return lax.dot_general(
        left, right, (((1,), (1,)), ((), ())), preferred_element_type=jnp.float32
    )


def dot_tn(left, right):
    return lax.dot_general(
        left, right, (((0,), (0,)), ((), ())), preferred_element_type=jnp.float32
    )


ANY_SPEC = pl.BlockSpec(memory_space=pl.ANY)
VMEM_SPEC = pl.BlockSpec(memory_space=pltpu.VMEM)
SMEM_SPEC = pl.BlockSpec(memory_space=pltpu.SMEM)
TALL = 2 * LEN
HALF = 256
PARAMS = pltpu.CompilerParams(vmem_limit_bytes=60 * 1024 * 1024)


def norm_parts(values):
    centre = values - jnp.mean(values, axis=-1, keepdims=True)
    spread = jnp.mean(centre * centre, axis=-1, keepdims=True)
    scale = lax.rsqrt(spread + NORM_EPS)
    return (centre * scale, scale)


def norm_back(unit, scale, grad, gain):
    scaled = grad * gain
    return scale * (
        scaled
        - jnp.mean(scaled, axis=-1, keepdims=True)
        - unit * jnp.mean(scaled * unit, axis=-1, keepdims=True)
    )


def start_fetch(kinds, plan, place_ref, refs, targets, sems):
    x, c, z, y = (place_ref[index] for index in range(4))
    mine = z * 2 + y
    copies = []

    def start(source, target):
        copy = pltpu.make_async_copy(source, target, sems.at[len(copies)])
        copy.start()
        copies.append(copy)

    for member, kind in enumerate(kinds):
        target = targets[member]
        if kind == "attn":
            start(refs[member], target.at[:, pl.ds(pl.multiple_of(mine * ROWS, ROWS), ROWS), :])
        elif kind == "inner":
            for quarter in range(4):
                start(
                    refs[member].at[:, quarter * D : quarter * D + D],
                    target.at[quarter, pl.ds(pl.multiple_of(mine * ROWS, ROWS), ROWS), :],
                )
        else:
            start(refs[member], target.at[z, pl.ds(pl.multiple_of(y * 384, ROWS), 384), :])
    for array, index, dx, dy, dc, dz, member in plan:
        quarter = (x ^ dx) * 2 + (c ^ dc)
        if kinds[member] == "outer":
            lead, row = z ^ dz, (y ^ dy) * 384 + quarter * ROWS
        else:
            lead, row = quarter, ((z ^ dz) * 2 + (y ^ dy)) * ROWS
        start(
            refs[len(kinds) + array].at[index],
            targets[member].at[lead, pl.ds(pl.multiple_of(row, ROWS), ROWS), :],
        )
    return copies


def pack_kernel(outputs, count, *refs):
    sources, targets, sems = refs[:count], refs[count:-1], refs[-1]
    pairs = []
    for target, parts in zip(targets, outputs):
        at = 0
        for source, first, held in parts:
            pairs.append((sources[source].at[first : first + held], target.at[at : at + held]))
            at += held
    finish(issue(pairs, sems))


def pack(outputs, sources):
    total = sum(len(parts) for parts in outputs)
    counts = [sum(held for unused, unused_first, held in parts) for parts in outputs]
    return pl.pallas_call(
        partial(pack_kernel, outputs, len(sources)),
        out_shape=[jax.ShapeDtypeStruct((count, ROWS, D), jnp.bfloat16) for count in counts],
        in_specs=[ANY_SPEC] * len(sources),
        out_specs=[VMEM_SPEC] * len(outputs),
        scratch_shapes=[pltpu.SemaphoreType.DMA((total,))],
        compiler_params=pltpu.CompilerParams(vmem_limit_bytes=16 * 1024 * 1024),
        cost_estimate=pl.CostEstimate(flops=0, bytes_accessed=300000 * sum(counts), transcendentals=0),
        name="pack",
    )(*sources)


def quarter_spans(place_ref, side):
    quarter = (place_ref[0] ^ side) * 2 + place_ref[1]
    return (
        quarter,
        pl.ds(pl.multiple_of(quarter * D, D), D),
        pl.ds(pl.multiple_of(quarter * ROWS, ROWS), ROWS),
    )


def cast_first_kernel(
    place_ref, attn_any, inner_any, outer_any, own_a0, plane_a0, own_f0, hold_ref, sems
):
    index, cols, rows = quarter_spans(place_ref, 0)
    other = quarter_spans(place_ref, 1)[0]
    finish(
        issue(
            (
                (attn_any.at[0, index], hold_ref.at[0]),
                (attn_any.at[0, other], hold_ref.at[1]),
                (inner_any.at[0, :, cols], hold_ref.at[2]),
                (outer_any.at[0, rows, :], hold_ref.at[3]),
            ),
            sems,
        )
    )
    own_a0[...] = hold_ref[0:1].astype(jnp.bfloat16)
    plane_a0[...] = hold_ref[0:2].astype(jnp.bfloat16)
    own_f0[...] = hold_ref[2:4].astype(jnp.bfloat16)


def cast_first(place, attn, inner, outer):
    return pl.pallas_call(
        cast_first_kernel,
        out_shape=[jax.ShapeDtypeStruct((count, ROWS, D), jnp.bfloat16) for count in (1, 2, 2)],
        in_specs=[SMEM_SPEC] + [ANY_SPEC] * 3,
        out_specs=[VMEM_SPEC] * 3,
        scratch_shapes=[pltpu.VMEM((4, ROWS, D), jnp.float32), pltpu.SemaphoreType.DMA((4,))],
        compiler_params=PARAMS,
        cost_estimate=pl.CostEstimate(flops=1000000, bytes_accessed=2000000, transcendentals=0),
        name="cast_first",
    )(place, attn, inner, outer)


def cast_rest_kernel(
    place_ref, attn_ref, inner_ref, outer_ref, attn_0, attn_1, inner_0, inner_1, outer_0, outer_1,
    plane_f0, own_1, oth_1,
):
    for layer, (attn_low, inner_low, outer_low) in enumerate(
        ((attn_0, inner_0, outer_0), (attn_1, inner_1, outer_1))
    ):
        attn_low[...] = attn_ref[layer].astype(jnp.bfloat16)
        inner_low[...] = inner_ref[layer].astype(jnp.bfloat16)
        outer_low[...] = outer_ref[layer].astype(jnp.bfloat16)
    for side, (target, first) in enumerate(((own_1, 0), (oth_1, 0))):
        index, cols, rows = quarter_spans(place_ref, side)
        plane_f0[2 * side] = inner_ref[0, :, cols].astype(jnp.bfloat16)
        plane_f0[2 * side + 1] = outer_ref[0, rows, :].astype(jnp.bfloat16)
        target[0] = attn_ref[1, index].astype(jnp.bfloat16)
        target[1] = inner_ref[1, :, cols].astype(jnp.bfloat16)
        target[2] = outer_ref[1, rows, :].astype(jnp.bfloat16)


def cast_rest(place, attn, inner, outer):
    low = [
        jax.ShapeDtypeStruct(array.shape[1:], jnp.bfloat16)
        for array in (attn, attn, inner, inner, outer, outer)
    ]
    return pl.pallas_call(
        cast_rest_kernel,
        out_shape=low
        + [jax.ShapeDtypeStruct((count, ROWS, D), jnp.bfloat16) for count in (4, 3, 3)],
        in_specs=[SMEM_SPEC] + [VMEM_SPEC] * 3,
        out_specs=[VMEM_SPEC] * 9,
        compiler_params=PARAMS,
        cost_estimate=pl.CostEstimate(flops=10000000, bytes_accessed=12000000, transcendentals=0),
        name="cast_rest",
    )(place, attn, inner, outer)


def project_kernel(plan, place_ref, small_ref, low_any, *refs):
    pieces = refs[:-14]
    (
        q_out, k_out, v_out, w_out, low_ref, q_ref, k_ref, v_ref, w_ref,
        sems, load_sem, keep_sem, store_sems, unused,
    ) = refs[-14:]
    load = pltpu.make_async_copy(low_any, low_ref, load_sem)
    load.start()
    fetches = start_fetch(("attn",), plan, place_ref, pieces, (w_ref,), sems)
    load.wait()
    for copy in fetches:
        copy.wait()
    keep = pltpu.make_async_copy(w_ref, w_out, keep_sem)
    keep.start()
    bias_q = small_ref[0:1, :]
    bias_v = small_ref[1:2, :]
    stores = []

    def store(source, target):
        copy = pltpu.make_async_copy(source, target, store_sems.at[len(stores)])
        copy.start()
        stores.append(copy)

    for row in range(0, TALL, HALF):
        span = slice(row, row + HALF)
        rows = low_ref[span, :]
        q_ref[span, :] = (dot_nn(rows, w_ref[0]) + bias_q).astype(jnp.bfloat16)
        if row < LEN:
            k_ref[span, :] = dot_nn(rows, w_ref[1]).astype(jnp.bfloat16)
            v_ref[span, :] = (dot_nn(rows, w_ref[2]) + bias_v).astype(jnp.bfloat16)
        if row == LEN - HALF:
            store(k_ref, k_out)
            store(v_ref, v_out)
            store(q_ref.at[:LEN, :], q_out.at[:LEN, :])
    store(q_ref.at[LEN:, :], q_out.at[LEN:, :])
    for copy in stores:
        copy.wait()
    keep.wait()


def project(place, low, small, group):
    plan, pieces = group
    return pl.pallas_call(
        partial(project_kernel, plan),
        out_shape=[
            jax.ShapeDtypeStruct((TALL, D), jnp.bfloat16),
            jax.ShapeDtypeStruct((LEN, D), jnp.bfloat16),
            jax.ShapeDtypeStruct((LEN, D), jnp.bfloat16),
            jax.ShapeDtypeStruct((4, D, D), jnp.bfloat16),
        ],
        in_specs=[SMEM_SPEC, VMEM_SPEC, ANY_SPEC] + [ANY_SPEC] * len(pieces),
        out_specs=[ANY_SPEC] * 4,
        scratch_shapes=[
            pltpu.VMEM((TALL, D), jnp.bfloat16),
            pltpu.VMEM((TALL, D), jnp.bfloat16),
            pltpu.VMEM((LEN, D), jnp.bfloat16),
            pltpu.VMEM((LEN, D), jnp.bfloat16),
            pltpu.VMEM((4, D, D), jnp.bfloat16),
            pltpu.SemaphoreType.DMA((32,)),
            pltpu.SemaphoreType.DMA,
            pltpu.SemaphoreType.DMA,
            pltpu.SemaphoreType.DMA((4,)),
            pltpu.SemaphoreType.DMA,
        ],
        compiler_params=PARAMS,
        cost_estimate=pl.CostEstimate(flops=2 * 2048 * D * D, bytes_accessed=16000000, transcendentals=0),
        name="project",
    )(place, small, low, *pieces)


def build_masks(length, row_flags, col_flags, mask_ref, alive_ref):
    flags = row_flags[...]

    def body(step, carry):
        start = pl.multiple_of(step * 64, 64)
        key = lax.broadcasted_iota(jnp.int32, (64, LEN), 0) + start
        query = lax.broadcasted_iota(jnp.int32, (64, LEN), 1)
        valid = key < length
        free = jnp.broadcast_to(col_flags[pl.ds(start, 64), :], (64, LEN)) == 0.0
        marked = jnp.broadcast_to(flags, (64, LEN)) == 1.0
        content_ok = valid & (free | (marked & (key <= query)))
        query_ok = valid & (key != query) & (free | (key < query))
        mask_ref[pl.ds(start, 64), :LEN] = content_ok.astype(jnp.float32)
        mask_ref[pl.ds(start, 64), LEN:] = query_ok.astype(jnp.float32)
        return carry

    lax.fori_loop(0, 8, body, 0)
    alive_ref[...] = jnp.max(mask_ref[...], axis=0, keepdims=True)


def build_tiles(t_row, tile_ref):
    spread = jnp.broadcast_to(t_row, (128, 512))
    rolled = pltpu.roll(spread, 0, 1, stride=1, stride_axis=0)
    tile_ref[...] = rolled[:, :384]


def position_bias(tile_ref, far_ref, head, query_block, key_block):
    apart = query_block - key_block
    if apart >= 2:
        return far_ref[head, 0]
    if apart <= -2:
        return far_ref[head, 1]
    return tile_ref[:, 128 * (apart + 1) : 128 * (apart + 2)]


def head_lanes(shape, head):
    lane = lax.broadcasted_iota(jnp.int32, shape, 1)
    return (lane >= 64) if head else (lane < 64)


def mix_kernel(
    length_ref, far_ref, q_ref, k_ref, v_ref, row_flags, col_flags, t_ref,
    a_ref, p_ref, inverse_ref, dead_ref, mask_ref, alive_ref, tile_ref, o_ref,
):
    pair = pl.program_id(0)

    @pl.when(pair == 0)
    def _():
        build_masks(length_ref[0], row_flags, col_flags, mask_ref, alive_ref)
        dead_ref[...] = (1.0 - alive_ref[...]) * (1.0 / LEN)

    keys = k_ref[...].astype(jnp.float32) * SCORE_SCALE
    values_t = v_ref[...].astype(jnp.float32).T.astype(jnp.bfloat16)
    keys_own = [
        jnp.where(head_lanes(keys.shape, head), keys, 0.0).astype(jnp.bfloat16) for head in range(2)
    ]
    for head in range(2):
        build_tiles(t_ref[head], tile_ref.at[head])
    work = [(head, chunk) for head in range(2) for chunk in range(4)]

    def score(head, chunk):
        return dot_nt(keys_own[head], q_ref[chunk * HALF : chunk * HALF + HALF, :])

    def mixture(head, chunk):
        span = slice(chunk * HALF, chunk * HALF + HALF)
        own = slice(8 + head * 64, 8 + head * 64 + 64)
        mixed = dot_nn(values_t[head * 64 : head * 64 + 64, :], p_ref[head, :, span])
        o_ref[own, span] = mixed * o_ref[head : head + 1, span]

    following = score(*work[0])
    for index, (head, chunk) in enumerate(work):
        scores = following
        if index + 1 < len(work):
            following = score(*work[index + 1])
        at = chunk * HALF
        for side in range(2):
            lanes = slice(at + side * 128, at + side * 128 + 128)
            blocks = []
            peak = None
            for key_block in range(4):
                rows = slice(key_block * 128, key_block * 128 + 128)
                block = scores[rows, side * 128 : side * 128 + 128] + position_bias(
                    tile_ref.at[head], far_ref, pair * 2 + head, (chunk % 2) * 2 + side, key_block
                )
                block = jnp.where(mask_ref[rows, lanes] > 0.0, block, MASKED)
                blocks.append(block)
                high = jnp.max(block, axis=0, keepdims=True)
                peak = high if peak is None else jnp.maximum(peak, high)
            total = None
            for key_block in range(4):
                rows = slice(key_block * 128, key_block * 128 + 128)
                expo = jnp.exp(blocks[key_block] - peak)
                part = jnp.sum(expo, axis=0, keepdims=True)
                total = part if total is None else total + part
                p_ref[head, rows, lanes] = expo.astype(jnp.bfloat16)
            inverse = 1.0 / total
            inverse_ref[head, :, lanes] = inverse * alive_ref[:, lanes]
            o_ref[head : head + 1, lanes] = inverse
        if index:
            mixture(*work[index - 1])
    mixture(*work[-1])
    a_ref[...] = o_ref[8:, :].T.astype(jnp.bfloat16)


def mix(length, far, tvec, q, k, v, row_flags, col_flags):
    tall = pl.BlockSpec((TALL, 128), lambda p: (0, p))
    short = pl.BlockSpec((LEN, 128), lambda p: (0, p))
    return pl.pallas_call(
        mix_kernel,
        grid=(H // 2,),
        out_shape=[
            jax.ShapeDtypeStruct((TALL, D), jnp.bfloat16),
            jax.ShapeDtypeStruct((H, LEN, TALL), jnp.bfloat16),
            jax.ShapeDtypeStruct((H, 1, TALL), jnp.float32),
            jax.ShapeDtypeStruct((1, TALL), jnp.float32),
        ],
        in_specs=[
            SMEM_SPEC, SMEM_SPEC, tall, short, short,
            pl.BlockSpec((1, LEN), lambda p: (0, 0)),
            pl.BlockSpec((LEN, 1), lambda p: (0, 0)),
            pl.BlockSpec((2, 1, 512), lambda p: (p, 0, 0)),
        ],
        out_specs=[
            tall,
            pl.BlockSpec((2, LEN, TALL), lambda p: (p, 0, 0)),
            pl.BlockSpec((2, 1, TALL), lambda p: (p, 0, 0)),
            pl.BlockSpec((1, TALL), lambda p: (0, 0)),
        ],
        scratch_shapes=[
            pltpu.VMEM((LEN, TALL), jnp.float32),
            pltpu.VMEM((1, TALL), jnp.float32),
            pltpu.VMEM((2, 128, 384), jnp.float32),
            pltpu.VMEM((136, TALL), jnp.float32),
        ],
        compiler_params=PARAMS,
        cost_estimate=pl.CostEstimate(flops=6500000000, bytes_accessed=8000000, transcendentals=6300000),
        name="mix",
    )(length, far, q, k, v, row_flags, col_flags, tvec)


def mix_back_kernel(q_ref, k_ref, v_ref, da_ref, a_ref, p_ref, inverse_ref, dead_ref, *refs):
    (
        dq_ref, dk_ref, dv_ref, table_ref, s_ref, near_ref, da_t, low_t, q_t, g_ref,
    ) = refs[-10:]
    keys = k_ref[...].astype(jnp.float32) * SCORE_SCALE
    keys_t = keys.T.astype(jnp.bfloat16)
    q_t[...] = q_ref[...].astype(jnp.float32).T.astype(jnp.bfloat16)
    da_t[...] = da_ref[...].astype(jnp.float32).T
    product = a_ref[...].astype(jnp.float32).T * da_t[...]
    values = v_ref[...].astype(jnp.float32)
    near_ref[...] = jnp.zeros(near_ref.shape, jnp.float32)
    turn = (
        lax.broadcasted_iota(jnp.int32, (128, 128), 0)
        + lax.broadcasted_iota(jnp.int32, (128, 128), 1)
        == 127
    ).astype(jnp.float32)
    deltas = []
    for head in range(2):
        rows = slice(head * 64, head * 64 + 64)
        inverse = inverse_ref[head]
        deltas.append(jnp.sum(product[rows, :], axis=0, keepdims=True) * inverse)
        low_t[rows, :] = (da_t[rows, :] * inverse).astype(jnp.bfloat16)
    for head in range(2):
        own = slice(head * 64, head * 64 + 64)
        values_own = jnp.where(head_lanes(values.shape, head), values, 0.0).astype(jnp.bfloat16)
        delta = deltas[head]
        far_low = jnp.zeros((8, 128), jnp.float32)
        far_high = jnp.zeros((8, 128), jnp.float32)
        for chunk in range(4):
            at = chunk * HALF
            pulls = dot_nn(values_own, low_t[:, at : at + HALF])
            for side in range(2):
                lanes = slice(at + side * 128, at + side * 128 + 128)
                shift = delta[:, lanes]
                query_block = (chunk % 2) * 2 + side
                for key_block in range(4):
                    rows = slice(key_block * 128, key_block * 128 + 128)
                    cols = slice(side * 128, side * 128 + 128)
                    grad = p_ref[head, rows, lanes].astype(jnp.float32) * (
                        pulls[rows, cols] - shift
                    )
                    s_ref[head, rows, lanes] = grad.astype(jnp.bfloat16)
                    apart = query_block - key_block
                    if apart >= 2:
                        far_low = far_low + jnp.sum(grad.reshape(16, 8, 128), axis=0)
                    elif apart <= -2:
                        far_high = far_high + jnp.sum(grad.reshape(16, 8, 128), axis=0)
                    else:
                        near_ref[head, :, 128 * (apart + 1) : 128 * (apart + 2)] += grad
        g_ref[own, :LEN] = dot_nt(low_t[own, :], p_ref[head])
        g_ref[own, LEN:] = dot_nt(q_t[own, :], s_ref[head]) * SCORE_SCALE
        da_t[own, :] = dot_nn(keys_t[own, :], s_ref[head])
        turned = jnp.dot(
            turn, near_ref[head], precision=lax.Precision.HIGHEST, preferred_element_type=jnp.float32
        )
        aligned = pltpu.roll(turned, 0, 1, stride=1, stride_axis=0)
        table_ref[head, :, :512] = jnp.sum(aligned, axis=0, keepdims=True)
        table_ref[head, :, 512:640] = jnp.sum(far_low, axis=0, keepdims=True)
        table_ref[head, :, 640:] = jnp.sum(far_high, axis=0, keepdims=True)
    uniform = dot_nn(dead_ref[...].astype(jnp.bfloat16), da_ref[...])
    dv_ref[...] = (g_ref[:, :LEN].T + uniform).astype(jnp.bfloat16)
    dk_ref[...] = g_ref[:, LEN:].T.astype(jnp.bfloat16)
    dq_ref[...] = da_t[...].T.astype(jnp.bfloat16)


def mix_back(first, q, k, v, da, a, p, inverse, dead, held=()):
    tall = pl.BlockSpec((TALL, 128), lambda i: (0, i + first))
    short = pl.BlockSpec((LEN, 128), lambda i: (0, i + first))
    return pl.pallas_call(
        mix_back_kernel,
        grid=(H // 4,),
        out_shape=[
            jax.ShapeDtypeStruct((TALL, D), jnp.bfloat16),
            jax.ShapeDtypeStruct((LEN, D), jnp.bfloat16),
            jax.ShapeDtypeStruct((LEN, D), jnp.bfloat16),
            jax.ShapeDtypeStruct((H // 2, 1, 768), jnp.float32),
        ],
        in_specs=[
            tall, short, short, tall, tall,
            pl.BlockSpec((2, LEN, TALL), lambda i: (i + first, 0, 0)),
            pl.BlockSpec((2, 1, TALL), lambda i: (i + first, 0, 0)),
            pl.BlockSpec((1, TALL), lambda i: (0, 0)),
        ]
        + [ANY_SPEC] * len(held),
        out_specs=[tall, short, short, pl.BlockSpec((2, 1, 768), lambda i: (i, 0, 0))],
        input_output_aliases={8 + index: index for index in range(len(held))},
        scratch_shapes=[
            pltpu.VMEM((2, LEN, TALL), jnp.bfloat16),
            pltpu.VMEM((2, 128, 512), jnp.float32),
            pltpu.VMEM((128, TALL), jnp.float32),
            pltpu.VMEM((128, TALL), jnp.bfloat16),
            pltpu.VMEM((128, TALL), jnp.bfloat16),
            pltpu.VMEM((128, TALL), jnp.float32),
        ],
        compiler_params=PARAMS,
        cost_estimate=pl.CostEstimate(flops=8000000000, bytes_accessed=16000000, transcendentals=0),
        name="mix_back",
    )(q, k, v, da, a, p, inverse, dead, *held)


GELU_SCALE = 0.7978845608028654
GELU_CUBE = 0.044715


def feed_rows(rows, small_ref, hidden_bias_ref, resid, normed_ref, pre_ref, inner_ref, outer_ref):
    unit, scale = norm_parts(resid)
    normed = unit * small_ref[3:4, :] + small_ref[4:5, :]
    low = normed.astype(jnp.bfloat16)
    normed_ref[rows, :] = low
    total = normed + small_ref[5:6, :]
    for chunk in range(4):
        pre = dot_nn(low, inner_ref[chunk]) + hidden_bias_ref[:, chunk * D : chunk * D + D]
        pre_ref[chunk, rows, :] = pre.astype(jnp.bfloat16)
        tanh = jnp.tanh(GELU_SCALE * (pre + GELU_CUBE * (pre * pre * pre)))
        active = (pre * (0.5 + 0.5 * tanh)).astype(jnp.bfloat16)
        total = total + dot_nn(active, outer_ref[chunk])
    return total


def norm_two_back(unit, scale, grad, small_ref, sums):
    back = norm_back(unit, scale, grad, small_ref[6:7, :])
    low = back.astype(jnp.bfloat16)
    parts = (low.astype(jnp.float32), grad * unit, grad)
    return back, low, [
        total + jnp.sum(part, axis=0, keepdims=True) for total, part in zip(sums, parts)
    ]


def issue(pairs, sems, first=0):
    copies = [
        pltpu.make_async_copy(source, target, sems.at[first + index])
        for index, (source, target) in enumerate(pairs)
    ]
    for copy in copies:
        copy.start()
    return copies


def finish(copies):
    for copy in copies:
        copy.wait()


def storer(sems):
    copies = []

    def store(source, target):
        copy = pltpu.make_async_copy(source, target, sems.at[len(copies)])
        copy.start()
        copies.append(copy)

    return store, copies


def feed_kernel(
    plan, place_ref, small_ref, hidden_bias_ref, mix_any, hidden_any, attn_any, *refs
):
    (
        resid_out, pre_out, normed_out, low_out, summed_out,
        mix_ref, hidden_ref, wo_ref, inner_ref, outer_ref, resid_ref, total_ref, normed_ref,
        pre_ref, low_ref, sems, load_sems, store_sems,
    ) = refs[-18:]
    finish(
        issue(
            ((mix_any, mix_ref), (attn_any.at[3], wo_ref), (hidden_any, hidden_ref)), load_sems
        )
    )
    fetches = start_fetch(
        ("inner", "outer"), plan, place_ref, refs[:-18], (inner_ref, outer_ref), sems
    )
    for row in range(0, TALL, HALF):
        rows = slice(row, row + HALF)
        resid_ref[rows, :] = (
            hidden_ref[rows, :].astype(jnp.float32)
            + dot_nn(mix_ref[rows, :], wo_ref[...])
            + small_ref[2:3, :]
        )
    finish(fetches)
    store, stores = storer(store_sems)
    store(resid_ref, resid_out)
    for row in range(0, TALL, HALF):
        rows = slice(row, row + HALF)
        total = feed_rows(
            rows, small_ref, hidden_bias_ref, resid_ref[rows, :], normed_ref, pre_ref, inner_ref,
            outer_ref,
        )
        total_ref[rows, :] = total
        store(pre_ref.at[:, rows, :], pre_out.at[:, rows, :])
        store(total_ref.at[rows, :], summed_out.at[rows, :])
        store(normed_ref.at[rows, :], normed_out.at[rows, :])
        unit, scale = norm_parts(total)
        following = unit * small_ref[6:7, :] + small_ref[7:8, :]
        low_ref[rows, :] = following.astype(jnp.bfloat16)
        store(low_ref.at[rows, :], low_out.at[rows, :])
    finish(stores)


def feed(place, small, hidden_bias, mixed, hidden, attn, group):
    plan, pieces = group
    tall = jax.ShapeDtypeStruct((TALL, D), jnp.float32)
    tall_low = jax.ShapeDtypeStruct((TALL, D), jnp.bfloat16)
    return pl.pallas_call(
        partial(feed_kernel, plan),
        out_shape=[
            tall, jax.ShapeDtypeStruct((4, TALL, D), jnp.bfloat16), tall_low, tall_low, tall
        ],
        in_specs=[SMEM_SPEC, VMEM_SPEC, VMEM_SPEC] + [ANY_SPEC] * (3 + len(pieces)),
        out_specs=[ANY_SPEC] * 5,
        scratch_shapes=[
            pltpu.VMEM((TALL, D), jnp.bfloat16),
            pltpu.VMEM((TALL, D), jnp.bfloat16),
            pltpu.VMEM((D, D), jnp.bfloat16),
            pltpu.VMEM((4, D, D), jnp.bfloat16),
            pltpu.VMEM((4, D, D), jnp.bfloat16),
            pltpu.VMEM((TALL, D), jnp.float32),
            pltpu.VMEM((TALL, D), jnp.float32),
            pltpu.VMEM((TALL, D), jnp.bfloat16),
            pltpu.VMEM((4, TALL, D), jnp.bfloat16),
            pltpu.VMEM((TALL, D), jnp.bfloat16),
            pltpu.SemaphoreType.DMA((64,)),
            pltpu.SemaphoreType.DMA((3,)),
            pltpu.SemaphoreType.DMA((17,)),
        ],
        compiler_params=PARAMS,
        cost_estimate=pl.CostEstimate(flops=2 * TALL * D * (D + 2 * FF), bytes_accessed=30000000, transcendentals=3000000),
        name="feed",
    )(place, small, hidden_bias, mixed, hidden, attn, *pieces)


def back_steps(
    place_ref, small_ref, before, store, outs, vec_ref, dhidden_ref, branch_ref, total_ref,
    normed_ref, resid_ref, pre_ref, mix_ref, wo_ref, inner_ref, outer_ref, active_ref, dpre_ref,
    dinner_ref, douter_ref, dwo_ref,
):
    dresid_out, dmix_out, dwo_out, keep_out, send_out = outs
    x, c, z, y = (place_ref[index] for index in range(4))
    order = [(1 - step // 2, step % 2) for step in range(4)]
    chunks = [side * 2 + (c ^ apart) for apart, side in order]
    sums = [jnp.zeros((1, D), jnp.float32)] * 3
    for step in range(4):
        apart, side = order[step]
        chunk = chunks[step]
        before(step)
        bias_grad = jnp.zeros((1, D), jnp.float32)
        for row in range(0, TALL, HALF):
            rows = slice(row, row + HALF)
            pull = dot_nt(branch_ref[rows, :], outer_ref[chunk])
            pre = pre_ref[chunk, rows, :].astype(jnp.float32)
            square = pre * pre
            tanh = jnp.tanh(GELU_SCALE * pre * (1.0 + GELU_CUBE * square))
            half = 0.5 + 0.5 * tanh
            active_ref[rows, :] = (pre * half).astype(jnp.bfloat16)
            slope = half + (0.5 * GELU_SCALE) * pre * (1.0 - tanh * tanh) * (
                1.0 + (3.0 * GELU_CUBE) * square
            )
            dpre = (pull * slope).astype(jnp.bfloat16)
            dpre_ref[rows, :] = dpre
            bias_grad += jnp.sum(dpre.astype(jnp.float32), axis=0, keepdims=True)
            grad = total_ref[rows, :] + dot_nt(dpre, inner_ref[chunk])
            if step < 3:
                total_ref[rows, :] = grad
            else:
                unit, scale = norm_parts(resid_ref[rows, :])
                back = norm_back(unit, scale, grad, small_ref[3:4, :])
                resid_ref[rows, :] = back
                low = back.astype(jnp.bfloat16)
                pre_ref[chunks[0], rows, :] = low
                pre_ref[chunks[1], rows, :] = dot_nt(low, wo_ref[...]).astype(jnp.bfloat16)
                parts = (low.astype(jnp.float32), grad * unit, grad)
                sums = [
                    value + jnp.sum(part, axis=0, keepdims=True)
                    for value, part in zip(sums, parts)
                ]
        dhidden_ref[chunk] = bias_grad
        if step == 3:
            store(resid_ref, dresid_out)
            store(pre_ref.at[chunks[1]], dmix_out)
        douter_ref[step] = (
            dot_tn(active_ref[...], branch_ref[...]).astype(jnp.bfloat16).reshape(2, 2, 2, ROWS, D)
        )
        for y_block in range(2):
            for x_block in range(2):
                spot = (y_block ^ y, x_block ^ x, chunk, 1)
                store(douter_ref.at[step, y_block, x_block, c], keep_out.at[spot])
                store(douter_ref.at[step, y_block, x_block, 1 - c], send_out.at[spot])
        dinner_ref[step] = (
            dot_tn(normed_ref[...], dpre_ref[...]).astype(jnp.bfloat16).reshape(4, 2, ROWS, D)
        )
        target = send_out if apart else keep_out
        for y_block in range(2):
            store(dinner_ref.at[step, :, y_block], target.at[y_block ^ y, side ^ x, :, 0])
    dwo_ref[...] = dot_tn(mix_ref[...], pre_ref[chunks[0]]).astype(jnp.bfloat16)
    store(dwo_ref, dwo_out)
    for index, value in enumerate(sums):
        vec_ref[index : index + 1, :] = value


BACK_SHAPES = [
    jax.ShapeDtypeStruct((TALL, D), jnp.float32),
    jax.ShapeDtypeStruct((TALL, D), jnp.bfloat16),
    jax.ShapeDtypeStruct((D, D), jnp.bfloat16),
    jax.ShapeDtypeStruct((2, 2, 4, 2, ROWS, D), jnp.bfloat16),
    jax.ShapeDtypeStruct((2, 2, 4, 2, ROWS, D), jnp.bfloat16),
    jax.ShapeDtypeStruct((6, D), jnp.float32),
    jax.ShapeDtypeStruct((4, 1, D), jnp.float32),
]
BACK_SCRATCH = [
    pltpu.VMEM((TALL, D), jnp.bfloat16),
    pltpu.VMEM((TALL, D), jnp.float32),
    pltpu.VMEM((TALL, D), jnp.bfloat16),
    pltpu.VMEM((TALL, D), jnp.float32),
    pltpu.VMEM((4, TALL, D), jnp.bfloat16),
    pltpu.VMEM((TALL, D), jnp.bfloat16),
    pltpu.VMEM((D, D), jnp.bfloat16),
    pltpu.VMEM((4, D, D), jnp.bfloat16),
    pltpu.VMEM((4, D, D), jnp.bfloat16),
    pltpu.VMEM((TALL, D), jnp.bfloat16),
    pltpu.VMEM((TALL, D), jnp.bfloat16),
    pltpu.VMEM((4, 4, 2, ROWS, D), jnp.bfloat16),
    pltpu.VMEM((4, 2, 2, 2, ROWS, D), jnp.bfloat16),
    pltpu.VMEM((D, D), jnp.bfloat16),
    pltpu.SemaphoreType.DMA((64,)),
    pltpu.SemaphoreType.DMA((16,)),
    pltpu.SemaphoreType.DMA((48,)),
]


def turn_kernel(
    plan, place_ref, length_ref, small_ref, below_ref, hidden_bias_ref, mix_any, summed_any,
    attn_any, cot_c_any, cot_q_any, *refs
):
    content_out, query_out = refs[-27:-25]
    outs = refs[-25:-20]
    vec_ref, dhidden_ref = refs[-20:-18]
    low_ref = refs[-18]
    (
        branch_ref, total_ref, normed_ref, resid_ref, pre_ref, mix_ref, wo_ref, inner_ref,
        outer_ref, active_ref, dpre_ref, dinner_ref, douter_ref, dwo_ref,
        sems, load_sems, store_sems,
    ) = refs[-17:]
    store, stores = storer(store_sems)
    finish(
        issue(
            ((mix_any, mix_ref), (attn_any.at[3], wo_ref), (summed_any, resid_ref)), load_sems
        )
    )
    fetches = start_fetch(
        ("inner", "outer"), plan, place_ref, refs[:-27], (inner_ref, outer_ref), sems
    )
    fetches += issue(
        ((cot_c_any, low_ref.at[:LEN, :]), (cot_q_any, low_ref.at[LEN:, :])), load_sems, 3
    )
    for row in range(0, TALL, HALF):
        rows = slice(row, row + HALF)
        unit, scale = norm_parts(resid_ref[rows, :])
        resid_ref[rows, :] = (
            unit * below_ref[6:7, :]
            + below_ref[7:8, :]
            + dot_nn(mix_ref[rows, :], wo_ref[...])
            + small_ref[2:3, :]
        )
    finish(fetches)
    sums = [jnp.zeros((1, D), jnp.float32)] * 3
    for row in range(0, TALL, HALF):
        rows = slice(row, row + HALF)
        total = feed_rows(
            rows, small_ref, hidden_bias_ref, resid_ref[rows, :], normed_ref, pre_ref, inner_ref,
            outer_ref,
        )
        unit, scale = norm_parts(total)
        position = lax.broadcasted_iota(jnp.int32, (HALF, 1), 0) + row % LEN
        valid = (position < length_ref[0]).astype(jnp.float32)
        grad = low_ref[rows, :].astype(jnp.float32) * valid
        low_ref[rows, :] = (unit * small_ref[6:7, :] + small_ref[7:8, :]).astype(jnp.bfloat16)
        total_ref[rows, :], branch_ref[rows, :], sums = norm_two_back(
            unit, scale, grad, small_ref, sums
        )
    store(low_ref.at[:LEN, :], content_out)
    store(low_ref.at[LEN:, :], query_out)
    for index, value in enumerate(sums):
        vec_ref[3 + index : 4 + index, :] = value
    back_steps(
        place_ref, small_ref, lambda step: None, store, outs, vec_ref, dhidden_ref, branch_ref,
        total_ref, normed_ref, resid_ref, pre_ref, mix_ref, wo_ref, inner_ref, outer_ref,
        active_ref, dpre_ref, dinner_ref, douter_ref, dwo_ref,
    )
    finish(stores)


def turn(place, length, small, below, hidden_bias, mixed, summed, attn, cots, group):
    plan, pieces = group
    half_low = jax.ShapeDtypeStruct((LEN, D), jnp.bfloat16)
    return pl.pallas_call(
        partial(turn_kernel, plan),
        out_shape=[half_low, half_low] + BACK_SHAPES,
        in_specs=[SMEM_SPEC] * 2 + [VMEM_SPEC] * 3 + [ANY_SPEC] * (5 + len(pieces)),
        out_specs=[ANY_SPEC] * 7 + [VMEM_SPEC] * 2,
        scratch_shapes=[pltpu.VMEM((TALL, D), jnp.bfloat16)] + BACK_SCRATCH,
        compiler_params=PARAMS,
        cost_estimate=pl.CostEstimate(flops=6 * TALL * D * (D + 2 * FF), bytes_accessed=60000000, transcendentals=6000000),
        name="turn",
    )(place, length, small, below, hidden_bias, mixed, summed, attn, *cots, *pieces)


def down_kernel(
    plan, place_ref, small_ref, dq_any, dk_any, dv_any, w_any, dresid_any, summed_any,
    normed_any, resid_any, pre_any, mix_any, attn_any, *refs
):
    outs = refs[-29:-24]
    vec_ref, dhidden_ref = refs[-24:-22]
    dq_ref, dk_ref, dv_ref, w_ref, summed_ref = refs[-22:-17]
    (
        branch_ref, total_ref, normed_ref, resid_ref, pre_ref, mix_ref, wo_ref, inner_ref,
        outer_ref, active_ref, dpre_ref, dinner_ref, douter_ref, dwo_ref,
        sems, load_sems, store_sems,
    ) = refs[-17:]
    x, c, z, y = (place_ref[index] for index in range(4))
    chunks = [side * 2 + (c ^ apart) for apart in (1, 0) for side in range(2)]
    store, stores = storer(store_sems)
    loads = issue(
        (
            (w_any.at[0], w_ref.at[0]), (dq_any, dq_ref), (dresid_any, total_ref),
            (summed_any, summed_ref), (w_any.at[1:3], w_ref.at[1:3]), (dk_any, dk_ref),
            (dv_any, dv_ref),
        ),
        load_sems,
    )
    finish(loads[:4])
    fetches = start_fetch(
        ("inner", "outer"), plan, place_ref, refs[:-29], (inner_ref, outer_ref), sems
    )
    fetches += issue(((pre_any.at[chunks[0]], pre_ref.at[chunks[0]]),), load_sems, 7)
    sums = [jnp.zeros((1, D), jnp.float32)] * 3
    for index, row in enumerate((LEN, LEN + HALF, 0, HALF)):
        rows = slice(row, row + HALF)
        if index == 2:
            finish(loads[4:])
        total = total_ref[rows, :] + dot_nt(dq_ref[rows, :], w_ref[0])
        if index >= 2:
            total = total + dot_nt(dk_ref[rows, :], w_ref[1]) + dot_nt(dv_ref[rows, :], w_ref[2])
        unit, scale = norm_parts(summed_ref[rows, :])
        total_ref[rows, :], branch_ref[rows, :], sums = norm_two_back(
            unit, scale, total, small_ref, sums
        )
    for index, value in enumerate(sums):
        vec_ref[3 + index : 4 + index, :] = value
    finish(fetches)
    late = []

    def before(step):
        if step == 0:
            late.append(issue(((normed_any, normed_ref),), load_sems, 8))
        else:
            finish(late.pop())
        if step < 3:
            chunk = chunks[step + 1]
            late.insert(0, issue(((pre_any.at[chunk], pre_ref.at[chunk]),), load_sems, 9 + step))
        if step == 0:
            finish(late.pop())
        if step == 2:
            late[0].extend(
                issue(
                    ((resid_any, resid_ref), (mix_any, mix_ref), (attn_any.at[3], wo_ref)),
                    load_sems,
                    12,
                )
            )

    back_steps(
        place_ref, small_ref, before, store, outs, vec_ref, dhidden_ref, branch_ref, total_ref,
        normed_ref, resid_ref, pre_ref, mix_ref, wo_ref, inner_ref, outer_ref, active_ref,
        dpre_ref, dinner_ref, douter_ref, dwo_ref,
    )
    finish(stores)


def down(place, small, dq, dk, dv, w_above, dresid, summed, normed, resid, pre, mixed, attn, group):
    plan, pieces = group
    return pl.pallas_call(
        partial(down_kernel, plan),
        out_shape=BACK_SHAPES,
        in_specs=[SMEM_SPEC, VMEM_SPEC] + [ANY_SPEC] * (11 + len(pieces)),
        out_specs=[ANY_SPEC] * 5 + [VMEM_SPEC] * 2,
        scratch_shapes=[
            pltpu.VMEM((TALL, D), jnp.bfloat16),
            pltpu.VMEM((LEN, D), jnp.bfloat16),
            pltpu.VMEM((LEN, D), jnp.bfloat16),
            pltpu.VMEM((3, D, D), jnp.bfloat16),
            pltpu.VMEM((TALL, D), jnp.float32),
        ]
        + BACK_SCRATCH,
        compiler_params=PARAMS,
        cost_estimate=pl.CostEstimate(flops=5 * TALL * D * (D + 2 * FF), bytes_accessed=60000000, transcendentals=3000000),
        name="down",
    )(place, small, dq, dk, dv, w_above, dresid, summed, normed, resid, pre, mixed, attn, *pieces)


def weight_back_kernel(
    place_ref, low_any, dq_any, dk_any, dv_any, dwo_any, keep_out, send_out, vec_ref,
    low_ref, dq_ref, dk_ref, dv_ref, dwo_ref, grads_ref, load_sems, sems,
):
    x, c, z, y = (place_ref[index] for index in range(4))
    load = [
        pltpu.make_async_copy(source, target, load_sems.at[index])
        for index, (source, target) in enumerate(
            (
                (low_any.at[:LEN, :], low_ref.at[:LEN, :]), (dk_any, dk_ref), (dv_any, dv_ref),
                (low_any.at[LEN:, :], low_ref.at[LEN:, :]), (dq_any, dq_ref), (dwo_any, dwo_ref),
            )
        )
    ]
    for copy in load:
        copy.start()
    load[0].wait()
    load[1].wait()
    grads_ref[1] = (
        dot_tn(low_ref[:LEN, :], dk_ref[...]).astype(jnp.bfloat16).reshape(4, 2, ROWS, D)
    )
    load[2].wait()
    grads_ref[2] = (
        dot_tn(low_ref[:LEN, :], dv_ref[...]).astype(jnp.bfloat16).reshape(4, 2, ROWS, D)
    )
    vec_ref[1:2, :] = jnp.sum(dv_ref[...].astype(jnp.float32), axis=0, keepdims=True)
    for copy in load[3:]:
        copy.wait()
    grads_ref[3] = dwo_ref[...].reshape(4, 2, ROWS, D)
    grads_ref[0] = dot_tn(low_ref[...], dq_ref[...]).astype(jnp.bfloat16).reshape(4, 2, ROWS, D)
    vec_ref[0:1, :] = jnp.sum(dq_ref[...].astype(jnp.float32), axis=0, keepdims=True)
    blocks = []
    for apart, target in ((1, send_out), (0, keep_out)):
        for side in range(2):
            for y_block in range(2):
                copy = pltpu.make_async_copy(
                    grads_ref.at[side * 2 + (c ^ apart), :, y_block],
                    target.at[y_block ^ y, side ^ x, :, 0],
                    sems.at[len(blocks)],
                )
                copy.start()
                blocks.append(copy)
    for block in blocks:
        block.wait()


def weight_back(place, low, dq, dk, dv, dwo):
    blocks = jax.ShapeDtypeStruct((2, 2, 4, 1, ROWS, D), jnp.bfloat16)
    return pl.pallas_call(
        weight_back_kernel,
        out_shape=[blocks, blocks, jax.ShapeDtypeStruct((2, D), jnp.float32)],
        in_specs=[SMEM_SPEC] + [ANY_SPEC] * 5,
        out_specs=[ANY_SPEC] * 2 + [VMEM_SPEC],
        scratch_shapes=[
            pltpu.VMEM((TALL, D), jnp.bfloat16),
            pltpu.VMEM((TALL, D), jnp.bfloat16),
            pltpu.VMEM((LEN, D), jnp.bfloat16),
            pltpu.VMEM((LEN, D), jnp.bfloat16),
            pltpu.VMEM((D, D), jnp.bfloat16),
            pltpu.VMEM((4, 4, 2, ROWS, D), jnp.bfloat16),
            pltpu.SemaphoreType.DMA((6,)),
            pltpu.SemaphoreType.DMA((8,)),
        ],
        compiler_params=PARAMS,
        cost_estimate=pl.CostEstimate(flops=2 * 2048 * D * D, bytes_accessed=12000000, transcendentals=0),
        name="weight_back",
    )(place, low, dq, dk, dv, dwo)


def input_back_kernel(
    dq_any, dk_any, dv_any, w_any, dresid_any, first_out, second_out,
    dq_ref, dk_ref, dv_ref, w_ref, dresid_ref, load_sems, store_sems,
):
    loads = issue(
        (
            (w_any.at[0], w_ref.at[0]), (dq_any, dq_ref), (dresid_any, dresid_ref),
            (w_any.at[1:3], w_ref.at[1:3]), (dk_any, dk_ref), (dv_any, dv_ref),
        ),
        load_sems,
    )
    finish(loads[:3])
    store, stores = storer(store_sems)
    for index, row in enumerate((LEN, LEN + HALF, 0, HALF)):
        rows = slice(row, row + HALF)
        if index == 2:
            finish(loads[3:])
        total = dresid_ref[rows, :] + dot_nt(dq_ref[rows, :], w_ref[0])
        if index >= 2:
            total = total + dot_nt(dk_ref[rows, :], w_ref[1]) + dot_nt(dv_ref[rows, :], w_ref[2])
        dresid_ref[rows, :] = total
        target = first_out if index >= 2 else second_out
        store(dresid_ref.at[rows, :], target.at[row % LEN : row % LEN + HALF, :])
    finish(stores)


def input_back(dq, dk, dv, attn, dresid):
    half = jax.ShapeDtypeStruct((LEN, D), jnp.float32)
    return pl.pallas_call(
        input_back_kernel,
        out_shape=[half, half],
        in_specs=[ANY_SPEC] * 5,
        out_specs=[ANY_SPEC] * 2,
        scratch_shapes=[
            pltpu.VMEM((TALL, D), jnp.bfloat16),
            pltpu.VMEM((LEN, D), jnp.bfloat16),
            pltpu.VMEM((LEN, D), jnp.bfloat16),
            pltpu.VMEM((3, D, D), jnp.bfloat16),
            pltpu.VMEM((TALL, D), jnp.float32),
            pltpu.SemaphoreType.DMA((6,)),
            pltpu.SemaphoreType.DMA((4,)),
        ],
        compiler_params=PARAMS,
        cost_estimate=pl.CostEstimate(flops=2 * 2048 * D * D, bytes_accessed=16000000, transcendentals=0),
        name="input_back",
    )(dq, dk, dv, attn, dresid)


def bias_vectors(table):
    lane = jnp.arange(512, dtype=jnp.int32)
    offset = jnp.where(lane < 384, 128 - lane, 640 - lane)
    onehot = bucket_of(offset)[:, None] == jnp.arange(NB, dtype=jnp.int32)[None, :]
    near = jnp.dot(table, onehot.astype(jnp.float32).T, precision=lax.Precision.HIGHEST)
    return (near[:, None, :], jnp.stack([table[:, 15], table[:, 31]], axis=1), onehot)


def bucket_of(offset):
    distance = jnp.abs(offset)
    far_bucket = jnp.full(distance.shape, 8, jnp.int32)
    for exponent in range(1, 8):
        far_bucket = far_bucket + (distance * distance >= 64 * 2**exponent).astype(jnp.int32)
    near_or_far = jnp.where(distance < 8, distance, far_bucket)
    return near_or_far + NB // 2 * (offset > 0).astype(jnp.int32)


def table_grad(sums, onehot):
    near = jnp.roll(onehot.astype(jnp.float32), 127, axis=0)
    far = jnp.arange(NB, dtype=jnp.int32)[None, :] == jnp.repeat(jnp.array([15, 31]), 128)[:, None]
    return jnp.dot(
        sums[:, 0, :],
        jnp.concatenate([near, far.astype(jnp.float32)]),
        precision=lax.Precision.HIGHEST,
    )


RATES = (ATTENTION_RATE, FEED_RATE, FEED_RATE)


def adam_kernel(*refs):
    states, grads, outs = refs[:9], refs[9:12], refs[-9:]
    for kind, rate in enumerate(RATES):
        master_ref, first_ref, second_ref = states[3 * kind : 3 * kind + 3]
        master_out, first_out, second_out = outs[3 * kind : 3 * kind + 3]
        grad = grads[kind][...].astype(jnp.float32).reshape(master_ref.shape)
        master = master_ref[...]
        first = BETA_ONE * first_ref[...] + (1.0 - BETA_ONE) * grad
        second = BETA_TWO * second_ref[...] + (1.0 - BETA_TWO) * grad * grad
        first_out[...] = first
        second_out[...] = second
        first_scale = rate / (1.0 - BETA_ONE**STEP)
        second_scale = 1.0 / (1.0 - BETA_TWO**STEP)
        step = (first_scale * first) / (jnp.sqrt(second_scale * second) + ADAM_EPS)
        master_out[...] = master - (step + (rate * WEIGHT_DECAY) * master)


def adam(layer, state, quarters, held):
    half = ROWS // 2
    blocks = (
        [pl.BlockSpec((1, 1, half, D), lambda i: (layer, i // 2, i % 2, 0))] * 3
        + [pl.BlockSpec((1, half, D), lambda i: (layer, i % 2, i // 2))] * 3
        + [pl.BlockSpec((1, half, D), lambda i: (layer, i, 0))] * 3
    )
    grads = [
        pl.BlockSpec((1, 1, half, D), partial(lambda member, i: (i // 2, member, i % 2, 0), member))
        for member in (2, 0, 1)
    ]
    return pl.pallas_call(
        adam_kernel,
        grid=(8,),
        out_shape=[jax.ShapeDtypeStruct(array.shape, jnp.float32) for array in state],
        in_specs=blocks + grads + [ANY_SPEC] * len(held),
        out_specs=blocks,
        input_output_aliases={12 + index: index for index in range(len(held))},
        compiler_params=PARAMS,
        cost_estimate=pl.CostEstimate(flops=20000000, bytes_accessed=22000000, transcendentals=0),
        name="adam",
    )(*state, quarters, quarters, quarters, *held)


def fetch_forward(shards):
    low = tuple(shard.astype(jnp.bfloat16) for shard in shards)
    return (
        lax.all_gather(low[0], "fsdp", axis=1, tiled=True),
        lax.all_gather(low[1], "fsdp", axis=0, tiled=True),
        lax.all_gather(low[2], "fsdp", axis=0, tiled=True),
    )


def reduce_layer(grads):
    owned = tuple(
        lax.psum_scatter(
            grad.astype(jnp.bfloat16), "fsdp", scatter_dimension=axis, tiled=True
        ).astype(jnp.float32)
        for grad, axis in zip(grads, (1, 0, 0))
    )
    return lax.psum(owned, "dp")


def forward_layer(hidden_c, hidden_q, weights, lengths, flag_rows, onehot):
    attn_w, inner_w, outer_w, small_w = weights
    pieces, hidden_bias, bias_table = unpack(small_w.astype(jnp.float32))
    bias_q, bias_v, bias_o, gain_one, shift_one, bias_two, gain_two, shift_two = pieces
    table_low = bias_table.astype(jnp.bfloat16)
    low_c = hidden_c.astype(jnp.bfloat16)
    low_q = hidden_q.astype(jnp.bfloat16)
    projected = jnp.einsum("td,sde->ste", low_c, attn_w[:3], preferred_element_type=jnp.float32)
    query_c = (projected[0] + bias_q).astype(jnp.bfloat16)
    key_rows = projected[1].astype(jnp.bfloat16)
    value_rows = (projected[2] + bias_v).astype(jnp.bfloat16)
    query_q = (jnp.dot(low_q, attn_w[0], preferred_element_type=jnp.float32) + bias_q).astype(
        jnp.bfloat16
    )
    mixed_c, mixed_q, lse_c, lse_q = lax.map(
        partial(attend_slot, onehot, table_low),
        (
            to_heads(query_c),
            to_heads(query_q),
            to_heads(key_rows),
            to_heads(value_rows),
            lengths,
            flag_rows,
        ),
    )
    mixed_c = mixed_c.reshape(-1, D)
    mixed_q = mixed_q.reshape(-1, D)
    outputs = []
    kept = []
    for hidden_in, mixed in ((hidden_c, mixed_c), (hidden_q, mixed_q)):
        resid = hidden_in + jnp.dot(mixed, attn_w[3], preferred_element_type=jnp.float32) + bias_o
        normed = layer_norm(resid, gain_one, shift_one)
        pre_act = (
            jnp.dot(normed.astype(jnp.bfloat16), inner_w, preferred_element_type=jnp.float32)
            + hidden_bias
        )
        active = jax.nn.gelu(pre_act, approximate=True).astype(jnp.bfloat16)
        summed = normed + jnp.dot(active, outer_w, preferred_element_type=jnp.float32) + bias_two
        outputs.append(layer_norm(summed, gain_two, shift_two))
        kept.append((resid, summed, pre_act))
    saved = (
        hidden_c,
        hidden_q,
        query_c,
        query_q,
        key_rows,
        value_rows,
        lse_c,
        lse_q,
        mixed_c,
        mixed_q,
        kept[0],
        kept[1],
    )
    return (outputs[0], outputs[1], saved)


def backward_layer(saved, weights, grad_c, grad_q, lengths, flag_rows, onehot):
    attn_w, inner_w, outer_w, small_w = weights
    pieces, hidden_bias, bias_table = unpack(small_w.astype(jnp.float32))
    bias_q, bias_v, bias_o, gain_one, shift_one, bias_two, gain_two, shift_two = pieces
    table_low = bias_table.astype(jnp.bfloat16)
    (
        hidden_c,
        hidden_q,
        query_c,
        query_q,
        key_rows,
        value_rows,
        lse_c,
        lse_q,
        mixed_c,
        mixed_q,
        kept_c,
        kept_q,
    ) = saved
    gelu_tanh = partial(jax.nn.gelu, approximate=True)
    grad_outer = jnp.zeros(outer_w.shape, jnp.float32)
    grad_inner = jnp.zeros(inner_w.shape, jnp.float32)
    grad_attn_out = jnp.zeros((D, D), jnp.float32)
    grad_bias_two = jnp.zeros((D,), jnp.float32)
    grad_hidden_bias = jnp.zeros((FF,), jnp.float32)
    grad_bias_o = jnp.zeros((D,), jnp.float32)
    grad_gain_one = jnp.zeros((D,), jnp.float32)
    grad_shift_one = jnp.zeros((D,), jnp.float32)
    grad_gain_two = jnp.zeros((D,), jnp.float32)
    grad_shift_two = jnp.zeros((D,), jnp.float32)
    residual_grads = []
    mix_grads = []
    for kept_rows, grad_out, mixed in ((kept_c, grad_c, mixed_c), (kept_q, grad_q, mixed_q)):
        resid, summed, pre_act = kept_rows
        normed, norm_one_back = jax.vjp(layer_norm, resid, gain_one, shift_one)
        unused_out, norm_two_back = jax.vjp(layer_norm, summed, gain_two, shift_two)
        grad_summed, grad_g2, grad_s2 = norm_two_back(grad_out)
        grad_gain_two = grad_gain_two + grad_g2
        grad_shift_two = grad_shift_two + grad_s2
        grad_branch = grad_summed.astype(jnp.bfloat16)
        grad_bias_two = grad_bias_two + jnp.sum(grad_branch.astype(jnp.float32), axis=0)
        active, gelu_back = jax.vjp(gelu_tanh, pre_act)
        grad_outer = grad_outer + jnp.einsum(
            "tf,td->fd",
            active.astype(jnp.bfloat16),
            grad_branch,
            preferred_element_type=jnp.float32,
        )
        grad_active = jnp.einsum(
            "td,fd->tf", grad_branch, outer_w, preferred_element_type=jnp.float32
        )
        grad_pre = gelu_back(grad_active)[0].astype(jnp.bfloat16)
        grad_hidden_bias = grad_hidden_bias + jnp.sum(grad_pre.astype(jnp.float32), axis=0)
        grad_inner = grad_inner + jnp.einsum(
            "td,tf->df", normed.astype(jnp.bfloat16), grad_pre, preferred_element_type=jnp.float32
        )
        grad_normed = grad_summed + jnp.einsum(
            "tf,df->td", grad_pre, inner_w, preferred_element_type=jnp.float32
        )
        grad_resid, grad_g1, grad_s1 = norm_one_back(grad_normed)
        grad_gain_one = grad_gain_one + grad_g1
        grad_shift_one = grad_shift_one + grad_s1
        grad_proj = grad_resid.astype(jnp.bfloat16)
        grad_bias_o = grad_bias_o + jnp.sum(grad_proj.astype(jnp.float32), axis=0)
        grad_attn_out = grad_attn_out + jnp.einsum(
            "td,te->de", mixed, grad_proj, preferred_element_type=jnp.float32
        )
        mix_grads.append(
            jnp.einsum(
                "te,de->td", grad_proj, attn_w[3], preferred_element_type=jnp.float32
            ).astype(jnp.bfloat16)
        )
        residual_grads.append(grad_resid)
    grad_query_c, grad_query_q, grad_keys, grad_values, grad_table = lax.map(
        partial(attend_back, onehot, table_low),
        (
            to_heads(query_c),
            to_heads(query_q),
            to_heads(key_rows),
            to_heads(value_rows),
            lengths,
            flag_rows,
            lse_c,
            lse_q,
            to_heads(mix_grads[0]),
            to_heads(mix_grads[1]),
        ),
    )
    grad_table = jnp.sum(grad_table, axis=0)
    low_query_c = grad_query_c.reshape(-1, D).astype(jnp.bfloat16)
    low_query_q = grad_query_q.reshape(-1, D).astype(jnp.bfloat16)
    low_keys = grad_keys.reshape(-1, D).astype(jnp.bfloat16)
    low_values = grad_values.reshape(-1, D).astype(jnp.bfloat16)
    low_c = hidden_c.astype(jnp.bfloat16)
    low_q = hidden_q.astype(jnp.bfloat16)
    stacked_grads = jnp.stack([low_query_c, low_keys, low_values])
    grad_qkv = jnp.einsum("td,ste->sde", low_c, stacked_grads, preferred_element_type=jnp.float32)
    grad_wq = grad_qkv[0] + jnp.einsum(
        "td,te->de", low_q, low_query_q, preferred_element_type=jnp.float32
    )
    grad_attn = jnp.stack([grad_wq, grad_qkv[1], grad_qkv[2], grad_attn_out])
    grad_bias_q = jnp.sum(low_query_c.astype(jnp.float32), axis=0) + jnp.sum(
        low_query_q.astype(jnp.float32), axis=0
    )
    grad_bias_v = jnp.sum(low_values.astype(jnp.float32), axis=0)
    grad_content = residual_grads[0] + jnp.einsum(
        "ste,sde->td", stacked_grads, attn_w[:3], preferred_element_type=jnp.float32
    )
    grad_query_in = residual_grads[1] + jnp.einsum(
        "te,de->td", low_query_q, attn_w[0], preferred_element_type=jnp.float32
    )
    grad_small = jnp.concatenate(
        [
            grad_bias_q,
            grad_bias_v,
            grad_bias_o,
            grad_gain_one,
            grad_shift_one,
            grad_bias_two,
            grad_gain_two,
            grad_shift_two,
            grad_hidden_bias,
            grad_table.reshape(-1),
        ]
    )
    return (grad_content, grad_query_in, (grad_attn, grad_inner, grad_outer, grad_small))


def adam_update(master, first, second, grad, rate):
    first_new = BETA_ONE * first + (1.0 - BETA_ONE) * grad
    second_new = BETA_TWO * second + (1.0 - BETA_TWO) * grad * grad
    first_hat = first_new / (1.0 - BETA_ONE**STEP)
    second_hat = second_new / (1.0 - BETA_TWO**STEP)
    master_new = master - rate * (
        first_hat / (jnp.sqrt(second_hat) + ADAM_EPS) + WEIGHT_DECAY * master
    )
    return (master_new, first_new, second_new)


def per_device(
    content,
    query,
    lengths,
    predicted,
    content_cot,
    query_cot,
    attn_master,
    attn_first,
    attn_second,
    inner_master,
    inner_first,
    inner_second,
    outer_master,
    outer_first,
    outer_second,
    small_master,
    small_first,
    small_second,
):
    masters = (attn_master, inner_master, outer_master, small_master)
    slot_count = lengths.shape[0]
    flag_rows = predicted.reshape(slot_count, LEN)
    onehot = bucket_onehot()
    hidden_c = content.astype(jnp.float32)
    hidden_q = query.astype(jnp.float32)
    kept_weights = []
    saved_layers = []
    small_all = lax.all_gather(
        small_master.astype(jnp.bfloat16), "fsdp", axis=1, tiled=True
    )
    for layer_index in range(LAYERS):
        shards = tuple((master[layer_index] for master in masters[:3]))
        gathered = fetch_forward(shards) + (small_all[layer_index],)
        kept_weights.append(gathered)
        hidden_c, hidden_q, saved = forward_layer(
            hidden_c, hidden_q, gathered, lengths, flag_rows, onehot
        )
        saved_layers.append(saved)
    position = jnp.arange(LEN, dtype=jnp.int32)
    valid_rows = (position[None, :] < lengths[:, None]).reshape(-1, 1).astype(jnp.float32)
    grad_c = content_cot.astype(jnp.float32) * valid_rows
    grad_q = query_cot.astype(jnp.float32) * valid_rows
    layer_grads = [None] * LAYERS
    small_grads = [None] * LAYERS
    for layer_index in reversed(range(LAYERS)):
        grad_c, grad_q, local_grads = backward_layer(
            saved_layers[layer_index],
            kept_weights[layer_index],
            grad_c,
            grad_q,
            lengths,
            flag_rows,
            onehot,
        )
        small_grads[layer_index] = local_grads[3]
        layer_grads[layer_index] = reduce_layer(local_grads[:3])
    small_sum = lax.psum(jnp.stack(small_grads), ("dp", "fsdp"))
    owned = small_master.shape[1]
    small_own = lax.dynamic_slice_in_dim(
        small_sum, lax.axis_index("fsdp") * owned, owned, 1
    )
    reduced = tuple(
        (
            jnp.stack([layer_grads[layer_index][member] for layer_index in range(LAYERS)])
            for member in range(3)
        )
    ) + (small_own,)
    attn_new = adam_update(attn_master, attn_first, attn_second, reduced[0], ATTENTION_RATE)
    inner_new = adam_update(inner_master, inner_first, inner_second, reduced[1], FEED_RATE)
    outer_new = adam_update(outer_master, outer_first, outer_second, reduced[2], FEED_RATE)
    small_new = adam_update(small_master, small_first, small_second, reduced[3], SMALL_RATE)
    return (
        hidden_c.astype(jnp.bfloat16),
        hidden_q.astype(jnp.bfloat16),
        grad_c,
        grad_q,
        attn_new[0],
        attn_new[1],
        attn_new[2],
        inner_new[0],
        inner_new[1],
        inner_new[2],
        outer_new[0],
        outer_new[1],
        outer_new[2],
        small_new[0],
        small_new[1],
        small_new[2],
    )


def after(value, *others):
    return lax.optimization_barrier((value, others))[0]


def join(*values):
    return lax.optimization_barrier(values)


def gather_group(count, shards, plane, column, sides, corners, mine, theirs):
    plan = []
    for core, arrays in enumerate((mine, theirs)):
        base = core * len(mine)
        for member in range(count):
            array, first = plane
            plan += [
                (base + array, first + side * count + member, side, 1, core, 0, member)
                for side in range(2)
            ]
            for apart in (1, 2, 3):
                index = (apart - 1) * count + member
                array, first = column
                plan.append((base + array, first + index, 0, 0, core, apart, member))
                for dx, dy, (array, first) in ((1, 0, sides[0]), (0, 1, sides[1])):
                    plan.append((base + array, first + index, dx, dy, core, apart, member))
                skipped = 0
                for array, first, held in corners:
                    if skipped <= index < skipped + held:
                        plan.append(
                            (base + array, first + index - skipped, 1, 1, core, apart, member)
                        )
                    skipped += held
    return (tuple(plan), tuple(shards) + tuple(mine) + tuple(theirs))


def gather_small(blocks, place):
    low, high = place[2] % 2, place[2] // 2
    blocks = jnp.where(low == 0, blocks, blocks[jnp.array([1, 0, 3, 2])])
    blocks = jnp.where(high == 0, blocks, blocks[jnp.array([2, 3, 0, 1])])
    return blocks.transpose(2, 0, 1, 3).reshape(blocks.shape[2], -1)


def add_low(*values):
    total = values[0].astype(jnp.float32)
    for value in values[1:]:
        total = total + value.astype(jnp.float32)
    return total.astype(jnp.bfloat16)


def reduce_corners(keep, get):
    corner = add_low(keep[1, 1], get[1, 1])
    return (swap_x(corner[:2]), swap_y(corner[2:]))


def side_payloads(keep, get, corners):
    by_x, by_y = corners
    pad = ((0, 0),) * 3
    for_x = add_low(keep[0, 1], get[0, 1], jnp.pad(by_y, ((2, 0),) + pad))
    for_y = add_low(keep[1, 0], get[1, 0], jnp.pad(by_x, ((0, 2),) + pad))
    return (for_x, for_y)


def reduce_sides(payloads):
    return (swap_x(payloads[0]), swap_y(payloads[1]))


def z_pair(values, half):
    return add_low(*(lax.dynamic_slice_in_dim(value, 2 * half, 2, 0) for value in values))


def far_payload(keep, get, sides, place):
    return z_pair((keep[0, 0], get[0, 0]) + tuple(sides), 1 - place[2] // 2)


def own_pair(keep, get, sides, far, place):
    half = place[2] // 2
    pair = (
        lax.dynamic_slice_in_dim(value, 2 * half, 2, 0)
        for value in (keep[0, 0], get[0, 0]) + tuple(sides)
    )
    return add_low(*pair, far)


def pick(pair, index):
    return lax.dynamic_index_in_dim(pair, index, 0, keepdims=False)


def reduce_near(pair, place):
    return swap_z(pick(pair, 1 - place[2] % 2), 1)


def reduce_total(pair, near, place):
    return add_low(pick(pair, place[2] % 2), near)


def reduce_direct(column, place):
    return tuple(swap_z(pick(column, place[2] ^ apart), apart) for apart in (1, 2, 3))


def share_core(pair, place):
    x, c = place[0], place[1]
    other = swap_core(pair)
    cores = jnp.where(c == 0, jnp.stack([pair, other], 1), jnp.stack([other, pair], 1))
    sides = jnp.where(x == 0, cores, cores[::-1])
    return sides.reshape((4,) + pair.shape[1:])


def small_parts(vectors):
    values = vectors.astype(jnp.float32)
    return (
        values[: 8 * D].reshape(8, D),
        values[8 * D : 8 * D + FF].reshape(1, FF),
        bias_vectors(values[8 * D + FF :].reshape(H, NB)),
    )


def per_device_fast(
    content,
    query,
    lengths,
    predicted,
    content_cot,
    query_cot,
    attn_master,
    attn_first,
    attn_second,
    inner_master,
    inner_first,
    inner_second,
    outer_master,
    outer_first,
    outer_second,
    small_master,
    small_first,
    small_second,
):
    place_parts = my_place()
    place = jnp.stack(place_parts).astype(jnp.int32)
    own_a0, plane_a0, own_f0 = cast_first(place, attn_master, inner_master, outer_master)
    z_a0 = tuple(swap_z(own_a0, apart) for apart in (1, 2, 3))
    plane_a0 = swap_y(plane_a0)
    near_f0 = swap_z(own_f0, 1)
    attn_low0, attn_low1, inner_low0, inner_low1, outer_low0, outer_low1, plane_f0, own_1, oth_1 = (
        cast_rest(place, attn_master, inner_master, outer_master)
    )
    low0 = jnp.concatenate([content, query])
    row_flags = predicted.reshape(1, LEN).astype(jnp.float32)
    col_flags = predicted.reshape(LEN, 1).astype(jnp.float32)
    small_low = small_master.astype(jnp.bfloat16)
    small_y = swap_y(small_low)
    z_a0, plane_a0, near_f0, plane_f0, own_1, oth_1, low0, row_flags, col_flags, small_y = join(
        z_a0, plane_a0, near_f0, plane_f0, own_1, oth_1, low0, row_flags, col_flags, small_y
    )
    col_a0, to_far_f0 = pack(
        ([(0, 0, 1), (1, 0, 1), (2, 0, 1)], [(3, 0, 2), (4, 0, 2)]), (*z_a0, own_f0, near_f0)
    )
    x0 = swap_x(col_a0)
    y0 = swap_y(col_a0)
    far_f0 = swap_z(to_far_f0, 2)
    plane_f0 = swap_y(after(plane_f0, col_a0))
    near_1 = swap_z(after(own_1, col_a0), 1)
    odd = place_parts[3] == 1
    small_pair = jnp.stack(
        [jnp.where(odd, small_y, small_low), jnp.where(odd, small_low, small_y)]
    )
    small_near = swap_z(small_pair, 1)
    x0, y0, far_f0, plane_f0, near_1, small_near = join(
        x0, y0, far_f0, plane_f0, near_1, small_near
    )
    to_x1, to_y1, to_far_a1 = pack(
        (
            [(0, 0, 2), (1, 0, 4), (2, 0, 2)],
            [(0, 0, 2), (1, 0, 4), (3, 2, 1)],
            [(4, 0, 1), (5, 0, 1)],
        ),
        (near_f0, far_f0, y0, x0, own_1, near_1),
    )
    x1 = swap_x(to_x1)
    y1 = swap_y(to_y1)
    far_a1 = swap_z(to_far_a1, 2)
    (mine_0,) = pack(
        (
            [(0, 0, 2), (1, 0, 3), (2, 0, 3), (3, 0, 3), (4, 0, 4), (5, 0, 2), (6, 0, 4)],
        ),
        after((plane_a0, col_a0, x0, y0, plane_f0, near_f0, far_f0), far_a1),
    )
    theirs_0 = swap_core(mine_0)
    small_four = jnp.stack([small_pair, small_near])
    small_far = swap_z(small_four, 2)
    small_all = gather_small(jnp.concatenate([small_four, small_far]), place_parts)
    x1, y1, far_a1, theirs_0, small_all = join(x1, y1, far_a1, theirs_0, small_all)
    to_x2, to_y2, to_far_f1, col_a1 = pack(
        (
            [(0, 0, 1), (1, 0, 2), (2, 0, 4)],
            [(0, 0, 1), (1, 0, 2), (3, 4, 2), (4, 0, 1), (5, 0, 1)],
            [(4, 1, 2), (0, 1, 2)],
            [(0, 0, 1), (1, 0, 2)],
        ),
        (near_1, far_a1, y1, x1, own_1, oth_1),
    )
    x2 = swap_x(to_x2)
    y2 = swap_y(to_y2)
    far_f1 = swap_z(to_far_f1, 2)
    their_x1, their_y1 = swap_core(x1), swap_core(y1)
    group_a0 = gather_group(
        1, (attn_low0,), (0, 0), (0, 2), ((0, 5), (0, 8)), ((1, 6, 2), (2, 6, 1)),
        (mine_0, x1, y1), (theirs_0, their_x1, their_y1),
    )
    small0, hidden_bias0, (tvec0, far0, onehot) = small_parts(small_all[0])
    small1, hidden_bias1, (tvec1, far1, onehot) = small_parts(small_all[1])
    q0, k0, v0, attn0 = project(place, low0, small0, group_a0)
    mixed0, p0, inverse0, dead = mix(lengths, far0, tvec0, q0, k0, v0, row_flags, col_flags)
    x2, y2, far_f1, mixed0 = join(x2, y2, far_f1, mixed0)
    to_x3, to_y3, col_f1 = pack(
        (
            [(0, 1, 2), (1, 0, 4), (2, 0, 3)],
            [(0, 1, 2), (1, 0, 4), (3, 1, 2), (4, 1, 2)],
            [(0, 1, 2), (1, 0, 4)],
        ),
        (near_1, far_f1, y2, own_1, oth_1),
    )
    x3 = swap_x(to_x3)
    y3 = swap_y(to_y3)
    their_x2, their_y2, their_a1 = swap_core(x2), swap_core(y2), swap_core(after(col_a1, x2))
    group_f0 = gather_group(
        2, (inner_low0, outer_low0), (0, 11), (0, 15), ((1, 0), (2, 0)), ((3, 3, 4), (4, 3, 2)),
        (mine_0, x1, y1, x2, y2), (theirs_0, their_x1, their_y1, their_x2, their_y2),
    )
    resid0, pre0, normed0, low1, summed0 = feed(
        place, small0, hidden_bias0, mixed0, low0, attn0, group_f0
    )
    x3, y3, low1 = join(x3, y3, low1)
    to_x4, to_y4 = pack(([(0, 0, 3)], [(1, 3, 3)]), (y3, x3))
    x4 = swap_x(to_x4)
    y4 = swap_y(to_y4)
    their_x3, their_y3 = swap_core(x3), swap_core(y3)
    group_a1 = gather_group(
        1, (attn_low1,), (1, 5), (2, 0), ((0, 0), (1, 0)), ((3, 6, 3),),
        (x2, y2, col_a1, x3), (their_x2, their_y2, their_a1, their_x3),
    )
    q1, k1, v1, attn1 = project(place, low1, small1, group_a1)
    x4, y4, q1 = join(x4, y4, q1)
    their_x4, their_y4, their_f1 = swap_core(x4), swap_core(y4), swap_core(after(col_f1, q1))
    group_f1 = gather_group(
        2, (inner_low1, outer_low1), (1, 6), (4, 0), ((0, 0), (1, 0)), ((2, 0, 3), (3, 0, 3)),
        (x3, y3, x4, y4, col_f1), (their_x3, their_y3, their_x4, their_y4, their_f1),
    )
    mixed1, p1, inverse1, dead = mix(
        lengths, far1, tvec1, q1, k1, v1, row_flags, col_flags
    )
    content_out, query_out, dresid1, dmix1, dwo1, keep_f1, send_f1, vec_f1, dhidden1 = turn(
        place, lengths, small1, small0, hidden_bias1, mixed1, summed0, attn1,
        (content_cot, query_cot), group_f1
    )
    get_f1 = swap_core(send_f1)
    *first1, table1_a = mix_back(0, q1, k1, v1, dmix1, mixed1, p1, inverse1, dead)
    by_f1 = reduce_corners(keep_f1, after(get_f1, table1_a))
    dq1, dk1, dv1, table1_b = mix_back(
        3, after(q1, get_f1, table1_a), k1, v1, dmix1, mixed1, p1, inverse1, dead, tuple(first1)
    )
    sides_rf1 = reduce_sides(side_payloads(keep_f1, get_f1, after(by_f1, table1_b)))
    keep_a1, send_a1, vec_a1 = weight_back(place, after(low1, by_f1), dq1, dk1, dv1, dwo1)
    get_a1 = swap_core(send_a1)
    by_a1 = reduce_corners(keep_a1, get_a1)
    dresid0, dmix0, dwo0, keep_f0, send_f0, vec_f0, dhidden0 = down(
        place, small0, dq1, dk1, dv1, after(attn1, get_a1), dresid1, summed0, normed0, resid0,
        pre0, mixed0, attn0, group_f0
    )
    get_f0 = swap_core(after(send_f0, sides_rf1, by_a1))
    sides_ra1 = reduce_sides(side_payloads(keep_a1, get_a1, after(by_a1, dmix0)))
    sides_rf1 = after(sides_rf1, dmix0)
    zfar_f1 = swap_z(far_payload(keep_f1, get_f1, sides_rf1, place_parts), 2)
    *first0, table0_a = mix_back(
        0, after(q0, by_a1, sides_rf1), k0, v0, dmix0, mixed0, p0, inverse0, dead
    )
    by_f0 = reduce_corners(keep_f0, after(get_f0, table0_a))
    dq0, dk0, dv0, table0_b = mix_back(
        3, after(q0, get_f0, table0_a), k0, v0, dmix0, mixed0, p0, inverse0, dead, tuple(first0)
    )
    by_f0, sides_ra1, zfar_f1, table0_b = join(by_f0, sides_ra1, zfar_f1, table0_b)
    payloads_f0 = side_payloads(keep_f0, get_f0, by_f0)
    sides_rf0 = reduce_sides(payloads_f0)
    keep_a0, send_a0, vec_a0 = weight_back(
        place, after(low0, payloads_f0, table0_b), dq0, dk0, dv0, dwo0
    )
    get_a0 = swap_core(send_a0)
    zfar_a1 = swap_z(far_payload(keep_a1, get_a1, sides_ra1, place_parts), 2)
    small_sum = jnp.concatenate(
        [
            jnp.stack([vec_a0, vec_a1]).reshape(LAYERS, -1),
            jnp.stack([vec_f0, vec_f1]).reshape(LAYERS, -1),
            jnp.stack([dhidden0, dhidden1]).reshape(LAYERS, -1),
            table_grad(
                jnp.concatenate([table0_a, table0_b, table1_a, table1_b]), onehot
            ).reshape(LAYERS, -1),
        ],
        axis=1,
    )
    pair_f1 = own_pair(keep_f1, get_f1, sides_rf1, after(zfar_f1, get_a0), place_parts)
    znear_f1 = reduce_near(pair_f1, place_parts)
    sides_rf0, get_a0, zfar_a1, znear_f1, small_sum = join(
        sides_rf0, get_a0, zfar_a1, znear_f1, small_sum
    )
    payload_f0 = far_payload(keep_f0, get_f0, sides_rf0, place_parts)
    zfar_f0 = swap_z(payload_f0, 2)
    by_a0 = reduce_corners(keep_a0, after(get_a0, payload_f0))
    pair_a1 = own_pair(keep_a1, get_a1, sides_ra1, zfar_a1, place_parts)
    znear_a1 = reduce_near(after(pair_a1, payload_f0), place_parts)
    content_grad, query_grad = input_back(after(dq0, sides_rf0), dk0, dv0, attn0, dresid0)
    small_c = swap_core(after(small_sum, payload_f0))
    by_a0, content_grad, znear_a1, small_c = join(by_a0, content_grad, znear_a1, small_c)
    payloads_a0 = side_payloads(keep_a0, get_a0, by_a0)
    sides_ra0 = reduce_sides(payloads_a0)
    own_1 = jnp.concatenate(
        [
            reduce_total(pair_f1, znear_f1, place_parts),
            reduce_total(pair_a1, znear_a1, place_parts),
        ]
    )
    across_1 = swap_x(after(own_1, payloads_a0))
    small_sum = after(small_sum, payloads_a0) + small_c
    small_y = swap_y(small_sum)
    sides_ra0, zfar_f0, small_y = join(sides_ra0, zfar_f0, small_y)
    column_a0 = add_low(keep_a0[0, 0], get_a0[0, 0], *sides_ra0)
    shifts_a0 = reduce_direct(column_a0, place_parts)
    pair_f0 = own_pair(keep_f0, get_f0, sides_rf0, zfar_f0, place_parts)
    znear_f0 = reduce_near(after(pair_f0, column_a0), place_parts)
    small_sum = after(small_sum, column_a0) + small_y
    small_z = swap_z(small_sum, 1)
    shifts_a0, znear_f0, across_1, small_z = join(shifts_a0, znear_f0, across_1, small_z)
    own_0 = jnp.concatenate(
        [
            reduce_total(pair_f0, znear_f0, place_parts),
            add_low(pick(column_a0, place_parts[2]), *shifts_a0),
        ]
    )
    across_0 = swap_x(own_0)
    four_1 = share_core(jnp.stack([own_1, after(across_1, own_0)]), place_parts)
    state = (
        attn_master, attn_first, attn_second, inner_master, inner_first, inner_second,
        outer_master, outer_first, outer_second,
    )
    new_1 = adam(1, state, four_1, ())
    small_sum = after(small_sum, own_0) + small_z
    small_z = swap_z(small_sum, 2)
    across_0, new_1, small_z = join(across_0, new_1, small_z)
    four_0 = share_core(jnp.stack([own_0, across_0]), place_parts)
    small_sum = small_sum + small_z
    small_x = swap_x(small_sum)
    new_0 = adam(0, state, four_0, tuple(new_1))
    small_sum = small_sum + small_x
    size = small_master.shape[1]
    small_own = lax.dynamic_slice_in_dim(small_sum, lax.axis_index("fsdp") * size, size, 1)
    small_new = adam_update(small_master, small_first, small_second, small_own, SMALL_RATE)
    return (
        (content_out, query_out, content_grad, query_grad)
        + tuple(new_0)
        + small_new
    )


def solution(mesh):
    placed = (
        P(("dp", "fsdp"), None),
        P(("dp", "fsdp"), None),
        P(("dp", "fsdp")),
        P(("dp", "fsdp")),
        P(("dp", "fsdp"), None),
        P(("dp", "fsdp"), None),
        P(None, None, "fsdp", None),
        P(None, None, "fsdp", None),
        P(None, None, "fsdp", None),
        P(None, "fsdp", None),
        P(None, "fsdp", None),
        P(None, "fsdp", None),
        P(None, "fsdp", None),
        P(None, "fsdp", None),
        P(None, "fsdp", None),
        P(None, "fsdp"),
        P(None, "fsdp"),
        P(None, "fsdp"),
    )
    fast = tuple(mesh.shape.values()) == (4, 8)
    return jax.shard_map(
        per_device_fast if fast else per_device,
        mesh=mesh,
        in_specs=placed,
        out_specs=(
            P(("dp", "fsdp"), None),
            P(("dp", "fsdp"), None),
            P(("dp", "fsdp"), None),
            P(("dp", "fsdp"), None),
            P(None, None, "fsdp", None),
            P(None, None, "fsdp", None),
            P(None, None, "fsdp", None),
            P(None, "fsdp", None),
            P(None, "fsdp", None),
            P(None, "fsdp", None),
            P(None, "fsdp", None),
            P(None, "fsdp", None),
            P(None, "fsdp", None),
            P(None, "fsdp"),
            P(None, "fsdp"),
            P(None, "fsdp"),
        ),
        check_vma=False,
    )
```

```python
from functools import partial

import jax
import jax.numpy as jnp
from jax import lax
from jax.experimental import pallas as pl
from jax.experimental.pallas import tpu as pltpu
from jax.sharding import PartitionSpec as P

D = 768
H = 12
DH = 64
FF = 3072
LEN = 512
NB = 32
LAYERS = 2
STEP = 10


NORM_EPS = 1e-05
MASKED = -1000000000.0
BETA_ONE = 0.9
BETA_TWO = 0.999
ATTENTION_RATE = 0.1
FEED_RATE = 0.02
SMALL_RATE = 0.4
WEIGHT_DECAY = 0.01
ADAM_EPS = 1e-08
SCORE_SCALE = 0.125


def layer_norm(values, gain, shift):
    centre = values - jnp.mean(values, axis=-1, keepdims=True)
    spread = jnp.mean(centre * centre, axis=-1, keepdims=True)
    return centre * lax.rsqrt(spread + NORM_EPS) * gain + shift


def unpack(vectors):
    pieces = [vectors[piece_index * D : (piece_index + 1) * D] for piece_index in range(8)]
    hidden_bias = vectors[8 * D : 8 * D + FF]
    bias_table = vectors[8 * D + FF :].reshape(H, NB)
    return (pieces, hidden_bias, bias_table)


def bucket_ids():
    position = jnp.arange(LEN, dtype=jnp.int32)
    offset = position[None, :] - position[:, None]
    distance = jnp.abs(offset)
    far_bucket = jnp.full(distance.shape, 8, jnp.int32)
    for exponent in range(1, 8):
        far_bucket = far_bucket + (distance * distance >= 64 * 2**exponent).astype(jnp.int32)
    near_or_far = jnp.where(distance < 8, distance, far_bucket)
    return near_or_far + NB // 2 * (offset > 0).astype(jnp.int32)


def bucket_onehot():
    return (bucket_ids()[:, :, None] == jnp.arange(NB, dtype=jnp.int32)[None, None, :]).astype(
        jnp.bfloat16
    )


def allowed_pairs(length, pred_flags):
    position = jnp.arange(LEN, dtype=jnp.int32)
    valid_key = (position < length)[None, :]
    row_pos = position[:, None]
    col_pos = position[None, :]
    free_key = (pred_flags == 0)[None, :]
    content_ok = valid_key & (free_key | (pred_flags[:, None] == 1) & (col_pos <= row_pos))
    query_ok = valid_key & (col_pos != row_pos) & (free_key | (col_pos < row_pos))
    return (content_ok, query_ok)


def masked_scores(query_rows, key_rows, position_bias, allowed):
    scores = (
        jnp.einsum("qhd,khd->hqk", query_rows, key_rows, preferred_element_type=jnp.float32)
        * SCORE_SCALE
        + position_bias
    )
    return jnp.where(allowed[None], scores, MASKED)


def table_bias(onehot, table_low):
    return jnp.einsum("qkb,hb->hqk", onehot, table_low, preferred_element_type=jnp.float32)


def attend_slot(onehot, table_low, slot_item):
    query_c, query_q, key_rows, value_rows, length, pred_flags = slot_item
    position_bias = table_bias(onehot, table_low)
    content_ok, query_ok = allowed_pairs(length, pred_flags)
    results = []
    for query_rows, allowed in ((query_c, content_ok), (query_q, query_ok)):
        scores = masked_scores(query_rows, key_rows, position_bias, allowed)
        peak = jnp.max(scores, axis=-1, keepdims=True)
        expos = jnp.exp(scores - peak)
        totals = jnp.sum(expos, axis=-1, keepdims=True)
        probs = (expos / totals).astype(jnp.bfloat16)
        mixed = jnp.einsum(
            "hqk,khd->qhd", probs, value_rows, preferred_element_type=jnp.float32
        ).astype(jnp.bfloat16)
        results.append((mixed, peak[..., 0] + jnp.log(totals[..., 0])))
    return (results[0][0], results[1][0], results[0][1], results[1][1])


def attend_back(onehot, table_low, slot_item):
    (
        query_c,
        query_q,
        key_rows,
        value_rows,
        length,
        pred_flags,
        lse_c,
        lse_q,
        grad_mix_c,
        grad_mix_q,
    ) = slot_item
    position_bias = table_bias(onehot, table_low)
    content_ok, query_ok = allowed_pairs(length, pred_flags)
    grad_keys = jnp.zeros(key_rows.shape, jnp.float32)
    grad_values = jnp.zeros(value_rows.shape, jnp.float32)
    grad_table = jnp.zeros((H, NB), jnp.float32)
    grads_query = []
    for query_rows, allowed, log_total, grad_mix in (
        (query_c, content_ok, lse_c, grad_mix_c),
        (query_q, query_ok, lse_q, grad_mix_q),
    ):
        scores = masked_scores(query_rows, key_rows, position_bias, allowed)
        probs = jnp.exp(scores - log_total[..., None])
        grad_values = grad_values + jnp.einsum(
            "hqk,qhd->khd", probs.astype(jnp.bfloat16), grad_mix, preferred_element_type=jnp.float32
        )
        grad_probs = jnp.einsum(
            "qhd,khd->hqk", grad_mix, value_rows, preferred_element_type=jnp.float32
        )
        grad_scores = probs * (grad_probs - jnp.sum(probs * grad_probs, axis=-1, keepdims=True))
        grad_scores = jnp.where(allowed[None], grad_scores, 0.0).astype(jnp.bfloat16)
        grad_table = grad_table + jnp.einsum(
            "hqk,qkb->hb", grad_scores, onehot, preferred_element_type=jnp.float32
        )
        grads_query.append(
            jnp.einsum("hqk,khd->qhd", grad_scores, key_rows, preferred_element_type=jnp.float32)
            * SCORE_SCALE
        )
        grad_keys = (
            grad_keys
            + jnp.einsum(
                "hqk,qhd->khd", grad_scores, query_rows, preferred_element_type=jnp.float32
            )
            * SCORE_SCALE
        )
    return (grads_query[0], grads_query[1], grad_keys, grad_values, grad_table)


def to_heads(values):
    return values.reshape(-1, LEN, H, DH)


AXES = ("dp", "fsdp")
GRID = (2, 2, 4, 2)
ROWS = 96


def places():
    return [
        (x, c, z, y) for x in range(2) for c in range(2) for z in range(4) for y in range(2)
    ]


def flat(x, c, z, y):
    return ((x * 2 + c) * 4 + z) * 2 + y


def move(value, shift):
    pairs = [(flat(*place), flat(*shift(*place))) for place in places()]
    return lax.ppermute(value, AXES, pairs)


def swap_core(value):
    return move(value, lambda x, c, z, y: (x, 1 - c, z, y))


def swap_x(value):
    return move(value, lambda x, c, z, y: (1 - x, c, z, y))


def swap_y(value):
    return move(value, lambda x, c, z, y: (x, c, z, 1 - y))


def swap_z(value, apart):
    return move(value, lambda x, c, z, y: (x, c, z ^ apart, y))


def my_place():
    dp = lax.axis_index("dp")
    fsdp = lax.axis_index("fsdp")
    return (dp // 2, dp % 2, fsdp // 2, fsdp % 2)


def dot_nn(left, right):
    return jnp.dot(left, right, preferred_element_type=jnp.float32)


def dot_nt(left, right):
    return lax.dot_general(
        left, right, (((1,), (1,)), ((), ())), preferred_element_type=jnp.float32
    )


def dot_tn(left, right):
    return lax.dot_general(
        left, right, (((0,), (0,)), ((), ())), preferred_element_type=jnp.float32
    )


ANY_SPEC = pl.BlockSpec(memory_space=pl.ANY)
VMEM_SPEC = pl.BlockSpec(memory_space=pltpu.VMEM)
SMEM_SPEC = pl.BlockSpec(memory_space=pltpu.SMEM)
TALL = 2 * LEN
HALF = 256
PARAMS = pltpu.CompilerParams(vmem_limit_bytes=60 * 1024 * 1024)


def norm_parts(values):
    centre = values - jnp.mean(values, axis=-1, keepdims=True)
    spread = jnp.mean(centre * centre, axis=-1, keepdims=True)
    scale = lax.rsqrt(spread + NORM_EPS)
    return (centre * scale, scale)


def norm_back(unit, scale, grad, gain):
    scaled = grad * gain
    return scale * (
        scaled
        - jnp.mean(scaled, axis=-1, keepdims=True)
        - unit * jnp.mean(scaled * unit, axis=-1, keepdims=True)
    )


def start_fetch(kinds, plan, place_ref, refs, targets, sems):
    x, c, z, y = (place_ref[index] for index in range(4))
    mine = z * 2 + y
    copies = []

    def start(source, target):
        copy = pltpu.make_async_copy(source, target, sems.at[len(copies)])
        copy.start()
        copies.append(copy)

    for member, kind in enumerate(kinds):
        target = targets[member]
        if kind == "attn":
            start(refs[member], target.at[:, pl.ds(pl.multiple_of(mine * ROWS, ROWS), ROWS), :])
        elif kind == "inner":
            for quarter in range(4):
                start(
                    refs[member].at[:, quarter * D : quarter * D + D],
                    target.at[quarter, pl.ds(pl.multiple_of(mine * ROWS, ROWS), ROWS), :],
                )
        else:
            start(refs[member], target.at[z, pl.ds(pl.multiple_of(y * 384, ROWS), 384), :])
    for array, index, dx, dy, dc, dz, member in plan:
        quarter = (x ^ dx) * 2 + (c ^ dc)
        if kinds[member] == "outer":
            lead, row = z ^ dz, (y ^ dy) * 384 + quarter * ROWS
        else:
            lead, row = quarter, ((z ^ dz) * 2 + (y ^ dy)) * ROWS
        start(
            refs[len(kinds) + array].at[index],
            targets[member].at[lead, pl.ds(pl.multiple_of(row, ROWS), ROWS), :],
        )
    return copies


def pack_kernel(outputs, count, *refs):
    sources, targets, sems = refs[:count], refs[count:-1], refs[-1]
    pairs = []
    for target, parts in zip(targets, outputs):
        at = 0
        for source, first, held in parts:
            pairs.append((sources[source].at[first : first + held], target.at[at : at + held]))
            at += held
    finish(issue(pairs, sems))


def pack(outputs, sources):
    total = sum(len(parts) for parts in outputs)
    counts = [sum(held for unused, unused_first, held in parts) for parts in outputs]
    return pl.pallas_call(
        partial(pack_kernel, outputs, len(sources)),
        out_shape=[jax.ShapeDtypeStruct((count, ROWS, D), jnp.bfloat16) for count in counts],
        in_specs=[ANY_SPEC] * len(sources),
        out_specs=[VMEM_SPEC] * len(outputs),
        scratch_shapes=[pltpu.SemaphoreType.DMA((total,))],
        compiler_params=pltpu.CompilerParams(vmem_limit_bytes=16 * 1024 * 1024),
        cost_estimate=pl.CostEstimate(flops=0, bytes_accessed=300000 * sum(counts), transcendentals=0),
        name="pack",
    )(*sources)


def quarter_spans(place_ref, side):
    quarter = (place_ref[0] ^ side) * 2 + place_ref[1]
    return (
        quarter,
        pl.ds(pl.multiple_of(quarter * D, D), D),
        pl.ds(pl.multiple_of(quarter * ROWS, ROWS), ROWS),
    )


def cast_first_kernel(
    place_ref, attn_any, inner_any, outer_any, own_a0, plane_a0, own_f0, hold_ref, sems
):
    index, cols, rows = quarter_spans(place_ref, 0)
    other = quarter_spans(place_ref, 1)[0]
    finish(
        issue(
            (
                (attn_any.at[0, index], hold_ref.at[0]),
                (attn_any.at[0, other], hold_ref.at[1]),
                (inner_any.at[0, :, cols], hold_ref.at[2]),
                (outer_any.at[0, rows, :], hold_ref.at[3]),
            ),
            sems,
        )
    )
    own_a0[...] = hold_ref[0:1].astype(jnp.bfloat16)
    plane_a0[...] = hold_ref[0:2].astype(jnp.bfloat16)
    own_f0[...] = hold_ref[2:4].astype(jnp.bfloat16)


def cast_first(place, attn, inner, outer):
    return pl.pallas_call(
        cast_first_kernel,
        out_shape=[jax.ShapeDtypeStruct((count, ROWS, D), jnp.bfloat16) for count in (1, 2, 2)],
        in_specs=[SMEM_SPEC] + [ANY_SPEC] * 3,
        out_specs=[VMEM_SPEC] * 3,
        scratch_shapes=[pltpu.VMEM((4, ROWS, D), jnp.float32), pltpu.SemaphoreType.DMA((4,))],
        compiler_params=PARAMS,
        cost_estimate=pl.CostEstimate(flops=1000000, bytes_accessed=2000000, transcendentals=0),
        name="cast_first",
    )(place, attn, inner, outer)


def cast_rest_kernel(
    place_ref, attn_ref, inner_ref, outer_ref, attn_0, attn_1, inner_0, inner_1, outer_0, outer_1,
    plane_f0, own_1, oth_1,
):
    for layer, (attn_low, inner_low, outer_low) in enumerate(
        ((attn_0, inner_0, outer_0), (attn_1, inner_1, outer_1))
    ):
        attn_low[...] = attn_ref[layer].astype(jnp.bfloat16)
        inner_low[...] = inner_ref[layer].astype(jnp.bfloat16)
        outer_low[...] = outer_ref[layer].astype(jnp.bfloat16)
    for side, (target, first) in enumerate(((own_1, 0), (oth_1, 0))):
        index, cols, rows = quarter_spans(place_ref, side)
        plane_f0[2 * side] = inner_ref[0, :, cols].astype(jnp.bfloat16)
        plane_f0[2 * side + 1] = outer_ref[0, rows, :].astype(jnp.bfloat16)
        target[0] = attn_ref[1, index].astype(jnp.bfloat16)
        target[1] = inner_ref[1, :, cols].astype(jnp.bfloat16)
        target[2] = outer_ref[1, rows, :].astype(jnp.bfloat16)


def cast_rest(place, attn, inner, outer):
    low = [
        jax.ShapeDtypeStruct(array.shape[1:], jnp.bfloat16)
        for array in (attn, attn, inner, inner, outer, outer)
    ]
    return pl.pallas_call(
        cast_rest_kernel,
        out_shape=low
        + [jax.ShapeDtypeStruct((count, ROWS, D), jnp.bfloat16) for count in (4, 3, 3)],
        in_specs=[SMEM_SPEC] + [VMEM_SPEC] * 3,
        out_specs=[VMEM_SPEC] * 9,
        compiler_params=PARAMS,
        cost_estimate=pl.CostEstimate(flops=10000000, bytes_accessed=12000000, transcendentals=0),
        name="cast_rest",
    )(place, attn, inner, outer)


def project_kernel(plan, place_ref, small_ref, low_any, *refs):
    pieces = refs[:-14]
    (
        q_out, k_out, v_out, w_out, low_ref, q_ref, k_ref, v_ref, w_ref,
        sems, load_sem, keep_sem, store_sems, unused,
    ) = refs[-14:]
    load = pltpu.make_async_copy(low_any, low_ref, load_sem)
    load.start()
    fetches = start_fetch(("attn",), plan, place_ref, pieces, (w_ref,), sems)
    load.wait()
    for copy in fetches:
        copy.wait()
    keep = pltpu.make_async_copy(w_ref, w_out, keep_sem)
    keep.start()
    bias_q = small_ref[0:1, :]
    bias_v = small_ref[1:2, :]
    stores = []

    def store(source, target):
        copy = pltpu.make_async_copy(source, target, store_sems.at[len(stores)])
        copy.start()
        stores.append(copy)

    for row in range(0, TALL, HALF):
        span = slice(row, row + HALF)
        rows = low_ref[span, :]
        q_ref[span, :] = (dot_nn(rows, w_ref[0]) + bias_q).astype(jnp.bfloat16)
        if row < LEN:
            k_ref[span, :] = dot_nn(rows, w_ref[1]).astype(jnp.bfloat16)
            v_ref[span, :] = (dot_nn(rows, w_ref[2]) + bias_v).astype(jnp.bfloat16)
        if row == LEN - HALF:
            store(k_ref, k_out)
            store(v_ref, v_out)
            store(q_ref.at[:LEN, :], q_out.at[:LEN, :])
    store(q_ref.at[LEN:, :], q_out.at[LEN:, :])
    for copy in stores:
        copy.wait()
    keep.wait()


def project(place, low, small, group):
    plan, pieces = group
    return pl.pallas_call(
        partial(project_kernel, plan),
        out_shape=[
            jax.ShapeDtypeStruct((TALL, D), jnp.bfloat16),
            jax.ShapeDtypeStruct((LEN, D), jnp.bfloat16),
            jax.ShapeDtypeStruct((LEN, D), jnp.bfloat16),
            jax.ShapeDtypeStruct((4, D, D), jnp.bfloat16),
        ],
        in_specs=[SMEM_SPEC, VMEM_SPEC, ANY_SPEC] + [ANY_SPEC] * len(pieces),
        out_specs=[ANY_SPEC] * 4,
        scratch_shapes=[
            pltpu.VMEM((TALL, D), jnp.bfloat16),
            pltpu.VMEM((TALL, D), jnp.bfloat16),
            pltpu.VMEM((LEN, D), jnp.bfloat16),
            pltpu.VMEM((LEN, D), jnp.bfloat16),
            pltpu.VMEM((4, D, D), jnp.bfloat16),
            pltpu.SemaphoreType.DMA((32,)),
            pltpu.SemaphoreType.DMA,
            pltpu.SemaphoreType.DMA,
            pltpu.SemaphoreType.DMA((4,)),
            pltpu.SemaphoreType.DMA,
        ],
        compiler_params=PARAMS,
        cost_estimate=pl.CostEstimate(flops=2 * 2048 * D * D, bytes_accessed=16000000, transcendentals=0),
        name="project",
    )(place, small, low, *pieces)


def build_masks(length, row_flags, col_flags, mask_ref, alive_ref):
    flags = row_flags[...]

    def body(step, carry):
        start = pl.multiple_of(step * 64, 64)
        key = lax.broadcasted_iota(jnp.int32, (64, LEN), 0) + start
        query = lax.broadcasted_iota(jnp.int32, (64, LEN), 1)
        valid = key < length
        free = jnp.broadcast_to(col_flags[pl.ds(start, 64), :], (64, LEN)) == 0.0
        marked = jnp.broadcast_to(flags, (64, LEN)) == 1.0
        content_ok = valid & (free | (marked & (key <= query)))
        query_ok = valid & (key != query) & (free | (key < query))
        mask_ref[pl.ds(start, 64), :LEN] = content_ok.astype(jnp.float32)
        mask_ref[pl.ds(start, 64), LEN:] = query_ok.astype(jnp.float32)
        return carry

    lax.fori_loop(0, 8, body, 0)
    alive_ref[...] = jnp.max(mask_ref[...], axis=0, keepdims=True)


def build_tiles(t_row, tile_ref):
    spread = jnp.broadcast_to(t_row, (128, 512))
    rolled = pltpu.roll(spread, 0, 1, stride=1, stride_axis=0)
    tile_ref[...] = rolled[:, :384]


def position_bias(tile_ref, far_ref, head, query_block, key_block):
    apart = query_block - key_block
    if apart >= 2:
        return far_ref[head, 0]
    if apart <= -2:
        return far_ref[head, 1]
    return tile_ref[:, 128 * (apart + 1) : 128 * (apart + 2)]


def head_lanes(shape, head):
    lane = lax.broadcasted_iota(jnp.int32, shape, 1)
    return (lane >= 64) if head else (lane < 64)


def mix_kernel(
    length_ref, far_ref, q_ref, k_ref, v_ref, row_flags, col_flags, t_ref,
    a_ref, p_ref, inverse_ref, dead_ref, mask_ref, alive_ref, tile_ref, o_ref,
):
    pair = pl.program_id(0)

    @pl.when(pair == 0)
    def _():
        build_masks(length_ref[0], row_flags, col_flags, mask_ref, alive_ref)
        dead_ref[...] = (1.0 - alive_ref[...]) * (1.0 / LEN)

    keys = k_ref[...].astype(jnp.float32) * SCORE_SCALE
    values_t = v_ref[...].astype(jnp.float32).T.astype(jnp.bfloat16)
    keys_own = [
        jnp.where(head_lanes(keys.shape, head), keys, 0.0).astype(jnp.bfloat16) for head in range(2)
    ]
    for head in range(2):
        build_tiles(t_ref[head], tile_ref.at[head])
    work = [(head, chunk) for head in range(2) for chunk in range(4)]

    def score(head, chunk):
        return dot_nt(keys_own[head], q_ref[chunk * HALF : chunk * HALF + HALF, :])

    def mixture(head, chunk):
        span = slice(chunk * HALF, chunk * HALF + HALF)
        own = slice(8 + head * 64, 8 + head * 64 + 64)
        mixed = dot_nn(values_t[head * 64 : head * 64 + 64, :], p_ref[head, :, span])
        o_ref[own, span] = mixed * o_ref[head : head + 1, span]

    following = score(*work[0])
    for index, (head, chunk) in enumerate(work):
        scores = following
        if index + 1 < len(work):
            following = score(*work[index + 1])
        at = chunk * HALF
        for side in range(2):
            lanes = slice(at + side * 128, at + side * 128 + 128)
            blocks = []
            peak = None
            for key_block in range(4):
                rows = slice(key_block * 128, key_block * 128 + 128)
                block = scores[rows, side * 128 : side * 128 + 128] + position_bias(
                    tile_ref.at[head], far_ref, pair * 2 + head, (chunk % 2) * 2 + side, key_block
                )
                block = jnp.where(mask_ref[rows, lanes] > 0.0, block, MASKED)
                blocks.append(block)
                high = jnp.max(block, axis=0, keepdims=True)
                peak = high if peak is None else jnp.maximum(peak, high)
            total = None
            for key_block in range(4):
                rows = slice(key_block * 128, key_block * 128 + 128)
                expo = jnp.exp(blocks[key_block] - peak)
                part = jnp.sum(expo, axis=0, keepdims=True)
                total = part if total is None else total + part
                p_ref[head, rows, lanes] = expo.astype(jnp.bfloat16)
            inverse = 1.0 / total
            inverse_ref[head, :, lanes] = inverse * alive_ref[:, lanes]
            o_ref[head : head + 1, lanes] = inverse
        if index:
            mixture(*work[index - 1])
    mixture(*work[-1])
    a_ref[...] = o_ref[8:, :].T.astype(jnp.bfloat16)


def mix(length, far, tvec, q, k, v, row_flags, col_flags):
    tall = pl.BlockSpec((TALL, 128), lambda p: (0, p))
    short = pl.BlockSpec((LEN, 128), lambda p: (0, p))
    return pl.pallas_call(
        mix_kernel,
        grid=(H // 2,),
        out_shape=[
            jax.ShapeDtypeStruct((TALL, D), jnp.bfloat16),
            jax.ShapeDtypeStruct((H, LEN, TALL), jnp.bfloat16),
            jax.ShapeDtypeStruct((H, 1, TALL), jnp.float32),
            jax.ShapeDtypeStruct((1, TALL), jnp.float32),
        ],
        in_specs=[
            SMEM_SPEC, SMEM_SPEC, tall, short, short,
            pl.BlockSpec((1, LEN), lambda p: (0, 0)),
            pl.BlockSpec((LEN, 1), lambda p: (0, 0)),
            pl.BlockSpec((2, 1, 512), lambda p: (p, 0, 0)),
        ],
        out_specs=[
            tall,
            pl.BlockSpec((2, LEN, TALL), lambda p: (p, 0, 0)),
            pl.BlockSpec((2, 1, TALL), lambda p: (p, 0, 0)),
            pl.BlockSpec((1, TALL), lambda p: (0, 0)),
        ],
        scratch_shapes=[
            pltpu.VMEM((LEN, TALL), jnp.float32),
            pltpu.VMEM((1, TALL), jnp.float32),
            pltpu.VMEM((2, 128, 384), jnp.float32),
            pltpu.VMEM((136, TALL), jnp.float32),
        ],
        compiler_params=PARAMS,
        cost_estimate=pl.CostEstimate(flops=6500000000, bytes_accessed=8000000, transcendentals=6300000),
        name="mix",
    )(length, far, q, k, v, row_flags, col_flags, tvec)


def mix_back_kernel(q_ref, k_ref, v_ref, da_ref, a_ref, p_ref, inverse_ref, dead_ref, *refs):
    (
        dq_ref, dk_ref, dv_ref, table_ref, s_ref, near_ref, da_t, low_t, q_t, g_ref,
    ) = refs[-10:]
    keys = k_ref[...].astype(jnp.float32) * SCORE_SCALE
    keys_t = keys.T.astype(jnp.bfloat16)
    q_t[...] = q_ref[...].astype(jnp.float32).T.astype(jnp.bfloat16)
    da_t[...] = da_ref[...].astype(jnp.float32).T
    product = a_ref[...].astype(jnp.float32).T * da_t[...]
    values = v_ref[...].astype(jnp.float32)
    near_ref[...] = jnp.zeros(near_ref.shape, jnp.float32)
    turn = (
        lax.broadcasted_iota(jnp.int32, (128, 128), 0)
        + lax.broadcasted_iota(jnp.int32, (128, 128), 1)
        == 127
    ).astype(jnp.float32)
    deltas = []
    for head in range(2):
        rows = slice(head * 64, head * 64 + 64)
        inverse = inverse_ref[head]
        deltas.append(jnp.sum(product[rows, :], axis=0, keepdims=True) * inverse)
        low_t[rows, :] = (da_t[rows, :] * inverse).astype(jnp.bfloat16)
    for head in range(2):
        own = slice(head * 64, head * 64 + 64)
        values_own = jnp.where(head_lanes(values.shape, head), values, 0.0).astype(jnp.bfloat16)
        delta = deltas[head]
        far_low = jnp.zeros((8, 128), jnp.float32)
        far_high = jnp.zeros((8, 128), jnp.float32)
        for chunk in range(4):
            at = chunk * HALF
            pulls = dot_nn(values_own, low_t[:, at : at + HALF])
            for side in range(2):
                lanes = slice(at + side * 128, at + side * 128 + 128)
                shift = delta[:, lanes]
                query_block = (chunk % 2) * 2 + side
                for key_block in range(4):
                    rows = slice(key_block * 128, key_block * 128 + 128)
                    cols = slice(side * 128, side * 128 + 128)
                    grad = p_ref[head, rows, lanes].astype(jnp.float32) * (
                        pulls[rows, cols] - shift
                    )
                    s_ref[head, rows, lanes] = grad.astype(jnp.bfloat16)
                    apart = query_block - key_block
                    if apart >= 2:
                        far_low = far_low + jnp.sum(grad.reshape(16, 8, 128), axis=0)
                    elif apart <= -2:
                        far_high = far_high + jnp.sum(grad.reshape(16, 8, 128), axis=0)
                    else:
                        near_ref[head, :, 128 * (apart + 1) : 128 * (apart + 2)] += grad
        g_ref[own, :LEN] = dot_nt(low_t[own, :], p_ref[head])
        g_ref[own, LEN:] = dot_nt(q_t[own, :], s_ref[head]) * SCORE_SCALE
        da_t[own, :] = dot_nn(keys_t[own, :], s_ref[head])
        turned = jnp.dot(
            turn, near_ref[head], precision=lax.Precision.HIGHEST, preferred_element_type=jnp.float32
        )
        aligned = pltpu.roll(turned, 0, 1, stride=1, stride_axis=0)
        table_ref[head, :, :512] = jnp.sum(aligned, axis=0, keepdims=True)
        table_ref[head, :, 512:640] = jnp.sum(far_low, axis=0, keepdims=True)
        table_ref[head, :, 640:] = jnp.sum(far_high, axis=0, keepdims=True)
    uniform = dot_nn(dead_ref[...].astype(jnp.bfloat16), da_ref[...])
    dv_ref[...] = (g_ref[:, :LEN].T + uniform).astype(jnp.bfloat16)
    dk_ref[...] = g_ref[:, LEN:].T.astype(jnp.bfloat16)
    dq_ref[...] = da_t[...].T.astype(jnp.bfloat16)


def mix_back(first, q, k, v, da, a, p, inverse, dead, held=()):
    tall = pl.BlockSpec((TALL, 128), lambda i: (0, i + first))
    short = pl.BlockSpec((LEN, 128), lambda i: (0, i + first))
    return pl.pallas_call(
        mix_back_kernel,
        grid=(H // 4,),
        out_shape=[
            jax.ShapeDtypeStruct((TALL, D), jnp.bfloat16),
            jax.ShapeDtypeStruct((LEN, D), jnp.bfloat16),
            jax.ShapeDtypeStruct((LEN, D), jnp.bfloat16),
            jax.ShapeDtypeStruct((H // 2, 1, 768), jnp.float32),
        ],
        in_specs=[
            tall, short, short, tall, tall,
            pl.BlockSpec((2, LEN, TALL), lambda i: (i + first, 0, 0)),
            pl.BlockSpec((2, 1, TALL), lambda i: (i + first, 0, 0)),
            pl.BlockSpec((1, TALL), lambda i: (0, 0)),
        ]
        + [ANY_SPEC] * len(held),
        out_specs=[tall, short, short, pl.BlockSpec((2, 1, 768), lambda i: (i, 0, 0))],
        input_output_aliases={8 + index: index for index in range(len(held))},
        scratch_shapes=[
            pltpu.VMEM((2, LEN, TALL), jnp.bfloat16),
            pltpu.VMEM((2, 128, 512), jnp.float32),
            pltpu.VMEM((128, TALL), jnp.float32),
            pltpu.VMEM((128, TALL), jnp.bfloat16),
            pltpu.VMEM((128, TALL), jnp.bfloat16),
            pltpu.VMEM((128, TALL), jnp.float32),
        ],
        compiler_params=PARAMS,
        cost_estimate=pl.CostEstimate(flops=8000000000, bytes_accessed=16000000, transcendentals=0),
        name="mix_back",
    )(q, k, v, da, a, p, inverse, dead, *held)


GELU_SCALE = 0.7978845608028654
GELU_CUBE = 0.044715


def feed_rows(rows, small_ref, hidden_bias_ref, resid, normed_ref, pre_ref, inner_ref, outer_ref):
    unit, scale = norm_parts(resid)
    normed = unit * small_ref[3:4, :] + small_ref[4:5, :]
    low = normed.astype(jnp.bfloat16)
    normed_ref[rows, :] = low
    total = normed + small_ref[5:6, :]
    for chunk in range(4):
        pre = dot_nn(low, inner_ref[chunk]) + hidden_bias_ref[:, chunk * D : chunk * D + D]
        pre_ref[chunk, rows, :] = pre.astype(jnp.bfloat16)
        tanh = jnp.tanh(GELU_SCALE * (pre + GELU_CUBE * (pre * pre * pre)))
        active = (pre * (0.5 + 0.5 * tanh)).astype(jnp.bfloat16)
        total = total + dot_nn(active, outer_ref[chunk])
    return total


def norm_two_back(unit, scale, grad, small_ref, sums):
    back = norm_back(unit, scale, grad, small_ref[6:7, :])
    low = back.astype(jnp.bfloat16)
    parts = (low.astype(jnp.float32), grad * unit, grad)
    return back, low, [
        total + jnp.sum(part, axis=0, keepdims=True) for total, part in zip(sums, parts)
    ]


def issue(pairs, sems, first=0):
    copies = [
        pltpu.make_async_copy(source, target, sems.at[first + index])
        for index, (source, target) in enumerate(pairs)
    ]
    for copy in copies:
        copy.start()
    return copies


def finish(copies):
    for copy in copies:
        copy.wait()


def storer(sems):
    copies = []

    def store(source, target):
        copy = pltpu.make_async_copy(source, target, sems.at[len(copies)])
        copy.start()
        copies.append(copy)

    return store, copies


def feed_kernel(
    plan, place_ref, small_ref, hidden_bias_ref, mix_any, hidden_any, attn_any, *refs
):
    (
        resid_out, pre_out, normed_out, low_out, summed_out,
        mix_ref, hidden_ref, wo_ref, inner_ref, outer_ref, resid_ref, total_ref, normed_ref,
        pre_ref, low_ref, sems, load_sems, store_sems,
    ) = refs[-18:]
    finish(
        issue(
            ((mix_any, mix_ref), (attn_any.at[3], wo_ref), (hidden_any, hidden_ref)), load_sems
        )
    )
    fetches = start_fetch(
        ("inner", "outer"), plan, place_ref, refs[:-18], (inner_ref, outer_ref), sems
    )
    for row in range(0, TALL, HALF):
        rows = slice(row, row + HALF)
        resid_ref[rows, :] = (
            hidden_ref[rows, :].astype(jnp.float32)
            + dot_nn(mix_ref[rows, :], wo_ref[...])
            + small_ref[2:3, :]
        )
    finish(fetches)
    store, stores = storer(store_sems)
    store(resid_ref, resid_out)
    for row in range(0, TALL, HALF):
        rows = slice(row, row + HALF)
        total = feed_rows(
            rows, small_ref, hidden_bias_ref, resid_ref[rows, :], normed_ref, pre_ref, inner_ref,
            outer_ref,
        )
        total_ref[rows, :] = total
        store(pre_ref.at[:, rows, :], pre_out.at[:, rows, :])
        store(total_ref.at[rows, :], summed_out.at[rows, :])
        store(normed_ref.at[rows, :], normed_out.at[rows, :])
        unit, scale = norm_parts(total)
        following = unit * small_ref[6:7, :] + small_ref[7:8, :]
        low_ref[rows, :] = following.astype(jnp.bfloat16)
        store(low_ref.at[rows, :], low_out.at[rows, :])
    finish(stores)


def feed(place, small, hidden_bias, mixed, hidden, attn, group):
    plan, pieces = group
    tall = jax.ShapeDtypeStruct((TALL, D), jnp.float32)
    tall_low = jax.ShapeDtypeStruct((TALL, D), jnp.bfloat16)
    return pl.pallas_call(
        partial(feed_kernel, plan),
        out_shape=[
            tall, jax.ShapeDtypeStruct((4, TALL, D), jnp.bfloat16), tall_low, tall_low, tall
        ],
        in_specs=[SMEM_SPEC, VMEM_SPEC, VMEM_SPEC] + [ANY_SPEC] * (3 + len(pieces)),
        out_specs=[ANY_SPEC] * 5,
        scratch_shapes=[
            pltpu.VMEM((TALL, D), jnp.bfloat16),
            pltpu.VMEM((TALL, D), jnp.bfloat16),
            pltpu.VMEM((D, D), jnp.bfloat16),
            pltpu.VMEM((4, D, D), jnp.bfloat16),
            pltpu.VMEM((4, D, D), jnp.bfloat16),
            pltpu.VMEM((TALL, D), jnp.float32),
            pltpu.VMEM((TALL, D), jnp.float32),
            pltpu.VMEM((TALL, D), jnp.bfloat16),
            pltpu.VMEM((4, TALL, D), jnp.bfloat16),
            pltpu.VMEM((TALL, D), jnp.bfloat16),
            pltpu.SemaphoreType.DMA((64,)),
            pltpu.SemaphoreType.DMA((3,)),
            pltpu.SemaphoreType.DMA((17,)),
        ],
        compiler_params=PARAMS,
        cost_estimate=pl.CostEstimate(flops=2 * TALL * D * (D + 2 * FF), bytes_accessed=30000000, transcendentals=3000000),
        name="feed",
    )(place, small, hidden_bias, mixed, hidden, attn, *pieces)


def back_steps(
    place_ref, small_ref, before, store, outs, vec_ref, dhidden_ref, branch_ref, total_ref,
    normed_ref, resid_ref, pre_ref, mix_ref, wo_ref, inner_ref, outer_ref, active_ref, dpre_ref,
    dinner_ref, douter_ref, dwo_ref,
):
    dresid_out, dmix_out, dwo_out, keep_out, send_out = outs
    x, c, z, y = (place_ref[index] for index in range(4))
    order = [(1 - step // 2, step % 2) for step in range(4)]
    chunks = [side * 2 + (c ^ apart) for apart, side in order]
    sums = [jnp.zeros((1, D), jnp.float32)] * 3
    for step in range(4):
        apart, side = order[step]
        chunk = chunks[step]
        before(step)
        bias_grad = jnp.zeros((1, D), jnp.float32)
        for row in range(0, TALL, HALF):
            rows = slice(row, row + HALF)
            pull = dot_nt(branch_ref[rows, :], outer_ref[chunk])
            pre = pre_ref[chunk, rows, :].astype(jnp.float32)
            square = pre * pre
            tanh = jnp.tanh(GELU_SCALE * pre * (1.0 + GELU_CUBE * square))
            half = 0.5 + 0.5 * tanh
            active_ref[rows, :] = (pre * half).astype(jnp.bfloat16)
            slope = half + (0.5 * GELU_SCALE) * pre * (1.0 - tanh * tanh) * (
                1.0 + (3.0 * GELU_CUBE) * square
            )
            dpre = (pull * slope).astype(jnp.bfloat16)
            dpre_ref[rows, :] = dpre
            bias_grad += jnp.sum(dpre.astype(jnp.float32), axis=0, keepdims=True)
            grad = total_ref[rows, :] + dot_nt(dpre, inner_ref[chunk])
            if step < 3:
                total_ref[rows, :] = grad
            else:
                unit, scale = norm_parts(resid_ref[rows, :])
                back = norm_back(unit, scale, grad, small_ref[3:4, :])
                resid_ref[rows, :] = back
                low = back.astype(jnp.bfloat16)
                pre_ref[chunks[0], rows, :] = low
                pre_ref[chunks[1], rows, :] = dot_nt(low, wo_ref[...]).astype(jnp.bfloat16)
                parts = (low.astype(jnp.float32), grad * unit, grad)
                sums = [
                    value + jnp.sum(part, axis=0, keepdims=True)
                    for value, part in zip(sums, parts)
                ]
        dhidden_ref[chunk] = bias_grad
        if step == 3:
            store(resid_ref, dresid_out)
            store(pre_ref.at[chunks[1]], dmix_out)
        douter_ref[step] = (
            dot_tn(active_ref[...], branch_ref[...]).astype(jnp.bfloat16).reshape(2, 2, 2, ROWS, D)
        )
        for y_block in range(2):
            for x_block in range(2):
                spot = (y_block ^ y, x_block ^ x, chunk, 1)
                store(douter_ref.at[step, y_block, x_block, c], keep_out.at[spot])
                store(douter_ref.at[step, y_block, x_block, 1 - c], send_out.at[spot])
        dinner_ref[step] = (
            dot_tn(normed_ref[...], dpre_ref[...]).astype(jnp.bfloat16).reshape(4, 2, ROWS, D)
        )
        target = send_out if apart else keep_out
        for y_block in range(2):
            store(dinner_ref.at[step, :, y_block], target.at[y_block ^ y, side ^ x, :, 0])
    dwo_ref[...] = dot_tn(mix_ref[...], pre_ref[chunks[0]]).astype(jnp.bfloat16)
    store(dwo_ref, dwo_out)
    for index, value in enumerate(sums):
        vec_ref[index : index + 1, :] = value


BACK_SHAPES = [
    jax.ShapeDtypeStruct((TALL, D), jnp.float32),
    jax.ShapeDtypeStruct((TALL, D), jnp.bfloat16),
    jax.ShapeDtypeStruct((D, D), jnp.bfloat16),
    jax.ShapeDtypeStruct((2, 2, 4, 2, ROWS, D), jnp.bfloat16),
    jax.ShapeDtypeStruct((2, 2, 4, 2, ROWS, D), jnp.bfloat16),
    jax.ShapeDtypeStruct((6, D), jnp.float32),
    jax.ShapeDtypeStruct((4, 1, D), jnp.float32),
]
BACK_SCRATCH = [
    pltpu.VMEM((TALL, D), jnp.bfloat16),
    pltpu.VMEM((TALL, D), jnp.float32),
    pltpu.VMEM((TALL, D), jnp.bfloat16),
    pltpu.VMEM((TALL, D), jnp.float32),
    pltpu.VMEM((4, TALL, D), jnp.bfloat16),
    pltpu.VMEM((TALL, D), jnp.bfloat16),
    pltpu.VMEM((D, D), jnp.bfloat16),
    pltpu.VMEM((4, D, D), jnp.bfloat16),
    pltpu.VMEM((4, D, D), jnp.bfloat16),
    pltpu.VMEM((TALL, D), jnp.bfloat16),
    pltpu.VMEM((TALL, D), jnp.bfloat16),
    pltpu.VMEM((4, 4, 2, ROWS, D), jnp.bfloat16),
    pltpu.VMEM((4, 2, 2, 2, ROWS, D), jnp.bfloat16),
    pltpu.VMEM((D, D), jnp.bfloat16),
    pltpu.SemaphoreType.DMA((64,)),
    pltpu.SemaphoreType.DMA((16,)),
    pltpu.SemaphoreType.DMA((48,)),
]


def turn_kernel(
    plan, place_ref, length_ref, small_ref, below_ref, hidden_bias_ref, mix_any, summed_any,
    attn_any, cot_c_any, cot_q_any, *refs
):
    content_out, query_out = refs[-27:-25]
    outs = refs[-25:-20]
    vec_ref, dhidden_ref = refs[-20:-18]
    low_ref = refs[-18]
    (
        branch_ref, total_ref, normed_ref, resid_ref, pre_ref, mix_ref, wo_ref, inner_ref,
        outer_ref, active_ref, dpre_ref, dinner_ref, douter_ref, dwo_ref,
        sems, load_sems, store_sems,
    ) = refs[-17:]
    store, stores = storer(store_sems)
    finish(
        issue(
            ((mix_any, mix_ref), (attn_any.at[3], wo_ref), (summed_any, resid_ref)), load_sems
        )
    )
    fetches = start_fetch(
        ("inner", "outer"), plan, place_ref, refs[:-27], (inner_ref, outer_ref), sems
    )
    fetches += issue(
        ((cot_c_any, low_ref.at[:LEN, :]), (cot_q_any, low_ref.at[LEN:, :])), load_sems, 3
    )
    for row in range(0, TALL, HALF):
        rows = slice(row, row + HALF)
        unit, scale = norm_parts(resid_ref[rows, :])
        resid_ref[rows, :] = (
            unit * below_ref[6:7, :]
            + below_ref[7:8, :]
            + dot_nn(mix_ref[rows, :], wo_ref[...])
            + small_ref[2:3, :]
        )
    finish(fetches)
    sums = [jnp.zeros((1, D), jnp.float32)] * 3
    for row in range(0, TALL, HALF):
        rows = slice(row, row + HALF)
        total = feed_rows(
            rows, small_ref, hidden_bias_ref, resid_ref[rows, :], normed_ref, pre_ref, inner_ref,
            outer_ref,
        )
        unit, scale = norm_parts(total)
        position = lax.broadcasted_iota(jnp.int32, (HALF, 1), 0) + row % LEN
        valid = (position < length_ref[0]).astype(jnp.float32)
        grad = low_ref[rows, :].astype(jnp.float32) * valid
        low_ref[rows, :] = (unit * small_ref[6:7, :] + small_ref[7:8, :]).astype(jnp.bfloat16)
        total_ref[rows, :], branch_ref[rows, :], sums = norm_two_back(
            unit, scale, grad, small_ref, sums
        )
    store(low_ref.at[:LEN, :], content_out)
    store(low_ref.at[LEN:, :], query_out)
    for index, value in enumerate(sums):
        vec_ref[3 + index : 4 + index, :] = value
    back_steps(
        place_ref, small_ref, lambda step: None, store, outs, vec_ref, dhidden_ref, branch_ref,
        total_ref, normed_ref, resid_ref, pre_ref, mix_ref, wo_ref, inner_ref, outer_ref,
        active_ref, dpre_ref, dinner_ref, douter_ref, dwo_ref,
    )
    finish(stores)


def turn(place, length, small, below, hidden_bias, mixed, summed, attn, cots, group):
    plan, pieces = group
    half_low = jax.ShapeDtypeStruct((LEN, D), jnp.bfloat16)
    return pl.pallas_call(
        partial(turn_kernel, plan),
        out_shape=[half_low, half_low] + BACK_SHAPES,
        in_specs=[SMEM_SPEC] * 2 + [VMEM_SPEC] * 3 + [ANY_SPEC] * (5 + len(pieces)),
        out_specs=[ANY_SPEC] * 7 + [VMEM_SPEC] * 2,
        scratch_shapes=[pltpu.VMEM((TALL, D), jnp.bfloat16)] + BACK_SCRATCH,
        compiler_params=PARAMS,
        cost_estimate=pl.CostEstimate(flops=6 * TALL * D * (D + 2 * FF), bytes_accessed=60000000, transcendentals=6000000),
        name="turn",
    )(place, length, small, below, hidden_bias, mixed, summed, attn, *cots, *pieces)


def down_kernel(
    plan, place_ref, small_ref, dq_any, dk_any, dv_any, w_any, dresid_any, summed_any,
    normed_any, resid_any, pre_any, mix_any, attn_any, *refs
):
    outs = refs[-29:-24]
    vec_ref, dhidden_ref = refs[-24:-22]
    dq_ref, dk_ref, dv_ref, w_ref, summed_ref = refs[-22:-17]
    (
        branch_ref, total_ref, normed_ref, resid_ref, pre_ref, mix_ref, wo_ref, inner_ref,
        outer_ref, active_ref, dpre_ref, dinner_ref, douter_ref, dwo_ref,
        sems, load_sems, store_sems,
    ) = refs[-17:]
    x, c, z, y = (place_ref[index] for index in range(4))
    chunks = [side * 2 + (c ^ apart) for apart in (1, 0) for side in range(2)]
    store, stores = storer(store_sems)
    loads = issue(
        (
            (w_any.at[0], w_ref.at[0]), (dq_any, dq_ref), (dresid_any, total_ref),
            (summed_any, summed_ref), (w_any.at[1:3], w_ref.at[1:3]), (dk_any, dk_ref),
            (dv_any, dv_ref),
        ),
        load_sems,
    )
    finish(loads[:4])
    fetches = start_fetch(
        ("inner", "outer"), plan, place_ref, refs[:-29], (inner_ref, outer_ref), sems
    )
    fetches += issue(((pre_any.at[chunks[0]], pre_ref.at[chunks[0]]),), load_sems, 7)
    sums = [jnp.zeros((1, D), jnp.float32)] * 3
    for index, row in enumerate((LEN, LEN + HALF, 0, HALF)):
        rows = slice(row, row + HALF)
        if index == 2:
            finish(loads[4:])
        total = total_ref[rows, :] + dot_nt(dq_ref[rows, :], w_ref[0])
        if index >= 2:
            total = total + dot_nt(dk_ref[rows, :], w_ref[1]) + dot_nt(dv_ref[rows, :], w_ref[2])
        unit, scale = norm_parts(summed_ref[rows, :])
        total_ref[rows, :], branch_ref[rows, :], sums = norm_two_back(
            unit, scale, total, small_ref, sums
        )
    for index, value in enumerate(sums):
        vec_ref[3 + index : 4 + index, :] = value
    finish(fetches)
    late = []

    def before(step):
        if step == 0:
            late.append(issue(((normed_any, normed_ref),), load_sems, 8))
        else:
            finish(late.pop())
        if step < 3:
            chunk = chunks[step + 1]
            late.insert(0, issue(((pre_any.at[chunk], pre_ref.at[chunk]),), load_sems, 9 + step))
        if step == 0:
            finish(late.pop())
        if step == 2:
            late[0].extend(
                issue(
                    ((resid_any, resid_ref), (mix_any, mix_ref), (attn_any.at[3], wo_ref)),
                    load_sems,
                    12,
                )
            )

    back_steps(
        place_ref, small_ref, before, store, outs, vec_ref, dhidden_ref, branch_ref, total_ref,
        normed_ref, resid_ref, pre_ref, mix_ref, wo_ref, inner_ref, outer_ref, active_ref,
        dpre_ref, dinner_ref, douter_ref, dwo_ref,
    )
    finish(stores)


def down(place, small, dq, dk, dv, w_above, dresid, summed, normed, resid, pre, mixed, attn, group):
    plan, pieces = group
    return pl.pallas_call(
        partial(down_kernel, plan),
        out_shape=BACK_SHAPES,
        in_specs=[SMEM_SPEC, VMEM_SPEC] + [ANY_SPEC] * (11 + len(pieces)),
        out_specs=[ANY_SPEC] * 5 + [VMEM_SPEC] * 2,
        scratch_shapes=[
            pltpu.VMEM((TALL, D), jnp.bfloat16),
            pltpu.VMEM((LEN, D), jnp.bfloat16),
            pltpu.VMEM((LEN, D), jnp.bfloat16),
            pltpu.VMEM((3, D, D), jnp.bfloat16),
            pltpu.VMEM((TALL, D), jnp.float32),
        ]
        + BACK_SCRATCH,
        compiler_params=PARAMS,
        cost_estimate=pl.CostEstimate(flops=5 * TALL * D * (D + 2 * FF), bytes_accessed=60000000, transcendentals=3000000),
        name="down",
    )(place, small, dq, dk, dv, w_above, dresid, summed, normed, resid, pre, mixed, attn, *pieces)


def weight_back_kernel(
    place_ref, low_any, dq_any, dk_any, dv_any, dwo_any, keep_out, send_out, vec_ref,
    low_ref, dq_ref, dk_ref, dv_ref, dwo_ref, grads_ref, load_sems, sems,
):
    x, c, z, y = (place_ref[index] for index in range(4))
    load = [
        pltpu.make_async_copy(source, target, load_sems.at[index])
        for index, (source, target) in enumerate(
            (
                (low_any.at[:LEN, :], low_ref.at[:LEN, :]), (dk_any, dk_ref), (dv_any, dv_ref),
                (low_any.at[LEN:, :], low_ref.at[LEN:, :]), (dq_any, dq_ref), (dwo_any, dwo_ref),
            )
        )
    ]
    for copy in load:
        copy.start()
    load[0].wait()
    load[1].wait()
    grads_ref[1] = (
        dot_tn(low_ref[:LEN, :], dk_ref[...]).astype(jnp.bfloat16).reshape(4, 2, ROWS, D)
    )
    load[2].wait()
    grads_ref[2] = (
        dot_tn(low_ref[:LEN, :], dv_ref[...]).astype(jnp.bfloat16).reshape(4, 2, ROWS, D)
    )
    vec_ref[1:2, :] = jnp.sum(dv_ref[...].astype(jnp.float32), axis=0, keepdims=True)
    for copy in load[3:]:
        copy.wait()
    grads_ref[3] = dwo_ref[...].reshape(4, 2, ROWS, D)
    grads_ref[0] = dot_tn(low_ref[...], dq_ref[...]).astype(jnp.bfloat16).reshape(4, 2, ROWS, D)
    vec_ref[0:1, :] = jnp.sum(dq_ref[...].astype(jnp.float32), axis=0, keepdims=True)
    blocks = []
    for apart, target in ((1, send_out), (0, keep_out)):
        for side in range(2):
            for y_block in range(2):
                copy = pltpu.make_async_copy(
                    grads_ref.at[side * 2 + (c ^ apart), :, y_block],
                    target.at[y_block ^ y, side ^ x, :, 0],
                    sems.at[len(blocks)],
                )
                copy.start()
                blocks.append(copy)
    for block in blocks:
        block.wait()


def weight_back(place, low, dq, dk, dv, dwo):
    blocks = jax.ShapeDtypeStruct((2, 2, 4, 1, ROWS, D), jnp.bfloat16)
    return pl.pallas_call(
        weight_back_kernel,
        out_shape=[blocks, blocks, jax.ShapeDtypeStruct((2, D), jnp.float32)],
        in_specs=[SMEM_SPEC] + [ANY_SPEC] * 5,
        out_specs=[ANY_SPEC] * 2 + [VMEM_SPEC],
        scratch_shapes=[
            pltpu.VMEM((TALL, D), jnp.bfloat16),
            pltpu.VMEM((TALL, D), jnp.bfloat16),
            pltpu.VMEM((LEN, D), jnp.bfloat16),
            pltpu.VMEM((LEN, D), jnp.bfloat16),
            pltpu.VMEM((D, D), jnp.bfloat16),
            pltpu.VMEM((4, 4, 2, ROWS, D), jnp.bfloat16),
            pltpu.SemaphoreType.DMA((6,)),
            pltpu.SemaphoreType.DMA((8,)),
        ],
        compiler_params=PARAMS,
        cost_estimate=pl.CostEstimate(flops=2 * 2048 * D * D, bytes_accessed=12000000, transcendentals=0),
        name="weight_back",
    )(place, low, dq, dk, dv, dwo)


def input_back_kernel(
    dq_any, dk_any, dv_any, w_any, dresid_any, first_out, second_out,
    dq_ref, dk_ref, dv_ref, w_ref, dresid_ref, load_sems, store_sems,
):
    loads = issue(
        (
            (w_any.at[0], w_ref.at[0]), (dq_any, dq_ref), (dresid_any, dresid_ref),
            (w_any.at[1:3], w_ref.at[1:3]), (dk_any, dk_ref), (dv_any, dv_ref),
        ),
        load_sems,
    )
    finish(loads[:3])
    store, stores = storer(store_sems)
    for index, row in enumerate((LEN, LEN + HALF, 0, HALF)):
        rows = slice(row, row + HALF)
        if index == 2:
            finish(loads[3:])
        total = dresid_ref[rows, :] + dot_nt(dq_ref[rows, :], w_ref[0])
        if index >= 2:
            total = total + dot_nt(dk_ref[rows, :], w_ref[1]) + dot_nt(dv_ref[rows, :], w_ref[2])
        dresid_ref[rows, :] = total
        target = first_out if index >= 2 else second_out
        store(dresid_ref.at[rows, :], target.at[row % LEN : row % LEN + HALF, :])
    finish(stores)


def input_back(dq, dk, dv, attn, dresid):
    half = jax.ShapeDtypeStruct((LEN, D), jnp.float32)
    return pl.pallas_call(
        input_back_kernel,
        out_shape=[half, half],
        in_specs=[ANY_SPEC] * 5,
        out_specs=[ANY_SPEC] * 2,
        scratch_shapes=[
            pltpu.VMEM((TALL, D), jnp.bfloat16),
            pltpu.VMEM((LEN, D), jnp.bfloat16),
            pltpu.VMEM((LEN, D), jnp.bfloat16),
            pltpu.VMEM((3, D, D), jnp.bfloat16),
            pltpu.VMEM((TALL, D), jnp.float32),
            pltpu.SemaphoreType.DMA((6,)),
            pltpu.SemaphoreType.DMA((4,)),
        ],
        compiler_params=PARAMS,
        cost_estimate=pl.CostEstimate(flops=2 * 2048 * D * D, bytes_accessed=16000000, transcendentals=0),
        name="input_back",
    )(dq, dk, dv, attn, dresid)


def bias_vectors(table):
    lane = jnp.arange(512, dtype=jnp.int32)
    offset = jnp.where(lane < 384, 128 - lane, 640 - lane)
    onehot = bucket_of(offset)[:, None] == jnp.arange(NB, dtype=jnp.int32)[None, :]
    near = jnp.dot(table, onehot.astype(jnp.float32).T, precision=lax.Precision.HIGHEST)
    return (near[:, None, :], jnp.stack([table[:, 15], table[:, 31]], axis=1), onehot)


def bucket_of(offset):
    distance = jnp.abs(offset)
    far_bucket = jnp.full(distance.shape, 8, jnp.int32)
    for exponent in range(1, 8):
        far_bucket = far_bucket + (distance * distance >= 64 * 2**exponent).astype(jnp.int32)
    near_or_far = jnp.where(distance < 8, distance, far_bucket)
    return near_or_far + NB // 2 * (offset > 0).astype(jnp.int32)


def table_grad(sums, onehot):
    near = jnp.roll(onehot.astype(jnp.float32), 127, axis=0)
    far = jnp.arange(NB, dtype=jnp.int32)[None, :] == jnp.repeat(jnp.array([15, 31]), 128)[:, None]
    return jnp.dot(
        sums[:, 0, :],
        jnp.concatenate([near, far.astype(jnp.float32)]),
        precision=lax.Precision.HIGHEST,
    )


RATES = (ATTENTION_RATE, FEED_RATE, FEED_RATE)


def adam_kernel(*refs):
    states, grads, outs = refs[:9], refs[9:12], refs[-9:]
    for kind, rate in enumerate(RATES):
        master_ref, first_ref, second_ref = states[3 * kind : 3 * kind + 3]
        master_out, first_out, second_out = outs[3 * kind : 3 * kind + 3]
        grad = grads[kind][...].astype(jnp.float32).reshape(master_ref.shape)
        master = master_ref[...]
        first = BETA_ONE * first_ref[...] + (1.0 - BETA_ONE) * grad
        second = BETA_TWO * second_ref[...] + (1.0 - BETA_TWO) * grad * grad
        first_out[...] = first
        second_out[...] = second
        first_scale = rate / (1.0 - BETA_ONE**STEP)
        second_scale = 1.0 / (1.0 - BETA_TWO**STEP)
        step = (first_scale * first) / (jnp.sqrt(second_scale * second) + ADAM_EPS)
        master_out[...] = master - (step + (rate * WEIGHT_DECAY) * master)


def adam(layer, state, quarters, held):
    half = ROWS // 2
    blocks = (
        [pl.BlockSpec((1, 1, half, D), lambda i: (layer, i // 2, i % 2, 0))] * 3
        + [pl.BlockSpec((1, half, D), lambda i: (layer, i % 2, i // 2))] * 3
        + [pl.BlockSpec((1, half, D), lambda i: (layer, i, 0))] * 3
    )
    grads = [
        pl.BlockSpec((1, 1, half, D), partial(lambda member, i: (i // 2, member, i % 2, 0), member))
        for member in (2, 0, 1)
    ]
    return pl.pallas_call(
        adam_kernel,
        grid=(8,),
        out_shape=[jax.ShapeDtypeStruct(array.shape, jnp.float32) for array in state],
        in_specs=blocks + grads + [ANY_SPEC] * len(held),
        out_specs=blocks,
        input_output_aliases={12 + index: index for index in range(len(held))},
        compiler_params=PARAMS,
        cost_estimate=pl.CostEstimate(flops=20000000, bytes_accessed=22000000, transcendentals=0),
        name="adam",
    )(*state, quarters, quarters, quarters, *held)


def fetch_forward(shards):
    low = tuple(shard.astype(jnp.bfloat16) for shard in shards)
    return (
        lax.all_gather(low[0], "fsdp", axis=1, tiled=True),
        lax.all_gather(low[1], "fsdp", axis=0, tiled=True),
        lax.all_gather(low[2], "fsdp", axis=0, tiled=True),
    )


def reduce_layer(grads):
    owned = tuple(
        lax.psum_scatter(
            grad.astype(jnp.bfloat16), "fsdp", scatter_dimension=axis, tiled=True
        ).astype(jnp.float32)
        for grad, axis in zip(grads, (1, 0, 0))
    )
    return lax.psum(owned, "dp")


def forward_layer(hidden_c, hidden_q, weights, lengths, flag_rows, onehot):
    attn_w, inner_w, outer_w, small_w = weights
    pieces, hidden_bias, bias_table = unpack(small_w.astype(jnp.float32))
    bias_q, bias_v, bias_o, gain_one, shift_one, bias_two, gain_two, shift_two = pieces
    table_low = bias_table.astype(jnp.bfloat16)
    low_c = hidden_c.astype(jnp.bfloat16)
    low_q = hidden_q.astype(jnp.bfloat16)
    projected = jnp.einsum("td,sde->ste", low_c, attn_w[:3], preferred_element_type=jnp.float32)
    query_c = (projected[0] + bias_q).astype(jnp.bfloat16)
    key_rows = projected[1].astype(jnp.bfloat16)
    value_rows = (projected[2] + bias_v).astype(jnp.bfloat16)
    query_q = (jnp.dot(low_q, attn_w[0], preferred_element_type=jnp.float32) + bias_q).astype(
        jnp.bfloat16
    )
    mixed_c, mixed_q, lse_c, lse_q = lax.map(
        partial(attend_slot, onehot, table_low),
        (
            to_heads(query_c),
            to_heads(query_q),
            to_heads(key_rows),
            to_heads(value_rows),
            lengths,
            flag_rows,
        ),
    )
    mixed_c = mixed_c.reshape(-1, D)
    mixed_q = mixed_q.reshape(-1, D)
    outputs = []
    kept = []
    for hidden_in, mixed in ((hidden_c, mixed_c), (hidden_q, mixed_q)):
        resid = hidden_in + jnp.dot(mixed, attn_w[3], preferred_element_type=jnp.float32) + bias_o
        normed = layer_norm(resid, gain_one, shift_one)
        pre_act = (
            jnp.dot(normed.astype(jnp.bfloat16), inner_w, preferred_element_type=jnp.float32)
            + hidden_bias
        )
        active = jax.nn.gelu(pre_act, approximate=True).astype(jnp.bfloat16)
        summed = normed + jnp.dot(active, outer_w, preferred_element_type=jnp.float32) + bias_two
        outputs.append(layer_norm(summed, gain_two, shift_two))
        kept.append((resid, summed, pre_act))
    saved = (
        hidden_c,
        hidden_q,
        query_c,
        query_q,
        key_rows,
        value_rows,
        lse_c,
        lse_q,
        mixed_c,
        mixed_q,
        kept[0],
        kept[1],
    )
    return (outputs[0], outputs[1], saved)


def backward_layer(saved, weights, grad_c, grad_q, lengths, flag_rows, onehot):
    attn_w, inner_w, outer_w, small_w = weights
    pieces, hidden_bias, bias_table = unpack(small_w.astype(jnp.float32))
    bias_q, bias_v, bias_o, gain_one, shift_one, bias_two, gain_two, shift_two = pieces
    table_low = bias_table.astype(jnp.bfloat16)
    (
        hidden_c,
        hidden_q,
        query_c,
        query_q,
        key_rows,
        value_rows,
        lse_c,
        lse_q,
        mixed_c,
        mixed_q,
        kept_c,
        kept_q,
    ) = saved
    gelu_tanh = partial(jax.nn.gelu, approximate=True)
    grad_outer = jnp.zeros(outer_w.shape, jnp.float32)
    grad_inner = jnp.zeros(inner_w.shape, jnp.float32)
    grad_attn_out = jnp.zeros((D, D), jnp.float32)
    grad_bias_two = jnp.zeros((D,), jnp.float32)
    grad_hidden_bias = jnp.zeros((FF,), jnp.float32)
    grad_bias_o = jnp.zeros((D,), jnp.float32)
    grad_gain_one = jnp.zeros((D,), jnp.float32)
    grad_shift_one = jnp.zeros((D,), jnp.float32)
    grad_gain_two = jnp.zeros((D,), jnp.float32)
    grad_shift_two = jnp.zeros((D,), jnp.float32)
    residual_grads = []
    mix_grads = []
    for kept_rows, grad_out, mixed in ((kept_c, grad_c, mixed_c), (kept_q, grad_q, mixed_q)):
        resid, summed, pre_act = kept_rows
        normed, norm_one_back = jax.vjp(layer_norm, resid, gain_one, shift_one)
        unused_out, norm_two_back = jax.vjp(layer_norm, summed, gain_two, shift_two)
        grad_summed, grad_g2, grad_s2 = norm_two_back(grad_out)
        grad_gain_two = grad_gain_two + grad_g2
        grad_shift_two = grad_shift_two + grad_s2
        grad_branch = grad_summed.astype(jnp.bfloat16)
        grad_bias_two = grad_bias_two + jnp.sum(grad_branch.astype(jnp.float32), axis=0)
        active, gelu_back = jax.vjp(gelu_tanh, pre_act)
        grad_outer = grad_outer + jnp.einsum(
            "tf,td->fd",
            active.astype(jnp.bfloat16),
            grad_branch,
            preferred_element_type=jnp.float32,
        )
        grad_active = jnp.einsum(
            "td,fd->tf", grad_branch, outer_w, preferred_element_type=jnp.float32
        )
        grad_pre = gelu_back(grad_active)[0].astype(jnp.bfloat16)
        grad_hidden_bias = grad_hidden_bias + jnp.sum(grad_pre.astype(jnp.float32), axis=0)
        grad_inner = grad_inner + jnp.einsum(
            "td,tf->df", normed.astype(jnp.bfloat16), grad_pre, preferred_element_type=jnp.float32
        )
        grad_normed = grad_summed + jnp.einsum(
            "tf,df->td", grad_pre, inner_w, preferred_element_type=jnp.float32
        )
        grad_resid, grad_g1, grad_s1 = norm_one_back(grad_normed)
        grad_gain_one = grad_gain_one + grad_g1
        grad_shift_one = grad_shift_one + grad_s1
        grad_proj = grad_resid.astype(jnp.bfloat16)
        grad_bias_o = grad_bias_o + jnp.sum(grad_proj.astype(jnp.float32), axis=0)
        grad_attn_out = grad_attn_out + jnp.einsum(
            "td,te->de", mixed, grad_proj, preferred_element_type=jnp.float32
        )
        mix_grads.append(
            jnp.einsum(
                "te,de->td", grad_proj, attn_w[3], preferred_element_type=jnp.float32
            ).astype(jnp.bfloat16)
        )
        residual_grads.append(grad_resid)
    grad_query_c, grad_query_q, grad_keys, grad_values, grad_table = lax.map(
        partial(attend_back, onehot, table_low),
        (
            to_heads(query_c),
            to_heads(query_q),
            to_heads(key_rows),
            to_heads(value_rows),
            lengths,
            flag_rows,
            lse_c,
            lse_q,
            to_heads(mix_grads[0]),
            to_heads(mix_grads[1]),
        ),
    )
    grad_table = jnp.sum(grad_table, axis=0)
    low_query_c = grad_query_c.reshape(-1, D).astype(jnp.bfloat16)
    low_query_q = grad_query_q.reshape(-1, D).astype(jnp.bfloat16)
    low_keys = grad_keys.reshape(-1, D).astype(jnp.bfloat16)
    low_values = grad_values.reshape(-1, D).astype(jnp.bfloat16)
    low_c = hidden_c.astype(jnp.bfloat16)
    low_q = hidden_q.astype(jnp.bfloat16)
    stacked_grads = jnp.stack([low_query_c, low_keys, low_values])
    grad_qkv = jnp.einsum("td,ste->sde", low_c, stacked_grads, preferred_element_type=jnp.float32)
    grad_wq = grad_qkv[0] + jnp.einsum(
        "td,te->de", low_q, low_query_q, preferred_element_type=jnp.float32
    )
    grad_attn = jnp.stack([grad_wq, grad_qkv[1], grad_qkv[2], grad_attn_out])
    grad_bias_q = jnp.sum(low_query_c.astype(jnp.float32), axis=0) + jnp.sum(
        low_query_q.astype(jnp.float32), axis=0
    )
    grad_bias_v = jnp.sum(low_values.astype(jnp.float32), axis=0)
    grad_content = residual_grads[0] + jnp.einsum(
        "ste,sde->td", stacked_grads, attn_w[:3], preferred_element_type=jnp.float32
    )
    grad_query_in = residual_grads[1] + jnp.einsum(
        "te,de->td", low_query_q, attn_w[0], preferred_element_type=jnp.float32
    )
    grad_small = jnp.concatenate(
        [
            grad_bias_q,
            grad_bias_v,
            grad_bias_o,
            grad_gain_one,
            grad_shift_one,
            grad_bias_two,
            grad_gain_two,
            grad_shift_two,
            grad_hidden_bias,
            grad_table.reshape(-1),
        ]
    )
    return (grad_content, grad_query_in, (grad_attn, grad_inner, grad_outer, grad_small))


def adam_update(master, first, second, grad, rate):
    first_new = BETA_ONE * first + (1.0 - BETA_ONE) * grad
    second_new = BETA_TWO * second + (1.0 - BETA_TWO) * grad * grad
    first_hat = first_new / (1.0 - BETA_ONE**STEP)
    second_hat = second_new / (1.0 - BETA_TWO**STEP)
    master_new = master - rate * (
        first_hat / (jnp.sqrt(second_hat) + ADAM_EPS) + WEIGHT_DECAY * master
    )
    return (master_new, first_new, second_new)


def per_device(
    content,
    query,
    lengths,
    predicted,
    content_cot,
    query_cot,
    attn_master,
    attn_first,
    attn_second,
    inner_master,
    inner_first,
    inner_second,
    outer_master,
    outer_first,
    outer_second,
    small_master,
    small_first,
    small_second,
):
    masters = (attn_master, inner_master, outer_master, small_master)
    slot_count = lengths.shape[0]
    flag_rows = predicted.reshape(slot_count, LEN)
    onehot = bucket_onehot()
    hidden_c = content.astype(jnp.float32)
    hidden_q = query.astype(jnp.float32)
    kept_weights = []
    saved_layers = []
    small_all = lax.all_gather(
        small_master.astype(jnp.bfloat16), "fsdp", axis=1, tiled=True
    )
    for layer_index in range(LAYERS):
        shards = tuple((master[layer_index] for master in masters[:3]))
        gathered = fetch_forward(shards) + (small_all[layer_index],)
        kept_weights.append(gathered)
        hidden_c, hidden_q, saved = forward_layer(
            hidden_c, hidden_q, gathered, lengths, flag_rows, onehot
        )
        saved_layers.append(saved)
    position = jnp.arange(LEN, dtype=jnp.int32)
    valid_rows = (position[None, :] < lengths[:, None]).reshape(-1, 1).astype(jnp.float32)
    grad_c = content_cot.astype(jnp.float32) * valid_rows
    grad_q = query_cot.astype(jnp.float32) * valid_rows
    layer_grads = [None] * LAYERS
    small_grads = [None] * LAYERS
    for layer_index in reversed(range(LAYERS)):
        grad_c, grad_q, local_grads = backward_layer(
            saved_layers[layer_index],
            kept_weights[layer_index],
            grad_c,
            grad_q,
            lengths,
            flag_rows,
            onehot,
        )
        small_grads[layer_index] = local_grads[3]
        layer_grads[layer_index] = reduce_layer(local_grads[:3])
    small_sum = lax.psum(jnp.stack(small_grads), ("dp", "fsdp"))
    owned = small_master.shape[1]
    small_own = lax.dynamic_slice_in_dim(
        small_sum, lax.axis_index("fsdp") * owned, owned, 1
    )
    reduced = tuple(
        (
            jnp.stack([layer_grads[layer_index][member] for layer_index in range(LAYERS)])
            for member in range(3)
        )
    ) + (small_own,)
    attn_new = adam_update(attn_master, attn_first, attn_second, reduced[0], ATTENTION_RATE)
    inner_new = adam_update(inner_master, inner_first, inner_second, reduced[1], FEED_RATE)
    outer_new = adam_update(outer_master, outer_first, outer_second, reduced[2], FEED_RATE)
    small_new = adam_update(small_master, small_first, small_second, reduced[3], SMALL_RATE)
    return (
        hidden_c.astype(jnp.bfloat16),
        hidden_q.astype(jnp.bfloat16),
        grad_c,
        grad_q,
        attn_new[0],
        attn_new[1],
        attn_new[2],
        inner_new[0],
        inner_new[1],
        inner_new[2],
        outer_new[0],
        outer_new[1],
        outer_new[2],
        small_new[0],
        small_new[1],
        small_new[2],
    )


def after(value, *others):
    return lax.optimization_barrier((value, others))[0]


def join(*values):
    return lax.optimization_barrier(values)


def gather_group(count, shards, plane, column, sides, corners, mine, theirs):
    plan = []
    for core, arrays in enumerate((mine, theirs)):
        base = core * len(mine)
        for member in range(count):
            array, first = plane
            plan += [
                (base + array, first + side * count + member, side, 1, core, 0, member)
                for side in range(2)
            ]
            for apart in (1, 2, 3):
                index = (apart - 1) * count + member
                array, first = column
                plan.append((base + array, first + index, 0, 0, core, apart, member))
                for dx, dy, (array, first) in ((1, 0, sides[0]), (0, 1, sides[1])):
                    plan.append((base + array, first + index, dx, dy, core, apart, member))
                skipped = 0
                for array, first, held in corners:
                    if skipped <= index < skipped + held:
                        plan.append(
                            (base + array, first + index - skipped, 1, 1, core, apart, member)
                        )
                    skipped += held
    return (tuple(plan), tuple(shards) + tuple(mine) + tuple(theirs))


def gather_small(blocks, place):
    low, high = place[2] % 2, place[2] // 2
    blocks = jnp.where(low == 0, blocks, blocks[jnp.array([1, 0, 3, 2])])
    blocks = jnp.where(high == 0, blocks, blocks[jnp.array([2, 3, 0, 1])])
    return blocks.transpose(2, 0, 1, 3).reshape(blocks.shape[2], -1)


def add_low(*values):
    total = values[0].astype(jnp.float32)
    for value in values[1:]:
        total = total + value.astype(jnp.float32)
    return total.astype(jnp.bfloat16)


def reduce_corners(keep, get):
    corner = add_low(keep[1, 1], get[1, 1])
    return (swap_x(corner[:2]), swap_y(corner[2:]))


def side_payloads(keep, get, corners):
    by_x, by_y = corners
    pad = ((0, 0),) * 3
    for_x = add_low(keep[0, 1], get[0, 1], jnp.pad(by_y, ((2, 0),) + pad))
    for_y = add_low(keep[1, 0], get[1, 0], jnp.pad(by_x, ((0, 2),) + pad))
    return (for_x, for_y)


def reduce_sides(payloads):
    return (swap_x(payloads[0]), swap_y(payloads[1]))


def z_half(value, half):
    if value.ndim == 4:
        return lax.dynamic_slice_in_dim(value, 2 * half, 2, 0)
    part = lax.dynamic_slice(value, (0, 0, 2 * half, 0, 0, 0), (1, 1, 2) + value.shape[3:])
    return part[0, 0]


def far_payload(keep, get, sides, place):
    half = 1 - place[2] // 2
    return add_low(*(z_half(value, half) for value in (keep, get) + tuple(sides)))


def own_pair(keep, get, sides, far, place):
    half = place[2] // 2
    return add_low(*(z_half(value, half) for value in (keep, get) + tuple(sides)), far)


def pick(pair, index):
    return lax.dynamic_index_in_dim(pair, index, 0, keepdims=False)


def reduce_near(pair, place):
    return swap_z(pick(pair, 1 - place[2] % 2), 1)


def reduce_total(pair, near, place):
    return add_low(pick(pair, place[2] % 2), near)


def reduce_direct(column, place):
    return tuple(swap_z(pick(column, place[2] ^ apart), apart) for apart in (1, 2, 3))


def share_core(pair, place):
    x, c = place[0], place[1]
    other = swap_core(pair)
    cores = jnp.where(c == 0, jnp.stack([pair, other], 1), jnp.stack([other, pair], 1))
    sides = jnp.where(x == 0, cores, cores[::-1])
    return sides.reshape((4,) + pair.shape[1:])


def small_parts(vectors):
    values = vectors.astype(jnp.float32)
    return (
        values[: 8 * D].reshape(8, D),
        values[8 * D : 8 * D + FF].reshape(1, FF),
        bias_vectors(values[8 * D + FF :].reshape(H, NB)),
    )


def per_device_fast(
    content,
    query,
    lengths,
    predicted,
    content_cot,
    query_cot,
    attn_master,
    attn_first,
    attn_second,
    inner_master,
    inner_first,
    inner_second,
    outer_master,
    outer_first,
    outer_second,
    small_master,
    small_first,
    small_second,
):
    place_parts = my_place()
    place = jnp.stack(place_parts).astype(jnp.int32)
    own_a0, plane_a0, own_f0 = cast_first(place, attn_master, inner_master, outer_master)
    z_a0 = tuple(swap_z(own_a0, apart) for apart in (1, 2, 3))
    plane_a0 = swap_y(plane_a0)
    near_f0 = swap_z(own_f0, 1)
    attn_low0, attn_low1, inner_low0, inner_low1, outer_low0, outer_low1, plane_f0, own_1, oth_1 = (
        cast_rest(place, attn_master, inner_master, outer_master)
    )
    low0 = jnp.concatenate([content, query])
    row_flags = predicted.reshape(1, LEN).astype(jnp.float32)
    col_flags = predicted.reshape(LEN, 1).astype(jnp.float32)
    small_low = small_master.astype(jnp.bfloat16)
    small_y = swap_y(small_low)
    z_a0, plane_a0, near_f0, plane_f0, own_1, oth_1, low0, row_flags, col_flags, small_y = join(
        z_a0, plane_a0, near_f0, plane_f0, own_1, oth_1, low0, row_flags, col_flags, small_y
    )
    col_a0, to_far_f0 = pack(
        ([(0, 0, 1), (1, 0, 1), (2, 0, 1)], [(3, 0, 2), (4, 0, 2)]), (*z_a0, own_f0, near_f0)
    )
    x0 = swap_x(col_a0)
    y0 = swap_y(col_a0)
    far_f0 = swap_z(to_far_f0, 2)
    plane_f0 = swap_y(after(plane_f0, col_a0))
    near_1 = swap_z(after(own_1, col_a0), 1)
    odd = place_parts[3] == 1
    small_pair = jnp.stack(
        [jnp.where(odd, small_y, small_low), jnp.where(odd, small_low, small_y)]
    )
    small_near = swap_z(small_pair, 1)
    x0, y0, far_f0, plane_f0, near_1, small_near = join(
        x0, y0, far_f0, plane_f0, near_1, small_near
    )
    to_x1, to_y1, to_far_a1 = pack(
        (
            [(0, 0, 2), (1, 0, 4), (2, 0, 2)],
            [(0, 0, 2), (1, 0, 4), (3, 2, 1)],
            [(4, 0, 1), (5, 0, 1)],
        ),
        (near_f0, far_f0, y0, x0, own_1, near_1),
    )
    x1 = swap_x(to_x1)
    y1 = swap_y(to_y1)
    far_a1 = swap_z(to_far_a1, 2)
    (mine_0,) = pack(
        (
            [(0, 0, 2), (1, 0, 3), (2, 0, 3), (3, 0, 3), (4, 0, 4), (5, 0, 2), (6, 0, 4)],
        ),
        after((plane_a0, col_a0, x0, y0, plane_f0, near_f0, far_f0), to_x1),
    )
    theirs_0 = swap_core(mine_0)
    small_four = jnp.stack([small_pair, small_near])
    small_far = swap_z(small_four, 2)
    small_all = gather_small(jnp.concatenate([small_four, small_far]), place_parts)
    x1, y1, far_a1, theirs_0, small_all = join(x1, y1, far_a1, theirs_0, small_all)
    to_x2, to_y2, to_far_f1, col_a1 = pack(
        (
            [(0, 0, 1), (1, 0, 2), (2, 0, 4)],
            [(0, 0, 1), (1, 0, 2), (3, 4, 2), (4, 0, 1), (5, 0, 1)],
            [(4, 1, 2), (0, 1, 2)],
            [(0, 0, 1), (1, 0, 2)],
        ),
        (near_1, far_a1, y1, x1, own_1, oth_1),
    )
    x2 = swap_x(to_x2)
    y2 = swap_y(to_y2)
    far_f1 = swap_z(to_far_f1, 2)
    their_x1, their_y1 = swap_core(x1), swap_core(y1)
    group_a0 = gather_group(
        1, (attn_low0,), (0, 0), (0, 2), ((0, 5), (0, 8)), ((1, 6, 2), (2, 6, 1)),
        (mine_0, x1, y1), (theirs_0, their_x1, their_y1),
    )
    small0, hidden_bias0, (tvec0, far0, onehot) = small_parts(small_all[0])
    small1, hidden_bias1, (tvec1, far1, onehot) = small_parts(small_all[1])
    q0, k0, v0, attn0 = project(place, low0, small0, group_a0)
    mixed0, p0, inverse0, dead = mix(lengths, far0, tvec0, q0, k0, v0, row_flags, col_flags)
    x2, y2, far_f1, mixed0 = join(x2, y2, far_f1, mixed0)
    to_x3, to_y3, col_f1 = pack(
        (
            [(0, 1, 2), (1, 0, 4), (2, 0, 3)],
            [(0, 1, 2), (1, 0, 4), (3, 1, 2), (4, 1, 2)],
            [(0, 1, 2), (1, 0, 4)],
        ),
        (near_1, far_f1, y2, own_1, oth_1),
    )
    x3 = swap_x(to_x3)
    y3 = swap_y(to_y3)
    their_x2, their_y2, their_a1 = swap_core(x2), swap_core(y2), swap_core(after(col_a1, x2))
    group_f0 = gather_group(
        2, (inner_low0, outer_low0), (0, 11), (0, 15), ((1, 0), (2, 0)), ((3, 3, 4), (4, 3, 2)),
        (mine_0, x1, y1, x2, y2), (theirs_0, their_x1, their_y1, their_x2, their_y2),
    )
    resid0, pre0, normed0, low1, summed0 = feed(
        place, small0, hidden_bias0, mixed0, low0, attn0, group_f0
    )
    x3, y3, low1 = join(x3, y3, low1)
    to_x4, to_y4 = pack(([(0, 0, 3)], [(1, 3, 3)]), (y3, x3))
    x4 = swap_x(to_x4)
    y4 = swap_y(to_y4)
    their_x3, their_y3 = swap_core(x3), swap_core(y3)
    group_a1 = gather_group(
        1, (attn_low1,), (1, 5), (2, 0), ((0, 0), (1, 0)), ((3, 6, 3),),
        (x2, y2, col_a1, x3), (their_x2, their_y2, their_a1, their_x3),
    )
    q1, k1, v1, attn1 = project(place, low1, small1, group_a1)
    x4, y4, q1 = join(x4, y4, q1)
    their_x4, their_y4, their_f1 = swap_core(x4), swap_core(y4), swap_core(after(col_f1, q1))
    group_f1 = gather_group(
        2, (inner_low1, outer_low1), (1, 6), (4, 0), ((0, 0), (1, 0)), ((2, 0, 3), (3, 0, 3)),
        (x3, y3, x4, y4, col_f1), (their_x3, their_y3, their_x4, their_y4, their_f1),
    )
    mixed1, p1, inverse1, dead = mix(
        lengths, far1, tvec1, q1, k1, v1, row_flags, col_flags
    )
    content_out, query_out, dresid1, dmix1, dwo1, keep_f1, send_f1, vec_f1, dhidden1 = turn(
        place, lengths, small1, small0, hidden_bias1, mixed1, summed0, attn1,
        (content_cot, query_cot), group_f1
    )
    get_f1 = swap_core(send_f1)
    *first1, table1_a = mix_back(0, q1, k1, v1, dmix1, mixed1, p1, inverse1, dead)
    by_f1 = reduce_corners(keep_f1, after(get_f1, table1_a))
    dq1, dk1, dv1, table1_b = mix_back(
        3, after(q1, get_f1, table1_a), k1, v1, dmix1, mixed1, p1, inverse1, dead, tuple(first1)
    )
    sides_rf1 = reduce_sides(side_payloads(keep_f1, get_f1, after(by_f1, table1_b)))
    keep_a1, send_a1, vec_a1 = weight_back(place, after(low1, by_f1), dq1, dk1, dv1, dwo1)
    get_a1 = swap_core(send_a1)
    by_a1 = reduce_corners(keep_a1, get_a1)
    dresid0, dmix0, dwo0, keep_f0, send_f0, vec_f0, dhidden0 = down(
        place, small0, dq1, dk1, dv1, after(attn1, get_a1), dresid1, summed0, normed0, resid0,
        pre0, mixed0, attn0, group_f0
    )
    get_f0 = swap_core(after(send_f0, sides_rf1, by_a1))
    sides_ra1 = reduce_sides(side_payloads(keep_a1, get_a1, after(by_a1, dmix0)))
    sides_rf1 = after(sides_rf1, dmix0)
    zfar_f1 = swap_z(far_payload(keep_f1, get_f1, sides_rf1, place_parts), 2)
    *first0, table0_a = mix_back(
        0, after(q0, by_a1, sides_rf1), k0, v0, dmix0, mixed0, p0, inverse0, dead
    )
    by_f0 = reduce_corners(keep_f0, after(get_f0, table0_a))
    dq0, dk0, dv0, table0_b = mix_back(
        3, after(q0, get_f0, table0_a), k0, v0, dmix0, mixed0, p0, inverse0, dead, tuple(first0)
    )
    by_f0, sides_ra1, zfar_f1, table0_b = join(by_f0, sides_ra1, zfar_f1, table0_b)
    payloads_f0 = side_payloads(keep_f0, get_f0, by_f0)
    sides_rf0 = reduce_sides(payloads_f0)
    keep_a0, send_a0, vec_a0 = weight_back(
        place, after(low0, payloads_f0, table0_b), dq0, dk0, dv0, dwo0
    )
    get_a0 = swap_core(send_a0)
    zfar_a1 = swap_z(far_payload(keep_a1, get_a1, sides_ra1, place_parts), 2)
    small_sum = jnp.concatenate(
        [
            jnp.stack([vec_a0, vec_a1]).reshape(LAYERS, -1),
            jnp.stack([vec_f0, vec_f1]).reshape(LAYERS, -1),
            jnp.stack([dhidden0, dhidden1]).reshape(LAYERS, -1),
            table_grad(
                jnp.concatenate([table0_a, table0_b, table1_a, table1_b]), onehot
            ).reshape(LAYERS, -1),
        ],
        axis=1,
    )
    pair_f1 = own_pair(keep_f1, get_f1, sides_rf1, zfar_f1, place_parts)
    znear_f1 = reduce_near(pair_f1, place_parts)
    small_c = swap_core(small_sum)
    sides_rf0, get_a0, zfar_a1, znear_f1, small_c = join(
        sides_rf0, get_a0, zfar_a1, znear_f1, small_c
    )
    payload_f0 = far_payload(keep_f0, get_f0, sides_rf0, place_parts)
    zfar_f0 = swap_z(payload_f0, 2)
    by_a0 = reduce_corners(keep_a0, after(get_a0, payload_f0))
    pair_a1 = own_pair(keep_a1, get_a1, sides_ra1, zfar_a1, place_parts)
    znear_a1 = reduce_near(after(pair_a1, payload_f0), place_parts)
    content_grad, query_grad = input_back(after(dq0, sides_rf0), dk0, dv0, attn0, dresid0)
    small_sum = after(small_sum, payload_f0) + small_c
    small_y = swap_y(small_sum)
    by_a0, content_grad, znear_a1, small_y = join(by_a0, content_grad, znear_a1, small_y)
    payloads_a0 = side_payloads(keep_a0, get_a0, by_a0)
    sides_ra0 = reduce_sides(payloads_a0)
    own_1 = jnp.concatenate(
        [
            reduce_total(pair_f1, znear_f1, place_parts),
            reduce_total(pair_a1, znear_a1, place_parts),
        ]
    )
    across_1 = swap_x(after(own_1, payloads_a0))
    small_sum = after(small_sum, payloads_a0) + small_y
    small_x = swap_x(small_sum)
    sides_ra0, zfar_f0, small_x = join(sides_ra0, zfar_f0, small_x)
    column_a0 = add_low(keep_a0[0, 0], get_a0[0, 0], *sides_ra0)
    shifts_a0 = reduce_direct(column_a0, place_parts)
    pair_f0 = own_pair(keep_f0, get_f0, sides_rf0, zfar_f0, place_parts)
    znear_f0 = reduce_near(after(pair_f0, column_a0), place_parts)
    small_sum = after(small_sum, column_a0) + small_x
    small_z = swap_z(small_sum, 1)
    shifts_a0, znear_f0, across_1, small_z = join(shifts_a0, znear_f0, across_1, small_z)
    own_0 = jnp.concatenate(
        [
            reduce_total(pair_f0, znear_f0, place_parts),
            add_low(pick(column_a0, place_parts[2]), *shifts_a0),
        ]
    )
    across_0 = swap_x(own_0)
    four_1 = share_core(jnp.stack([own_1, after(across_1, own_0)]), place_parts)
    state = (
        attn_master, attn_first, attn_second, inner_master, inner_first, inner_second,
        outer_master, outer_first, outer_second,
    )
    new_1 = adam(1, state, four_1, ())
    small_sum = after(small_sum, own_0) + small_z
    small_z = swap_z(small_sum, 2)
    across_0, new_1, small_z = join(across_0, new_1, small_z)
    four_0 = share_core(jnp.stack([own_0, across_0]), place_parts)
    small_sum = small_sum + small_z
    new_0 = adam(0, state, four_0, tuple(new_1))
    size = small_master.shape[1]
    small_own = lax.dynamic_slice_in_dim(small_sum, lax.axis_index("fsdp") * size, size, 1)
    small_new = adam_update(small_master, small_first, small_second, small_own, SMALL_RATE)
    return (
        (content_out, query_out, content_grad, query_grad)
        + tuple(new_0)
        + small_new
    )


def solution(mesh):
    placed = (
        P(("dp", "fsdp"), None),
        P(("dp", "fsdp"), None),
        P(("dp", "fsdp")),
        P(("dp", "fsdp")),
        P(("dp", "fsdp"), None),
        P(("dp", "fsdp"), None),
        P(None, None, "fsdp", None),
        P(None, None, "fsdp", None),
        P(None, None, "fsdp", None),
        P(None, "fsdp", None),
        P(None, "fsdp", None),
        P(None, "fsdp", None),
        P(None, "fsdp", None),
        P(None, "fsdp", None),
        P(None, "fsdp", None),
        P(None, "fsdp"),
        P(None, "fsdp"),
        P(None, "fsdp"),
    )
    fast = tuple(mesh.shape.values()) == (4, 8)
    return jax.shard_map(
        per_device_fast if fast else per_device,
        mesh=mesh,
        in_specs=placed,
        out_specs=(
            P(("dp", "fsdp"), None),
            P(("dp", "fsdp"), None),
            P(("dp", "fsdp"), None),
            P(("dp", "fsdp"), None),
            P(None, None, "fsdp", None),
            P(None, None, "fsdp", None),
            P(None, None, "fsdp", None),
            P(None, "fsdp", None),
            P(None, "fsdp", None),
            P(None, "fsdp", None),
            P(None, "fsdp", None),
            P(None, "fsdp", None),
            P(None, "fsdp", None),
            P(None, "fsdp"),
            P(None, "fsdp"),
            P(None, "fsdp"),
        ),
        check_vma=False,
    )
```

```python
from functools import partial

import jax
import jax.numpy as jnp
from jax import lax
from jax.experimental import pallas as pl
from jax.experimental.pallas import tpu as pltpu
from jax.sharding import PartitionSpec as P

D = 768
H = 12
DH = 64
FF = 3072
LEN = 512
NB = 32
LAYERS = 2
STEP = 10


NORM_EPS = 1e-05
MASKED = -1000000000.0
BETA_ONE = 0.9
BETA_TWO = 0.999
ATTENTION_RATE = 0.1
FEED_RATE = 0.02
SMALL_RATE = 0.4
WEIGHT_DECAY = 0.01
ADAM_EPS = 1e-08
SCORE_SCALE = 0.125


def layer_norm(values, gain, shift):
    centre = values - jnp.mean(values, axis=-1, keepdims=True)
    spread = jnp.mean(centre * centre, axis=-1, keepdims=True)
    return centre * lax.rsqrt(spread + NORM_EPS) * gain + shift


def unpack(vectors):
    pieces = [vectors[piece_index * D : (piece_index + 1) * D] for piece_index in range(8)]
    hidden_bias = vectors[8 * D : 8 * D + FF]
    bias_table = vectors[8 * D + FF :].reshape(H, NB)
    return (pieces, hidden_bias, bias_table)


def bucket_ids():
    position = jnp.arange(LEN, dtype=jnp.int32)
    offset = position[None, :] - position[:, None]
    distance = jnp.abs(offset)
    far_bucket = jnp.full(distance.shape, 8, jnp.int32)
    for exponent in range(1, 8):
        far_bucket = far_bucket + (distance * distance >= 64 * 2**exponent).astype(jnp.int32)
    near_or_far = jnp.where(distance < 8, distance, far_bucket)
    return near_or_far + NB // 2 * (offset > 0).astype(jnp.int32)


def bucket_onehot():
    return (bucket_ids()[:, :, None] == jnp.arange(NB, dtype=jnp.int32)[None, None, :]).astype(
        jnp.bfloat16
    )


def allowed_pairs(length, pred_flags):
    position = jnp.arange(LEN, dtype=jnp.int32)
    valid_key = (position < length)[None, :]
    row_pos = position[:, None]
    col_pos = position[None, :]
    free_key = (pred_flags == 0)[None, :]
    content_ok = valid_key & (free_key | (pred_flags[:, None] == 1) & (col_pos <= row_pos))
    query_ok = valid_key & (col_pos != row_pos) & (free_key | (col_pos < row_pos))
    return (content_ok, query_ok)


def masked_scores(query_rows, key_rows, position_bias, allowed):
    scores = (
        jnp.einsum("qhd,khd->hqk", query_rows, key_rows, preferred_element_type=jnp.float32)
        * SCORE_SCALE
        + position_bias
    )
    return jnp.where(allowed[None], scores, MASKED)


def table_bias(onehot, table_low):
    return jnp.einsum("qkb,hb->hqk", onehot, table_low, preferred_element_type=jnp.float32)


def attend_slot(onehot, table_low, slot_item):
    query_c, query_q, key_rows, value_rows, length, pred_flags = slot_item
    position_bias = table_bias(onehot, table_low)
    content_ok, query_ok = allowed_pairs(length, pred_flags)
    results = []
    for query_rows, allowed in ((query_c, content_ok), (query_q, query_ok)):
        scores = masked_scores(query_rows, key_rows, position_bias, allowed)
        peak = jnp.max(scores, axis=-1, keepdims=True)
        expos = jnp.exp(scores - peak)
        totals = jnp.sum(expos, axis=-1, keepdims=True)
        probs = (expos / totals).astype(jnp.bfloat16)
        mixed = jnp.einsum(
            "hqk,khd->qhd", probs, value_rows, preferred_element_type=jnp.float32
        ).astype(jnp.bfloat16)
        results.append((mixed, peak[..., 0] + jnp.log(totals[..., 0])))
    return (results[0][0], results[1][0], results[0][1], results[1][1])


def attend_back(onehot, table_low, slot_item):
    (
        query_c,
        query_q,
        key_rows,
        value_rows,
        length,
        pred_flags,
        lse_c,
        lse_q,
        grad_mix_c,
        grad_mix_q,
    ) = slot_item
    position_bias = table_bias(onehot, table_low)
    content_ok, query_ok = allowed_pairs(length, pred_flags)
    grad_keys = jnp.zeros(key_rows.shape, jnp.float32)
    grad_values = jnp.zeros(value_rows.shape, jnp.float32)
    grad_table = jnp.zeros((H, NB), jnp.float32)
    grads_query = []
    for query_rows, allowed, log_total, grad_mix in (
        (query_c, content_ok, lse_c, grad_mix_c),
        (query_q, query_ok, lse_q, grad_mix_q),
    ):
        scores = masked_scores(query_rows, key_rows, position_bias, allowed)
        probs = jnp.exp(scores - log_total[..., None])
        grad_values = grad_values + jnp.einsum(
            "hqk,qhd->khd", probs.astype(jnp.bfloat16), grad_mix, preferred_element_type=jnp.float32
        )
        grad_probs = jnp.einsum(
            "qhd,khd->hqk", grad_mix, value_rows, preferred_element_type=jnp.float32
        )
        grad_scores = probs * (grad_probs - jnp.sum(probs * grad_probs, axis=-1, keepdims=True))
        grad_scores = jnp.where(allowed[None], grad_scores, 0.0).astype(jnp.bfloat16)
        grad_table = grad_table + jnp.einsum(
            "hqk,qkb->hb", grad_scores, onehot, preferred_element_type=jnp.float32
        )
        grads_query.append(
            jnp.einsum("hqk,khd->qhd", grad_scores, key_rows, preferred_element_type=jnp.float32)
            * SCORE_SCALE
        )
        grad_keys = (
            grad_keys
            + jnp.einsum(
                "hqk,qhd->khd", grad_scores, query_rows, preferred_element_type=jnp.float32
            )
            * SCORE_SCALE
        )
    return (grads_query[0], grads_query[1], grad_keys, grad_values, grad_table)


def to_heads(values):
    return values.reshape(-1, LEN, H, DH)


AXES = ("dp", "fsdp")
GRID = (2, 2, 4, 2)
ROWS = 96


def places():
    return [
        (x, c, z, y) for x in range(2) for c in range(2) for z in range(4) for y in range(2)
    ]


def flat(x, c, z, y):
    return ((x * 2 + c) * 4 + z) * 2 + y


def move(value, shift):
    pairs = [(flat(*place), flat(*shift(*place))) for place in places()]
    return lax.ppermute(value, AXES, pairs)


def swap_core(value):
    return move(value, lambda x, c, z, y: (x, 1 - c, z, y))


def swap_x(value):
    return move(value, lambda x, c, z, y: (1 - x, c, z, y))


def swap_y(value):
    return move(value, lambda x, c, z, y: (x, c, z, 1 - y))


def swap_z(value, apart):
    return move(value, lambda x, c, z, y: (x, c, z ^ apart, y))


def my_place():
    dp = lax.axis_index("dp")
    fsdp = lax.axis_index("fsdp")
    return (dp // 2, dp % 2, fsdp // 2, fsdp % 2)


def dot_nn(left, right):
    return jnp.dot(left, right, preferred_element_type=jnp.float32)


def dot_nt(left, right):
    return lax.dot_general(
        left, right, (((1,), (1,)), ((), ())), preferred_element_type=jnp.float32
    )


def dot_tn(left, right):
    return lax.dot_general(
        left, right, (((0,), (0,)), ((), ())), preferred_element_type=jnp.float32
    )


ANY_SPEC = pl.BlockSpec(memory_space=pl.ANY)
VMEM_SPEC = pl.BlockSpec(memory_space=pltpu.VMEM)
SMEM_SPEC = pl.BlockSpec(memory_space=pltpu.SMEM)
TALL = 2 * LEN
HALF = 256
PARAMS = pltpu.CompilerParams(vmem_limit_bytes=60 * 1024 * 1024)


def norm_parts(values):
    centre = values - jnp.mean(values, axis=-1, keepdims=True)
    spread = jnp.mean(centre * centre, axis=-1, keepdims=True)
    scale = lax.rsqrt(spread + NORM_EPS)
    return (centre * scale, scale)


def norm_back(unit, scale, grad, gain):
    scaled = grad * gain
    return scale * (
        scaled
        - jnp.mean(scaled, axis=-1, keepdims=True)
        - unit * jnp.mean(scaled * unit, axis=-1, keepdims=True)
    )


def start_fetch(kinds, plan, place_ref, refs, targets, sems):
    x, c, z, y = (place_ref[index] for index in range(4))
    mine = z * 2 + y
    copies = []

    def start(source, target):
        copy = pltpu.make_async_copy(source, target, sems.at[len(copies)])
        copy.start()
        copies.append(copy)

    for member, kind in enumerate(kinds):
        target = targets[member]
        if kind == "attn":
            start(refs[member], target.at[:, pl.ds(pl.multiple_of(mine * ROWS, ROWS), ROWS), :])
        elif kind == "inner":
            for quarter in range(4):
                start(
                    refs[member].at[:, quarter * D : quarter * D + D],
                    target.at[quarter, pl.ds(pl.multiple_of(mine * ROWS, ROWS), ROWS), :],
                )
        else:
            start(refs[member], target.at[z, pl.ds(pl.multiple_of(y * 384, ROWS), 384), :])
    for array, index, dx, dy, dc, dz, member in plan:
        quarter = (x ^ dx) * 2 + (c ^ dc)
        if kinds[member] == "outer":
            lead, row = z ^ dz, (y ^ dy) * 384 + quarter * ROWS
        else:
            lead, row = quarter, ((z ^ dz) * 2 + (y ^ dy)) * ROWS
        start(
            refs[len(kinds) + array].at[index],
            targets[member].at[lead, pl.ds(pl.multiple_of(row, ROWS), ROWS), :],
        )
    return copies


def pack_kernel(outputs, count, *refs):
    sources, targets, sems = refs[:count], refs[count:-1], refs[-1]
    pairs = []
    for target, parts in zip(targets, outputs):
        at = 0
        for source, first, held in parts:
            pairs.append((sources[source].at[first : first + held], target.at[at : at + held]))
            at += held
    finish(issue(pairs, sems))


def pack(outputs, sources):
    total = sum(len(parts) for parts in outputs)
    counts = [sum(held for unused, unused_first, held in parts) for parts in outputs]
    return pl.pallas_call(
        partial(pack_kernel, outputs, len(sources)),
        out_shape=[jax.ShapeDtypeStruct((count, ROWS, D), jnp.bfloat16) for count in counts],
        in_specs=[ANY_SPEC] * len(sources),
        out_specs=[VMEM_SPEC] * len(outputs),
        scratch_shapes=[pltpu.SemaphoreType.DMA((total,))],
        compiler_params=pltpu.CompilerParams(vmem_limit_bytes=16 * 1024 * 1024),
        cost_estimate=pl.CostEstimate(flops=0, bytes_accessed=300000 * sum(counts), transcendentals=0),
        name="pack",
    )(*sources)


def quarter_spans(place_ref, side):
    quarter = (place_ref[0] ^ side) * 2 + place_ref[1]
    return (
        quarter,
        pl.ds(pl.multiple_of(quarter * D, D), D),
        pl.ds(pl.multiple_of(quarter * ROWS, ROWS), ROWS),
    )


def cast_first_kernel(
    place_ref, attn_any, inner_any, outer_any, own_a0, plane_a0, own_f0, hold_ref, sems
):
    index, cols, rows = quarter_spans(place_ref, 0)
    other = quarter_spans(place_ref, 1)[0]
    finish(
        issue(
            (
                (attn_any.at[0, index], hold_ref.at[0]),
                (attn_any.at[0, other], hold_ref.at[1]),
                (inner_any.at[0, :, cols], hold_ref.at[2]),
                (outer_any.at[0, rows, :], hold_ref.at[3]),
            ),
            sems,
        )
    )
    own_a0[...] = hold_ref[0:1].astype(jnp.bfloat16)
    plane_a0[...] = hold_ref[0:2].astype(jnp.bfloat16)
    own_f0[...] = hold_ref[2:4].astype(jnp.bfloat16)


def cast_first(place, attn, inner, outer):
    return pl.pallas_call(
        cast_first_kernel,
        out_shape=[jax.ShapeDtypeStruct((count, ROWS, D), jnp.bfloat16) for count in (1, 2, 2)],
        in_specs=[SMEM_SPEC] + [ANY_SPEC] * 3,
        out_specs=[VMEM_SPEC] * 3,
        scratch_shapes=[pltpu.VMEM((4, ROWS, D), jnp.float32), pltpu.SemaphoreType.DMA((4,))],
        compiler_params=PARAMS,
        cost_estimate=pl.CostEstimate(flops=1000000, bytes_accessed=2000000, transcendentals=0),
        name="cast_first",
    )(place, attn, inner, outer)


def cast_rest_kernel(
    place_ref, attn_ref, inner_ref, outer_ref, attn_0, attn_1, inner_0, inner_1, outer_0, outer_1,
    plane_f0, own_1, oth_1,
):
    for layer, (attn_low, inner_low, outer_low) in enumerate(
        ((attn_0, inner_0, outer_0), (attn_1, inner_1, outer_1))
    ):
        attn_low[...] = attn_ref[layer].astype(jnp.bfloat16)
        inner_low[...] = inner_ref[layer].astype(jnp.bfloat16)
        outer_low[...] = outer_ref[layer].astype(jnp.bfloat16)
    for side, (target, first) in enumerate(((own_1, 0), (oth_1, 0))):
        index, cols, rows = quarter_spans(place_ref, side)
        plane_f0[2 * side] = inner_ref[0, :, cols].astype(jnp.bfloat16)
        plane_f0[2 * side + 1] = outer_ref[0, rows, :].astype(jnp.bfloat16)
        target[0] = attn_ref[1, index].astype(jnp.bfloat16)
        target[1] = inner_ref[1, :, cols].astype(jnp.bfloat16)
        target[2] = outer_ref[1, rows, :].astype(jnp.bfloat16)


def cast_rest(place, attn, inner, outer):
    low = [
        jax.ShapeDtypeStruct(array.shape[1:], jnp.bfloat16)
        for array in (attn, attn, inner, inner, outer, outer)
    ]
    return pl.pallas_call(
        cast_rest_kernel,
        out_shape=low
        + [jax.ShapeDtypeStruct((count, ROWS, D), jnp.bfloat16) for count in (4, 3, 3)],
        in_specs=[SMEM_SPEC] + [VMEM_SPEC] * 3,
        out_specs=[VMEM_SPEC] * 9,
        compiler_params=PARAMS,
        cost_estimate=pl.CostEstimate(flops=10000000, bytes_accessed=12000000, transcendentals=0),
        name="cast_rest",
    )(place, attn, inner, outer)


def project_kernel(plan, place_ref, small_ref, low_any, *refs):
    pieces = refs[:-14]
    (
        q_out, k_out, v_out, w_out, low_ref, q_ref, k_ref, v_ref, w_ref,
        sems, load_sem, keep_sem, store_sems, unused,
    ) = refs[-14:]
    load = pltpu.make_async_copy(low_any, low_ref, load_sem)
    load.start()
    fetches = start_fetch(("attn",), plan, place_ref, pieces, (w_ref,), sems)
    load.wait()
    for copy in fetches:
        copy.wait()
    keep = pltpu.make_async_copy(w_ref, w_out, keep_sem)
    keep.start()
    bias_q = small_ref[0:1, :]
    bias_v = small_ref[1:2, :]
    stores = []

    def store(source, target):
        copy = pltpu.make_async_copy(source, target, store_sems.at[len(stores)])
        copy.start()
        stores.append(copy)

    for row in range(0, TALL, HALF):
        span = slice(row, row + HALF)
        rows = low_ref[span, :]
        q_ref[span, :] = (dot_nn(rows, w_ref[0]) + bias_q).astype(jnp.bfloat16)
        if row < LEN:
            k_ref[span, :] = dot_nn(rows, w_ref[1]).astype(jnp.bfloat16)
            v_ref[span, :] = (dot_nn(rows, w_ref[2]) + bias_v).astype(jnp.bfloat16)
        if row == LEN - HALF:
            store(k_ref, k_out)
            store(v_ref, v_out)
            store(q_ref.at[:LEN, :], q_out.at[:LEN, :])
    store(q_ref.at[LEN:, :], q_out.at[LEN:, :])
    for copy in stores:
        copy.wait()
    keep.wait()


def project(place, low, small, group):
    plan, pieces = group
    return pl.pallas_call(
        partial(project_kernel, plan),
        out_shape=[
            jax.ShapeDtypeStruct((TALL, D), jnp.bfloat16),
            jax.ShapeDtypeStruct((LEN, D), jnp.bfloat16),
            jax.ShapeDtypeStruct((LEN, D), jnp.bfloat16),
            jax.ShapeDtypeStruct((4, D, D), jnp.bfloat16),
        ],
        in_specs=[SMEM_SPEC, VMEM_SPEC, ANY_SPEC] + [ANY_SPEC] * len(pieces),
        out_specs=[ANY_SPEC] * 4,
        scratch_shapes=[
            pltpu.VMEM((TALL, D), jnp.bfloat16),
            pltpu.VMEM((TALL, D), jnp.bfloat16),
            pltpu.VMEM((LEN, D), jnp.bfloat16),
            pltpu.VMEM((LEN, D), jnp.bfloat16),
            pltpu.VMEM((4, D, D), jnp.bfloat16),
            pltpu.SemaphoreType.DMA((32,)),
            pltpu.SemaphoreType.DMA,
            pltpu.SemaphoreType.DMA,
            pltpu.SemaphoreType.DMA((4,)),
            pltpu.SemaphoreType.DMA,
        ],
        compiler_params=PARAMS,
        cost_estimate=pl.CostEstimate(flops=2 * 2048 * D * D, bytes_accessed=16000000, transcendentals=0),
        name="project",
    )(place, small, low, *pieces)


def build_masks(length, row_flags, col_flags, mask_ref, alive_ref):
    flags = row_flags[...]

    def body(step, carry):
        start = pl.multiple_of(step * 64, 64)
        key = lax.broadcasted_iota(jnp.int32, (64, LEN), 0) + start
        query = lax.broadcasted_iota(jnp.int32, (64, LEN), 1)
        valid = key < length
        free = jnp.broadcast_to(col_flags[pl.ds(start, 64), :], (64, LEN)) == 0.0
        marked = jnp.broadcast_to(flags, (64, LEN)) == 1.0
        content_ok = valid & (free | (marked & (key <= query)))
        query_ok = valid & (key != query) & (free | (key < query))
        mask_ref[pl.ds(start, 64), :LEN] = content_ok.astype(jnp.float32)
        mask_ref[pl.ds(start, 64), LEN:] = query_ok.astype(jnp.float32)
        return carry

    lax.fori_loop(0, 8, body, 0)
    alive_ref[...] = jnp.max(mask_ref[...], axis=0, keepdims=True)


def build_tiles(t_row, tile_ref):
    spread = jnp.broadcast_to(t_row, (128, 512))
    rolled = pltpu.roll(spread, 0, 1, stride=1, stride_axis=0)
    tile_ref[...] = rolled[:, :384]


def position_bias(tile_ref, far_ref, head, query_block, key_block):
    apart = query_block - key_block
    if apart >= 2:
        return far_ref[head, 0]
    if apart <= -2:
        return far_ref[head, 1]
    return tile_ref[:, 128 * (apart + 1) : 128 * (apart + 2)]


def head_lanes(shape, head):
    lane = lax.broadcasted_iota(jnp.int32, shape, 1)
    return (lane >= 64) if head else (lane < 64)


def mix_kernel(
    length_ref, far_ref, q_ref, k_ref, v_ref, row_flags, col_flags, t_ref,
    a_ref, p_ref, inverse_ref, dead_ref, mask_ref, alive_ref, tile_ref, o_ref,
):
    pair = pl.program_id(0)

    @pl.when(pair == 0)
    def _():
        build_masks(length_ref[0], row_flags, col_flags, mask_ref, alive_ref)
        dead_ref[...] = (1.0 - alive_ref[...]) * (1.0 / LEN)

    keys = k_ref[...].astype(jnp.float32) * SCORE_SCALE
    values_t = v_ref[...].astype(jnp.float32).T.astype(jnp.bfloat16)
    keys_own = [
        jnp.where(head_lanes(keys.shape, head), keys, 0.0).astype(jnp.bfloat16) for head in range(2)
    ]
    for head in range(2):
        build_tiles(t_ref[head], tile_ref.at[head])
    work = [(head, chunk) for head in range(2) for chunk in range(4)]

    def score(head, chunk):
        return dot_nt(keys_own[head], q_ref[chunk * HALF : chunk * HALF + HALF, :])

    def mixture(head, chunk):
        span = slice(chunk * HALF, chunk * HALF + HALF)
        own = slice(8 + head * 64, 8 + head * 64 + 64)
        mixed = dot_nn(values_t[head * 64 : head * 64 + 64, :], p_ref[head, :, span])
        o_ref[own, span] = mixed * o_ref[head : head + 1, span]

    following = score(*work[0])
    for index, (head, chunk) in enumerate(work):
        scores = following
        if index + 1 < len(work):
            following = score(*work[index + 1])
        at = chunk * HALF
        for side in range(2):
            lanes = slice(at + side * 128, at + side * 128 + 128)
            blocks = []
            peak = None
            for key_block in range(4):
                rows = slice(key_block * 128, key_block * 128 + 128)
                block = scores[rows, side * 128 : side * 128 + 128] + position_bias(
                    tile_ref.at[head], far_ref, pair * 2 + head, (chunk % 2) * 2 + side, key_block
                )
                block = jnp.where(mask_ref[rows, lanes] > 0.0, block, MASKED)
                blocks.append(block)
                high = jnp.max(block, axis=0, keepdims=True)
                peak = high if peak is None else jnp.maximum(peak, high)
            total = None
            for key_block in range(4):
                rows = slice(key_block * 128, key_block * 128 + 128)
                expo = jnp.exp(blocks[key_block] - peak)
                part = jnp.sum(expo, axis=0, keepdims=True)
                total = part if total is None else total + part
                p_ref[head, rows, lanes] = expo.astype(jnp.bfloat16)
            inverse = 1.0 / total
            inverse_ref[head, :, lanes] = inverse * alive_ref[:, lanes]
            o_ref[head : head + 1, lanes] = inverse
        if index:
            mixture(*work[index - 1])
    mixture(*work[-1])
    a_ref[...] = o_ref[8:, :].T.astype(jnp.bfloat16)


def mix(length, far, tvec, q, k, v, row_flags, col_flags):
    tall = pl.BlockSpec((TALL, 128), lambda p: (0, p))
    short = pl.BlockSpec((LEN, 128), lambda p: (0, p))
    return pl.pallas_call(
        mix_kernel,
        grid=(H // 2,),
        out_shape=[
            jax.ShapeDtypeStruct((TALL, D), jnp.bfloat16),
            jax.ShapeDtypeStruct((H, LEN, TALL), jnp.bfloat16),
            jax.ShapeDtypeStruct((H, 1, TALL), jnp.float32),
            jax.ShapeDtypeStruct((1, TALL), jnp.float32),
        ],
        in_specs=[
            SMEM_SPEC, SMEM_SPEC, tall, short, short,
            pl.BlockSpec((1, LEN), lambda p: (0, 0)),
            pl.BlockSpec((LEN, 1), lambda p: (0, 0)),
            pl.BlockSpec((2, 1, 512), lambda p: (p, 0, 0)),
        ],
        out_specs=[
            tall,
            pl.BlockSpec((2, LEN, TALL), lambda p: (p, 0, 0)),
            pl.BlockSpec((2, 1, TALL), lambda p: (p, 0, 0)),
            pl.BlockSpec((1, TALL), lambda p: (0, 0)),
        ],
        scratch_shapes=[
            pltpu.VMEM((LEN, TALL), jnp.float32),
            pltpu.VMEM((1, TALL), jnp.float32),
            pltpu.VMEM((2, 128, 384), jnp.float32),
            pltpu.VMEM((136, TALL), jnp.float32),
        ],
        compiler_params=PARAMS,
        cost_estimate=pl.CostEstimate(flops=6500000000, bytes_accessed=8000000, transcendentals=6300000),
        name="mix",
    )(length, far, q, k, v, row_flags, col_flags, tvec)


def mix_back_kernel(q_ref, k_ref, v_ref, da_ref, a_ref, p_ref, inverse_ref, dead_ref, *refs):
    (
        dq_ref, dk_ref, dv_ref, table_ref, s_ref, near_ref, da_t, low_t, q_t, g_ref,
    ) = refs[-10:]
    keys = k_ref[...].astype(jnp.float32) * SCORE_SCALE
    keys_t = keys.T.astype(jnp.bfloat16)
    q_t[...] = q_ref[...].astype(jnp.float32).T.astype(jnp.bfloat16)
    da_t[...] = da_ref[...].astype(jnp.float32).T
    product = a_ref[...].astype(jnp.float32).T * da_t[...]
    values = v_ref[...].astype(jnp.float32)
    near_ref[...] = jnp.zeros(near_ref.shape, jnp.float32)
    turn = (
        lax.broadcasted_iota(jnp.int32, (128, 128), 0)
        + lax.broadcasted_iota(jnp.int32, (128, 128), 1)
        == 127
    ).astype(jnp.float32)
    deltas = []
    for head in range(2):
        rows = slice(head * 64, head * 64 + 64)
        inverse = inverse_ref[head]
        deltas.append(jnp.sum(product[rows, :], axis=0, keepdims=True) * inverse)
        low_t[rows, :] = (da_t[rows, :] * inverse).astype(jnp.bfloat16)
    for head in range(2):
        own = slice(head * 64, head * 64 + 64)
        values_own = jnp.where(head_lanes(values.shape, head), values, 0.0).astype(jnp.bfloat16)
        delta = deltas[head]
        far_low = jnp.zeros((8, 128), jnp.float32)
        far_high = jnp.zeros((8, 128), jnp.float32)
        for chunk in range(4):
            at = chunk * HALF
            pulls = dot_nn(values_own, low_t[:, at : at + HALF])
            for side in range(2):
                lanes = slice(at + side * 128, at + side * 128 + 128)
                shift = delta[:, lanes]
                query_block = (chunk % 2) * 2 + side
                for key_block in range(4):
                    rows = slice(key_block * 128, key_block * 128 + 128)
                    cols = slice(side * 128, side * 128 + 128)
                    grad = p_ref[head, rows, lanes].astype(jnp.float32) * (
                        pulls[rows, cols] - shift
                    )
                    s_ref[head, rows, lanes] = grad.astype(jnp.bfloat16)
                    apart = query_block - key_block
                    if apart >= 2:
                        far_low = far_low + jnp.sum(grad.reshape(16, 8, 128), axis=0)
                    elif apart <= -2:
                        far_high = far_high + jnp.sum(grad.reshape(16, 8, 128), axis=0)
                    else:
                        near_ref[head, :, 128 * (apart + 1) : 128 * (apart + 2)] += grad
        g_ref[own, :LEN] = dot_nt(low_t[own, :], p_ref[head])
        g_ref[own, LEN:] = dot_nt(q_t[own, :], s_ref[head]) * SCORE_SCALE
        da_t[own, :] = dot_nn(keys_t[own, :], s_ref[head])
        turned = jnp.dot(
            turn, near_ref[head], precision=lax.Precision.HIGHEST, preferred_element_type=jnp.float32
        )
        aligned = pltpu.roll(turned, 0, 1, stride=1, stride_axis=0)
        table_ref[head, :, :512] = jnp.sum(aligned, axis=0, keepdims=True)
        table_ref[head, :, 512:640] = jnp.sum(far_low, axis=0, keepdims=True)
        table_ref[head, :, 640:] = jnp.sum(far_high, axis=0, keepdims=True)
    uniform = dot_nn(dead_ref[...].astype(jnp.bfloat16), da_ref[...])
    dv_ref[...] = (g_ref[:, :LEN].T + uniform).astype(jnp.bfloat16)
    dk_ref[...] = g_ref[:, LEN:].T.astype(jnp.bfloat16)
    dq_ref[...] = da_t[...].T.astype(jnp.bfloat16)


def mix_back(first, q, k, v, da, a, p, inverse, dead, held=()):
    tall = pl.BlockSpec((TALL, 128), lambda i: (0, i + first))
    short = pl.BlockSpec((LEN, 128), lambda i: (0, i + first))
    return pl.pallas_call(
        mix_back_kernel,
        grid=(H // 4,),
        out_shape=[
            jax.ShapeDtypeStruct((TALL, D), jnp.bfloat16),
            jax.ShapeDtypeStruct((LEN, D), jnp.bfloat16),
            jax.ShapeDtypeStruct((LEN, D), jnp.bfloat16),
            jax.ShapeDtypeStruct((H // 2, 1, 768), jnp.float32),
        ],
        in_specs=[
            tall, short, short, tall, tall,
            pl.BlockSpec((2, LEN, TALL), lambda i: (i + first, 0, 0)),
            pl.BlockSpec((2, 1, TALL), lambda i: (i + first, 0, 0)),
            pl.BlockSpec((1, TALL), lambda i: (0, 0)),
        ]
        + [ANY_SPEC] * len(held),
        out_specs=[tall, short, short, pl.BlockSpec((2, 1, 768), lambda i: (i, 0, 0))],
        input_output_aliases={8 + index: index for index in range(len(held))},
        scratch_shapes=[
            pltpu.VMEM((2, LEN, TALL), jnp.bfloat16),
            pltpu.VMEM((2, 128, 512), jnp.float32),
            pltpu.VMEM((128, TALL), jnp.float32),
            pltpu.VMEM((128, TALL), jnp.bfloat16),
            pltpu.VMEM((128, TALL), jnp.bfloat16),
            pltpu.VMEM((128, TALL), jnp.float32),
        ],
        compiler_params=PARAMS,
        cost_estimate=pl.CostEstimate(flops=8000000000, bytes_accessed=16000000, transcendentals=0),
        name="mix_back",
    )(q, k, v, da, a, p, inverse, dead, *held)


GELU_SCALE = 0.7978845608028654
GELU_CUBE = 0.044715


def feed_rows(rows, small_ref, hidden_bias_ref, resid, normed_ref, pre_ref, inner_ref, outer_ref):
    unit, scale = norm_parts(resid)
    normed = unit * small_ref[3:4, :] + small_ref[4:5, :]
    low = normed.astype(jnp.bfloat16)
    normed_ref[rows, :] = low
    total = normed + small_ref[5:6, :]
    for chunk in range(4):
        pre = dot_nn(low, inner_ref[chunk]) + hidden_bias_ref[:, chunk * D : chunk * D + D]
        pre_ref[chunk, rows, :] = pre.astype(jnp.bfloat16)
        tanh = jnp.tanh(GELU_SCALE * (pre + GELU_CUBE * (pre * pre * pre)))
        active = (pre * (0.5 + 0.5 * tanh)).astype(jnp.bfloat16)
        total = total + dot_nn(active, outer_ref[chunk])
    return total


def norm_two_back(unit, scale, grad, small_ref, sums):
    back = norm_back(unit, scale, grad, small_ref[6:7, :])
    low = back.astype(jnp.bfloat16)
    parts = (low.astype(jnp.float32), grad * unit, grad)
    return back, low, [
        total + jnp.sum(part, axis=0, keepdims=True) for total, part in zip(sums, parts)
    ]


def issue(pairs, sems, first=0):
    copies = [
        pltpu.make_async_copy(source, target, sems.at[first + index])
        for index, (source, target) in enumerate(pairs)
    ]
    for copy in copies:
        copy.start()
    return copies


def finish(copies):
    for copy in copies:
        copy.wait()


def storer(sems):
    copies = []

    def store(source, target):
        copy = pltpu.make_async_copy(source, target, sems.at[len(copies)])
        copy.start()
        copies.append(copy)

    return store, copies


def feed_kernel(
    plan, place_ref, small_ref, hidden_bias_ref, mix_any, hidden_any, attn_any, *refs
):
    (
        resid_out, pre_out, normed_out, low_out, summed_out,
        mix_ref, hidden_ref, wo_ref, inner_ref, outer_ref, resid_ref, total_ref, normed_ref,
        pre_ref, low_ref, sems, load_sems, store_sems,
    ) = refs[-18:]
    finish(
        issue(
            ((mix_any, mix_ref), (attn_any.at[3], wo_ref), (hidden_any, hidden_ref)), load_sems
        )
    )
    fetches = start_fetch(
        ("inner", "outer"), plan, place_ref, refs[:-18], (inner_ref, outer_ref), sems
    )
    for row in range(0, TALL, HALF):
        rows = slice(row, row + HALF)
        resid_ref[rows, :] = (
            hidden_ref[rows, :].astype(jnp.float32)
            + dot_nn(mix_ref[rows, :], wo_ref[...])
            + small_ref[2:3, :]
        )
    finish(fetches)
    store, stores = storer(store_sems)
    store(resid_ref, resid_out)
    for row in range(0, TALL, HALF):
        rows = slice(row, row + HALF)
        total = feed_rows(
            rows, small_ref, hidden_bias_ref, resid_ref[rows, :], normed_ref, pre_ref, inner_ref,
            outer_ref,
        )
        total_ref[rows, :] = total
        store(pre_ref.at[:, rows, :], pre_out.at[:, rows, :])
        store(total_ref.at[rows, :], summed_out.at[rows, :])
        store(normed_ref.at[rows, :], normed_out.at[rows, :])
        unit, scale = norm_parts(total)
        following = unit * small_ref[6:7, :] + small_ref[7:8, :]
        low_ref[rows, :] = following.astype(jnp.bfloat16)
        store(low_ref.at[rows, :], low_out.at[rows, :])
    finish(stores)


def feed(place, small, hidden_bias, mixed, hidden, attn, group):
    plan, pieces = group
    tall = jax.ShapeDtypeStruct((TALL, D), jnp.float32)
    tall_low = jax.ShapeDtypeStruct((TALL, D), jnp.bfloat16)
    return pl.pallas_call(
        partial(feed_kernel, plan),
        out_shape=[
            tall, jax.ShapeDtypeStruct((4, TALL, D), jnp.bfloat16), tall_low, tall_low, tall
        ],
        in_specs=[SMEM_SPEC, VMEM_SPEC, VMEM_SPEC] + [ANY_SPEC] * (3 + len(pieces)),
        out_specs=[ANY_SPEC] * 5,
        scratch_shapes=[
            pltpu.VMEM((TALL, D), jnp.bfloat16),
            pltpu.VMEM((TALL, D), jnp.bfloat16),
            pltpu.VMEM((D, D), jnp.bfloat16),
            pltpu.VMEM((4, D, D), jnp.bfloat16),
            pltpu.VMEM((4, D, D), jnp.bfloat16),
            pltpu.VMEM((TALL, D), jnp.float32),
            pltpu.VMEM((TALL, D), jnp.float32),
            pltpu.VMEM((TALL, D), jnp.bfloat16),
            pltpu.VMEM((4, TALL, D), jnp.bfloat16),
            pltpu.VMEM((TALL, D), jnp.bfloat16),
            pltpu.SemaphoreType.DMA((64,)),
            pltpu.SemaphoreType.DMA((3,)),
            pltpu.SemaphoreType.DMA((17,)),
        ],
        compiler_params=PARAMS,
        cost_estimate=pl.CostEstimate(flops=2 * TALL * D * (D + 2 * FF), bytes_accessed=30000000, transcendentals=3000000),
        name="feed",
    )(place, small, hidden_bias, mixed, hidden, attn, *pieces)


def back_steps(
    place_ref, small_ref, before, store, outs, vec_ref, dhidden_ref, branch_ref, total_ref,
    normed_ref, resid_ref, pre_ref, mix_ref, wo_ref, inner_ref, outer_ref, active_ref, dpre_ref,
    dinner_ref, douter_ref, dwo_ref,
):
    dresid_out, dmix_out, dwo_out, keep_out, send_out = outs
    x, c, z, y = (place_ref[index] for index in range(4))
    order = [(1 - step // 2, step % 2) for step in range(4)]
    chunks = [side * 2 + (c ^ apart) for apart, side in order]
    sums = [jnp.zeros((1, D), jnp.float32)] * 3
    for step in range(4):
        apart, side = order[step]
        chunk = chunks[step]
        before(step)
        bias_grad = jnp.zeros((1, D), jnp.float32)
        for row in range(0, TALL, HALF):
            rows = slice(row, row + HALF)
            pull = dot_nt(branch_ref[rows, :], outer_ref[chunk])
            pre = pre_ref[chunk, rows, :].astype(jnp.float32)
            square = pre * pre
            tanh = jnp.tanh(GELU_SCALE * pre * (1.0 + GELU_CUBE * square))
            half = 0.5 + 0.5 * tanh
            active_ref[rows, :] = (pre * half).astype(jnp.bfloat16)
            slope = half + (0.5 * GELU_SCALE) * pre * (1.0 - tanh * tanh) * (
                1.0 + (3.0 * GELU_CUBE) * square
            )
            dpre = (pull * slope).astype(jnp.bfloat16)
            dpre_ref[rows, :] = dpre
            bias_grad += jnp.sum(dpre.astype(jnp.float32), axis=0, keepdims=True)
            grad = total_ref[rows, :] + dot_nt(dpre, inner_ref[chunk])
            if step < 3:
                total_ref[rows, :] = grad
            else:
                unit, scale = norm_parts(resid_ref[rows, :])
                back = norm_back(unit, scale, grad, small_ref[3:4, :])
                resid_ref[rows, :] = back
                low = back.astype(jnp.bfloat16)
                pre_ref[chunks[0], rows, :] = low
                pre_ref[chunks[1], rows, :] = dot_nt(low, wo_ref[...]).astype(jnp.bfloat16)
                parts = (low.astype(jnp.float32), grad * unit, grad)
                sums = [
                    value + jnp.sum(part, axis=0, keepdims=True)
                    for value, part in zip(sums, parts)
                ]
        dhidden_ref[chunk] = bias_grad
        if step == 3:
            store(resid_ref, dresid_out)
            store(pre_ref.at[chunks[1]], dmix_out)
        douter_ref[step] = (
            dot_tn(active_ref[...], branch_ref[...]).astype(jnp.bfloat16).reshape(2, 2, 2, ROWS, D)
        )
        for y_block in range(2):
            for x_block in range(2):
                spot = (y_block ^ y, x_block ^ x, chunk, 1)
                store(douter_ref.at[step, y_block, x_block, c], keep_out.at[spot])
                store(douter_ref.at[step, y_block, x_block, 1 - c], send_out.at[spot])
        dinner_ref[step] = (
            dot_tn(normed_ref[...], dpre_ref[...]).astype(jnp.bfloat16).reshape(4, 2, ROWS, D)
        )
        target = send_out if apart else keep_out
        for y_block in range(2):
            store(dinner_ref.at[step, :, y_block], target.at[y_block ^ y, side ^ x, :, 0])
    dwo_ref[...] = dot_tn(mix_ref[...], pre_ref[chunks[0]]).astype(jnp.bfloat16)
    store(dwo_ref, dwo_out)
    for index, value in enumerate(sums):
        vec_ref[index : index + 1, :] = value


BACK_SHAPES = [
    jax.ShapeDtypeStruct((TALL, D), jnp.float32),
    jax.ShapeDtypeStruct((TALL, D), jnp.bfloat16),
    jax.ShapeDtypeStruct((D, D), jnp.bfloat16),
    jax.ShapeDtypeStruct((2, 2, 4, 2, ROWS, D), jnp.bfloat16),
    jax.ShapeDtypeStruct((2, 2, 4, 2, ROWS, D), jnp.bfloat16),
    jax.ShapeDtypeStruct((6, D), jnp.float32),
    jax.ShapeDtypeStruct((4, 1, D), jnp.float32),
]
BACK_SCRATCH = [
    pltpu.VMEM((TALL, D), jnp.bfloat16),
    pltpu.VMEM((TALL, D), jnp.float32),
    pltpu.VMEM((TALL, D), jnp.bfloat16),
    pltpu.VMEM((TALL, D), jnp.float32),
    pltpu.VMEM((4, TALL, D), jnp.bfloat16),
    pltpu.VMEM((TALL, D), jnp.bfloat16),
    pltpu.VMEM((D, D), jnp.bfloat16),
    pltpu.VMEM((4, D, D), jnp.bfloat16),
    pltpu.VMEM((4, D, D), jnp.bfloat16),
    pltpu.VMEM((TALL, D), jnp.bfloat16),
    pltpu.VMEM((TALL, D), jnp.bfloat16),
    pltpu.VMEM((4, 4, 2, ROWS, D), jnp.bfloat16),
    pltpu.VMEM((4, 2, 2, 2, ROWS, D), jnp.bfloat16),
    pltpu.VMEM((D, D), jnp.bfloat16),
    pltpu.SemaphoreType.DMA((64,)),
    pltpu.SemaphoreType.DMA((16,)),
    pltpu.SemaphoreType.DMA((48,)),
]


def turn_kernel(
    plan, place_ref, length_ref, small_ref, below_ref, hidden_bias_ref, mix_any, summed_any,
    attn_any, cot_c_any, cot_q_any, *refs
):
    content_out, query_out = refs[-27:-25]
    outs = refs[-25:-20]
    vec_ref, dhidden_ref = refs[-20:-18]
    low_ref = refs[-18]
    (
        branch_ref, total_ref, normed_ref, resid_ref, pre_ref, mix_ref, wo_ref, inner_ref,
        outer_ref, active_ref, dpre_ref, dinner_ref, douter_ref, dwo_ref,
        sems, load_sems, store_sems,
    ) = refs[-17:]
    store, stores = storer(store_sems)
    finish(
        issue(
            ((mix_any, mix_ref), (attn_any.at[3], wo_ref), (summed_any, resid_ref)), load_sems
        )
    )
    fetches = start_fetch(
        ("inner", "outer"), plan, place_ref, refs[:-27], (inner_ref, outer_ref), sems
    )
    fetches += issue(
        ((cot_c_any, low_ref.at[:LEN, :]), (cot_q_any, low_ref.at[LEN:, :])), load_sems, 3
    )
    for row in range(0, TALL, HALF):
        rows = slice(row, row + HALF)
        unit, scale = norm_parts(resid_ref[rows, :])
        resid_ref[rows, :] = (
            unit * below_ref[6:7, :]
            + below_ref[7:8, :]
            + dot_nn(mix_ref[rows, :], wo_ref[...])
            + small_ref[2:3, :]
        )
    finish(fetches)
    sums = [jnp.zeros((1, D), jnp.float32)] * 3
    for row in range(0, TALL, HALF):
        rows = slice(row, row + HALF)
        total = feed_rows(
            rows, small_ref, hidden_bias_ref, resid_ref[rows, :], normed_ref, pre_ref, inner_ref,
            outer_ref,
        )
        unit, scale = norm_parts(total)
        position = lax.broadcasted_iota(jnp.int32, (HALF, 1), 0) + row % LEN
        valid = (position < length_ref[0]).astype(jnp.float32)
        grad = low_ref[rows, :].astype(jnp.float32) * valid
        low_ref[rows, :] = (unit * small_ref[6:7, :] + small_ref[7:8, :]).astype(jnp.bfloat16)
        total_ref[rows, :], branch_ref[rows, :], sums = norm_two_back(
            unit, scale, grad, small_ref, sums
        )
    store(low_ref.at[:LEN, :], content_out)
    store(low_ref.at[LEN:, :], query_out)
    for index, value in enumerate(sums):
        vec_ref[3 + index : 4 + index, :] = value
    back_steps(
        place_ref, small_ref, lambda step: None, store, outs, vec_ref, dhidden_ref, branch_ref,
        total_ref, normed_ref, resid_ref, pre_ref, mix_ref, wo_ref, inner_ref, outer_ref,
        active_ref, dpre_ref, dinner_ref, douter_ref, dwo_ref,
    )
    finish(stores)


def turn(place, length, small, below, hidden_bias, mixed, summed, attn, cots, group):
    plan, pieces = group
    half_low = jax.ShapeDtypeStruct((LEN, D), jnp.bfloat16)
    return pl.pallas_call(
        partial(turn_kernel, plan),
        out_shape=[half_low, half_low] + BACK_SHAPES,
        in_specs=[SMEM_SPEC] * 2 + [VMEM_SPEC] * 3 + [ANY_SPEC] * (5 + len(pieces)),
        out_specs=[ANY_SPEC] * 7 + [VMEM_SPEC] * 2,
        scratch_shapes=[pltpu.VMEM((TALL, D), jnp.bfloat16)] + BACK_SCRATCH,
        compiler_params=PARAMS,
        cost_estimate=pl.CostEstimate(flops=6 * TALL * D * (D + 2 * FF), bytes_accessed=60000000, transcendentals=6000000),
        name="turn",
    )(place, length, small, below, hidden_bias, mixed, summed, attn, *cots, *pieces)


def down_kernel(
    plan, place_ref, small_ref, dq_any, dk_any, dv_any, w_any, dresid_any, summed_any,
    normed_any, resid_any, pre_any, mix_any, attn_any, *refs
):
    outs = refs[-29:-24]
    vec_ref, dhidden_ref = refs[-24:-22]
    dq_ref, dk_ref, dv_ref, w_ref, summed_ref = refs[-22:-17]
    (
        branch_ref, total_ref, normed_ref, resid_ref, pre_ref, mix_ref, wo_ref, inner_ref,
        outer_ref, active_ref, dpre_ref, dinner_ref, douter_ref, dwo_ref,
        sems, load_sems, store_sems,
    ) = refs[-17:]
    x, c, z, y = (place_ref[index] for index in range(4))
    chunks = [side * 2 + (c ^ apart) for apart in (1, 0) for side in range(2)]
    store, stores = storer(store_sems)
    loads = issue(
        (
            (w_any.at[0], w_ref.at[0]), (dq_any, dq_ref), (dresid_any, total_ref),
            (summed_any, summed_ref), (w_any.at[1:3], w_ref.at[1:3]), (dk_any, dk_ref),
            (dv_any, dv_ref),
        ),
        load_sems,
    )
    finish(loads[:4])
    fetches = start_fetch(
        ("inner", "outer"), plan, place_ref, refs[:-29], (inner_ref, outer_ref), sems
    )
    fetches += issue(((pre_any.at[chunks[0]], pre_ref.at[chunks[0]]),), load_sems, 7)
    sums = [jnp.zeros((1, D), jnp.float32)] * 3
    for index, row in enumerate((LEN, LEN + HALF, 0, HALF)):
        rows = slice(row, row + HALF)
        if index == 2:
            finish(loads[4:])
        total = total_ref[rows, :] + dot_nt(dq_ref[rows, :], w_ref[0])
        if index >= 2:
            total = total + dot_nt(dk_ref[rows, :], w_ref[1]) + dot_nt(dv_ref[rows, :], w_ref[2])
        unit, scale = norm_parts(summed_ref[rows, :])
        total_ref[rows, :], branch_ref[rows, :], sums = norm_two_back(
            unit, scale, total, small_ref, sums
        )
    for index, value in enumerate(sums):
        vec_ref[3 + index : 4 + index, :] = value
    finish(fetches)
    late = []

    def before(step):
        if step == 0:
            late.append(issue(((normed_any, normed_ref),), load_sems, 8))
        else:
            finish(late.pop())
        if step < 3:
            chunk = chunks[step + 1]
            late.insert(0, issue(((pre_any.at[chunk], pre_ref.at[chunk]),), load_sems, 9 + step))
        if step == 0:
            finish(late.pop())
        if step == 2:
            late[0].extend(
                issue(
                    ((resid_any, resid_ref), (mix_any, mix_ref), (attn_any.at[3], wo_ref)),
                    load_sems,
                    12,
                )
            )

    back_steps(
        place_ref, small_ref, before, store, outs, vec_ref, dhidden_ref, branch_ref, total_ref,
        normed_ref, resid_ref, pre_ref, mix_ref, wo_ref, inner_ref, outer_ref, active_ref,
        dpre_ref, dinner_ref, douter_ref, dwo_ref,
    )
    finish(stores)


def down(place, small, dq, dk, dv, w_above, dresid, summed, normed, resid, pre, mixed, attn, group):
    plan, pieces = group
    return pl.pallas_call(
        partial(down_kernel, plan),
        out_shape=BACK_SHAPES,
        in_specs=[SMEM_SPEC, VMEM_SPEC] + [ANY_SPEC] * (11 + len(pieces)),
        out_specs=[ANY_SPEC] * 5 + [VMEM_SPEC] * 2,
        scratch_shapes=[
            pltpu.VMEM((TALL, D), jnp.bfloat16),
            pltpu.VMEM((LEN, D), jnp.bfloat16),
            pltpu.VMEM((LEN, D), jnp.bfloat16),
            pltpu.VMEM((3, D, D), jnp.bfloat16),
            pltpu.VMEM((TALL, D), jnp.float32),
        ]
        + BACK_SCRATCH,
        compiler_params=PARAMS,
        cost_estimate=pl.CostEstimate(flops=5 * TALL * D * (D + 2 * FF), bytes_accessed=60000000, transcendentals=3000000),
        name="down",
    )(place, small, dq, dk, dv, w_above, dresid, summed, normed, resid, pre, mixed, attn, *pieces)


def weight_back_kernel(
    place_ref, low_any, dq_any, dk_any, dv_any, dwo_any, keep_out, send_out, vec_ref,
    low_ref, dq_ref, dk_ref, dv_ref, dwo_ref, grads_ref, load_sems, sems,
):
    x, c, z, y = (place_ref[index] for index in range(4))
    load = [
        pltpu.make_async_copy(source, target, load_sems.at[index])
        for index, (source, target) in enumerate(
            (
                (low_any.at[:LEN, :], low_ref.at[:LEN, :]), (dk_any, dk_ref), (dv_any, dv_ref),
                (low_any.at[LEN:, :], low_ref.at[LEN:, :]), (dq_any, dq_ref), (dwo_any, dwo_ref),
            )
        )
    ]
    for copy in load:
        copy.start()
    load[0].wait()
    load[1].wait()
    grads_ref[1] = (
        dot_tn(low_ref[:LEN, :], dk_ref[...]).astype(jnp.bfloat16).reshape(4, 2, ROWS, D)
    )
    load[2].wait()
    grads_ref[2] = (
        dot_tn(low_ref[:LEN, :], dv_ref[...]).astype(jnp.bfloat16).reshape(4, 2, ROWS, D)
    )
    vec_ref[1:2, :] = jnp.sum(dv_ref[...].astype(jnp.float32), axis=0, keepdims=True)
    for copy in load[3:]:
        copy.wait()
    grads_ref[3] = dwo_ref[...].reshape(4, 2, ROWS, D)
    grads_ref[0] = dot_tn(low_ref[...], dq_ref[...]).astype(jnp.bfloat16).reshape(4, 2, ROWS, D)
    vec_ref[0:1, :] = jnp.sum(dq_ref[...].astype(jnp.float32), axis=0, keepdims=True)
    blocks = []
    for apart, target in ((1, send_out), (0, keep_out)):
        for side in range(2):
            for y_block in range(2):
                copy = pltpu.make_async_copy(
                    grads_ref.at[side * 2 + (c ^ apart), :, y_block],
                    target.at[y_block ^ y, side ^ x, :, 0],
                    sems.at[len(blocks)],
                )
                copy.start()
                blocks.append(copy)
    for block in blocks:
        block.wait()


def weight_back(place, low, dq, dk, dv, dwo):
    blocks = jax.ShapeDtypeStruct((2, 2, 4, 1, ROWS, D), jnp.bfloat16)
    return pl.pallas_call(
        weight_back_kernel,
        out_shape=[blocks, blocks, jax.ShapeDtypeStruct((2, D), jnp.float32)],
        in_specs=[SMEM_SPEC] + [ANY_SPEC] * 5,
        out_specs=[ANY_SPEC] * 2 + [VMEM_SPEC],
        scratch_shapes=[
            pltpu.VMEM((TALL, D), jnp.bfloat16),
            pltpu.VMEM((TALL, D), jnp.bfloat16),
            pltpu.VMEM((LEN, D), jnp.bfloat16),
            pltpu.VMEM((LEN, D), jnp.bfloat16),
            pltpu.VMEM((D, D), jnp.bfloat16),
            pltpu.VMEM((4, 4, 2, ROWS, D), jnp.bfloat16),
            pltpu.SemaphoreType.DMA((6,)),
            pltpu.SemaphoreType.DMA((8,)),
        ],
        compiler_params=PARAMS,
        cost_estimate=pl.CostEstimate(flops=2 * 2048 * D * D, bytes_accessed=12000000, transcendentals=0),
        name="weight_back",
    )(place, low, dq, dk, dv, dwo)


def input_back_kernel(
    dq_any, dk_any, dv_any, w_any, dresid_any, first_out, second_out,
    dq_ref, dk_ref, dv_ref, w_ref, dresid_ref, load_sems, store_sems,
):
    loads = issue(
        (
            (w_any.at[0], w_ref.at[0]), (dq_any, dq_ref), (dresid_any, dresid_ref),
            (w_any.at[1:3], w_ref.at[1:3]), (dk_any, dk_ref), (dv_any, dv_ref),
        ),
        load_sems,
    )
    finish(loads[:3])
    store, stores = storer(store_sems)
    for index, row in enumerate((LEN, LEN + HALF, 0, HALF)):
        rows = slice(row, row + HALF)
        if index == 2:
            finish(loads[3:])
        total = dresid_ref[rows, :] + dot_nt(dq_ref[rows, :], w_ref[0])
        if index >= 2:
            total = total + dot_nt(dk_ref[rows, :], w_ref[1]) + dot_nt(dv_ref[rows, :], w_ref[2])
        dresid_ref[rows, :] = total
        target = first_out if index >= 2 else second_out
        store(dresid_ref.at[rows, :], target.at[row % LEN : row % LEN + HALF, :])
    finish(stores)


def input_back(dq, dk, dv, attn, dresid):
    half = jax.ShapeDtypeStruct((LEN, D), jnp.float32)
    return pl.pallas_call(
        input_back_kernel,
        out_shape=[half, half],
        in_specs=[ANY_SPEC] * 5,
        out_specs=[ANY_SPEC] * 2,
        scratch_shapes=[
            pltpu.VMEM((TALL, D), jnp.bfloat16),
            pltpu.VMEM((LEN, D), jnp.bfloat16),
            pltpu.VMEM((LEN, D), jnp.bfloat16),
            pltpu.VMEM((3, D, D), jnp.bfloat16),
            pltpu.VMEM((TALL, D), jnp.float32),
            pltpu.SemaphoreType.DMA((6,)),
            pltpu.SemaphoreType.DMA((4,)),
        ],
        compiler_params=PARAMS,
        cost_estimate=pl.CostEstimate(flops=2 * 2048 * D * D, bytes_accessed=16000000, transcendentals=0),
        name="input_back",
    )(dq, dk, dv, attn, dresid)


def bias_vectors(table):
    lane = jnp.arange(512, dtype=jnp.int32)
    offset = jnp.where(lane < 384, 128 - lane, 640 - lane)
    onehot = bucket_of(offset)[:, None] == jnp.arange(NB, dtype=jnp.int32)[None, :]
    near = jnp.dot(table, onehot.astype(jnp.float32).T, precision=lax.Precision.HIGHEST)
    return (near[:, None, :], jnp.stack([table[:, 15], table[:, 31]], axis=1), onehot)


def bucket_of(offset):
    distance = jnp.abs(offset)
    far_bucket = jnp.full(distance.shape, 8, jnp.int32)
    for exponent in range(1, 8):
        far_bucket = far_bucket + (distance * distance >= 64 * 2**exponent).astype(jnp.int32)
    near_or_far = jnp.where(distance < 8, distance, far_bucket)
    return near_or_far + NB // 2 * (offset > 0).astype(jnp.int32)


def table_grad(sums, onehot):
    near = jnp.roll(onehot.astype(jnp.float32), 127, axis=0)
    far = jnp.arange(NB, dtype=jnp.int32)[None, :] == jnp.repeat(jnp.array([15, 31]), 128)[:, None]
    return jnp.dot(
        sums[:, 0, :],
        jnp.concatenate([near, far.astype(jnp.float32)]),
        precision=lax.Precision.HIGHEST,
    )


RATES = (ATTENTION_RATE, FEED_RATE, FEED_RATE)


def adam_kernel(*refs):
    states, grads, outs = refs[:9], refs[9:12], refs[-9:]
    for kind, rate in enumerate(RATES):
        master_ref, first_ref, second_ref = states[3 * kind : 3 * kind + 3]
        master_out, first_out, second_out = outs[3 * kind : 3 * kind + 3]
        grad = grads[kind][...].astype(jnp.float32).reshape(master_ref.shape)
        master = master_ref[...]
        first = BETA_ONE * first_ref[...] + (1.0 - BETA_ONE) * grad
        second = BETA_TWO * second_ref[...] + (1.0 - BETA_TWO) * grad * grad
        first_out[...] = first
        second_out[...] = second
        first_scale = rate / (1.0 - BETA_ONE**STEP)
        second_scale = 1.0 / (1.0 - BETA_TWO**STEP)
        step = (first_scale * first) / (jnp.sqrt(second_scale * second) + ADAM_EPS)
        master_out[...] = master - (step + (rate * WEIGHT_DECAY) * master)


def adam(layer, state, quarters, held):
    blocks = (
        [pl.BlockSpec((1, 1, ROWS, D), lambda i: (layer, i, 0, 0))] * 3
        + [pl.BlockSpec((1, ROWS, D), lambda i: (layer, 0, i))] * 3
        + [pl.BlockSpec((1, ROWS, D), lambda i: (layer, i, 0))] * 3
    )
    grads = [
        pl.BlockSpec((1, 1, ROWS, D), partial(lambda member, i: (i, member, 0, 0), member))
        for member in (2, 0, 1)
    ]
    return pl.pallas_call(
        adam_kernel,
        grid=(4,),
        out_shape=[jax.ShapeDtypeStruct(array.shape, jnp.float32) for array in state],
        in_specs=blocks + grads + [ANY_SPEC] * len(held),
        out_specs=blocks,
        input_output_aliases={12 + index: index for index in range(len(held))},
        compiler_params=PARAMS,
        cost_estimate=pl.CostEstimate(flops=20000000, bytes_accessed=22000000, transcendentals=0),
        name="adam",
    )(*state, quarters, quarters, quarters, *held)


def fetch_forward(shards):
    low = tuple(shard.astype(jnp.bfloat16) for shard in shards)
    return (
        lax.all_gather(low[0], "fsdp", axis=1, tiled=True),
        lax.all_gather(low[1], "fsdp", axis=0, tiled=True),
        lax.all_gather(low[2], "fsdp", axis=0, tiled=True),
    )


def reduce_layer(grads):
    owned = tuple(
        lax.psum_scatter(
            grad.astype(jnp.bfloat16), "fsdp", scatter_dimension=axis, tiled=True
        ).astype(jnp.float32)
        for grad, axis in zip(grads, (1, 0, 0))
    )
    return lax.psum(owned, "dp")


def forward_layer(hidden_c, hidden_q, weights, lengths, flag_rows, onehot):
    attn_w, inner_w, outer_w, small_w = weights
    pieces, hidden_bias, bias_table = unpack(small_w.astype(jnp.float32))
    bias_q, bias_v, bias_o, gain_one, shift_one, bias_two, gain_two, shift_two = pieces
    table_low = bias_table.astype(jnp.bfloat16)
    low_c = hidden_c.astype(jnp.bfloat16)
    low_q = hidden_q.astype(jnp.bfloat16)
    projected = jnp.einsum("td,sde->ste", low_c, attn_w[:3], preferred_element_type=jnp.float32)
    query_c = (projected[0] + bias_q).astype(jnp.bfloat16)
    key_rows = projected[1].astype(jnp.bfloat16)
    value_rows = (projected[2] + bias_v).astype(jnp.bfloat16)
    query_q = (jnp.dot(low_q, attn_w[0], preferred_element_type=jnp.float32) + bias_q).astype(
        jnp.bfloat16
    )
    mixed_c, mixed_q, lse_c, lse_q = lax.map(
        partial(attend_slot, onehot, table_low),
        (
            to_heads(query_c),
            to_heads(query_q),
            to_heads(key_rows),
            to_heads(value_rows),
            lengths,
            flag_rows,
        ),
    )
    mixed_c = mixed_c.reshape(-1, D)
    mixed_q = mixed_q.reshape(-1, D)
    outputs = []
    kept = []
    for hidden_in, mixed in ((hidden_c, mixed_c), (hidden_q, mixed_q)):
        resid = hidden_in + jnp.dot(mixed, attn_w[3], preferred_element_type=jnp.float32) + bias_o
        normed = layer_norm(resid, gain_one, shift_one)
        pre_act = (
            jnp.dot(normed.astype(jnp.bfloat16), inner_w, preferred_element_type=jnp.float32)
            + hidden_bias
        )
        active = jax.nn.gelu(pre_act, approximate=True).astype(jnp.bfloat16)
        summed = normed + jnp.dot(active, outer_w, preferred_element_type=jnp.float32) + bias_two
        outputs.append(layer_norm(summed, gain_two, shift_two))
        kept.append((resid, summed, pre_act))
    saved = (
        hidden_c,
        hidden_q,
        query_c,
        query_q,
        key_rows,
        value_rows,
        lse_c,
        lse_q,
        mixed_c,
        mixed_q,
        kept[0],
        kept[1],
    )
    return (outputs[0], outputs[1], saved)


def backward_layer(saved, weights, grad_c, grad_q, lengths, flag_rows, onehot):
    attn_w, inner_w, outer_w, small_w = weights
    pieces, hidden_bias, bias_table = unpack(small_w.astype(jnp.float32))
    bias_q, bias_v, bias_o, gain_one, shift_one, bias_two, gain_two, shift_two = pieces
    table_low = bias_table.astype(jnp.bfloat16)
    (
        hidden_c,
        hidden_q,
        query_c,
        query_q,
        key_rows,
        value_rows,
        lse_c,
        lse_q,
        mixed_c,
        mixed_q,
        kept_c,
        kept_q,
    ) = saved
    gelu_tanh = partial(jax.nn.gelu, approximate=True)
    grad_outer = jnp.zeros(outer_w.shape, jnp.float32)
    grad_inner = jnp.zeros(inner_w.shape, jnp.float32)
    grad_attn_out = jnp.zeros((D, D), jnp.float32)
    grad_bias_two = jnp.zeros((D,), jnp.float32)
    grad_hidden_bias = jnp.zeros((FF,), jnp.float32)
    grad_bias_o = jnp.zeros((D,), jnp.float32)
    grad_gain_one = jnp.zeros((D,), jnp.float32)
    grad_shift_one = jnp.zeros((D,), jnp.float32)
    grad_gain_two = jnp.zeros((D,), jnp.float32)
    grad_shift_two = jnp.zeros((D,), jnp.float32)
    residual_grads = []
    mix_grads = []
    for kept_rows, grad_out, mixed in ((kept_c, grad_c, mixed_c), (kept_q, grad_q, mixed_q)):
        resid, summed, pre_act = kept_rows
        normed, norm_one_back = jax.vjp(layer_norm, resid, gain_one, shift_one)
        unused_out, norm_two_back = jax.vjp(layer_norm, summed, gain_two, shift_two)
        grad_summed, grad_g2, grad_s2 = norm_two_back(grad_out)
        grad_gain_two = grad_gain_two + grad_g2
        grad_shift_two = grad_shift_two + grad_s2
        grad_branch = grad_summed.astype(jnp.bfloat16)
        grad_bias_two = grad_bias_two + jnp.sum(grad_branch.astype(jnp.float32), axis=0)
        active, gelu_back = jax.vjp(gelu_tanh, pre_act)
        grad_outer = grad_outer + jnp.einsum(
            "tf,td->fd",
            active.astype(jnp.bfloat16),
            grad_branch,
            preferred_element_type=jnp.float32,
        )
        grad_active = jnp.einsum(
            "td,fd->tf", grad_branch, outer_w, preferred_element_type=jnp.float32
        )
        grad_pre = gelu_back(grad_active)[0].astype(jnp.bfloat16)
        grad_hidden_bias = grad_hidden_bias + jnp.sum(grad_pre.astype(jnp.float32), axis=0)
        grad_inner = grad_inner + jnp.einsum(
            "td,tf->df", normed.astype(jnp.bfloat16), grad_pre, preferred_element_type=jnp.float32
        )
        grad_normed = grad_summed + jnp.einsum(
            "tf,df->td", grad_pre, inner_w, preferred_element_type=jnp.float32
        )
        grad_resid, grad_g1, grad_s1 = norm_one_back(grad_normed)
        grad_gain_one = grad_gain_one + grad_g1
        grad_shift_one = grad_shift_one + grad_s1
        grad_proj = grad_resid.astype(jnp.bfloat16)
        grad_bias_o = grad_bias_o + jnp.sum(grad_proj.astype(jnp.float32), axis=0)
        grad_attn_out = grad_attn_out + jnp.einsum(
            "td,te->de", mixed, grad_proj, preferred_element_type=jnp.float32
        )
        mix_grads.append(
            jnp.einsum(
                "te,de->td", grad_proj, attn_w[3], preferred_element_type=jnp.float32
            ).astype(jnp.bfloat16)
        )
        residual_grads.append(grad_resid)
    grad_query_c, grad_query_q, grad_keys, grad_values, grad_table = lax.map(
        partial(attend_back, onehot, table_low),
        (
            to_heads(query_c),
            to_heads(query_q),
            to_heads(key_rows),
            to_heads(value_rows),
            lengths,
            flag_rows,
            lse_c,
            lse_q,
            to_heads(mix_grads[0]),
            to_heads(mix_grads[1]),
        ),
    )
    grad_table = jnp.sum(grad_table, axis=0)
    low_query_c = grad_query_c.reshape(-1, D).astype(jnp.bfloat16)
    low_query_q = grad_query_q.reshape(-1, D).astype(jnp.bfloat16)
    low_keys = grad_keys.reshape(-1, D).astype(jnp.bfloat16)
    low_values = grad_values.reshape(-1, D).astype(jnp.bfloat16)
    low_c = hidden_c.astype(jnp.bfloat16)
    low_q = hidden_q.astype(jnp.bfloat16)
    stacked_grads = jnp.stack([low_query_c, low_keys, low_values])
    grad_qkv = jnp.einsum("td,ste->sde", low_c, stacked_grads, preferred_element_type=jnp.float32)
    grad_wq = grad_qkv[0] + jnp.einsum(
        "td,te->de", low_q, low_query_q, preferred_element_type=jnp.float32
    )
    grad_attn = jnp.stack([grad_wq, grad_qkv[1], grad_qkv[2], grad_attn_out])
    grad_bias_q = jnp.sum(low_query_c.astype(jnp.float32), axis=0) + jnp.sum(
        low_query_q.astype(jnp.float32), axis=0
    )
    grad_bias_v = jnp.sum(low_values.astype(jnp.float32), axis=0)
    grad_content = residual_grads[0] + jnp.einsum(
        "ste,sde->td", stacked_grads, attn_w[:3], preferred_element_type=jnp.float32
    )
    grad_query_in = residual_grads[1] + jnp.einsum(
        "te,de->td", low_query_q, attn_w[0], preferred_element_type=jnp.float32
    )
    grad_small = jnp.concatenate(
        [
            grad_bias_q,
            grad_bias_v,
            grad_bias_o,
            grad_gain_one,
            grad_shift_one,
            grad_bias_two,
            grad_gain_two,
            grad_shift_two,
            grad_hidden_bias,
            grad_table.reshape(-1),
        ]
    )
    return (grad_content, grad_query_in, (grad_attn, grad_inner, grad_outer, grad_small))


def adam_update(master, first, second, grad, rate):
    first_new = BETA_ONE * first + (1.0 - BETA_ONE) * grad
    second_new = BETA_TWO * second + (1.0 - BETA_TWO) * grad * grad
    first_hat = first_new / (1.0 - BETA_ONE**STEP)
    second_hat = second_new / (1.0 - BETA_TWO**STEP)
    master_new = master - rate * (
        first_hat / (jnp.sqrt(second_hat) + ADAM_EPS) + WEIGHT_DECAY * master
    )
    return (master_new, first_new, second_new)


def per_device(
    content,
    query,
    lengths,
    predicted,
    content_cot,
    query_cot,
    attn_master,
    attn_first,
    attn_second,
    inner_master,
    inner_first,
    inner_second,
    outer_master,
    outer_first,
    outer_second,
    small_master,
    small_first,
    small_second,
):
    masters = (attn_master, inner_master, outer_master, small_master)
    slot_count = lengths.shape[0]
    flag_rows = predicted.reshape(slot_count, LEN)
    onehot = bucket_onehot()
    hidden_c = content.astype(jnp.float32)
    hidden_q = query.astype(jnp.float32)
    kept_weights = []
    saved_layers = []
    small_all = lax.all_gather(
        small_master.astype(jnp.bfloat16), "fsdp", axis=1, tiled=True
    )
    for layer_index in range(LAYERS):
        shards = tuple((master[layer_index] for master in masters[:3]))
        gathered = fetch_forward(shards) + (small_all[layer_index],)
        kept_weights.append(gathered)
        hidden_c, hidden_q, saved = forward_layer(
            hidden_c, hidden_q, gathered, lengths, flag_rows, onehot
        )
        saved_layers.append(saved)
    position = jnp.arange(LEN, dtype=jnp.int32)
    valid_rows = (position[None, :] < lengths[:, None]).reshape(-1, 1).astype(jnp.float32)
    grad_c = content_cot.astype(jnp.float32) * valid_rows
    grad_q = query_cot.astype(jnp.float32) * valid_rows
    layer_grads = [None] * LAYERS
    small_grads = [None] * LAYERS
    for layer_index in reversed(range(LAYERS)):
        grad_c, grad_q, local_grads = backward_layer(
            saved_layers[layer_index],
            kept_weights[layer_index],
            grad_c,
            grad_q,
            lengths,
            flag_rows,
            onehot,
        )
        small_grads[layer_index] = local_grads[3]
        layer_grads[layer_index] = reduce_layer(local_grads[:3])
    small_sum = lax.psum(jnp.stack(small_grads), ("dp", "fsdp"))
    owned = small_master.shape[1]
    small_own = lax.dynamic_slice_in_dim(
        small_sum, lax.axis_index("fsdp") * owned, owned, 1
    )
    reduced = tuple(
        (
            jnp.stack([layer_grads[layer_index][member] for layer_index in range(LAYERS)])
            for member in range(3)
        )
    ) + (small_own,)
    attn_new = adam_update(attn_master, attn_first, attn_second, reduced[0], ATTENTION_RATE)
    inner_new = adam_update(inner_master, inner_first, inner_second, reduced[1], FEED_RATE)
    outer_new = adam_update(outer_master, outer_first, outer_second, reduced[2], FEED_RATE)
    small_new = adam_update(small_master, small_first, small_second, reduced[3], SMALL_RATE)
    return (
        hidden_c.astype(jnp.bfloat16),
        hidden_q.astype(jnp.bfloat16),
        grad_c,
        grad_q,
        attn_new[0],
        attn_new[1],
        attn_new[2],
        inner_new[0],
        inner_new[1],
        inner_new[2],
        outer_new[0],
        outer_new[1],
        outer_new[2],
        small_new[0],
        small_new[1],
        small_new[2],
    )


def after(value, *others):
    return lax.optimization_barrier((value, others))[0]


def join(*values):
    return lax.optimization_barrier(values)


def gather_group(count, shards, plane, column, sides, corners, mine, theirs):
    plan = []
    for core, arrays in enumerate((mine, theirs)):
        base = core * len(mine)
        for member in range(count):
            array, first = plane
            plan += [
                (base + array, first + side * count + member, side, 1, core, 0, member)
                for side in range(2)
            ]
            for apart in (1, 2, 3):
                index = (apart - 1) * count + member
                array, first = column
                plan.append((base + array, first + index, 0, 0, core, apart, member))
                for dx, dy, (array, first) in ((1, 0, sides[0]), (0, 1, sides[1])):
                    plan.append((base + array, first + index, dx, dy, core, apart, member))
                skipped = 0
                for array, first, held in corners:
                    if skipped <= index < skipped + held:
                        plan.append(
                            (base + array, first + index - skipped, 1, 1, core, apart, member)
                        )
                    skipped += held
    return (tuple(plan), tuple(shards) + tuple(mine) + tuple(theirs))


def gather_small(blocks, place):
    low, high = place[2] % 2, place[2] // 2
    blocks = jnp.where(low == 0, blocks, blocks[jnp.array([1, 0, 3, 2])])
    blocks = jnp.where(high == 0, blocks, blocks[jnp.array([2, 3, 0, 1])])
    return blocks.transpose(2, 0, 1, 3).reshape(blocks.shape[2], -1)


def add_low(*values):
    total = values[0].astype(jnp.float32)
    for value in values[1:]:
        total = total + value.astype(jnp.float32)
    return total.astype(jnp.bfloat16)


def reduce_corners(keep, get):
    corner = add_low(keep[1, 1], get[1, 1])
    return (swap_x(corner[:2]), swap_y(corner[2:]))


def side_payloads(keep, get, corners):
    by_x, by_y = corners
    pad = ((0, 0),) * 3
    for_x = add_low(keep[0, 1], get[0, 1], jnp.pad(by_y, ((2, 0),) + pad))
    for_y = add_low(keep[1, 0], get[1, 0], jnp.pad(by_x, ((0, 2),) + pad))
    return (for_x, for_y)


def reduce_sides(payloads):
    return (swap_x(payloads[0]), swap_y(payloads[1]))


def z_half(value, half):
    if value.ndim == 4:
        return lax.dynamic_slice_in_dim(value, 2 * half, 2, 0)
    part = lax.dynamic_slice(value, (0, 0, 2 * half, 0, 0, 0), (1, 1, 2) + value.shape[3:])
    return part[0, 0]


def far_payload(keep, get, sides, place):
    half = 1 - place[2] // 2
    return add_low(*(z_half(value, half) for value in (keep, get) + tuple(sides)))


def own_pair(keep, get, sides, far, place):
    half = place[2] // 2
    return add_low(*(z_half(value, half) for value in (keep, get) + tuple(sides)), far)


def pick(pair, index):
    return lax.dynamic_index_in_dim(pair, index, 0, keepdims=False)


def reduce_near(pair, place):
    return swap_z(pick(pair, 1 - place[2] % 2), 1)


def reduce_total(pair, near, place):
    return add_low(pick(pair, place[2] % 2), near)


def reduce_direct(column, place):
    return tuple(swap_z(pick(column, place[2] ^ apart), apart) for apart in (1, 2, 3))


def share_core(pair, place):
    x, c = place[0], place[1]
    other = swap_core(pair)
    cores = jnp.where(c == 0, jnp.stack([pair, other], 1), jnp.stack([other, pair], 1))
    sides = jnp.where(x == 0, cores, cores[::-1])
    return sides.reshape((4,) + pair.shape[1:])


def small_parts(vectors):
    values = vectors.astype(jnp.float32)
    return (
        values[: 8 * D].reshape(8, D),
        values[8 * D : 8 * D + FF].reshape(1, FF),
        bias_vectors(values[8 * D + FF :].reshape(H, NB)),
    )


def per_device_fast(
    content,
    query,
    lengths,
    predicted,
    content_cot,
    query_cot,
    attn_master,
    attn_first,
    attn_second,
    inner_master,
    inner_first,
    inner_second,
    outer_master,
    outer_first,
    outer_second,
    small_master,
    small_first,
    small_second,
):
    place_parts = my_place()
    place = jnp.stack(place_parts).astype(jnp.int32)
    own_a0, plane_a0, own_f0 = cast_first(place, attn_master, inner_master, outer_master)
    z_a0 = tuple(swap_z(own_a0, apart) for apart in (1, 2, 3))
    plane_a0 = swap_y(plane_a0)
    near_f0 = swap_z(own_f0, 1)
    attn_low0, attn_low1, inner_low0, inner_low1, outer_low0, outer_low1, plane_f0, own_1, oth_1 = (
        cast_rest(place, attn_master, inner_master, outer_master)
    )
    low0 = jnp.concatenate([content, query])
    row_flags = predicted.reshape(1, LEN).astype(jnp.float32)
    col_flags = predicted.reshape(LEN, 1).astype(jnp.float32)
    small_low = small_master.astype(jnp.bfloat16)
    small_y = swap_y(small_low)
    z_a0, plane_a0, near_f0, plane_f0, own_1, oth_1, low0, row_flags, col_flags, small_y = join(
        z_a0, plane_a0, near_f0, plane_f0, own_1, oth_1, low0, row_flags, col_flags, small_y
    )
    col_a0, to_far_f0 = pack(
        ([(0, 0, 1), (1, 0, 1), (2, 0, 1)], [(3, 0, 2), (4, 0, 2)]), (*z_a0, own_f0, near_f0)
    )
    x0 = swap_x(col_a0)
    y0 = swap_y(col_a0)
    far_f0 = swap_z(to_far_f0, 2)
    plane_f0 = swap_y(after(plane_f0, col_a0))
    near_1 = swap_z(after(own_1, col_a0), 1)
    odd = place_parts[3] == 1
    small_pair = jnp.stack(
        [jnp.where(odd, small_y, small_low), jnp.where(odd, small_low, small_y)]
    )
    small_near = swap_z(small_pair, 1)
    x0, y0, far_f0, plane_f0, near_1, small_near = join(
        x0, y0, far_f0, plane_f0, near_1, small_near
    )
    to_x1, to_y1, to_far_a1 = pack(
        (
            [(0, 0, 2), (1, 0, 4), (2, 0, 2)],
            [(0, 0, 2), (1, 0, 4), (3, 2, 1)],
            [(4, 0, 1), (5, 0, 1)],
        ),
        (near_f0, far_f0, y0, x0, own_1, near_1),
    )
    x1 = swap_x(to_x1)
    y1 = swap_y(to_y1)
    far_a1 = swap_z(to_far_a1, 2)
    (mine_0,) = pack(
        (
            [(0, 0, 2), (1, 0, 3), (2, 0, 3), (3, 0, 3), (4, 0, 4), (5, 0, 2), (6, 0, 4)],
        ),
        after((plane_a0, col_a0, x0, y0, plane_f0, near_f0, far_f0), to_x1),
    )
    theirs_0 = swap_core(mine_0)
    small_four = jnp.stack([small_pair, small_near])
    small_far = swap_z(small_four, 2)
    small_all = gather_small(jnp.concatenate([small_four, small_far]), place_parts)
    small0, hidden_bias0, (tvec0, far0, onehot) = small_parts(small_all[0])
    small1, hidden_bias1, (tvec1, far1, onehot) = small_parts(small_all[1])
    x1, y1, far_a1, theirs_0, small0, hidden_bias0, tvec0, far0 = join(
        x1, y1, far_a1, theirs_0, small0, hidden_bias0, tvec0, far0
    )
    to_x2, to_y2, to_far_f1, col_a1 = pack(
        (
            [(0, 0, 1), (1, 0, 2), (2, 0, 4)],
            [(0, 0, 1), (1, 0, 2), (3, 4, 2), (4, 0, 1), (5, 0, 1)],
            [(4, 1, 2), (0, 1, 2)],
            [(0, 0, 1), (1, 0, 2)],
        ),
        (near_1, far_a1, y1, x1, own_1, oth_1),
    )
    x2 = swap_x(to_x2)
    y2 = swap_y(to_y2)
    far_f1 = swap_z(to_far_f1, 2)
    their_x1, their_y1 = swap_core(x1), swap_core(y1)
    group_a0 = gather_group(
        1, (attn_low0,), (0, 0), (0, 2), ((0, 5), (0, 8)), ((1, 6, 2), (2, 6, 1)),
        (mine_0, x1, y1), (theirs_0, their_x1, their_y1),
    )
    q0, k0, v0, attn0 = project(place, low0, small0, group_a0)
    mixed0, p0, inverse0, dead = mix(lengths, far0, tvec0, q0, k0, v0, row_flags, col_flags)
    x2, y2, far_f1, mixed0 = join(x2, y2, far_f1, mixed0)
    to_x3, to_y3, col_f1 = pack(
        (
            [(0, 1, 2), (1, 0, 4), (2, 0, 3)],
            [(0, 1, 2), (1, 0, 4), (3, 1, 2), (4, 1, 2)],
            [(0, 1, 2), (1, 0, 4)],
        ),
        (near_1, far_f1, y2, own_1, oth_1),
    )
    x3 = swap_x(to_x3)
    y3 = swap_y(to_y3)
    their_x2, their_y2, their_a1 = swap_core(x2), swap_core(y2), swap_core(after(col_a1, x2))
    group_f0 = gather_group(
        2, (inner_low0, outer_low0), (0, 11), (0, 15), ((1, 0), (2, 0)), ((3, 3, 4), (4, 3, 2)),
        (mine_0, x1, y1, x2, y2), (theirs_0, their_x1, their_y1, their_x2, their_y2),
    )
    resid0, pre0, normed0, low1, summed0 = feed(
        place, small0, hidden_bias0, mixed0, low0, attn0, group_f0
    )
    x3, y3, low1 = join(x3, y3, low1)
    to_x4, to_y4 = pack(([(0, 0, 3)], [(1, 3, 3)]), (y3, x3))
    x4 = swap_x(to_x4)
    y4 = swap_y(to_y4)
    their_x3, their_y3 = swap_core(x3), swap_core(y3)
    group_a1 = gather_group(
        1, (attn_low1,), (1, 5), (2, 0), ((0, 0), (1, 0)), ((3, 6, 3),),
        (x2, y2, col_a1, x3), (their_x2, their_y2, their_a1, their_x3),
    )
    q1, k1, v1, attn1 = project(place, low1, small1, group_a1)
    x4, y4, q1 = join(x4, y4, q1)
    their_x4, their_y4, their_f1 = swap_core(x4), swap_core(y4), swap_core(after(col_f1, q1))
    group_f1 = gather_group(
        2, (inner_low1, outer_low1), (1, 6), (4, 0), ((0, 0), (1, 0)), ((2, 0, 3), (3, 0, 3)),
        (x3, y3, x4, y4, col_f1), (their_x3, their_y3, their_x4, their_y4, their_f1),
    )
    mixed1, p1, inverse1, dead = mix(
        lengths, far1, tvec1, q1, k1, v1, row_flags, col_flags
    )
    content_out, query_out, dresid1, dmix1, dwo1, keep_f1, send_f1, vec_f1, dhidden1 = turn(
        place, lengths, small1, small0, hidden_bias1, mixed1, summed0, attn1,
        (content_cot, query_cot), group_f1
    )
    get_f1 = swap_core(send_f1)
    *first1, table1_a = mix_back(0, q1, k1, v1, dmix1, mixed1, p1, inverse1, dead)
    by_f1 = reduce_corners(keep_f1, after(get_f1, table1_a))
    dq1, dk1, dv1, table1_b = mix_back(
        3, after(q1, get_f1, table1_a), k1, v1, dmix1, mixed1, p1, inverse1, dead, tuple(first1)
    )
    sides_rf1 = reduce_sides(side_payloads(keep_f1, get_f1, after(by_f1, table1_b)))
    keep_a1, send_a1, vec_a1 = weight_back(place, after(low1, by_f1), dq1, dk1, dv1, dwo1)
    get_a1 = swap_core(send_a1)
    by_a1 = reduce_corners(keep_a1, get_a1)
    dresid0, dmix0, dwo0, keep_f0, send_f0, vec_f0, dhidden0 = down(
        place, small0, dq1, dk1, dv1, after(attn1, get_a1), dresid1, summed0, normed0, resid0,
        pre0, mixed0, attn0, group_f0
    )
    get_f0 = swap_core(after(send_f0, sides_rf1, by_a1))
    sides_ra1 = reduce_sides(side_payloads(keep_a1, get_a1, after(by_a1, dmix0)))
    sides_rf1 = after(sides_rf1, dmix0)
    zfar_f1 = swap_z(far_payload(keep_f1, get_f1, sides_rf1, place_parts), 2)
    *first0, table0_a = mix_back(
        0, after(q0, by_a1, sides_rf1), k0, v0, dmix0, mixed0, p0, inverse0, dead
    )
    by_f0 = reduce_corners(keep_f0, after(get_f0, table0_a))
    dq0, dk0, dv0, table0_b = mix_back(
        3, after(q0, get_f0, table0_a), k0, v0, dmix0, mixed0, p0, inverse0, dead, tuple(first0)
    )
    by_f0, sides_ra1, zfar_f1, table0_b = join(by_f0, sides_ra1, zfar_f1, table0_b)
    payloads_f0 = side_payloads(keep_f0, get_f0, by_f0)
    sides_rf0 = reduce_sides(payloads_f0)
    keep_a0, send_a0, vec_a0 = weight_back(
        place, after(low0, payloads_f0, table0_b), dq0, dk0, dv0, dwo0
    )
    get_a0 = swap_core(send_a0)
    zfar_a1 = swap_z(far_payload(keep_a1, get_a1, sides_ra1, place_parts), 2)
    small_sum = jnp.concatenate(
        [
            jnp.stack([vec_a0, vec_a1]).reshape(LAYERS, -1),
            jnp.stack([vec_f0, vec_f1]).reshape(LAYERS, -1),
            jnp.stack([dhidden0, dhidden1]).reshape(LAYERS, -1),
            table_grad(
                jnp.concatenate([table0_a, table0_b, table1_a, table1_b]), onehot
            ).reshape(LAYERS, -1),
        ],
        axis=1,
    )
    pair_f1 = own_pair(keep_f1, get_f1, sides_rf1, zfar_f1, place_parts)
    znear_f1 = reduce_near(pair_f1, place_parts)
    small_c = swap_core(small_sum)
    by_a0 = reduce_corners(keep_a0, get_a0)
    sides_rf0, by_a0, zfar_a1, znear_f1, small_c = join(
        sides_rf0, by_a0, zfar_a1, znear_f1, small_c
    )
    payload_f0 = far_payload(keep_f0, get_f0, sides_rf0, place_parts)
    zfar_f0 = swap_z(payload_f0, 2)
    pair_a1 = own_pair(keep_a1, get_a1, sides_ra1, zfar_a1, place_parts)
    znear_a1 = reduce_near(after(pair_a1, payload_f0), place_parts)
    content_grad, query_grad = input_back(after(dq0, sides_rf0), dk0, dv0, attn0, dresid0)
    small_sum = after(small_sum, payload_f0) + small_c
    small_y = swap_y(small_sum)
    payloads_a0 = side_payloads(keep_a0, get_a0, after(by_a0, payload_f0))
    sides_ra0 = reduce_sides(payloads_a0)
    own_1 = jnp.concatenate(
        [
            reduce_total(pair_f1, znear_f1, place_parts),
            reduce_total(pair_a1, znear_a1, place_parts),
        ]
    )
    across_1 = swap_x(after(own_1, payloads_a0))
    sides_ra0, zfar_f0, small_y, content_grad = join(sides_ra0, zfar_f0, small_y, content_grad)
    column_a0 = add_low(keep_a0[0, 0], get_a0[0, 0], *sides_ra0)
    shifts_a0 = reduce_direct(column_a0, place_parts)
    pair_f0 = own_pair(keep_f0, get_f0, sides_rf0, zfar_f0, place_parts)
    znear_f0 = reduce_near(after(pair_f0, column_a0), place_parts)
    small_sum = after(small_sum, column_a0) + small_y
    small_x = swap_x(small_sum)
    shifts_a0, znear_f0, across_1, small_x = join(shifts_a0, znear_f0, across_1, small_x)
    own_0 = jnp.concatenate(
        [
            reduce_total(pair_f0, znear_f0, place_parts),
            add_low(pick(column_a0, place_parts[2]), *shifts_a0),
        ]
    )
    across_0 = swap_x(own_0)
    four_1 = share_core(jnp.stack([own_1, after(across_1, own_0)]), place_parts)
    state = (
        attn_master, attn_first, attn_second, inner_master, inner_first, inner_second,
        outer_master, outer_first, outer_second,
    )
    new_1 = adam(1, state, four_1, ())
    small_sum = after(small_sum, own_0) + small_x
    small_z = tuple(swap_z(small_sum, apart) for apart in (1, 2, 3))
    across_0, new_1, small_z = join(across_0, new_1, small_z)
    four_0 = share_core(jnp.stack([own_0, across_0]), place_parts)
    small_sum = small_sum + small_z[0] + small_z[1] + small_z[2]
    new_0 = adam(0, state, four_0, tuple(new_1))
    size = small_master.shape[1]
    small_own = lax.dynamic_slice_in_dim(small_sum, lax.axis_index("fsdp") * size, size, 1)
    small_new = adam_update(small_master, small_first, small_second, small_own, SMALL_RATE)
    return (
        (content_out, query_out, content_grad, query_grad)
        + tuple(new_0)
        + small_new
    )


def solution(mesh):
    placed = (
        P(("dp", "fsdp"), None),
        P(("dp", "fsdp"), None),
        P(("dp", "fsdp")),
        P(("dp", "fsdp")),
        P(("dp", "fsdp"), None),
        P(("dp", "fsdp"), None),
        P(None, None, "fsdp", None),
        P(None, None, "fsdp", None),
        P(None, None, "fsdp", None),
        P(None, "fsdp", None),
        P(None, "fsdp", None),
        P(None, "fsdp", None),
        P(None, "fsdp", None),
        P(None, "fsdp", None),
        P(None, "fsdp", None),
        P(None, "fsdp"),
        P(None, "fsdp"),
        P(None, "fsdp"),
    )
    fast = tuple(mesh.shape.values()) == (4, 8)
    return jax.shard_map(
        per_device_fast if fast else per_device,
        mesh=mesh,
        in_specs=placed,
        out_specs=(
            P(("dp", "fsdp"), None),
            P(("dp", "fsdp"), None),
            P(("dp", "fsdp"), None),
            P(("dp", "fsdp"), None),
            P(None, None, "fsdp", None),
            P(None, None, "fsdp", None),
            P(None, None, "fsdp", None),
            P(None, "fsdp", None),
            P(None, "fsdp", None),
            P(None, "fsdp", None),
            P(None, "fsdp", None),
            P(None, "fsdp", None),
            P(None, "fsdp", None),
            P(None, "fsdp"),
            P(None, "fsdp"),
            P(None, "fsdp"),
        ),
        check_vma=False,
    )
```
